32 devices in a mesh: shard: 4 (over x, core), heads: 4 (over z), tensor: 2 (over y).
Axes of the slice: x: 2, y: 2, z: 4, core: 2. Of those that a mesh axis runs over, the one named last changes fastest.
Arguments:
- tokens: bfloat16 [64, 197, 768], P(('shard', 'tensor')), may hold values from -6 to 6
- norm_scales: bfloat16 [2, 768], P(None, ('shard', 'tensor')), may hold values from 0.5 to 1.5
- norm_biases: bfloat16 [2, 768], P(None, ('shard', 'tensor')), may hold values from -0.59765625 to 0.59765625
- w_attn: bfloat16 [4, 768, 768], P(None, ('shard', 'tensor'), 'heads'), may hold values from -0.3125 to 0.3125
- phi: bfloat16 [768, 64], P(('shard', 'tensor'), 'heads'), may hold values from -0.109375 to 0.109375
- experts: bfloat16 [768, 2, 64, 3072], P('shard', None, 'heads', 'tensor'), may hold values from -2 to 2
- in_bias: bfloat16 [64, 3072], P('heads', ('shard', 'tensor')), may hold values from -0.59765625 to 0.59765625
- out_bias: bfloat16 [64, 768], P('heads', ('shard', 'tensor')), may hold values from -4.78125 to 4.78125
- cotangent: bfloat16 [64, 197, 768], P(('shard', 'tensor')), may hold values from -6 to 6
Outputs:
- output: bfloat16 [64, 197, 768], P(('shard', 'tensor'))
- input_grad: bfloat16 [64, 197, 768], P(('shard', 'tensor'))
- scales_grad: float32 [2, 768], P(None, ('shard', 'tensor'))
- biases_grad: float32 [2, 768], P(None, ('shard', 'tensor'))
- attn_grad: float32 [4, 768, 768], P(None, ('shard', 'tensor'), 'heads')
- phi_grad: float32 [768, 64], P(('shard', 'tensor'), 'heads')
- experts_grad: float32 [768, 2, 64, 3072], P('shard', None, 'heads', 'tensor')
- in_bias_grad: float32 [64, 3072], P('heads', ('shard', 'tensor'))
- out_bias_grad: float32 [64, 768], P('heads', ('shard', 'tensor'))
The draws below stay inside these ranges and needn't reach their ends.
All inputs are finite; a program needn't handle non-finite values.
Results may differ from the reference program's by a relative error of at most 0.019.
Values may be sent and summed in bfloat16 or wider, within the bound.
A program may use at most 576 MiB of HBM per device.

```python
from functools import partial
import jax
import jax.numpy as jnp
from jax import lax

D = 768
HEADS = 12
HEAD_DIM = 64
EXPERTS = 64
FF = 3072
SEQ = 197
IMG_DEV = 8
IMAGES = 64
N_TENSOR = 2


def draw_experts(key, part):
    key = jax.random.fold_in(key, 5)
    values = jax.random.truncated_normal(key, -4.0, 4.0, (D, 2, EXPERTS, FF), jnp.float32)
    factors = jnp.array([8.0 * D ** (-0.5), 12.0 * FF ** (-0.5)], jnp.float32)
    scaled = jnp.clip(values * factors[None, :, None, None], -2.0, 2.0)
    return scaled.astype(jnp.bfloat16)


def block_levels(rng, dims, shards, low, high):
    factor_of, own = 1.0, jax.random.fold_in(rng, 6)
    for dim, shards_of in shards:
        draws = jnp.exp(jax.random.uniform(jax.random.fold_in(own, dim), (shards_of,), jnp.float32, low / len(shards), high / len(shards)))
        factor_of = factor_of * jnp.repeat(draws, dims[dim] // shards_of).reshape([-1 if axis == dim else 1 for axis in range(len(dims))])
    return factor_of


def scatter_about(own_key, extent, width, limit, split=(), kind=jnp.bfloat16):
    values = jax.random.normal(own_key, extent, jnp.float32) * width
    if len(split) > 0:
        values = block_levels(own_key, extent, split, -0.22, 0.18) * values
    return jnp.clip(values, min=-limit, max=limit).astype(kind)


def setup_inputs(seed: int = 0) -> dict:
    keys = jax.random.split(jax.random.key(seed), 10)
    return {
        "tokens": scatter_about(keys[0], (IMAGES, SEQ, D), 1.0, 6.0, ((0, 8),)),
        "norm_scales": jnp.clip(1.0 + 0.1 * jax.random.normal(keys[1], (2, D), jnp.float32), 0.5, 1.5).astype(jnp.bfloat16),
        "norm_biases": scatter_about(keys[2], (2, D), 0.1, 0.59765625, ((1, 8),)),
        "w_attn": scatter_about(keys[3], (4, D, D), (D // 2) ** -0.5, 0.3125, ((1, 8), (2, 4))),
        "phi": scatter_about(keys[4], (D, EXPERTS), (4 * D) ** -0.5, 0.109375, ((0, 8), (1, 4))),
        "experts": draw_experts(jax.random.fold_in(keys[9], 71), 0),
        "in_bias": scatter_about(keys[6], (EXPERTS, FF), 0.1, 0.59765625, ((0, 4), (1, 8))),
        "out_bias": scatter_about(keys[7], (EXPERTS, D), 0.8, 4.78125, ((0, 4), (1, 8))),
        "cotangent": scatter_about(keys[8], (IMAGES, SEQ, D), 1.0, 6.0, ((0, 8),)),
    }


@jax.custom_vjp
def low(v):
    return lax.optimization_barrier(v.astype(jnp.bfloat16)).astype(jnp.float32)

@jax.custom_vjp
def low_back(v):
    return v

def low_keep(v):
    return (low(v), None)

def low_pass(kept, grad):
    return (grad,)

def back_keep(v):
    return (v, None)

def back_low(kept, grad):
    return (low(grad),)
low.defvjp(low_keep, low_pass)
low_back.defvjp(back_keep, back_low)
epsilon = 1e-06
highest = lax.Precision.HIGHEST

def rounded_both(values):
    return low(low_back(values))

def normalize(values, scale, shift):
    centered = values - lax.optimization_barrier(jnp.mean(values, axis=-1, keepdims=True))
    variance = lax.optimization_barrier(jnp.mean(centered * centered, axis=-1, keepdims=True))
    return centered * lax.rsqrt(variance + epsilon) * scale + shift

def group_forward(params, images):
    scales, biases, w_attn, phi, experts, in_bias, out_bias = params
    batch_images = images.shape[0]
    normed_one = low(normalize(images, scales[0], biases[0]))
    projected = jnp.einsum('gsd,kdc->kgsc', normed_one, w_attn[:3], precision=highest)
    head_shape = (batch_images, SEQ, HEADS, HEAD_DIM)
    query = rounded_both(projected[0]).reshape(head_shape)
    keyed = rounded_both(projected[1]).reshape(head_shape)
    valued = rounded_both(projected[2]).reshape(head_shape)
    scores = low_back(jnp.einsum('gqhe,gkhe->ghqk', query, keyed, precision=highest) * HEAD_DIM ** (-0.5))
    probs = low(jax.nn.softmax(scores, axis=-1))
    context = rounded_both(jnp.einsum('ghqk,gkhe->gqhe', probs, valued, precision=highest)).reshape(batch_images, SEQ, D)
    attended = low_back(jnp.einsum('gsc,dc->gsd', context, w_attn[3], precision=highest))
    hidden_one = images + attended
    normed_two = low(normalize(hidden_one, scales[1], biases[1]))
    logits = low_back(jnp.einsum('gsd,de->gse', normed_two, phi, precision=highest))
    dispatch = low(jax.nn.softmax(logits, axis=1))
    combine = low(jax.nn.softmax(logits, axis=-1))
    slot_in = jnp.einsum('gse,gsd->ged', dispatch, normed_two, precision=highest)
    block_width = FF // N_TENSOR
    summed = jnp.zeros((batch_images, EXPERTS, D), jnp.float32)
    for portion in range(N_TENSOR):
        lower = portion * block_width
        upper = lower + block_width
        pre_act = jnp.einsum('ged,def->gef', rounded_both(slot_in), experts[:, 0, :, lower:upper], precision=highest)
        pre_act = low_back(pre_act + in_bias[:, lower:upper])
        activated = low(jax.nn.gelu(pre_act, approximate=False))
        summed = summed + jnp.einsum('gef,def->ged', activated, experts[:, 1, :, lower:upper], precision=highest)
    slot_out = rounded_both(summed + out_bias)
    mixed = jnp.einsum('gse,ged->gsd', combine, slot_out, precision=highest)
    return hidden_one + mixed

def forward(tokens, scales, biases, w_attn, phi, experts, in_bias, out_bias):
    params = (scales, biases, w_attn, phi, experts, in_bias, out_bias)
    group_size = IMG_DEV * N_TENSOR
    stacked = tokens.reshape(IMAGES // group_size, group_size, SEQ, D)
    results = lax.map(jax.checkpoint(partial(group_forward, params)), stacked)
    return results.reshape(IMAGES, SEQ, D)

def reference(tokens, norm_scales, norm_biases, w_attn, phi, experts, in_bias, out_bias, cotangent):
    primals = tuple((values.astype(jnp.float32) for values in (tokens, norm_scales, norm_biases, w_attn, phi, experts, in_bias, out_bias)))
    output, pullback = jax.vjp(forward, *primals)
    grads = pullback(cotangent.astype(jnp.float32))
    return (output.astype(jnp.bfloat16), grads[0].astype(jnp.bfloat16), grads[1], grads[2], grads[3], grads[4], grads[5], grads[6], grads[7])
```

```python
from functools import partial

import jax
import jax.numpy as jnp
from jax import lax
from jax.sharding import PartitionSpec as P

HEAD_DIM = 64
F32 = jnp.float32
BF16 = jnp.bfloat16
ROWS = ("shard", "tensor")
epsilon = 1e-06
einsum = partial(jnp.einsum, preferred_element_type=F32)


def normalize(values, scale, shift):
    centered = values - jnp.mean(values, axis=-1, keepdims=True)
    variance = jnp.mean(centered * centered, axis=-1, keepdims=True)
    inverse = lax.rsqrt(variance + epsilon)
    unit_part = centered * inverse
    return (unit_part * scale + shift, unit_part, inverse)


def normalize_back(grad_output, unit_part, inverse, scale):
    scaled = grad_output * scale
    average = jnp.mean(scaled, axis=-1, keepdims=True)
    projection = jnp.mean(scaled * unit_part, axis=-1, keepdims=True)
    grad_input = inverse * (scaled - average - unit_part * projection)
    return (
        grad_input,
        jnp.sum(grad_output * unit_part, axis=(0, 1)),
        jnp.sum(grad_output, axis=(0, 1)),
    )


def to_experts(slots):
    slots = lax.all_to_all(slots, "heads", split_axis=1, concat_axis=0, tiled=True)
    slots = lax.all_to_all(slots, "shard", split_axis=2, concat_axis=0, tiled=True)
    return lax.all_gather(slots, "tensor", axis=0, tiled=True)


def to_images(slots):
    slots = lax.psum_scatter(slots, "tensor", scatter_dimension=0, tiled=True)
    slots = lax.all_to_all(slots, "shard", split_axis=0, concat_axis=2, tiled=True)
    return lax.all_to_all(slots, "heads", split_axis=0, concat_axis=1, tiled=True)


def shards(tokens, norm_scales, norm_biases, w_attn, phi, experts, in_bias, out_bias, cotangent):
    heads_n = lax.axis_size("heads")
    group, seq_len, width = tokens.shape
    own = group // heads_n
    heads_index = lax.axis_index("heads")
    tensor_index = lax.axis_index("tensor")
    shard_index = lax.axis_index("shard")
    hidden = experts.shape[3]
    rows = experts.shape[0]
    scales, biases, in_full = (
        lax.all_gather(norm_scales, ROWS, axis=1, tiled=True).astype(F32),
        lax.all_gather(norm_biases, ROWS, axis=1, tiled=True).astype(F32),
        lax.all_gather(in_bias, ROWS, axis=1, tiled=True).astype(F32),
    )
    attn = lax.all_gather(
        lax.all_gather(w_attn, "heads", axis=2, tiled=True), ROWS, axis=1, tiled=True
    )
    phi_full = lax.all_gather(
        lax.all_gather(phi, "heads", axis=1, tiled=True), ROWS, axis=0, tiled=True
    )
    out_rows = lax.all_gather(out_bias, "tensor", axis=1, tiled=True).astype(F32)
    e_own = experts.shape[2] // lax.axis_size("shard") if experts.shape[2] % lax.axis_size("shard") == 0 else 0
    in_local = lax.dynamic_slice_in_dim(in_full, tensor_index * hidden, hidden, 1)
    factor = HEAD_DIM ** (-0.5)
    tokens = lax.dynamic_slice_in_dim(tokens, heads_index * own, own, 0)
    cotangent = lax.dynamic_slice_in_dim(cotangent, heads_index * own, own, 0)
    n_heads = width // HEAD_DIM
    inputs = tokens.astype(F32)
    normed_one, unit_one, inverse_one = normalize(inputs, scales[0], biases[0])
    normed_one_b = normed_one.astype(BF16)
    projected = einsum("nsd,kdc->knsc", normed_one_b, attn[:3]).astype(BF16)
    query, keyed, valued = projected.reshape(3, own, seq_len, n_heads, HEAD_DIM)
    scores = einsum("nqhe,nkhe->nhqk", query, keyed) * factor
    score_peak = jnp.max(scores, axis=-1, keepdims=True)
    exponent = jnp.exp(scores - score_peak)
    probs = exponent / jnp.sum(exponent, axis=-1, keepdims=True)
    probs_b = probs.astype(BF16)
    context_b = (
        einsum("nhqk,nkhe->nqhe", probs_b, valued).astype(BF16).reshape(own, seq_len, width)
    )
    hidden_one = inputs + einsum("nsc,dc->nsd", context_b, attn[3])
    normed_two, unit_two, inverse_two = normalize(hidden_one, scales[1], biases[1])
    normed_two_b = normed_two.astype(BF16)
    logits = einsum("nsd,de->nse", normed_two_b, phi_full)
    dispatch = jax.nn.softmax(logits, axis=1)
    dispatch_b = dispatch.astype(BF16)
    combine = jax.nn.softmax(logits, axis=2)
    combine_b = combine.astype(BF16)
    slot_in = to_experts(einsum("nse,nsd->ned", dispatch_b, normed_two_b).astype(BF16))
    share = 1 if e_own else 0

    def meet(partial_sum):
        return lax.psum_scatter(partial_sum, "shard", scatter_dimension=share, tiled=True)

    def spread(values):
        return lax.all_gather(values, "shard", axis=share, tiled=True)

    pre = meet(einsum("ned,def->nef", slot_in, experts[:, 0]))
    if e_own:
        pre = pre + lax.dynamic_slice_in_dim(in_local, shard_index * e_own, e_own, 0)
    else:
        pre = pre + in_local
    gelu_value, gelu_back = jax.vjp(partial(jax.nn.gelu, approximate=False), pre)
    activated = spread(gelu_value.astype(BF16))
    slot_out_part = einsum("nef,def->ned", activated, experts[:, 1])
    slot_out_part = slot_out_part + jnp.where(tensor_index == 0, out_rows, 0.0)
    slot_out = to_images(slot_out_part).astype(BF16)
    output = (hidden_one + einsum("nse,ned->nsd", combine_b, slot_out)).astype(BF16)
    output = lax.all_gather(output, "heads", axis=0, tiled=True)
    grad_combine = einsum("nsd,ned->nse", cotangent, slot_out)
    grad_slot = to_experts(einsum("nse,nsd->ned", combine_b, cotangent).astype(BF16))
    grad_act = meet(einsum("ned,def->nef", grad_slot, experts[:, 1]))
    grad_pre = spread(gelu_back(grad_act)[0].astype(BF16))
    grad_slot_in = einsum("nef,def->ned", grad_pre, experts[:, 0]).astype(BF16)
    input_term = einsum("ned,nef->def", slot_in, grad_pre)
    output_term = einsum("ned,nef->def", grad_slot, activated)
    experts_grad = jnp.stack((input_term, output_term), axis=1)
    grad_slot_in = to_images(grad_slot_in.astype(F32)).astype(BF16)
    in_bias_grad = lax.dynamic_slice_in_dim(
        lax.all_gather(jnp.sum(grad_pre.astype(F32), axis=0), "tensor", axis=1, tiled=True),
        (shard_index * lax.axis_size("tensor") + tensor_index) * in_bias.shape[1],
        in_bias.shape[1],
        1,
    )
    out_bias_grad = lax.dynamic_slice_in_dim(
        jnp.sum(grad_slot.astype(F32), axis=0),
        tensor_index * out_bias.shape[1],
        out_bias.shape[1],
        1,
    )
    grad_dispatch = einsum("nsd,ned->nse", normed_two_b, grad_slot_in)
    grad_logits = (
        dispatch * (grad_dispatch - jnp.sum(dispatch * grad_dispatch, axis=1, keepdims=True))
        + combine * (grad_combine - jnp.sum(combine * grad_combine, axis=2, keepdims=True))
    ).astype(BF16)
    phi_grad = einsum("nsd,nse->de", normed_two_b, grad_logits)
    grad_normed_two = einsum("nse,ned->nsd", dispatch_b, grad_slot_in) + einsum(
        "nse,de->nsd", grad_logits, phi_full
    )
    grad_hidden_norm, scale_two_grad, bias_two_grad = normalize_back(
        grad_normed_two, unit_two, inverse_two, scales[1]
    )
    grad_hidden = cotangent.astype(F32) + grad_hidden_norm
    grad_hidden_b = grad_hidden.astype(BF16)
    out_weight_grad = einsum("nsd,nsc->dc", grad_hidden_b, context_b)
    grad_context = einsum("nsd,dc->nsc", grad_hidden_b, attn[3]).astype(BF16)
    grad_context = grad_context.reshape(own, seq_len, n_heads, HEAD_DIM)
    grad_value = einsum("nhqk,nqhe->nkhe", probs_b, grad_context).astype(BF16)
    grad_probs = einsum("nqhe,nkhe->nhqk", grad_context, valued)
    grad_scores = (
        probs * (grad_probs - jnp.sum(probs * grad_probs, axis=-1, keepdims=True))
    ).astype(BF16)
    grad_query = (einsum("nhqk,nkhe->nqhe", grad_scores, keyed) * factor).astype(BF16)
    grad_key = (einsum("nhqk,nqhe->nkhe", grad_scores, query) * factor).astype(BF16)
    grad_proj = jnp.stack((grad_query, grad_key, grad_value)).reshape(3, own, seq_len, width)
    proj_grad = einsum("nsd,knsc->kdc", normed_one_b, grad_proj)
    grad_normed_one = einsum("knsc,kdc->nsd", grad_proj, attn[:3])
    grad_input_norm, scale_one_grad, bias_one_grad = normalize_back(
        grad_normed_one, unit_one, inverse_one, scales[0]
    )
    input_grad = (grad_hidden + grad_input_norm).astype(BF16)
    input_grad = lax.all_gather(input_grad, "heads", axis=0, tiled=True)
    attn_grad = jnp.concatenate((proj_grad, out_weight_grad[None]), axis=0)
    attn_grad = lax.psum_scatter(attn_grad, ROWS, scatter_dimension=1, tiled=True)
    attn_grad = lax.psum_scatter(attn_grad, "heads", scatter_dimension=2, tiled=True)
    phi_grad = lax.psum_scatter(phi_grad, ROWS, scatter_dimension=0, tiled=True)
    phi_grad = lax.psum_scatter(phi_grad, "heads", scatter_dimension=1, tiled=True)
    norms = jnp.stack((scale_one_grad, scale_two_grad, bias_one_grad, bias_two_grad))
    norms = lax.psum(lax.psum_scatter(norms, ROWS, scatter_dimension=1, tiled=True), "heads")
    return (
        output,
        input_grad,
        norms[:2],
        norms[2:],
        attn_grad,
        phi_grad,
        experts_grad,
        in_bias_grad,
        out_bias_grad,
    )


def solution(mesh):
    images = P(ROWS, None, None)
    return jax.shard_map(
        shards,
        mesh=mesh,
        in_specs=(
            images,
            P(None, ROWS),
            P(None, ROWS),
            P(None, ROWS, "heads"),
            P(ROWS, "heads"),
            P("shard", None, "heads", "tensor"),
            P("heads", ROWS),
            P("heads", ROWS),
            images,
        ),
        out_specs=(
            images,
            images,
            P(None, ROWS),
            P(None, ROWS),
            P(None, ROWS, "heads"),
            P(ROWS, "heads"),
            P("shard", None, "heads", "tensor"),
            P("heads", ROWS),
            P("heads", ROWS),
        ),
        check_vma=False,
    )
```

```python
from functools import partial

import jax
import jax.numpy as jnp
from jax import lax
from jax.experimental import pallas as pl
from jax.experimental.pallas import tpu as pltpu
from jax.sharding import PartitionSpec as P

HEAD_DIM = 64
F32 = jnp.float32
BF16 = jnp.bfloat16
ROWS = ("shard", "tensor")
MESH = pl.DeviceIdType.MESH
VMEM_BYTES = 58 * 1024 * 1024
epsilon = 1e-06
einsum = partial(jnp.einsum, preferred_element_type=F32)


def dot(a, b):
    return lax.dot_general(a, b, (((1,), (0,)), ((), ())), preferred_element_type=F32)


def dot_t(a, b):
    return lax.dot_general(a, b, (((1,), (1,)), ((), ())), preferred_element_type=F32)


def swap_matrix(n):
    out = lax.broadcasted_iota(jnp.int32, (n * n, n * n), 0)
    row = lax.broadcasted_iota(jnp.int32, (n * n, n * n), 1)
    return ((out // n == row % n) & (out % n == row // n)).astype(F32).astype(BF16)


class Peers:
    def __init__(self, sizes):
        self.sizes = sizes
        self.at = tuple(lax.axis_index(name) for name in ("shard", "heads", "tensor"))
        self.count = sizes[0] * sizes[1] * sizes[2]

    def flat(self, place):
        return (place[0] * self.sizes[1] + place[1]) * self.sizes[2] + place[2]

    def step(self, k, sign):
        _, n_h, n_t = self.sizes
        steps = (k // (n_h * n_t), (k // n_t) % n_h, k % n_t)
        return tuple(
            lax.rem(at + n + sign * d, n) for at, n, d in zip(self.at, self.sizes, steps)
        )

    def greet_all(self):
        barrier = pltpu.get_barrier_semaphore()

        def signal(k, carry):
            pl.semaphore_signal(barrier, inc=1, device_id=self.step(k, 1), device_id_type=MESH)
            return carry

        lax.fori_loop(1, self.count, signal, 0)
        pl.semaphore_wait(barrier, self.count - 1)


def remote(src, dst, send, recv, place):
    return pltpu.make_async_remote_copy(
        src_ref=src, dst_ref=dst, send_sem=send, recv_sem=recv, device_id=place, device_id_type=MESH
    )


def expert_kernel(sizes, backward, *refs):
    if backward:
        (blocks, weights, gate, output, slots_out, act_out, back_out, bias_out, gathered,
         w_a, w_b, gate_v, sums, slots, act, core_out, core_in, x_out, x_in, land, leave, back, land_back,
         w_sem, o_sem, in_sems, back_sems, core_sems, x_sems, act_sems, g_sems, b_sems,
         bias_all, bias_send, bias_land) = refs
    else:
        (blocks, weights, gate, slots_out, act_out, gate_out, back_out,
         w_a, w_b, sums, slots, act, core_out, core_in, x_out, x_in, land, leave, back, land_back,
         w_sem, o_sem, in_sems, back_sems, core_sems, x_sems, act_sems) = refs
    peers = Peers(sizes)
    s, h, t = peers.at
    n_s, n_h, n_t = sizes
    me = peers.flat(peers.at)
    core, chip = lax.rem(s, 2), s // 2
    sibling = (s + 1 - 2 * core, h, t)
    across = (lax.rem(s + 2, n_s), h, t)
    half = act.shape[0] // 2
    own, other = core * half, (1 - core) * half
    n_blocks = peers.count
    first = 1 if backward else 0
    loads = [
        pltpu.make_async_copy(weights.at[first], w_a, w_sem.at[0]),
        pltpu.make_async_copy(weights.at[1 - first], w_b, w_sem.at[1]),
    ]
    for load in loads:
        load.start()
    if backward:
        gate_load = pltpu.make_async_copy(gate, gate_v, o_sem.at[0])
        gate_load.start()
    peers.greet_all()

    def block_out(k):
        place = peers.step(k, 1)
        return remote(
            blocks.at[place[1], place[0]], land.at[me], in_sems.at[0, k], in_sems.at[1, k], place
        )

    def block_in(k):
        source = peers.flat(peers.step(k, -1))
        return remote(
            blocks.at[0, 0], land.at[source], in_sems.at[0, k], in_sems.at[1, k], sibling
        )

    def each(function, count=n_blocks, start=1):
        lax.fori_loop(start, count, lambda k, carry: (function(k), carry)[1], 0)

    each(lambda k: block_out(k).start())
    land[me] = blocks[h, s]
    swap = swap_matrix(16)
    each(lambda k: block_in(k).wait_recv())
    group = 8
    for b in range(n_blocks // group):
        rows = land[b * group : (b + 1) * group].reshape(group * 32, land.shape[2])
        turned = dot(swap, rows).astype(BF16)
        slots[:, b * 16 : (b + 1) * 16, :] = turned.reshape(16, 16, land.shape[2])
    if backward:
        g_copies = []
        own_rows = output.shape[0]
        mine = gathered.at[pl.ds(h * own_rows, own_rows)]
        for d in range(1, n_h):
            g_copies.append(
                remote(output, mine, g_sems.at[0, d], g_sems.at[1, d], (s, lax.rem(h + d, n_h), t))
            )
        for copy in g_copies:
            copy.start()
        g_own = pltpu.make_async_copy(output, mine, g_sems.at[0, 0])
        g_own.start()
    loads[0].wait()

    def core_copy(j):
        return remote(
            core_out.at[j], core_in.at[j], core_sems.at[0, j], core_sems.at[1, j], sibling
        )

    def x_copy(j):
        return remote(x_out.at[j], x_in.at[j], x_sems.at[0, j], x_sems.at[1, j], across)

    def act_copy(j):
        return remote(
            act.at[own + j], act.at[own + j], act_sems.at[0, j], act_sems.at[1, j], sibling
        )

    def act_in(j):
        return remote(
            act.at[other + j], act.at[other + j], act_sems.at[0, j], act_sems.at[1, j], sibling
        )

    def meet(j):
        core_copy(j).wait_recv()
        sums[j] = sums[j] + core_in[j].astype(F32)
        x_out[j] = sums[j].astype(BF16)
        x_copy(j).start()

    def first_sums(j):
        core_out[j] = dot(slots[other + j], w_a[other + j]).astype(BF16)
        core_copy(j).start()
        sums[j] = dot(slots[own + j], w_a[own + j])

        @pl.when(j > 0)
        def _():
            meet(j - 1)

    each(first_sums, half, 0)
    meet(half - 1)
    loads[1].wait()
    if backward:
        gate_load.wait()

    def second(e):
        leave[e] = dot_t(act[e], w_b[e]).astype(BF16)

    def finish(j):
        x_copy(j).wait_recv()
        value = sums[j] + x_in[j].astype(F32)
        if backward:
            act[own + j] = (value * gate_v[j]).astype(BF16)
        else:
            value = value + gate[own + j]
            cumulative = 0.5 + 0.5 * lax.erf(value * 0.7071067811865476)
            act[own + j] = (value * cumulative).astype(BF16)
            sums[j] = cumulative + value * (
                jnp.exp(value * value * -0.5) * 0.3989422804014327
            )
        act_copy(j).start()
        second(own + j)

        @pl.when(j > 0)
        def _():
            act_in(j - 1).wait_recv()
            second(other + j - 1)

    each(finish, half, 0)
    act_in(half - 1).wait_recv()
    second(other + half - 1)

    for b in range(n_blocks // group):
        rows = leave[:, b * 16 : (b + 1) * 16, :].reshape(group * 32, leave.shape[2])
        turned = dot(swap, rows).astype(BF16)
        back[b * group : (b + 1) * group] = turned.reshape(group, 32, leave.shape[2])

    def back_copy(k):
        place = peers.step(k, 1)
        return remote(
            back.at[peers.flat(place)], land_back.at[me], back_sems.at[0, k], back_sems.at[1, k],
            place,
        )

    def back_in(k):
        source = peers.flat(peers.step(k, -1))
        return remote(
            back.at[0], land_back.at[source], back_sems.at[0, k], back_sems.at[1, k], sibling
        )

    each(lambda k: back_copy(k).start())
    land_back[me] = back[me]
    stores = [pltpu.make_async_copy(act, act_out, o_sem.at[1])]
    if not backward:
        stores.append(pltpu.make_async_copy(sums, gate_out, o_sem.at[0]))
    for store in stores:
        store.start()
    slots_out[...] = slots[...]
    if backward:
        across_t = (s, h, 1 - t)
        width = bias_out.shape[1]

        def bias_row(e):
            bias_all[pl.ds(e, 1), :] = jnp.sum(act[e].astype(F32), axis=0, keepdims=True)

        each(bias_row, 2 * half, 0)

        def piece(for_t):
            return bias_all[:, pl.ds(pl.multiple_of((core * n_t + for_t) * width, 128), width)]

        bias_send[...] = piece(1 - t)
        bias_copy = remote(bias_send, bias_land, b_sems.at[0], b_sems.at[1], across_t)
        bias_copy.start()
        bias_copy.wait()
        bias_out[...] = jnp.where(t == chip, piece(t), bias_land[...])
    each(lambda k: back_in(k).wait_recv())
    back_out[...] = land_back[...]
    for store in stores:
        store.wait()
    if backward:
        for copy in g_copies:
            copy.wait()
        g_own.wait()
    each(lambda k: block_out(k).wait_send())
    each(lambda k: back_copy(k).wait_send())
    for copy in (core_copy, x_copy, act_copy):
        each(lambda j: copy(j).wait_send(), half, 0)


def expert_pass(sizes, backward, blocks, weights, gate, output=None, bias_width=0):
    _, experts, rows, hidden = weights.shape
    devices = sizes[0] * sizes[1] * sizes[2]
    images = 2 * devices
    half = experts // 2
    vmem = pl.BlockSpec(memory_space=pltpu.VMEM)
    hbm = pl.BlockSpec(memory_space=pl.ANY)
    slots = jax.ShapeDtypeStruct((experts, images, rows), BF16)
    act = jax.ShapeDtypeStruct((experts, images, hidden), BF16)
    gate_shape = (half, images, hidden)
    returned = jax.ShapeDtypeStruct((devices, 2 * experts, rows), BF16)
    if backward:
        operands, in_specs = (blocks, weights, gate, output), [vmem, hbm, hbm, hbm]
        gathered = (sizes[1] * output.shape[0], *output.shape[1:])
        outs = (
            slots, act, returned, jax.ShapeDtypeStruct((experts, bias_width), F32),
            jax.ShapeDtypeStruct(gathered, BF16),
        )
        out_specs = (vmem, hbm, vmem, vmem, hbm)
    else:
        operands, in_specs = (blocks, weights, gate), [vmem, hbm, vmem]
        outs = (slots, act, jax.ShapeDtypeStruct(gate_shape, F32), returned)
        out_specs = (vmem, hbm, hbm, vmem)
    weight = pltpu.VMEM((experts, rows, hidden), BF16)
    chunk = pltpu.VMEM((half, images, hidden), BF16)
    block = pltpu.VMEM((devices, 2 * experts, rows), BF16)
    dma = pltpu.SemaphoreType.DMA
    scratch = [weight, weight]
    if backward:
        scratch.append(pltpu.VMEM(gate_shape, F32))
    scratch += [
        pltpu.VMEM(gate_shape, F32),
        pltpu.VMEM(slots.shape, BF16),
        pltpu.VMEM(act.shape, BF16),
        chunk, chunk, chunk, chunk, block,
        pltpu.VMEM(slots.shape, BF16),
        block, block,
        dma((2,)), dma((2,)), dma((2, devices)), dma((2, devices)),
        dma((2, half)), dma((2, half)), dma((2, half)),
    ]
    if backward:
        scratch += [
            dma((2, sizes[1])), dma((2,)),
            pltpu.VMEM((experts, hidden), F32),
            pltpu.VMEM((experts, bias_width), F32),
            pltpu.VMEM((experts, bias_width), F32),
        ]
    return pl.pallas_call(
        partial(expert_kernel, sizes, backward),
        out_shape=outs,
        in_specs=in_specs,
        out_specs=out_specs,
        scratch_shapes=scratch,
        compiler_params=pltpu.CompilerParams(
            collective_id=2 if backward else 1, has_side_effects=True, vmem_limit_bytes=VMEM_BYTES
        ),
        cost_estimate=pl.CostEstimate(
            flops=8 * images * experts * rows * hidden,
            bytes_accessed=weights.size * 2,
            transcendentals=0,
        ),
        name="experts_back" if backward else "experts_ahead",
    )(*operands)


def weight_grad_kernel(slots_0, act_0, slots_1, act_1, out):
    group = out.shape[2]
    d_block = out.shape[0]
    images, rows = slots_0.shape[1:]
    g, first = pl.program_id(1), pl.program_id(2) * d_block
    n = group * d_block
    row = lax.broadcasted_iota(jnp.int32, (n, rows), 0)
    column = lax.broadcasted_iota(jnp.int32, (n, rows), 1)
    pick = (column == first + row // group).astype(F32).astype(BF16)
    row = lax.broadcasted_iota(jnp.int32, (n, group * images), 0)
    column = lax.broadcasted_iota(jnp.int32, (n, group * images), 1)
    same = row % group == column // images

    def term(slots, act):
        lines = slots[pl.ds(g * group, group)].reshape(group * images, rows)
        spread = jnp.where(same, dot_t(pick, lines), 0.0).astype(BF16)
        values = act[pl.ds(g * group, group)].reshape(group * images, act.shape[2])
        out[...] = dot(spread, values).reshape(out.shape)

    @pl.when(pl.program_id(0) == 0)
    def _():
        term(slots_0, act_0)

    @pl.when(pl.program_id(0) == 1)
    def _():
        term(slots_1, act_1)


def weight_grads(slots_0, act_0, slots_1, act_1):
    experts, images, rows = slots_0.shape
    hidden = act_0.shape[2]
    group, d_block = 8, 32
    vmem = pl.BlockSpec(memory_space=pltpu.VMEM)
    return pl.pallas_call(
        weight_grad_kernel,
        grid=(2, experts // group, rows // d_block),
        out_shape=jax.ShapeDtypeStruct((rows, 2, experts, hidden), F32),
        in_specs=[vmem] * 4,
        out_specs=pl.BlockSpec((d_block, 1, group, hidden), lambda m, g, d: (d, m, g, 0)),
        compiler_params=pltpu.CompilerParams(vmem_limit_bytes=VMEM_BYTES),
        cost_estimate=pl.CostEstimate(
            flops=4 * images * experts * rows * hidden,
            bytes_accessed=8 * rows * experts * hidden,
            transcendentals=0,
        ),
        name="weight_grads",
    )(slots_0, act_0, slots_1, act_1)


def normalize(values, scale, shift):
    centered = values - jnp.mean(values, axis=-1, keepdims=True)
    variance = jnp.mean(centered * centered, axis=-1, keepdims=True)
    inverse = lax.rsqrt(variance + epsilon)
    unit_part = centered * inverse
    return (unit_part * scale + shift, unit_part, inverse)


def normalize_back(grad_output, unit_part, inverse, scale):
    scaled = grad_output * scale
    average = jnp.mean(scaled, axis=-1, keepdims=True)
    projection = jnp.mean(scaled * unit_part, axis=-1, keepdims=True)
    grad_input = inverse * (scaled - average - unit_part * projection)
    return (
        grad_input,
        jnp.sum(grad_output * unit_part, axis=(0, 1)),
        jnp.sum(grad_output, axis=(0, 1)),
    )


def to_experts(slots):
    slots = lax.all_to_all(slots, "heads", split_axis=1, concat_axis=0, tiled=True)
    slots = lax.all_to_all(slots, "shard", split_axis=2, concat_axis=0, tiled=True)
    return lax.all_gather(slots, "tensor", axis=0, tiled=True)


def to_blocks(slots, sizes):
    own, experts, width = slots.shape
    n_s, n_h, _ = sizes
    slots = slots.reshape(own, n_h, experts // n_h, n_s, width // n_s)
    return slots.transpose(1, 3, 0, 2, 4).reshape(n_h, n_s, own * experts // n_h, width // n_s)


def from_blocks(blocks, sizes):
    n_s, n_h, n_t = sizes
    rows = blocks.shape[2]
    blocks = jnp.sum(blocks.reshape(n_s, n_h, n_t, 2, -1, rows).astype(F32), axis=2)
    return blocks.transpose(2, 1, 3, 0, 4).reshape(2, -1, n_s * rows)


def to_images(slots):
    slots = lax.psum_scatter(slots, "tensor", scatter_dimension=0, tiled=True)
    slots = lax.all_to_all(slots, "shard", split_axis=0, concat_axis=2, tiled=True)
    return lax.all_to_all(slots, "heads", split_axis=0, concat_axis=1, tiled=True)


def shards(tokens, norm_scales, norm_biases, w_attn, phi, experts, in_bias, out_bias, cotangent):
    heads_n = lax.axis_size("heads")
    sizes = tuple(lax.axis_size(name) for name in ("shard", "heads", "tensor"))
    if sizes != (4, 4, 2) or tokens.shape[0] != 8 or experts.shape[2] != 16:
        sizes = None
    group, seq_len, width = tokens.shape
    own = group // heads_n
    heads_index = lax.axis_index("heads")
    tensor_index = lax.axis_index("tensor")
    shard_index = lax.axis_index("shard")
    hidden = experts.shape[3]
    rows = experts.shape[0]
    scales, biases, in_full = (
        lax.all_gather(norm_scales, ROWS, axis=1, tiled=True).astype(F32),
        lax.all_gather(norm_biases, ROWS, axis=1, tiled=True).astype(F32),
        lax.all_gather(in_bias, ROWS, axis=1, tiled=True).astype(F32),
    )
    attn = lax.all_gather(
        lax.all_gather(w_attn, "heads", axis=2, tiled=True), ROWS, axis=1, tiled=True
    )
    phi_full = lax.all_gather(
        lax.all_gather(phi, "heads", axis=1, tiled=True), ROWS, axis=0, tiled=True
    )
    out_rows = lax.all_gather(out_bias, "tensor", axis=1, tiled=True).astype(F32)
    e_own = experts.shape[2] // lax.axis_size("shard")
    in_local = lax.dynamic_slice_in_dim(in_full, tensor_index * hidden, hidden, 1)
    factor = HEAD_DIM ** (-0.5)
    tokens = lax.dynamic_slice_in_dim(tokens, heads_index * own, own, 0)
    cotangent = lax.dynamic_slice_in_dim(cotangent, heads_index * own, own, 0)
    n_heads = width // HEAD_DIM
    inputs = tokens.astype(F32)
    normed_one, unit_one, inverse_one = normalize(inputs, scales[0], biases[0])
    normed_one_b = normed_one.astype(BF16)
    projected = einsum("nsd,kdc->knsc", normed_one_b, attn[:3]).astype(BF16)
    query, keyed, valued = projected.reshape(3, own, seq_len, n_heads, HEAD_DIM)
    scores = einsum("nqhe,nkhe->nhqk", query, keyed) * factor
    score_peak = jnp.max(scores, axis=-1, keepdims=True)
    exponent = jnp.exp(scores - score_peak)
    probs = exponent / jnp.sum(exponent, axis=-1, keepdims=True)
    probs_b = probs.astype(BF16)
    context_b = (
        einsum("nhqk,nkhe->nqhe", probs_b, valued).astype(BF16).reshape(own, seq_len, width)
    )
    hidden_one = inputs + einsum("nsc,dc->nsd", context_b, attn[3])
    normed_two, unit_two, inverse_two = normalize(hidden_one, scales[1], biases[1])
    normed_two_b = normed_two.astype(BF16)
    logits = einsum("nsd,de->nse", normed_two_b, phi_full)
    dispatch = jax.nn.softmax(logits, axis=1)
    dispatch_b = dispatch.astype(BF16)
    combine = jax.nn.softmax(logits, axis=2)
    combine_b = combine.astype(BF16)
    slot_in = einsum("nse,nsd->ned", dispatch_b, normed_two_b).astype(BF16)
    if sizes is not None:
        turned = jnp.transpose(experts, (1, 2, 0, 3))
        slot_in, activated, gate, back = expert_pass(
            sizes, False, to_blocks(slot_in, sizes), turned, in_local[:, None, :]
        )
        out_all = lax.all_gather(
            lax.all_gather(out_bias, "heads", axis=0, tiled=True), ROWS, axis=1, tiled=True
        )
        slot_out = (from_blocks(back, sizes) + out_all.astype(F32)).astype(BF16)
    else:
        slot_in = to_experts(slot_in)
        share = 1 if e_own else 0

        def meet(partial_sum):
            return lax.psum_scatter(partial_sum, "shard", scatter_dimension=share, tiled=True)

        def spread(values):
            return lax.all_gather(values, "shard", axis=share, tiled=True)

        pre = meet(einsum("ned,def->nef", slot_in, experts[:, 0]))
        if e_own:
            pre = pre + lax.dynamic_slice_in_dim(in_local, shard_index * e_own, e_own, 0)
        else:
            pre = pre + in_local
        gelu_value, gelu_back = jax.vjp(partial(jax.nn.gelu, approximate=False), pre)
        activated = spread(gelu_value.astype(BF16))
        slot_out_part = einsum("nef,def->ned", activated, experts[:, 1])
        slot_out_part = slot_out_part + jnp.where(tensor_index == 0, out_rows, 0.0)
        slot_out = to_images(slot_out_part).astype(BF16)
    output = (hidden_one + einsum("nse,ned->nsd", combine_b, slot_out)).astype(BF16)
    grad_combine = einsum("nsd,ned->nse", cotangent, slot_out)
    grad_slot = einsum("nse,nsd->ned", combine_b, cotangent).astype(BF16)
    if sizes is not None:
        grad_slot, grad_pre, back, in_bias_grad, output = expert_pass(
            sizes, True, to_blocks(grad_slot, sizes), turned, gate, output, in_bias.shape[1]
        )
        grad_slot_in = from_blocks(back, sizes).astype(BF16)
        experts_grad = weight_grads(slot_in, grad_pre, grad_slot, activated)
        grad_slot_sum = jnp.sum(grad_slot.astype(F32), axis=1)
    else:
        output = lax.all_gather(output, "heads", axis=0, tiled=True)
        grad_slot = to_experts(grad_slot)
        grad_act = meet(einsum("ned,def->nef", grad_slot, experts[:, 1]))
        grad_pre = spread(gelu_back(grad_act)[0].astype(BF16))
        grad_slot_in = einsum("nef,def->ned", grad_pre, experts[:, 0]).astype(BF16)
        input_term = einsum("ned,nef->def", slot_in, grad_pre)
        output_term = einsum("ned,nef->def", grad_slot, activated)
        experts_grad = jnp.stack((input_term, output_term), axis=1)
        grad_slot_in = to_images(grad_slot_in.astype(F32)).astype(BF16)
        in_bias_grad = lax.dynamic_slice_in_dim(
            lax.all_gather(jnp.sum(grad_pre.astype(F32), axis=0), "tensor", axis=1, tiled=True),
            (shard_index * lax.axis_size("tensor") + tensor_index) * in_bias.shape[1],
            in_bias.shape[1],
            1,
        )
        grad_slot_sum = jnp.sum(grad_slot.astype(F32), axis=0)
    out_bias_grad = lax.dynamic_slice_in_dim(
        grad_slot_sum,
        tensor_index * out_bias.shape[1],
        out_bias.shape[1],
        1,
    )
    grad_dispatch = einsum("nsd,ned->nse", normed_two_b, grad_slot_in)
    grad_logits = (
        dispatch * (grad_dispatch - jnp.sum(dispatch * grad_dispatch, axis=1, keepdims=True))
        + combine * (grad_combine - jnp.sum(combine * grad_combine, axis=2, keepdims=True))
    ).astype(BF16)
    phi_grad = einsum("nsd,nse->de", normed_two_b, grad_logits)
    grad_normed_two = einsum("nse,ned->nsd", dispatch_b, grad_slot_in) + einsum(
        "nse,de->nsd", grad_logits, phi_full
    )
    grad_hidden_norm, scale_two_grad, bias_two_grad = normalize_back(
        grad_normed_two, unit_two, inverse_two, scales[1]
    )
    grad_hidden = cotangent.astype(F32) + grad_hidden_norm
    grad_hidden_b = grad_hidden.astype(BF16)
    out_weight_grad = einsum("nsd,nsc->dc", grad_hidden_b, context_b)
    grad_context = einsum("nsd,dc->nsc", grad_hidden_b, attn[3]).astype(BF16)
    grad_context = grad_context.reshape(own, seq_len, n_heads, HEAD_DIM)
    grad_value = einsum("nhqk,nqhe->nkhe", probs_b, grad_context).astype(BF16)
    grad_probs = einsum("nqhe,nkhe->nhqk", grad_context, valued)
    grad_scores = (
        probs * (grad_probs - jnp.sum(probs * grad_probs, axis=-1, keepdims=True))
    ).astype(BF16)
    grad_query = (einsum("nhqk,nkhe->nqhe", grad_scores, keyed) * factor).astype(BF16)
    grad_key = (einsum("nhqk,nqhe->nkhe", grad_scores, query) * factor).astype(BF16)
    grad_proj = jnp.stack((grad_query, grad_key, grad_value)).reshape(3, own, seq_len, width)
    proj_grad = einsum("nsd,knsc->kdc", normed_one_b, grad_proj)
    grad_normed_one = einsum("knsc,kdc->nsd", grad_proj, attn[:3])
    grad_input_norm, scale_one_grad, bias_one_grad = normalize_back(
        grad_normed_one, unit_one, inverse_one, scales[0]
    )
    input_grad = (grad_hidden + grad_input_norm).astype(BF16)
    input_grad = lax.all_gather(input_grad, "heads", axis=0, tiled=True)
    attn_grad = jnp.concatenate((proj_grad, out_weight_grad[None]), axis=0)
    attn_grad = lax.psum_scatter(attn_grad, ROWS, scatter_dimension=1, tiled=True)
    attn_grad = lax.psum_scatter(attn_grad, "heads", scatter_dimension=2, tiled=True)
    phi_grad = lax.psum_scatter(phi_grad, ROWS, scatter_dimension=0, tiled=True)
    phi_grad = lax.psum_scatter(phi_grad, "heads", scatter_dimension=1, tiled=True)
    norms = jnp.stack((scale_one_grad, scale_two_grad, bias_one_grad, bias_two_grad))
    norms = lax.psum(lax.psum_scatter(norms, ROWS, scatter_dimension=1, tiled=True), "heads")
    return (
        output,
        input_grad,
        norms[:2],
        norms[2:],
        attn_grad,
        phi_grad,
        experts_grad,
        in_bias_grad,
        out_bias_grad,
    )


def solution(mesh):
    images = P(ROWS, None, None)
    return jax.shard_map(
        shards,
        mesh=mesh,
        in_specs=(
            images,
            P(None, ROWS),
            P(None, ROWS),
            P(None, ROWS, "heads"),
            P(ROWS, "heads"),
            P("shard", None, "heads", "tensor"),
            P("heads", ROWS),
            P("heads", ROWS),
            images,
        ),
        out_specs=(
            images,
            images,
            P(None, ROWS),
            P(None, ROWS),
            P(None, ROWS, "heads"),
            P(ROWS, "heads"),
            P("shard", None, "heads", "tensor"),
            P("heads", ROWS),
            P("heads", ROWS),
        ),
        check_vma=False,
    )
```

```python
from functools import partial

import jax
import jax.numpy as jnp
from jax import lax
from jax.experimental import pallas as pl
from jax.experimental.pallas import tpu as pltpu
from jax.sharding import PartitionSpec as P

HEAD_DIM = 64
F32 = jnp.float32
BF16 = jnp.bfloat16
ROWS = ("shard", "tensor")
MESH = pl.DeviceIdType.MESH
VMEM_BYTES = 58 * 1024 * 1024
epsilon = 1e-06
einsum = partial(jnp.einsum, preferred_element_type=F32)


def dot(a, b):
    return lax.dot_general(a, b, (((1,), (0,)), ((), ())), preferred_element_type=F32)


def dot_t(a, b):
    return lax.dot_general(a, b, (((1,), (1,)), ((), ())), preferred_element_type=F32)


def swap_matrix(n):
    out = lax.broadcasted_iota(jnp.int32, (n * n, n * n), 0)
    row = lax.broadcasted_iota(jnp.int32, (n * n, n * n), 1)
    return ((out // n == row % n) & (out % n == row // n)).astype(F32).astype(BF16)


class Peers:
    def __init__(self, sizes):
        self.sizes = sizes
        self.at = tuple(lax.axis_index(name) for name in ("shard", "heads", "tensor"))
        self.count = sizes[0] * sizes[1] * sizes[2]

    def flat(self, place):
        return (place[0] * self.sizes[1] + place[1]) * self.sizes[2] + place[2]

    def step(self, k, sign):
        _, n_h, n_t = self.sizes
        steps = (k // (n_h * n_t), (k // n_t) % n_h, k % n_t)
        return tuple(
            lax.rem(at + n + sign * d, n) for at, n, d in zip(self.at, self.sizes, steps)
        )

    def greet_all(self):
        barrier = pltpu.get_barrier_semaphore()

        def signal(k, carry):
            pl.semaphore_signal(barrier, inc=1, device_id=self.step(k, 1), device_id_type=MESH)
            return carry

        lax.fori_loop(1, self.count, signal, 0)
        pl.semaphore_wait(barrier, self.count - 1)


def remote(src, dst, send, recv, place):
    return pltpu.make_async_remote_copy(
        src_ref=src, dst_ref=dst, send_sem=send, recv_sem=recv, device_id=place, device_id_type=MESH
    )


def plane(sizes):
    n_s, n_h, n_t = sizes
    s, h, t = (lax.axis_index(name) for name in ("shard", "heads", "tensor"))
    core, chip = lax.rem(s, 2), s // 2
    sibling = (s + 1 - 2 * core, h, t)
    across_x = (lax.rem(s + 2, n_s), h, t)
    across_y = (s, h, 1 - t)
    line = [(s, lax.rem(h + d, n_h), t) for d in range(n_h)]
    barrier = pltpu.get_barrier_semaphore()
    others = [sibling, across_x, across_y] + line[1:]
    for place in others:
        pl.semaphore_signal(barrier, inc=1, device_id=place, device_id_type=MESH)
    pl.semaphore_wait(barrier, len(others))
    return (s, h, t), core, chip, sibling, across_x, across_y, line


def gather_kernel(
    sizes, packet, extra, experts, w_out, small_out, turned,
    w, small, lined, tile_in, tile_out,
    z_sems, x_sems, y_sems, d_sems, c_sems, t_sems, o_sems,
):
    (s, h, t), core, chip, sibling, across_x, across_y, line = plane(sizes)
    n_k, rows, wide = packet.shape
    n_h, n_t = sizes[1], sizes[2]
    width = w.shape[2]
    side = 16
    n_tiles = experts.shape[0] // side

    def load(i):
        return pltpu.make_async_copy(
            experts.at[pl.ds((i % n_tiles) * side, side), i // n_tiles],
            tile_in.at[i % 2],
            t_sems.at[0, i % 2],
        )

    def store(i):
        return pltpu.make_async_copy(
            tile_out.at[i % 2],
            turned.at[i // n_tiles, :, pl.ds((i % n_tiles) * side, side)],
            t_sems.at[1, i % 2],
        )

    swap = swap_matrix(side)

    def turn(first, last):
        def step(i, carry):
            load(i).wait()

            @pl.when(i + 1 < 2 * n_tiles)
            def _():
                load(i + 1).start()

            @pl.when(i >= 2)
            def _():
                store(i - 2).wait()

            rows_in = tile_in[i % 2].reshape(side * side, tile_in.shape[3])
            tile_out[i % 2] = dot(swap, rows_in).astype(BF16).reshape(tile_out.shape[1:])
            store(i).start()
            return carry

        lax.fori_loop(first, last, step, 0)

    def z_copy(k, d):
        return remote(
            packet.at[k], lined.at[h, k], z_sems.at[0, k, d], z_sems.at[1, k, d], line[d]
        )

    def at(k, place):
        first = pl.multiple_of((place[0] * n_t + place[2]) * rows, 16)
        lines = pl.ds(first, rows)
        return small.at[lines] if k == n_k else w.at[k, lines]

    def hop(k, origin, place, sems, j):
        return remote(at(k, origin), at(k, origin), sems.at[0, j], sems.at[1, j], place)

    for k in range(n_k):
        for d in range(1, n_h):
            z_copy(k, d).start()
        lined[h, k] = packet[k]
    load(0).start()
    third = 2 * n_tiles // 3
    turn(0, third // 2)

    shape = (n_h * wide, width + small.shape[1])
    row = lax.broadcasted_iota(jnp.int32, shape, 0)
    column = lax.broadcasted_iota(jnp.int32, shape, 1)
    lane, of = row % wide, row // wide
    block = width // n_h
    slot = small.shape[1] // 16
    place = (lane < block) & (column == of * block + lane)
    place |= (lane >= block) & (lane < block + slot) & (column == width + of * slot + lane - block)
    place |= (
        (lane >= block + slot) & (lane < block + 2 * slot)
        & (column == width + 4 * slot + of * slot + lane - block - slot)
    )
    place = place.astype(F32).astype(BF16)

    me = (s, h, t)
    sent = []
    chunks = [0, 2, 1, 3]
    order = []
    for k in chunks:
        for d in range(1, n_h):
            z_copy(k, d).wait_recv()
        lines = jnp.concatenate([lined[i, k] for i in range(n_h)], axis=1)
        if k == 0:
            joined = dot(lines, place)
            at(0, me)[...] = joined[:, :width].astype(BF16)
            at(n_k, me)[...] = (joined[:, width:] + extra[...].astype(F32)).astype(BF16)
            ready = [0, n_k]
        else:
            at(k, me)[...] = dot(lines, place[:, :width]).astype(BF16)
            ready = [k]
        for q in ready:
            order.append(q)
            sent.append(hop(q, me, across_x, x_sems, q))
            sent.append(hop(q, me, across_y, y_sems, q))
            sent.append(hop(q, me, sibling, c_sems, 4 * q))
            for copy in sent[-3:]:
                copy.start()
    turn(third // 2, third)
    from_x = across_x
    from_y = across_y
    from_d = (across_x[0], h, across_y[2])
    x_first = {0: True, 1: True, 2: False, 3: False, n_k: False}
    for q in order:
        hop(q, from_x, across_x, x_sems, q).wait_recv()
        sent.append(hop(q, from_x, sibling, c_sems, 4 * q + 1))
        sent[-1].start()
        if x_first[q]:
            sent.append(hop(q, from_x, across_y, d_sems, q))
            sent[-1].start()
        hop(q, from_y, across_y, y_sems, q).wait_recv()
        sent.append(hop(q, from_y, sibling, c_sems, 4 * q + 2))
        sent[-1].start()
        if not x_first[q]:
            sent.append(hop(q, from_y, across_x, d_sems, q))
            sent[-1].start()
        turn(third + third * order.index(q) // len(order), third + third * (order.index(q) + 1) // len(order))
    for q in order:
        hop(q, from_d, across_x, d_sems, q).wait_recv()
        sent.append(hop(q, from_d, sibling, c_sems, 4 * q + 3))
        sent[-1].start()
    turn(2 * third, 2 * n_tiles)
    stores = []
    for q in order:
        for j in range(4):
            hop(q, me, sibling, c_sems, 4 * q + j).wait_recv()
        if q == n_k:
            stores.append(pltpu.make_async_copy(small, small_out, o_sems.at[q]))
        else:
            stores.append(pltpu.make_async_copy(w.at[q], w_out.at[q], o_sems.at[q]))
        stores[-1].start()
    for copy in sent:
        copy.wait_send()
    for k in range(n_k):
        for d in range(1, n_h):
            z_copy(k, d).wait_send()
    store(2 * n_tiles - 2).wait()
    store(2 * n_tiles - 1).wait()
    for copy in stores:
        copy.wait()


def gather_weights(sizes, packet, extra, experts):
    n_k, rows, wide = packet.shape
    n_s, n_h, n_t = sizes
    width = n_s * n_t * rows
    vmem = pl.BlockSpec(memory_space=pltpu.VMEM)
    hbm = pl.BlockSpec(memory_space=pl.ANY)
    dma = pltpu.SemaphoreType.DMA
    hidden = experts.shape[3]
    small = (width, extra.shape[1])
    return pl.pallas_call(
        partial(gather_kernel, sizes),
        out_shape=(
            jax.ShapeDtypeStruct((n_k, width, width), BF16),
            jax.ShapeDtypeStruct(small, BF16),
            jax.ShapeDtypeStruct((2, experts.shape[2], experts.shape[0], hidden), BF16),
        ),
        in_specs=[vmem, vmem, hbm],
        out_specs=(hbm, hbm, hbm),
        scratch_shapes=[
            pltpu.VMEM((n_k, width, width), BF16),
            pltpu.VMEM(small, BF16),
            pltpu.VMEM((n_h, n_k, rows, wide), BF16),
            pltpu.VMEM((2, 16, 16, hidden), BF16),
            pltpu.VMEM((2, 16, 16, hidden), BF16),
            dma((2, n_k, n_h)), dma((2, n_k + 1)), dma((2, n_k + 1)), dma((2, n_k + 1)),
            dma((2, 4 * (n_k + 1))), dma((2, 2)), dma((n_k + 1,)),
        ],
        compiler_params=pltpu.CompilerParams(
            collective_id=3, has_side_effects=True, vmem_limit_bytes=VMEM_BYTES
        ),
        name="gather_weights",
    )(packet, extra, experts)


def reduce_kernel(
    sizes, grads, small, out, core_in, core_small, met, met_small,
    d_in, d_small, x_in, x_small, y_in, y_small, pieces, z_in,
    c_sems, d_sems, x_sems, y_sems, z_sems,
):
    (s, h, t), core, chip, sibling, across_x, across_y, line = plane(sizes)
    n_k, width, _ = grads.shape
    n_s, n_h, n_t = sizes
    rows = width // (n_s * n_t)
    wide = pieces.shape[3]
    pair = n_t * rows
    order = (0, n_k, 2, 1, 3)

    def pick(q, large, little):
        return little if q == n_k else large.at[q]

    def core_copy(q, x):
        first = pl.multiple_of((2 * x + 1 - core) * pair, 16)
        return remote(
            pick(q, grads, small).at[pl.ds(first, pair)],
            pick(q, core_in, core_small).at[x],
            c_sems.at[0, 2 * q + x], c_sems.at[1, 2 * q + x], sibling,
        )

    for q in order:
        for x in range(2):
            core_copy(q, x).start()

    def hop(q, kind, source, sems, place):
        return remote(source, pick(q, *kind), sems.at[0, q], sems.at[1, q], place)

    sent = []
    x_first = {0: True, 1: True, 2: False, 3: False, n_k: False}
    to_d, to_x, to_y = (d_in, d_small), (x_in, x_small), (y_in, y_small)

    def send(copy):
        copy.start()
        sent.append(copy)

    for q in order:
        part = pick(q, met, met_small)
        for x in range(2):
            core_copy(q, x).wait_recv()
            first = pl.multiple_of((2 * x + core) * pair, 16)
            own = pick(q, grads, small)[pl.ds(first, pair)].astype(F32)
            total = own + pick(q, core_in, core_small)[x].astype(F32)
            part[x] = total.astype(BF16).reshape(n_t, rows, total.shape[1])
        diagonal = part.at[1 - chip, 1 - t]
        if x_first[q]:
            send(hop(q, to_d, diagonal, d_sems, across_x))
            send(hop(q, to_x, part.at[1 - chip, t], x_sems, across_x))
        else:
            send(hop(q, to_d, diagonal, d_sems, across_y))
            send(hop(q, to_y, part.at[chip, 1 - t], y_sems, across_y))
    for q in order:
        part = pick(q, met, met_small)
        hop(q, to_d, part.at[0, 0], d_sems, across_x).wait_recv()
        passing = pick(q, *to_d)[...].astype(F32)
        if x_first[q]:
            total = part[chip, 1 - t].astype(F32) + passing
            part[chip, 1 - t] = total.astype(BF16)
            send(hop(q, to_y, part.at[chip, 1 - t], y_sems, across_y))
        else:
            total = part[1 - chip, t].astype(F32) + passing
            part[1 - chip, t] = total.astype(BF16)
            send(hop(q, to_x, part.at[1 - chip, t], x_sems, across_x))

    block = width // n_h
    shape = (width, n_h * wide)
    row = lax.broadcasted_iota(jnp.int32, shape, 0)
    column = lax.broadcasted_iota(jnp.int32, shape, 1)
    lane, of = column % wide, column // wide
    split = ((lane < block) & (row == of * block + lane)).astype(F32).astype(BF16)
    shape = (small.shape[1], n_h * wide)
    row = lax.broadcasted_iota(jnp.int32, shape, 0)
    column = lax.broadcasted_iota(jnp.int32, shape, 1)
    lane, of = column % wide - block, column // wide
    beside = (lane >= 0) & (lane < 16) & (row == of * 16 + lane)
    beside |= (lane >= 16) & (lane < 20) & (row == n_h * 16 + lane - 16)
    beside = beside.astype(F32).astype(BF16)

    def whole(q):
        part = pick(q, met, met_small)
        hop(q, to_x, part.at[0, 0], x_sems, across_x).wait_recv()
        hop(q, to_y, part.at[0, 0], y_sems, across_y).wait_recv()
        total = part[chip, t].astype(F32) + pick(q, *to_x)[...].astype(F32)
        return (total + pick(q, *to_y)[...].astype(F32)).astype(BF16)

    def z_copy(k, d):
        return remote(
            pieces.at[line[d][1], k], z_in.at[h, k], z_sems.at[0, k, d], z_sems.at[1, k, d], line[d]
        )

    for k in (0, 2, 1, 3):
        value = dot(whole(k), split)
        if k == 0:
            value = value + dot(whole(n_k), beside)
        value = value.astype(BF16)
        for i in range(n_h):
            pieces[i, k] = value[:, i * wide : (i + 1) * wide]
        for d in range(1, n_h):
            z_copy(k, d).start()
    for k in (0, 2, 1, 3):
        total = pieces[h, k].astype(F32)
        for d in range(1, n_h):
            z_copy(k, d).wait_recv()
        for d in range(1, n_h):
            total = total + z_in[line[d][1], k].astype(F32)
        out[k] = total
    for q in order:
        for x in range(2):
            core_copy(q, x).wait_send()
    for copy in sent:
        copy.wait_send()
    for k in range(n_k):
        for d in range(1, n_h):
            z_copy(k, d).wait_send()


def reduce_grads(sizes, grads, small):
    n_k, width, _ = grads.shape
    n_s, n_h, n_t = sizes
    rows, wide, thin = width // (n_s * n_t), 256, small.shape[1]
    vmem = pl.BlockSpec(memory_space=pltpu.VMEM)
    dma = pltpu.SemaphoreType.DMA

    def buffers(*lead):
        return [
            pltpu.VMEM((n_k, *lead, width), BF16),
            pltpu.VMEM((*lead, thin), BF16),
        ]

    return pl.pallas_call(
        partial(reduce_kernel, sizes),
        out_shape=jax.ShapeDtypeStruct((n_k, rows, wide), F32),
        in_specs=[vmem, vmem],
        out_specs=vmem,
        scratch_shapes=[
            *buffers(2, n_t * rows), *buffers(2, n_t, rows),
            *buffers(rows), *buffers(rows), *buffers(rows),
            pltpu.VMEM((n_h, n_k, rows, wide), BF16),
            pltpu.VMEM((n_h, n_k, rows, wide), BF16),
            dma((2, 2 * (n_k + 1))), dma((2, n_k + 1)), dma((2, n_k + 1)), dma((2, n_k + 1)),
            dma((2, n_k, n_h)),
        ],
        compiler_params=pltpu.CompilerParams(
            collective_id=4, has_side_effects=True, vmem_limit_bytes=VMEM_BYTES
        ),
        name="reduce_grads",
    )(grads, small)


def expert_kernel(sizes, backward, *refs):
    if backward:
        (blocks, weights, gate, output, slots_out, act_out, back_out, bias_out, gathered,
         w_a, w_b, gate_v, sums, slots, act, core_out, core_in, x_out, x_in, land, leave, back, land_back,
         w_sem, o_sem, in_sems, back_sems, core_sems, x_sems, act_sems, g_sems, b_sems,
         bias_all, bias_send, bias_land) = refs
    else:
        (blocks, weights, gate, slots_out, act_out, gate_out, back_out,
         w_a, w_b, sums, slots, act, core_out, core_in, x_out, x_in, land, leave, back, land_back,
         w_sem, o_sem, in_sems, back_sems, core_sems, x_sems, act_sems) = refs
    peers = Peers(sizes)
    s, h, t = peers.at
    n_s, n_h, n_t = sizes
    me = peers.flat(peers.at)
    core, chip = lax.rem(s, 2), s // 2
    sibling = (s + 1 - 2 * core, h, t)
    across = (lax.rem(s + 2, n_s), h, t)
    half = act.shape[0] // 2
    own, other = core * half, (1 - core) * half
    n_blocks = peers.count
    first = 1 if backward else 0
    loads = [
        pltpu.make_async_copy(weights.at[first], w_a, w_sem.at[0]),
        pltpu.make_async_copy(weights.at[1 - first], w_b, w_sem.at[1]),
    ]
    for load in loads:
        load.start()
    if backward:
        gate_load = pltpu.make_async_copy(gate, gate_v, o_sem.at[0])
        gate_load.start()
    peers.greet_all()

    def block_out(k):
        place = peers.step(k, 1)
        return remote(
            blocks.at[place[1], place[0]], land.at[me], in_sems.at[0, k], in_sems.at[1, k], place
        )

    def block_in(k):
        source = peers.flat(peers.step(k, -1))
        return remote(
            blocks.at[0, 0], land.at[source], in_sems.at[0, k], in_sems.at[1, k], sibling
        )

    def each(function, count=n_blocks, start=1):
        lax.fori_loop(start, count, lambda k, carry: (function(k), carry)[1], 0)

    each(lambda k: block_out(k).start())
    land[me] = blocks[h, s]
    swap = swap_matrix(16)
    each(lambda k: block_in(k).wait_recv())
    group = 8
    for b in range(n_blocks // group):
        rows = land[b * group : (b + 1) * group].reshape(group * 32, land.shape[2])
        turned = dot(swap, rows).astype(BF16)
        slots[:, b * 16 : (b + 1) * 16, :] = turned.reshape(16, 16, land.shape[2])
    if backward:
        g_copies = []
        own_rows = output.shape[0]
        mine = gathered.at[pl.ds(h * own_rows, own_rows)]
        for d in range(1, n_h):
            g_copies.append(
                remote(output, mine, g_sems.at[0, d], g_sems.at[1, d], (s, lax.rem(h + d, n_h), t))
            )
        for copy in g_copies:
            copy.start()
        g_own = pltpu.make_async_copy(output, mine, g_sems.at[0, 0])
        g_own.start()
    loads[0].wait()

    def core_copy(j):
        return remote(
            core_out.at[j], core_in.at[j], core_sems.at[0, j], core_sems.at[1, j], sibling
        )

    def x_copy(j):
        return remote(x_out.at[j], x_in.at[j], x_sems.at[0, j], x_sems.at[1, j], across)

    def act_copy(j):
        return remote(
            act.at[own + j], act.at[own + j], act_sems.at[0, j], act_sems.at[1, j], sibling
        )

    def act_in(j):
        return remote(
            act.at[other + j], act.at[other + j], act_sems.at[0, j], act_sems.at[1, j], sibling
        )

    def meet(j):
        core_copy(j).wait_recv()
        sums[j] = sums[j] + core_in[j].astype(F32)
        x_out[j] = sums[j].astype(BF16)
        x_copy(j).start()

    def first_sums(j):
        core_out[j] = dot(slots[other + j], w_a[other + j]).astype(BF16)
        core_copy(j).start()
        sums[j] = dot(slots[own + j], w_a[own + j])

        @pl.when(j > 0)
        def _():
            meet(j - 1)

    each(first_sums, half, 0)
    meet(half - 1)
    loads[1].wait()
    if backward:
        gate_load.wait()

    def second(e):
        leave[e] = dot_t(act[e], w_b[e]).astype(BF16)

    def finish(j):
        x_copy(j).wait_recv()
        value = sums[j] + x_in[j].astype(F32)
        if backward:
            act[own + j] = (value * gate_v[j]).astype(BF16)
        else:
            value = value + gate[own + j]
            cumulative = 0.5 + 0.5 * lax.erf(value * 0.7071067811865476)
            act[own + j] = (value * cumulative).astype(BF16)
            sums[j] = cumulative + value * (
                jnp.exp(value * value * -0.5) * 0.3989422804014327
            )
        act_copy(j).start()
        second(own + j)

        @pl.when(j > 0)
        def _():
            act_in(j - 1).wait_recv()
            second(other + j - 1)

    each(finish, half, 0)
    act_in(half - 1).wait_recv()
    second(other + half - 1)

    for b in range(n_blocks // group):
        rows = leave[:, b * 16 : (b + 1) * 16, :].reshape(group * 32, leave.shape[2])
        turned = dot(swap, rows).astype(BF16)
        back[b * group : (b + 1) * group] = turned.reshape(group, 32, leave.shape[2])

    def back_copy(k):
        place = peers.step(k, 1)
        return remote(
            back.at[peers.flat(place)], land_back.at[me], back_sems.at[0, k], back_sems.at[1, k],
            place,
        )

    def back_in(k):
        source = peers.flat(peers.step(k, -1))
        return remote(
            back.at[0], land_back.at[source], back_sems.at[0, k], back_sems.at[1, k], sibling
        )

    each(lambda k: back_copy(k).start())
    land_back[me] = back[me]
    stores = [pltpu.make_async_copy(act, act_out, o_sem.at[1])]
    if not backward:
        stores.append(pltpu.make_async_copy(sums, gate_out, o_sem.at[0]))
    for store in stores:
        store.start()
    slots_out[...] = slots[...]
    if backward:
        across_t = (s, h, 1 - t)
        width = bias_out.shape[1]

        def bias_row(e):
            bias_all[pl.ds(e, 1), :] = jnp.sum(act[e].astype(F32), axis=0, keepdims=True)

        each(bias_row, 2 * half, 0)

        def piece(for_t):
            return bias_all[:, pl.ds(pl.multiple_of((core * n_t + for_t) * width, 128), width)]

        bias_send[...] = piece(1 - t)
        bias_copy = remote(bias_send, bias_land, b_sems.at[0], b_sems.at[1], across_t)
        bias_copy.start()
        bias_copy.wait()
        bias_out[...] = jnp.where(t == chip, piece(t), bias_land[...])
    each(lambda k: back_in(k).wait_recv())
    back_out[...] = land_back[...]
    for store in stores:
        store.wait()
    if backward:
        for copy in g_copies:
            copy.wait()
        g_own.wait()
    each(lambda k: block_out(k).wait_send())
    each(lambda k: back_copy(k).wait_send())
    for copy in (core_copy, x_copy, act_copy):
        each(lambda j: copy(j).wait_send(), half, 0)


def expert_pass(sizes, backward, blocks, weights, gate, output=None, bias_width=0):
    _, experts, rows, hidden = weights.shape
    devices = sizes[0] * sizes[1] * sizes[2]
    images = 2 * devices
    half = experts // 2
    vmem = pl.BlockSpec(memory_space=pltpu.VMEM)
    hbm = pl.BlockSpec(memory_space=pl.ANY)
    slots = jax.ShapeDtypeStruct((experts, images, rows), BF16)
    act = jax.ShapeDtypeStruct((experts, images, hidden), BF16)
    gate_shape = (half, images, hidden)
    returned = jax.ShapeDtypeStruct((devices, 2 * experts, rows), BF16)
    if backward:
        operands, in_specs = (blocks, weights, gate, output), [vmem, hbm, hbm, hbm]
        gathered = (sizes[1] * output.shape[0], *output.shape[1:])
        outs = (
            slots, act, returned, jax.ShapeDtypeStruct((experts, bias_width), F32),
            jax.ShapeDtypeStruct(gathered, BF16),
        )
        out_specs = (vmem, hbm, vmem, vmem, hbm)
    else:
        operands, in_specs = (blocks, weights, gate), [vmem, hbm, vmem]
        outs = (slots, act, jax.ShapeDtypeStruct(gate_shape, F32), returned)
        out_specs = (vmem, hbm, hbm, vmem)
    weight = pltpu.VMEM((experts, rows, hidden), BF16)
    chunk = pltpu.VMEM((half, images, hidden), BF16)
    block = pltpu.VMEM((devices, 2 * experts, rows), BF16)
    dma = pltpu.SemaphoreType.DMA
    scratch = [weight, weight]
    if backward:
        scratch.append(pltpu.VMEM(gate_shape, F32))
    scratch += [
        pltpu.VMEM(gate_shape, F32),
        pltpu.VMEM(slots.shape, BF16),
        pltpu.VMEM(act.shape, BF16),
        chunk, chunk, chunk, chunk, block,
        pltpu.VMEM(slots.shape, BF16),
        block, block,
        dma((2,)), dma((2,)), dma((2, devices)), dma((2, devices)),
        dma((2, half)), dma((2, half)), dma((2, half)),
    ]
    if backward:
        scratch += [
            dma((2, sizes[1])), dma((2,)),
            pltpu.VMEM((experts, hidden), F32),
            pltpu.VMEM((experts, bias_width), F32),
            pltpu.VMEM((experts, bias_width), F32),
        ]
    return pl.pallas_call(
        partial(expert_kernel, sizes, backward),
        out_shape=outs,
        in_specs=in_specs,
        out_specs=out_specs,
        scratch_shapes=scratch,
        compiler_params=pltpu.CompilerParams(
            collective_id=2 if backward else 1, has_side_effects=True, vmem_limit_bytes=VMEM_BYTES
        ),
        cost_estimate=pl.CostEstimate(
            flops=8 * images * experts * rows * hidden,
            bytes_accessed=weights.size * 2,
            transcendentals=0,
        ),
        name="experts_back" if backward else "experts_ahead",
    )(*operands)


def weight_grad_kernel(slots_0, act_0, slots_1, act_1, out):
    group = out.shape[2]
    d_block = out.shape[0]
    images, rows = slots_0.shape[1:]
    g, first = pl.program_id(1), pl.program_id(2) * d_block
    n = group * d_block
    row = lax.broadcasted_iota(jnp.int32, (n, rows), 0)
    column = lax.broadcasted_iota(jnp.int32, (n, rows), 1)
    pick = (column == first + row // group).astype(F32).astype(BF16)
    row = lax.broadcasted_iota(jnp.int32, (n, group * images), 0)
    column = lax.broadcasted_iota(jnp.int32, (n, group * images), 1)
    same = row % group == column // images

    def term(slots, act):
        lines = slots[pl.ds(g * group, group)].reshape(group * images, rows)
        spread = jnp.where(same, dot_t(pick, lines), 0.0).astype(BF16)
        values = act[pl.ds(g * group, group)].reshape(group * images, act.shape[2])
        out[...] = dot(spread, values).reshape(out.shape)

    @pl.when(pl.program_id(0) == 0)
    def _():
        term(slots_0, act_0)

    @pl.when(pl.program_id(0) == 1)
    def _():
        term(slots_1, act_1)


def weight_grads(slots_0, act_0, slots_1, act_1):
    experts, images, rows = slots_0.shape
    hidden = act_0.shape[2]
    group, d_block = 8, 32
    vmem = pl.BlockSpec(memory_space=pltpu.VMEM)
    return pl.pallas_call(
        weight_grad_kernel,
        grid=(2, experts // group, rows // d_block),
        out_shape=jax.ShapeDtypeStruct((rows, 2, experts, hidden), F32),
        in_specs=[vmem] * 4,
        out_specs=pl.BlockSpec((d_block, 1, group, hidden), lambda m, g, d: (d, m, g, 0)),
        compiler_params=pltpu.CompilerParams(vmem_limit_bytes=VMEM_BYTES),
        cost_estimate=pl.CostEstimate(
            flops=4 * images * experts * rows * hidden,
            bytes_accessed=8 * rows * experts * hidden,
            transcendentals=0,
        ),
        name="weight_grads",
    )(slots_0, act_0, slots_1, act_1)


def normalize(values, scale, shift):
    centered = values - jnp.mean(values, axis=-1, keepdims=True)
    variance = jnp.mean(centered * centered, axis=-1, keepdims=True)
    inverse = lax.rsqrt(variance + epsilon)
    unit_part = centered * inverse
    return (unit_part * scale + shift, unit_part, inverse)


def normalize_back(grad_output, unit_part, inverse, scale):
    scaled = grad_output * scale
    average = jnp.mean(scaled, axis=-1, keepdims=True)
    projection = jnp.mean(scaled * unit_part, axis=-1, keepdims=True)
    grad_input = inverse * (scaled - average - unit_part * projection)
    return (
        grad_input,
        jnp.sum(grad_output * unit_part, axis=(0, 1)),
        jnp.sum(grad_output, axis=(0, 1)),
    )


def to_experts(slots):
    slots = lax.all_to_all(slots, "heads", split_axis=1, concat_axis=0, tiled=True)
    slots = lax.all_to_all(slots, "shard", split_axis=2, concat_axis=0, tiled=True)
    return lax.all_gather(slots, "tensor", axis=0, tiled=True)


def to_blocks(slots, sizes):
    own, experts, width = slots.shape
    n_s, n_h, _ = sizes
    slots = slots.reshape(own, n_h, experts // n_h, n_s, width // n_s)
    return slots.transpose(1, 3, 0, 2, 4).reshape(n_h, n_s, own * experts // n_h, width // n_s)


def from_blocks(blocks, sizes):
    n_s, n_h, n_t = sizes
    rows = blocks.shape[2]
    blocks = jnp.sum(blocks.reshape(n_s, n_h, n_t, 2, -1, rows).astype(F32), axis=2)
    return blocks.transpose(2, 1, 3, 0, 4).reshape(2, -1, n_s * rows)


def to_images(slots):
    slots = lax.psum_scatter(slots, "tensor", scatter_dimension=0, tiled=True)
    slots = lax.all_to_all(slots, "shard", split_axis=0, concat_axis=2, tiled=True)
    return lax.all_to_all(slots, "heads", split_axis=0, concat_axis=1, tiled=True)


def shards(tokens, norm_scales, norm_biases, w_attn, phi, experts, in_bias, out_bias, cotangent):
    heads_n = lax.axis_size("heads")
    sizes = tuple(lax.axis_size(name) for name in ("shard", "heads", "tensor"))
    if sizes != (4, 4, 2) or tokens.shape[0] != 8 or experts.shape[2] != 16:
        sizes = None
    group, seq_len, width = tokens.shape
    own = group // heads_n
    heads_index = lax.axis_index("heads")
    tensor_index = lax.axis_index("tensor")
    shard_index = lax.axis_index("shard")
    hidden = experts.shape[3]
    rows = experts.shape[0]
    if sizes is not None:
        n_s, n_h, n_t = sizes
        block, slot = w_attn.shape[2], phi.shape[1]
        beside = jnp.concatenate((phi, out_bias.T), axis=1)
        beside = jnp.pad(beside, ((0, 0), (0, 256 - block - 2 * slot)))
        beside = jnp.concatenate((beside[None], jnp.zeros((3, *beside.shape), BF16)), axis=0)
        packet = jnp.concatenate((w_attn, beside), axis=2)
        extra = jnp.concatenate(
            (
                in_bias.reshape(-1, 64),
                norm_scales.T,
                norm_biases.T,
            ),
            axis=1,
        )
        extra = jnp.pad(extra, ((0, 0), (128, 60)))
        attn, small, turned = gather_weights(sizes, packet, extra, experts)
        phi_full = small[:, :64]
        out_all = small[:, 64:128].T.astype(F32)
        in_full = small[:, 128:192].reshape(n_s * n_t, -1, in_bias.shape[1])
        in_full = in_full.transpose(1, 0, 2).reshape(in_bias.shape[0], -1).astype(F32)
        scales = small[:, 192:194].T.astype(F32)
        biases = small[:, 194:196].T.astype(F32)
    else:
        scales, biases, in_full = (
            lax.all_gather(norm_scales, ROWS, axis=1, tiled=True).astype(F32),
            lax.all_gather(norm_biases, ROWS, axis=1, tiled=True).astype(F32),
            lax.all_gather(in_bias, ROWS, axis=1, tiled=True).astype(F32),
        )
        attn = lax.all_gather(
            lax.all_gather(w_attn, "heads", axis=2, tiled=True), ROWS, axis=1, tiled=True
        )
        phi_full = lax.all_gather(
            lax.all_gather(phi, "heads", axis=1, tiled=True), ROWS, axis=0, tiled=True
        )
        out_rows = lax.all_gather(out_bias, "tensor", axis=1, tiled=True).astype(F32)
    e_own = experts.shape[2] // lax.axis_size("shard")
    in_local = lax.dynamic_slice_in_dim(in_full, tensor_index * hidden, hidden, 1)
    factor = HEAD_DIM ** (-0.5)
    tokens = lax.dynamic_slice_in_dim(tokens, heads_index * own, own, 0)
    cotangent = lax.dynamic_slice_in_dim(cotangent, heads_index * own, own, 0)
    n_heads = width // HEAD_DIM
    inputs = tokens.astype(F32)
    normed_one, unit_one, inverse_one = normalize(inputs, scales[0], biases[0])
    normed_one_b = normed_one.astype(BF16)
    projected = einsum("nsd,kdc->knsc", normed_one_b, attn[:3]).astype(BF16)
    query, keyed, valued = projected.reshape(3, own, seq_len, n_heads, HEAD_DIM)
    scores = einsum("nqhe,nkhe->nhqk", query, keyed) * factor
    score_peak = jnp.max(scores, axis=-1, keepdims=True)
    exponent = jnp.exp(scores - score_peak)
    probs = exponent / jnp.sum(exponent, axis=-1, keepdims=True)
    probs_b = probs.astype(BF16)
    context_b = (
        einsum("nhqk,nkhe->nqhe", probs_b, valued).astype(BF16).reshape(own, seq_len, width)
    )
    hidden_one = inputs + einsum("nsc,dc->nsd", context_b, attn[3])
    normed_two, unit_two, inverse_two = normalize(hidden_one, scales[1], biases[1])
    normed_two_b = normed_two.astype(BF16)
    logits = einsum("nsd,de->nse", normed_two_b, phi_full)
    dispatch = jax.nn.softmax(logits, axis=1)
    dispatch_b = dispatch.astype(BF16)
    combine = jax.nn.softmax(logits, axis=2)
    combine_b = combine.astype(BF16)
    slot_in = einsum("nse,nsd->ned", dispatch_b, normed_two_b).astype(BF16)
    if sizes is not None:
        slot_in, activated, gate, back = expert_pass(
            sizes, False, to_blocks(slot_in, sizes), turned, in_local[:, None, :]
        )
        slot_out = (from_blocks(back, sizes) + out_all).astype(BF16)
    else:
        slot_in = to_experts(slot_in)
        share = 1 if e_own else 0

        def meet(partial_sum):
            return lax.psum_scatter(partial_sum, "shard", scatter_dimension=share, tiled=True)

        def spread(values):
            return lax.all_gather(values, "shard", axis=share, tiled=True)

        pre = meet(einsum("ned,def->nef", slot_in, experts[:, 0]))
        if e_own:
            pre = pre + lax.dynamic_slice_in_dim(in_local, shard_index * e_own, e_own, 0)
        else:
            pre = pre + in_local
        gelu_value, gelu_back = jax.vjp(partial(jax.nn.gelu, approximate=False), pre)
        activated = spread(gelu_value.astype(BF16))
        slot_out_part = einsum("nef,def->ned", activated, experts[:, 1])
        slot_out_part = slot_out_part + jnp.where(tensor_index == 0, out_rows, 0.0)
        slot_out = to_images(slot_out_part).astype(BF16)
    output = (hidden_one + einsum("nse,ned->nsd", combine_b, slot_out)).astype(BF16)
    grad_combine = einsum("nsd,ned->nse", cotangent, slot_out)
    grad_slot = einsum("nse,nsd->ned", combine_b, cotangent).astype(BF16)
    if sizes is not None:
        grad_slot, grad_pre, back, in_bias_grad, output = expert_pass(
            sizes, True, to_blocks(grad_slot, sizes), turned, gate, output, in_bias.shape[1]
        )
        grad_slot_in = from_blocks(back, sizes).astype(BF16)
        experts_grad = weight_grads(slot_in, grad_pre, grad_slot, activated)
        grad_slot_sum = jnp.sum(grad_slot.astype(F32), axis=1)
    else:
        output = lax.all_gather(output, "heads", axis=0, tiled=True)
        grad_slot = to_experts(grad_slot)
        grad_act = meet(einsum("ned,def->nef", grad_slot, experts[:, 1]))
        grad_pre = spread(gelu_back(grad_act)[0].astype(BF16))
        grad_slot_in = einsum("nef,def->ned", grad_pre, experts[:, 0]).astype(BF16)
        input_term = einsum("ned,nef->def", slot_in, grad_pre)
        output_term = einsum("ned,nef->def", grad_slot, activated)
        experts_grad = jnp.stack((input_term, output_term), axis=1)
        grad_slot_in = to_images(grad_slot_in.astype(F32)).astype(BF16)
        in_bias_grad = lax.dynamic_slice_in_dim(
            lax.all_gather(jnp.sum(grad_pre.astype(F32), axis=0), "tensor", axis=1, tiled=True),
            (shard_index * lax.axis_size("tensor") + tensor_index) * in_bias.shape[1],
            in_bias.shape[1],
            1,
        )
        grad_slot_sum = jnp.sum(grad_slot.astype(F32), axis=0)
    out_bias_grad = lax.dynamic_slice_in_dim(
        grad_slot_sum,
        tensor_index * out_bias.shape[1],
        out_bias.shape[1],
        1,
    )
    grad_dispatch = einsum("nsd,ned->nse", normed_two_b, grad_slot_in)
    grad_logits = (
        dispatch * (grad_dispatch - jnp.sum(dispatch * grad_dispatch, axis=1, keepdims=True))
        + combine * (grad_combine - jnp.sum(combine * grad_combine, axis=2, keepdims=True))
    ).astype(BF16)
    phi_grad = einsum("nsd,nse->de", normed_two_b, grad_logits)
    grad_normed_two = einsum("nse,ned->nsd", dispatch_b, grad_slot_in) + einsum(
        "nse,de->nsd", grad_logits, phi_full
    )
    grad_hidden_norm, scale_two_grad, bias_two_grad = normalize_back(
        grad_normed_two, unit_two, inverse_two, scales[1]
    )
    grad_hidden = cotangent.astype(F32) + grad_hidden_norm
    grad_hidden_b = grad_hidden.astype(BF16)
    out_weight_grad = einsum("nsd,nsc->dc", grad_hidden_b, context_b)
    grad_context = einsum("nsd,dc->nsc", grad_hidden_b, attn[3]).astype(BF16)
    grad_context = grad_context.reshape(own, seq_len, n_heads, HEAD_DIM)
    grad_value = einsum("nhqk,nqhe->nkhe", probs_b, grad_context).astype(BF16)
    grad_probs = einsum("nqhe,nkhe->nhqk", grad_context, valued)
    grad_scores = (
        probs * (grad_probs - jnp.sum(probs * grad_probs, axis=-1, keepdims=True))
    ).astype(BF16)
    grad_query = (einsum("nhqk,nkhe->nqhe", grad_scores, keyed) * factor).astype(BF16)
    grad_key = (einsum("nhqk,nqhe->nkhe", grad_scores, query) * factor).astype(BF16)
    grad_proj = jnp.stack((grad_query, grad_key, grad_value)).reshape(3, own, seq_len, width)
    proj_grad = einsum("nsd,knsc->kdc", normed_one_b, grad_proj)
    grad_normed_one = einsum("knsc,kdc->nsd", grad_proj, attn[:3])
    grad_input_norm, scale_one_grad, bias_one_grad = normalize_back(
        grad_normed_one, unit_one, inverse_one, scales[0]
    )
    input_grad = (grad_hidden + grad_input_norm).astype(BF16)
    input_grad = lax.all_gather(input_grad, "heads", axis=0, tiled=True)
    attn_grad = jnp.concatenate((proj_grad, out_weight_grad[None]), axis=0)
    norms = jnp.stack((scale_one_grad, scale_two_grad, bias_one_grad, bias_two_grad))
    if sizes is not None:
        small = jnp.concatenate((phi_grad, norms.T), axis=1)
        small = jnp.pad(small, ((0, 0), (0, 128 - small.shape[1]))).astype(BF16)
        summed = reduce_grads(sizes, attn_grad.astype(BF16), small)
        attn_grad = summed[:, :, :block]
        phi_grad = summed[0, :, block : block + slot]
        norms = summed[0, :, block + slot : block + slot + 4].T
    else:
        attn_grad = lax.psum_scatter(attn_grad, ROWS, scatter_dimension=1, tiled=True)
        attn_grad = lax.psum_scatter(attn_grad, "heads", scatter_dimension=2, tiled=True)
        phi_grad = lax.psum_scatter(phi_grad, ROWS, scatter_dimension=0, tiled=True)
        phi_grad = lax.psum_scatter(phi_grad, "heads", scatter_dimension=1, tiled=True)
        norms = lax.psum(lax.psum_scatter(norms, ROWS, scatter_dimension=1, tiled=True), "heads")
    return (
        output,
        input_grad,
        norms[:2],
        norms[2:],
        attn_grad,
        phi_grad,
        experts_grad,
        in_bias_grad,
        out_bias_grad,
    )


def solution(mesh):
    images = P(ROWS, None, None)
    return jax.shard_map(
        shards,
        mesh=mesh,
        in_specs=(
            images,
            P(None, ROWS),
            P(None, ROWS),
            P(None, ROWS, "heads"),
            P(ROWS, "heads"),
            P("shard", None, "heads", "tensor"),
            P("heads", ROWS),
            P("heads", ROWS),
            images,
        ),
        out_specs=(
            images,
            images,
            P(None, ROWS),
            P(None, ROWS),
            P(None, ROWS, "heads"),
            P(ROWS, "heads"),
            P("shard", None, "heads", "tensor"),
            P("heads", ROWS),
            P("heads", ROWS),
        ),
        check_vma=False,
    )
```

```python
from functools import partial

import jax
import jax.numpy as jnp
from jax import lax
from jax.experimental import pallas as pl
from jax.experimental.pallas import tpu as pltpu
from jax.sharding import PartitionSpec as P

HEAD_DIM = 64
F32 = jnp.float32
BF16 = jnp.bfloat16
ROWS = ("shard", "tensor")
MESH = pl.DeviceIdType.MESH
VMEM_BYTES = 58 * 1024 * 1024
epsilon = 1e-06
einsum = partial(jnp.einsum, preferred_element_type=F32)


def dot(a, b):
    return lax.dot_general(a, b, (((1,), (0,)), ((), ())), preferred_element_type=F32)


def dot_t(a, b):
    return lax.dot_general(a, b, (((1,), (1,)), ((), ())), preferred_element_type=F32)


def swap_matrix(n):
    out = lax.broadcasted_iota(jnp.int32, (n * n, n * n), 0)
    row = lax.broadcasted_iota(jnp.int32, (n * n, n * n), 1)
    return ((out // n == row % n) & (out % n == row // n)).astype(F32).astype(BF16)


class Peers:
    def __init__(self, sizes):
        self.sizes = sizes
        self.at = tuple(lax.axis_index(name) for name in ("shard", "heads", "tensor"))
        self.count = sizes[0] * sizes[1] * sizes[2]

    def flat(self, place):
        return (place[0] * self.sizes[1] + place[1]) * self.sizes[2] + place[2]

    def step(self, k, sign):
        _, n_h, n_t = self.sizes
        steps = (k // (n_h * n_t), (k // n_t) % n_h, k % n_t)
        return tuple(
            lax.rem(at + n + sign * d, n) for at, n, d in zip(self.at, self.sizes, steps)
        )

    def greet_all(self):
        barrier = pltpu.get_barrier_semaphore()

        def signal(k, carry):
            pl.semaphore_signal(barrier, inc=1, device_id=self.step(k, 1), device_id_type=MESH)
            return carry

        lax.fori_loop(1, self.count, signal, 0)
        pl.semaphore_wait(barrier, self.count - 1)


def remote(src, dst, send, recv, place):
    return pltpu.make_async_remote_copy(
        src_ref=src, dst_ref=dst, send_sem=send, recv_sem=recv, device_id=place, device_id_type=MESH
    )


def plane(sizes):
    n_s, n_h, n_t = sizes
    s, h, t = (lax.axis_index(name) for name in ("shard", "heads", "tensor"))
    core, chip = lax.rem(s, 2), s // 2
    sibling = (s + 1 - 2 * core, h, t)
    across_x = (lax.rem(s + 2, n_s), h, t)
    across_y = (s, h, 1 - t)
    line = [(s, lax.rem(h + d, n_h), t) for d in range(n_h)]
    barrier = pltpu.get_barrier_semaphore()
    others = [sibling, across_x, across_y] + line[1:]
    for place in others:
        pl.semaphore_signal(barrier, inc=1, device_id=place, device_id_type=MESH)
    pl.semaphore_wait(barrier, len(others))
    return (s, h, t), core, chip, sibling, across_x, across_y, line


def pair_matrix(block, wide, transposed):
    shape = (2 * block, 2 * wide) if transposed else (2 * wide, 2 * block)
    tight = lax.broadcasted_iota(jnp.int32, shape, 0 if transposed else 1)
    padded = lax.broadcasted_iota(jnp.int32, shape, 1 if transposed else 0)
    second = padded >= wide
    lane = jnp.where(second, padded - wide, padded)
    same = (lane < block) & (tight == jnp.where(second, lane + block, lane))
    return same.astype(F32).astype(BF16)


def gather_kernel(
    sizes, packet, extra, experts, w_out, small_out, turned,
    w, small, lined, tile_in, tile_out,
    z_send, z_recv, x_sems, y_sems, d_sems, c_sems, t_sems, o_sems,
):
    (s, h, t), core, chip, sibling, across_x, across_y, line = plane(sizes)
    n_k, rows, wide = packet.shape
    n_h, n_t = sizes[1], sizes[2]
    width = w.shape[2]
    block = width // n_h
    side = 16
    n_tiles = experts.shape[0] // side
    halves = ((0, rows // 2), (rows // 2, rows // 2))

    def z_hop(k, origin, up):
        place = line[1] if up else line[n_h - 1]
        return remote(
            lined.at[origin, k], lined.at[origin, k],
            z_send.at[k, origin, up], z_recv.at[k, origin], place,
        )

    def relay(k, d):
        @pl.when(h >= d)
        def _():
            z_hop(k, h - d, 1).wait_recv()

            @pl.when(h < n_h - 1)
            def _():
                z_hop(k, h - d, 1).start()

        @pl.when(h + d < n_h)
        def _():
            z_hop(k, h + d, 0).wait_recv()

            @pl.when(h > 0)
            def _():
                z_hop(k, h + d, 0).start()

    chunks = (0, 2, 1, 3)
    lined[h] = packet[...]
    for k in chunks:
        @pl.when(h < n_h - 1)
        def _():
            z_hop(k, h, 1).start()

        @pl.when(h > 0)
        def _():
            z_hop(k, h, 0).start()

    def load(i):
        return pltpu.make_async_copy(
            experts.at[pl.ds((i % n_tiles) * side, side), i // n_tiles],
            tile_in.at[i % 2],
            t_sems.at[0, i % 2],
        )

    def store(i):
        return pltpu.make_async_copy(
            tile_out.at[i % 2],
            turned.at[i // n_tiles, :, pl.ds((i % n_tiles) * side, side)],
            t_sems.at[1, i % 2],
        )

    load(0).start()
    swap = swap_matrix(side)
    done = [0]

    def turn(count):
        def step(i, carry):
            load(i).wait()

            @pl.when(i + 1 < 2 * n_tiles)
            def _():
                load(i + 1).start()

            @pl.when(i >= 2)
            def _():
                store(i - 2).wait()

            rows_in = tile_in[i % 2].reshape(side * side, tile_in.shape[3])
            tile_out[i % 2] = dot(swap, rows_in).astype(BF16).reshape(tile_out.shape[1:])
            store(i).start()
            return carry

        last = min(done[0] + count, 2 * n_tiles)
        lax.fori_loop(done[0], last, step, 0)
        done[0] = last

    pair = pair_matrix(block, wide, False)
    shape = (n_h * wide, small.shape[1])
    row = lax.broadcasted_iota(jnp.int32, shape, 0)
    column = lax.broadcasted_iota(jnp.int32, shape, 1)
    lane, of = row % wide - block, row // wide
    beside = (lane >= 0) & (lane < 16) & (column == of * 16 + lane)
    beside |= (lane >= 16) & (lane < 32) & (column == n_h * 16 + of * 16 + lane - 16)
    beside = beside.astype(F32).astype(BF16)

    def at(k, place):
        first = pl.multiple_of((place[0] * n_t + place[2]) * rows, 16)
        lines = pl.ds(first, rows)
        return small.at[lines] if k == n_k else w.at[k, lines]

    def hop(q, origin, place, sems, j):
        return remote(at(q, origin), at(q, origin), sems.at[0, j], sems.at[1, j], place)

    def half_hop(q, origin, place, half):
        part = at(q, origin).at[pl.ds(*halves[half])]
        j = 2 * q + half
        return remote(part, part, d_sems.at[0, j], d_sems.at[1, j], place)

    me = (s, h, t)
    from_d = (across_x[0], h, across_y[2])
    sent = []

    def send(copy):
        copy.start()
        sent.append(copy)

    def assemble(k):
        for i in range(0, n_h, 2):
            lines = jnp.concatenate([lined[i, k], lined[i + 1, k]], axis=1)
            at(k, me)[:, i * block : (i + 2) * block] = dot(lines, pair).astype(BF16)
        if k == 0:
            lines = jnp.concatenate([lined[i, k] for i in range(n_h)], axis=1)
            at(n_k, me)[...] = (dot(lines, beside) + extra[...].astype(F32)).astype(BF16)
        for q in members(k):
            send(hop(q, me, across_x, x_sems, q))
            send(hop(q, me, across_y, y_sems, q))
            send(hop(q, me, sibling, c_sems, 4 * q))

    def members(k):
        return (0, n_k) if k == 0 else (k,)

    def relay_xy(k):
        for q in members(k):
            hop(q, across_x, across_x, x_sems, q).wait_recv()
            send(half_hop(q, across_x, across_y, 0))
            send(hop(q, across_x, sibling, c_sems, 4 * q + 1))
            hop(q, across_y, across_y, y_sems, q).wait_recv()
            send(half_hop(q, across_y, across_x, 1))
            send(hop(q, across_y, sibling, c_sems, 4 * q + 2))

    def relay_d(k):
        for q in members(k):
            half_hop(q, from_d, across_y, 0).wait_recv()
            half_hop(q, from_d, across_x, 1).wait_recv()
            send(hop(q, from_d, sibling, c_sems, 4 * q + 3))

    for wave in range(n_k + n_h - 2):
        for d in range(1, n_h):
            if 0 <= wave - d + 1 < n_k:
                relay(chunks[wave - d + 1], d)
        turn(2)
        i = wave - n_h + 2
        if i >= 0:
            assemble(chunks[i])
            if i >= 1:
                relay_xy(chunks[i - 1])
            if i >= 2:
                relay_d(chunks[i - 2])
            turn(2)
    relay_xy(chunks[-1])
    relay_d(chunks[-2])
    turn(2 * n_tiles)
    relay_d(chunks[-1])
    stores = []
    for k in chunks:
        for q in members(k):
            for j in range(4):
                hop(q, me, sibling, c_sems, 4 * q + j).wait_recv()
            if q == n_k:
                stores.append(pltpu.make_async_copy(small, small_out, o_sems.at[q]))
            else:
                stores.append(pltpu.make_async_copy(w.at[q], w_out.at[q], o_sems.at[q]))
            stores[-1].start()
    for copy in sent:
        copy.wait_send()
    for origin in range(n_h):
        @pl.when((origin <= h) & (h < n_h - 1))
        def _():
            for k in range(n_k):
                z_hop(k, origin, 1).wait_send()

        @pl.when((origin >= h) & (h > 0))
        def _():
            for k in range(n_k):
                z_hop(k, origin, 0).wait_send()

    store(2 * n_tiles - 2).wait()
    store(2 * n_tiles - 1).wait()
    for copy in stores:
        copy.wait()


def gather_weights(sizes, packet, extra, experts):
    n_k, rows, wide = packet.shape
    n_s, n_h, n_t = sizes
    width = n_s * n_t * rows
    vmem = pl.BlockSpec(memory_space=pltpu.VMEM)
    hbm = pl.BlockSpec(memory_space=pl.ANY)
    dma = pltpu.SemaphoreType.DMA
    hidden = experts.shape[3]
    small = (width, extra.shape[1])
    return pl.pallas_call(
        partial(gather_kernel, sizes),
        out_shape=(
            jax.ShapeDtypeStruct((n_k, width, width), BF16),
            jax.ShapeDtypeStruct(small, BF16),
            jax.ShapeDtypeStruct((2, experts.shape[2], experts.shape[0], hidden), BF16),
        ),
        in_specs=[vmem, vmem, hbm],
        out_specs=(hbm, hbm, hbm),
        scratch_shapes=[
            pltpu.VMEM((n_k, width, width), BF16),
            pltpu.VMEM(small, BF16),
            pltpu.VMEM((n_h, n_k, rows, wide), BF16),
            pltpu.VMEM((2, 16, 16, hidden), BF16),
            pltpu.VMEM((2, 16, 16, hidden), BF16),
            dma((n_k, n_h, 2)), dma((n_k, n_h)), dma((2, n_k + 1)), dma((2, n_k + 1)),
            dma((2, 2 * (n_k + 1))), dma((2, 4 * (n_k + 1))), dma((2, 2)), dma((n_k + 1,)),
        ],
        compiler_params=pltpu.CompilerParams(
            collective_id=3, has_side_effects=True, vmem_limit_bytes=VMEM_BYTES
        ),
        name="gather_weights",
    )(packet, extra, experts)


def reduce_kernel(
    sizes, grads, small, out, core_in, core_small, met, met_small,
    d_in, d_small, x_in, x_small, y_in, y_small, pieces, z_in,
    c_sems, d_sems, x_sems, y_sems, z_sems,
):
    (s, h, t), core, chip, sibling, across_x, across_y, line = plane(sizes)
    n_k, width, _ = grads.shape
    n_s, n_h, n_t = sizes
    rows = width // (n_s * n_t)
    wide = pieces.shape[3]
    pair = n_t * rows
    half = rows // 2
    halves = (pl.ds(0, half), pl.ds(half, half))
    chunks = (0, 2, 1, 3)

    def members(k):
        return (0, n_k) if k == 0 else (k,)

    def pick(q, large, little):
        return little if q == n_k else large.at[q]

    def core_copy(q, x):
        first = pl.multiple_of((2 * x + 1 - core) * pair, 16)
        return remote(
            pick(q, grads, small).at[pl.ds(first, pair)],
            pick(q, core_in, core_small).at[x],
            c_sems.at[0, 2 * q + x], c_sems.at[1, 2 * q + x], sibling,
        )

    for k in chunks:
        for q in members(k):
            for x in range(2):
                core_copy(q, x).start()
    joined = pair_matrix(width // n_h, wide, True)
    shape = (small.shape[1], n_h * wide)
    row = lax.broadcasted_iota(jnp.int32, shape, 0)
    column = lax.broadcasted_iota(jnp.int32, shape, 1)
    lane, of = column % wide - width // n_h, column // wide
    beside = (lane >= 0) & (lane < 16) & (row == of * 16 + lane)
    beside |= (lane >= 16) & (lane < 20) & (row == n_h * 16 + lane - 16)
    beside = beside.astype(F32).astype(BF16)
    to_d, to_x, to_y = (d_in, d_small), (x_in, x_small), (y_in, y_small)
    sent = []

    def hop(q, kind, part, source, place):
        sems = {id(to_d): d_sems, id(to_x): x_sems, id(to_y): y_sems}[id(kind)]
        target = pick(q, *kind)
        target = target.at[part] if kind is to_d else target.at[halves[part]]
        j = 2 * q + part
        return remote(source, target, sems.at[0, j], sems.at[1, j], place)

    def send(copy):
        copy.start()
        sent.append(copy)

    def part_of(q, x, y, part):
        return pick(q, met, met_small).at[x, y].at[halves[part]]

    def arrived(q, kind, part):
        hop(q, kind, part, part_of(q, 0, 0, part), sibling).wait_recv()

    def open_up(q):
        part = pick(q, met, met_small)
        for x in range(2):
            core_copy(q, x).wait_recv()
            first = pl.multiple_of((2 * x + core) * pair, 16)
            own = pick(q, grads, small)[pl.ds(first, pair)].astype(F32)
            total = own + pick(q, core_in, core_small)[x].astype(F32)
            part[x] = total.astype(BF16).reshape(n_t, rows, total.shape[1])
        send(hop(q, to_d, 0, part_of(q, 1 - chip, 1 - t, 0), across_x))
        send(hop(q, to_d, 1, part_of(q, 1 - chip, 1 - t, 1), across_y))
        send(hop(q, to_x, 0, part_of(q, 1 - chip, t, 0), across_x))
        send(hop(q, to_y, 1, part_of(q, chip, 1 - t, 1), across_y))

    def pass_on(q):
        for part, kind, x, y, place in (
            (0, to_y, chip, 1 - t, across_y),
            (1, to_x, 1 - chip, t, across_x),
        ):
            arrived(q, to_d, part)
            block = part_of(q, x, y, part)
            total = block[...].astype(F32) + pick(q, *to_d)[part].astype(F32)
            block[...] = total.astype(BF16)
            send(hop(q, kind, part, block, place))

    def whole(q):
        for kind in (to_x, to_y):
            for part in range(2):
                arrived(q, kind, part)
        total = pick(q, met, met_small)[chip, t].astype(F32) + pick(q, *to_x)[...].astype(F32)
        return (total + pick(q, *to_y)[...].astype(F32)).astype(BF16)

    def z_copy(k, d):
        return remote(
            pieces.at[line[d][1], k], z_in.at[h, k], z_sems.at[0, k, d], z_sems.at[1, k, d], line[d]
        )

    def share_out(k):
        value = whole(k)
        columns = width // n_h
        if k == 0:
            little = dot(whole(n_k), beside)
        for i in range(0, n_h, 2):
            lanes = dot(value[:, i * columns : (i + 2) * columns], joined)
            if k == 0:
                lanes = lanes + little[:, i * wide : (i + 2) * wide]
            pieces[i, k] = lanes[:, :wide].astype(BF16)
            pieces[i + 1, k] = lanes[:, wide:].astype(BF16)
        for d in range(n_h - 1, 0, -1):
            z_copy(k, d).start()

    for i in range(n_k + 2):
        if i < n_k:
            for q in members(chunks[i]):
                open_up(q)
        if 0 <= i - 1 < n_k:
            for q in members(chunks[i - 1]):
                pass_on(q)
        if i >= 2:
            share_out(chunks[i - 2])
    for k in chunks:
        total = pieces[h, k].astype(F32)
        for d in range(1, n_h):
            z_copy(k, d).wait_recv()
        for d in range(1, n_h):
            total = total + z_in[line[d][1], k].astype(F32)
        out[k] = total
    for k in chunks:
        for q in members(k):
            for x in range(2):
                core_copy(q, x).wait_send()
    for copy in sent:
        copy.wait_send()
    for k in range(n_k):
        for d in range(1, n_h):
            z_copy(k, d).wait_send()


def reduce_grads(sizes, grads, small):
    n_k, width, _ = grads.shape
    n_s, n_h, n_t = sizes
    rows, wide, thin = width // (n_s * n_t), 256, small.shape[1]
    vmem = pl.BlockSpec(memory_space=pltpu.VMEM)
    dma = pltpu.SemaphoreType.DMA

    def buffers(*lead):
        return [
            pltpu.VMEM((n_k, *lead, width), BF16),
            pltpu.VMEM((*lead, thin), BF16),
        ]

    return pl.pallas_call(
        partial(reduce_kernel, sizes),
        out_shape=jax.ShapeDtypeStruct((n_k, rows, wide), F32),
        in_specs=[vmem, vmem],
        out_specs=vmem,
        scratch_shapes=[
            *buffers(2, n_t * rows), *buffers(2, n_t, rows),
            *buffers(2, rows // 2), *buffers(rows), *buffers(rows),
            pltpu.VMEM((n_h, n_k, rows, wide), BF16),
            pltpu.VMEM((n_h, n_k, rows, wide), BF16),
            dma((2, 2 * (n_k + 1))), dma((2, 2 * (n_k + 1))), dma((2, 2 * (n_k + 1))),
            dma((2, 2 * (n_k + 1))), dma((2, n_k, n_h)),
        ],
        compiler_params=pltpu.CompilerParams(
            collective_id=4, has_side_effects=True, vmem_limit_bytes=VMEM_BYTES
        ),
        name="reduce_grads",
    )(grads, small)


def expert_kernel(sizes, backward, *refs):
    if backward:
        (blocks, weights, gate, slots_out, act_out, back_out, bias_out,
         w_a, w_b, gate_v, sums, slots, act, core_out, core_in, x_out, x_in, land, leave, back, land_back,
         w_sem, o_sem, in_sems, back_sems, core_sems, x_sems, act_sems, b_sems,
         bias_all, bias_send, bias_land) = refs
    else:
        (blocks, weights, gate, slots_out, act_out, gate_out, back_out,
         w_a, w_b, sums, slots, act, core_out, core_in, x_out, x_in, land, leave, back, land_back,
         w_sem, o_sem, in_sems, back_sems, core_sems, x_sems, act_sems) = refs
    peers = Peers(sizes)
    s, h, t = peers.at
    n_s, n_h, n_t = sizes
    me = peers.flat(peers.at)
    core, chip = lax.rem(s, 2), s // 2
    sibling = (s + 1 - 2 * core, h, t)
    across = (lax.rem(s + 2, n_s), h, t)
    half = act.shape[0] // 2
    own, other = core * half, (1 - core) * half
    n_blocks = peers.count
    first = 1 if backward else 0
    loads = [
        pltpu.make_async_copy(weights.at[first], w_a, w_sem.at[0]),
        pltpu.make_async_copy(weights.at[1 - first], w_b, w_sem.at[1]),
    ]
    for load in loads:
        load.start()
    if backward:
        gate_load = pltpu.make_async_copy(gate, gate_v, o_sem.at[0])
        gate_load.start()
    peers.greet_all()

    def block_out(p, k):
        place = peers.step(k, 1)
        return remote(
            blocks.at[place[1], place[0], p], land.at[p, me],
            in_sems.at[0, p, k], in_sems.at[1, p, k], place,
        )

    def block_in(p, k):
        source = peers.flat(peers.step(k, -1))
        return remote(
            blocks.at[0, 0, p], land.at[p, source], in_sems.at[0, p, k], in_sems.at[1, p, k], sibling
        )

    def each(function, count=n_blocks, start=1):
        lax.fori_loop(start, count, lambda k, carry: (function(k), carry)[1], 0)

    for p in range(2):
        each(lambda k: block_out(p, k).start())
        land[p, me] = blocks[h, s, p]
    few = half // 2
    group = 16
    many = 2 * group
    out_row = lax.broadcasted_iota(jnp.int32, (16 * group, 16 * group), 0)
    in_row = lax.broadcasted_iota(jnp.int32, (16 * group, 16 * group), 1)
    there = (out_row // many == in_row % (2 * few)) & (out_row % many == in_row // (2 * few))
    there = there.astype(F32).astype(BF16)
    again = (in_row // many == out_row % (2 * few)) & (in_row % many == out_row // (2 * few))
    again = again.astype(F32).astype(BF16)

    def receive(p):
        each(lambda k: block_in(p, k).wait_recv())
        for b in range(n_blocks // group):
            rows = land[p, b * group : (b + 1) * group].reshape(group * 16, land.shape[3])
            turned = dot(there, rows).astype(BF16).reshape(2 * few, many, land.shape[3])
            for c in range(2):
                first = c * half + p * few
                slots[first : first + few, b * many : (b + 1) * many, :] = turned[
                    c * few : (c + 1) * few
                ]

    receive(0)
    loads[0].wait()

    def core_copy(j):
        return remote(
            core_out.at[j], core_in.at[j], core_sems.at[0, j], core_sems.at[1, j], sibling
        )

    def x_copy(j):
        return remote(x_out.at[j], x_in.at[j], x_sems.at[0, j], x_sems.at[1, j], across)

    def act_copy(j):
        return remote(
            act.at[own + j], act.at[own + j], act_sems.at[0, j], act_sems.at[1, j], sibling
        )

    def act_in(j):
        return remote(
            act.at[other + j], act.at[other + j], act_sems.at[0, j], act_sems.at[1, j], sibling
        )

    def meet(j):
        core_copy(j).wait_recv()
        sums[j] = sums[j] + core_in[j].astype(F32)
        x_out[j] = sums[j].astype(BF16)
        x_copy(j).start()

    def first_sums(j):
        core_out[j] = dot(slots[other + j], w_a[other + j]).astype(BF16)
        core_copy(j).start()
        sums[j] = dot(slots[own + j], w_a[own + j])

        @pl.when(j > 0)
        def _():
            meet(j - 1)

    each(first_sums, few, 0)
    receive(1)
    each(first_sums, half, few)
    meet(half - 1)
    loads[1].wait()
    if backward:
        gate_load.wait()

    def second(e):
        leave[e] = dot_t(act[e], w_b[e]).astype(BF16)

    def finish(j):
        x_copy(j).wait_recv()
        value = sums[j] + x_in[j].astype(F32)
        if backward:
            act[own + j] = (value * gate_v[j]).astype(BF16)
        else:
            value = value + gate[own + j]
            cumulative = 0.5 + 0.5 * lax.erf(value * 0.7071067811865476)
            act[own + j] = (value * cumulative).astype(BF16)
            sums[j] = cumulative + value * (
                jnp.exp(value * value * -0.5) * 0.3989422804014327
            )
        act_copy(j).start()
        second(own + j)

        @pl.when(j > 0)
        def _():
            act_in(j - 1).wait_recv()
            second(other + j - 1)

    def back_copy(p, k):
        place = peers.step(k, 1)
        return remote(
            back.at[p, peers.flat(place)], land_back.at[p, me],
            back_sems.at[0, p, k], back_sems.at[1, p, k], place,
        )

    def back_in(p, k):
        source = peers.flat(peers.step(k, -1))
        return remote(
            back.at[p, 0], land_back.at[p, source],
            back_sems.at[0, p, k], back_sems.at[1, p, k], sibling,
        )

    def give_back(p):
        for b in range(n_blocks // group):
            rows = jnp.concatenate(
                [
                    leave[c * half + p * few : c * half + (p + 1) * few, b * many : (b + 1) * many, :]
                    for c in range(2)
                ],
                axis=0,
            ).reshape(group * 16, leave.shape[2])
            turned = dot(again, rows).astype(BF16)
            back[p, b * group : (b + 1) * group] = turned.reshape(group, 16, leave.shape[2])
        each(lambda k: back_copy(p, k).start())
        land_back[p, me] = back[p, me]

    each(finish, few + 1, 0)
    give_back(0)
    each(finish, half, few + 1)
    act_in(half - 1).wait_recv()
    second(other + half - 1)
    give_back(1)
    stores = [pltpu.make_async_copy(act, act_out, o_sem.at[1])]
    if not backward:
        stores.append(pltpu.make_async_copy(sums, gate_out, o_sem.at[0]))
    for store in stores:
        store.start()
    slots_out[...] = slots[...]
    if backward:
        across_t = (s, h, 1 - t)
        width = bias_out.shape[1]

        def bias_row(e):
            bias_all[pl.ds(e, 1), :] = jnp.sum(act[e].astype(F32), axis=0, keepdims=True)

        each(bias_row, 2 * half, 0)

        def piece(for_t):
            return bias_all[:, pl.ds(pl.multiple_of((core * n_t + for_t) * width, 128), width)]

        bias_send[...] = piece(1 - t)
        bias_copy = remote(bias_send, bias_land, b_sems.at[0], b_sems.at[1], across_t)
        bias_copy.start()
        bias_copy.wait()
        bias_out[...] = jnp.where(t == chip, piece(t), bias_land[...])
    for p in range(2):
        each(lambda k: back_in(p, k).wait_recv())
    back_out[...] = land_back[...]
    for store in stores:
        store.wait()
    for p in range(2):
        each(lambda k: block_out(p, k).wait_send())
        each(lambda k: back_copy(p, k).wait_send())
    for copy in (core_copy, x_copy, act_copy):
        each(lambda j: copy(j).wait_send(), half, 0)


def expert_pass(sizes, backward, blocks, weights, gate, bias_width=0):
    _, experts, rows, hidden = weights.shape
    devices = sizes[0] * sizes[1] * sizes[2]
    images = 2 * devices
    half = experts // 2
    vmem = pl.BlockSpec(memory_space=pltpu.VMEM)
    hbm = pl.BlockSpec(memory_space=pl.ANY)
    slots = jax.ShapeDtypeStruct((experts, images, rows), BF16)
    act = jax.ShapeDtypeStruct((experts, images, hidden), BF16)
    gate_shape = (half, images, hidden)
    returned = jax.ShapeDtypeStruct((2, devices, experts, rows), BF16)
    if backward:
        operands, in_specs = (blocks, weights, gate), [vmem, hbm, hbm]
        outs = (slots, act, returned, jax.ShapeDtypeStruct((experts, bias_width), F32))
        out_specs = (vmem, hbm, vmem, vmem)
    else:
        operands, in_specs = (blocks, weights, gate), [vmem, hbm, vmem]
        outs = (slots, act, jax.ShapeDtypeStruct(gate_shape, F32), returned)
        out_specs = (vmem, hbm, hbm, vmem)
    weight = pltpu.VMEM((experts, rows, hidden), BF16)
    chunk = pltpu.VMEM((half, images, hidden), BF16)
    block = pltpu.VMEM((2, devices, experts, rows), BF16)
    dma = pltpu.SemaphoreType.DMA
    scratch = [weight, weight]
    if backward:
        scratch.append(pltpu.VMEM(gate_shape, F32))
    scratch += [
        pltpu.VMEM(gate_shape, F32),
        pltpu.VMEM(slots.shape, BF16),
        pltpu.VMEM(act.shape, BF16),
        chunk, chunk, chunk, chunk, block,
        pltpu.VMEM(slots.shape, BF16),
        block, block,
        dma((2,)), dma((2,)), dma((2, 2, devices)), dma((2, 2, devices)),
        dma((2, half)), dma((2, half)), dma((2, half)),
    ]
    if backward:
        scratch += [
            dma((2,)),
            pltpu.VMEM((experts, hidden), F32),
            pltpu.VMEM((experts, bias_width), F32),
            pltpu.VMEM((experts, bias_width), F32),
        ]
    return pl.pallas_call(
        partial(expert_kernel, sizes, backward),
        out_shape=outs,
        in_specs=in_specs,
        out_specs=out_specs,
        scratch_shapes=scratch,
        compiler_params=pltpu.CompilerParams(
            collective_id=2 if backward else 1, has_side_effects=True, vmem_limit_bytes=VMEM_BYTES
        ),
        cost_estimate=pl.CostEstimate(
            flops=8 * images * experts * rows * hidden,
            bytes_accessed=weights.size * 2,
            transcendentals=0,
        ),
        name="experts_back" if backward else "experts_ahead",
    )(*operands)


def weight_grad_kernel(slots_0, act_0, slots_1, act_1, out, lines, pick, same):
    group, images, rows = slots_0.shape
    d_block = out.shape[0]
    n = group * d_block
    m, d = pl.program_id(0), pl.program_id(2)

    @pl.when((m == 0) & (pl.program_id(1) == 0) & (d == 0))
    def _():
        row = lax.broadcasted_iota(jnp.int32, pick.shape, 0)
        column = lax.broadcasted_iota(jnp.int32, pick.shape, 1)
        pick[...] = (column == row // group).astype(F32).astype(BF16)
        row = lax.broadcasted_iota(jnp.int32, same.shape, 0)
        column = lax.broadcasted_iota(jnp.int32, same.shape, 1)
        same[...] = (row % group == column // images).astype(F32)

    def prepare(slots):
        @pl.when(d == 0)
        def _():
            turned = slots[...].reshape(group * images, rows).astype(F32)
            lines[...] = jnp.swapaxes(turned, 0, 1).astype(BF16)

    def term(act):
        mine = lines[pl.ds(pl.multiple_of(d * d_block, d_block), d_block)]
        spread = (dot(pick[...], mine) * same[...]).astype(BF16)
        values = act[...].reshape(group * images, act.shape[2])
        out[...] = dot(spread, values).reshape(out.shape)

    @pl.when(m == 0)
    def _():
        prepare(slots_0)
        term(act_0)

    @pl.when(m == 1)
    def _():
        prepare(slots_1)
        term(act_1)


def weight_grads(slots_0, act_0, slots_1, act_1):
    experts, images, rows = slots_0.shape
    hidden = act_0.shape[2]
    group, d_block = 8, 32
    last = experts // group - 1

    def early(m, g, d):
        return jnp.where(m == 0, g, last), 0, 0

    def late(m, g, d):
        return jnp.where(m == 0, 0, g), 0, 0

    slots, act = (group, images, rows), (group, images, hidden)
    return pl.pallas_call(
        weight_grad_kernel,
        grid=(2, experts // group, rows // d_block),
        out_shape=jax.ShapeDtypeStruct((rows, 2, experts, hidden), F32),
        in_specs=[
            pl.BlockSpec(slots, early), pl.BlockSpec(act, early),
            pl.BlockSpec(slots, late), pl.BlockSpec(act, late),
        ],
        out_specs=pl.BlockSpec((d_block, 1, group, hidden), lambda m, g, d: (d, m, g, 0)),
        scratch_shapes=[
            pltpu.VMEM((rows, group * images), BF16),
            pltpu.VMEM((group * d_block, d_block), BF16),
            pltpu.VMEM((group * d_block, group * images), F32),
        ],
        compiler_params=pltpu.CompilerParams(vmem_limit_bytes=VMEM_BYTES),
        cost_estimate=pl.CostEstimate(
            flops=4 * images * experts * rows * hidden,
            bytes_accessed=8 * rows * experts * hidden,
            transcendentals=0,
        ),
        name="weight_grads",
    )(slots_0, act_0, slots_1, act_1)


def normalize(values, scale, shift):
    centered = values - jnp.mean(values, axis=-1, keepdims=True)
    variance = jnp.mean(centered * centered, axis=-1, keepdims=True)
    inverse = lax.rsqrt(variance + epsilon)
    unit_part = centered * inverse
    return (unit_part * scale + shift, unit_part, inverse)


def normalize_back(grad_output, unit_part, inverse, scale):
    scaled = grad_output * scale
    average = jnp.mean(scaled, axis=-1, keepdims=True)
    projection = jnp.mean(scaled * unit_part, axis=-1, keepdims=True)
    grad_input = inverse * (scaled - average - unit_part * projection)
    return (
        grad_input,
        jnp.sum(grad_output * unit_part, axis=(0, 1)),
        jnp.sum(grad_output, axis=(0, 1)),
    )


def to_experts(slots):
    slots = lax.all_to_all(slots, "heads", split_axis=1, concat_axis=0, tiled=True)
    slots = lax.all_to_all(slots, "shard", split_axis=2, concat_axis=0, tiled=True)
    return lax.all_gather(slots, "tensor", axis=0, tiled=True)


def to_blocks(slots, sizes):
    own, experts, width = slots.shape
    n_s, n_h, _ = sizes
    few = experts // n_h // 4
    slots = slots.reshape(own, n_h, 2, 2, few, n_s, width // n_s)
    return slots.transpose(1, 5, 3, 0, 2, 4, 6).reshape(n_h, n_s, 2, own * 2 * few, width // n_s)


def from_blocks(blocks, sizes):
    n_s, n_h, n_t = sizes
    rows = blocks.shape[3]
    blocks = jnp.sum(blocks.reshape(2, n_s, n_h, n_t, 2, 2, -1, rows).astype(F32), axis=3)
    return blocks.transpose(3, 2, 4, 0, 5, 1, 6).reshape(2, -1, n_s * rows)


def to_images(slots):
    slots = lax.psum_scatter(slots, "tensor", scatter_dimension=0, tiled=True)
    slots = lax.all_to_all(slots, "shard", split_axis=0, concat_axis=2, tiled=True)
    return lax.all_to_all(slots, "heads", split_axis=0, concat_axis=1, tiled=True)


def shards(tokens, norm_scales, norm_biases, w_attn, phi, experts, in_bias, out_bias, cotangent):
    heads_n = lax.axis_size("heads")
    sizes = tuple(lax.axis_size(name) for name in ("shard", "heads", "tensor"))
    if sizes != (4, 4, 2) or tokens.shape[0] != 8 or experts.shape[2] != 16:
        sizes = None
    group, seq_len, width = tokens.shape
    own = group // heads_n
    heads_index = lax.axis_index("heads")
    tensor_index = lax.axis_index("tensor")
    shard_index = lax.axis_index("shard")
    hidden = experts.shape[3]
    rows = experts.shape[0]
    if sizes is not None:
        n_s, n_h, n_t = sizes
        block, slot = w_attn.shape[2], phi.shape[1]
        beside = jnp.concatenate((phi, out_bias.T), axis=1)
        beside = jnp.pad(beside, ((0, 0), (0, 256 - block - 2 * slot)))
        beside = jnp.concatenate((beside[None], jnp.zeros((3, *beside.shape), BF16)), axis=0)
        packet = jnp.concatenate((w_attn, beside), axis=2)
        extra = jnp.concatenate(
            (
                in_bias.reshape(-1, 64),
                norm_scales.T,
                norm_biases.T,
            ),
            axis=1,
        )
        extra = jnp.pad(extra, ((0, 0), (128, 60)))
        attn, small, turned = gather_weights(sizes, packet, extra, experts)
        phi_full = small[:, :64]
        out_all = small[:, 64:128].T.astype(F32)
        in_full = small[:, 128:192].reshape(n_s * n_t, -1, in_bias.shape[1])
        in_full = in_full.transpose(1, 0, 2).reshape(in_bias.shape[0], -1).astype(F32)
        scales = small[:, 192:194].T.astype(F32)
        biases = small[:, 194:196].T.astype(F32)
    else:
        scales, biases, in_full = (
            lax.all_gather(norm_scales, ROWS, axis=1, tiled=True).astype(F32),
            lax.all_gather(norm_biases, ROWS, axis=1, tiled=True).astype(F32),
            lax.all_gather(in_bias, ROWS, axis=1, tiled=True).astype(F32),
        )
        attn = lax.all_gather(
            lax.all_gather(w_attn, "heads", axis=2, tiled=True), ROWS, axis=1, tiled=True
        )
        phi_full = lax.all_gather(
            lax.all_gather(phi, "heads", axis=1, tiled=True), ROWS, axis=0, tiled=True
        )
        out_rows = lax.all_gather(out_bias, "tensor", axis=1, tiled=True).astype(F32)
    e_own = experts.shape[2] // lax.axis_size("shard")
    in_local = lax.dynamic_slice_in_dim(in_full, tensor_index * hidden, hidden, 1)
    factor = HEAD_DIM ** (-0.5)
    tokens = lax.dynamic_slice_in_dim(tokens, heads_index * own, own, 0)
    cotangent = lax.dynamic_slice_in_dim(cotangent, heads_index * own, own, 0)
    n_heads = width // HEAD_DIM
    inputs = tokens.astype(F32)
    normed_one, unit_one, inverse_one = normalize(inputs, scales[0], biases[0])
    normed_one_b = normed_one.astype(BF16)
    projected = einsum("nsd,kdc->knsc", normed_one_b, attn[:3]).astype(BF16)
    query, keyed, valued = projected.reshape(3, own, seq_len, n_heads, HEAD_DIM)
    scores = einsum("nqhe,nkhe->nhqk", query, keyed) * factor
    score_peak = jnp.max(scores, axis=-1, keepdims=True)
    exponent = jnp.exp(scores - score_peak)
    probs = exponent / jnp.sum(exponent, axis=-1, keepdims=True)
    probs_b = probs.astype(BF16)
    context_b = (
        einsum("nhqk,nkhe->nqhe", probs_b, valued).astype(BF16).reshape(own, seq_len, width)
    )
    hidden_one = inputs + einsum("nsc,dc->nsd", context_b, attn[3])
    normed_two, unit_two, inverse_two = normalize(hidden_one, scales[1], biases[1])
    normed_two_b = normed_two.astype(BF16)
    logits = einsum("nsd,de->nse", normed_two_b, phi_full)
    dispatch = jax.nn.softmax(logits, axis=1)
    dispatch_b = dispatch.astype(BF16)
    combine = jax.nn.softmax(logits, axis=2)
    combine_b = combine.astype(BF16)
    slot_in = einsum("nse,nsd->ned", dispatch_b, normed_two_b).astype(BF16)
    if sizes is not None:
        slot_in, activated, gate, back = expert_pass(
            sizes, False, to_blocks(slot_in, sizes), turned, in_local[:, None, :]
        )
        slot_out = (from_blocks(back, sizes) + out_all).astype(BF16)
    else:
        slot_in = to_experts(slot_in)
        share = 1 if e_own else 0

        def meet(partial_sum):
            return lax.psum_scatter(partial_sum, "shard", scatter_dimension=share, tiled=True)

        def spread(values):
            return lax.all_gather(values, "shard", axis=share, tiled=True)

        pre = meet(einsum("ned,def->nef", slot_in, experts[:, 0]))
        if e_own:
            pre = pre + lax.dynamic_slice_in_dim(in_local, shard_index * e_own, e_own, 0)
        else:
            pre = pre + in_local
        gelu_value, gelu_back = jax.vjp(partial(jax.nn.gelu, approximate=False), pre)
        activated = spread(gelu_value.astype(BF16))
        slot_out_part = einsum("nef,def->ned", activated, experts[:, 1])
        slot_out_part = slot_out_part + jnp.where(tensor_index == 0, out_rows, 0.0)
        slot_out = to_images(slot_out_part).astype(BF16)
    output = (hidden_one + einsum("nse,ned->nsd", combine_b, slot_out)).astype(BF16)
    grad_combine = einsum("nsd,ned->nse", cotangent, slot_out)
    grad_slot = einsum("nse,nsd->ned", combine_b, cotangent).astype(BF16)
    if sizes is not None:
        grad_slot, grad_pre, back, in_bias_grad = expert_pass(
            sizes, True, to_blocks(grad_slot, sizes), turned, gate, in_bias.shape[1]
        )
        back, output = lax.optimization_barrier((back, output))
        output = lax.all_gather(output, "heads", axis=0, tiled=True)
        grad_slot_in = from_blocks(back, sizes).astype(BF16)
        experts_grad = weight_grads(slot_in, grad_pre, grad_slot, activated)
        grad_slot_sum = jnp.sum(grad_slot.astype(F32), axis=1)
    else:
        output = lax.all_gather(output, "heads", axis=0, tiled=True)
        grad_slot = to_experts(grad_slot)
        grad_act = meet(einsum("ned,def->nef", grad_slot, experts[:, 1]))
        grad_pre = spread(gelu_back(grad_act)[0].astype(BF16))
        grad_slot_in = einsum("nef,def->ned", grad_pre, experts[:, 0]).astype(BF16)
        input_term = einsum("ned,nef->def", slot_in, grad_pre)
        output_term = einsum("ned,nef->def", grad_slot, activated)
        experts_grad = jnp.stack((input_term, output_term), axis=1)
        grad_slot_in = to_images(grad_slot_in.astype(F32)).astype(BF16)
        in_bias_grad = lax.dynamic_slice_in_dim(
            lax.all_gather(jnp.sum(grad_pre.astype(F32), axis=0), "tensor", axis=1, tiled=True),
            (shard_index * lax.axis_size("tensor") + tensor_index) * in_bias.shape[1],
            in_bias.shape[1],
            1,
        )
        grad_slot_sum = jnp.sum(grad_slot.astype(F32), axis=0)
    out_bias_grad = lax.dynamic_slice_in_dim(
        grad_slot_sum,
        tensor_index * out_bias.shape[1],
        out_bias.shape[1],
        1,
    )
    grad_dispatch = einsum("nsd,ned->nse", normed_two_b, grad_slot_in)
    grad_logits = (
        dispatch * (grad_dispatch - jnp.sum(dispatch * grad_dispatch, axis=1, keepdims=True))
        + combine * (grad_combine - jnp.sum(combine * grad_combine, axis=2, keepdims=True))
    ).astype(BF16)
    phi_grad = einsum("nsd,nse->de", normed_two_b, grad_logits)
    grad_normed_two = einsum("nse,ned->nsd", dispatch_b, grad_slot_in) + einsum(
        "nse,de->nsd", grad_logits, phi_full
    )
    grad_hidden_norm, scale_two_grad, bias_two_grad = normalize_back(
        grad_normed_two, unit_two, inverse_two, scales[1]
    )
    grad_hidden = cotangent.astype(F32) + grad_hidden_norm
    grad_hidden_b = grad_hidden.astype(BF16)
    out_weight_grad = einsum("nsd,nsc->dc", grad_hidden_b, context_b)
    grad_context = einsum("nsd,dc->nsc", grad_hidden_b, attn[3]).astype(BF16)
    grad_context = grad_context.reshape(own, seq_len, n_heads, HEAD_DIM)
    grad_value = einsum("nhqk,nqhe->nkhe", probs_b, grad_context).astype(BF16)
    grad_probs = einsum("nqhe,nkhe->nhqk", grad_context, valued)
    grad_scores = (
        probs * (grad_probs - jnp.sum(probs * grad_probs, axis=-1, keepdims=True))
    ).astype(BF16)
    grad_query = (einsum("nhqk,nkhe->nqhe", grad_scores, keyed) * factor).astype(BF16)
    grad_key = (einsum("nhqk,nqhe->nkhe", grad_scores, query) * factor).astype(BF16)
    grad_proj = jnp.stack((grad_query, grad_key, grad_value)).reshape(3, own, seq_len, width)
    proj_grad = einsum("nsd,knsc->kdc", normed_one_b, grad_proj)
    grad_normed_one = einsum("knsc,kdc->nsd", grad_proj, attn[:3])
    grad_input_norm, scale_one_grad, bias_one_grad = normalize_back(
        grad_normed_one, unit_one, inverse_one, scales[0]
    )
    input_grad = (grad_hidden + grad_input_norm).astype(BF16)
    input_grad = lax.all_gather(input_grad, "heads", axis=0, tiled=True)
    attn_grad = jnp.concatenate((proj_grad, out_weight_grad[None]), axis=0)
    norms = jnp.stack((scale_one_grad, scale_two_grad, bias_one_grad, bias_two_grad))
    if sizes is not None:
        small = jnp.concatenate((phi_grad, norms.T), axis=1)
        small = jnp.pad(small, ((0, 0), (0, 128 - small.shape[1]))).astype(BF16)
        summed = reduce_grads(sizes, attn_grad.astype(BF16), small)
        attn_grad = summed[:, :, :block]
        phi_grad = summed[0, :, block : block + slot]
        norms = summed[0, :, block + slot : block + slot + 4].T
    else:
        attn_grad = lax.psum_scatter(attn_grad, ROWS, scatter_dimension=1, tiled=True)
        attn_grad = lax.psum_scatter(attn_grad, "heads", scatter_dimension=2, tiled=True)
        phi_grad = lax.psum_scatter(phi_grad, ROWS, scatter_dimension=0, tiled=True)
        phi_grad = lax.psum_scatter(phi_grad, "heads", scatter_dimension=1, tiled=True)
        norms = lax.psum(lax.psum_scatter(norms, ROWS, scatter_dimension=1, tiled=True), "heads")
    return (
        output,
        input_grad,
        norms[:2],
        norms[2:],
        attn_grad,
        phi_grad,
        experts_grad,
        in_bias_grad,
        out_bias_grad,
    )


def solution(mesh):
    images = P(ROWS, None, None)
    return jax.shard_map(
        shards,
        mesh=mesh,
        in_specs=(
            images,
            P(None, ROWS),
            P(None, ROWS),
            P(None, ROWS, "heads"),
            P(ROWS, "heads"),
            P("shard", None, "heads", "tensor"),
            P("heads", ROWS),
            P("heads", ROWS),
            images,
        ),
        out_specs=(
            images,
            images,
            P(None, ROWS),
            P(None, ROWS),
            P(None, ROWS, "heads"),
            P(ROWS, "heads"),
            P("shard", None, "heads", "tensor"),
            P("heads", ROWS),
            P("heads", ROWS),
        ),
        check_vma=False,
    )
```

```python
from functools import partial

import jax
import jax.numpy as jnp
from jax import lax
from jax.experimental import pallas as pl
from jax.experimental.pallas import tpu as pltpu
from jax.sharding import PartitionSpec as P

HEAD_DIM = 64
F32 = jnp.float32
BF16 = jnp.bfloat16
ROWS = ("shard", "tensor")
MESH = pl.DeviceIdType.MESH
VMEM_BYTES = 58 * 1024 * 1024
epsilon = 1e-06
einsum = partial(jnp.einsum, preferred_element_type=F32)


def dot(a, b):
    return lax.dot_general(a, b, (((1,), (0,)), ((), ())), preferred_element_type=F32)


def dot_t(a, b):
    return lax.dot_general(a, b, (((1,), (1,)), ((), ())), preferred_element_type=F32)


def swap_matrix(n):
    out = lax.broadcasted_iota(jnp.int32, (n * n, n * n), 0)
    row = lax.broadcasted_iota(jnp.int32, (n * n, n * n), 1)
    return ((out // n == row % n) & (out % n == row // n)).astype(F32).astype(BF16)


class Peers:
    def __init__(self, sizes):
        self.sizes = sizes
        self.at = tuple(lax.axis_index(name) for name in ("shard", "heads", "tensor"))
        self.count = sizes[0] * sizes[1] * sizes[2]

    def flat(self, place):
        return (place[0] * self.sizes[1] + place[1]) * self.sizes[2] + place[2]

    def step(self, k, sign):
        _, n_h, n_t = self.sizes
        steps = (k // (n_h * n_t), (k // n_t) % n_h, k % n_t)
        return tuple(
            lax.rem(at + n + sign * d, n) for at, n, d in zip(self.at, self.sizes, steps)
        )

    def greet_all(self):
        barrier = pltpu.get_barrier_semaphore()

        def signal(k, carry):
            pl.semaphore_signal(barrier, inc=1, device_id=self.step(k, 1), device_id_type=MESH)
            return carry

        lax.fori_loop(1, self.count, signal, 0)
        pl.semaphore_wait(barrier, self.count - 1)


def remote(src, dst, send, recv, place):
    return pltpu.make_async_remote_copy(
        src_ref=src, dst_ref=dst, send_sem=send, recv_sem=recv, device_id=place, device_id_type=MESH
    )


def plane(sizes):
    n_s, n_h, n_t = sizes
    s, h, t = (lax.axis_index(name) for name in ("shard", "heads", "tensor"))
    core, chip = lax.rem(s, 2), s // 2
    sibling = (s + 1 - 2 * core, h, t)
    across_x = (lax.rem(s + 2, n_s), h, t)
    across_y = (s, h, 1 - t)
    line = [(s, lax.rem(h + d, n_h), t) for d in range(n_h)]
    barrier = pltpu.get_barrier_semaphore()
    others = [sibling, across_x, across_y] + line[1:]
    for place in others:
        pl.semaphore_signal(barrier, inc=1, device_id=place, device_id_type=MESH)
    pl.semaphore_wait(barrier, len(others))
    return (s, h, t), core, chip, sibling, across_x, across_y, line


def pair_matrix(block, wide, transposed):
    shape = (2 * block, 2 * wide) if transposed else (2 * wide, 2 * block)
    tight = lax.broadcasted_iota(jnp.int32, shape, 0 if transposed else 1)
    padded = lax.broadcasted_iota(jnp.int32, shape, 1 if transposed else 0)
    second = padded >= wide
    lane = jnp.where(second, padded - wide, padded)
    same = (lane < block) & (tight == jnp.where(second, lane + block, lane))
    return same.astype(F32).astype(BF16)


def gather_kernel(
    sizes, packet, extra, experts, w_out, small_out, turned,
    w, small, lined, tile_in, tile_out,
    z_send, z_recv, x_sems, y_sems, d_sems, c_sems, t_sems, o_sems,
):
    (s, h, t), core, chip, sibling, across_x, across_y, line = plane(sizes)
    n_k, rows, wide = packet.shape
    n_h, n_t = sizes[1], sizes[2]
    width = w.shape[2]
    block = width // n_h
    side = 16
    n_tiles = experts.shape[0] // side
    depth = tile_in.shape[0]
    halves = ((0, rows // 2), (rows // 2, rows // 2))

    def z_hop(k, origin, up):
        place = line[1] if up else line[n_h - 1]
        return remote(
            lined.at[origin, k], lined.at[origin, k],
            z_send.at[k, origin, up], z_recv.at[k, origin], place,
        )

    def relay(k, d):
        @pl.when(h >= d)
        def _():
            z_hop(k, h - d, 1).wait_recv()

            @pl.when(h < n_h - 1)
            def _():
                z_hop(k, h - d, 1).start()

        @pl.when(h + d < n_h)
        def _():
            z_hop(k, h + d, 0).wait_recv()

            @pl.when(h > 0)
            def _():
                z_hop(k, h + d, 0).start()

    chunks = (0, 2, 1, 3)
    lined[h] = packet[...]
    for k in chunks:
        @pl.when(h < n_h - 1)
        def _():
            z_hop(k, h, 1).start()

        @pl.when(h > 0)
        def _():
            z_hop(k, h, 0).start()

    def load(i):
        return pltpu.make_async_copy(
            experts.at[pl.ds((i % n_tiles) * side, side), i // n_tiles],
            tile_in.at[i % depth],
            t_sems.at[0, i % depth],
        )

    def store(i):
        return pltpu.make_async_copy(
            tile_out.at[i % depth],
            turned.at[i // n_tiles, :, pl.ds((i % n_tiles) * side, side)],
            t_sems.at[1, i % depth],
        )

    for i in range(depth - 1):
        load(i).start()
    swap = swap_matrix(side)
    done = [0]

    def turn(count):
        def step(i, carry):
            load(i).wait()

            @pl.when(i + depth - 1 < 2 * n_tiles)
            def _():
                load(i + depth - 1).start()

            @pl.when(i >= depth)
            def _():
                store(i - depth).wait()

            rows_in = tile_in[i % depth].reshape(side * side, tile_in.shape[3])
            tile_out[i % depth] = dot(swap, rows_in).astype(BF16).reshape(tile_out.shape[1:])
            store(i).start()
            return carry

        last = min(done[0] + count, 2 * n_tiles)
        lax.fori_loop(done[0], last, step, 0)
        done[0] = last

    pair = pair_matrix(block, wide, False)
    shape = (n_h * wide, small.shape[1])
    row = lax.broadcasted_iota(jnp.int32, shape, 0)
    column = lax.broadcasted_iota(jnp.int32, shape, 1)
    lane, of = row % wide - block, row // wide
    beside = (lane >= 0) & (lane < 16) & (column == of * 16 + lane)
    beside |= (lane >= 16) & (lane < 32) & (column == n_h * 16 + of * 16 + lane - 16)
    beside = beside.astype(F32).astype(BF16)

    def at(k, place):
        first = pl.multiple_of((place[0] * n_t + place[2]) * rows, 16)
        lines = pl.ds(first, rows)
        return small.at[lines] if k == n_k else w.at[k, lines]

    def hop(q, origin, place, sems, j):
        return remote(at(q, origin), at(q, origin), sems.at[0, j], sems.at[1, j], place)

    def half_hop(q, origin, place, half):
        part = at(q, origin).at[pl.ds(*halves[half])]
        j = 2 * q + half
        return remote(part, part, d_sems.at[0, j], d_sems.at[1, j], place)

    me = (s, h, t)
    from_d = (across_x[0], h, across_y[2])
    sent = []

    def send(copy):
        copy.start()
        sent.append(copy)

    def assemble(k):
        for i in range(0, n_h, 2):
            lines = jnp.concatenate([lined[i, k], lined[i + 1, k]], axis=1)
            at(k, me)[:, i * block : (i + 2) * block] = dot(lines, pair).astype(BF16)
        if k == 0:
            lines = jnp.concatenate([lined[i, k] for i in range(n_h)], axis=1)
            at(n_k, me)[...] = (dot(lines, beside) + extra[...].astype(F32)).astype(BF16)
        for q in members(k):
            send(hop(q, me, across_x, x_sems, q))
            send(hop(q, me, across_y, y_sems, q))
            send(hop(q, me, sibling, c_sems, 4 * q))

    def members(k):
        return (0, n_k) if k == 0 else (k,)

    def relay_xy(k):
        for q in members(k):
            hop(q, across_x, across_x, x_sems, q).wait_recv()
            send(half_hop(q, across_x, across_y, 0))
            send(hop(q, across_x, sibling, c_sems, 4 * q + 1))
            hop(q, across_y, across_y, y_sems, q).wait_recv()
            send(half_hop(q, across_y, across_x, 1))
            send(hop(q, across_y, sibling, c_sems, 4 * q + 2))

    def relay_d(k):
        for q in members(k):
            half_hop(q, from_d, across_y, 0).wait_recv()
            half_hop(q, from_d, across_x, 1).wait_recv()
            send(hop(q, from_d, sibling, c_sems, 4 * q + 3))

    for wave in range(n_k + n_h - 2):
        for d in range(1, n_h):
            if 0 <= wave - d + 1 < n_k:
                relay(chunks[wave - d + 1], d)
        turn(2)
        i = wave - n_h + 2
        if i >= 0:
            assemble(chunks[i])
            if i >= 1:
                relay_xy(chunks[i - 1])
            if i >= 2:
                relay_d(chunks[i - 2])
            turn(2)
    relay_xy(chunks[-1])
    relay_d(chunks[-2])
    turn(2 * n_tiles)
    relay_d(chunks[-1])
    stores = []
    for k in chunks:
        for q in members(k):
            for j in range(4):
                hop(q, me, sibling, c_sems, 4 * q + j).wait_recv()
            if q == n_k:
                stores.append(pltpu.make_async_copy(small, small_out, o_sems.at[q]))
            else:
                stores.append(pltpu.make_async_copy(w.at[q], w_out.at[q], o_sems.at[q]))
            stores[-1].start()
    for copy in sent:
        copy.wait_send()
    for origin in range(n_h):
        @pl.when((origin <= h) & (h < n_h - 1))
        def _():
            for k in range(n_k):
                z_hop(k, origin, 1).wait_send()

        @pl.when((origin >= h) & (h > 0))
        def _():
            for k in range(n_k):
                z_hop(k, origin, 0).wait_send()

    for i in range(depth):
        store(2 * n_tiles - depth + i).wait()
    for copy in stores:
        copy.wait()


def gather_weights(sizes, packet, extra, experts):
    n_k, rows, wide = packet.shape
    n_s, n_h, n_t = sizes
    width = n_s * n_t * rows
    vmem = pl.BlockSpec(memory_space=pltpu.VMEM)
    hbm = pl.BlockSpec(memory_space=pl.ANY)
    dma = pltpu.SemaphoreType.DMA
    hidden = experts.shape[3]
    small = (width, extra.shape[1])
    return pl.pallas_call(
        partial(gather_kernel, sizes),
        out_shape=(
            jax.ShapeDtypeStruct((n_k, width, width), BF16),
            jax.ShapeDtypeStruct(small, BF16),
            jax.ShapeDtypeStruct((2, experts.shape[2], experts.shape[0], hidden), BF16),
        ),
        in_specs=[vmem, vmem, hbm],
        out_specs=(hbm, hbm, hbm),
        scratch_shapes=[
            pltpu.VMEM((n_k, width, width), BF16),
            pltpu.VMEM(small, BF16),
            pltpu.VMEM((n_h, n_k, rows, wide), BF16),
            pltpu.VMEM((4, 16, 16, hidden), BF16),
            pltpu.VMEM((4, 16, 16, hidden), BF16),
            dma((n_k, n_h, 2)), dma((n_k, n_h)), dma((2, n_k + 1)), dma((2, n_k + 1)),
            dma((2, 2 * (n_k + 1))), dma((2, 4 * (n_k + 1))), dma((2, 4)), dma((n_k + 1,)),
        ],
        compiler_params=pltpu.CompilerParams(
            collective_id=3, has_side_effects=True, vmem_limit_bytes=VMEM_BYTES
        ),
        name="gather_weights",
    )(packet, extra, experts)


def reduce_kernel(
    sizes, grads, small, out, core_in, core_small, met, met_small,
    d_in, d_small, x_in, x_small, y_in, y_small, pieces, z_in,
    c_sems, d_sems, x_sems, y_sems, z_sems,
):
    (s, h, t), core, chip, sibling, across_x, across_y, line = plane(sizes)
    n_k, width, _ = grads.shape
    n_s, n_h, n_t = sizes
    rows = width // (n_s * n_t)
    wide = pieces.shape[3]
    pair = n_t * rows
    half = rows // 2
    halves = (pl.ds(0, half), pl.ds(half, half))
    chunks = (0, 2, 1, 3)

    def members(k):
        return (0, n_k) if k == 0 else (k,)

    def pick(q, large, little):
        return little if q == n_k else large.at[q]

    def core_copy(q, x):
        first = pl.multiple_of((2 * x + 1 - core) * pair, 16)
        return remote(
            pick(q, grads, small).at[pl.ds(first, pair)],
            pick(q, core_in, core_small).at[x],
            c_sems.at[0, 2 * q + x], c_sems.at[1, 2 * q + x], sibling,
        )

    for k in chunks:
        for q in members(k):
            for x in range(2):
                core_copy(q, x).start()
    joined = pair_matrix(width // n_h, wide, True)
    shape = (small.shape[1], n_h * wide)
    row = lax.broadcasted_iota(jnp.int32, shape, 0)
    column = lax.broadcasted_iota(jnp.int32, shape, 1)
    lane, of = column % wide - width // n_h, column // wide
    beside = (lane >= 0) & (lane < 16) & (row == of * 16 + lane)
    beside |= (lane >= 16) & (lane < 20) & (row == n_h * 16 + lane - 16)
    beside = beside.astype(F32).astype(BF16)
    to_d, to_x, to_y = (d_in, d_small), (x_in, x_small), (y_in, y_small)
    sent = []

    def hop(q, kind, part, source, place):
        sems = {id(to_d): d_sems, id(to_x): x_sems, id(to_y): y_sems}[id(kind)]
        target = pick(q, *kind)
        target = target.at[part] if kind is to_d else target.at[halves[part]]
        j = 2 * q + part
        return remote(source, target, sems.at[0, j], sems.at[1, j], place)

    def send(copy):
        copy.start()
        sent.append(copy)

    def part_of(q, x, y, part):
        return pick(q, met, met_small).at[x, y].at[halves[part]]

    def arrived(q, kind, part):
        hop(q, kind, part, part_of(q, 0, 0, part), sibling).wait_recv()

    def open_up(q):
        part = pick(q, met, met_small)
        for x in range(2):
            core_copy(q, x).wait_recv()
            first = pl.multiple_of((2 * x + core) * pair, 16)
            own = pick(q, grads, small)[pl.ds(first, pair)].astype(F32)
            total = own + pick(q, core_in, core_small)[x].astype(F32)
            part[x] = total.astype(BF16).reshape(n_t, rows, total.shape[1])
        send(hop(q, to_d, 0, part_of(q, 1 - chip, 1 - t, 0), across_x))
        send(hop(q, to_d, 1, part_of(q, 1 - chip, 1 - t, 1), across_y))
        send(hop(q, to_x, 0, part_of(q, 1 - chip, t, 0), across_x))
        send(hop(q, to_y, 1, part_of(q, chip, 1 - t, 1), across_y))

    def pass_on(q):
        for part, kind, x, y, place in (
            (0, to_y, chip, 1 - t, across_y),
            (1, to_x, 1 - chip, t, across_x),
        ):
            arrived(q, to_d, part)
            block = part_of(q, x, y, part)
            total = block[...].astype(F32) + pick(q, *to_d)[part].astype(F32)
            block[...] = total.astype(BF16)
            send(hop(q, kind, part, block, place))

    def whole(q):
        for kind in (to_x, to_y):
            for part in range(2):
                arrived(q, kind, part)
        total = pick(q, met, met_small)[chip, t].astype(F32) + pick(q, *to_x)[...].astype(F32)
        return (total + pick(q, *to_y)[...].astype(F32)).astype(BF16)

    def z_copy(k, d):
        return remote(
            pieces.at[line[d][1], k], z_in.at[h, k], z_sems.at[0, k, d], z_sems.at[1, k, d], line[d]
        )

    def share_out(k):
        value = whole(k)
        columns = width // n_h
        if k == 0:
            little = dot(whole(n_k), beside)
        for i in range(0, n_h, 2):
            lanes = dot(value[:, i * columns : (i + 2) * columns], joined)
            if k == 0:
                lanes = lanes + little[:, i * wide : (i + 2) * wide]
            pieces[i, k] = lanes[:, :wide].astype(BF16)
            pieces[i + 1, k] = lanes[:, wide:].astype(BF16)
        for d in range(n_h - 1, 0, -1):
            z_copy(k, d).start()

    for i in range(n_k + 2):
        if i < n_k:
            for q in members(chunks[i]):
                open_up(q)
        if 0 <= i - 1 < n_k:
            for q in members(chunks[i - 1]):
                pass_on(q)
        if i >= 2:
            share_out(chunks[i - 2])
    for k in chunks:
        total = pieces[h, k].astype(F32)
        for d in range(1, n_h):
            z_copy(k, d).wait_recv()
        for d in range(1, n_h):
            total = total + z_in[line[d][1], k].astype(F32)
        out[k] = total
    for k in chunks:
        for q in members(k):
            for x in range(2):
                core_copy(q, x).wait_send()
    for copy in sent:
        copy.wait_send()
    for k in range(n_k):
        for d in range(1, n_h):
            z_copy(k, d).wait_send()


def reduce_grads(sizes, grads, small):
    n_k, width, _ = grads.shape
    n_s, n_h, n_t = sizes
    rows, wide, thin = width // (n_s * n_t), 256, small.shape[1]
    vmem = pl.BlockSpec(memory_space=pltpu.VMEM)
    dma = pltpu.SemaphoreType.DMA

    def buffers(*lead):
        return [
            pltpu.VMEM((n_k, *lead, width), BF16),
            pltpu.VMEM((*lead, thin), BF16),
        ]

    return pl.pallas_call(
        partial(reduce_kernel, sizes),
        out_shape=jax.ShapeDtypeStruct((n_k, rows, wide), F32),
        in_specs=[vmem, vmem],
        out_specs=vmem,
        scratch_shapes=[
            *buffers(2, n_t * rows), *buffers(2, n_t, rows),
            *buffers(2, rows // 2), *buffers(rows), *buffers(rows),
            pltpu.VMEM((n_h, n_k, rows, wide), BF16),
            pltpu.VMEM((n_h, n_k, rows, wide), BF16),
            dma((2, 2 * (n_k + 1))), dma((2, 2 * (n_k + 1))), dma((2, 2 * (n_k + 1))),
            dma((2, 2 * (n_k + 1))), dma((2, n_k, n_h)),
        ],
        compiler_params=pltpu.CompilerParams(
            collective_id=4, has_side_effects=True, vmem_limit_bytes=VMEM_BYTES
        ),
        name="reduce_grads",
    )(grads, small)


def expert_kernel(sizes, backward, *refs):
    if backward:
        (blocks, weights, gate, slots_out, act_out, back_out, bias_out,
         w_a, w_b, gate_v, sums, slots, act, core_out, core_in, x_out, x_in, land, leave, back, land_back,
         w_sem, o_sem, in_sems, back_sems, core_sems, x_sems, act_sems, b_sems,
         bias_all, bias_send, bias_land) = refs
    else:
        (blocks, weights, gate, slots_out, act_out, gate_out, back_out,
         w_a, w_b, sums, slots, act, core_out, core_in, x_out, x_in, land, leave, back, land_back,
         w_sem, o_sem, in_sems, back_sems, core_sems, x_sems, act_sems) = refs
    peers = Peers(sizes)
    s, h, t = peers.at
    n_s, n_h, n_t = sizes
    me = peers.flat(peers.at)
    core, chip = lax.rem(s, 2), s // 2
    sibling = (s + 1 - 2 * core, h, t)
    across = (lax.rem(s + 2, n_s), h, t)
    half = act.shape[0] // 2
    own, other = core * half, (1 - core) * half
    n_blocks = peers.count
    first = 1 if backward else 0
    loads = [
        pltpu.make_async_copy(weights.at[first], w_a, w_sem.at[0]),
        pltpu.make_async_copy(weights.at[1 - first], w_b, w_sem.at[1]),
    ]
    for load in loads:
        load.start()
    if backward:
        gate_load = pltpu.make_async_copy(gate, gate_v, o_sem.at[0])
        gate_load.start()
    peers.greet_all()

    def block_out(p, k):
        place = peers.step(k, 1)
        return remote(
            blocks.at[place[1], place[0], p], land.at[p, me],
            in_sems.at[0, p, k], in_sems.at[1, p, k], place,
        )

    def block_in(p, k):
        source = peers.flat(peers.step(k, -1))
        return remote(
            blocks.at[0, 0, p], land.at[p, source], in_sems.at[0, p, k], in_sems.at[1, p, k], sibling
        )

    def each(function, count=n_blocks, start=1):
        lax.fori_loop(start, count, lambda k, carry: (function(k), carry)[1], 0)

    for p in range(2):
        each(lambda k: block_out(p, k).start())
        land[p, me] = blocks[h, s, p]
    few = half // 2
    group = 16
    many = 2 * group
    out_row = lax.broadcasted_iota(jnp.int32, (16 * group, 16 * group), 0)
    in_row = lax.broadcasted_iota(jnp.int32, (16 * group, 16 * group), 1)
    there = (out_row // many == in_row % (2 * few)) & (out_row % many == in_row // (2 * few))
    there = there.astype(F32).astype(BF16)
    again = (in_row // many == out_row % (2 * few)) & (in_row % many == out_row // (2 * few))
    again = again.astype(F32).astype(BF16)

    def receive(p):
        each(lambda k: block_in(p, k).wait_recv())
        for b in range(n_blocks // group):
            rows = land[p, b * group : (b + 1) * group].reshape(group * 16, land.shape[3])
            turned = dot(there, rows).astype(BF16).reshape(2 * few, many, land.shape[3])
            for c in range(2):
                first = c * half + p * few
                slots[first : first + few, b * many : (b + 1) * many, :] = turned[
                    c * few : (c + 1) * few
                ]

    receive(0)
    loads[0].wait()

    def core_copy(j):
        return remote(
            core_out.at[j], core_in.at[j], core_sems.at[0, j], core_sems.at[1, j], sibling
        )

    def x_copy(j):
        return remote(x_out.at[j], x_in.at[j], x_sems.at[0, j], x_sems.at[1, j], across)

    def act_copy(j):
        return remote(
            act.at[own + j], act.at[own + j], act_sems.at[0, j], act_sems.at[1, j], sibling
        )

    def act_in(j):
        return remote(
            act.at[other + j], act.at[other + j], act_sems.at[0, j], act_sems.at[1, j], sibling
        )

    def meet(j):
        core_copy(j).wait_recv()
        sums[j] = sums[j] + core_in[j].astype(F32)
        x_out[j] = sums[j].astype(BF16)
        x_copy(j).start()

    def first_sums(j):
        core_out[j] = dot(slots[other + j], w_a[other + j]).astype(BF16)
        core_copy(j).start()
        sums[j] = dot(slots[own + j], w_a[own + j])

        @pl.when(j > 0)
        def _():
            meet(j - 1)

    each(first_sums, few, 0)
    receive(1)
    each(first_sums, half, few)
    meet(half - 1)
    loads[1].wait()
    if backward:
        gate_load.wait()

    def second(e):
        leave[e] = dot_t(act[e], w_b[e]).astype(BF16)

    def finish(j):
        x_copy(j).wait_recv()
        value = sums[j] + x_in[j].astype(F32)
        if backward:
            act[own + j] = (value * gate_v[j]).astype(BF16)
        else:
            value = value + gate[own + j]
            cumulative = 0.5 + 0.5 * lax.erf(value * 0.7071067811865476)
            act[own + j] = (value * cumulative).astype(BF16)
            sums[j] = cumulative + value * (
                jnp.exp(value * value * -0.5) * 0.3989422804014327
            )
        act_copy(j).start()
        second(own + j)

        @pl.when(j > 0)
        def _():
            act_in(j - 1).wait_recv()
            second(other + j - 1)

    def back_copy(p, k):
        place = peers.step(k, 1)
        return remote(
            back.at[p, peers.flat(place)], land_back.at[p, me],
            back_sems.at[0, p, k], back_sems.at[1, p, k], place,
        )

    def back_in(p, k):
        source = peers.flat(peers.step(k, -1))
        return remote(
            back.at[p, 0], land_back.at[p, source],
            back_sems.at[0, p, k], back_sems.at[1, p, k], sibling,
        )

    def give_back(p):
        for b in range(n_blocks // group):
            rows = jnp.concatenate(
                [
                    leave[c * half + p * few : c * half + (p + 1) * few, b * many : (b + 1) * many, :]
                    for c in range(2)
                ],
                axis=0,
            ).reshape(group * 16, leave.shape[2])
            turned = dot(again, rows).astype(BF16)
            back[p, b * group : (b + 1) * group] = turned.reshape(group, 16, leave.shape[2])
        each(lambda k: back_copy(p, k).start())
        land_back[p, me] = back[p, me]

    each(finish, few + 1, 0)
    give_back(0)
    each(finish, half, few + 1)
    act_in(half - 1).wait_recv()
    second(other + half - 1)
    give_back(1)
    stores = [pltpu.make_async_copy(act, act_out, o_sem.at[1])]
    if not backward:
        stores.append(pltpu.make_async_copy(sums, gate_out, o_sem.at[0]))
    for store in stores:
        store.start()
    slots_out[...] = slots[...]
    if backward:
        across_t = (s, h, 1 - t)
        width = bias_out.shape[1]

        def bias_row(e):
            bias_all[pl.ds(e, 1), :] = jnp.sum(act[e].astype(F32), axis=0, keepdims=True)

        each(bias_row, 2 * half, 0)

        def piece(for_t):
            return bias_all[:, pl.ds(pl.multiple_of((core * n_t + for_t) * width, 128), width)]

        bias_send[...] = piece(1 - t)
        bias_copy = remote(bias_send, bias_land, b_sems.at[0], b_sems.at[1], across_t)
        bias_copy.start()
        bias_copy.wait()
        bias_out[...] = jnp.where(t == chip, piece(t), bias_land[...])
    for p in range(2):
        each(lambda k: back_in(p, k).wait_recv())
    back_out[...] = land_back[...]
    for store in stores:
        store.wait()
    for p in range(2):
        each(lambda k: block_out(p, k).wait_send())
        each(lambda k: back_copy(p, k).wait_send())
    for copy in (core_copy, x_copy, act_copy):
        each(lambda j: copy(j).wait_send(), half, 0)


def expert_pass(sizes, backward, blocks, weights, gate, bias_width=0):
    _, experts, rows, hidden = weights.shape
    devices = sizes[0] * sizes[1] * sizes[2]
    images = 2 * devices
    half = experts // 2
    vmem = pl.BlockSpec(memory_space=pltpu.VMEM)
    hbm = pl.BlockSpec(memory_space=pl.ANY)
    slots = jax.ShapeDtypeStruct((experts, images, rows), BF16)
    act = jax.ShapeDtypeStruct((experts, images, hidden), BF16)
    gate_shape = (half, images, hidden)
    returned = jax.ShapeDtypeStruct((2, devices, experts, rows), BF16)
    if backward:
        operands, in_specs = (blocks, weights, gate), [vmem, hbm, hbm]
        outs = (slots, act, returned, jax.ShapeDtypeStruct((experts, bias_width), F32))
        out_specs = (vmem, hbm, vmem, vmem)
    else:
        operands, in_specs = (blocks, weights, gate), [vmem, hbm, vmem]
        outs = (slots, act, jax.ShapeDtypeStruct(gate_shape, F32), returned)
        out_specs = (vmem, hbm, hbm, vmem)
    weight = pltpu.VMEM((experts, rows, hidden), BF16)
    chunk = pltpu.VMEM((half, images, hidden), BF16)
    block = pltpu.VMEM((2, devices, experts, rows), BF16)
    dma = pltpu.SemaphoreType.DMA
    scratch = [weight, weight]
    if backward:
        scratch.append(pltpu.VMEM(gate_shape, F32))
    scratch += [
        pltpu.VMEM(gate_shape, F32),
        pltpu.VMEM(slots.shape, BF16),
        pltpu.VMEM(act.shape, BF16),
        chunk, chunk, chunk, chunk, block,
        pltpu.VMEM(slots.shape, BF16),
        block, block,
        dma((2,)), dma((2,)), dma((2, 2, devices)), dma((2, 2, devices)),
        dma((2, half)), dma((2, half)), dma((2, half)),
    ]
    if backward:
        scratch += [
            dma((2,)),
            pltpu.VMEM((experts, hidden), F32),
            pltpu.VMEM((experts, bias_width), F32),
            pltpu.VMEM((experts, bias_width), F32),
        ]
    return pl.pallas_call(
        partial(expert_kernel, sizes, backward),
        out_shape=outs,
        in_specs=in_specs,
        out_specs=out_specs,
        scratch_shapes=scratch,
        compiler_params=pltpu.CompilerParams(
            collective_id=2 if backward else 1, has_side_effects=True, vmem_limit_bytes=VMEM_BYTES
        ),
        cost_estimate=pl.CostEstimate(
            flops=8 * images * experts * rows * hidden,
            bytes_accessed=weights.size * 2,
            transcendentals=0,
        ),
        name="experts_back" if backward else "experts_ahead",
    )(*operands)


def weight_grad_kernel(slots_0, act_0, slots_1, act_1, out, lines, pick, same):
    group, images, rows = slots_0.shape
    d_block = out.shape[0]
    n = group * d_block
    m, d = pl.program_id(0), pl.program_id(2)

    @pl.when((m == 0) & (pl.program_id(1) == 0) & (d == 0))
    def _():
        row = lax.broadcasted_iota(jnp.int32, pick.shape, 0)
        column = lax.broadcasted_iota(jnp.int32, pick.shape, 1)
        pick[...] = (column == row // group).astype(F32).astype(BF16)
        row = lax.broadcasted_iota(jnp.int32, same.shape, 0)
        column = lax.broadcasted_iota(jnp.int32, same.shape, 1)
        same[...] = (row % group == column // images).astype(F32)

    def prepare(slots):
        @pl.when(d == 0)
        def _():
            turned = slots[...].reshape(group * images, rows).astype(F32)
            lines[...] = jnp.swapaxes(turned, 0, 1).astype(BF16)

    def term(act):
        mine = lines[pl.ds(pl.multiple_of(d * d_block, d_block), d_block)]
        spread = (dot(pick[...], mine) * same[...]).astype(BF16)
        values = act[...].reshape(group * images, act.shape[2])
        out[...] = dot(spread, values).reshape(out.shape)

    @pl.when(m == 0)
    def _():
        prepare(slots_0)
        term(act_0)

    @pl.when(m == 1)
    def _():
        prepare(slots_1)
        term(act_1)


def weight_grads(slots_0, act_0, slots_1, act_1):
    experts, images, rows = slots_0.shape
    hidden = act_0.shape[2]
    group, d_block = 8, 96
    last = experts // group - 1

    def early(m, g, d):
        return jnp.where(m == 0, g, last), 0, 0

    def late(m, g, d):
        return jnp.where(m == 0, 0, g), 0, 0

    slots, act = (group, images, rows), (group, images, hidden)
    return pl.pallas_call(
        weight_grad_kernel,
        grid=(2, experts // group, rows // d_block),
        out_shape=jax.ShapeDtypeStruct((rows, 2, experts, hidden), F32),
        in_specs=[
            pl.BlockSpec(slots, early), pl.BlockSpec(act, early),
            pl.BlockSpec(slots, late), pl.BlockSpec(act, late),
        ],
        out_specs=pl.BlockSpec((d_block, 1, group, hidden), lambda m, g, d: (d, m, g, 0)),
        scratch_shapes=[
            pltpu.VMEM((rows, group * images), BF16),
            pltpu.VMEM((group * d_block, d_block), BF16),
            pltpu.VMEM((group * d_block, group * images), F32),
        ],
        compiler_params=pltpu.CompilerParams(vmem_limit_bytes=VMEM_BYTES),
        cost_estimate=pl.CostEstimate(
            flops=4 * images * experts * rows * hidden,
            bytes_accessed=8 * rows * experts * hidden,
            transcendentals=0,
        ),
        name="weight_grads",
    )(slots_0, act_0, slots_1, act_1)


def normalize(values, scale, shift):
    centered = values - jnp.mean(values, axis=-1, keepdims=True)
    variance = jnp.mean(centered * centered, axis=-1, keepdims=True)
    inverse = lax.rsqrt(variance + epsilon)
    unit_part = centered * inverse
    return (unit_part * scale + shift, unit_part, inverse)


def normalize_back(grad_output, unit_part, inverse, scale):
    scaled = grad_output * scale
    average = jnp.mean(scaled, axis=-1, keepdims=True)
    projection = jnp.mean(scaled * unit_part, axis=-1, keepdims=True)
    grad_input = inverse * (scaled - average - unit_part * projection)
    return (
        grad_input,
        jnp.sum(grad_output * unit_part, axis=(0, 1)),
        jnp.sum(grad_output, axis=(0, 1)),
    )


def to_experts(slots):
    slots = lax.all_to_all(slots, "heads", split_axis=1, concat_axis=0, tiled=True)
    slots = lax.all_to_all(slots, "shard", split_axis=2, concat_axis=0, tiled=True)
    return lax.all_gather(slots, "tensor", axis=0, tiled=True)


def to_blocks(slots, sizes):
    own, experts, width = slots.shape
    n_s, n_h, _ = sizes
    few = experts // n_h // 4
    slots = slots.reshape(own, n_h, 2, 2, few, n_s, width // n_s)
    return slots.transpose(1, 5, 3, 0, 2, 4, 6).reshape(n_h, n_s, 2, own * 2 * few, width // n_s)


def from_blocks(blocks, sizes):
    n_s, n_h, n_t = sizes
    rows = blocks.shape[3]
    blocks = jnp.sum(blocks.reshape(2, n_s, n_h, n_t, 2, 2, -1, rows).astype(F32), axis=3)
    return blocks.transpose(3, 2, 4, 0, 5, 1, 6).reshape(2, -1, n_s * rows)


def to_images(slots):
    slots = lax.psum_scatter(slots, "tensor", scatter_dimension=0, tiled=True)
    slots = lax.all_to_all(slots, "shard", split_axis=0, concat_axis=2, tiled=True)
    return lax.all_to_all(slots, "heads", split_axis=0, concat_axis=1, tiled=True)


def shards(tokens, norm_scales, norm_biases, w_attn, phi, experts, in_bias, out_bias, cotangent):
    heads_n = lax.axis_size("heads")
    sizes = tuple(lax.axis_size(name) for name in ("shard", "heads", "tensor"))
    if sizes != (4, 4, 2) or tokens.shape[0] != 8 or experts.shape[2] != 16:
        sizes = None
    group, seq_len, width = tokens.shape
    own = group // heads_n
    heads_index = lax.axis_index("heads")
    tensor_index = lax.axis_index("tensor")
    shard_index = lax.axis_index("shard")
    hidden = experts.shape[3]
    rows = experts.shape[0]
    if sizes is not None:
        n_s, n_h, n_t = sizes
        block, slot = w_attn.shape[2], phi.shape[1]
        beside = jnp.concatenate((phi, out_bias.T), axis=1)
        beside = jnp.pad(beside, ((0, 0), (0, 256 - block - 2 * slot)))
        beside = jnp.concatenate((beside[None], jnp.zeros((3, *beside.shape), BF16)), axis=0)
        packet = jnp.concatenate((w_attn, beside), axis=2)
        extra = jnp.concatenate(
            (
                in_bias.reshape(-1, 64),
                norm_scales.T,
                norm_biases.T,
            ),
            axis=1,
        )
        extra = jnp.pad(extra, ((0, 0), (128, 60)))
        attn, small, turned = gather_weights(sizes, packet, extra, experts)
        phi_full = small[:, :64]
        out_all = small[:, 64:128].T.astype(F32)
        in_full = small[:, 128:192].reshape(n_s * n_t, -1, in_bias.shape[1])
        in_full = in_full.transpose(1, 0, 2).reshape(in_bias.shape[0], -1).astype(F32)
        scales = small[:, 192:194].T.astype(F32)
        biases = small[:, 194:196].T.astype(F32)
    else:
        scales, biases, in_full = (
            lax.all_gather(norm_scales, ROWS, axis=1, tiled=True).astype(F32),
            lax.all_gather(norm_biases, ROWS, axis=1, tiled=True).astype(F32),
            lax.all_gather(in_bias, ROWS, axis=1, tiled=True).astype(F32),
        )
        attn = lax.all_gather(
            lax.all_gather(w_attn, "heads", axis=2, tiled=True), ROWS, axis=1, tiled=True
        )
        phi_full = lax.all_gather(
            lax.all_gather(phi, "heads", axis=1, tiled=True), ROWS, axis=0, tiled=True
        )
        out_rows = lax.all_gather(out_bias, "tensor", axis=1, tiled=True).astype(F32)
    e_own = experts.shape[2] // lax.axis_size("shard")
    in_local = lax.dynamic_slice_in_dim(in_full, tensor_index * hidden, hidden, 1)
    factor = HEAD_DIM ** (-0.5)
    tokens = lax.dynamic_slice_in_dim(tokens, heads_index * own, own, 0)
    cotangent = lax.dynamic_slice_in_dim(cotangent, heads_index * own, own, 0)
    n_heads = width // HEAD_DIM
    inputs = tokens.astype(F32)
    normed_one, unit_one, inverse_one = normalize(inputs, scales[0], biases[0])
    normed_one_b = normed_one.astype(BF16)
    projected = einsum("nsd,kdc->knsc", normed_one_b, attn[:3]).astype(BF16)
    query, keyed, valued = projected.reshape(3, own, seq_len, n_heads, HEAD_DIM)
    scores = einsum("nqhe,nkhe->nhqk", query, keyed) * factor
    score_peak = jnp.max(scores, axis=-1, keepdims=True)
    exponent = jnp.exp(scores - score_peak)
    probs = exponent / jnp.sum(exponent, axis=-1, keepdims=True)
    probs_b = probs.astype(BF16)
    context_b = (
        einsum("nhqk,nkhe->nqhe", probs_b, valued).astype(BF16).reshape(own, seq_len, width)
    )
    hidden_one = inputs + einsum("nsc,dc->nsd", context_b, attn[3])
    normed_two, unit_two, inverse_two = normalize(hidden_one, scales[1], biases[1])
    normed_two_b = normed_two.astype(BF16)
    logits = einsum("nsd,de->nse", normed_two_b, phi_full)
    dispatch = jax.nn.softmax(logits, axis=1)
    dispatch_b = dispatch.astype(BF16)
    combine = jax.nn.softmax(logits, axis=2)
    combine_b = combine.astype(BF16)
    slot_in = einsum("nse,nsd->ned", dispatch_b, normed_two_b).astype(BF16)
    if sizes is not None:
        slot_in, activated, gate, back = expert_pass(
            sizes, False, to_blocks(slot_in, sizes), turned, in_local[:, None, :]
        )
        slot_out = (from_blocks(back, sizes) + out_all).astype(BF16)
    else:
        slot_in = to_experts(slot_in)
        share = 1 if e_own else 0

        def meet(partial_sum):
            return lax.psum_scatter(partial_sum, "shard", scatter_dimension=share, tiled=True)

        def spread(values):
            return lax.all_gather(values, "shard", axis=share, tiled=True)

        pre = meet(einsum("ned,def->nef", slot_in, experts[:, 0]))
        if e_own:
            pre = pre + lax.dynamic_slice_in_dim(in_local, shard_index * e_own, e_own, 0)
        else:
            pre = pre + in_local
        gelu_value, gelu_back = jax.vjp(partial(jax.nn.gelu, approximate=False), pre)
        activated = spread(gelu_value.astype(BF16))
        slot_out_part = einsum("nef,def->ned", activated, experts[:, 1])
        slot_out_part = slot_out_part + jnp.where(tensor_index == 0, out_rows, 0.0)
        slot_out = to_images(slot_out_part).astype(BF16)
    output = (hidden_one + einsum("nse,ned->nsd", combine_b, slot_out)).astype(BF16)
    grad_combine = einsum("nsd,ned->nse", cotangent, slot_out)
    grad_slot = einsum("nse,nsd->ned", combine_b, cotangent).astype(BF16)
    if sizes is not None:
        grad_slot, grad_pre, back, in_bias_grad = expert_pass(
            sizes, True, to_blocks(grad_slot, sizes), turned, gate, in_bias.shape[1]
        )
        back, output = lax.optimization_barrier((back, output))
        output = lax.all_gather(output, "heads", axis=0, tiled=True)
        grad_slot_in = from_blocks(back, sizes).astype(BF16)
        grad_slot_sum = jnp.sum(grad_slot.astype(F32), axis=1)
    else:
        output = lax.all_gather(output, "heads", axis=0, tiled=True)
        grad_slot = to_experts(grad_slot)
        grad_act = meet(einsum("ned,def->nef", grad_slot, experts[:, 1]))
        grad_pre = spread(gelu_back(grad_act)[0].astype(BF16))
        grad_slot_in = einsum("nef,def->ned", grad_pre, experts[:, 0]).astype(BF16)
        input_term = einsum("ned,nef->def", slot_in, grad_pre)
        output_term = einsum("ned,nef->def", grad_slot, activated)
        experts_grad = jnp.stack((input_term, output_term), axis=1)
        grad_slot_in = to_images(grad_slot_in.astype(F32)).astype(BF16)
        in_bias_grad = lax.dynamic_slice_in_dim(
            lax.all_gather(jnp.sum(grad_pre.astype(F32), axis=0), "tensor", axis=1, tiled=True),
            (shard_index * lax.axis_size("tensor") + tensor_index) * in_bias.shape[1],
            in_bias.shape[1],
            1,
        )
        grad_slot_sum = jnp.sum(grad_slot.astype(F32), axis=0)
    out_bias_grad = lax.dynamic_slice_in_dim(
        grad_slot_sum,
        tensor_index * out_bias.shape[1],
        out_bias.shape[1],
        1,
    )
    grad_dispatch = einsum("nsd,ned->nse", normed_two_b, grad_slot_in)
    grad_logits = (
        dispatch * (grad_dispatch - jnp.sum(dispatch * grad_dispatch, axis=1, keepdims=True))
        + combine * (grad_combine - jnp.sum(combine * grad_combine, axis=2, keepdims=True))
    ).astype(BF16)
    phi_grad = einsum("nsd,nse->de", normed_two_b, grad_logits)
    grad_normed_two = einsum("nse,ned->nsd", dispatch_b, grad_slot_in) + einsum(
        "nse,de->nsd", grad_logits, phi_full
    )
    grad_hidden_norm, scale_two_grad, bias_two_grad = normalize_back(
        grad_normed_two, unit_two, inverse_two, scales[1]
    )
    grad_hidden = cotangent.astype(F32) + grad_hidden_norm
    grad_hidden_b = grad_hidden.astype(BF16)
    out_weight_grad = einsum("nsd,nsc->dc", grad_hidden_b, context_b)
    grad_context = einsum("nsd,dc->nsc", grad_hidden_b, attn[3]).astype(BF16)
    grad_context = grad_context.reshape(own, seq_len, n_heads, HEAD_DIM)
    grad_value = einsum("nhqk,nqhe->nkhe", probs_b, grad_context).astype(BF16)
    grad_probs = einsum("nqhe,nkhe->nhqk", grad_context, valued)
    grad_scores = (
        probs * (grad_probs - jnp.sum(probs * grad_probs, axis=-1, keepdims=True))
    ).astype(BF16)
    grad_query = (einsum("nhqk,nkhe->nqhe", grad_scores, keyed) * factor).astype(BF16)
    grad_key = (einsum("nhqk,nqhe->nkhe", grad_scores, query) * factor).astype(BF16)
    grad_proj = jnp.stack((grad_query, grad_key, grad_value)).reshape(3, own, seq_len, width)
    proj_grad = einsum("nsd,knsc->kdc", normed_one_b, grad_proj)
    grad_normed_one = einsum("knsc,kdc->nsd", grad_proj, attn[:3])
    grad_input_norm, scale_one_grad, bias_one_grad = normalize_back(
        grad_normed_one, unit_one, inverse_one, scales[0]
    )
    input_grad = (grad_hidden + grad_input_norm).astype(BF16)
    if sizes is not None:
        input_grad, output = lax.optimization_barrier((input_grad, output))
    input_grad = lax.all_gather(input_grad, "heads", axis=0, tiled=True)
    attn_grad = jnp.concatenate((proj_grad, out_weight_grad[None]), axis=0)
    norms = jnp.stack((scale_one_grad, scale_two_grad, bias_one_grad, bias_two_grad))
    if sizes is not None:
        small = jnp.concatenate((phi_grad, norms.T), axis=1)
        small = jnp.pad(small, ((0, 0), (0, 128 - small.shape[1]))).astype(BF16)
        attn_grad, grad_pre = lax.optimization_barrier((attn_grad.astype(BF16), grad_pre))
        experts_grad = weight_grads(slot_in, grad_pre, grad_slot, activated)
        attn_grad, experts_grad = lax.optimization_barrier((attn_grad, experts_grad))
        summed = reduce_grads(sizes, attn_grad, small)
        attn_grad = summed[:, :, :block]
        phi_grad = summed[0, :, block : block + slot]
        norms = summed[0, :, block + slot : block + slot + 4].T
    else:
        attn_grad = lax.psum_scatter(attn_grad, ROWS, scatter_dimension=1, tiled=True)
        attn_grad = lax.psum_scatter(attn_grad, "heads", scatter_dimension=2, tiled=True)
        phi_grad = lax.psum_scatter(phi_grad, ROWS, scatter_dimension=0, tiled=True)
        phi_grad = lax.psum_scatter(phi_grad, "heads", scatter_dimension=1, tiled=True)
        norms = lax.psum(lax.psum_scatter(norms, ROWS, scatter_dimension=1, tiled=True), "heads")
    return (
        output,
        input_grad,
        norms[:2],
        norms[2:],
        attn_grad,
        phi_grad,
        experts_grad,
        in_bias_grad,
        out_bias_grad,
    )


def solution(mesh):
    images = P(ROWS, None, None)
    return jax.shard_map(
        shards,
        mesh=mesh,
        in_specs=(
            images,
            P(None, ROWS),
            P(None, ROWS),
            P(None, ROWS, "heads"),
            P(ROWS, "heads"),
            P("shard", None, "heads", "tensor"),
            P("heads", ROWS),
            P("heads", ROWS),
            images,
        ),
        out_specs=(
            images,
            images,
            P(None, ROWS),
            P(None, ROWS),
            P(None, ROWS, "heads"),
            P(ROWS, "heads"),
            P("shard", None, "heads", "tensor"),
            P("heads", ROWS),
            P("heads", ROWS),
        ),
        check_vma=False,
    )
```

```python
from functools import partial

import jax
import jax.numpy as jnp
from jax import lax
from jax.experimental import pallas as pl
from jax.experimental.pallas import tpu as pltpu
from jax.sharding import PartitionSpec as P

HEAD_DIM = 64
F32 = jnp.float32
BF16 = jnp.bfloat16
ROWS = ("shard", "tensor")
MESH = pl.DeviceIdType.MESH
VMEM_BYTES = 58 * 1024 * 1024
epsilon = 1e-06
einsum = partial(jnp.einsum, preferred_element_type=F32)


def dot(a, b):
    return lax.dot_general(a, b, (((1,), (0,)), ((), ())), preferred_element_type=F32)


def dot_t(a, b):
    return lax.dot_general(a, b, (((1,), (1,)), ((), ())), preferred_element_type=F32)


def swap_matrix(n):
    out = lax.broadcasted_iota(jnp.int32, (n * n, n * n), 0)
    row = lax.broadcasted_iota(jnp.int32, (n * n, n * n), 1)
    return ((out // n == row % n) & (out % n == row // n)).astype(F32).astype(BF16)


class Peers:
    def __init__(self, sizes):
        self.sizes = sizes
        self.at = tuple(lax.axis_index(name) for name in ("shard", "heads", "tensor"))
        self.count = sizes[0] * sizes[1] * sizes[2]

    def flat(self, place):
        return (place[0] * self.sizes[1] + place[1]) * self.sizes[2] + place[2]

    def step(self, k, sign):
        _, n_h, n_t = self.sizes
        steps = (k // (n_h * n_t), (k // n_t) % n_h, k % n_t)
        return tuple(
            lax.rem(at + n + sign * d, n) for at, n, d in zip(self.at, self.sizes, steps)
        )

    def greet_all(self):
        barrier = pltpu.get_barrier_semaphore()

        def signal(k, carry):
            pl.semaphore_signal(barrier, inc=1, device_id=self.step(k, 1), device_id_type=MESH)
            return carry

        lax.fori_loop(1, self.count, signal, 0)
        pl.semaphore_wait(barrier, self.count - 1)


def remote(src, dst, send, recv, place):
    return pltpu.make_async_remote_copy(
        src_ref=src, dst_ref=dst, send_sem=send, recv_sem=recv, device_id=place, device_id_type=MESH
    )


def plane(sizes):
    n_s, n_h, n_t = sizes
    s, h, t = (lax.axis_index(name) for name in ("shard", "heads", "tensor"))
    core, chip = lax.rem(s, 2), s // 2
    sibling = (s + 1 - 2 * core, h, t)
    across_x = (lax.rem(s + 2, n_s), h, t)
    across_y = (s, h, 1 - t)
    line = [(s, lax.rem(h + d, n_h), t) for d in range(n_h)]
    barrier = pltpu.get_barrier_semaphore()
    others = [sibling, across_x, across_y] + line[1:]
    for place in others:
        pl.semaphore_signal(barrier, inc=1, device_id=place, device_id_type=MESH)
    pl.semaphore_wait(barrier, len(others))
    return (s, h, t), core, chip, sibling, across_x, across_y, line


def pair_matrix(block, wide, transposed):
    shape = (2 * block, 2 * wide) if transposed else (2 * wide, 2 * block)
    tight = lax.broadcasted_iota(jnp.int32, shape, 0 if transposed else 1)
    padded = lax.broadcasted_iota(jnp.int32, shape, 1 if transposed else 0)
    second = padded >= wide
    lane = jnp.where(second, padded - wide, padded)
    same = (lane < block) & (tight == jnp.where(second, lane + block, lane))
    return same.astype(F32).astype(BF16)


def gather_kernel(
    sizes, packet, extra, experts, w_out, small_out, turned,
    w, small, lined, tile_in, tile_out,
    z_send, z_recv, x_sems, y_sems, d_sems, c_sems, t_sems, o_sems,
):
    (s, h, t), core, chip, sibling, across_x, across_y, line = plane(sizes)
    n_k, rows, wide = packet.shape
    n_h, n_t = sizes[1], sizes[2]
    width = w.shape[2]
    block = width // n_h
    side = 16
    n_tiles = experts.shape[0] // side
    depth = tile_in.shape[0]
    halves = ((0, rows // 2), (rows // 2, rows // 2))

    def z_hop(k, origin, up):
        place = line[1] if up else line[n_h - 1]
        return remote(
            lined.at[origin, k], lined.at[origin, k],
            z_send.at[k, origin, up], z_recv.at[k, origin], place,
        )

    def relay(k, d):
        @pl.when(h >= d)
        def _():
            z_hop(k, h - d, 1).wait_recv()

            @pl.when(h < n_h - 1)
            def _():
                z_hop(k, h - d, 1).start()

        @pl.when(h + d < n_h)
        def _():
            z_hop(k, h + d, 0).wait_recv()

            @pl.when(h > 0)
            def _():
                z_hop(k, h + d, 0).start()

    chunks = (0, 2, 1, 3)
    lined[h] = packet[...]
    for k in chunks:
        @pl.when(h < n_h - 1)
        def _():
            z_hop(k, h, 1).start()

        @pl.when(h > 0)
        def _():
            z_hop(k, h, 0).start()

    def load(i):
        return pltpu.make_async_copy(
            experts.at[pl.ds((i % n_tiles) * side, side), i // n_tiles],
            tile_in.at[i % depth],
            t_sems.at[0, i % depth],
        )

    def store(i):
        return pltpu.make_async_copy(
            tile_out.at[i % depth],
            turned.at[i // n_tiles, :, pl.ds((i % n_tiles) * side, side)],
            t_sems.at[1, i % depth],
        )

    for i in range(depth - 1):
        load(i).start()
    swap = swap_matrix(side)
    done = [0]

    def turn(count):
        def step(i, carry):
            load(i).wait()

            @pl.when(i + depth - 1 < 2 * n_tiles)
            def _():
                load(i + depth - 1).start()

            @pl.when(i >= depth)
            def _():
                store(i - depth).wait()

            rows_in = tile_in[i % depth].reshape(side * side, tile_in.shape[3])
            tile_out[i % depth] = dot(swap, rows_in).astype(BF16).reshape(tile_out.shape[1:])
            store(i).start()
            return carry

        last = min(done[0] + count, 2 * n_tiles)
        lax.fori_loop(done[0], last, step, 0)
        done[0] = last

    pair = pair_matrix(block, wide, False)
    shape = (n_h * wide, small.shape[1])
    row = lax.broadcasted_iota(jnp.int32, shape, 0)
    column = lax.broadcasted_iota(jnp.int32, shape, 1)
    lane, of = row % wide - block, row // wide
    beside = (lane >= 0) & (lane < 16) & (column == of * 16 + lane)
    beside |= (lane >= 16) & (lane < 32) & (column == n_h * 16 + of * 16 + lane - 16)
    beside = beside.astype(F32).astype(BF16)

    def at(k, place):
        first = pl.multiple_of((place[0] * n_t + place[2]) * rows, 16)
        lines = pl.ds(first, rows)
        return small.at[lines] if k == n_k else w.at[k, lines]

    def hop(q, origin, place, sems, j):
        return remote(at(q, origin), at(q, origin), sems.at[0, j], sems.at[1, j], place)

    def half_hop(q, origin, place, half):
        part = at(q, origin).at[pl.ds(*halves[half])]
        j = 2 * q + half
        return remote(part, part, d_sems.at[0, j], d_sems.at[1, j], place)

    me = (s, h, t)
    from_d = (across_x[0], h, across_y[2])
    sent = []

    def send(copy):
        copy.start()
        sent.append(copy)

    def assemble(k):
        for i in range(0, n_h, 2):
            lines = jnp.concatenate([lined[i, k], lined[i + 1, k]], axis=1)
            at(k, me)[:, i * block : (i + 2) * block] = dot(lines, pair).astype(BF16)
        if k == 0:
            lines = jnp.concatenate([lined[i, k] for i in range(n_h)], axis=1)
            at(n_k, me)[...] = (dot(lines, beside) + extra[...].astype(F32)).astype(BF16)
        for q in members(k):
            send(hop(q, me, across_x, x_sems, q))
            send(hop(q, me, across_y, y_sems, q))
            send(hop(q, me, sibling, c_sems, 4 * q))

    def members(k):
        return (0, n_k) if k == 0 else (k,)

    def relay_xy(k):
        for q in members(k):
            hop(q, across_x, across_x, x_sems, q).wait_recv()
            send(half_hop(q, across_x, across_y, 0))
            send(hop(q, across_x, sibling, c_sems, 4 * q + 1))
            hop(q, across_y, across_y, y_sems, q).wait_recv()
            send(half_hop(q, across_y, across_x, 1))
            send(hop(q, across_y, sibling, c_sems, 4 * q + 2))

    def relay_d(k):
        for q in members(k):
            half_hop(q, from_d, across_y, 0).wait_recv()
            half_hop(q, from_d, across_x, 1).wait_recv()
            send(hop(q, from_d, sibling, c_sems, 4 * q + 3))

    for wave in range(n_k + n_h - 2):
        for d in range(1, n_h):
            if 0 <= wave - d + 1 < n_k:
                relay(chunks[wave - d + 1], d)
        turn(2)
        i = wave - n_h + 2
        if i >= 0:
            assemble(chunks[i])
            if i >= 1:
                relay_xy(chunks[i - 1])
            if i >= 2:
                relay_d(chunks[i - 2])
            turn(2)
    relay_xy(chunks[-1])
    relay_d(chunks[-2])
    turn(2 * n_tiles)
    relay_d(chunks[-1])
    stores = []
    for k in chunks:
        for q in members(k):
            for j in range(4):
                hop(q, me, sibling, c_sems, 4 * q + j).wait_recv()
            if q == n_k:
                stores.append(pltpu.make_async_copy(small, small_out, o_sems.at[q]))
            else:
                stores.append(pltpu.make_async_copy(w.at[q], w_out.at[q], o_sems.at[q]))
            stores[-1].start()
    for copy in sent:
        copy.wait_send()
    for origin in range(n_h):
        @pl.when((origin <= h) & (h < n_h - 1))
        def _():
            for k in range(n_k):
                z_hop(k, origin, 1).wait_send()

        @pl.when((origin >= h) & (h > 0))
        def _():
            for k in range(n_k):
                z_hop(k, origin, 0).wait_send()

    for i in range(depth):
        store(2 * n_tiles - depth + i).wait()
    for copy in stores:
        copy.wait()


def gather_weights(sizes, packet, extra, experts):
    n_k, rows, wide = packet.shape
    n_s, n_h, n_t = sizes
    width = n_s * n_t * rows
    vmem = pl.BlockSpec(memory_space=pltpu.VMEM)
    hbm = pl.BlockSpec(memory_space=pl.ANY)
    dma = pltpu.SemaphoreType.DMA
    hidden = experts.shape[3]
    small = (width, extra.shape[1])
    return pl.pallas_call(
        partial(gather_kernel, sizes),
        out_shape=(
            jax.ShapeDtypeStruct((n_k, width, width), BF16),
            jax.ShapeDtypeStruct(small, BF16),
            jax.ShapeDtypeStruct((2, experts.shape[2], experts.shape[0], hidden), BF16),
        ),
        in_specs=[vmem, vmem, hbm],
        out_specs=(hbm, hbm, hbm),
        scratch_shapes=[
            pltpu.VMEM((n_k, width, width), BF16),
            pltpu.VMEM(small, BF16),
            pltpu.VMEM((n_h, n_k, rows, wide), BF16),
            pltpu.VMEM((4, 16, 16, hidden), BF16),
            pltpu.VMEM((4, 16, 16, hidden), BF16),
            dma((n_k, n_h, 2)), dma((n_k, n_h)), dma((2, n_k + 1)), dma((2, n_k + 1)),
            dma((2, 2 * (n_k + 1))), dma((2, 4 * (n_k + 1))), dma((2, 4)), dma((n_k + 1,)),
        ],
        compiler_params=pltpu.CompilerParams(
            collective_id=3, has_side_effects=True, vmem_limit_bytes=VMEM_BYTES
        ),
        name="gather_weights",
    )(packet, extra, experts)


def reduce_kernel(
    sizes, grads, small, out, core_in, core_small, met, met_small,
    d_in, d_small, x_in, x_small, y_in, y_small, pieces, z_in,
    c_sems, d_sems, x_sems, y_sems, z_sems,
):
    (s, h, t), core, chip, sibling, across_x, across_y, line = plane(sizes)
    n_k, width, _ = grads.shape
    n_s, n_h, n_t = sizes
    rows = width // (n_s * n_t)
    wide = pieces.shape[3]
    pair = n_t * rows
    half = rows // 2
    halves = (pl.ds(0, half), pl.ds(half, half))
    chunks = (0, 2, 1, 3)

    def members(k):
        return (0, n_k) if k == 0 else (k,)

    def pick(q, large, little):
        return little if q == n_k else large.at[q]

    def core_copy(q, x):
        first = pl.multiple_of((2 * x + 1 - core) * pair, 16)
        return remote(
            pick(q, grads, small).at[pl.ds(first, pair)],
            pick(q, core_in, core_small).at[x],
            c_sems.at[0, 2 * q + x], c_sems.at[1, 2 * q + x], sibling,
        )

    for k in chunks:
        for q in members(k):
            for x in range(2):
                core_copy(q, x).start()
    joined = pair_matrix(width // n_h, wide, True)
    shape = (small.shape[1], n_h * wide)
    row = lax.broadcasted_iota(jnp.int32, shape, 0)
    column = lax.broadcasted_iota(jnp.int32, shape, 1)
    lane, of = column % wide - width // n_h, column // wide
    beside = (lane >= 0) & (lane < 16) & (row == of * 16 + lane)
    beside |= (lane >= 16) & (lane < 20) & (row == n_h * 16 + lane - 16)
    beside = beside.astype(F32).astype(BF16)
    to_d, to_x, to_y = (d_in, d_small), (x_in, x_small), (y_in, y_small)
    sent = []

    def hop(q, kind, part, source, place):
        sems = {id(to_d): d_sems, id(to_x): x_sems, id(to_y): y_sems}[id(kind)]
        target = pick(q, *kind)
        target = target.at[part] if kind is to_d else target.at[halves[part]]
        j = 2 * q + part
        return remote(source, target, sems.at[0, j], sems.at[1, j], place)

    def send(copy):
        copy.start()
        sent.append(copy)

    def part_of(q, x, y, part):
        return pick(q, met, met_small).at[x, y].at[halves[part]]

    def arrived(q, kind, part):
        hop(q, kind, part, part_of(q, 0, 0, part), sibling).wait_recv()

    def open_up(q):
        part = pick(q, met, met_small)
        for x in range(2):
            core_copy(q, x).wait_recv()
            first = pl.multiple_of((2 * x + core) * pair, 16)
            own = pick(q, grads, small)[pl.ds(first, pair)].astype(F32)
            total = own + pick(q, core_in, core_small)[x].astype(F32)
            part[x] = total.astype(BF16).reshape(n_t, rows, total.shape[1])
        send(hop(q, to_d, 0, part_of(q, 1 - chip, 1 - t, 0), across_x))
        send(hop(q, to_d, 1, part_of(q, 1 - chip, 1 - t, 1), across_y))
        send(hop(q, to_x, 0, part_of(q, 1 - chip, t, 0), across_x))
        send(hop(q, to_y, 1, part_of(q, chip, 1 - t, 1), across_y))

    def pass_on(q):
        for part, kind, x, y, place in (
            (0, to_y, chip, 1 - t, across_y),
            (1, to_x, 1 - chip, t, across_x),
        ):
            arrived(q, to_d, part)
            block = part_of(q, x, y, part)
            total = block[...].astype(F32) + pick(q, *to_d)[part].astype(F32)
            block[...] = total.astype(BF16)
            send(hop(q, kind, part, block, place))

    def whole(q):
        for kind in (to_x, to_y):
            for part in range(2):
                arrived(q, kind, part)
        total = pick(q, met, met_small)[chip, t].astype(F32) + pick(q, *to_x)[...].astype(F32)
        return (total + pick(q, *to_y)[...].astype(F32)).astype(BF16)

    def z_copy(k, d):
        return remote(
            pieces.at[line[d][1], k], z_in.at[h, k], z_sems.at[0, k, d], z_sems.at[1, k, d], line[d]
        )

    def share_out(k):
        value = whole(k)
        columns = width // n_h
        if k == 0:
            little = dot(whole(n_k), beside)
        for i in range(0, n_h, 2):
            lanes = dot(value[:, i * columns : (i + 2) * columns], joined)
            if k == 0:
                lanes = lanes + little[:, i * wide : (i + 2) * wide]
            pieces[i, k] = lanes[:, :wide].astype(BF16)
            pieces[i + 1, k] = lanes[:, wide:].astype(BF16)
        for d in range(n_h - 1, 0, -1):
            z_copy(k, d).start()

    for i in range(n_k + 2):
        if i < n_k:
            for q in members(chunks[i]):
                open_up(q)
        if 0 <= i - 1 < n_k:
            for q in members(chunks[i - 1]):
                pass_on(q)
        if i >= 2:
            share_out(chunks[i - 2])
    for k in chunks:
        total = pieces[h, k].astype(F32)
        for d in range(1, n_h):
            z_copy(k, d).wait_recv()
        for d in range(1, n_h):
            total = total + z_in[line[d][1], k].astype(F32)
        out[k] = total
    for k in chunks:
        for q in members(k):
            for x in range(2):
                core_copy(q, x).wait_send()
    for copy in sent:
        copy.wait_send()
    for k in range(n_k):
        for d in range(1, n_h):
            z_copy(k, d).wait_send()


def reduce_grads(sizes, grads, small):
    n_k, width, _ = grads.shape
    n_s, n_h, n_t = sizes
    rows, wide, thin = width // (n_s * n_t), 256, small.shape[1]
    vmem = pl.BlockSpec(memory_space=pltpu.VMEM)
    dma = pltpu.SemaphoreType.DMA

    def buffers(*lead):
        return [
            pltpu.VMEM((n_k, *lead, width), BF16),
            pltpu.VMEM((*lead, thin), BF16),
        ]

    return pl.pallas_call(
        partial(reduce_kernel, sizes),
        out_shape=jax.ShapeDtypeStruct((n_k, rows, wide), F32),
        in_specs=[vmem, vmem],
        out_specs=vmem,
        scratch_shapes=[
            *buffers(2, n_t * rows), *buffers(2, n_t, rows),
            *buffers(2, rows // 2), *buffers(rows), *buffers(rows),
            pltpu.VMEM((n_h, n_k, rows, wide), BF16),
            pltpu.VMEM((n_h, n_k, rows, wide), BF16),
            dma((2, 2 * (n_k + 1))), dma((2, 2 * (n_k + 1))), dma((2, 2 * (n_k + 1))),
            dma((2, 2 * (n_k + 1))), dma((2, n_k, n_h)),
        ],
        compiler_params=pltpu.CompilerParams(
            collective_id=4, has_side_effects=True, vmem_limit_bytes=VMEM_BYTES
        ),
        name="reduce_grads",
    )(grads, small)


def expert_kernel(sizes, backward, *refs):
    if backward:
        (blocks, weights, gate, output, slots_out, act_out, back_out, bias_out, sum_out, gathered,
         w_a, w_b, gate_v, sums, slots, act, core_out, core_in, x_out, x_in, land, leave, back, land_back,
         w_sem, o_sem, in_sems, back_sems, core_sems, x_sems, act_sems, b_sems,
         g_send, g_recv, g_sem,
         bias_all, bias_send, bias_land) = refs
    else:
        (blocks, weights, gate, slots_out, act_out, gate_out, back_out,
         w_a, w_b, sums, slots, act, core_out, core_in, x_out, x_in, land, leave, back, land_back,
         w_sem, o_sem, in_sems, back_sems, core_sems, x_sems, act_sems, bias) = refs
    peers = Peers(sizes)
    s, h, t = peers.at
    n_s, n_h, n_t = sizes
    me = peers.flat(peers.at)
    core, chip = lax.rem(s, 2), s // 2
    sibling = (s + 1 - 2 * core, h, t)
    across = (lax.rem(s + 2, n_s), h, t)
    half = act.shape[0] // 2
    own, other = core * half, (1 - core) * half
    n_blocks = peers.count
    first = 1 if backward else 0
    loads = [
        pltpu.make_async_copy(weights.at[first], w_a, w_sem.at[0]),
        pltpu.make_async_copy(weights.at[1 - first], w_b, w_sem.at[1]),
    ]
    for load in loads:
        load.start()
    if backward:
        gate_load = pltpu.make_async_copy(gate, gate_v, o_sem.at[0])
        gate_load.start()
    peers.greet_all()

    def block_out(p, k):
        place = peers.step(k, 1)
        return remote(
            blocks.at[place[1], place[0], p], land.at[p, me],
            in_sems.at[0, p, k], in_sems.at[1, p, k], place,
        )

    def block_in(p, k):
        source = peers.flat(peers.step(k, -1))
        return remote(
            blocks.at[0, 0, p], land.at[p, source], in_sems.at[0, p, k], in_sems.at[1, p, k], sibling
        )

    def each(function, count=n_blocks, start=1):
        lax.fori_loop(start, count, lambda k, carry: (function(k), carry)[1], 0)

    for p in range(2):
        each(lambda k: block_out(p, k).start())
        land[p, me] = blocks[h, s, p]
    few = half // 2
    group = 16
    many = 2 * group
    out_row = lax.broadcasted_iota(jnp.int32, (16 * group, 16 * group), 0)
    in_row = lax.broadcasted_iota(jnp.int32, (16 * group, 16 * group), 1)
    there = (out_row // many == in_row % (2 * few)) & (out_row % many == in_row // (2 * few))
    there = there.astype(F32).astype(BF16)
    again = (in_row // many == out_row % (2 * few)) & (in_row % many == out_row // (2 * few))
    again = again.astype(F32).astype(BF16)

    def receive(p):
        each(lambda k: block_in(p, k).wait_recv())
        for b in range(n_blocks // group):
            rows = land[p, b * group : (b + 1) * group].reshape(group * 16, land.shape[3])
            turned = dot(there, rows).astype(BF16).reshape(2 * few, many, land.shape[3])
            for c in range(2):
                first = c * half + p * few
                slots[first : first + few, b * many : (b + 1) * many, :] = turned[
                    c * few : (c + 1) * few
                ]

    if backward:
        own_images = output.shape[0]
        line = [(s, lax.rem(h + d, n_h), t) for d in range(n_h)]
        g_own = pltpu.make_async_copy(output, gathered.at[pl.ds(h * own_images, own_images)], g_sem)
        g_own.start()

        def z_hop(i, origin, up, source=None):
            there = gathered.at[origin * own_images + i]
            return remote(
                there if source is None else source, there,
                g_send.at[i, origin, up], g_recv.at[i, origin], line[1] if up else line[n_h - 1],
            )

        def relay(wave):
            for d in range(1, n_h):
                i = wave - d + 1
                if 0 <= i < own_images:
                    @pl.when(h >= d)
                    def _():
                        z_hop(i, h - d, 1).wait_recv()

                        @pl.when(h < n_h - 1)
                        def _():
                            z_hop(i, h - d, 1).start()

                    @pl.when(h + d < n_h)
                    def _():
                        z_hop(i, h + d, 0).wait_recv()

                        @pl.when(h > 0)
                        def _():
                            z_hop(i, h + d, 0).start()

        def gather_output():
            for i in range(own_images):
                @pl.when(h < n_h - 1)
                def _():
                    z_hop(i, h, 1, output.at[i]).start()

                @pl.when(h > 0)
                def _():
                    z_hop(i, h, 0, output.at[i]).start()
    else:
        piece, count = 6 * 64, act.shape[2] // (6 * 64)
        row = lax.broadcasted_iota(jnp.int32, (6 * 128, piece), 0)
        column = lax.broadcasted_iota(jnp.int32, (6 * 128, piece), 1)
        lane = row % 128
        place = (lane < 64) & (column == (row // 128) * 64 + lane)
        place = place.astype(F32).astype(BF16)
        for m in range(count):
            first = (t * count + m) * 96
            lines = [
                gate[pl.ds(pl.multiple_of(first + j * 16, 16), 16), 128:256] for j in range(6)
            ]
            bias[:, m * piece : (m + 1) * piece] = dot(jnp.concatenate(lines, axis=1), place)

    receive(0)
    loads[0].wait()

    def core_copy(j):
        return remote(
            core_out.at[j], core_in.at[j], core_sems.at[0, j], core_sems.at[1, j], sibling
        )

    def x_copy(j):
        return remote(x_out.at[j], x_in.at[j], x_sems.at[0, j], x_sems.at[1, j], across)

    def act_copy(j):
        return remote(
            act.at[own + j], act.at[own + j], act_sems.at[0, j], act_sems.at[1, j], sibling
        )

    def act_in(j):
        return remote(
            act.at[other + j], act.at[other + j], act_sems.at[0, j], act_sems.at[1, j], sibling
        )

    def meet(j):
        core_copy(j).wait_recv()
        sums[j] = sums[j] + core_in[j].astype(F32)
        x_out[j] = sums[j].astype(BF16)
        x_copy(j).start()

    def first_sums(j):
        core_out[j] = dot(slots[other + j], w_a[other + j]).astype(BF16)
        core_copy(j).start()
        sums[j] = dot(slots[own + j], w_a[own + j])

        @pl.when(j > 0)
        def _():
            meet(j - 1)

    each(first_sums, few, 0)
    receive(1)
    if backward:
        gather_output()
    each(first_sums, half, few)
    meet(half - 1)
    loads[1].wait()
    if backward:
        gate_load.wait()

    def second(e):
        leave[e] = dot_t(act[e], w_b[e]).astype(BF16)

    def finish(j):
        x_copy(j).wait_recv()
        value = sums[j] + x_in[j].astype(F32)
        if backward:
            act[own + j] = (value * gate_v[j]).astype(BF16)
        else:
            value = value + bias[pl.ds(own + j, 1), :]
            cumulative = 0.5 + 0.5 * lax.erf(value * 0.7071067811865476)
            act[own + j] = (value * cumulative).astype(BF16)
            sums[j] = cumulative + value * (
                jnp.exp(value * value * -0.5) * 0.3989422804014327
            )
        act_copy(j).start()
        second(own + j)

        @pl.when(j > 0)
        def _():
            act_in(j - 1).wait_recv()
            second(other + j - 1)

        if backward:
            for wave in range(3):
                @pl.when(j == 3 + 2 * wave)
                def _():
                    relay(wave)

    def back_copy(p, k):
        place = peers.step(k, 1)
        return remote(
            back.at[p, peers.flat(place)], land_back.at[p, me],
            back_sems.at[0, p, k], back_sems.at[1, p, k], place,
        )

    def back_in(p, k):
        source = peers.flat(peers.step(k, -1))
        return remote(
            back.at[p, 0], land_back.at[p, source],
            back_sems.at[0, p, k], back_sems.at[1, p, k], sibling,
        )

    def give_back(p):
        for b in range(n_blocks // group):
            rows = jnp.concatenate(
                [
                    leave[c * half + p * few : c * half + (p + 1) * few, b * many : (b + 1) * many, :]
                    for c in range(2)
                ],
                axis=0,
            ).reshape(group * 16, leave.shape[2])
            turned = dot(again, rows).astype(BF16)
            back[p, b * group : (b + 1) * group] = turned.reshape(group, 16, leave.shape[2])
        each(lambda k: back_copy(p, k).start())
        land_back[p, me] = back[p, me]

    each(finish, few + 1, 0)
    give_back(0)
    each(finish, half, few + 1)
    act_in(half - 1).wait_recv()
    second(other + half - 1)
    give_back(1)
    stores = [pltpu.make_async_copy(act, act_out, o_sem.at[1])]
    if not backward:
        stores.append(pltpu.make_async_copy(sums, gate_out, o_sem.at[0]))
    for store in stores:
        store.start()
    slots_out[...] = slots[...]
    if backward:
        across_t = (s, h, 1 - t)
        width = bias_out.shape[1]

        def bias_row(e):
            bias_all[pl.ds(e, 1), :] = jnp.sum(act[e].astype(F32), axis=0, keepdims=True)

        each(bias_row, 2 * half, 0)

        def slot_row(e):
            sum_out[pl.ds(e, 1), :] = jnp.sum(slots[e].astype(F32), axis=0, keepdims=True)

        each(slot_row, 2 * half, 0)

        def piece(for_t):
            return bias_all[:, pl.ds(pl.multiple_of((core * n_t + for_t) * width, 128), width)]

        bias_send[...] = piece(1 - t)
        bias_copy = remote(bias_send, bias_land, b_sems.at[0], b_sems.at[1], across_t)
        bias_copy.start()
        bias_copy.wait()
        bias_out[...] = jnp.where(t == chip, piece(t), bias_land[...])
    for p in range(2):
        each(lambda k: back_in(p, k).wait_recv())
    back_out[...] = land_back[...]
    for store in stores:
        store.wait()
    if backward:
        relay(3)
        g_own.wait()
        for origin in range(n_h):
            @pl.when((origin < h) & (h < n_h - 1))
            def _():
                for i in range(own_images):
                    z_hop(i, origin, 1).wait_send()

            @pl.when((origin > h) & (h > 0))
            def _():
                for i in range(own_images):
                    z_hop(i, origin, 0).wait_send()

        @pl.when(h < n_h - 1)
        def _():
            for i in range(own_images):
                z_hop(i, h, 1, output.at[i]).wait_send()

        @pl.when(h > 0)
        def _():
            for i in range(own_images):
                z_hop(i, h, 0, output.at[i]).wait_send()

    for p in range(2):
        each(lambda k: block_out(p, k).wait_send())
        each(lambda k: back_copy(p, k).wait_send())
    for copy in (core_copy, x_copy, act_copy):
        each(lambda j: copy(j).wait_send(), half, 0)


def expert_pass(sizes, backward, blocks, weights, gate, output=None, bias_width=0):
    _, experts, rows, hidden = weights.shape
    devices = sizes[0] * sizes[1] * sizes[2]
    images = 2 * devices
    half = experts // 2
    vmem = pl.BlockSpec(memory_space=pltpu.VMEM)
    hbm = pl.BlockSpec(memory_space=pl.ANY)
    slots = jax.ShapeDtypeStruct((experts, images, rows), BF16)
    act = jax.ShapeDtypeStruct((experts, images, hidden), BF16)
    gate_shape = (half, images, hidden)
    returned = jax.ShapeDtypeStruct((2, devices, experts, rows), BF16)
    if backward:
        operands, in_specs = (blocks, weights, gate, output), [vmem, hbm, hbm, hbm]
        outs = (
            slots, act, returned,
            jax.ShapeDtypeStruct((experts, bias_width), F32),
            jax.ShapeDtypeStruct((experts, rows), F32),
            jax.ShapeDtypeStruct((sizes[1] * output.shape[0], *output.shape[1:]), BF16),
        )
        out_specs = (vmem, hbm, vmem, vmem, vmem, hbm)
    else:
        operands, in_specs = (blocks, weights, gate), [vmem, hbm, vmem]
        outs = (slots, act, jax.ShapeDtypeStruct(gate_shape, F32), returned)
        out_specs = (vmem, hbm, hbm, vmem)
    weight = pltpu.VMEM((experts, rows, hidden), BF16)
    chunk = pltpu.VMEM((half, images, hidden), BF16)
    block = pltpu.VMEM((2, devices, experts, rows), BF16)
    dma = pltpu.SemaphoreType.DMA
    scratch = [weight, weight]
    if backward:
        scratch.append(pltpu.VMEM(gate_shape, F32))
    scratch += [
        pltpu.VMEM(gate_shape, F32),
        pltpu.VMEM(slots.shape, BF16),
        pltpu.VMEM(act.shape, BF16),
        chunk, chunk, chunk, chunk, block,
        pltpu.VMEM(slots.shape, BF16),
        block, block,
        dma((2,)), dma((2,)), dma((2, 2, devices)), dma((2, 2, devices)),
        dma((2, half)), dma((2, half)), dma((2, half)),
    ]
    if backward:
        scratch += [
            dma((2,)), dma((output.shape[0], sizes[1], 2)), dma((output.shape[0], sizes[1])), dma,
            pltpu.VMEM((experts, hidden), F32),
            pltpu.VMEM((experts, bias_width), F32),
            pltpu.VMEM((experts, bias_width), F32),
        ]
    else:
        scratch.append(pltpu.VMEM((experts, hidden), F32))
    return pl.pallas_call(
        partial(expert_kernel, sizes, backward),
        out_shape=outs,
        in_specs=in_specs,
        out_specs=out_specs,
        scratch_shapes=scratch,
        compiler_params=pltpu.CompilerParams(
            collective_id=2 if backward else 1, has_side_effects=True, vmem_limit_bytes=VMEM_BYTES
        ),
        cost_estimate=pl.CostEstimate(
            flops=8 * images * experts * rows * hidden,
            bytes_accessed=weights.size * 2,
            transcendentals=0,
        ),
        name="experts_back" if backward else "experts_ahead",
    )(*operands)


def weight_grad_kernel(slots_0, act_0, slots_1, act_1, out, lines, pick, same):
    group, images, rows = slots_0.shape
    d_block = out.shape[0]
    n = group * d_block
    m, d = pl.program_id(0), pl.program_id(2)

    @pl.when((m == 0) & (pl.program_id(1) == 0) & (d == 0))
    def _():
        row = lax.broadcasted_iota(jnp.int32, pick.shape, 0)
        column = lax.broadcasted_iota(jnp.int32, pick.shape, 1)
        pick[...] = (column == row // group).astype(F32).astype(BF16)
        row = lax.broadcasted_iota(jnp.int32, same.shape, 0)
        column = lax.broadcasted_iota(jnp.int32, same.shape, 1)
        same[...] = (row % group == column // images).astype(F32)

    def prepare(slots):
        @pl.when(d == 0)
        def _():
            turned = slots[...].reshape(group * images, rows).astype(F32)
            lines[...] = jnp.swapaxes(turned, 0, 1).astype(BF16)

    def term(act):
        mine = lines[pl.ds(pl.multiple_of(d * d_block, d_block), d_block)]
        spread = (dot(pick[...], mine) * same[...]).astype(BF16)
        values = act[...].reshape(group * images, act.shape[2])
        out[...] = dot(spread, values).reshape(out.shape)

    @pl.when(m == 0)
    def _():
        prepare(slots_0)
        term(act_0)

    @pl.when(m == 1)
    def _():
        prepare(slots_1)
        term(act_1)


def weight_grads(slots_0, act_0, slots_1, act_1):
    experts, images, rows = slots_0.shape
    hidden = act_0.shape[2]
    group, d_block = 8, 96
    last = experts // group - 1

    def early(m, g, d):
        return jnp.where(m == 0, g, last), 0, 0

    def late(m, g, d):
        return jnp.where(m == 0, 0, g), 0, 0

    slots, act = (group, images, rows), (group, images, hidden)
    return pl.pallas_call(
        weight_grad_kernel,
        grid=(2, experts // group, rows // d_block),
        out_shape=jax.ShapeDtypeStruct((rows, 2, experts, hidden), F32),
        in_specs=[
            pl.BlockSpec(slots, early), pl.BlockSpec(act, early),
            pl.BlockSpec(slots, late), pl.BlockSpec(act, late),
        ],
        out_specs=pl.BlockSpec((d_block, 1, group, hidden), lambda m, g, d: (d, m, g, 0)),
        scratch_shapes=[
            pltpu.VMEM((rows, group * images), BF16),
            pltpu.VMEM((group * d_block, d_block), BF16),
            pltpu.VMEM((group * d_block, group * images), F32),
        ],
        compiler_params=pltpu.CompilerParams(vmem_limit_bytes=VMEM_BYTES),
        cost_estimate=pl.CostEstimate(
            flops=4 * images * experts * rows * hidden,
            bytes_accessed=8 * rows * experts * hidden,
            transcendentals=0,
        ),
        name="weight_grads",
    )(slots_0, act_0, slots_1, act_1)


def dot_r(a, b):
    return lax.dot_general(a, b, (((0,), (0,)), ((), ())), preferred_element_type=F32)


def row_of(shape, axis):
    return lax.broadcasted_iota(jnp.int32, shape, axis)


def one_hot(mask):
    return mask.astype(F32).astype(BF16)


def order_matrix(n_h, few, back):
    n = n_h * 8 * few
    shape = (n, n)
    blocked, natural = row_of(shape, 1 if back else 0), row_of(shape, 0 if back else 1)
    f, half, image = blocked % few, (blocked // few) % 2, (blocked // (2 * few)) % 2
    group = blocked // (4 * few)
    if back:
        part, h = group // n_h, group % n_h
    else:
        h, part = group // 2, group % 2
    expert = ((h * 2 + half) * 2 + part) * few + f
    return one_hot(natural == image * (4 * n_h * few) + expert)


def norm_parts(x, scale, shift, live):
    centered = x - jnp.mean(x, axis=-1, keepdims=True)
    inverse = lax.rsqrt(jnp.mean(centered * centered, axis=-1, keepdims=True) + epsilon)
    unit = centered * inverse
    return unit * scale + shift, unit, inverse


def norm_back(grad, unit, inverse, scale):
    scaled = grad * scale
    average = jnp.mean(scaled, axis=-1, keepdims=True)
    projection = jnp.mean(scaled * unit, axis=-1, keepdims=True)
    return (
        inverse * (scaled - average - unit * projection),
        jnp.sum(grad * unit, axis=0, keepdims=True),
        jnp.sum(grad, axis=0, keepdims=True),
    )


def norm_rows(small):
    return jnp.swapaxes(small[:, 128:].astype(F32), 0, 1)[64:68]


def slots_to_blocks(slots, blocks, columns, joined, order):
    n_h, n_s = blocks.shape[:2]
    turned = dot(order, slots).astype(BF16)
    wide = joined.shape[1] // 2
    for s in range(0, n_s, 2):
        lanes = dot(turned[:, s * columns : (s + 2) * columns], joined).astype(BF16)
        for h in range(n_h):
            for p in range(2):
                rows = (h * 2 + p) * 16
                for e in range(2):
                    blocks[h, s + e, p] = lanes[rows : rows + 16, e * wide : e * wide + columns]


def blocks_to_slots(back, sizes, order, pair, padded):
    n_s, n_h, n_t = sizes
    columns = back.shape[3]
    both = jnp.concatenate([order] * n_t, axis=1)
    results = []
    for s in range(n_s):
        rows = jnp.concatenate(
            [
                back[p, (s * n_h + h) * n_t + t]
                for t in range(n_t)
                for p in range(2)
                for h in range(n_h)
            ],
            axis=0,
        )
        padded[s % 2, :, :columns] = dot(both, rows)
        if s % 2:
            value = jnp.concatenate([padded[0], padded[1]], axis=1)
            high = value.astype(BF16)
            rest = (value - high.astype(F32)).astype(BF16)
            results.append(dot(high, pair) + dot(rest, pair))
    return jnp.concatenate(results, axis=1)


def live_rows(shape, length):
    return row_of(shape, 0) < length


def ahead_kernel(
    length, tokens, small, w_hbm, blocks, normed_1, query, keyed, valued, context, hidden, normed_2,
    dispatch_out, combine_out, w, joined, order, w_sem,
):
    n, rows, width = tokens.shape
    keys = keyed.shape[1]
    loads = [pltpu.make_async_copy(w_hbm.at[k], w.at[k], w_sem.at[k]) for k in range(4)]
    for load in loads:
        load.start()
    norms = norm_rows(small)
    live = live_rows((rows, 1), length)
    for i in range(n):
        value, _, _ = norm_parts(tokens[i].astype(F32), norms[0:1], norms[2:3], live)
        normed_1[i] = jnp.where(live, value, 0.0).astype(BF16)
    joined[...] = pair_matrix(blocks.shape[4], joined.shape[1] // 2, True)
    order[...] = order_matrix(blocks.shape[0], 4, False)
    flat = (n * rows, width)
    for k, target in enumerate((query, keyed, valued)):
        loads[k].wait()
        value = dot(normed_1[...].reshape(flat), w[k]).astype(BF16).reshape(n, rows, width)
        if k == 0:
            target[...] = value
        else:
            target[:, :rows] = value
            target[:, rows:] = jnp.zeros((n, keys - rows, width), BF16)
    factor = HEAD_DIM ** (-0.5)
    pairs = width // 128
    lane = row_of((rows, 128), 1)
    shown = row_of((rows, keys), 1) < length

    def attend(step, carry):
        i = step // pairs
        lanes = pl.ds(pl.multiple_of((step % pairs) * 128, 128), 128)
        q, k, v = query[i, :, lanes], keyed[i, :, lanes], valued[i, :, lanes]
        parts = []
        for a in range(2):
            mine = (lane < 64) if a == 0 else (lane >= 64)
            scores = dot_t(jnp.where(mine, q, jnp.zeros_like(q)), k) * factor
            scores = jnp.where(shown, scores, -1e30)
            exponent = jnp.exp(scores - jnp.max(scores, axis=-1, keepdims=True))
            probs = exponent / jnp.sum(exponent, axis=-1, keepdims=True)
            parts.append(dot(probs.astype(BF16), v))
        context[i, :, lanes] = jnp.where(lane < 64, parts[0], parts[1]).astype(BF16)
        return carry

    lax.fori_loop(0, n * pairs, attend, 0, unroll=2)
    loads[3].wait()
    attended = dot_t(context[...].reshape(flat), w[3]).reshape(n, rows, width)
    for i in range(n):
        value = tokens[i].astype(F32) + attended[i]
        hidden[i] = value
        value, _, _ = norm_parts(value, norms[1:2], norms[3:4], live)
        normed_2[i] = jnp.where(live, value, 0.0).astype(BF16)
    logits = dot(normed_2[...].reshape(flat), small[:, :128]).reshape(n, rows, 128)
    experts = row_of((rows, 128), 1) < 64
    slots = []
    for i in range(n):
        here = logits[i]
        down = jnp.where(live, here, -1e30)
        exponent = jnp.exp(down - jnp.max(down, axis=0, keepdims=True))
        dispatch = exponent / jnp.sum(exponent, axis=0, keepdims=True)
        dispatch = jnp.where(experts, dispatch, 0.0)
        across = jnp.where(experts, here, -1e30)
        exponent = jnp.exp(across - jnp.max(across, axis=1, keepdims=True))
        combine = exponent / jnp.sum(exponent, axis=1, keepdims=True)
        dispatch_out[i] = dispatch
        combine_out[i] = combine
        slots.append(dot_r(dispatch.astype(BF16), normed_2[i])[:64].astype(BF16))
    slots_to_blocks(
        jnp.concatenate(slots, axis=0), blocks, blocks.shape[4], joined[...], order[...]
    )


def tokens_ahead(sizes, length, tokens, small, weights):
    n, rows, width = tokens.shape
    keys = 256
    vmem = pl.BlockSpec(memory_space=pltpu.VMEM)
    shape = jax.ShapeDtypeStruct
    wide = (n, keys, width)
    thin = shape((n, rows, 128), F32)
    return pl.pallas_call(
        partial(ahead_kernel, length),
        out_shape=(
            shape((sizes[1], sizes[0], 2, 16, width // sizes[0]), BF16),
            shape(tokens.shape, BF16), shape(tokens.shape, BF16), shape(wide, BF16),
            shape(wide, BF16), shape(tokens.shape, BF16), shape(tokens.shape, F32),
            shape(tokens.shape, BF16), thin, thin,
        ),
        in_specs=[vmem, vmem, pl.BlockSpec(memory_space=pl.ANY)],
        out_specs=(vmem,) * 10,
        scratch_shapes=[
            pltpu.VMEM(weights.shape, BF16),
            pltpu.VMEM((2 * width // sizes[0], 512), BF16),
            pltpu.VMEM((128, 128), BF16),
            pltpu.SemaphoreType.DMA((4,)),
        ],
        compiler_params=pltpu.CompilerParams(vmem_limit_bytes=VMEM_BYTES),
        name="tokens_ahead",
    )(tokens, small, weights)


def middle_kernel(
    sizes, back, small, combine, hidden, cotangent, output, blocks, grad_logits, padded
):
    n, rows, _ = hidden.shape
    columns = back.shape[3]
    padded[...] = jnp.zeros_like(padded)
    pair = pair_matrix(columns, padded.shape[2], False)
    joined = pair_matrix(columns, padded.shape[2], True)
    total = blocks_to_slots(back, sizes, order_matrix(sizes[1], 4, True), pair, padded)
    bias = jnp.swapaxes(small[:, :128].astype(F32), 0, 1)[64:]
    slots = []
    for i in range(n):
        slot_out = (total[i * 64 : (i + 1) * 64] + bias).astype(BF16)
        combine_b = combine[i].astype(BF16)[:, :64]
        output[i] = (hidden[i] + dot(combine_b, slot_out)).astype(BF16)
        grad_combine = dot_t(cotangent[i], slot_out)
        weight = combine[i][:, :64]
        weighted = jnp.sum(weight * grad_combine, axis=1, keepdims=True)
        grad_logits[i] = weight * (grad_combine - weighted)
        slots.append(dot_r(combine_b, cotangent[i]).astype(BF16))
    slots_to_blocks(
        jnp.concatenate(slots, axis=0), blocks, columns, joined, order_matrix(sizes[1], 4, False)
    )


def tokens_middle(sizes, back, small, combine, hidden, cotangent):
    n, rows, width = hidden.shape
    vmem = pl.BlockSpec(memory_space=pltpu.VMEM)
    shape = jax.ShapeDtypeStruct
    return pl.pallas_call(
        partial(middle_kernel, sizes),
        out_shape=(
            shape(hidden.shape, BF16),
            shape((sizes[1], sizes[0], 2, 16, width // sizes[0]), BF16),
            shape((n, rows, 64), F32),
        ),
        in_specs=[vmem] * 5,
        out_specs=(vmem,) * 3,
        scratch_shapes=[pltpu.VMEM((2, 128, 256), F32)],
        compiler_params=pltpu.CompilerParams(vmem_limit_bytes=VMEM_BYTES),
        name="tokens_middle",
    )(back, small, combine, hidden, cotangent)


def behind_kernel(
    sizes, length, back, small, w_hbm, tokens, normed_1, query, keyed, valued, context, hidden,
    normed_2, dispatch, grad_logits, cotangent, grads, small_grads, input_grad,
    w, padded, grad_hidden, rounded, grad_context, grad_q, grad_k, grad_v, w_sem,
):
    n, rows, width = tokens.shape
    keys = keyed.shape[1]
    loads = [pltpu.make_async_copy(w_hbm.at[k], w.at[k], w_sem.at[k]) for k in range(4)]
    for load in loads:
        load.start()
    norms = norm_rows(small)
    padded[...] = jnp.zeros_like(padded)
    pair = pair_matrix(back.shape[3], padded.shape[2], False)
    grad_slots = blocks_to_slots(
        back, sizes, order_matrix(sizes[1], 4, True), pair, padded
    ).astype(BF16)
    phi = small[:, :64]
    phi_grad = jnp.zeros((width, 64), F32)
    sums = []
    flat = (n * rows, width)
    for i in range(n):
        slots = grad_slots[i * 64 : (i + 1) * 64]
        weight = dispatch[i][:, :64]
        grad_dispatch = dot_t(normed_2[i], slots)
        weighted = jnp.sum(weight * grad_dispatch, axis=0, keepdims=True)
        logits = (weight * (grad_dispatch - weighted) + grad_logits[i]).astype(BF16)
        phi_grad = phi_grad + dot_r(normed_2[i], logits)
        grad = dot(weight.astype(BF16), slots) + dot_t(logits, phi)
        _, unit, inverse = norm_parts(hidden[i], norms[1:2], norms[3:4], None)
        grad_in, scale_grad, bias_grad = norm_back(grad, unit, inverse, norms[1:2])
        value = cotangent[i].astype(F32) + grad_in
        grad_hidden[i] = value
        rounded[i] = value.astype(BF16)
        sums.append((scale_grad, bias_grad))
    scale_2, bias_2 = sums[0][0] + sums[1][0], sums[0][1] + sums[1][1]
    flat_rounded = rounded[...].reshape(flat)
    loads[3].wait()
    grad_context[...] = dot(flat_rounded, w[3]).astype(BF16).reshape(n, rows, width)
    grads[3] = dot_r(flat_rounded, context[...].reshape(flat)).astype(BF16)
    factor = HEAD_DIM ** (-0.5)
    pairs = width // 128
    lane = row_of((rows, 128), 1)
    key_lane = row_of((keys, 128), 1)
    shown = row_of((rows, keys), 1) < length

    def attend(step, carry):
        i = step // pairs
        lanes = pl.ds(pl.multiple_of((step % pairs) * 128, 128), 128)
        q, k, v = query[i, :, lanes], keyed[i, :, lanes], valued[i, :, lanes]
        g = grad_context[i, :, lanes]
        to_q, to_k, to_v = [], [], []
        for a in range(2):
            mine = (lane < 64) if a == 0 else (lane >= 64)
            scores = dot_t(jnp.where(mine, q, jnp.zeros_like(q)), k) * factor
            grad_probs = dot_t(jnp.where(mine, g, jnp.zeros_like(g)), v)
            scores = jnp.where(shown, scores, -1e30)
            exponent = jnp.exp(scores - jnp.max(scores, axis=-1, keepdims=True))
            probs = exponent / jnp.sum(exponent, axis=-1, keepdims=True)
            weighted = jnp.sum(probs * grad_probs, axis=-1, keepdims=True)
            grad_scores = (probs * (grad_probs - weighted)).astype(BF16)
            to_v.append(dot_r(probs.astype(BF16), g))
            to_q.append(dot(grad_scores, k))
            to_k.append(dot_r(grad_scores, q))
        grad_q[i, :, lanes] = (jnp.where(lane < 64, to_q[0], to_q[1]) * factor).astype(BF16)
        kept = key_lane < 64
        grad_k[i, :, lanes] = (jnp.where(kept, to_k[0], to_k[1]) * factor)[:rows].astype(BF16)
        grad_v[i, :, lanes] = jnp.where(kept, to_v[0], to_v[1])[:rows].astype(BF16)
        return carry

    lax.fori_loop(0, n * pairs, attend, 0, unroll=2)
    total = jnp.zeros(flat, F32)
    turned = jnp.swapaxes(normed_1[...].reshape(flat).astype(F32), 0, 1).astype(BF16)
    for k, source in enumerate((grad_q, grad_k, grad_v)):
        loads[k].wait()
        value = source[...].reshape(flat)
        total = total + dot_t(value, w[k])
        grads[k] = dot(turned, value).astype(BF16)
    total = total.reshape(n, rows, width)
    sums = []
    for i in range(n):
        _, unit, inverse = norm_parts(tokens[i].astype(F32), norms[0:1], norms[2:3], None)
        grad_in, scale_grad, bias_grad = norm_back(total[i], unit, inverse, norms[0:1])
        input_grad[i] = (grad_hidden[i] + grad_in).astype(BF16)
        sums.append((scale_grad, bias_grad))
    scale_1, bias_1 = sums[0][0] + sums[1][0], sums[0][1] + sums[1][1]
    line = row_of((128, width), 0)
    spread = jnp.zeros((128, width), F32)
    for j, value in enumerate((scale_1, scale_2, bias_1, bias_2)):
        spread = jnp.where(line == 64 + j, value, spread)
    small_grads[...] = jnp.swapaxes(spread, 0, 1).astype(BF16)
    small_grads[:, :64] = phi_grad.astype(BF16)


def tokens_behind(sizes, length, back, small, weights, tokens, kept, grad_logits, cotangent):
    n, rows, width = tokens.shape
    vmem = pl.BlockSpec(memory_space=pltpu.VMEM)
    shape = jax.ShapeDtypeStruct
    low = pltpu.VMEM(tokens.shape, BF16)
    return pl.pallas_call(
        partial(behind_kernel, sizes, length),
        out_shape=(
            shape((4, width, width), BF16), shape((width, 128), BF16), shape(tokens.shape, BF16)
        ),
        in_specs=[vmem, vmem, pl.BlockSpec(memory_space=pl.ANY)] + [vmem] * 11,
        out_specs=(vmem,) * 3,
        scratch_shapes=[
            pltpu.VMEM(weights.shape, BF16),
            pltpu.VMEM((2, 128, 256), F32),
            pltpu.VMEM(tokens.shape, F32),
            low, low, low, low, low,
            pltpu.SemaphoreType.DMA((4,)),
        ],
        compiler_params=pltpu.CompilerParams(vmem_limit_bytes=VMEM_BYTES),
        name="tokens_behind",
    )(back, small, weights, tokens, *kept, grad_logits, cotangent)


def normalize(values, scale, shift):
    centered = values - jnp.mean(values, axis=-1, keepdims=True)
    variance = jnp.mean(centered * centered, axis=-1, keepdims=True)
    inverse = lax.rsqrt(variance + epsilon)
    unit_part = centered * inverse
    return (unit_part * scale + shift, unit_part, inverse)


def normalize_back(grad_output, unit_part, inverse, scale):
    scaled = grad_output * scale
    average = jnp.mean(scaled, axis=-1, keepdims=True)
    projection = jnp.mean(scaled * unit_part, axis=-1, keepdims=True)
    grad_input = inverse * (scaled - average - unit_part * projection)
    return (
        grad_input,
        jnp.sum(grad_output * unit_part, axis=(0, 1)),
        jnp.sum(grad_output, axis=(0, 1)),
    )


def to_experts(slots):
    slots = lax.all_to_all(slots, "heads", split_axis=1, concat_axis=0, tiled=True)
    slots = lax.all_to_all(slots, "shard", split_axis=2, concat_axis=0, tiled=True)
    return lax.all_gather(slots, "tensor", axis=0, tiled=True)


def to_images(slots):
    slots = lax.psum_scatter(slots, "tensor", scatter_dimension=0, tiled=True)
    slots = lax.all_to_all(slots, "shard", split_axis=0, concat_axis=2, tiled=True)
    return lax.all_to_all(slots, "heads", split_axis=0, concat_axis=1, tiled=True)


def general_shards(tokens, norm_scales, norm_biases, w_attn, phi, experts, in_bias, out_bias, cotangent):
    heads_n = lax.axis_size("heads")
    group, seq_len, width = tokens.shape
    own = group // heads_n
    heads_index = lax.axis_index("heads")
    tensor_index = lax.axis_index("tensor")
    shard_index = lax.axis_index("shard")
    hidden = experts.shape[3]
    rows = experts.shape[0]
    scales, biases, in_full = (
        lax.all_gather(norm_scales, ROWS, axis=1, tiled=True).astype(F32),
        lax.all_gather(norm_biases, ROWS, axis=1, tiled=True).astype(F32),
        lax.all_gather(in_bias, ROWS, axis=1, tiled=True).astype(F32),
    )
    attn = lax.all_gather(
        lax.all_gather(w_attn, "heads", axis=2, tiled=True), ROWS, axis=1, tiled=True
    )
    phi_full = lax.all_gather(
        lax.all_gather(phi, "heads", axis=1, tiled=True), ROWS, axis=0, tiled=True
    )
    out_rows = lax.all_gather(out_bias, "tensor", axis=1, tiled=True).astype(F32)
    e_own = experts.shape[2] // lax.axis_size("shard")
    in_local = lax.dynamic_slice_in_dim(in_full, tensor_index * hidden, hidden, 1)
    factor = HEAD_DIM ** (-0.5)
    tokens = lax.dynamic_slice_in_dim(tokens, heads_index * own, own, 0)
    cotangent = lax.dynamic_slice_in_dim(cotangent, heads_index * own, own, 0)
    n_heads = width // HEAD_DIM
    inputs = tokens.astype(F32)
    normed_one, unit_one, inverse_one = normalize(inputs, scales[0], biases[0])
    normed_one_b = normed_one.astype(BF16)
    projected = einsum("nsd,kdc->knsc", normed_one_b, attn[:3]).astype(BF16)
    query, keyed, valued = projected.reshape(3, own, seq_len, n_heads, HEAD_DIM)
    scores = einsum("nqhe,nkhe->nhqk", query, keyed) * factor
    score_peak = jnp.max(scores, axis=-1, keepdims=True)
    exponent = jnp.exp(scores - score_peak)
    probs = exponent / jnp.sum(exponent, axis=-1, keepdims=True)
    probs_b = probs.astype(BF16)
    context_b = (
        einsum("nhqk,nkhe->nqhe", probs_b, valued).astype(BF16).reshape(own, seq_len, width)
    )
    hidden_one = inputs + einsum("nsc,dc->nsd", context_b, attn[3])
    normed_two, unit_two, inverse_two = normalize(hidden_one, scales[1], biases[1])
    normed_two_b = normed_two.astype(BF16)
    logits = einsum("nsd,de->nse", normed_two_b, phi_full)
    dispatch = jax.nn.softmax(logits, axis=1)
    dispatch_b = dispatch.astype(BF16)
    combine = jax.nn.softmax(logits, axis=2)
    combine_b = combine.astype(BF16)
    slot_in = to_experts(einsum("nse,nsd->ned", dispatch_b, normed_two_b).astype(BF16))
    share = 1 if e_own else 0

    def meet(partial_sum):
        return lax.psum_scatter(partial_sum, "shard", scatter_dimension=share, tiled=True)

    def spread(values):
        return lax.all_gather(values, "shard", axis=share, tiled=True)

    pre = meet(einsum("ned,def->nef", slot_in, experts[:, 0]))
    if e_own:
        pre = pre + lax.dynamic_slice_in_dim(in_local, shard_index * e_own, e_own, 0)
    else:
        pre = pre + in_local
    gelu_value, gelu_back = jax.vjp(partial(jax.nn.gelu, approximate=False), pre)
    activated = spread(gelu_value.astype(BF16))
    slot_out_part = einsum("nef,def->ned", activated, experts[:, 1])
    slot_out_part = slot_out_part + jnp.where(tensor_index == 0, out_rows, 0.0)
    slot_out = to_images(slot_out_part).astype(BF16)
    output = (hidden_one + einsum("nse,ned->nsd", combine_b, slot_out)).astype(BF16)
    output = lax.all_gather(output, "heads", axis=0, tiled=True)
    grad_combine = einsum("nsd,ned->nse", cotangent, slot_out)
    grad_slot = to_experts(einsum("nse,nsd->ned", combine_b, cotangent).astype(BF16))
    grad_act = meet(einsum("ned,def->nef", grad_slot, experts[:, 1]))
    grad_pre = spread(gelu_back(grad_act)[0].astype(BF16))
    grad_slot_in = einsum("nef,def->ned", grad_pre, experts[:, 0]).astype(BF16)
    input_term = einsum("ned,nef->def", slot_in, grad_pre)
    output_term = einsum("ned,nef->def", grad_slot, activated)
    experts_grad = jnp.stack((input_term, output_term), axis=1)
    grad_slot_in = to_images(grad_slot_in.astype(F32)).astype(BF16)
    in_bias_grad = lax.dynamic_slice_in_dim(
        lax.all_gather(jnp.sum(grad_pre.astype(F32), axis=0), "tensor", axis=1, tiled=True),
        (shard_index * lax.axis_size("tensor") + tensor_index) * in_bias.shape[1],
        in_bias.shape[1],
        1,
    )
    out_bias_grad = lax.dynamic_slice_in_dim(
        jnp.sum(grad_slot.astype(F32), axis=0),
        tensor_index * out_bias.shape[1],
        out_bias.shape[1],
        1,
    )
    grad_dispatch = einsum("nsd,ned->nse", normed_two_b, grad_slot_in)
    grad_logits = (
        dispatch * (grad_dispatch - jnp.sum(dispatch * grad_dispatch, axis=1, keepdims=True))
        + combine * (grad_combine - jnp.sum(combine * grad_combine, axis=2, keepdims=True))
    ).astype(BF16)
    phi_grad = einsum("nsd,nse->de", normed_two_b, grad_logits)
    grad_normed_two = einsum("nse,ned->nsd", dispatch_b, grad_slot_in) + einsum(
        "nse,de->nsd", grad_logits, phi_full
    )
    grad_hidden_norm, scale_two_grad, bias_two_grad = normalize_back(
        grad_normed_two, unit_two, inverse_two, scales[1]
    )
    grad_hidden = cotangent.astype(F32) + grad_hidden_norm
    grad_hidden_b = grad_hidden.astype(BF16)
    out_weight_grad = einsum("nsd,nsc->dc", grad_hidden_b, context_b)
    grad_context = einsum("nsd,dc->nsc", grad_hidden_b, attn[3]).astype(BF16)
    grad_context = grad_context.reshape(own, seq_len, n_heads, HEAD_DIM)
    grad_value = einsum("nhqk,nqhe->nkhe", probs_b, grad_context).astype(BF16)
    grad_probs = einsum("nqhe,nkhe->nhqk", grad_context, valued)
    grad_scores = (
        probs * (grad_probs - jnp.sum(probs * grad_probs, axis=-1, keepdims=True))
    ).astype(BF16)
    grad_query = (einsum("nhqk,nkhe->nqhe", grad_scores, keyed) * factor).astype(BF16)
    grad_key = (einsum("nhqk,nqhe->nkhe", grad_scores, query) * factor).astype(BF16)
    grad_proj = jnp.stack((grad_query, grad_key, grad_value)).reshape(3, own, seq_len, width)
    proj_grad = einsum("nsd,knsc->kdc", normed_one_b, grad_proj)
    grad_normed_one = einsum("knsc,kdc->nsd", grad_proj, attn[:3])
    grad_input_norm, scale_one_grad, bias_one_grad = normalize_back(
        grad_normed_one, unit_one, inverse_one, scales[0]
    )
    input_grad = (grad_hidden + grad_input_norm).astype(BF16)
    input_grad = lax.all_gather(input_grad, "heads", axis=0, tiled=True)
    attn_grad = jnp.concatenate((proj_grad, out_weight_grad[None]), axis=0)
    attn_grad = lax.psum_scatter(attn_grad, ROWS, scatter_dimension=1, tiled=True)
    attn_grad = lax.psum_scatter(attn_grad, "heads", scatter_dimension=2, tiled=True)
    phi_grad = lax.psum_scatter(phi_grad, ROWS, scatter_dimension=0, tiled=True)
    phi_grad = lax.psum_scatter(phi_grad, "heads", scatter_dimension=1, tiled=True)
    norms = jnp.stack((scale_one_grad, scale_two_grad, bias_one_grad, bias_two_grad))
    norms = lax.psum(lax.psum_scatter(norms, ROWS, scatter_dimension=1, tiled=True), "heads")
    return (
        output,
        input_grad,
        norms[:2],
        norms[2:],
        attn_grad,
        phi_grad,
        experts_grad,
        in_bias_grad,
        out_bias_grad,
    )


def shards(tokens, norm_scales, norm_biases, w_attn, phi, experts, in_bias, out_bias, cotangent):
    arrays = (tokens, norm_scales, norm_biases, w_attn, phi, experts, in_bias, out_bias, cotangent)
    sizes = tuple(lax.axis_size(name) for name in ("shard", "heads", "tensor"))
    group, length, width = tokens.shape
    fits = (sizes, group, width, *experts.shape[:3]) == ((4, 4, 2), 8, 768, 192, 2, 16)
    if not fits or length > 208 or in_bias.shape[1] != 384:
        return general_shards(*arrays)
    n_s, n_h, n_t = sizes
    own = group // n_h
    block, slot = w_attn.shape[2], phi.shape[1]
    beside = jnp.concatenate((phi, out_bias.T), axis=1)
    beside = jnp.pad(beside, ((0, 0), (0, 256 - block - 2 * slot)))
    beside = jnp.concatenate((beside[None], jnp.zeros((3, *beside.shape), BF16)), axis=0)
    packet = jnp.concatenate((w_attn, beside), axis=2)
    hidden_bias = in_bias.reshape(16, 6, 64).transpose(1, 0, 2).reshape(96, 64)
    extra = jnp.concatenate((hidden_bias, norm_scales.T, norm_biases.T), axis=1)
    extra = jnp.pad(extra, ((0, 0), (128, 60)))
    attn, small, turned = gather_weights(sizes, packet, extra, experts)

    def mine(values):
        values = lax.dynamic_slice_in_dim(values, lax.axis_index("heads") * own, own, 0)
        return jnp.pad(values, ((0, 0), (0, 208 - length), (0, 0)))

    tokens, cotangent = mine(tokens), mine(cotangent)
    blocks, *kept, combine = tokens_ahead(sizes, length, tokens, small, attn)
    hidden = kept[5]
    slot_in, activated, gate, back = expert_pass(sizes, False, blocks, turned, small)
    output, blocks, grad_logits = tokens_middle(sizes, back, small, combine, hidden, cotangent)
    grad_slot, grad_pre, back, in_bias_grad, out_sum, output = expert_pass(
        sizes, True, blocks, turned, gate, output, in_bias.shape[1]
    )
    attn_grad, small_grad, input_grad = tokens_behind(
        sizes, length, back, small, attn, tokens, kept, grad_logits, cotangent
    )
    input_grad = lax.all_gather(input_grad, "heads", axis=0, tiled=True)
    attn_grad, grad_pre = lax.optimization_barrier((attn_grad, grad_pre))
    experts_grad = weight_grads(slot_in, grad_pre, grad_slot, activated)
    attn_grad, experts_grad = lax.optimization_barrier((attn_grad, experts_grad))
    summed = reduce_grads(sizes, attn_grad, small_grad)
    norms = summed[0, :, block + slot : block + slot + 4].T
    out_bias_grad = lax.dynamic_slice_in_dim(
        out_sum, lax.axis_index("tensor") * out_bias.shape[1], out_bias.shape[1], 1
    )
    return (
        output[:, :length],
        input_grad[:, :length],
        norms[:2],
        norms[2:],
        summed[:, :, :block],
        summed[0, :, block : block + slot],
        experts_grad,
        in_bias_grad,
        out_bias_grad,
    )


def solution(mesh):
    images = P(ROWS, None, None)
    return jax.shard_map(
        shards,
        mesh=mesh,
        in_specs=(
            images,
            P(None, ROWS),
            P(None, ROWS),
            P(None, ROWS, "heads"),
            P(ROWS, "heads"),
            P("shard", None, "heads", "tensor"),
            P("heads", ROWS),
            P("heads", ROWS),
            images,
        ),
        out_specs=(
            images,
            images,
            P(None, ROWS),
            P(None, ROWS),
            P(None, ROWS, "heads"),
            P(ROWS, "heads"),
            P("shard", None, "heads", "tensor"),
            P("heads", ROWS),
            P("heads", ROWS),
        ),
        check_vma=False,
    )
```

```python
from functools import partial

import jax
import jax.numpy as jnp
from jax import lax
from jax.experimental import pallas as pl
from jax.experimental.pallas import tpu as pltpu
from jax.sharding import PartitionSpec as P

HEAD_DIM = 64
F32 = jnp.float32
BF16 = jnp.bfloat16
ROWS = ("shard", "tensor")
MESH = pl.DeviceIdType.MESH
VMEM_BYTES = 58 * 1024 * 1024
epsilon = 1e-06
einsum = partial(jnp.einsum, preferred_element_type=F32)


def dot(a, b):
    return lax.dot_general(a, b, (((1,), (0,)), ((), ())), preferred_element_type=F32)


def dot_t(a, b):
    return lax.dot_general(a, b, (((1,), (1,)), ((), ())), preferred_element_type=F32)


def swap_matrix(n):
    out = lax.broadcasted_iota(jnp.int32, (n * n, n * n), 0)
    row = lax.broadcasted_iota(jnp.int32, (n * n, n * n), 1)
    return ((out // n == row % n) & (out % n == row // n)).astype(F32).astype(BF16)


class Peers:
    def __init__(self, sizes):
        self.sizes = sizes
        self.at = tuple(lax.axis_index(name) for name in ("shard", "heads", "tensor"))
        self.count = sizes[0] * sizes[1] * sizes[2]

    def flat(self, place):
        return (place[0] * self.sizes[1] + place[1]) * self.sizes[2] + place[2]

    def step(self, k, sign):
        _, n_h, n_t = self.sizes
        steps = (k // (n_h * n_t), (k // n_t) % n_h, k % n_t)
        return tuple(
            lax.rem(at + n + sign * d, n) for at, n, d in zip(self.at, self.sizes, steps)
        )

    def greet_all(self):
        barrier = pltpu.get_barrier_semaphore()

        def signal(k, carry):
            pl.semaphore_signal(barrier, inc=1, device_id=self.step(k, 1), device_id_type=MESH)
            return carry

        lax.fori_loop(1, self.count, signal, 0)
        pl.semaphore_wait(barrier, self.count - 1)


def remote(src, dst, send, recv, place):
    return pltpu.make_async_remote_copy(
        src_ref=src, dst_ref=dst, send_sem=send, recv_sem=recv, device_id=place, device_id_type=MESH
    )


def plane(sizes):
    n_s, n_h, n_t = sizes
    s, h, t = (lax.axis_index(name) for name in ("shard", "heads", "tensor"))
    core, chip = lax.rem(s, 2), s // 2
    sibling = (s + 1 - 2 * core, h, t)
    across_x = (lax.rem(s + 2, n_s), h, t)
    across_y = (s, h, 1 - t)
    line = [(s, lax.rem(h + d, n_h), t) for d in range(n_h)]
    barrier = pltpu.get_barrier_semaphore()
    others = [sibling, across_x, across_y] + line[1:]
    for place in others:
        pl.semaphore_signal(barrier, inc=1, device_id=place, device_id_type=MESH)
    pl.semaphore_wait(barrier, len(others))
    return (s, h, t), core, chip, sibling, across_x, across_y, line


def pair_matrix(block, wide, transposed):
    shape = (2 * block, 2 * wide) if transposed else (2 * wide, 2 * block)
    tight = lax.broadcasted_iota(jnp.int32, shape, 0 if transposed else 1)
    padded = lax.broadcasted_iota(jnp.int32, shape, 1 if transposed else 0)
    second = padded >= wide
    lane = jnp.where(second, padded - wide, padded)
    same = (lane < block) & (tight == jnp.where(second, lane + block, lane))
    return same.astype(F32).astype(BF16)


def gather_kernel(
    sizes, packet, extra, experts, tokens, cotangent, w_out, small_out, turned, own_tokens, own_cot,
    w, small, lined, tile_in, tile_out, images, picked,
    z_send, z_recv, x_sems, y_sems, d_sems, c_sems, t_sems, o_sems, i_sems,
):
    (s, h, t), core, chip, sibling, across_x, across_y, line = plane(sizes)
    n_k, rows, wide = packet.shape
    n_h, n_t = sizes[1], sizes[2]
    width = w.shape[2]
    block = width // n_h
    side = 16
    n_tiles = experts.shape[0] // side
    depth = tile_in.shape[0]
    halves = ((0, rows // 2), (rows // 2, rows // 2))

    def z_hop(k, origin, up):
        place = line[1] if up else line[n_h - 1]
        return remote(
            lined.at[origin, k], lined.at[origin, k],
            z_send.at[k, origin, up], z_recv.at[k, origin], place,
        )

    def relay(k, d):
        @pl.when(h >= d)
        def _():
            z_hop(k, h - d, 1).wait_recv()

            @pl.when(h < n_h - 1)
            def _():
                z_hop(k, h - d, 1).start()

        @pl.when(h + d < n_h)
        def _():
            z_hop(k, h + d, 0).wait_recv()

            @pl.when(h > 0)
            def _():
                z_hop(k, h + d, 0).start()

    chunks = (0, 2, 1, 3)
    lined[h] = packet[...]
    for k in chunks:
        @pl.when(h < n_h - 1)
        def _():
            z_hop(k, h, 1).start()

        @pl.when(h > 0)
        def _():
            z_hop(k, h, 0).start()

    def load(i):
        return pltpu.make_async_copy(
            experts.at[pl.ds((i % n_tiles) * side, side), i // n_tiles],
            tile_in.at[i % depth],
            t_sems.at[0, i % depth],
        )

    def store(i):
        return pltpu.make_async_copy(
            tile_out.at[i % depth],
            turned.at[i // n_tiles, :, pl.ds((i % n_tiles) * side, side)],
            t_sems.at[1, i % depth],
        )

    image_loads = [
        pltpu.make_async_copy(source, images.at[j], i_sems.at[0, j])
        for j, source in enumerate((tokens, cotangent))
    ]
    for i in range(depth - 1):
        load(i).start()
    for copy in image_loads:
        copy.start()
    swap = swap_matrix(side)
    done = [0]

    def turn(count):
        def step(i, carry):
            load(i).wait()

            @pl.when(i + depth - 1 < 2 * n_tiles)
            def _():
                load(i + depth - 1).start()

            @pl.when(i >= depth)
            def _():
                store(i - depth).wait()

            rows_in = tile_in[i % depth].reshape(side * side, tile_in.shape[3])
            tile_out[i % depth] = dot(swap, rows_in).astype(BF16).reshape(tile_out.shape[1:])
            store(i).start()
            return carry

        last = min(done[0] + count, 2 * n_tiles)
        lax.fori_loop(done[0], last, step, 0)
        done[0] = last

    pair = pair_matrix(block, wide, False)
    shape = (n_h * wide, small.shape[1])
    row = lax.broadcasted_iota(jnp.int32, shape, 0)
    column = lax.broadcasted_iota(jnp.int32, shape, 1)
    lane, of = row % wide - block, row // wide
    beside = (lane >= 0) & (lane < 16) & (column == of * 16 + lane)
    beside |= (lane >= 16) & (lane < 32) & (column == n_h * 16 + of * 16 + lane - 16)
    beside = beside.astype(F32).astype(BF16)

    image_stores = [
        pltpu.make_async_copy(picked.at[j], target, i_sems.at[1, j])
        for j, target in enumerate((own_tokens, own_cot))
    ]

    def pick_images(j):
        own, padded = picked.shape[1:3]
        group = own * n_h
        lines = images.shape[1]
        image_loads[j].wait()
        step = 256 // group
        for first in range(0, padded, step):
            count = min(step, padded - first)
            taken = min(step * group, lines - first * group)
            shape = (own * count, taken)
            row = lax.broadcasted_iota(jnp.int32, shape, 0)
            column = lax.broadcasted_iota(jnp.int32, shape, 1)
            wanted = (row % count) * group + own * h + row // count
            chosen = (column == wanted).astype(F32).astype(BF16)
            source = images[j, first * group : first * group + taken]
            picked[j, :, first : first + count] = (
                dot(chosen, source).astype(BF16).reshape(own, count, images.shape[2])
            )
        image_stores[j].start()

    def at(k, place):
        first = pl.multiple_of((place[0] * n_t + place[2]) * rows, 16)
        lines = pl.ds(first, rows)
        return small.at[lines] if k == n_k else w.at[k, lines]

    def hop(q, origin, place, sems, j):
        return remote(at(q, origin), at(q, origin), sems.at[0, j], sems.at[1, j], place)

    def half_hop(q, origin, place, half):
        part = at(q, origin).at[pl.ds(*halves[half])]
        j = 2 * q + half
        return remote(part, part, d_sems.at[0, j], d_sems.at[1, j], place)

    me = (s, h, t)
    from_d = (across_x[0], h, across_y[2])
    sent = []

    def send(copy):
        copy.start()
        sent.append(copy)

    def assemble(k):
        for i in range(0, n_h, 2):
            lines = jnp.concatenate([lined[i, k], lined[i + 1, k]], axis=1)
            at(k, me)[:, i * block : (i + 2) * block] = dot(lines, pair).astype(BF16)
        if k == 0:
            lines = jnp.concatenate([lined[i, k] for i in range(n_h)], axis=1)
            at(n_k, me)[...] = (dot(lines, beside) + extra[...].astype(F32)).astype(BF16)
        for q in members(k):
            send(hop(q, me, across_x, x_sems, q))
            send(hop(q, me, across_y, y_sems, q))
            send(hop(q, me, sibling, c_sems, 4 * q))

    def members(k):
        return (0, n_k) if k == 0 else (k,)

    def relay_xy(k):
        for q in members(k):
            hop(q, across_x, across_x, x_sems, q).wait_recv()
            send(half_hop(q, across_x, across_y, 0))
            send(hop(q, across_x, sibling, c_sems, 4 * q + 1))
            hop(q, across_y, across_y, y_sems, q).wait_recv()
            send(half_hop(q, across_y, across_x, 1))
            send(hop(q, across_y, sibling, c_sems, 4 * q + 2))

    def relay_d(k):
        for q in members(k):
            half_hop(q, from_d, across_y, 0).wait_recv()
            half_hop(q, from_d, across_x, 1).wait_recv()
            send(hop(q, from_d, sibling, c_sems, 4 * q + 3))

    for wave in range(n_k + n_h - 2):
        for d in range(1, n_h):
            if 0 <= wave - d + 1 < n_k:
                relay(chunks[wave - d + 1], d)
        turn(2)
        i = wave - n_h + 2
        if i >= 0:
            assemble(chunks[i])
            if i in (1, 2):
                pick_images(i - 1)
            if i >= 1:
                relay_xy(chunks[i - 1])
            if i >= 2:
                relay_d(chunks[i - 2])
            turn(2)
    relay_xy(chunks[-1])
    relay_d(chunks[-2])
    turn(2 * n_tiles)
    relay_d(chunks[-1])
    stores = []
    for k in chunks:
        for q in members(k):
            for j in range(4):
                hop(q, me, sibling, c_sems, 4 * q + j).wait_recv()
            if q == n_k:
                stores.append(pltpu.make_async_copy(small, small_out, o_sems.at[q]))
            else:
                stores.append(pltpu.make_async_copy(w.at[q], w_out.at[q], o_sems.at[q]))
            stores[-1].start()
    for copy in sent:
        copy.wait_send()
    for origin in range(n_h):
        @pl.when((origin <= h) & (h < n_h - 1))
        def _():
            for k in range(n_k):
                z_hop(k, origin, 1).wait_send()

        @pl.when((origin >= h) & (h > 0))
        def _():
            for k in range(n_k):
                z_hop(k, origin, 0).wait_send()

    for i in range(depth):
        store(2 * n_tiles - depth + i).wait()
    for copy in image_stores:
        copy.wait()
    for copy in stores:
        copy.wait()


def gather_weights(sizes, packet, extra, experts, tokens, cotangent):
    n_k, rows, wide = packet.shape
    n_s, n_h, n_t = sizes
    width = n_s * n_t * rows
    vmem = pl.BlockSpec(memory_space=pltpu.VMEM)
    hbm = pl.BlockSpec(memory_space=pl.ANY)
    dma = pltpu.SemaphoreType.DMA
    hidden = experts.shape[3]
    small = (width, extra.shape[1])
    images = jax.ShapeDtypeStruct((2, 208, width), BF16)
    return pl.pallas_call(
        partial(gather_kernel, sizes),
        out_shape=(
            jax.ShapeDtypeStruct((n_k, width, width), BF16),
            jax.ShapeDtypeStruct(small, BF16),
            jax.ShapeDtypeStruct((2, experts.shape[2], experts.shape[0], hidden), BF16),
            images, images,
        ),
        in_specs=[vmem, vmem, hbm, hbm, hbm],
        out_specs=(hbm,) * 5,
        scratch_shapes=[
            pltpu.VMEM((n_k, width, width), BF16),
            pltpu.VMEM(small, BF16),
            pltpu.VMEM((n_h, n_k, rows, wide), BF16),
            pltpu.VMEM((4, 16, 16, hidden), BF16),
            pltpu.VMEM((4, 16, 16, hidden), BF16),
            pltpu.VMEM((2, *tokens.shape), BF16),
            pltpu.VMEM((2, *images.shape), BF16),
            dma((n_k, n_h, 2)), dma((n_k, n_h)), dma((2, n_k + 1)), dma((2, n_k + 1)),
            dma((2, 2 * (n_k + 1))), dma((2, 4 * (n_k + 1))), dma((2, 4)), dma((n_k + 1,)),
            dma((2, 2)),
        ],
        compiler_params=pltpu.CompilerParams(
            collective_id=3, has_side_effects=True, vmem_limit_bytes=VMEM_BYTES
        ),
        name="gather_weights",
    )(packet, extra, experts, tokens, cotangent)


def reduce_kernel(
    sizes, grads, small, out, core_in, core_small, met, met_small,
    d_in, d_small, x_in, x_small, y_in, y_small, pieces, z_in,
    c_sems, d_sems, x_sems, y_sems, z_sems,
):
    (s, h, t), core, chip, sibling, across_x, across_y, line = plane(sizes)
    n_k, width, _ = grads.shape
    n_s, n_h, n_t = sizes
    rows = width // (n_s * n_t)
    wide = pieces.shape[3]
    pair = n_t * rows
    half = rows // 2
    halves = (pl.ds(0, half), pl.ds(half, half))
    chunks = (0, 2, 1, 3)

    def members(k):
        return (0, n_k) if k == 0 else (k,)

    def pick(q, large, little):
        return little if q == n_k else large.at[q]

    def core_copy(q, x):
        first = pl.multiple_of((2 * x + 1 - core) * pair, 16)
        return remote(
            pick(q, grads, small).at[pl.ds(first, pair)],
            pick(q, core_in, core_small).at[x],
            c_sems.at[0, 2 * q + x], c_sems.at[1, 2 * q + x], sibling,
        )

    for k in chunks:
        for q in members(k):
            for x in range(2):
                core_copy(q, x).start()
    joined = pair_matrix(width // n_h, wide, True)
    shape = (small.shape[1], n_h * wide)
    row = lax.broadcasted_iota(jnp.int32, shape, 0)
    column = lax.broadcasted_iota(jnp.int32, shape, 1)
    lane, of = column % wide - width // n_h, column // wide
    beside = (lane >= 0) & (lane < 16) & (row == of * 16 + lane)
    beside |= (lane >= 16) & (lane < 20) & (row == n_h * 16 + lane - 16)
    beside = beside.astype(F32).astype(BF16)
    to_d, to_x, to_y = (d_in, d_small), (x_in, x_small), (y_in, y_small)
    sent = []

    def hop(q, kind, part, source, place):
        sems = {id(to_d): d_sems, id(to_x): x_sems, id(to_y): y_sems}[id(kind)]
        target = pick(q, *kind)
        target = target.at[part] if kind is to_d else target.at[halves[part]]
        j = 2 * q + part
        return remote(source, target, sems.at[0, j], sems.at[1, j], place)

    def send(copy):
        copy.start()
        sent.append(copy)

    def part_of(q, x, y, part):
        return pick(q, met, met_small).at[x, y].at[halves[part]]

    def arrived(q, kind, part):
        hop(q, kind, part, part_of(q, 0, 0, part), sibling).wait_recv()

    def open_up(q):
        part = pick(q, met, met_small)
        for x in range(2):
            core_copy(q, x).wait_recv()
            first = pl.multiple_of((2 * x + core) * pair, 16)
            own = pick(q, grads, small)[pl.ds(first, pair)].astype(F32)
            total = own + pick(q, core_in, core_small)[x].astype(F32)
            part[x] = total.astype(BF16).reshape(n_t, rows, total.shape[1])
        send(hop(q, to_d, 0, part_of(q, 1 - chip, 1 - t, 0), across_x))
        send(hop(q, to_d, 1, part_of(q, 1 - chip, 1 - t, 1), across_y))
        send(hop(q, to_x, 0, part_of(q, 1 - chip, t, 0), across_x))
        send(hop(q, to_y, 1, part_of(q, chip, 1 - t, 1), across_y))

    def pass_on(q):
        for part, kind, x, y, place in (
            (0, to_y, chip, 1 - t, across_y),
            (1, to_x, 1 - chip, t, across_x),
        ):
            arrived(q, to_d, part)
            block = part_of(q, x, y, part)
            total = block[...].astype(F32) + pick(q, *to_d)[part].astype(F32)
            block[...] = total.astype(BF16)
            send(hop(q, kind, part, block, place))

    def whole(q):
        for kind in (to_x, to_y):
            for part in range(2):
                arrived(q, kind, part)
        total = pick(q, met, met_small)[chip, t].astype(F32) + pick(q, *to_x)[...].astype(F32)
        return (total + pick(q, *to_y)[...].astype(F32)).astype(BF16)

    def z_copy(k, d):
        return remote(
            pieces.at[line[d][1], k], z_in.at[h, k], z_sems.at[0, k, d], z_sems.at[1, k, d], line[d]
        )

    def share_out(k):
        value = whole(k)
        columns = width // n_h
        if k == 0:
            little = dot(whole(n_k), beside)
        for i in range(0, n_h, 2):
            lanes = dot(value[:, i * columns : (i + 2) * columns], joined)
            if k == 0:
                lanes = lanes + little[:, i * wide : (i + 2) * wide]
            pieces[i, k] = lanes[:, :wide].astype(BF16)
            pieces[i + 1, k] = lanes[:, wide:].astype(BF16)
        for d in range(n_h - 1, 0, -1):
            z_copy(k, d).start()

    for i in range(n_k + 2):
        if i < n_k:
            for q in members(chunks[i]):
                open_up(q)
        if 0 <= i - 1 < n_k:
            for q in members(chunks[i - 1]):
                pass_on(q)
        if i >= 2:
            share_out(chunks[i - 2])
    for k in chunks:
        total = pieces[h, k].astype(F32)
        for d in range(1, n_h):
            z_copy(k, d).wait_recv()
        for d in range(1, n_h):
            total = total + z_in[line[d][1], k].astype(F32)
        out[k] = total
    for k in chunks:
        for q in members(k):
            for x in range(2):
                core_copy(q, x).wait_send()
    for copy in sent:
        copy.wait_send()
    for k in range(n_k):
        for d in range(1, n_h):
            z_copy(k, d).wait_send()


def reduce_grads(sizes, grads, small):
    n_k, width, _ = grads.shape
    n_s, n_h, n_t = sizes
    rows, wide, thin = width // (n_s * n_t), 256, small.shape[1]
    vmem = pl.BlockSpec(memory_space=pltpu.VMEM)
    dma = pltpu.SemaphoreType.DMA

    def buffers(*lead):
        return [
            pltpu.VMEM((n_k, *lead, width), BF16),
            pltpu.VMEM((*lead, thin), BF16),
        ]

    return pl.pallas_call(
        partial(reduce_kernel, sizes),
        out_shape=jax.ShapeDtypeStruct((n_k, rows, wide), F32),
        in_specs=[vmem, vmem],
        out_specs=vmem,
        scratch_shapes=[
            *buffers(2, n_t * rows), *buffers(2, n_t, rows),
            *buffers(2, rows // 2), *buffers(rows), *buffers(rows),
            pltpu.VMEM((n_h, n_k, rows, wide), BF16),
            pltpu.VMEM((n_h, n_k, rows, wide), BF16),
            dma((2, 2 * (n_k + 1))), dma((2, 2 * (n_k + 1))), dma((2, 2 * (n_k + 1))),
            dma((2, 2 * (n_k + 1))), dma((2, n_k, n_h)),
        ],
        compiler_params=pltpu.CompilerParams(
            collective_id=4, has_side_effects=True, vmem_limit_bytes=VMEM_BYTES
        ),
        name="reduce_grads",
    )(grads, small)


def expert_kernel(sizes, backward, *refs):
    if backward:
        (blocks, weights, gate, output, slots_out, act_out, back_out, bias_out, sum_out, gathered,
         w_a, w_b, gate_v, sums, slots, act, core_out, core_in, x_out, x_in, land, leave, back, land_back,
         w_sem, o_sem, in_sems, back_sems, core_sems, x_sems, act_sems, b_sems,
         g_send, g_recv, g_sem,
         bias_all, bias_send, bias_land) = refs
    else:
        (blocks, weights, gate, slots_out, act_out, gate_out, back_out,
         w_a, w_b, sums, slots, act, core_out, core_in, x_out, x_in, land, leave, back, land_back,
         w_sem, o_sem, in_sems, back_sems, core_sems, x_sems, act_sems, bias) = refs
    peers = Peers(sizes)
    s, h, t = peers.at
    n_s, n_h, n_t = sizes
    me = peers.flat(peers.at)
    core, chip = lax.rem(s, 2), s // 2
    sibling = (s + 1 - 2 * core, h, t)
    across = (lax.rem(s + 2, n_s), h, t)
    half = act.shape[0] // 2
    own, other = core * half, (1 - core) * half
    n_blocks = peers.count
    first = 1 if backward else 0
    loads = [
        pltpu.make_async_copy(weights.at[first], w_a, w_sem.at[0]),
        pltpu.make_async_copy(weights.at[1 - first], w_b, w_sem.at[1]),
    ]
    for load in loads:
        load.start()
    if backward:
        gate_load = pltpu.make_async_copy(gate, gate_v, o_sem.at[0])
        gate_load.start()
    peers.greet_all()

    def block_out(p, k):
        place = peers.step(k, 1)
        return remote(
            blocks.at[place[1], place[0], p], land.at[p, me],
            in_sems.at[0, p, k], in_sems.at[1, p, k], place,
        )

    def block_in(p, k):
        source = peers.flat(peers.step(k, -1))
        return remote(
            blocks.at[0, 0, p], land.at[p, source], in_sems.at[0, p, k], in_sems.at[1, p, k], sibling
        )

    def each(function, count=n_blocks, start=1):
        lax.fori_loop(start, count, lambda k, carry: (function(k), carry)[1], 0)

    for p in range(2):
        for k in range(1, n_blocks):
            block_out(p, k).start()
        land[p, me] = blocks[h, s, p]
    few = half // 2
    group = 16
    many = 2 * group
    out_row = lax.broadcasted_iota(jnp.int32, (16 * group, 16 * group), 0)
    in_row = lax.broadcasted_iota(jnp.int32, (16 * group, 16 * group), 1)
    there = (out_row // many == in_row % (2 * few)) & (out_row % many == in_row // (2 * few))
    there = there.astype(F32).astype(BF16)
    again = (in_row // many == out_row % (2 * few)) & (in_row % many == out_row // (2 * few))
    again = again.astype(F32).astype(BF16)

    def receive(p):
        each(lambda k: block_in(p, k).wait_recv())
        for b in range(n_blocks // group):
            rows = land[p, b * group : (b + 1) * group].reshape(group * 16, land.shape[3])
            turned = dot(there, rows).astype(BF16).reshape(2 * few, many, land.shape[3])
            for c in range(2):
                first = c * half + p * few
                slots[first : first + few, b * many : (b + 1) * many, :] = turned[
                    c * few : (c + 1) * few
                ]

    if backward:
        own_images = output.shape[0]
        line = [(s, lax.rem(h + d, n_h), t) for d in range(n_h)]
        g_own = pltpu.make_async_copy(output, gathered.at[pl.ds(h * own_images, own_images)], g_sem)
        g_own.start()

        def z_hop(i, origin, up, source=None):
            there = gathered.at[origin * own_images + i]
            return remote(
                there if source is None else source, there,
                g_send.at[i, origin, up], g_recv.at[i, origin], line[1] if up else line[n_h - 1],
            )

        def relay(i, d):
            @pl.when(h >= d)
            def _():
                z_hop(i, h - d, 1).wait_recv()

                @pl.when((h < n_h - 1) & (d < n_h - 1))
                def _():
                    z_hop(i, h - d, 1).start()

            @pl.when(h + d < n_h)
            def _():
                z_hop(i, h + d, 0).wait_recv()

                @pl.when((h > 0) & (d < n_h - 1))
                def _():
                    z_hop(i, h + d, 0).start()

        def gather_output():
            for i in range(own_images):
                @pl.when(h < n_h - 1)
                def _():
                    z_hop(i, h, 1, output.at[i]).start()

                @pl.when(h > 0)
                def _():
                    z_hop(i, h, 0, output.at[i]).start()
    else:
        piece, count = 6 * 64, act.shape[2] // (6 * 64)
        row = lax.broadcasted_iota(jnp.int32, (6 * 128, piece), 0)
        column = lax.broadcasted_iota(jnp.int32, (6 * 128, piece), 1)
        lane = row % 128
        place = (lane < 64) & (column == (row // 128) * 64 + lane)
        place = place.astype(F32).astype(BF16)
        for m in range(count):
            first = (t * count + m) * 96
            lines = [
                gate[pl.ds(pl.multiple_of(first + j * 16, 16), 16), 128:256] for j in range(6)
            ]
            bias[:, m * piece : (m + 1) * piece] = dot(jnp.concatenate(lines, axis=1), place)

    receive(0)
    if backward:
        gather_output()
    loads[0].wait()

    def core_copy(j):
        return remote(
            core_out.at[j], core_in.at[j], core_sems.at[0, j], core_sems.at[1, j], sibling
        )

    def x_copy(j):
        return remote(x_out.at[j], x_in.at[j], x_sems.at[0, j], x_sems.at[1, j], across)

    def act_copy(j):
        return remote(
            act.at[own + j], act.at[own + j], act_sems.at[0, j], act_sems.at[1, j], sibling
        )

    def act_in(j):
        return remote(
            act.at[other + j], act.at[other + j], act_sems.at[0, j], act_sems.at[1, j], sibling
        )

    def meet(j):
        core_copy(j).wait_recv()
        sums[j] = sums[j] + core_in[j].astype(F32)
        x_out[j] = sums[j].astype(BF16)
        x_copy(j).start()

    def first_sums(j):
        core_out[j] = dot(slots[other + j], w_a[other + j]).astype(BF16)
        core_copy(j).start()
        sums[j] = dot(slots[own + j], w_a[own + j])

        @pl.when(j > 0)
        def _():
            meet(j - 1)

    each(first_sums, few, 0)
    receive(1)
    each(first_sums, half, few)
    meet(half - 1)
    loads[1].wait()
    if backward:
        gate_load.wait()

    def second(e):
        leave[e] = dot_t(act[e], w_b[e]).astype(BF16)

    def finish(j):
        x_copy(j).wait_recv()
        value = sums[j] + x_in[j].astype(F32)
        if backward:
            act[own + j] = (value * gate_v[j]).astype(BF16)
        else:
            value = value + bias[pl.ds(own + j, 1), :]
            cumulative = 0.5 + 0.5 * lax.erf(value * 0.7071067811865476)
            act[own + j] = (value * cumulative).astype(BF16)
            sums[j] = cumulative + value * (
                jnp.exp(value * value * -0.5) * 0.3989422804014327
            )
        act_copy(j).start()
        second(own + j)

        @pl.when(j > 0)
        def _():
            act_in(j - 1).wait_recv()
            second(other + j - 1)

        if backward:
            for when, i, d in ((2, 0, 1), (3, 1, 1), (5, 0, 2), (7, 1, 2)):
                @pl.when(j == when)
                def _():
                    relay(i, d)

    def back_copy(p, k):
        place = peers.step(k, 1)
        return remote(
            back.at[p, peers.flat(place)], land_back.at[p, me],
            back_sems.at[0, p, k], back_sems.at[1, p, k], place,
        )

    def back_in(p, k):
        source = peers.flat(peers.step(k, -1))
        return remote(
            back.at[p, 0], land_back.at[p, source],
            back_sems.at[0, p, k], back_sems.at[1, p, k], sibling,
        )

    def give_back(p):
        for b in range(n_blocks // group):
            rows = jnp.concatenate(
                [
                    leave[c * half + p * few : c * half + (p + 1) * few, b * many : (b + 1) * many, :]
                    for c in range(2)
                ],
                axis=0,
            ).reshape(group * 16, leave.shape[2])
            turned = dot(again, rows).astype(BF16)
            back[p, b * group : (b + 1) * group] = turned.reshape(group, 16, leave.shape[2])
        for k in range(1, n_blocks):
            back_copy(p, k).start()
        land_back[p, me] = back[p, me]

    each(finish, few + 1, 0)
    give_back(0)
    each(finish, half, few + 1)
    act_in(half - 1).wait_recv()
    second(other + half - 1)
    give_back(1)
    stores = [pltpu.make_async_copy(act, act_out, o_sem.at[1])]
    if not backward:
        stores.append(pltpu.make_async_copy(sums, gate_out, o_sem.at[0]))
    for store in stores:
        store.start()
    slots_out[...] = slots[...]
    if backward:
        across_t = (s, h, 1 - t)
        width = bias_out.shape[1]

        def bias_row(e):
            bias_all[pl.ds(e, 1), :] = jnp.sum(act[e].astype(F32), axis=0, keepdims=True)

        each(bias_row, 2 * half, 0)

        def slot_row(e):
            sum_out[pl.ds(e, 1), :] = jnp.sum(slots[e].astype(F32), axis=0, keepdims=True)

        each(slot_row, 2 * half, 0)

        def piece(for_t):
            return bias_all[:, pl.ds(pl.multiple_of((core * n_t + for_t) * width, 128), width)]

        bias_send[...] = piece(1 - t)
        bias_copy = remote(bias_send, bias_land, b_sems.at[0], b_sems.at[1], across_t)
        bias_copy.start()
        bias_copy.wait()
        bias_out[...] = jnp.where(t == chip, piece(t), bias_land[...])
    for p in range(2):
        each(lambda k: back_in(p, k).wait_recv())
    back_out[...] = land_back[...]
    for store in stores:
        store.wait()
    if backward:
        relay(0, 3)
        relay(1, 3)
        g_own.wait()
        for origin in range(n_h):
            @pl.when((origin < h) & (h < n_h - 1))
            def _():
                for i in range(own_images):
                    z_hop(i, origin, 1).wait_send()

            @pl.when((origin > h) & (h > 0))
            def _():
                for i in range(own_images):
                    z_hop(i, origin, 0).wait_send()

        @pl.when(h < n_h - 1)
        def _():
            for i in range(own_images):
                z_hop(i, h, 1, output.at[i]).wait_send()

        @pl.when(h > 0)
        def _():
            for i in range(own_images):
                z_hop(i, h, 0, output.at[i]).wait_send()

    for p in range(2):
        each(lambda k: block_out(p, k).wait_send())
        each(lambda k: back_copy(p, k).wait_send())
    for copy in (core_copy, x_copy, act_copy):
        each(lambda j: copy(j).wait_send(), half, 0)


def expert_pass(sizes, backward, blocks, weights, gate, output=None, bias_width=0):
    _, experts, rows, hidden = weights.shape
    devices = sizes[0] * sizes[1] * sizes[2]
    images = 2 * devices
    half = experts // 2
    vmem = pl.BlockSpec(memory_space=pltpu.VMEM)
    hbm = pl.BlockSpec(memory_space=pl.ANY)
    slots = jax.ShapeDtypeStruct((experts, images, rows), BF16)
    act = jax.ShapeDtypeStruct((experts, images, hidden), BF16)
    gate_shape = (half, images, hidden)
    returned = jax.ShapeDtypeStruct((2, devices, experts, rows), BF16)
    if backward:
        operands, in_specs = (blocks, weights, gate, output), [vmem, hbm, hbm, hbm]
        outs = (
            slots, act, returned,
            jax.ShapeDtypeStruct((experts, bias_width), F32),
            jax.ShapeDtypeStruct((experts, rows), F32),
            jax.ShapeDtypeStruct((sizes[1] * output.shape[0], *output.shape[1:]), BF16),
        )
        out_specs = (vmem, hbm, vmem, vmem, vmem, hbm)
    else:
        operands, in_specs = (blocks, weights, gate), [vmem, hbm, vmem]
        outs = (slots, act, jax.ShapeDtypeStruct(gate_shape, F32), returned)
        out_specs = (vmem, hbm, hbm, vmem)
    weight = pltpu.VMEM((experts, rows, hidden), BF16)
    chunk = pltpu.VMEM((half, images, hidden), BF16)
    block = pltpu.VMEM((2, devices, experts, rows), BF16)
    dma = pltpu.SemaphoreType.DMA
    scratch = [weight, weight]
    if backward:
        scratch.append(pltpu.VMEM(gate_shape, F32))
    scratch += [
        pltpu.VMEM(gate_shape, F32),
        pltpu.VMEM(slots.shape, BF16),
        pltpu.VMEM(act.shape, BF16),
        chunk, chunk, chunk, chunk, block,
        pltpu.VMEM(slots.shape, BF16),
        block, block,
        dma((2,)), dma((2,)), dma((2, 2, devices)), dma((2, 2, devices)),
        dma((2, half)), dma((2, half)), dma((2, half)),
    ]
    if backward:
        scratch += [
            dma((2,)), dma((output.shape[0], sizes[1], 2)), dma((output.shape[0], sizes[1])), dma,
            pltpu.VMEM((experts, hidden), F32),
            pltpu.VMEM((experts, bias_width), F32),
            pltpu.VMEM((experts, bias_width), F32),
        ]
    else:
        scratch.append(pltpu.VMEM((experts, hidden), F32))
    return pl.pallas_call(
        partial(expert_kernel, sizes, backward),
        out_shape=outs,
        in_specs=in_specs,
        out_specs=out_specs,
        scratch_shapes=scratch,
        compiler_params=pltpu.CompilerParams(
            collective_id=2 if backward else 1, has_side_effects=True, vmem_limit_bytes=VMEM_BYTES
        ),
        cost_estimate=pl.CostEstimate(
            flops=8 * images * experts * rows * hidden,
            bytes_accessed=weights.size * 2,
            transcendentals=0,
        ),
        name="experts_back" if backward else "experts_ahead",
    )(*operands)


def weight_grad_kernel(slots_0, act_0, slots_1, act_1, out, lines, pick, same):
    group, images, rows = slots_0.shape
    d_block = out.shape[0]
    n = group * d_block
    m, d = pl.program_id(0), pl.program_id(2)

    @pl.when((m == 0) & (pl.program_id(1) == 0) & (d == 0))
    def _():
        row = lax.broadcasted_iota(jnp.int32, pick.shape, 0)
        column = lax.broadcasted_iota(jnp.int32, pick.shape, 1)
        pick[...] = (column == row // group).astype(F32).astype(BF16)
        row = lax.broadcasted_iota(jnp.int32, same.shape, 0)
        column = lax.broadcasted_iota(jnp.int32, same.shape, 1)
        same[...] = (row % group == column // images).astype(F32)

    def prepare(slots):
        @pl.when(d == 0)
        def _():
            turned = slots[...].reshape(group * images, rows).astype(F32)
            lines[...] = jnp.swapaxes(turned, 0, 1).astype(BF16)

    def term(act):
        mine = lines[pl.ds(pl.multiple_of(d * d_block, d_block), d_block)]
        spread = (dot(pick[...], mine) * same[...]).astype(BF16)
        values = act[...].reshape(group * images, act.shape[2])
        out[...] = dot(spread, values).reshape(out.shape)

    @pl.when(m == 0)
    def _():
        prepare(slots_0)
        term(act_0)

    @pl.when(m == 1)
    def _():
        prepare(slots_1)
        term(act_1)


def weight_grads(slots_0, act_0, slots_1, act_1):
    experts, images, rows = slots_0.shape
    hidden = act_0.shape[2]
    group, d_block = 8, 96
    last = experts // group - 1

    def early(m, g, d):
        return jnp.where(m == 0, g, last), 0, 0

    def late(m, g, d):
        return jnp.where(m == 0, 0, g), 0, 0

    slots, act = (group, images, rows), (group, images, hidden)
    return pl.pallas_call(
        weight_grad_kernel,
        grid=(2, experts // group, rows // d_block),
        out_shape=jax.ShapeDtypeStruct((rows, 2, experts, hidden), F32),
        in_specs=[
            pl.BlockSpec(slots, early), pl.BlockSpec(act, early),
            pl.BlockSpec(slots, late), pl.BlockSpec(act, late),
        ],
        out_specs=pl.BlockSpec((d_block, 1, group, hidden), lambda m, g, d: (d, m, g, 0)),
        scratch_shapes=[
            pltpu.VMEM((rows, group * images), BF16),
            pltpu.VMEM((group * d_block, d_block), BF16),
            pltpu.VMEM((group * d_block, group * images), F32),
        ],
        compiler_params=pltpu.CompilerParams(vmem_limit_bytes=VMEM_BYTES),
        cost_estimate=pl.CostEstimate(
            flops=4 * images * experts * rows * hidden,
            bytes_accessed=8 * rows * experts * hidden,
            transcendentals=0,
        ),
        name="weight_grads",
    )(slots_0, act_0, slots_1, act_1)


def dot_r(a, b):
    return lax.dot_general(a, b, (((0,), (0,)), ((), ())), preferred_element_type=F32)


def row_of(shape, axis):
    return lax.broadcasted_iota(jnp.int32, shape, axis)


def one_hot(mask):
    return mask.astype(F32).astype(BF16)


def order_matrix(n_h, few, back):
    n = n_h * 8 * few
    shape = (n, n)
    blocked, natural = row_of(shape, 1 if back else 0), row_of(shape, 0 if back else 1)
    f, half, image = blocked % few, (blocked // few) % 2, (blocked // (2 * few)) % 2
    group = blocked // (4 * few)
    if back:
        part, h = group // n_h, group % n_h
    else:
        h, part = group // 2, group % 2
    expert = ((h * 2 + half) * 2 + part) * few + f
    return one_hot(natural == image * (4 * n_h * few) + expert)


def norm_parts(x, scale, shift, live):
    centered = x - jnp.mean(x, axis=-1, keepdims=True)
    inverse = lax.rsqrt(jnp.mean(centered * centered, axis=-1, keepdims=True) + epsilon)
    unit = centered * inverse
    return unit * scale + shift, unit, inverse


def norm_back(grad, unit, inverse, scale):
    scaled = grad * scale
    average = jnp.mean(scaled, axis=-1, keepdims=True)
    projection = jnp.mean(scaled * unit, axis=-1, keepdims=True)
    return (
        inverse * (scaled - average - unit * projection),
        jnp.sum(grad * unit, axis=0, keepdims=True),
        jnp.sum(grad, axis=0, keepdims=True),
    )


def norm_rows(small):
    return jnp.swapaxes(small[:, 128:].astype(F32), 0, 1)[64:68]


def slots_to_blocks(slots, blocks, columns, joined, order):
    n_h, n_s = blocks.shape[:2]
    turned = dot(order, slots).astype(BF16)
    wide = joined.shape[1] // 2
    for s in range(0, n_s, 2):
        lanes = dot(turned[:, s * columns : (s + 2) * columns], joined).astype(BF16)
        for h in range(n_h):
            for p in range(2):
                rows = (h * 2 + p) * 16
                for e in range(2):
                    blocks[h, s + e, p] = lanes[rows : rows + 16, e * wide : e * wide + columns]


def blocks_to_slots(back, sizes, order, pair, padded):
    n_s, n_h, n_t = sizes
    columns = back.shape[3]
    both = jnp.concatenate([order] * n_t, axis=1)
    results = []
    for s in range(n_s):
        rows = jnp.concatenate(
            [
                back[p, (s * n_h + h) * n_t + t]
                for t in range(n_t)
                for p in range(2)
                for h in range(n_h)
            ],
            axis=0,
        )
        padded[s % 2, :, :columns] = dot(both, rows)
        if s % 2:
            value = jnp.concatenate([padded[0], padded[1]], axis=1)
            high = value.astype(BF16)
            rest = (value - high.astype(F32)).astype(BF16)
            results.append(dot(high, pair) + dot(rest, pair))
    return jnp.concatenate(results, axis=1)


def live_rows(shape, length):
    return row_of(shape, 0) < length


def ahead_kernel(
    length, tokens, small, w_hbm, blocks, normed_1, query, keyed, valued, context, hidden, normed_2,
    dispatch_out, combine_out, w, joined, order, w_sem,
):
    n, rows, width = tokens.shape
    keys = keyed.shape[1]
    loads = [pltpu.make_async_copy(w_hbm.at[k], w.at[k], w_sem.at[k]) for k in range(4)]
    for load in loads:
        load.start()
    norms = norm_rows(small)
    live = live_rows((rows, 1), length)
    for i in range(n):
        value, _, _ = norm_parts(tokens[i].astype(F32), norms[0:1], norms[2:3], live)
        normed_1[i] = jnp.where(live, value, 0.0).astype(BF16)
    joined[...] = pair_matrix(blocks.shape[4], joined.shape[1] // 2, True)
    order[...] = order_matrix(blocks.shape[0], 4, False)
    flat = (n * rows, width)
    for k, target in enumerate((query, keyed, valued)):
        loads[k].wait()
        value = dot(normed_1[...].reshape(flat), w[k]).astype(BF16).reshape(n, rows, width)
        if k == 0:
            target[...] = value
        else:
            target[:, :rows] = value
            target[:, rows:] = jnp.zeros((n, keys - rows, width), BF16)
    factor = HEAD_DIM ** (-0.5)
    pairs = width // 128
    lane = row_of((rows, 128), 1)
    shown = row_of((rows, keys), 1) < length

    def attend(step, carry):
        i = step // pairs
        lanes = pl.ds(pl.multiple_of((step % pairs) * 128, 128), 128)
        q, k, v = query[i, :, lanes], keyed[i, :, lanes], valued[i, :, lanes]
        parts = []
        for a in range(2):
            mine = (lane < 64) if a == 0 else (lane >= 64)
            scores = dot_t(jnp.where(mine, q, jnp.zeros_like(q)), k) * factor
            scores = jnp.where(shown, scores, -1e30)
            exponent = jnp.exp(scores - jnp.max(scores, axis=-1, keepdims=True))
            probs = exponent / jnp.sum(exponent, axis=-1, keepdims=True)
            parts.append(dot(probs.astype(BF16), v))
        context[i, :, lanes] = jnp.where(lane < 64, parts[0], parts[1]).astype(BF16)
        return carry

    lax.fori_loop(0, n * pairs, attend, 0, unroll=2)
    loads[3].wait()
    attended = dot_t(context[...].reshape(flat), w[3]).reshape(n, rows, width)
    for i in range(n):
        value = tokens[i].astype(F32) + attended[i]
        hidden[i] = value
        value, _, _ = norm_parts(value, norms[1:2], norms[3:4], live)
        normed_2[i] = jnp.where(live, value, 0.0).astype(BF16)
    logits = dot(normed_2[...].reshape(flat), small[:, :128]).reshape(n, rows, 128)
    experts = row_of((rows, 128), 1) < 64
    slots = []
    for i in range(n):
        here = logits[i]
        down = jnp.where(live, here, -1e30)
        exponent = jnp.exp(down - jnp.max(down, axis=0, keepdims=True))
        dispatch = exponent / jnp.sum(exponent, axis=0, keepdims=True)
        dispatch = jnp.where(experts, dispatch, 0.0)
        across = jnp.where(experts, here, -1e30)
        exponent = jnp.exp(across - jnp.max(across, axis=1, keepdims=True))
        combine = exponent / jnp.sum(exponent, axis=1, keepdims=True)
        dispatch_out[i] = dispatch
        combine_out[i] = combine
        slots.append(dot_r(dispatch.astype(BF16), normed_2[i])[:64].astype(BF16))
    slots_to_blocks(
        jnp.concatenate(slots, axis=0), blocks, blocks.shape[4], joined[...], order[...]
    )


def tokens_ahead(sizes, length, tokens, small, weights):
    n, rows, width = tokens.shape
    keys = 256
    vmem = pl.BlockSpec(memory_space=pltpu.VMEM)
    shape = jax.ShapeDtypeStruct
    wide = (n, keys, width)
    thin = shape((n, rows, 128), F32)
    return pl.pallas_call(
        partial(ahead_kernel, length),
        out_shape=(
            shape((sizes[1], sizes[0], 2, 16, width // sizes[0]), BF16),
            shape(tokens.shape, BF16), shape(tokens.shape, BF16), shape(wide, BF16),
            shape(wide, BF16), shape(tokens.shape, BF16), shape(tokens.shape, F32),
            shape(tokens.shape, BF16), thin, thin,
        ),
        in_specs=[vmem, vmem, pl.BlockSpec(memory_space=pl.ANY)],
        out_specs=(vmem,) * 10,
        scratch_shapes=[
            pltpu.VMEM(weights.shape, BF16),
            pltpu.VMEM((2 * width // sizes[0], 512), BF16),
            pltpu.VMEM((128, 128), BF16),
            pltpu.SemaphoreType.DMA((4,)),
        ],
        compiler_params=pltpu.CompilerParams(vmem_limit_bytes=VMEM_BYTES),
        name="tokens_ahead",
    )(tokens, small, weights)


def middle_kernel(
    sizes, back, small, combine, hidden, cotangent, output, blocks, grad_logits, padded
):
    n, rows, _ = hidden.shape
    columns = back.shape[3]
    padded[...] = jnp.zeros_like(padded)
    pair = pair_matrix(columns, padded.shape[2], False)
    joined = pair_matrix(columns, padded.shape[2], True)
    total = blocks_to_slots(back, sizes, order_matrix(sizes[1], 4, True), pair, padded)
    bias = jnp.swapaxes(small[:, :128].astype(F32), 0, 1)[64:]
    slots = []
    for i in range(n):
        slot_out = (total[i * 64 : (i + 1) * 64] + bias).astype(BF16)
        combine_b = combine[i].astype(BF16)[:, :64]
        output[i] = (hidden[i] + dot(combine_b, slot_out)).astype(BF16)
        grad_combine = dot_t(cotangent[i], slot_out)
        weight = combine[i][:, :64]
        weighted = jnp.sum(weight * grad_combine, axis=1, keepdims=True)
        grad_logits[i] = weight * (grad_combine - weighted)
        slots.append(dot_r(combine_b, cotangent[i]).astype(BF16))
    slots_to_blocks(
        jnp.concatenate(slots, axis=0), blocks, columns, joined, order_matrix(sizes[1], 4, False)
    )


def tokens_middle(sizes, back, small, combine, hidden, cotangent):
    n, rows, width = hidden.shape
    vmem = pl.BlockSpec(memory_space=pltpu.VMEM)
    shape = jax.ShapeDtypeStruct
    return pl.pallas_call(
        partial(middle_kernel, sizes),
        out_shape=(
            shape(hidden.shape, BF16),
            shape((sizes[1], sizes[0], 2, 16, width // sizes[0]), BF16),
            shape((n, rows, 64), F32),
        ),
        in_specs=[vmem] * 5,
        out_specs=(vmem,) * 3,
        scratch_shapes=[pltpu.VMEM((2, 128, 256), F32)],
        compiler_params=pltpu.CompilerParams(vmem_limit_bytes=VMEM_BYTES),
        name="tokens_middle",
    )(back, small, combine, hidden, cotangent)


def behind_kernel(
    sizes, length, back, small, w_hbm, tokens, normed_1, query, keyed, valued, context, hidden,
    normed_2, dispatch, grad_logits, cotangent, grads, small_grads, input_grad,
    w, padded, grad_hidden, rounded, grad_context, grad_q, grad_k, grad_v, w_sem,
):
    n, rows, width = tokens.shape
    keys = keyed.shape[1]
    loads = [pltpu.make_async_copy(w_hbm.at[k], w.at[k], w_sem.at[k]) for k in range(4)]
    for load in loads:
        load.start()
    norms = norm_rows(small)
    padded[...] = jnp.zeros_like(padded)
    pair = pair_matrix(back.shape[3], padded.shape[2], False)
    grad_slots = blocks_to_slots(
        back, sizes, order_matrix(sizes[1], 4, True), pair, padded
    ).astype(BF16)
    phi = small[:, :64]
    phi_grad = jnp.zeros((width, 64), F32)
    sums = []
    flat = (n * rows, width)
    for i in range(n):
        slots = grad_slots[i * 64 : (i + 1) * 64]
        weight = dispatch[i][:, :64]
        grad_dispatch = dot_t(normed_2[i], slots)
        weighted = jnp.sum(weight * grad_dispatch, axis=0, keepdims=True)
        logits = (weight * (grad_dispatch - weighted) + grad_logits[i]).astype(BF16)
        phi_grad = phi_grad + dot_r(normed_2[i], logits)
        grad = dot(weight.astype(BF16), slots) + dot_t(logits, phi)
        _, unit, inverse = norm_parts(hidden[i], norms[1:2], norms[3:4], None)
        grad_in, scale_grad, bias_grad = norm_back(grad, unit, inverse, norms[1:2])
        value = cotangent[i].astype(F32) + grad_in
        grad_hidden[i] = value
        rounded[i] = value.astype(BF16)
        sums.append((scale_grad, bias_grad))
    scale_2, bias_2 = sums[0][0] + sums[1][0], sums[0][1] + sums[1][1]
    flat_rounded = rounded[...].reshape(flat)
    loads[3].wait()
    grad_context[...] = dot(flat_rounded, w[3]).astype(BF16).reshape(n, rows, width)
    grads[3] = dot_r(flat_rounded, context[...].reshape(flat)).astype(BF16)
    factor = HEAD_DIM ** (-0.5)
    pairs = width // 128
    lane = row_of((rows, 128), 1)
    key_lane = row_of((keys, 128), 1)
    shown = row_of((rows, keys), 1) < length

    def attend(step, carry):
        i = step // pairs
        lanes = pl.ds(pl.multiple_of((step % pairs) * 128, 128), 128)
        q, k, v = query[i, :, lanes], keyed[i, :, lanes], valued[i, :, lanes]
        g = grad_context[i, :, lanes]
        to_q, to_k, to_v = [], [], []
        for a in range(2):
            mine = (lane < 64) if a == 0 else (lane >= 64)
            scores = dot_t(jnp.where(mine, q, jnp.zeros_like(q)), k) * factor
            grad_probs = dot_t(jnp.where(mine, g, jnp.zeros_like(g)), v)
            scores = jnp.where(shown, scores, -1e30)
            exponent = jnp.exp(scores - jnp.max(scores, axis=-1, keepdims=True))
            probs = exponent / jnp.sum(exponent, axis=-1, keepdims=True)
            weighted = jnp.sum(probs * grad_probs, axis=-1, keepdims=True)
            grad_scores = (probs * (grad_probs - weighted)).astype(BF16)
            to_v.append(dot_r(probs.astype(BF16), g))
            to_q.append(dot(grad_scores, k))
            to_k.append(dot_r(grad_scores, q))
        grad_q[i, :, lanes] = (jnp.where(lane < 64, to_q[0], to_q[1]) * factor).astype(BF16)
        kept = key_lane < 64
        grad_k[i, :, lanes] = (jnp.where(kept, to_k[0], to_k[1]) * factor)[:rows].astype(BF16)
        grad_v[i, :, lanes] = jnp.where(kept, to_v[0], to_v[1])[:rows].astype(BF16)
        return carry

    lax.fori_loop(0, n * pairs, attend, 0, unroll=2)
    total = jnp.zeros(flat, F32)
    turned = jnp.swapaxes(normed_1[...].reshape(flat).astype(F32), 0, 1).astype(BF16)
    for k, source in enumerate((grad_q, grad_k, grad_v)):
        loads[k].wait()
        value = source[...].reshape(flat)
        total = total + dot_t(value, w[k])
        grads[k] = dot(turned, value).astype(BF16)
    total = total.reshape(n, rows, width)
    sums = []
    for i in range(n):
        _, unit, inverse = norm_parts(tokens[i].astype(F32), norms[0:1], norms[2:3], None)
        grad_in, scale_grad, bias_grad = norm_back(total[i], unit, inverse, norms[0:1])
        input_grad[i] = (grad_hidden[i] + grad_in).astype(BF16)
        sums.append((scale_grad, bias_grad))
    scale_1, bias_1 = sums[0][0] + sums[1][0], sums[0][1] + sums[1][1]
    line = row_of((128, width), 0)
    spread = jnp.zeros((128, width), F32)
    for j, value in enumerate((scale_1, scale_2, bias_1, bias_2)):
        spread = jnp.where(line == 64 + j, value, spread)
    small_grads[...] = jnp.swapaxes(spread, 0, 1).astype(BF16)
    small_grads[:, :64] = phi_grad.astype(BF16)


def tokens_behind(sizes, length, back, small, weights, tokens, kept, grad_logits, cotangent):
    n, rows, width = tokens.shape
    vmem = pl.BlockSpec(memory_space=pltpu.VMEM)
    shape = jax.ShapeDtypeStruct
    low = pltpu.VMEM(tokens.shape, BF16)
    return pl.pallas_call(
        partial(behind_kernel, sizes, length),
        out_shape=(
            shape((4, width, width), BF16), shape((width, 128), BF16), shape(tokens.shape, BF16)
        ),
        in_specs=[vmem, vmem, pl.BlockSpec(memory_space=pl.ANY)] + [vmem] * 11,
        out_specs=(vmem,) * 3,
        scratch_shapes=[
            pltpu.VMEM(weights.shape, BF16),
            pltpu.VMEM((2, 128, 256), F32),
            pltpu.VMEM(tokens.shape, F32),
            low, low, low, low, low,
            pltpu.SemaphoreType.DMA((4,)),
        ],
        compiler_params=pltpu.CompilerParams(vmem_limit_bytes=VMEM_BYTES),
        name="tokens_behind",
    )(back, small, weights, tokens, *kept, grad_logits, cotangent)


def unpack_kernel(block, summed, attn, phi, scales, biases):
    attn[...] = summed[:, :, :block]
    rest = summed[0][:, 128:]
    phi[...] = pltpu.roll(rest, 64, 1)[:, : phi.shape[1]]
    turned = jnp.swapaxes(rest, 0, 1)
    scales[...] = turned[80:82]
    biases[...] = turned[82:84]


def unpack_grads(summed, block, slot):
    n_k, rows, _ = summed.shape
    vmem = pl.BlockSpec(memory_space=pltpu.VMEM)
    shape = jax.ShapeDtypeStruct
    return pl.pallas_call(
        partial(unpack_kernel, block),
        out_shape=(
            shape((n_k, rows, block), F32), shape((rows, slot), F32),
            shape((2, rows), F32), shape((2, rows), F32),
        ),
        in_specs=[vmem],
        out_specs=(vmem,) * 4,
        name="unpack_grads",
    )(summed)


def normalize(values, scale, shift):
    centered = values - jnp.mean(values, axis=-1, keepdims=True)
    variance = jnp.mean(centered * centered, axis=-1, keepdims=True)
    inverse = lax.rsqrt(variance + epsilon)
    unit_part = centered * inverse
    return (unit_part * scale + shift, unit_part, inverse)


def normalize_back(grad_output, unit_part, inverse, scale):
    scaled = grad_output * scale
    average = jnp.mean(scaled, axis=-1, keepdims=True)
    projection = jnp.mean(scaled * unit_part, axis=-1, keepdims=True)
    grad_input = inverse * (scaled - average - unit_part * projection)
    return (
        grad_input,
        jnp.sum(grad_output * unit_part, axis=(0, 1)),
        jnp.sum(grad_output, axis=(0, 1)),
    )


def to_experts(slots):
    slots = lax.all_to_all(slots, "heads", split_axis=1, concat_axis=0, tiled=True)
    slots = lax.all_to_all(slots, "shard", split_axis=2, concat_axis=0, tiled=True)
    return lax.all_gather(slots, "tensor", axis=0, tiled=True)


def to_images(slots):
    slots = lax.psum_scatter(slots, "tensor", scatter_dimension=0, tiled=True)
    slots = lax.all_to_all(slots, "shard", split_axis=0, concat_axis=2, tiled=True)
    return lax.all_to_all(slots, "heads", split_axis=0, concat_axis=1, tiled=True)


def general_shards(tokens, norm_scales, norm_biases, w_attn, phi, experts, in_bias, out_bias, cotangent):
    heads_n = lax.axis_size("heads")
    group, seq_len, width = tokens.shape
    own = group // heads_n
    heads_index = lax.axis_index("heads")
    tensor_index = lax.axis_index("tensor")
    shard_index = lax.axis_index("shard")
    hidden = experts.shape[3]
    rows = experts.shape[0]
    scales, biases, in_full = (
        lax.all_gather(norm_scales, ROWS, axis=1, tiled=True).astype(F32),
        lax.all_gather(norm_biases, ROWS, axis=1, tiled=True).astype(F32),
        lax.all_gather(in_bias, ROWS, axis=1, tiled=True).astype(F32),
    )
    attn = lax.all_gather(
        lax.all_gather(w_attn, "heads", axis=2, tiled=True), ROWS, axis=1, tiled=True
    )
    phi_full = lax.all_gather(
        lax.all_gather(phi, "heads", axis=1, tiled=True), ROWS, axis=0, tiled=True
    )
    out_rows = lax.all_gather(out_bias, "tensor", axis=1, tiled=True).astype(F32)
    e_own = experts.shape[2] // lax.axis_size("shard")
    in_local = lax.dynamic_slice_in_dim(in_full, tensor_index * hidden, hidden, 1)
    factor = HEAD_DIM ** (-0.5)
    tokens = lax.dynamic_slice_in_dim(tokens, heads_index * own, own, 0)
    cotangent = lax.dynamic_slice_in_dim(cotangent, heads_index * own, own, 0)
    n_heads = width // HEAD_DIM
    inputs = tokens.astype(F32)
    normed_one, unit_one, inverse_one = normalize(inputs, scales[0], biases[0])
    normed_one_b = normed_one.astype(BF16)
    projected = einsum("nsd,kdc->knsc", normed_one_b, attn[:3]).astype(BF16)
    query, keyed, valued = projected.reshape(3, own, seq_len, n_heads, HEAD_DIM)
    scores = einsum("nqhe,nkhe->nhqk", query, keyed) * factor
    score_peak = jnp.max(scores, axis=-1, keepdims=True)
    exponent = jnp.exp(scores - score_peak)
    probs = exponent / jnp.sum(exponent, axis=-1, keepdims=True)
    probs_b = probs.astype(BF16)
    context_b = (
        einsum("nhqk,nkhe->nqhe", probs_b, valued).astype(BF16).reshape(own, seq_len, width)
    )
    hidden_one = inputs + einsum("nsc,dc->nsd", context_b, attn[3])
    normed_two, unit_two, inverse_two = normalize(hidden_one, scales[1], biases[1])
    normed_two_b = normed_two.astype(BF16)
    logits = einsum("nsd,de->nse", normed_two_b, phi_full)
    dispatch = jax.nn.softmax(logits, axis=1)
    dispatch_b = dispatch.astype(BF16)
    combine = jax.nn.softmax(logits, axis=2)
    combine_b = combine.astype(BF16)
    slot_in = to_experts(einsum("nse,nsd->ned", dispatch_b, normed_two_b).astype(BF16))
    share = 1 if e_own else 0

    def meet(partial_sum):
        return lax.psum_scatter(partial_sum, "shard", scatter_dimension=share, tiled=True)

    def spread(values):
        return lax.all_gather(values, "shard", axis=share, tiled=True)

    pre = meet(einsum("ned,def->nef", slot_in, experts[:, 0]))
    if e_own:
        pre = pre + lax.dynamic_slice_in_dim(in_local, shard_index * e_own, e_own, 0)
    else:
        pre = pre + in_local
    gelu_value, gelu_back = jax.vjp(partial(jax.nn.gelu, approximate=False), pre)
    activated = spread(gelu_value.astype(BF16))
    slot_out_part = einsum("nef,def->ned", activated, experts[:, 1])
    slot_out_part = slot_out_part + jnp.where(tensor_index == 0, out_rows, 0.0)
    slot_out = to_images(slot_out_part).astype(BF16)
    output = (hidden_one + einsum("nse,ned->nsd", combine_b, slot_out)).astype(BF16)
    output = lax.all_gather(output, "heads", axis=0, tiled=True)
    grad_combine = einsum("nsd,ned->nse", cotangent, slot_out)
    grad_slot = to_experts(einsum("nse,nsd->ned", combine_b, cotangent).astype(BF16))
    grad_act = meet(einsum("ned,def->nef", grad_slot, experts[:, 1]))
    grad_pre = spread(gelu_back(grad_act)[0].astype(BF16))
    grad_slot_in = einsum("nef,def->ned", grad_pre, experts[:, 0]).astype(BF16)
    input_term = einsum("ned,nef->def", slot_in, grad_pre)
    output_term = einsum("ned,nef->def", grad_slot, activated)
    experts_grad = jnp.stack((input_term, output_term), axis=1)
    grad_slot_in = to_images(grad_slot_in.astype(F32)).astype(BF16)
    in_bias_grad = lax.dynamic_slice_in_dim(
        lax.all_gather(jnp.sum(grad_pre.astype(F32), axis=0), "tensor", axis=1, tiled=True),
        (shard_index * lax.axis_size("tensor") + tensor_index) * in_bias.shape[1],
        in_bias.shape[1],
        1,
    )
    out_bias_grad = lax.dynamic_slice_in_dim(
        jnp.sum(grad_slot.astype(F32), axis=0),
        tensor_index * out_bias.shape[1],
        out_bias.shape[1],
        1,
    )
    grad_dispatch = einsum("nsd,ned->nse", normed_two_b, grad_slot_in)
    grad_logits = (
        dispatch * (grad_dispatch - jnp.sum(dispatch * grad_dispatch, axis=1, keepdims=True))
        + combine * (grad_combine - jnp.sum(combine * grad_combine, axis=2, keepdims=True))
    ).astype(BF16)
    phi_grad = einsum("nsd,nse->de", normed_two_b, grad_logits)
    grad_normed_two = einsum("nse,ned->nsd", dispatch_b, grad_slot_in) + einsum(
        "nse,de->nsd", grad_logits, phi_full
    )
    grad_hidden_norm, scale_two_grad, bias_two_grad = normalize_back(
        grad_normed_two, unit_two, inverse_two, scales[1]
    )
    grad_hidden = cotangent.astype(F32) + grad_hidden_norm
    grad_hidden_b = grad_hidden.astype(BF16)
    out_weight_grad = einsum("nsd,nsc->dc", grad_hidden_b, context_b)
    grad_context = einsum("nsd,dc->nsc", grad_hidden_b, attn[3]).astype(BF16)
    grad_context = grad_context.reshape(own, seq_len, n_heads, HEAD_DIM)
    grad_value = einsum("nhqk,nqhe->nkhe", probs_b, grad_context).astype(BF16)
    grad_probs = einsum("nqhe,nkhe->nhqk", grad_context, valued)
    grad_scores = (
        probs * (grad_probs - jnp.sum(probs * grad_probs, axis=-1, keepdims=True))
    ).astype(BF16)
    grad_query = (einsum("nhqk,nkhe->nqhe", grad_scores, keyed) * factor).astype(BF16)
    grad_key = (einsum("nhqk,nqhe->nkhe", grad_scores, query) * factor).astype(BF16)
    grad_proj = jnp.stack((grad_query, grad_key, grad_value)).reshape(3, own, seq_len, width)
    proj_grad = einsum("nsd,knsc->kdc", normed_one_b, grad_proj)
    grad_normed_one = einsum("knsc,kdc->nsd", grad_proj, attn[:3])
    grad_input_norm, scale_one_grad, bias_one_grad = normalize_back(
        grad_normed_one, unit_one, inverse_one, scales[0]
    )
    input_grad = (grad_hidden + grad_input_norm).astype(BF16)
    input_grad = lax.all_gather(input_grad, "heads", axis=0, tiled=True)
    attn_grad = jnp.concatenate((proj_grad, out_weight_grad[None]), axis=0)
    attn_grad = lax.psum_scatter(attn_grad, ROWS, scatter_dimension=1, tiled=True)
    attn_grad = lax.psum_scatter(attn_grad, "heads", scatter_dimension=2, tiled=True)
    phi_grad = lax.psum_scatter(phi_grad, ROWS, scatter_dimension=0, tiled=True)
    phi_grad = lax.psum_scatter(phi_grad, "heads", scatter_dimension=1, tiled=True)
    norms = jnp.stack((scale_one_grad, scale_two_grad, bias_one_grad, bias_two_grad))
    norms = lax.psum(lax.psum_scatter(norms, ROWS, scatter_dimension=1, tiled=True), "heads")
    return (
        output,
        input_grad,
        norms[:2],
        norms[2:],
        attn_grad,
        phi_grad,
        experts_grad,
        in_bias_grad,
        out_bias_grad,
    )


def shards(tokens, norm_scales, norm_biases, w_attn, phi, experts, in_bias, out_bias, cotangent):
    arrays = (tokens, norm_scales, norm_biases, w_attn, phi, experts, in_bias, out_bias, cotangent)
    sizes = tuple(lax.axis_size(name) for name in ("shard", "heads", "tensor"))
    group, length, width = tokens.shape
    fits = (sizes, group, width, *experts.shape[:3]) == ((4, 4, 2), 8, 768, 192, 2, 16)
    if not fits or not 192 < length <= 208 or in_bias.shape[1] != 384:
        return general_shards(*arrays)
    n_s, n_h, n_t = sizes
    block, slot = w_attn.shape[2], phi.shape[1]
    beside = jnp.concatenate((phi, out_bias.T), axis=1)
    beside = jnp.pad(beside, ((0, 0), (0, 256 - block - 2 * slot)))
    beside = jnp.concatenate((beside[None], jnp.zeros((3, *beside.shape), BF16)), axis=0)
    packet = jnp.concatenate((w_attn, beside), axis=2)
    hidden_bias = in_bias.reshape(16, 6, 64).transpose(1, 0, 2).reshape(96, 64)
    extra = jnp.concatenate((hidden_bias, norm_scales.T, norm_biases.T), axis=1)
    extra = jnp.pad(extra, ((0, 0), (128, 60)))
    tokens, cotangent = (
        values.transpose(1, 0, 2).reshape(group * length, width) for values in (tokens, cotangent)
    )
    attn, small, turned, tokens, cotangent = gather_weights(
        sizes, packet, extra, experts, tokens, cotangent
    )
    blocks, *kept, combine = tokens_ahead(sizes, length, tokens, small, attn)
    hidden = kept[5]
    slot_in, activated, gate, back = expert_pass(sizes, False, blocks, turned, small)
    output, blocks, grad_logits = tokens_middle(sizes, back, small, combine, hidden, cotangent)
    grad_slot, grad_pre, back, in_bias_grad, out_sum, output = expert_pass(
        sizes, True, blocks, turned, gate, output, in_bias.shape[1]
    )
    attn_grad, small_grad, input_grad = tokens_behind(
        sizes, length, back, small, attn, tokens, kept, grad_logits, cotangent
    )
    input_grad = lax.all_gather(input_grad, "heads", axis=0, tiled=True)
    attn_grad, grad_pre = lax.optimization_barrier((attn_grad, grad_pre))
    experts_grad = weight_grads(slot_in, grad_pre, grad_slot, activated)
    attn_grad, experts_grad = lax.optimization_barrier((attn_grad, experts_grad))
    summed = reduce_grads(sizes, attn_grad, small_grad)
    attn_grad, phi_grad, scales_grad, biases_grad = unpack_grads(summed, block, slot)
    out_bias_grad = lax.dynamic_slice_in_dim(
        out_sum, lax.axis_index("tensor") * out_bias.shape[1], out_bias.shape[1], 1
    )
    return (
        output[:, :length],
        input_grad[:, :length],
        scales_grad,
        biases_grad,
        attn_grad,
        phi_grad,
        experts_grad,
        in_bias_grad,
        out_bias_grad,
    )


def solution(mesh):
    images = P(ROWS, None, None)
    return jax.shard_map(
        shards,
        mesh=mesh,
        in_specs=(
            images,
            P(None, ROWS),
            P(None, ROWS),
            P(None, ROWS, "heads"),
            P(ROWS, "heads"),
            P("shard", None, "heads", "tensor"),
            P("heads", ROWS),
            P("heads", ROWS),
            images,
        ),
        out_specs=(
            images,
            images,
            P(None, ROWS),
            P(None, ROWS),
            P(None, ROWS, "heads"),
            P(ROWS, "heads"),
            P("shard", None, "heads", "tensor"),
            P("heads", ROWS),
            P("heads", ROWS),
        ),
        check_vma=False,
    )
```

```python
from functools import partial

import jax
import jax.numpy as jnp
from jax import lax
from jax.experimental import pallas as pl
from jax.experimental.pallas import tpu as pltpu
from jax.sharding import PartitionSpec as P

HEAD_DIM = 64
F32 = jnp.float32
BF16 = jnp.bfloat16
ROWS = ("shard", "tensor")
MESH = pl.DeviceIdType.MESH
VMEM_BYTES = 58 * 1024 * 1024
epsilon = 1e-06
einsum = partial(jnp.einsum, preferred_element_type=F32)


def dot(a, b):
    return lax.dot_general(a, b, (((1,), (0,)), ((), ())), preferred_element_type=F32)


def dot_t(a, b):
    return lax.dot_general(a, b, (((1,), (1,)), ((), ())), preferred_element_type=F32)


def swap_matrix(n):
    out = lax.broadcasted_iota(jnp.int32, (n * n, n * n), 0)
    row = lax.broadcasted_iota(jnp.int32, (n * n, n * n), 1)
    return ((out // n == row % n) & (out % n == row // n)).astype(F32).astype(BF16)


class Peers:
    def __init__(self, sizes):
        self.sizes = sizes
        self.at = tuple(lax.axis_index(name) for name in ("shard", "heads", "tensor"))
        self.count = sizes[0] * sizes[1] * sizes[2]

    def flat(self, place):
        return (place[0] * self.sizes[1] + place[1]) * self.sizes[2] + place[2]

    def step(self, k, sign):
        _, n_h, n_t = self.sizes
        steps = (k // (n_h * n_t), (k // n_t) % n_h, k % n_t)
        return tuple(
            lax.rem(at + n + sign * d, n) for at, n, d in zip(self.at, self.sizes, steps)
        )

    def greet_all(self):
        barrier = pltpu.get_barrier_semaphore()

        def signal(k, carry):
            pl.semaphore_signal(barrier, inc=1, device_id=self.step(k, 1), device_id_type=MESH)
            return carry

        lax.fori_loop(1, self.count, signal, 0)
        pl.semaphore_wait(barrier, self.count - 1)


def remote(src, dst, send, recv, place):
    return pltpu.make_async_remote_copy(
        src_ref=src, dst_ref=dst, send_sem=send, recv_sem=recv, device_id=place, device_id_type=MESH
    )


def plane(sizes):
    n_s, n_h, n_t = sizes
    s, h, t = (lax.axis_index(name) for name in ("shard", "heads", "tensor"))
    core, chip = lax.rem(s, 2), s // 2
    sibling = (s + 1 - 2 * core, h, t)
    across_x = (lax.rem(s + 2, n_s), h, t)
    across_y = (s, h, 1 - t)
    line = [(s, lax.rem(h + d, n_h), t) for d in range(n_h)]
    barrier = pltpu.get_barrier_semaphore()
    others = [sibling, across_x, across_y] + line[1:]
    for place in others:
        pl.semaphore_signal(barrier, inc=1, device_id=place, device_id_type=MESH)
    pl.semaphore_wait(barrier, len(others))
    return (s, h, t), core, chip, sibling, across_x, across_y, line


def pair_matrix(block, wide, transposed):
    shape = (2 * block, 2 * wide) if transposed else (2 * wide, 2 * block)
    tight = lax.broadcasted_iota(jnp.int32, shape, 0 if transposed else 1)
    padded = lax.broadcasted_iota(jnp.int32, shape, 1 if transposed else 0)
    second = padded >= wide
    lane = jnp.where(second, padded - wide, padded)
    same = (lane < block) & (tight == jnp.where(second, lane + block, lane))
    return same.astype(F32).astype(BF16)


def gather_kernel(
    sizes, w_attn, phi_t, out_bias, scales, biases, in_bias, experts, tokens, cotangent, w_out, small_out, turned, own_tokens, own_cot,
    w, small, lined, extra, stage, tile_in, tile_out, images, picked,
    z_send, z_recv, x_sems, y_sems, d_sems, c_sems, t_sems, o_sems, i_sems,
):
    n_k, rows, block = w_attn.shape
    wide = lined.shape[3]
    slot = phi_t.shape[0]
    own_h = lax.axis_index("heads")
    stage[...] = jnp.zeros_like(stage)
    stage[64 : 64 + slot] = phi_t[...].astype(F32)
    stage[64 + slot : 64 + 2 * slot] = out_bias[...].astype(F32)
    lined[own_h, :, :, 128:] = jnp.zeros((n_k, rows, wide - 128), BF16)
    lined[own_h, :, :, :block] = w_attn[...]
    first = lined[own_h, 0, :, 128:].astype(F32) + jnp.swapaxes(stage[...], 0, 1)
    lined[own_h, 0, :, 128:] = first.astype(BF16)
    (s, h, t), core, chip, sibling, across_x, across_y, line = plane(sizes)
    n_h, n_t = sizes[1], sizes[2]
    width = w.shape[2]
    side = 16
    n_tiles = experts.shape[0] // side
    depth = tile_in.shape[0]
    halves = ((0, rows // 2), (rows // 2, rows // 2))

    def z_hop(k, origin, up):
        place = line[1] if up else line[n_h - 1]
        return remote(
            lined.at[origin, k], lined.at[origin, k],
            z_send.at[k, origin, up], z_recv.at[k, origin], place,
        )

    def relay(k, d):
        @pl.when(h >= d)
        def _():
            z_hop(k, h - d, 1).wait_recv()

            @pl.when(h < n_h - 1)
            def _():
                z_hop(k, h - d, 1).start()

        @pl.when(h + d < n_h)
        def _():
            z_hop(k, h + d, 0).wait_recv()

            @pl.when(h > 0)
            def _():
                z_hop(k, h + d, 0).start()

    chunks = (0, 2, 1, 3)
    for k in chunks:
        @pl.when(h < n_h - 1)
        def _():
            z_hop(k, h, 1).start()

        @pl.when(h > 0)
        def _():
            z_hop(k, h, 0).start()

    def load(i):
        return pltpu.make_async_copy(
            experts.at[pl.ds((i % n_tiles) * side, side), i // n_tiles],
            tile_in.at[i % depth],
            t_sems.at[0, i % depth],
        )

    def store(i):
        return pltpu.make_async_copy(
            tile_out.at[i % depth],
            turned.at[i // n_tiles, :, pl.ds((i % n_tiles) * side, side)],
            t_sems.at[1, i % depth],
        )

    image_loads = [
        pltpu.make_async_copy(source, images.at[j], i_sems.at[0, j])
        for j, source in enumerate((tokens, cotangent))
    ]
    for i in range(depth - 1):
        load(i).start()
    for copy in image_loads:
        copy.start()
    swap = swap_matrix(side)
    done = [0]

    def turn(count):
        def step(i, carry):
            load(i).wait()

            @pl.when(i + depth - 1 < 2 * n_tiles)
            def _():
                load(i + depth - 1).start()

            @pl.when(i >= depth)
            def _():
                store(i - depth).wait()

            rows_in = tile_in[i % depth].reshape(side * side, tile_in.shape[3])
            tile_out[i % depth] = dot(swap, rows_in).astype(BF16).reshape(tile_out.shape[1:])
            store(i).start()
            return carry

        last = min(done[0] + count, 2 * n_tiles)
        lax.fori_loop(done[0], last, step, 0)
        done[0] = last

    pair = pair_matrix(block, wide, False)
    shape = (n_h * wide, small.shape[1])
    row = lax.broadcasted_iota(jnp.int32, shape, 0)
    column = lax.broadcasted_iota(jnp.int32, shape, 1)
    lane, of = row % wide - block, row // wide
    beside = (lane >= 0) & (lane < 16) & (column == of * 16 + lane)
    beside |= (lane >= 16) & (lane < 32) & (column == n_h * 16 + of * 16 + lane - 16)
    beside = beside.astype(F32).astype(BF16)

    stage[...] = jnp.zeros_like(stage)
    stage[64:66] = scales[...].astype(F32)
    stage[66:68] = biases[...].astype(F32)
    norms = jnp.swapaxes(stage[...], 0, 1)
    pieces = []
    for j in range(in_bias.shape[1] // 64):
        shape = (in_bias.shape[1], 128)
        row = lax.broadcasted_iota(jnp.int32, shape, 0)
        column = lax.broadcasted_iota(jnp.int32, shape, 1)
        chosen = ((row == 64 * j + column) & (column < 64)).astype(F32).astype(BF16)
        pieces.append(dot(in_bias[...], chosen))
    extra[:, :128] = jnp.zeros((rows, 128), F32)
    extra[:, 128:] = jnp.concatenate(pieces, axis=0) + norms

    image_stores = [
        pltpu.make_async_copy(picked.at[j], target, i_sems.at[1, j])
        for j, target in enumerate((own_tokens, own_cot))
    ]

    def pick_images(j):
        own, padded = picked.shape[1:3]
        group = own * n_h
        lines = images.shape[1]
        image_loads[j].wait()
        step = 256 // group
        for first in range(0, padded, step):
            count = min(step, padded - first)
            taken = min(step * group, lines - first * group)
            shape = (own * count, taken)
            row = lax.broadcasted_iota(jnp.int32, shape, 0)
            column = lax.broadcasted_iota(jnp.int32, shape, 1)
            wanted = (row % count) * group + own * h + row // count
            chosen = (column == wanted).astype(F32).astype(BF16)
            source = images[j, first * group : first * group + taken]
            picked[j, :, first : first + count] = (
                dot(chosen, source).astype(BF16).reshape(own, count, images.shape[2])
            )
        image_stores[j].start()

    def at(k, place):
        first = pl.multiple_of((place[0] * n_t + place[2]) * rows, 16)
        lines = pl.ds(first, rows)
        return small.at[lines] if k == n_k else w.at[k, lines]

    def hop(q, origin, place, sems, j):
        return remote(at(q, origin), at(q, origin), sems.at[0, j], sems.at[1, j], place)

    def half_hop(q, origin, place, half):
        part = at(q, origin).at[pl.ds(*halves[half])]
        j = 2 * q + half
        return remote(part, part, d_sems.at[0, j], d_sems.at[1, j], place)

    me = (s, h, t)
    from_d = (across_x[0], h, across_y[2])
    sent = []

    def send(copy):
        copy.start()
        sent.append(copy)

    def assemble(k):
        for i in range(0, n_h, 2):
            lines = jnp.concatenate([lined[i, k], lined[i + 1, k]], axis=1)
            at(k, me)[:, i * block : (i + 2) * block] = dot(lines, pair).astype(BF16)
        if k == 0:
            lines = jnp.concatenate([lined[i, k] for i in range(n_h)], axis=1)
            at(n_k, me)[...] = (dot(lines, beside) + extra[...]).astype(BF16)
        for q in members(k):
            send(hop(q, me, across_x, x_sems, q))
            send(hop(q, me, across_y, y_sems, q))
            send(hop(q, me, sibling, c_sems, 4 * q))

    def members(k):
        return (0, n_k) if k == 0 else (k,)

    def relay_xy(k):
        for q in members(k):
            hop(q, across_x, across_x, x_sems, q).wait_recv()
            send(half_hop(q, across_x, across_y, 0))
            send(hop(q, across_x, sibling, c_sems, 4 * q + 1))
            hop(q, across_y, across_y, y_sems, q).wait_recv()
            send(half_hop(q, across_y, across_x, 1))
            send(hop(q, across_y, sibling, c_sems, 4 * q + 2))

    def relay_d(k):
        for q in members(k):
            half_hop(q, from_d, across_y, 0).wait_recv()
            half_hop(q, from_d, across_x, 1).wait_recv()
            send(hop(q, from_d, sibling, c_sems, 4 * q + 3))

    for wave in range(n_k + n_h - 2):
        for d in range(1, n_h):
            if 0 <= wave - d + 1 < n_k:
                relay(chunks[wave - d + 1], d)
        turn(2)
        i = wave - n_h + 2
        if i >= 0:
            assemble(chunks[i])
            if i in (1, 2):
                pick_images(i - 1)
            if i >= 1:
                relay_xy(chunks[i - 1])
            if i >= 2:
                relay_d(chunks[i - 2])
            turn(2)
    relay_xy(chunks[-1])
    relay_d(chunks[-2])
    turn(2 * n_tiles)
    relay_d(chunks[-1])
    stores = []
    for k in chunks:
        for q in members(k):
            for j in range(4):
                hop(q, me, sibling, c_sems, 4 * q + j).wait_recv()
            if q == n_k:
                stores.append(pltpu.make_async_copy(small, small_out, o_sems.at[q]))
            else:
                stores.append(pltpu.make_async_copy(w.at[q], w_out.at[q], o_sems.at[q]))
            stores[-1].start()
    for copy in sent:
        copy.wait_send()
    for origin in range(n_h):
        @pl.when((origin <= h) & (h < n_h - 1))
        def _():
            for k in range(n_k):
                z_hop(k, origin, 1).wait_send()

        @pl.when((origin >= h) & (h > 0))
        def _():
            for k in range(n_k):
                z_hop(k, origin, 0).wait_send()

    for i in range(depth):
        store(2 * n_tiles - depth + i).wait()
    for copy in image_stores:
        copy.wait()
    for copy in stores:
        copy.wait()


def gather_weights(
    sizes, w_attn, phi_t, out_bias, scales, biases, in_bias, experts, tokens, cotangent
):
    n_k, rows, _ = w_attn.shape
    wide = 256
    n_s, n_h, n_t = sizes
    width = n_s * n_t * rows
    vmem = pl.BlockSpec(memory_space=pltpu.VMEM)
    hbm = pl.BlockSpec(memory_space=pl.ANY)
    dma = pltpu.SemaphoreType.DMA
    hidden = experts.shape[3]
    small = (width, wide)
    images = jax.ShapeDtypeStruct((2, 208, width), BF16)
    return pl.pallas_call(
        partial(gather_kernel, sizes),
        out_shape=(
            jax.ShapeDtypeStruct((n_k, width, width), BF16),
            jax.ShapeDtypeStruct(small, BF16),
            jax.ShapeDtypeStruct((2, experts.shape[2], experts.shape[0], hidden), BF16),
            images, images,
        ),
        in_specs=[vmem] * 6 + [hbm] * 3,
        out_specs=(hbm,) * 5,
        scratch_shapes=[
            pltpu.VMEM((n_k, width, width), BF16),
            pltpu.VMEM(small, BF16),
            pltpu.VMEM((n_h, n_k, rows, wide), BF16),
            pltpu.VMEM((rows, wide), F32),
            pltpu.VMEM((128, rows), F32),
            pltpu.VMEM((4, 16, 16, hidden), BF16),
            pltpu.VMEM((4, 16, 16, hidden), BF16),
            pltpu.VMEM((2, *tokens.shape), BF16),
            pltpu.VMEM((2, *images.shape), BF16),
            dma((n_k, n_h, 2)), dma((n_k, n_h)), dma((2, n_k + 1)), dma((2, n_k + 1)),
            dma((2, 2 * (n_k + 1))), dma((2, 4 * (n_k + 1))), dma((2, 4)), dma((n_k + 1,)),
            dma((2, 2)),
        ],
        compiler_params=pltpu.CompilerParams(
            collective_id=3, has_side_effects=True, vmem_limit_bytes=VMEM_BYTES
        ),
        name="gather_weights",
    )(w_attn, phi_t, out_bias, scales, biases, in_bias, experts, tokens, cotangent)


def reduce_kernel(
    sizes, grads, small, out, core_in, core_small, met, met_small,
    d_in, d_small, x_in, x_small, y_in, y_small, pieces, z_in,
    c_sems, d_sems, x_sems, y_sems, z_send, z_recv,
):
    (s, h, t), core, chip, sibling, across_x, across_y, line = plane(sizes)
    n_k, width, _ = grads.shape
    n_s, n_h, n_t = sizes
    rows = width // (n_s * n_t)
    wide = pieces.shape[3]
    pair = n_t * rows
    half = rows // 2
    halves = (pl.ds(0, half), pl.ds(half, half))
    chunks = (0, 2, 1, 3)

    def members(k):
        return (0, n_k) if k == 0 else (k,)

    def pick(q, large, little):
        return little if q == n_k else large.at[q]

    def core_copy(q, x):
        first = pl.multiple_of((2 * x + 1 - core) * pair, 16)
        return remote(
            pick(q, grads, small).at[pl.ds(first, pair)],
            pick(q, core_in, core_small).at[x],
            c_sems.at[0, 2 * q + x], c_sems.at[1, 2 * q + x], sibling,
        )

    for k in chunks:
        for q in members(k):
            for x in range(2):
                core_copy(q, x).start()
    joined = pair_matrix(width // n_h, wide, True)
    shape = (small.shape[1], n_h * wide)
    row = lax.broadcasted_iota(jnp.int32, shape, 0)
    column = lax.broadcasted_iota(jnp.int32, shape, 1)
    lane, of = column % wide - width // n_h, column // wide
    beside = (lane >= 0) & (lane < 16) & (row == of * 16 + lane)
    beside |= (lane >= 16) & (lane < 20) & (row == n_h * 16 + lane - 16)
    beside = beside.astype(F32).astype(BF16)
    to_d, to_x, to_y = (d_in, d_small), (x_in, x_small), (y_in, y_small)
    sent = []

    def hop(q, kind, part, source, place):
        sems = {id(to_d): d_sems, id(to_x): x_sems, id(to_y): y_sems}[id(kind)]
        target = pick(q, *kind)
        target = target.at[part] if kind is to_d else target.at[halves[part]]
        j = 2 * q + part
        return remote(source, target, sems.at[0, j], sems.at[1, j], place)

    def send(copy):
        copy.start()
        sent.append(copy)

    def part_of(q, x, y, part):
        return pick(q, met, met_small).at[x, y].at[halves[part]]

    def arrived(q, kind, part):
        hop(q, kind, part, part_of(q, 0, 0, part), sibling).wait_recv()

    def open_up(q):
        part = pick(q, met, met_small)
        for x in range(2):
            core_copy(q, x).wait_recv()
            first = pl.multiple_of((2 * x + core) * pair, 16)
            own = pick(q, grads, small)[pl.ds(first, pair)].astype(F32)
            total = own + pick(q, core_in, core_small)[x].astype(F32)
            part[x] = total.astype(BF16).reshape(n_t, rows, total.shape[1])
        send(hop(q, to_d, 0, part_of(q, 1 - chip, 1 - t, 0), across_x))
        send(hop(q, to_d, 1, part_of(q, 1 - chip, 1 - t, 1), across_y))
        send(hop(q, to_x, 0, part_of(q, 1 - chip, t, 0), across_x))
        send(hop(q, to_y, 1, part_of(q, chip, 1 - t, 1), across_y))

    def pass_on(q):
        for part, kind, x, y, place in (
            (0, to_y, chip, 1 - t, across_y),
            (1, to_x, 1 - chip, t, across_x),
        ):
            arrived(q, to_d, part)
            block = part_of(q, x, y, part)
            total = block[...].astype(F32) + pick(q, *to_d)[part].astype(F32)
            block[...] = total.astype(BF16)
            send(hop(q, kind, part, block, place))

    def whole(q):
        for kind in (to_x, to_y):
            for part in range(2):
                arrived(q, kind, part)
        total = pick(q, met, met_small)[chip, t].astype(F32) + pick(q, *to_x)[...].astype(F32)
        return (total + pick(q, *to_y)[...].astype(F32)).astype(BF16)

    def z_copy(k, target, up):
        place = line[1] if up else line[n_h - 1]
        return remote(
            pieces.at[target, k], z_in.at[up, target, k],
            z_send.at[up, target, k], z_recv.at[up, target, k], place,
        )

    def pass_along(k, hops):
        for up in range(2):
            for target in range(n_h - 1, -1, -1) if up else range(n_h):
                further = target > h if up else target < h

                @pl.when(further & (h == (hops if up else n_h - 1 - hops)))
                def _():
                    if hops > 0:
                        z_copy(k, target, up).wait_recv()
                        total = pieces[target, k].astype(F32) + z_in[up, target, k].astype(F32)
                        pieces[target, k] = total.astype(BF16)
                    z_copy(k, target, up).start()

    def share_out(k):
        value = whole(k)
        columns = width // n_h
        if k == 0:
            little = dot(whole(n_k), beside)
        for i in range(0, n_h, 2):
            lanes = dot(value[:, i * columns : (i + 2) * columns], joined)
            if k == 0:
                lanes = lanes + little[:, i * wide : (i + 2) * wide]
            pieces[i, k] = lanes[:, :wide].astype(BF16)
            pieces[i + 1, k] = lanes[:, wide:].astype(BF16)
        pass_along(k, 0)

    for i in range(n_k + 2 + n_h - 2):
        if i < n_k:
            for q in members(chunks[i]):
                open_up(q)
        if 0 <= i - 1 < n_k:
            for q in members(chunks[i - 1]):
                pass_on(q)
        if 0 <= i - 2 < n_k:
            share_out(chunks[i - 2])
        for hops in range(1, n_h - 1):
            if 0 <= i - 2 - hops < n_k:
                pass_along(chunks[i - 2 - hops], hops)
    for k in chunks:
        out[k] = pieces[h, k].astype(F32)
        for up, there in ((1, h > 0), (0, h < n_h - 1)):
            @pl.when(there)
            def _():
                z_copy(k, h, up).wait_recv()
                out[k] = out[k] + z_in[up, h, k].astype(F32)

    for k in chunks:
        for q in members(k):
            for x in range(2):
                core_copy(q, x).wait_send()
    for copy in sent:
        copy.wait_send()
    for target in range(n_h):
        for up in range(2):
            @pl.when(target > h if up else target < h)
            def _():
                for k in range(n_k):
                    z_copy(k, target, up).wait_send()


def reduce_grads(sizes, grads, small):
    n_k, width, _ = grads.shape
    n_s, n_h, n_t = sizes
    rows, wide, thin = width // (n_s * n_t), 256, small.shape[1]
    vmem = pl.BlockSpec(memory_space=pltpu.VMEM)
    dma = pltpu.SemaphoreType.DMA

    def buffers(*lead):
        return [
            pltpu.VMEM((n_k, *lead, width), BF16),
            pltpu.VMEM((*lead, thin), BF16),
        ]

    return pl.pallas_call(
        partial(reduce_kernel, sizes),
        out_shape=jax.ShapeDtypeStruct((n_k, rows, wide), F32),
        in_specs=[vmem, vmem],
        out_specs=vmem,
        scratch_shapes=[
            *buffers(2, n_t * rows), *buffers(2, n_t, rows),
            *buffers(2, rows // 2), *buffers(rows), *buffers(rows),
            pltpu.VMEM((n_h, n_k, rows, wide), BF16),
            pltpu.VMEM((2, n_h, n_k, rows, wide), BF16),
            dma((2, 2 * (n_k + 1))), dma((2, 2 * (n_k + 1))), dma((2, 2 * (n_k + 1))),
            dma((2, 2 * (n_k + 1))), dma((2, n_h, n_k)), dma((2, n_h, n_k)),
        ],
        compiler_params=pltpu.CompilerParams(
            collective_id=4, has_side_effects=True, vmem_limit_bytes=VMEM_BYTES
        ),
        name="reduce_grads",
    )(grads, small)


def expert_kernel(sizes, backward, *refs):
    if backward:
        (blocks, weights, gate, output, slots_out, act_out, back_out, bias_out, sum_out, gathered,
         w_a, w_b, gate_v, sums, slots, act, core_out, core_in, x_out, x_in, land, leave, back, land_back,
         w_sem, o_sem, in_sems, back_sems, core_sems, x_sems, act_sems, b_sems,
         g_send, g_recv, g_sem,
         bias_all, bias_send, bias_land) = refs
    else:
        (blocks, weights, gate, slots_out, act_out, gate_out, back_out,
         w_a, w_b, sums, slots, act, core_out, core_in, x_out, x_in, land, leave, back, land_back,
         w_sem, o_sem, in_sems, back_sems, core_sems, x_sems, act_sems, bias) = refs
    peers = Peers(sizes)
    s, h, t = peers.at
    n_s, n_h, n_t = sizes
    me = peers.flat(peers.at)
    core, chip = lax.rem(s, 2), s // 2
    sibling = (s + 1 - 2 * core, h, t)
    across = (lax.rem(s + 2, n_s), h, t)
    half = act.shape[0] // 2
    own, other = core * half, (1 - core) * half
    n_blocks = peers.count
    first = 1 if backward else 0
    loads = [
        pltpu.make_async_copy(weights.at[first], w_a, w_sem.at[0]),
        pltpu.make_async_copy(weights.at[1 - first], w_b, w_sem.at[1]),
    ]
    for load in loads:
        load.start()
    if backward:
        gate_load = pltpu.make_async_copy(gate, gate_v, o_sem.at[0])
        gate_load.start()
    peers.greet_all()

    def block_out(p, k):
        place = peers.step(k, 1)
        return remote(
            blocks.at[place[1], place[0], p], land.at[p, me],
            in_sems.at[0, p, k], in_sems.at[1, p, k], place,
        )

    def block_in(p, k):
        source = peers.flat(peers.step(k, -1))
        return remote(
            blocks.at[0, 0, p], land.at[p, source], in_sems.at[0, p, k], in_sems.at[1, p, k], sibling
        )

    def each(function, count=n_blocks, start=1):
        lax.fori_loop(start, count, lambda k, carry: (function(k), carry)[1], 0)

    for p in range(2):
        for k in range(1, n_blocks):
            block_out(p, k).start()
        land[p, me] = blocks[h, s, p]
    few = half // 2
    group = 16
    many = 2 * group
    out_row = lax.broadcasted_iota(jnp.int32, (16 * group, 16 * group), 0)
    in_row = lax.broadcasted_iota(jnp.int32, (16 * group, 16 * group), 1)
    there = (out_row // many == in_row % (2 * few)) & (out_row % many == in_row // (2 * few))
    there = there.astype(F32).astype(BF16)
    again = (in_row // many == out_row % (2 * few)) & (in_row % many == out_row // (2 * few))
    again = again.astype(F32).astype(BF16)

    def receive(p):
        each(lambda k: block_in(p, k).wait_recv())
        for b in range(n_blocks // group):
            rows = land[p, b * group : (b + 1) * group].reshape(group * 16, land.shape[3])
            turned = dot(there, rows).astype(BF16).reshape(2 * few, many, land.shape[3])
            for c in range(2):
                first = c * half + p * few
                slots[first : first + few, b * many : (b + 1) * many, :] = turned[
                    c * few : (c + 1) * few
                ]

    if backward:
        own_images = output.shape[0]
        line = [(s, lax.rem(h + d, n_h), t) for d in range(n_h)]
        g_own = pltpu.make_async_copy(output, gathered.at[pl.ds(h * own_images, own_images)], g_sem)
        g_own.start()

        def z_hop(i, origin, up, source=None):
            there = gathered.at[origin * own_images + i]
            return remote(
                there if source is None else source, there,
                g_send.at[i, origin, up], g_recv.at[i, origin], line[1] if up else line[n_h - 1],
            )

        def relay(i, d):
            @pl.when(h >= d)
            def _():
                z_hop(i, h - d, 1).wait_recv()

                @pl.when((h < n_h - 1) & (d < n_h - 1))
                def _():
                    z_hop(i, h - d, 1).start()

            @pl.when(h + d < n_h)
            def _():
                z_hop(i, h + d, 0).wait_recv()

                @pl.when((h > 0) & (d < n_h - 1))
                def _():
                    z_hop(i, h + d, 0).start()

        def gather_output():
            for i in range(own_images):
                @pl.when(h < n_h - 1)
                def _():
                    z_hop(i, h, 1, output.at[i]).start()

                @pl.when(h > 0)
                def _():
                    z_hop(i, h, 0, output.at[i]).start()
    else:
        piece, count = 6 * 64, act.shape[2] // (6 * 64)
        row = lax.broadcasted_iota(jnp.int32, (6 * 128, piece), 0)
        column = lax.broadcasted_iota(jnp.int32, (6 * 128, piece), 1)
        lane = row % 128
        place = (lane < 64) & (column == (row // 128) * 64 + lane)
        place = place.astype(F32).astype(BF16)
        for m in range(count):
            first = (t * count + m) * 96
            lines = [
                gate[pl.ds(pl.multiple_of(first + j * 16, 16), 16), 128:256] for j in range(6)
            ]
            bias[:, m * piece : (m + 1) * piece] = dot(jnp.concatenate(lines, axis=1), place)

    receive(0)
    if backward:
        gather_output()
    loads[0].wait()

    def core_copy(j):
        return remote(
            core_out.at[j], core_in.at[j], core_sems.at[0, j], core_sems.at[1, j], sibling
        )

    def x_copy(j):
        return remote(x_out.at[j], x_in.at[j], x_sems.at[0, j], x_sems.at[1, j], across)

    def act_copy(j):
        return remote(
            act.at[own + j], act.at[own + j], act_sems.at[0, j], act_sems.at[1, j], sibling
        )

    def act_in(j):
        return remote(
            act.at[other + j], act.at[other + j], act_sems.at[0, j], act_sems.at[1, j], sibling
        )

    def meet(j):
        core_copy(j).wait_recv()
        sums[j] = sums[j] + core_in[j].astype(F32)
        x_out[j] = sums[j].astype(BF16)
        x_copy(j).start()

    def first_sums(j):
        core_out[j] = dot(slots[other + j], w_a[other + j]).astype(BF16)
        core_copy(j).start()

        @pl.when(j > 0)
        def _():
            meet(j - 1)

        sums[j] = dot(slots[own + j], w_a[own + j])

    each(first_sums, few, 0)
    receive(1)
    each(first_sums, half, few)
    meet(half - 1)
    loads[1].wait()
    if backward:
        gate_load.wait()

    def second(e):
        leave[e] = dot_t(act[e], w_b[e]).astype(BF16)

    def finish(j):
        x_copy(j).wait_recv()
        value = sums[j] + x_in[j].astype(F32)
        if backward:
            act[own + j] = (value * gate_v[j]).astype(BF16)
        else:
            value = value + bias[pl.ds(own + j, 1), :]
            cumulative = 0.5 + 0.5 * lax.erf(value * 0.7071067811865476)
            act[own + j] = (value * cumulative).astype(BF16)
            sums[j] = cumulative + value * (
                jnp.exp(value * value * -0.5) * 0.3989422804014327
            )
        act_copy(j).start()
        second(own + j)

        @pl.when(j > 0)
        def _():
            act_in(j - 1).wait_recv()
            second(other + j - 1)

        if backward:
            for when, i, d in ((2, 0, 1), (3, 1, 1), (5, 0, 2), (7, 1, 2)):
                @pl.when(j == when)
                def _():
                    relay(i, d)

    def back_copy(p, k):
        place = peers.step(k, 1)
        return remote(
            back.at[p, peers.flat(place)], land_back.at[p, me],
            back_sems.at[0, p, k], back_sems.at[1, p, k], place,
        )

    def back_in(p, k):
        source = peers.flat(peers.step(k, -1))
        return remote(
            back.at[p, 0], land_back.at[p, source],
            back_sems.at[0, p, k], back_sems.at[1, p, k], sibling,
        )

    def give_back(p):
        for b in range(n_blocks // group):
            rows = jnp.concatenate(
                [
                    leave[c * half + p * few : c * half + (p + 1) * few, b * many : (b + 1) * many, :]
                    for c in range(2)
                ],
                axis=0,
            ).reshape(group * 16, leave.shape[2])
            turned = dot(again, rows).astype(BF16)
            back[p, b * group : (b + 1) * group] = turned.reshape(group, 16, leave.shape[2])
        for k in range(1, n_blocks):
            back_copy(p, k).start()
        land_back[p, me] = back[p, me]

    each(finish, few + 1, 0)
    give_back(0)
    each(finish, half, few + 1)
    act_in(half - 1).wait_recv()
    second(other + half - 1)
    give_back(1)
    stores = [pltpu.make_async_copy(act, act_out, o_sem.at[1])]
    if not backward:
        stores.append(pltpu.make_async_copy(sums, gate_out, o_sem.at[0]))
    for store in stores:
        store.start()
    slots_out[...] = slots[...]
    if backward:
        across_t = (s, h, 1 - t)
        width = bias_out.shape[1]

        def bias_row(e):
            bias_all[pl.ds(e, 1), :] = jnp.sum(act[e].astype(F32), axis=0, keepdims=True)

        each(bias_row, 2 * half, 0)

        def slot_row(e):
            sum_out[pl.ds(e, 1), :] = jnp.sum(slots[e].astype(F32), axis=0, keepdims=True)

        each(slot_row, 2 * half, 0)

        def piece(for_t):
            return bias_all[:, pl.ds(pl.multiple_of((core * n_t + for_t) * width, 128), width)]

        bias_send[...] = piece(1 - t)
        bias_copy = remote(bias_send, bias_land, b_sems.at[0], b_sems.at[1], across_t)
        bias_copy.start()
        bias_copy.wait()
        bias_out[...] = jnp.where(t == chip, piece(t), bias_land[...])
    for p in range(2):
        each(lambda k: back_in(p, k).wait_recv())
    back_out[...] = land_back[...]
    for store in stores:
        store.wait()
    if backward:
        relay(0, 3)
        relay(1, 3)
        g_own.wait()
        for origin in range(n_h):
            @pl.when((origin < h) & (h < n_h - 1))
            def _():
                for i in range(own_images):
                    z_hop(i, origin, 1).wait_send()

            @pl.when((origin > h) & (h > 0))
            def _():
                for i in range(own_images):
                    z_hop(i, origin, 0).wait_send()

        @pl.when(h < n_h - 1)
        def _():
            for i in range(own_images):
                z_hop(i, h, 1, output.at[i]).wait_send()

        @pl.when(h > 0)
        def _():
            for i in range(own_images):
                z_hop(i, h, 0, output.at[i]).wait_send()

    for p in range(2):
        each(lambda k: block_out(p, k).wait_send())
        each(lambda k: back_copy(p, k).wait_send())
    for copy in (core_copy, x_copy, act_copy):
        each(lambda j: copy(j).wait_send(), half, 0)


def expert_pass(sizes, backward, blocks, weights, gate, output=None, bias_width=0):
    _, experts, rows, hidden = weights.shape
    devices = sizes[0] * sizes[1] * sizes[2]
    images = 2 * devices
    half = experts // 2
    vmem = pl.BlockSpec(memory_space=pltpu.VMEM)
    hbm = pl.BlockSpec(memory_space=pl.ANY)
    slots = jax.ShapeDtypeStruct((experts, images, rows), BF16)
    act = jax.ShapeDtypeStruct((experts, images, hidden), BF16)
    gate_shape = (half, images, hidden)
    returned = jax.ShapeDtypeStruct((2, devices, experts, rows), BF16)
    if backward:
        operands, in_specs = (blocks, weights, gate, output), [vmem, hbm, hbm, hbm]
        outs = (
            slots, act, returned,
            jax.ShapeDtypeStruct((experts, bias_width), F32),
            jax.ShapeDtypeStruct((experts, rows), F32),
            jax.ShapeDtypeStruct((sizes[1] * output.shape[0], *output.shape[1:]), BF16),
        )
        out_specs = (vmem, hbm, vmem, vmem, vmem, hbm)
    else:
        operands, in_specs = (blocks, weights, gate), [vmem, hbm, vmem]
        outs = (slots, act, jax.ShapeDtypeStruct(gate_shape, F32), returned)
        out_specs = (vmem, hbm, hbm, vmem)
    weight = pltpu.VMEM((experts, rows, hidden), BF16)
    chunk = pltpu.VMEM((half, images, hidden), BF16)
    block = pltpu.VMEM((2, devices, experts, rows), BF16)
    dma = pltpu.SemaphoreType.DMA
    scratch = [weight, weight]
    if backward:
        scratch.append(pltpu.VMEM(gate_shape, F32))
    scratch += [
        pltpu.VMEM(gate_shape, F32),
        pltpu.VMEM(slots.shape, BF16),
        pltpu.VMEM(act.shape, BF16),
        chunk, chunk, chunk, chunk, block,
        pltpu.VMEM(slots.shape, BF16),
        block, block,
        dma((2,)), dma((2,)), dma((2, 2, devices)), dma((2, 2, devices)),
        dma((2, half)), dma((2, half)), dma((2, half)),
    ]
    if backward:
        scratch += [
            dma((2,)), dma((output.shape[0], sizes[1], 2)), dma((output.shape[0], sizes[1])), dma,
            pltpu.VMEM((experts, hidden), F32),
            pltpu.VMEM((experts, bias_width), F32),
            pltpu.VMEM((experts, bias_width), F32),
        ]
    else:
        scratch.append(pltpu.VMEM((experts, hidden), F32))
    return pl.pallas_call(
        partial(expert_kernel, sizes, backward),
        out_shape=outs,
        in_specs=in_specs,
        out_specs=out_specs,
        scratch_shapes=scratch,
        compiler_params=pltpu.CompilerParams(
            collective_id=2 if backward else 1, has_side_effects=True, vmem_limit_bytes=VMEM_BYTES
        ),
        cost_estimate=pl.CostEstimate(
            flops=8 * images * experts * rows * hidden,
            bytes_accessed=weights.size * 2,
            transcendentals=0,
        ),
        name="experts_back" if backward else "experts_ahead",
    )(*operands)


def weight_grad_kernel(slots_0, act_0, slots_1, act_1, out, lines, pick, same):
    group, images, rows = slots_0.shape
    d_block = out.shape[0]
    n = group * d_block
    m, d = pl.program_id(0), pl.program_id(2)

    @pl.when((m == 0) & (pl.program_id(1) == 0) & (d == 0))
    def _():
        row = lax.broadcasted_iota(jnp.int32, pick.shape, 0)
        column = lax.broadcasted_iota(jnp.int32, pick.shape, 1)
        pick[...] = (column == row // group).astype(F32).astype(BF16)
        row = lax.broadcasted_iota(jnp.int32, same.shape, 0)
        column = lax.broadcasted_iota(jnp.int32, same.shape, 1)
        same[...] = (row % group == column // images).astype(F32)

    def prepare(slots):
        @pl.when(d == 0)
        def _():
            turned = slots[...].reshape(group * images, rows).astype(F32)
            lines[...] = jnp.swapaxes(turned, 0, 1).astype(BF16)

    def term(act):
        mine = lines[pl.ds(pl.multiple_of(d * d_block, d_block), d_block)]
        spread = (dot(pick[...], mine) * same[...]).astype(BF16)
        values = act[...].reshape(group * images, act.shape[2])
        out[...] = dot(spread, values).reshape(out.shape)

    @pl.when(m == 0)
    def _():
        prepare(slots_0)
        term(act_0)

    @pl.when(m == 1)
    def _():
        prepare(slots_1)
        term(act_1)


def weight_grads(slots_0, act_0, slots_1, act_1):
    experts, images, rows = slots_0.shape
    hidden = act_0.shape[2]
    group, d_block = 8, 96
    last = experts // group - 1

    def early(m, g, d):
        return jnp.where(m == 0, g, last), 0, 0

    def late(m, g, d):
        return jnp.where(m == 0, 0, g), 0, 0

    slots, act = (group, images, rows), (group, images, hidden)
    return pl.pallas_call(
        weight_grad_kernel,
        grid=(2, experts // group, rows // d_block),
        out_shape=jax.ShapeDtypeStruct((rows, 2, experts, hidden), F32),
        in_specs=[
            pl.BlockSpec(slots, early), pl.BlockSpec(act, early),
            pl.BlockSpec(slots, late), pl.BlockSpec(act, late),
        ],
        out_specs=pl.BlockSpec((d_block, 1, group, hidden), lambda m, g, d: (d, m, g, 0)),
        scratch_shapes=[
            pltpu.VMEM((rows, group * images), BF16),
            pltpu.VMEM((group * d_block, d_block), BF16),
            pltpu.VMEM((group * d_block, group * images), F32),
        ],
        compiler_params=pltpu.CompilerParams(vmem_limit_bytes=VMEM_BYTES),
        cost_estimate=pl.CostEstimate(
            flops=4 * images * experts * rows * hidden,
            bytes_accessed=8 * rows * experts * hidden,
            transcendentals=0,
        ),
        name="weight_grads",
    )(slots_0, act_0, slots_1, act_1)


def dot_r(a, b):
    return lax.dot_general(a, b, (((0,), (0,)), ((), ())), preferred_element_type=F32)


def row_of(shape, axis):
    return lax.broadcasted_iota(jnp.int32, shape, axis)


def one_hot(mask):
    return mask.astype(F32).astype(BF16)


def order_matrix(n_h, few, back):
    n = n_h * 8 * few
    shape = (n, n)
    blocked, natural = row_of(shape, 1 if back else 0), row_of(shape, 0 if back else 1)
    f, half, image = blocked % few, (blocked // few) % 2, (blocked // (2 * few)) % 2
    group = blocked // (4 * few)
    if back:
        part, h = group // n_h, group % n_h
    else:
        h, part = group // 2, group % 2
    expert = ((h * 2 + half) * 2 + part) * few + f
    return one_hot(natural == image * (4 * n_h * few) + expert)


def norm_parts(x, scale, shift, live):
    centered = x - jnp.mean(x, axis=-1, keepdims=True)
    inverse = lax.rsqrt(jnp.mean(centered * centered, axis=-1, keepdims=True) + epsilon)
    unit = centered * inverse
    return unit * scale + shift, unit, inverse


def norm_back(grad, unit, inverse, scale):
    scaled = grad * scale
    average = jnp.mean(scaled, axis=-1, keepdims=True)
    projection = jnp.mean(scaled * unit, axis=-1, keepdims=True)
    return (
        inverse * (scaled - average - unit * projection),
        jnp.sum(grad * unit, axis=0, keepdims=True),
        jnp.sum(grad, axis=0, keepdims=True),
    )


def norm_rows(small):
    return jnp.swapaxes(small[:, 128:].astype(F32), 0, 1)[64:68]


def slots_to_blocks(slots, blocks, columns, joined, order):
    n_h, n_s = blocks.shape[:2]
    turned = dot(order, slots).astype(BF16)
    wide = joined.shape[1] // 2
    for s in range(0, n_s, 2):
        lanes = dot(turned[:, s * columns : (s + 2) * columns], joined).astype(BF16)
        for h in range(n_h):
            for p in range(2):
                rows = (h * 2 + p) * 16
                for e in range(2):
                    blocks[h, s + e, p] = lanes[rows : rows + 16, e * wide : e * wide + columns]


def blocks_to_slots(back, sizes, order, pair, padded):
    n_s, n_h, n_t = sizes
    columns = back.shape[3]
    both = jnp.concatenate([order] * n_t, axis=1)
    results = []
    for s in range(n_s):
        rows = jnp.concatenate(
            [
                back[p, (s * n_h + h) * n_t + t]
                for t in range(n_t)
                for p in range(2)
                for h in range(n_h)
            ],
            axis=0,
        )
        padded[s % 2, :, :columns] = dot(both, rows)
        if s % 2:
            value = jnp.concatenate([padded[0], padded[1]], axis=1)
            high = value.astype(BF16)
            rest = (value - high.astype(F32)).astype(BF16)
            results.append(dot(high, pair) + dot(rest, pair))
    return jnp.concatenate(results, axis=1)


def live_rows(shape, length):
    return row_of(shape, 0) < length


def ahead_kernel(
    length, tokens, small, w_hbm, blocks, normed_1, query, keyed, valued, context, hidden, normed_2,
    dispatch_out, combine_out, w, joined, order, w_sem,
):
    n, rows, width = tokens.shape
    keys = keyed.shape[1]
    loads = [pltpu.make_async_copy(w_hbm.at[k], w.at[k], w_sem.at[k]) for k in range(4)]
    for load in loads:
        load.start()
    norms = norm_rows(small)
    live = live_rows((rows, 1), length)
    for i in range(n):
        value, _, _ = norm_parts(tokens[i].astype(F32), norms[0:1], norms[2:3], live)
        normed_1[i] = jnp.where(live, value, 0.0).astype(BF16)
    joined[...] = pair_matrix(blocks.shape[4], joined.shape[1] // 2, True)
    order[...] = order_matrix(blocks.shape[0], 4, False)
    flat = (n * rows, width)
    for k, target in enumerate((query, keyed, valued)):
        loads[k].wait()
        value = dot(normed_1[...].reshape(flat), w[k]).astype(BF16).reshape(n, rows, width)
        if k == 0:
            target[...] = value
        else:
            target[:, :rows] = value
            target[:, rows:] = jnp.zeros((n, keys - rows, width), BF16)
    factor = HEAD_DIM ** (-0.5)
    pairs = width // 128
    lane = row_of((rows, 128), 1)
    shown = row_of((rows, keys), 1) < length

    def attend(step, carry):
        i = step // pairs
        lanes = pl.ds(pl.multiple_of((step % pairs) * 128, 128), 128)
        q, k, v = query[i, :, lanes], keyed[i, :, lanes], valued[i, :, lanes]
        scaled = q * jnp.bfloat16(factor)
        parts = []
        for a in range(2):
            mine = (lane < 64) if a == 0 else (lane >= 64)
            scores = dot_t(jnp.where(mine, scaled, jnp.zeros_like(q)), k)
            scores = jnp.where(shown, scores, -1e30)
            exponent = jnp.exp(scores - jnp.max(scores, axis=-1, keepdims=True))
            probs = exponent * (1.0 / jnp.sum(exponent, axis=-1, keepdims=True))
            parts.append(dot(probs.astype(BF16), v))
        context[i, :, lanes] = jnp.where(lane < 64, parts[0], parts[1]).astype(BF16)
        return carry

    lax.fori_loop(0, n * pairs, attend, 0, unroll=2)
    loads[3].wait()
    attended = dot_t(context[...].reshape(flat), w[3]).reshape(n, rows, width)
    for i in range(n):
        value = tokens[i].astype(F32) + attended[i]
        hidden[i] = value
        value, _, _ = norm_parts(value, norms[1:2], norms[3:4], live)
        normed_2[i] = jnp.where(live, value, 0.0).astype(BF16)
    logits = dot(normed_2[...].reshape(flat), small[:, :128]).reshape(n, rows, 128)
    experts = row_of((rows, 128), 1) < 64
    slots = []
    for i in range(n):
        here = logits[i]
        down = jnp.where(live, here, -1e30)
        exponent = jnp.exp(down - jnp.max(down, axis=0, keepdims=True))
        dispatch = exponent / jnp.sum(exponent, axis=0, keepdims=True)
        dispatch = jnp.where(experts, dispatch, 0.0)
        across = jnp.where(experts, here, -1e30)
        exponent = jnp.exp(across - jnp.max(across, axis=1, keepdims=True))
        combine = exponent / jnp.sum(exponent, axis=1, keepdims=True)
        dispatch_out[i] = dispatch
        combine_out[i] = combine
        slots.append(dot_r(dispatch.astype(BF16), normed_2[i])[:64].astype(BF16))
    slots_to_blocks(
        jnp.concatenate(slots, axis=0), blocks, blocks.shape[4], joined[...], order[...]
    )


def tokens_ahead(sizes, length, tokens, small, weights):
    n, rows, width = tokens.shape
    keys = 256
    vmem = pl.BlockSpec(memory_space=pltpu.VMEM)
    shape = jax.ShapeDtypeStruct
    wide = (n, keys, width)
    thin = shape((n, rows, 128), F32)
    return pl.pallas_call(
        partial(ahead_kernel, length),
        out_shape=(
            shape((sizes[1], sizes[0], 2, 16, width // sizes[0]), BF16),
            shape(tokens.shape, BF16), shape(tokens.shape, BF16), shape(wide, BF16),
            shape(wide, BF16), shape(tokens.shape, BF16), shape(tokens.shape, F32),
            shape(tokens.shape, BF16), thin, thin,
        ),
        in_specs=[vmem, vmem, pl.BlockSpec(memory_space=pl.ANY)],
        out_specs=(vmem,) * 10,
        scratch_shapes=[
            pltpu.VMEM(weights.shape, BF16),
            pltpu.VMEM((2 * width // sizes[0], 512), BF16),
            pltpu.VMEM((128, 128), BF16),
            pltpu.SemaphoreType.DMA((4,)),
        ],
        compiler_params=pltpu.CompilerParams(vmem_limit_bytes=VMEM_BYTES),
        name="tokens_ahead",
    )(tokens, small, weights)


def middle_kernel(
    sizes, back, small, combine, hidden, cotangent, output, blocks, grad_logits, padded
):
    n, rows, _ = hidden.shape
    columns = back.shape[3]
    padded[...] = jnp.zeros_like(padded)
    pair = pair_matrix(columns, padded.shape[2], False)
    joined = pair_matrix(columns, padded.shape[2], True)
    total = blocks_to_slots(back, sizes, order_matrix(sizes[1], 4, True), pair, padded)
    bias = jnp.swapaxes(small[:, :128].astype(F32), 0, 1)[64:]
    slots = []
    for i in range(n):
        slot_out = (total[i * 64 : (i + 1) * 64] + bias).astype(BF16)
        combine_b = combine[i].astype(BF16)[:, :64]
        output[i] = (hidden[i] + dot(combine_b, slot_out)).astype(BF16)
        grad_combine = dot_t(cotangent[i], slot_out)
        weight = combine[i][:, :64]
        weighted = jnp.sum(weight * grad_combine, axis=1, keepdims=True)
        grad_logits[i] = weight * (grad_combine - weighted)
        slots.append(dot_r(combine_b, cotangent[i]).astype(BF16))
    slots_to_blocks(
        jnp.concatenate(slots, axis=0), blocks, columns, joined, order_matrix(sizes[1], 4, False)
    )


def tokens_middle(sizes, back, small, combine, hidden, cotangent):
    n, rows, width = hidden.shape
    vmem = pl.BlockSpec(memory_space=pltpu.VMEM)
    shape = jax.ShapeDtypeStruct
    return pl.pallas_call(
        partial(middle_kernel, sizes),
        out_shape=(
            shape(hidden.shape, BF16),
            shape((sizes[1], sizes[0], 2, 16, width // sizes[0]), BF16),
            shape((n, rows, 64), F32),
        ),
        in_specs=[vmem] * 5,
        out_specs=(vmem,) * 3,
        scratch_shapes=[pltpu.VMEM((2, 128, 256), F32)],
        compiler_params=pltpu.CompilerParams(vmem_limit_bytes=VMEM_BYTES),
        name="tokens_middle",
    )(back, small, combine, hidden, cotangent)


def behind_kernel(
    sizes, length, back, small, w_hbm, tokens, normed_1, query, keyed, valued, context, hidden,
    normed_2, dispatch, grad_logits, cotangent, grads, small_grads, input_grad,
    w, padded, grad_hidden, rounded, grad_context, grad_q, grad_k, grad_v, w_sem,
):
    n, rows, width = tokens.shape
    keys = keyed.shape[1]
    loads = [pltpu.make_async_copy(w_hbm.at[k], w.at[k], w_sem.at[k]) for k in range(4)]
    for load in loads:
        load.start()
    norms = norm_rows(small)
    padded[...] = jnp.zeros_like(padded)
    pair = pair_matrix(back.shape[3], padded.shape[2], False)
    grad_slots = blocks_to_slots(
        back, sizes, order_matrix(sizes[1], 4, True), pair, padded
    ).astype(BF16)
    phi = small[:, :64]
    phi_grad = jnp.zeros((width, 64), F32)
    sums = []
    flat = (n * rows, width)
    for i in range(n):
        slots = grad_slots[i * 64 : (i + 1) * 64]
        weight = dispatch[i][:, :64]
        grad_dispatch = dot_t(normed_2[i], slots)
        weighted = jnp.sum(weight * grad_dispatch, axis=0, keepdims=True)
        logits = (weight * (grad_dispatch - weighted) + grad_logits[i]).astype(BF16)
        phi_grad = phi_grad + dot_r(normed_2[i], logits)
        grad = dot(weight.astype(BF16), slots) + dot_t(logits, phi)
        _, unit, inverse = norm_parts(hidden[i], norms[1:2], norms[3:4], None)
        grad_in, scale_grad, bias_grad = norm_back(grad, unit, inverse, norms[1:2])
        value = cotangent[i].astype(F32) + grad_in
        grad_hidden[i] = value
        rounded[i] = value.astype(BF16)
        sums.append((scale_grad, bias_grad))
    scale_2, bias_2 = sums[0][0] + sums[1][0], sums[0][1] + sums[1][1]
    flat_rounded = rounded[...].reshape(flat)
    loads[3].wait()
    grad_context[...] = dot(flat_rounded, w[3]).astype(BF16).reshape(n, rows, width)
    grads[3] = dot_r(flat_rounded, context[...].reshape(flat)).astype(BF16)
    factor = HEAD_DIM ** (-0.5)
    pairs = width // 128
    lane = row_of((rows, 128), 1)
    key_lane = row_of((keys, 128), 1)
    shown = row_of((rows, keys), 1) < length

    def attend(step, carry):
        i = step // pairs
        lanes = pl.ds(pl.multiple_of((step % pairs) * 128, 128), 128)
        q, k, v = query[i, :, lanes], keyed[i, :, lanes], valued[i, :, lanes]
        scaled = q * jnp.bfloat16(factor)
        g = grad_context[i, :, lanes]
        to_q, to_k, to_v = [], [], []
        for a in range(2):
            mine = (lane < 64) if a == 0 else (lane >= 64)
            scores = dot_t(jnp.where(mine, scaled, jnp.zeros_like(q)), k)
            grad_probs = dot_t(jnp.where(mine, g, jnp.zeros_like(g)), v)
            scores = jnp.where(shown, scores, -1e30)
            exponent = jnp.exp(scores - jnp.max(scores, axis=-1, keepdims=True))
            probs = exponent * (1.0 / jnp.sum(exponent, axis=-1, keepdims=True))
            weighted = jnp.sum(probs * grad_probs, axis=-1, keepdims=True)
            grad_scores = (probs * (grad_probs - weighted)).astype(BF16)
            to_v.append(dot_r(probs.astype(BF16), g))
            to_q.append(dot(grad_scores, k))
            to_k.append(dot_r(grad_scores, q))
        grad_q[i, :, lanes] = (jnp.where(lane < 64, to_q[0], to_q[1]) * factor).astype(BF16)
        kept = key_lane < 64
        grad_k[i, :, lanes] = (jnp.where(kept, to_k[0], to_k[1]) * factor)[:rows].astype(BF16)
        grad_v[i, :, lanes] = jnp.where(kept, to_v[0], to_v[1])[:rows].astype(BF16)
        return carry

    lax.fori_loop(0, n * pairs, attend, 0, unroll=2)
    total = jnp.zeros(flat, F32)
    turned = jnp.swapaxes(normed_1[...].reshape(flat).astype(F32), 0, 1).astype(BF16)
    for k, source in enumerate((grad_q, grad_k, grad_v)):
        loads[k].wait()
        value = source[...].reshape(flat)
        total = total + dot_t(value, w[k])
        grads[k] = dot(turned, value).astype(BF16)
    total = total.reshape(n, rows, width)
    sums = []
    for i in range(n):
        _, unit, inverse = norm_parts(tokens[i].astype(F32), norms[0:1], norms[2:3], None)
        grad_in, scale_grad, bias_grad = norm_back(total[i], unit, inverse, norms[0:1])
        input_grad[i] = (grad_hidden[i] + grad_in).astype(BF16)
        sums.append((scale_grad, bias_grad))
    scale_1, bias_1 = sums[0][0] + sums[1][0], sums[0][1] + sums[1][1]
    line = row_of((128, width), 0)
    spread = jnp.zeros((128, width), F32)
    for j, value in enumerate((scale_1, scale_2, bias_1, bias_2)):
        spread = jnp.where(line == 64 + j, value, spread)
    small_grads[...] = jnp.swapaxes(spread, 0, 1).astype(BF16)
    small_grads[:, :64] = phi_grad.astype(BF16)


def tokens_behind(sizes, length, back, small, weights, tokens, kept, grad_logits, cotangent):
    n, rows, width = tokens.shape
    vmem = pl.BlockSpec(memory_space=pltpu.VMEM)
    shape = jax.ShapeDtypeStruct
    low = pltpu.VMEM(tokens.shape, BF16)
    return pl.pallas_call(
        partial(behind_kernel, sizes, length),
        out_shape=(
            shape((4, width, width), BF16), shape((width, 128), BF16), shape(tokens.shape, BF16)
        ),
        in_specs=[vmem, vmem, pl.BlockSpec(memory_space=pl.ANY)] + [vmem] * 11,
        out_specs=(vmem,) * 3,
        scratch_shapes=[
            pltpu.VMEM(weights.shape, BF16),
            pltpu.VMEM((2, 128, 256), F32),
            pltpu.VMEM(tokens.shape, F32),
            low, low, low, low, low,
            pltpu.SemaphoreType.DMA((4,)),
        ],
        compiler_params=pltpu.CompilerParams(vmem_limit_bytes=VMEM_BYTES),
        name="tokens_behind",
    )(back, small, weights, tokens, *kept, grad_logits, cotangent)


def unpack_kernel(block, summed, attn, phi, scales, biases):
    attn[...] = summed[:, :, :block]
    rest = summed[0][:, 128:]
    phi[...] = pltpu.roll(rest, 64, 1)[:, : phi.shape[1]]
    turned = jnp.swapaxes(rest, 0, 1)
    scales[...] = turned[80:82]
    biases[...] = turned[82:84]


def unpack_grads(summed, block, slot):
    n_k, rows, _ = summed.shape
    vmem = pl.BlockSpec(memory_space=pltpu.VMEM)
    shape = jax.ShapeDtypeStruct
    return pl.pallas_call(
        partial(unpack_kernel, block),
        out_shape=(
            shape((n_k, rows, block), F32), shape((rows, slot), F32),
            shape((2, rows), F32), shape((2, rows), F32),
        ),
        in_specs=[vmem],
        out_specs=(vmem,) * 4,
        name="unpack_grads",
    )(summed)


def normalize(values, scale, shift):
    centered = values - jnp.mean(values, axis=-1, keepdims=True)
    variance = jnp.mean(centered * centered, axis=-1, keepdims=True)
    inverse = lax.rsqrt(variance + epsilon)
    unit_part = centered * inverse
    return (unit_part * scale + shift, unit_part, inverse)


def normalize_back(grad_output, unit_part, inverse, scale):
    scaled = grad_output * scale
    average = jnp.mean(scaled, axis=-1, keepdims=True)
    projection = jnp.mean(scaled * unit_part, axis=-1, keepdims=True)
    grad_input = inverse * (scaled - average - unit_part * projection)
    return (
        grad_input,
        jnp.sum(grad_output * unit_part, axis=(0, 1)),
        jnp.sum(grad_output, axis=(0, 1)),
    )


def to_experts(slots):
    slots = lax.all_to_all(slots, "heads", split_axis=1, concat_axis=0, tiled=True)
    slots = lax.all_to_all(slots, "shard", split_axis=2, concat_axis=0, tiled=True)
    return lax.all_gather(slots, "tensor", axis=0, tiled=True)


def to_images(slots):
    slots = lax.psum_scatter(slots, "tensor", scatter_dimension=0, tiled=True)
    slots = lax.all_to_all(slots, "shard", split_axis=0, concat_axis=2, tiled=True)
    return lax.all_to_all(slots, "heads", split_axis=0, concat_axis=1, tiled=True)


def general_shards(tokens, norm_scales, norm_biases, w_attn, phi, experts, in_bias, out_bias, cotangent):
    heads_n = lax.axis_size("heads")
    group, seq_len, width = tokens.shape
    own = group // heads_n
    heads_index = lax.axis_index("heads")
    tensor_index = lax.axis_index("tensor")
    shard_index = lax.axis_index("shard")
    hidden = experts.shape[3]
    rows = experts.shape[0]
    scales, biases, in_full = (
        lax.all_gather(norm_scales, ROWS, axis=1, tiled=True).astype(F32),
        lax.all_gather(norm_biases, ROWS, axis=1, tiled=True).astype(F32),
        lax.all_gather(in_bias, ROWS, axis=1, tiled=True).astype(F32),
    )
    attn = lax.all_gather(
        lax.all_gather(w_attn, "heads", axis=2, tiled=True), ROWS, axis=1, tiled=True
    )
    phi_full = lax.all_gather(
        lax.all_gather(phi, "heads", axis=1, tiled=True), ROWS, axis=0, tiled=True
    )
    out_rows = lax.all_gather(out_bias, "tensor", axis=1, tiled=True).astype(F32)
    e_own = experts.shape[2] // lax.axis_size("shard")
    in_local = lax.dynamic_slice_in_dim(in_full, tensor_index * hidden, hidden, 1)
    factor = HEAD_DIM ** (-0.5)
    tokens = lax.dynamic_slice_in_dim(tokens, heads_index * own, own, 0)
    cotangent = lax.dynamic_slice_in_dim(cotangent, heads_index * own, own, 0)
    n_heads = width // HEAD_DIM
    inputs = tokens.astype(F32)
    normed_one, unit_one, inverse_one = normalize(inputs, scales[0], biases[0])
    normed_one_b = normed_one.astype(BF16)
    projected = einsum("nsd,kdc->knsc", normed_one_b, attn[:3]).astype(BF16)
    query, keyed, valued = projected.reshape(3, own, seq_len, n_heads, HEAD_DIM)
    scores = einsum("nqhe,nkhe->nhqk", query, keyed) * factor
    score_peak = jnp.max(scores, axis=-1, keepdims=True)
    exponent = jnp.exp(scores - score_peak)
    probs = exponent / jnp.sum(exponent, axis=-1, keepdims=True)
    probs_b = probs.astype(BF16)
    context_b = (
        einsum("nhqk,nkhe->nqhe", probs_b, valued).astype(BF16).reshape(own, seq_len, width)
    )
    hidden_one = inputs + einsum("nsc,dc->nsd", context_b, attn[3])
    normed_two, unit_two, inverse_two = normalize(hidden_one, scales[1], biases[1])
    normed_two_b = normed_two.astype(BF16)
    logits = einsum("nsd,de->nse", normed_two_b, phi_full)
    dispatch = jax.nn.softmax(logits, axis=1)
    dispatch_b = dispatch.astype(BF16)
    combine = jax.nn.softmax(logits, axis=2)
    combine_b = combine.astype(BF16)
    slot_in = to_experts(einsum("nse,nsd->ned", dispatch_b, normed_two_b).astype(BF16))
    share = 1 if e_own else 0

    def meet(partial_sum):
        return lax.psum_scatter(partial_sum, "shard", scatter_dimension=share, tiled=True)

    def spread(values):
        return lax.all_gather(values, "shard", axis=share, tiled=True)

    pre = meet(einsum("ned,def->nef", slot_in, experts[:, 0]))
    if e_own:
        pre = pre + lax.dynamic_slice_in_dim(in_local, shard_index * e_own, e_own, 0)
    else:
        pre = pre + in_local
    gelu_value, gelu_back = jax.vjp(partial(jax.nn.gelu, approximate=False), pre)
    activated = spread(gelu_value.astype(BF16))
    slot_out_part = einsum("nef,def->ned", activated, experts[:, 1])
    slot_out_part = slot_out_part + jnp.where(tensor_index == 0, out_rows, 0.0)
    slot_out = to_images(slot_out_part).astype(BF16)
    output = (hidden_one + einsum("nse,ned->nsd", combine_b, slot_out)).astype(BF16)
    output = lax.all_gather(output, "heads", axis=0, tiled=True)
    grad_combine = einsum("nsd,ned->nse", cotangent, slot_out)
    grad_slot = to_experts(einsum("nse,nsd->ned", combine_b, cotangent).astype(BF16))
    grad_act = meet(einsum("ned,def->nef", grad_slot, experts[:, 1]))
    grad_pre = spread(gelu_back(grad_act)[0].astype(BF16))
    grad_slot_in = einsum("nef,def->ned", grad_pre, experts[:, 0]).astype(BF16)
    input_term = einsum("ned,nef->def", slot_in, grad_pre)
    output_term = einsum("ned,nef->def", grad_slot, activated)
    experts_grad = jnp.stack((input_term, output_term), axis=1)
    grad_slot_in = to_images(grad_slot_in.astype(F32)).astype(BF16)
    in_bias_grad = lax.dynamic_slice_in_dim(
        lax.all_gather(jnp.sum(grad_pre.astype(F32), axis=0), "tensor", axis=1, tiled=True),
        (shard_index * lax.axis_size("tensor") + tensor_index) * in_bias.shape[1],
        in_bias.shape[1],
        1,
    )
    out_bias_grad = lax.dynamic_slice_in_dim(
        jnp.sum(grad_slot.astype(F32), axis=0),
        tensor_index * out_bias.shape[1],
        out_bias.shape[1],
        1,
    )
    grad_dispatch = einsum("nsd,ned->nse", normed_two_b, grad_slot_in)
    grad_logits = (
        dispatch * (grad_dispatch - jnp.sum(dispatch * grad_dispatch, axis=1, keepdims=True))
        + combine * (grad_combine - jnp.sum(combine * grad_combine, axis=2, keepdims=True))
    ).astype(BF16)
    phi_grad = einsum("nsd,nse->de", normed_two_b, grad_logits)
    grad_normed_two = einsum("nse,ned->nsd", dispatch_b, grad_slot_in) + einsum(
        "nse,de->nsd", grad_logits, phi_full
    )
    grad_hidden_norm, scale_two_grad, bias_two_grad = normalize_back(
        grad_normed_two, unit_two, inverse_two, scales[1]
    )
    grad_hidden = cotangent.astype(F32) + grad_hidden_norm
    grad_hidden_b = grad_hidden.astype(BF16)
    out_weight_grad = einsum("nsd,nsc->dc", grad_hidden_b, context_b)
    grad_context = einsum("nsd,dc->nsc", grad_hidden_b, attn[3]).astype(BF16)
    grad_context = grad_context.reshape(own, seq_len, n_heads, HEAD_DIM)
    grad_value = einsum("nhqk,nqhe->nkhe", probs_b, grad_context).astype(BF16)
    grad_probs = einsum("nqhe,nkhe->nhqk", grad_context, valued)
    grad_scores = (
        probs * (grad_probs - jnp.sum(probs * grad_probs, axis=-1, keepdims=True))
    ).astype(BF16)
    grad_query = (einsum("nhqk,nkhe->nqhe", grad_scores, keyed) * factor).astype(BF16)
    grad_key = (einsum("nhqk,nqhe->nkhe", grad_scores, query) * factor).astype(BF16)
    grad_proj = jnp.stack((grad_query, grad_key, grad_value)).reshape(3, own, seq_len, width)
    proj_grad = einsum("nsd,knsc->kdc", normed_one_b, grad_proj)
    grad_normed_one = einsum("knsc,kdc->nsd", grad_proj, attn[:3])
    grad_input_norm, scale_one_grad, bias_one_grad = normalize_back(
        grad_normed_one, unit_one, inverse_one, scales[0]
    )
    input_grad = (grad_hidden + grad_input_norm).astype(BF16)
    input_grad = lax.all_gather(input_grad, "heads", axis=0, tiled=True)
    attn_grad = jnp.concatenate((proj_grad, out_weight_grad[None]), axis=0)
    attn_grad = lax.psum_scatter(attn_grad, ROWS, scatter_dimension=1, tiled=True)
    attn_grad = lax.psum_scatter(attn_grad, "heads", scatter_dimension=2, tiled=True)
    phi_grad = lax.psum_scatter(phi_grad, ROWS, scatter_dimension=0, tiled=True)
    phi_grad = lax.psum_scatter(phi_grad, "heads", scatter_dimension=1, tiled=True)
    norms = jnp.stack((scale_one_grad, scale_two_grad, bias_one_grad, bias_two_grad))
    norms = lax.psum(lax.psum_scatter(norms, ROWS, scatter_dimension=1, tiled=True), "heads")
    return (
        output,
        input_grad,
        norms[:2],
        norms[2:],
        attn_grad,
        phi_grad,
        experts_grad,
        in_bias_grad,
        out_bias_grad,
    )


def shards(tokens, norm_scales, norm_biases, w_attn, phi, experts, in_bias, out_bias, cotangent):
    arrays = (tokens, norm_scales, norm_biases, w_attn, phi, experts, in_bias, out_bias, cotangent)
    sizes = tuple(lax.axis_size(name) for name in ("shard", "heads", "tensor"))
    group, length, width = tokens.shape
    fits = (sizes, group, width, *experts.shape[:3]) == ((4, 4, 2), 8, 768, 192, 2, 16)
    if not fits or not 192 < length <= 208 or in_bias.shape[1] != 384:
        return general_shards(*arrays)
    n_s, n_h, n_t = sizes
    block, slot = w_attn.shape[2], phi.shape[1]
    tokens, cotangent = (
        values.transpose(1, 0, 2).reshape(group * length, width) for values in (tokens, cotangent)
    )
    attn, small, turned, tokens, cotangent = gather_weights(
        sizes, w_attn, phi.T, out_bias, norm_scales, norm_biases, in_bias, experts, tokens, cotangent
    )
    blocks, *kept, combine = tokens_ahead(sizes, length, tokens, small, attn)
    hidden = kept[5]
    slot_in, activated, gate, back = expert_pass(sizes, False, blocks, turned, small)
    output, blocks, grad_logits = tokens_middle(sizes, back, small, combine, hidden, cotangent)
    grad_slot, grad_pre, back, in_bias_grad, out_sum, output = expert_pass(
        sizes, True, blocks, turned, gate, output, in_bias.shape[1]
    )
    attn_grad, small_grad, input_grad = tokens_behind(
        sizes, length, back, small, attn, tokens, kept, grad_logits, cotangent
    )
    input_grad = lax.all_gather(input_grad, "heads", axis=0, tiled=True)
    attn_grad, grad_pre = lax.optimization_barrier((attn_grad, grad_pre))
    experts_grad = weight_grads(slot_in, grad_pre, grad_slot, activated)
    output = output[:, :length].transpose(1, 0, 2)
    out_bias_grad = lax.dynamic_slice_in_dim(
        out_sum, lax.axis_index("tensor") * out_bias.shape[1], out_bias.shape[1], 1
    )
    attn_grad, experts_grad, output, out_bias_grad = lax.optimization_barrier(
        (attn_grad, experts_grad, output, out_bias_grad)
    )
    summed = reduce_grads(sizes, attn_grad, small_grad)
    attn_grad, phi_grad, scales_grad, biases_grad = unpack_grads(summed, block, slot)
    return (
        output.transpose(1, 0, 2),
        input_grad[:, :length],
        scales_grad,
        biases_grad,
        attn_grad,
        phi_grad,
        experts_grad,
        in_bias_grad,
        out_bias_grad,
    )


def solution(mesh):
    images = P(ROWS, None, None)
    return jax.shard_map(
        shards,
        mesh=mesh,
        in_specs=(
            images,
            P(None, ROWS),
            P(None, ROWS),
            P(None, ROWS, "heads"),
            P(ROWS, "heads"),
            P("shard", None, "heads", "tensor"),
            P("heads", ROWS),
            P("heads", ROWS),
            images,
        ),
        out_specs=(
            images,
            images,
            P(None, ROWS),
            P(None, ROWS),
            P(None, ROWS, "heads"),
            P(ROWS, "heads"),
            P("shard", None, "heads", "tensor"),
            P("heads", ROWS),
            P("heads", ROWS),
        ),
        check_vma=False,
    )
```

```python
from functools import partial

import jax
import jax.numpy as jnp
from jax import lax
from jax.experimental import pallas as pl
from jax.experimental.pallas import tpu as pltpu
from jax.sharding import PartitionSpec as P

HEAD_DIM = 64
F32 = jnp.float32
BF16 = jnp.bfloat16
ROWS = ("shard", "tensor")
MESH = pl.DeviceIdType.MESH
VMEM_BYTES = 58 * 1024 * 1024
epsilon = 1e-06
einsum = partial(jnp.einsum, preferred_element_type=F32)


def dot(a, b):
    return lax.dot_general(a, b, (((1,), (0,)), ((), ())), preferred_element_type=F32)


def dot_t(a, b):
    return lax.dot_general(a, b, (((1,), (1,)), ((), ())), preferred_element_type=F32)


def swap_matrix(n):
    out = lax.broadcasted_iota(jnp.int32, (n * n, n * n), 0)
    row = lax.broadcasted_iota(jnp.int32, (n * n, n * n), 1)
    return ((out // n == row % n) & (out % n == row // n)).astype(F32).astype(BF16)


class Peers:
    def __init__(self, sizes):
        self.sizes = sizes
        self.at = tuple(lax.axis_index(name) for name in ("shard", "heads", "tensor"))
        self.count = sizes[0] * sizes[1] * sizes[2]

    def flat(self, place):
        return (place[0] * self.sizes[1] + place[1]) * self.sizes[2] + place[2]

    def step(self, k, sign):
        _, n_h, n_t = self.sizes
        steps = (k // (n_h * n_t), (k // n_t) % n_h, k % n_t)
        return tuple(
            lax.rem(at + n + sign * d, n) for at, n, d in zip(self.at, self.sizes, steps)
        )

    def greet_all(self):
        barrier = pltpu.get_barrier_semaphore()

        def signal(k, carry):
            pl.semaphore_signal(barrier, inc=1, device_id=self.step(k, 1), device_id_type=MESH)
            return carry

        lax.fori_loop(1, self.count, signal, 0)
        pl.semaphore_wait(barrier, self.count - 1)


def remote(src, dst, send, recv, place):
    return pltpu.make_async_remote_copy(
        src_ref=src, dst_ref=dst, send_sem=send, recv_sem=recv, device_id=place, device_id_type=MESH
    )


def plane(sizes):
    n_s, n_h, n_t = sizes
    s, h, t = (lax.axis_index(name) for name in ("shard", "heads", "tensor"))
    core, chip = lax.rem(s, 2), s // 2
    sibling = (s + 1 - 2 * core, h, t)
    across_x = (lax.rem(s + 2, n_s), h, t)
    across_y = (s, h, 1 - t)
    line = [(s, lax.rem(h + d, n_h), t) for d in range(n_h)]
    barrier = pltpu.get_barrier_semaphore()
    others = [sibling, across_x, across_y] + line[1:]
    for place in others:
        pl.semaphore_signal(barrier, inc=1, device_id=place, device_id_type=MESH)
    pl.semaphore_wait(barrier, len(others))
    return (s, h, t), core, chip, sibling, across_x, across_y, line


def pair_matrix(block, wide, transposed):
    shape = (2 * block, 2 * wide) if transposed else (2 * wide, 2 * block)
    tight = lax.broadcasted_iota(jnp.int32, shape, 0 if transposed else 1)
    padded = lax.broadcasted_iota(jnp.int32, shape, 1 if transposed else 0)
    second = padded >= wide
    lane = jnp.where(second, padded - wide, padded)
    same = (lane < block) & (tight == jnp.where(second, lane + block, lane))
    return same.astype(F32).astype(BF16)


def gather_kernel(
    sizes, w_attn, phi_t, out_bias, scales, biases, in_bias, experts, tokens, cotangent, w_out, small_out, turned, own_tokens, own_cot,
    w, small, lined, extra, stage, tile_in, tile_out, images, picked,
    z_send, z_recv, x_sems, y_sems, d_sems, c_sems, t_sems, o_sems, i_sems,
):
    n_k, rows, block = w_attn.shape
    wide = lined.shape[3]
    slot = phi_t.shape[0]
    own_h = lax.axis_index("heads")
    stage[...] = jnp.zeros_like(stage)
    stage[64 : 64 + slot] = phi_t[...].astype(F32)
    stage[64 + slot : 64 + 2 * slot] = out_bias[...].astype(F32)
    lined[own_h, :, :, 128:] = jnp.zeros((n_k, rows, wide - 128), BF16)
    lined[own_h, :, :, :block] = w_attn[...]
    first = lined[own_h, 0, :, 128:].astype(F32) + jnp.swapaxes(stage[...], 0, 1)
    lined[own_h, 0, :, 128:] = first.astype(BF16)
    (s, h, t), core, chip, sibling, across_x, across_y, line = plane(sizes)
    n_h, n_t = sizes[1], sizes[2]
    width = w.shape[2]
    side = 16
    n_tiles = experts.shape[0] // side
    depth = tile_in.shape[0]
    halves = ((0, rows // 2), (rows // 2, rows // 2))

    def z_hop(k, origin, up):
        place = line[1] if up else line[n_h - 1]
        return remote(
            lined.at[origin, k], lined.at[origin, k],
            z_send.at[k, origin, up], z_recv.at[k, origin], place,
        )

    def relay(k, d):
        @pl.when(h >= d)
        def _():
            z_hop(k, h - d, 1).wait_recv()

            @pl.when(h < n_h - 1)
            def _():
                z_hop(k, h - d, 1).start()

        @pl.when(h + d < n_h)
        def _():
            z_hop(k, h + d, 0).wait_recv()

            @pl.when(h > 0)
            def _():
                z_hop(k, h + d, 0).start()

    chunks = (0, 2, 1, 3)
    for k in chunks:
        @pl.when(h < n_h - 1)
        def _():
            z_hop(k, h, 1).start()

        @pl.when(h > 0)
        def _():
            z_hop(k, h, 0).start()

    def load(i):
        return pltpu.make_async_copy(
            experts.at[pl.ds((i % n_tiles) * side, side), i // n_tiles],
            tile_in.at[i % depth],
            t_sems.at[0, i % depth],
        )

    def store(i):
        return pltpu.make_async_copy(
            tile_out.at[i % depth],
            turned.at[i // n_tiles, :, pl.ds((i % n_tiles) * side, side)],
            t_sems.at[1, i % depth],
        )

    image_loads = [
        pltpu.make_async_copy(source, images.at[j], i_sems.at[0, j])
        for j, source in enumerate((tokens, cotangent))
    ]
    for i in range(depth - 1):
        load(i).start()
    for copy in image_loads:
        copy.start()
    swap = swap_matrix(side)
    done = [0]

    def turn(count):
        def step(i, carry):
            load(i).wait()

            @pl.when(i + depth - 1 < 2 * n_tiles)
            def _():
                load(i + depth - 1).start()

            @pl.when(i >= depth)
            def _():
                store(i - depth).wait()

            rows_in = tile_in[i % depth].reshape(side * side, tile_in.shape[3])
            tile_out[i % depth] = dot(swap, rows_in).astype(BF16).reshape(tile_out.shape[1:])
            store(i).start()
            return carry

        last = min(done[0] + count, 2 * n_tiles)
        lax.fori_loop(done[0], last, step, 0)
        done[0] = last

    pair = pair_matrix(block, wide, False)
    shape = (n_h * wide, small.shape[1])
    row = lax.broadcasted_iota(jnp.int32, shape, 0)
    column = lax.broadcasted_iota(jnp.int32, shape, 1)
    lane, of = row % wide - block, row // wide
    beside = (lane >= 0) & (lane < 16) & (column == of * 16 + lane)
    beside |= (lane >= 16) & (lane < 32) & (column == n_h * 16 + of * 16 + lane - 16)
    beside = beside.astype(F32).astype(BF16)

    stage[...] = jnp.zeros_like(stage)
    stage[64:66] = scales[...].astype(F32)
    stage[66:68] = biases[...].astype(F32)
    norms = jnp.swapaxes(stage[...], 0, 1)
    pieces = []
    for j in range(in_bias.shape[1] // 64):
        shape = (in_bias.shape[1], 128)
        row = lax.broadcasted_iota(jnp.int32, shape, 0)
        column = lax.broadcasted_iota(jnp.int32, shape, 1)
        chosen = ((row == 64 * j + column) & (column < 64)).astype(F32).astype(BF16)
        pieces.append(dot(in_bias[...], chosen))
    extra[:, :128] = jnp.zeros((rows, 128), F32)
    extra[:, 128:] = jnp.concatenate(pieces, axis=0) + norms

    image_stores = [
        pltpu.make_async_copy(picked.at[j], target, i_sems.at[1, j])
        for j, target in enumerate((own_tokens, own_cot))
    ]

    def pick_images(j):
        own, padded = picked.shape[1:3]
        group = own * n_h
        lines = images.shape[1]
        image_loads[j].wait()
        step = 256 // group
        for first in range(0, padded, step):
            count = min(step, padded - first)
            taken = min(step * group, lines - first * group)
            shape = (own * count, taken)
            row = lax.broadcasted_iota(jnp.int32, shape, 0)
            column = lax.broadcasted_iota(jnp.int32, shape, 1)
            wanted = (row % count) * group + own * h + row // count
            chosen = (column == wanted).astype(F32).astype(BF16)
            source = images[j, first * group : first * group + taken]
            picked[j, :, first : first + count] = (
                dot(chosen, source).astype(BF16).reshape(own, count, images.shape[2])
            )
        image_stores[j].start()

    def at(k, place):
        first = pl.multiple_of((place[0] * n_t + place[2]) * rows, 16)
        lines = pl.ds(first, rows)
        return small.at[lines] if k == n_k else w.at[k, lines]

    def hop(q, origin, place, sems, j):
        return remote(at(q, origin), at(q, origin), sems.at[0, j], sems.at[1, j], place)

    def half_hop(q, origin, place, half):
        part = at(q, origin).at[pl.ds(*halves[half])]
        j = 2 * q + half
        return remote(part, part, d_sems.at[0, j], d_sems.at[1, j], place)

    me = (s, h, t)
    from_d = (across_x[0], h, across_y[2])
    sent = []

    def send(copy):
        copy.start()
        sent.append(copy)

    def assemble(k):
        for i in range(0, n_h, 2):
            lines = jnp.concatenate([lined[i, k], lined[i + 1, k]], axis=1)
            at(k, me)[:, i * block : (i + 2) * block] = dot(lines, pair).astype(BF16)
        if k == 0:
            lines = jnp.concatenate([lined[i, k] for i in range(n_h)], axis=1)
            at(n_k, me)[...] = (dot(lines, beside) + extra[...]).astype(BF16)
        for q in members(k):
            send(hop(q, me, across_x, x_sems, q))
            send(hop(q, me, across_y, y_sems, q))
            send(hop(q, me, sibling, c_sems, 4 * q))

    def members(k):
        return (0, n_k) if k == 0 else (k,)

    def relay_xy(k):
        for q in members(k):
            hop(q, across_x, across_x, x_sems, q).wait_recv()
            send(half_hop(q, across_x, across_y, 0))
            send(hop(q, across_x, sibling, c_sems, 4 * q + 1))
            hop(q, across_y, across_y, y_sems, q).wait_recv()
            send(half_hop(q, across_y, across_x, 1))
            send(hop(q, across_y, sibling, c_sems, 4 * q + 2))

    def relay_d(k):
        for q in members(k):
            half_hop(q, from_d, across_y, 0).wait_recv()
            half_hop(q, from_d, across_x, 1).wait_recv()
            send(hop(q, from_d, sibling, c_sems, 4 * q + 3))

    for wave in range(n_k + n_h - 2):
        for d in range(1, n_h):
            if 0 <= wave - d + 1 < n_k:
                relay(chunks[wave - d + 1], d)
        turn(2)
        i = wave - n_h + 2
        if i >= 0:
            assemble(chunks[i])
            if i in (1, 2):
                pick_images(i - 1)
            if i >= 1:
                relay_xy(chunks[i - 1])
            if i >= 2:
                relay_d(chunks[i - 2])
            turn(2)
    relay_xy(chunks[-1])
    relay_d(chunks[-2])
    turn(2 * n_tiles)
    relay_d(chunks[-1])
    stores = []
    for k in chunks:
        for q in members(k):
            for j in range(4):
                hop(q, me, sibling, c_sems, 4 * q + j).wait_recv()
            if q == n_k:
                stores.append(pltpu.make_async_copy(small, small_out, o_sems.at[q]))
            else:
                stores.append(pltpu.make_async_copy(w.at[q], w_out.at[q], o_sems.at[q]))
            stores[-1].start()
    for copy in sent:
        copy.wait_send()
    for origin in range(n_h):
        @pl.when((origin <= h) & (h < n_h - 1))
        def _():
            for k in range(n_k):
                z_hop(k, origin, 1).wait_send()

        @pl.when((origin >= h) & (h > 0))
        def _():
            for k in range(n_k):
                z_hop(k, origin, 0).wait_send()

    for i in range(depth):
        store(2 * n_tiles - depth + i).wait()
    for copy in image_stores:
        copy.wait()
    for copy in stores:
        copy.wait()


def gather_weights(
    sizes, w_attn, phi_t, out_bias, scales, biases, in_bias, experts, tokens, cotangent
):
    n_k, rows, _ = w_attn.shape
    wide = 256
    n_s, n_h, n_t = sizes
    width = n_s * n_t * rows
    vmem = pl.BlockSpec(memory_space=pltpu.VMEM)
    hbm = pl.BlockSpec(memory_space=pl.ANY)
    dma = pltpu.SemaphoreType.DMA
    hidden = experts.shape[3]
    small = (width, wide)
    images = jax.ShapeDtypeStruct((2, 208, width), BF16)
    return pl.pallas_call(
        partial(gather_kernel, sizes),
        out_shape=(
            jax.ShapeDtypeStruct((n_k, width, width), BF16),
            jax.ShapeDtypeStruct(small, BF16),
            jax.ShapeDtypeStruct((2, experts.shape[2], experts.shape[0], hidden), BF16),
            images, images,
        ),
        in_specs=[vmem] * 6 + [hbm] * 3,
        out_specs=(hbm,) * 5,
        scratch_shapes=[
            pltpu.VMEM((n_k, width, width), BF16),
            pltpu.VMEM(small, BF16),
            pltpu.VMEM((n_h, n_k, rows, wide), BF16),
            pltpu.VMEM((rows, wide), F32),
            pltpu.VMEM((128, rows), F32),
            pltpu.VMEM((4, 16, 16, hidden), BF16),
            pltpu.VMEM((4, 16, 16, hidden), BF16),
            pltpu.VMEM((2, *tokens.shape), BF16),
            pltpu.VMEM((2, *images.shape), BF16),
            dma((n_k, n_h, 2)), dma((n_k, n_h)), dma((2, n_k + 1)), dma((2, n_k + 1)),
            dma((2, 2 * (n_k + 1))), dma((2, 4 * (n_k + 1))), dma((2, 4)), dma((n_k + 1,)),
            dma((2, 2)),
        ],
        compiler_params=pltpu.CompilerParams(
            collective_id=3, has_side_effects=True, vmem_limit_bytes=VMEM_BYTES
        ),
        name="gather_weights",
    )(w_attn, phi_t, out_bias, scales, biases, in_bias, experts, tokens, cotangent)


def reduce_kernel(
    sizes, grads, small, out, core_in, core_small, met, met_small,
    d_in, d_small, x_in, x_small, y_in, y_small, pieces, z_in,
    c_sems, d_sems, x_sems, y_sems, z_send, z_recv,
):
    (s, h, t), core, chip, sibling, across_x, across_y, line = plane(sizes)
    n_k, width, _ = grads.shape
    n_s, n_h, n_t = sizes
    rows = width // (n_s * n_t)
    wide = pieces.shape[3]
    pair = n_t * rows
    half = rows // 2
    halves = (pl.ds(0, half), pl.ds(half, half))
    chunks = (0, 2, 1, 3)

    def members(k):
        return (0, n_k) if k == 0 else (k,)

    def pick(q, large, little):
        return little if q == n_k else large.at[q]

    def core_copy(q, x):
        first = pl.multiple_of((2 * x + 1 - core) * pair, 16)
        return remote(
            pick(q, grads, small).at[pl.ds(first, pair)],
            pick(q, core_in, core_small).at[x],
            c_sems.at[0, 2 * q + x], c_sems.at[1, 2 * q + x], sibling,
        )

    for k in chunks:
        for q in members(k):
            for x in range(2):
                core_copy(q, x).start()
    joined = pair_matrix(width // n_h, wide, True)
    shape = (small.shape[1], n_h * wide)
    row = lax.broadcasted_iota(jnp.int32, shape, 0)
    column = lax.broadcasted_iota(jnp.int32, shape, 1)
    lane, of = column % wide - width // n_h, column // wide
    beside = (lane >= 0) & (lane < 16) & (row == of * 16 + lane)
    beside |= (lane >= 16) & (lane < 20) & (row == n_h * 16 + lane - 16)
    beside = beside.astype(F32).astype(BF16)
    to_d, to_x, to_y = (d_in, d_small), (x_in, x_small), (y_in, y_small)
    sent = []

    def hop(q, kind, part, source, place):
        sems = {id(to_d): d_sems, id(to_x): x_sems, id(to_y): y_sems}[id(kind)]
        target = pick(q, *kind)
        target = target.at[part] if kind is to_d else target.at[halves[part]]
        j = 2 * q + part
        return remote(source, target, sems.at[0, j], sems.at[1, j], place)

    def send(copy):
        copy.start()
        sent.append(copy)

    def part_of(q, x, y, part):
        return pick(q, met, met_small).at[x, y].at[halves[part]]

    def arrived(q, kind, part):
        hop(q, kind, part, part_of(q, 0, 0, part), sibling).wait_recv()

    def open_up(q):
        part = pick(q, met, met_small)
        for x in range(2):
            core_copy(q, x).wait_recv()
            first = pl.multiple_of((2 * x + core) * pair, 16)
            own = pick(q, grads, small)[pl.ds(first, pair)].astype(F32)
            total = own + pick(q, core_in, core_small)[x].astype(F32)
            part[x] = total.astype(BF16).reshape(n_t, rows, total.shape[1])
        send(hop(q, to_d, 0, part_of(q, 1 - chip, 1 - t, 0), across_x))
        send(hop(q, to_d, 1, part_of(q, 1 - chip, 1 - t, 1), across_y))
        send(hop(q, to_x, 0, part_of(q, 1 - chip, t, 0), across_x))
        send(hop(q, to_y, 1, part_of(q, chip, 1 - t, 1), across_y))

    def pass_on(q):
        for part, kind, x, y, place in (
            (0, to_y, chip, 1 - t, across_y),
            (1, to_x, 1 - chip, t, across_x),
        ):
            arrived(q, to_d, part)
            block = part_of(q, x, y, part)
            total = block[...].astype(F32) + pick(q, *to_d)[part].astype(F32)
            block[...] = total.astype(BF16)
            send(hop(q, kind, part, block, place))

    def whole(q):
        for kind in (to_x, to_y):
            for part in range(2):
                arrived(q, kind, part)
        total = pick(q, met, met_small)[chip, t].astype(F32) + pick(q, *to_x)[...].astype(F32)
        return (total + pick(q, *to_y)[...].astype(F32)).astype(BF16)

    def z_copy(k, target, up):
        place = line[1] if up else line[n_h - 1]
        return remote(
            pieces.at[target, k], z_in.at[up, target, k],
            z_send.at[up, target, k], z_recv.at[up, target, k], place,
        )

    def pass_along(k, hops):
        for up in range(2):
            for target in range(n_h - 1, -1, -1) if up else range(n_h):
                further = target > h if up else target < h

                @pl.when(further & (h == (hops if up else n_h - 1 - hops)))
                def _():
                    if hops > 0:
                        z_copy(k, target, up).wait_recv()
                        total = pieces[target, k].astype(F32) + z_in[up, target, k].astype(F32)
                        pieces[target, k] = total.astype(BF16)
                    z_copy(k, target, up).start()

    def share_out(k):
        value = whole(k)
        columns = width // n_h
        if k == 0:
            little = dot(whole(n_k), beside)
        for i in range(0, n_h, 2):
            lanes = dot(value[:, i * columns : (i + 2) * columns], joined)
            if k == 0:
                lanes = lanes + little[:, i * wide : (i + 2) * wide]
            pieces[i, k] = lanes[:, :wide].astype(BF16)
            pieces[i + 1, k] = lanes[:, wide:].astype(BF16)
        pass_along(k, 0)

    for i in range(n_k + 2 + n_h - 2):
        if i < n_k:
            for q in members(chunks[i]):
                open_up(q)
        if 0 <= i - 1 < n_k:
            for q in members(chunks[i - 1]):
                pass_on(q)
        if 0 <= i - 2 < n_k:
            share_out(chunks[i - 2])
        for hops in range(1, n_h - 1):
            if 0 <= i - 2 - hops < n_k:
                pass_along(chunks[i - 2 - hops], hops)
    for k in chunks:
        out[k] = pieces[h, k].astype(F32)
        for up, there in ((1, h > 0), (0, h < n_h - 1)):
            @pl.when(there)
            def _():
                z_copy(k, h, up).wait_recv()
                out[k] = out[k] + z_in[up, h, k].astype(F32)

    for k in chunks:
        for q in members(k):
            for x in range(2):
                core_copy(q, x).wait_send()
    for copy in sent:
        copy.wait_send()
    for target in range(n_h):
        for up in range(2):
            @pl.when(target > h if up else target < h)
            def _():
                for k in range(n_k):
                    z_copy(k, target, up).wait_send()


def reduce_grads(sizes, grads, small):
    n_k, width, _ = grads.shape
    n_s, n_h, n_t = sizes
    rows, wide, thin = width // (n_s * n_t), 256, small.shape[1]
    vmem = pl.BlockSpec(memory_space=pltpu.VMEM)
    dma = pltpu.SemaphoreType.DMA

    def buffers(*lead):
        return [
            pltpu.VMEM((n_k, *lead, width), BF16),
            pltpu.VMEM((*lead, thin), BF16),
        ]

    return pl.pallas_call(
        partial(reduce_kernel, sizes),
        out_shape=jax.ShapeDtypeStruct((n_k, rows, wide), F32),
        in_specs=[vmem, vmem],
        out_specs=vmem,
        scratch_shapes=[
            *buffers(2, n_t * rows), *buffers(2, n_t, rows),
            *buffers(2, rows // 2), *buffers(rows), *buffers(rows),
            pltpu.VMEM((n_h, n_k, rows, wide), BF16),
            pltpu.VMEM((2, n_h, n_k, rows, wide), BF16),
            dma((2, 2 * (n_k + 1))), dma((2, 2 * (n_k + 1))), dma((2, 2 * (n_k + 1))),
            dma((2, 2 * (n_k + 1))), dma((2, n_h, n_k)), dma((2, n_h, n_k)),
        ],
        compiler_params=pltpu.CompilerParams(
            collective_id=4, has_side_effects=True, vmem_limit_bytes=VMEM_BYTES
        ),
        name="reduce_grads",
    )(grads, small)


def expert_kernel(sizes, backward, *refs):
    if backward:
        (blocks, weights, gate, output, slots_out, act_out, back_out, bias_out, sum_out, gathered,
         w_a, w_b, gate_v, sums, slots, act, core_out, core_in, x_out, x_in, land, leave, back, land_back,
         w_sem, o_sem, in_sems, back_sems, core_sems, x_sems, act_sems, b_sems,
         g_send, g_recv, g_sem,
         bias_all, bias_send, bias_land) = refs
    else:
        (blocks, weights, gate, slots_out, act_out, gate_out, back_out,
         w_a, w_b, sums, slots, act, core_out, core_in, x_out, x_in, land, leave, back, land_back,
         w_sem, o_sem, in_sems, back_sems, core_sems, x_sems, act_sems, bias) = refs
    peers = Peers(sizes)
    s, h, t = peers.at
    n_s, n_h, n_t = sizes
    me = peers.flat(peers.at)
    core, chip = lax.rem(s, 2), s // 2
    sibling = (s + 1 - 2 * core, h, t)
    across = (lax.rem(s + 2, n_s), h, t)
    half = act.shape[0] // 2
    own, other = core * half, (1 - core) * half
    n_blocks = peers.count
    first = 1 if backward else 0
    loads = [
        pltpu.make_async_copy(weights.at[first], w_a, w_sem.at[0]),
        pltpu.make_async_copy(weights.at[1 - first], w_b, w_sem.at[1]),
    ]
    for load in loads:
        load.start()
    if backward:
        gate_load = pltpu.make_async_copy(gate, gate_v, o_sem.at[0])
        gate_load.start()
    peers.greet_all()

    def block_out(p, k):
        place = peers.step(k, 1)
        return remote(
            blocks.at[place[1], place[0], p], land.at[p, me],
            in_sems.at[0, p, k], in_sems.at[1, p, k], place,
        )

    def block_in(p, k):
        source = peers.flat(peers.step(k, -1))
        return remote(
            blocks.at[0, 0, p], land.at[p, source], in_sems.at[0, p, k], in_sems.at[1, p, k], sibling
        )

    def each(function, count=n_blocks, start=1):
        lax.fori_loop(start, count, lambda k, carry: (function(k), carry)[1], 0)

    for p in range(2):
        for k in range(1, n_blocks):
            block_out(p, k).start()
        land[p, me] = blocks[h, s, p]
    few = half // 2
    group = 16
    many = 2 * group
    out_row = lax.broadcasted_iota(jnp.int32, (16 * group, 16 * group), 0)
    in_row = lax.broadcasted_iota(jnp.int32, (16 * group, 16 * group), 1)
    there = (out_row // many == in_row % (2 * few)) & (out_row % many == in_row // (2 * few))
    there = there.astype(F32).astype(BF16)
    again = (in_row // many == out_row % (2 * few)) & (in_row % many == out_row // (2 * few))
    again = again.astype(F32).astype(BF16)

    def receive(p):
        each(lambda k: block_in(p, k).wait_recv())
        for b in range(n_blocks // group):
            rows = land[p, b * group : (b + 1) * group].reshape(group * 16, land.shape[3])
            turned = dot(there, rows).astype(BF16).reshape(2 * few, many, land.shape[3])
            for c in range(2):
                first = c * half + p * few
                slots[first : first + few, b * many : (b + 1) * many, :] = turned[
                    c * few : (c + 1) * few
                ]

    if backward:
        own_images = output.shape[0]
        line = [(s, lax.rem(h + d, n_h), t) for d in range(n_h)]
        g_own = pltpu.make_async_copy(output, gathered.at[pl.ds(h * own_images, own_images)], g_sem)
        g_own.start()

        def z_hop(i, origin, up, source=None):
            there = gathered.at[origin * own_images + i]
            return remote(
                there if source is None else source, there,
                g_send.at[i, origin, up], g_recv.at[i, origin], line[1] if up else line[n_h - 1],
            )

        def relay(i, d):
            @pl.when(h >= d)
            def _():
                z_hop(i, h - d, 1).wait_recv()

                @pl.when((h < n_h - 1) & (d < n_h - 1))
                def _():
                    z_hop(i, h - d, 1).start()

            @pl.when(h + d < n_h)
            def _():
                z_hop(i, h + d, 0).wait_recv()

                @pl.when((h > 0) & (d < n_h - 1))
                def _():
                    z_hop(i, h + d, 0).start()

        def gather_output():
            for i in range(own_images):
                @pl.when(h < n_h - 1)
                def _():
                    z_hop(i, h, 1, output.at[i]).start()

                @pl.when(h > 0)
                def _():
                    z_hop(i, h, 0, output.at[i]).start()
    else:
        piece, count = 6 * 64, act.shape[2] // (6 * 64)
        row = lax.broadcasted_iota(jnp.int32, (6 * 128, piece), 0)
        column = lax.broadcasted_iota(jnp.int32, (6 * 128, piece), 1)
        lane = row % 128
        place = (lane < 64) & (column == (row // 128) * 64 + lane)
        place = place.astype(F32).astype(BF16)
        for m in range(count):
            first = (t * count + m) * 96
            lines = [
                gate[pl.ds(pl.multiple_of(first + j * 16, 16), 16), 128:256] for j in range(6)
            ]
            bias[:, m * piece : (m + 1) * piece] = dot(jnp.concatenate(lines, axis=1), place)

    receive(0)
    if backward:
        gather_output()
    loads[0].wait()

    def core_copy(j):
        return remote(
            core_out.at[j], core_in.at[j], core_sems.at[0, j], core_sems.at[1, j], sibling
        )

    def x_copy(j):
        return remote(x_out.at[j], x_in.at[j], x_sems.at[0, j], x_sems.at[1, j], across)

    def act_copy(j):
        return remote(
            act.at[own + j], act.at[own + j], act_sems.at[0, j], act_sems.at[1, j], sibling
        )

    def act_in(j):
        return remote(
            act.at[other + j], act.at[other + j], act_sems.at[0, j], act_sems.at[1, j], sibling
        )

    def meet(j):
        core_copy(j).wait_recv()
        sums[j] = sums[j] + core_in[j].astype(F32)
        x_out[j] = sums[j].astype(BF16)
        x_copy(j).start()

    def first_sums(j):
        core_out[j] = dot(slots[other + j], w_a[other + j]).astype(BF16)
        core_copy(j).start()

        @pl.when(j > 0)
        def _():
            meet(j - 1)

        sums[j] = dot(slots[own + j], w_a[own + j])

    each(first_sums, few, 0)
    receive(1)
    each(first_sums, half, few)
    meet(half - 1)
    loads[1].wait()
    if backward:
        gate_load.wait()

    def second(e):
        leave[e] = dot_t(act[e], w_b[e]).astype(BF16)

    def finish(j):
        x_copy(j).wait_recv()
        value = sums[j] + x_in[j].astype(F32)
        if backward:
            act[own + j] = (value * gate_v[j]).astype(BF16)
        else:
            value = value + bias[pl.ds(own + j, 1), :]
            cumulative = 0.5 + 0.5 * lax.erf(value * 0.7071067811865476)
            act[own + j] = (value * cumulative).astype(BF16)
            sums[j] = cumulative + value * (
                jnp.exp(value * value * -0.5) * 0.3989422804014327
            )
        act_copy(j).start()
        second(own + j)

        @pl.when(j > 0)
        def _():
            act_in(j - 1).wait_recv()
            second(other + j - 1)

        if backward:
            for when, i, d in ((2, 0, 1), (3, 1, 1), (5, 0, 2), (7, 1, 2)):
                @pl.when(j == when)
                def _():
                    relay(i, d)

    def back_copy(p, k):
        place = peers.step(k, 1)
        return remote(
            back.at[p, peers.flat(place)], land_back.at[p, me],
            back_sems.at[0, p, k], back_sems.at[1, p, k], place,
        )

    def back_in(p, k):
        source = peers.flat(peers.step(k, -1))
        return remote(
            back.at[p, 0], land_back.at[p, source],
            back_sems.at[0, p, k], back_sems.at[1, p, k], sibling,
        )

    def give_back(p):
        for b in range(n_blocks // group):
            rows = jnp.concatenate(
                [
                    leave[c * half + p * few : c * half + (p + 1) * few, b * many : (b + 1) * many, :]
                    for c in range(2)
                ],
                axis=0,
            ).reshape(group * 16, leave.shape[2])
            turned = dot(again, rows).astype(BF16)
            back[p, b * group : (b + 1) * group] = turned.reshape(group, 16, leave.shape[2])
        for k in range(1, n_blocks):
            back_copy(p, k).start()
        land_back[p, me] = back[p, me]

    each(finish, few + 1, 0)
    give_back(0)
    each(finish, half, few + 1)
    act_in(half - 1).wait_recv()
    second(other + half - 1)
    give_back(1)
    stores = [pltpu.make_async_copy(act, act_out, o_sem.at[1])]
    if not backward:
        stores.append(pltpu.make_async_copy(sums, gate_out, o_sem.at[0]))
    for store in stores:
        store.start()
    slots_out[...] = slots[...]
    if backward:
        across_t = (s, h, 1 - t)
        width = bias_out.shape[1]

        def bias_row(e):
            bias_all[pl.ds(e, 1), :] = jnp.sum(act[e].astype(F32), axis=0, keepdims=True)

        each(bias_row, 2 * half, 0)

        def slot_row(e):
            total = jnp.sum(slots[e].astype(F32), axis=0, keepdims=True)
            sum_out[pl.ds(e, 1), : slots.shape[2]] = total

        sum_out[...] = jnp.zeros_like(sum_out)
        each(slot_row, 2 * half, 0)

        def piece(for_t):
            return bias_all[:, pl.ds(pl.multiple_of((core * n_t + for_t) * width, 128), width)]

        bias_send[...] = piece(1 - t)
        bias_copy = remote(bias_send, bias_land, b_sems.at[0], b_sems.at[1], across_t)
        bias_copy.start()
        bias_copy.wait()
        bias_out[...] = jnp.where(t == chip, piece(t), bias_land[...])
    for p in range(2):
        each(lambda k: back_in(p, k).wait_recv())
    back_out[...] = land_back[...]
    for store in stores:
        store.wait()
    if backward:
        relay(0, 3)
        relay(1, 3)
        g_own.wait()
        for origin in range(n_h):
            @pl.when((origin < h) & (h < n_h - 1))
            def _():
                for i in range(own_images):
                    z_hop(i, origin, 1).wait_send()

            @pl.when((origin > h) & (h > 0))
            def _():
                for i in range(own_images):
                    z_hop(i, origin, 0).wait_send()

        @pl.when(h < n_h - 1)
        def _():
            for i in range(own_images):
                z_hop(i, h, 1, output.at[i]).wait_send()

        @pl.when(h > 0)
        def _():
            for i in range(own_images):
                z_hop(i, h, 0, output.at[i]).wait_send()

    for p in range(2):
        each(lambda k: block_out(p, k).wait_send())
        each(lambda k: back_copy(p, k).wait_send())
    for copy in (core_copy, x_copy, act_copy):
        each(lambda j: copy(j).wait_send(), half, 0)


def expert_pass(sizes, backward, blocks, weights, gate, output=None, bias_width=0):
    _, experts, rows, hidden = weights.shape
    devices = sizes[0] * sizes[1] * sizes[2]
    images = 2 * devices
    half = experts // 2
    vmem = pl.BlockSpec(memory_space=pltpu.VMEM)
    hbm = pl.BlockSpec(memory_space=pl.ANY)
    slots = jax.ShapeDtypeStruct((experts, images, rows), BF16)
    act = jax.ShapeDtypeStruct((experts, images, hidden), BF16)
    gate_shape = (half, images, hidden)
    returned = jax.ShapeDtypeStruct((2, devices, experts, rows), BF16)
    if backward:
        operands, in_specs = (blocks, weights, gate, output), [vmem, hbm, hbm, hbm]
        outs = (
            slots, act, returned,
            jax.ShapeDtypeStruct((experts, bias_width), F32),
            jax.ShapeDtypeStruct((experts, 256), F32),
            jax.ShapeDtypeStruct((sizes[1] * output.shape[0], *output.shape[1:]), BF16),
        )
        out_specs = (vmem, hbm, vmem, vmem, vmem, hbm)
    else:
        operands, in_specs = (blocks, weights, gate), [vmem, hbm, vmem]
        outs = (slots, act, jax.ShapeDtypeStruct(gate_shape, F32), returned)
        out_specs = (vmem, hbm, hbm, vmem)
    weight = pltpu.VMEM((experts, rows, hidden), BF16)
    chunk = pltpu.VMEM((half, images, hidden), BF16)
    block = pltpu.VMEM((2, devices, experts, rows), BF16)
    dma = pltpu.SemaphoreType.DMA
    scratch = [weight, weight]
    if backward:
        scratch.append(pltpu.VMEM(gate_shape, F32))
    scratch += [
        pltpu.VMEM(gate_shape, F32),
        pltpu.VMEM(slots.shape, BF16),
        pltpu.VMEM(act.shape, BF16),
        chunk, chunk, chunk, chunk, block,
        pltpu.VMEM(slots.shape, BF16),
        block, block,
        dma((2,)), dma((2,)), dma((2, 2, devices)), dma((2, 2, devices)),
        dma((2, half)), dma((2, half)), dma((2, half)),
    ]
    if backward:
        scratch += [
            dma((2,)), dma((output.shape[0], sizes[1], 2)), dma((output.shape[0], sizes[1])), dma,
            pltpu.VMEM((experts, hidden), F32),
            pltpu.VMEM((experts, bias_width), F32),
            pltpu.VMEM((experts, bias_width), F32),
        ]
    else:
        scratch.append(pltpu.VMEM((experts, hidden), F32))
    return pl.pallas_call(
        partial(expert_kernel, sizes, backward),
        out_shape=outs,
        in_specs=in_specs,
        out_specs=out_specs,
        scratch_shapes=scratch,
        compiler_params=pltpu.CompilerParams(
            collective_id=2 if backward else 1, has_side_effects=True, vmem_limit_bytes=VMEM_BYTES
        ),
        cost_estimate=pl.CostEstimate(
            flops=8 * images * experts * rows * hidden,
            bytes_accessed=weights.size * 2,
            transcendentals=0,
        ),
        name="experts_back" if backward else "experts_ahead",
    )(*operands)


def weight_grad_kernel(slots_0, act_0, slots_1, act_1, out, lines, pick, same):
    group, images, rows = slots_0.shape
    d_block = out.shape[0]
    n = group * d_block
    m, d = pl.program_id(0), pl.program_id(2)

    @pl.when((m == 0) & (pl.program_id(1) == 0) & (d == 0))
    def _():
        row = lax.broadcasted_iota(jnp.int32, pick.shape, 0)
        column = lax.broadcasted_iota(jnp.int32, pick.shape, 1)
        pick[...] = (column == row // group).astype(F32).astype(BF16)
        row = lax.broadcasted_iota(jnp.int32, same.shape, 0)
        column = lax.broadcasted_iota(jnp.int32, same.shape, 1)
        same[...] = (row % group == column // images).astype(F32)

    def prepare(slots):
        @pl.when(d == 0)
        def _():
            turned = slots[...].reshape(group * images, rows).astype(F32)
            lines[...] = jnp.swapaxes(turned, 0, 1).astype(BF16)

    def term(act):
        mine = lines[pl.ds(pl.multiple_of(d * d_block, d_block), d_block)]
        spread = (dot(pick[...], mine) * same[...]).astype(BF16)
        values = act[...].reshape(group * images, act.shape[2])
        out[...] = dot(spread, values).reshape(out.shape)

    @pl.when(m == 0)
    def _():
        prepare(slots_0)
        term(act_0)

    @pl.when(m == 1)
    def _():
        prepare(slots_1)
        term(act_1)


def weight_grads(slots_0, act_0, slots_1, act_1):
    experts, images, rows = slots_0.shape
    hidden = act_0.shape[2]
    group, d_block = 8, 96
    last = experts // group - 1

    def early(m, g, d):
        return jnp.where(m == 0, g, last), 0, 0

    def late(m, g, d):
        return jnp.where(m == 0, 0, g), 0, 0

    slots, act = (group, images, rows), (group, images, hidden)
    return pl.pallas_call(
        weight_grad_kernel,
        grid=(2, experts // group, rows // d_block),
        out_shape=jax.ShapeDtypeStruct((rows, 2, experts, hidden), F32),
        in_specs=[
            pl.BlockSpec(slots, early), pl.BlockSpec(act, early),
            pl.BlockSpec(slots, late), pl.BlockSpec(act, late),
        ],
        out_specs=pl.BlockSpec((d_block, 1, group, hidden), lambda m, g, d: (d, m, g, 0)),
        scratch_shapes=[
            pltpu.VMEM((rows, group * images), BF16),
            pltpu.VMEM((group * d_block, d_block), BF16),
            pltpu.VMEM((group * d_block, group * images), F32),
        ],
        compiler_params=pltpu.CompilerParams(vmem_limit_bytes=VMEM_BYTES),
        cost_estimate=pl.CostEstimate(
            flops=4 * images * experts * rows * hidden,
            bytes_accessed=8 * rows * experts * hidden,
            transcendentals=0,
        ),
        name="weight_grads",
    )(slots_0, act_0, slots_1, act_1)


def dot_r(a, b):
    return lax.dot_general(a, b, (((0,), (0,)), ((), ())), preferred_element_type=F32)


def row_of(shape, axis):
    return lax.broadcasted_iota(jnp.int32, shape, axis)


def one_hot(mask):
    return mask.astype(F32).astype(BF16)


def order_matrix(n_h, few, back):
    n = n_h * 8 * few
    shape = (n, n)
    blocked, natural = row_of(shape, 1 if back else 0), row_of(shape, 0 if back else 1)
    f, half, image = blocked % few, (blocked // few) % 2, (blocked // (2 * few)) % 2
    group = blocked // (4 * few)
    if back:
        part, h = group // n_h, group % n_h
    else:
        h, part = group // 2, group % 2
    expert = ((h * 2 + half) * 2 + part) * few + f
    return one_hot(natural == image * (4 * n_h * few) + expert)


def norm_parts(x, scale, shift, live):
    centered = x - jnp.mean(x, axis=-1, keepdims=True)
    inverse = lax.rsqrt(jnp.mean(centered * centered, axis=-1, keepdims=True) + epsilon)
    unit = centered * inverse
    return unit * scale + shift, unit, inverse


def norm_back(grad, unit, inverse, scale):
    scaled = grad * scale
    average = jnp.mean(scaled, axis=-1, keepdims=True)
    projection = jnp.mean(scaled * unit, axis=-1, keepdims=True)
    return (
        inverse * (scaled - average - unit * projection),
        jnp.sum(grad * unit, axis=0, keepdims=True),
        jnp.sum(grad, axis=0, keepdims=True),
    )


def norm_rows(small):
    return jnp.swapaxes(small[:, 128:].astype(F32), 0, 1)[64:68]


def slots_to_blocks(slots, blocks, columns, joined, order):
    n_h, n_s = blocks.shape[:2]
    turned = dot(order, slots).astype(BF16)
    wide = joined.shape[1] // 2
    for s in range(0, n_s, 2):
        lanes = dot(turned[:, s * columns : (s + 2) * columns], joined).astype(BF16)
        for h in range(n_h):
            for p in range(2):
                rows = (h * 2 + p) * 16
                for e in range(2):
                    blocks[h, s + e, p] = lanes[rows : rows + 16, e * wide : e * wide + columns]


def blocks_to_slots(back, sizes, order, pair, padded):
    n_s, n_h, n_t = sizes
    columns = back.shape[3]
    both = jnp.concatenate([order] * n_t, axis=1)
    results = []
    for s in range(n_s):
        rows = jnp.concatenate(
            [
                back[p, (s * n_h + h) * n_t + t]
                for t in range(n_t)
                for p in range(2)
                for h in range(n_h)
            ],
            axis=0,
        )
        padded[s % 2, :, :columns] = dot(both, rows)
        if s % 2:
            value = jnp.concatenate([padded[0], padded[1]], axis=1)
            high = value.astype(BF16)
            rest = (value - high.astype(F32)).astype(BF16)
            results.append(dot(high, pair) + dot(rest, pair))
    return jnp.concatenate(results, axis=1)


def live_rows(shape, length):
    return row_of(shape, 0) < length


def ahead_kernel(
    length, tokens, small, w_hbm, blocks, normed_1, query, keyed, valued, context, hidden, normed_2,
    dispatch_out, combine_out, w, joined, order, w_sem,
):
    n, rows, width = tokens.shape
    keys = keyed.shape[1]
    loads = [pltpu.make_async_copy(w_hbm.at[k], w.at[k], w_sem.at[k]) for k in range(4)]
    for load in loads:
        load.start()
    norms = norm_rows(small)
    live = live_rows((rows, 1), length)
    for i in range(n):
        value, _, _ = norm_parts(tokens[i].astype(F32), norms[0:1], norms[2:3], live)
        normed_1[i] = jnp.where(live, value, 0.0).astype(BF16)
    joined[...] = pair_matrix(blocks.shape[4], joined.shape[1] // 2, True)
    order[...] = order_matrix(blocks.shape[0], 4, False)
    flat = (n * rows, width)
    for k, target in enumerate((query, keyed, valued)):
        loads[k].wait()
        value = dot(normed_1[...].reshape(flat), w[k]).astype(BF16).reshape(n, rows, width)
        if k == 0:
            target[...] = value
        else:
            target[:, :rows] = value
            target[:, rows:] = jnp.zeros((n, keys - rows, width), BF16)
    factor = HEAD_DIM ** (-0.5)
    pairs = width // 128
    lane = row_of((rows, 128), 1)
    shown = row_of((rows, keys), 1) < length

    def attend(step, carry):
        i = step // pairs
        lanes = pl.ds(pl.multiple_of((step % pairs) * 128, 128), 128)
        q, k, v = query[i, :, lanes], keyed[i, :, lanes], valued[i, :, lanes]
        scaled = q * jnp.bfloat16(factor)
        parts = []
        for a in range(2):
            mine = (lane < 64) if a == 0 else (lane >= 64)
            scores = dot_t(jnp.where(mine, scaled, jnp.zeros_like(q)), k)
            scores = jnp.where(shown, scores, -1e30)
            exponent = jnp.exp(scores - jnp.max(scores, axis=-1, keepdims=True))
            probs = exponent * (1.0 / jnp.sum(exponent, axis=-1, keepdims=True))
            parts.append(dot(probs.astype(BF16), v))
        context[i, :, lanes] = jnp.where(lane < 64, parts[0], parts[1]).astype(BF16)
        return carry

    lax.fori_loop(0, n * pairs, attend, 0, unroll=2)
    loads[3].wait()
    attended = dot_t(context[...].reshape(flat), w[3]).reshape(n, rows, width)
    for i in range(n):
        value = tokens[i].astype(F32) + attended[i]
        hidden[i] = value
        value, _, _ = norm_parts(value, norms[1:2], norms[3:4], live)
        normed_2[i] = jnp.where(live, value, 0.0).astype(BF16)
    logits = dot(normed_2[...].reshape(flat), small[:, :128]).reshape(n, rows, 128)
    experts = row_of((rows, 128), 1) < 64
    slots = []
    for i in range(n):
        here = logits[i]
        down = jnp.where(live, here, -1e30)
        exponent = jnp.exp(down - jnp.max(down, axis=0, keepdims=True))
        dispatch = exponent / jnp.sum(exponent, axis=0, keepdims=True)
        dispatch = jnp.where(experts, dispatch, 0.0)
        across = jnp.where(experts, here, -1e30)
        exponent = jnp.exp(across - jnp.max(across, axis=1, keepdims=True))
        combine = exponent / jnp.sum(exponent, axis=1, keepdims=True)
        dispatch_out[i] = dispatch
        combine_out[i] = combine
        slots.append(dot_r(dispatch.astype(BF16), normed_2[i])[:64].astype(BF16))
    slots_to_blocks(
        jnp.concatenate(slots, axis=0), blocks, blocks.shape[4], joined[...], order[...]
    )


def tokens_ahead(sizes, length, tokens, small, weights):
    n, rows, width = tokens.shape
    keys = 256
    vmem = pl.BlockSpec(memory_space=pltpu.VMEM)
    shape = jax.ShapeDtypeStruct
    wide = (n, keys, width)
    thin = shape((n, rows, 128), F32)
    return pl.pallas_call(
        partial(ahead_kernel, length),
        out_shape=(
            shape((sizes[1], sizes[0], 2, 16, width // sizes[0]), BF16),
            shape(tokens.shape, BF16), shape(tokens.shape, BF16), shape(wide, BF16),
            shape(wide, BF16), shape(tokens.shape, BF16), shape(tokens.shape, F32),
            shape(tokens.shape, BF16), thin, thin,
        ),
        in_specs=[vmem, vmem, pl.BlockSpec(memory_space=pl.ANY)],
        out_specs=(vmem,) * 10,
        scratch_shapes=[
            pltpu.VMEM(weights.shape, BF16),
            pltpu.VMEM((2 * width // sizes[0], 512), BF16),
            pltpu.VMEM((128, 128), BF16),
            pltpu.SemaphoreType.DMA((4,)),
        ],
        compiler_params=pltpu.CompilerParams(vmem_limit_bytes=VMEM_BYTES),
        name="tokens_ahead",
    )(tokens, small, weights)


def middle_kernel(
    sizes, back, small, combine, hidden, cotangent, output, blocks, grad_logits, padded
):
    n, rows, _ = hidden.shape
    columns = back.shape[3]
    padded[...] = jnp.zeros_like(padded)
    pair = pair_matrix(columns, padded.shape[2], False)
    joined = pair_matrix(columns, padded.shape[2], True)
    total = blocks_to_slots(back, sizes, order_matrix(sizes[1], 4, True), pair, padded)
    bias = jnp.swapaxes(small[:, :128].astype(F32), 0, 1)[64:]
    slots = []
    for i in range(n):
        slot_out = (total[i * 64 : (i + 1) * 64] + bias).astype(BF16)
        combine_b = combine[i].astype(BF16)[:, :64]
        output[i] = (hidden[i] + dot(combine_b, slot_out)).astype(BF16)
        grad_combine = dot_t(cotangent[i], slot_out)
        weight = combine[i][:, :64]
        weighted = jnp.sum(weight * grad_combine, axis=1, keepdims=True)
        grad_logits[i] = weight * (grad_combine - weighted)
        slots.append(dot_r(combine_b, cotangent[i]).astype(BF16))
    slots_to_blocks(
        jnp.concatenate(slots, axis=0), blocks, columns, joined, order_matrix(sizes[1], 4, False)
    )


def tokens_middle(sizes, back, small, combine, hidden, cotangent):
    n, rows, width = hidden.shape
    vmem = pl.BlockSpec(memory_space=pltpu.VMEM)
    shape = jax.ShapeDtypeStruct
    return pl.pallas_call(
        partial(middle_kernel, sizes),
        out_shape=(
            shape(hidden.shape, BF16),
            shape((sizes[1], sizes[0], 2, 16, width // sizes[0]), BF16),
            shape((n, rows, 64), F32),
        ),
        in_specs=[vmem] * 5,
        out_specs=(vmem,) * 3,
        scratch_shapes=[pltpu.VMEM((2, 128, 256), F32)],
        compiler_params=pltpu.CompilerParams(vmem_limit_bytes=VMEM_BYTES),
        name="tokens_middle",
    )(back, small, combine, hidden, cotangent)


def behind_kernel(
    sizes, length, back, small, w_hbm, tokens, normed_1, query, keyed, valued, context, hidden,
    normed_2, dispatch, grad_logits, cotangent, grads, small_grads, input_grad,
    w, padded, grad_hidden, rounded, grad_context, grad_q, grad_k, grad_v, w_sem,
):
    n, rows, width = tokens.shape
    keys = keyed.shape[1]
    loads = [pltpu.make_async_copy(w_hbm.at[k], w.at[k], w_sem.at[k]) for k in range(4)]
    for load in loads:
        load.start()
    norms = norm_rows(small)
    padded[...] = jnp.zeros_like(padded)
    pair = pair_matrix(back.shape[3], padded.shape[2], False)
    grad_slots = blocks_to_slots(
        back, sizes, order_matrix(sizes[1], 4, True), pair, padded
    ).astype(BF16)
    phi = small[:, :64]
    phi_grad = jnp.zeros((width, 64), F32)
    sums = []
    flat = (n * rows, width)
    for i in range(n):
        slots = grad_slots[i * 64 : (i + 1) * 64]
        weight = dispatch[i][:, :64]
        grad_dispatch = dot_t(normed_2[i], slots)
        weighted = jnp.sum(weight * grad_dispatch, axis=0, keepdims=True)
        logits = (weight * (grad_dispatch - weighted) + grad_logits[i]).astype(BF16)
        phi_grad = phi_grad + dot_r(normed_2[i], logits)
        grad = dot(weight.astype(BF16), slots) + dot_t(logits, phi)
        _, unit, inverse = norm_parts(hidden[i], norms[1:2], norms[3:4], None)
        grad_in, scale_grad, bias_grad = norm_back(grad, unit, inverse, norms[1:2])
        value = cotangent[i].astype(F32) + grad_in
        grad_hidden[i] = value
        rounded[i] = value.astype(BF16)
        sums.append((scale_grad, bias_grad))
    scale_2, bias_2 = sums[0][0] + sums[1][0], sums[0][1] + sums[1][1]
    flat_rounded = rounded[...].reshape(flat)
    loads[3].wait()
    grad_context[...] = dot(flat_rounded, w[3]).astype(BF16).reshape(n, rows, width)
    grads[3] = dot_r(flat_rounded, context[...].reshape(flat)).astype(BF16)
    factor = HEAD_DIM ** (-0.5)
    pairs = width // 128
    lane = row_of((rows, 128), 1)
    key_lane = row_of((keys, 128), 1)
    shown = row_of((rows, keys), 1) < length

    def attend(step, carry):
        i = step // pairs
        lanes = pl.ds(pl.multiple_of((step % pairs) * 128, 128), 128)
        q, k, v = query[i, :, lanes], keyed[i, :, lanes], valued[i, :, lanes]
        scaled = q * jnp.bfloat16(factor)
        g = grad_context[i, :, lanes]
        to_q, to_k, to_v = [], [], []
        for a in range(2):
            mine = (lane < 64) if a == 0 else (lane >= 64)
            scores = dot_t(jnp.where(mine, scaled, jnp.zeros_like(q)), k)
            grad_probs = dot_t(jnp.where(mine, g, jnp.zeros_like(g)), v)
            scores = jnp.where(shown, scores, -1e30)
            exponent = jnp.exp(scores - jnp.max(scores, axis=-1, keepdims=True))
            probs = exponent * (1.0 / jnp.sum(exponent, axis=-1, keepdims=True))
            weighted = jnp.sum(probs * grad_probs, axis=-1, keepdims=True)
            grad_scores = (probs * (grad_probs - weighted)).astype(BF16)
            to_v.append(dot_r(probs.astype(BF16), g))
            to_q.append(dot(grad_scores, k))
            to_k.append(dot_r(grad_scores, q))
        grad_q[i, :, lanes] = (jnp.where(lane < 64, to_q[0], to_q[1]) * factor).astype(BF16)
        kept = key_lane < 64
        grad_k[i, :, lanes] = (jnp.where(kept, to_k[0], to_k[1]) * factor)[:rows].astype(BF16)
        grad_v[i, :, lanes] = jnp.where(kept, to_v[0], to_v[1])[:rows].astype(BF16)
        return carry

    lax.fori_loop(0, n * pairs, attend, 0, unroll=2)
    total = jnp.zeros(flat, F32)
    turned = jnp.swapaxes(normed_1[...].reshape(flat).astype(F32), 0, 1).astype(BF16)
    for k, source in enumerate((grad_q, grad_k, grad_v)):
        loads[k].wait()
        value = source[...].reshape(flat)
        total = total + dot_t(value, w[k])
        grads[k] = dot(turned, value).astype(BF16)
    total = total.reshape(n, rows, width)
    sums = []
    for i in range(n):
        _, unit, inverse = norm_parts(tokens[i].astype(F32), norms[0:1], norms[2:3], None)
        grad_in, scale_grad, bias_grad = norm_back(total[i], unit, inverse, norms[0:1])
        input_grad[i] = (grad_hidden[i] + grad_in).astype(BF16)
        sums.append((scale_grad, bias_grad))
    scale_1, bias_1 = sums[0][0] + sums[1][0], sums[0][1] + sums[1][1]
    line = row_of((128, width), 0)
    spread = jnp.zeros((128, width), F32)
    for j, value in enumerate((scale_1, scale_2, bias_1, bias_2)):
        spread = jnp.where(line == 64 + j, value, spread)
    small_grads[...] = jnp.swapaxes(spread, 0, 1).astype(BF16)
    small_grads[:, :64] = phi_grad.astype(BF16)


def tokens_behind(sizes, length, back, small, weights, tokens, kept, grad_logits, cotangent):
    n, rows, width = tokens.shape
    vmem = pl.BlockSpec(memory_space=pltpu.VMEM)
    shape = jax.ShapeDtypeStruct
    low = pltpu.VMEM(tokens.shape, BF16)
    return pl.pallas_call(
        partial(behind_kernel, sizes, length),
        out_shape=(
            shape((4, width, width), BF16), shape((width, 128), BF16), shape(tokens.shape, BF16)
        ),
        in_specs=[vmem, vmem, pl.BlockSpec(memory_space=pl.ANY)] + [vmem] * 11,
        out_specs=(vmem,) * 3,
        scratch_shapes=[
            pltpu.VMEM(weights.shape, BF16),
            pltpu.VMEM((2, 128, 256), F32),
            pltpu.VMEM(tokens.shape, F32),
            low, low, low, low, low,
            pltpu.SemaphoreType.DMA((4,)),
        ],
        compiler_params=pltpu.CompilerParams(vmem_limit_bytes=VMEM_BYTES),
        name="tokens_behind",
    )(back, small, weights, tokens, *kept, grad_logits, cotangent)


def unpack_kernel(summed, in_bias_sum, out_sum, attn, phi_t, scales, biases, in_bias, out_bias):
    attn[...] = summed[:, :, : attn.shape[2]]
    turned = jnp.swapaxes(summed[0][:, 128:], 0, 1)
    phi_t[...] = turned[64:80]
    scales[...] = turned[80:82]
    biases[...] = turned[82:84]
    in_bias[...] = in_bias_sum[...]
    width = out_bias.shape[1]
    value = out_sum[...]
    later = pltpu.roll(value, value.shape[1] - width, 1)
    out_bias[...] = jnp.where(lax.axis_index("tensor") == 0, value[:, :width], later[:, :width])


def unpack_grads(summed, in_bias_sum, out_sum, block, slot):
    n_k, rows, _ = summed.shape
    vmem = pl.BlockSpec(memory_space=pltpu.VMEM)
    shape = jax.ShapeDtypeStruct
    return pl.pallas_call(
        unpack_kernel,
        out_shape=(
            shape((n_k, rows, block), F32), shape((slot, rows), F32),
            shape((2, rows), F32), shape((2, rows), F32),
            shape(in_bias_sum.shape, F32), shape((out_sum.shape[0], rows), F32),
        ),
        in_specs=[vmem] * 3,
        out_specs=(vmem,) * 6,
        name="unpack_grads",
    )(summed, in_bias_sum, out_sum)


def order_kernel(*refs):
    *parts, out = refs
    h, n_h = lax.axis_index("heads"), len(parts)
    own = parts[0].shape[0]
    group = own * n_h
    step = 256 // group
    length = out.shape[0]
    for first in range(0, length, step):
        count = min(step, length - first)
        taken = min(step, parts[0].shape[1] - first)
        shape = (count * group, group * taken)
        row = lax.broadcasted_iota(jnp.int32, shape, 0)
        column = lax.broadcasted_iota(jnp.int32, shape, 1)
        block = column // taken
        image = lax.rem(h + n_h - block // own, n_h) * own + block % own
        chosen = ((row // group == column % taken) & (row % group == image)).astype(F32)
        lines = jnp.concatenate(
            [part[i, first : first + taken] for part in parts for i in range(own)], axis=0
        )
        value = dot(chosen.astype(BF16), lines).astype(BF16)
        out[first : first + count] = value.reshape(count, group, value.shape[1])


def order_images(parts, length):
    own, _, width = parts[0].shape
    vmem = pl.BlockSpec(memory_space=pltpu.VMEM)
    return pl.pallas_call(
        order_kernel,
        out_shape=jax.ShapeDtypeStruct((length, own * len(parts), width), BF16),
        in_specs=[vmem] * len(parts),
        out_specs=vmem,
        compiler_params=pltpu.CompilerParams(vmem_limit_bytes=24 * 1024 * 1024),
        name="order_images",
    )(*parts)


def normalize(values, scale, shift):
    centered = values - jnp.mean(values, axis=-1, keepdims=True)
    variance = jnp.mean(centered * centered, axis=-1, keepdims=True)
    inverse = lax.rsqrt(variance + epsilon)
    unit_part = centered * inverse
    return (unit_part * scale + shift, unit_part, inverse)


def normalize_back(grad_output, unit_part, inverse, scale):
    scaled = grad_output * scale
    average = jnp.mean(scaled, axis=-1, keepdims=True)
    projection = jnp.mean(scaled * unit_part, axis=-1, keepdims=True)
    grad_input = inverse * (scaled - average - unit_part * projection)
    return (
        grad_input,
        jnp.sum(grad_output * unit_part, axis=(0, 1)),
        jnp.sum(grad_output, axis=(0, 1)),
    )


def to_experts(slots):
    slots = lax.all_to_all(slots, "heads", split_axis=1, concat_axis=0, tiled=True)
    slots = lax.all_to_all(slots, "shard", split_axis=2, concat_axis=0, tiled=True)
    return lax.all_gather(slots, "tensor", axis=0, tiled=True)


def to_images(slots):
    slots = lax.psum_scatter(slots, "tensor", scatter_dimension=0, tiled=True)
    slots = lax.all_to_all(slots, "shard", split_axis=0, concat_axis=2, tiled=True)
    return lax.all_to_all(slots, "heads", split_axis=0, concat_axis=1, tiled=True)


def general_shards(tokens, norm_scales, norm_biases, w_attn, phi, experts, in_bias, out_bias, cotangent):
    heads_n = lax.axis_size("heads")
    group, seq_len, width = tokens.shape
    own = group // heads_n
    heads_index = lax.axis_index("heads")
    tensor_index = lax.axis_index("tensor")
    shard_index = lax.axis_index("shard")
    hidden = experts.shape[3]
    rows = experts.shape[0]
    scales, biases, in_full = (
        lax.all_gather(norm_scales, ROWS, axis=1, tiled=True).astype(F32),
        lax.all_gather(norm_biases, ROWS, axis=1, tiled=True).astype(F32),
        lax.all_gather(in_bias, ROWS, axis=1, tiled=True).astype(F32),
    )
    attn = lax.all_gather(
        lax.all_gather(w_attn, "heads", axis=2, tiled=True), ROWS, axis=1, tiled=True
    )
    phi_full = lax.all_gather(
        lax.all_gather(phi, "heads", axis=1, tiled=True), ROWS, axis=0, tiled=True
    )
    out_rows = lax.all_gather(out_bias, "tensor", axis=1, tiled=True).astype(F32)
    e_own = experts.shape[2] // lax.axis_size("shard")
    in_local = lax.dynamic_slice_in_dim(in_full, tensor_index * hidden, hidden, 1)
    factor = HEAD_DIM ** (-0.5)
    tokens = lax.dynamic_slice_in_dim(tokens, heads_index * own, own, 0)
    cotangent = lax.dynamic_slice_in_dim(cotangent, heads_index * own, own, 0)
    n_heads = width // HEAD_DIM
    inputs = tokens.astype(F32)
    normed_one, unit_one, inverse_one = normalize(inputs, scales[0], biases[0])
    normed_one_b = normed_one.astype(BF16)
    projected = einsum("nsd,kdc->knsc", normed_one_b, attn[:3]).astype(BF16)
    query, keyed, valued = projected.reshape(3, own, seq_len, n_heads, HEAD_DIM)
    scores = einsum("nqhe,nkhe->nhqk", query, keyed) * factor
    score_peak = jnp.max(scores, axis=-1, keepdims=True)
    exponent = jnp.exp(scores - score_peak)
    probs = exponent / jnp.sum(exponent, axis=-1, keepdims=True)
    probs_b = probs.astype(BF16)
    context_b = (
        einsum("nhqk,nkhe->nqhe", probs_b, valued).astype(BF16).reshape(own, seq_len, width)
    )
    hidden_one = inputs + einsum("nsc,dc->nsd", context_b, attn[3])
    normed_two, unit_two, inverse_two = normalize(hidden_one, scales[1], biases[1])
    normed_two_b = normed_two.astype(BF16)
    logits = einsum("nsd,de->nse", normed_two_b, phi_full)
    dispatch = jax.nn.softmax(logits, axis=1)
    dispatch_b = dispatch.astype(BF16)
    combine = jax.nn.softmax(logits, axis=2)
    combine_b = combine.astype(BF16)
    slot_in = to_experts(einsum("nse,nsd->ned", dispatch_b, normed_two_b).astype(BF16))
    share = 1 if e_own else 0

    def meet(partial_sum):
        return lax.psum_scatter(partial_sum, "shard", scatter_dimension=share, tiled=True)

    def spread(values):
        return lax.all_gather(values, "shard", axis=share, tiled=True)

    pre = meet(einsum("ned,def->nef", slot_in, experts[:, 0]))
    if e_own:
        pre = pre + lax.dynamic_slice_in_dim(in_local, shard_index * e_own, e_own, 0)
    else:
        pre = pre + in_local
    gelu_value, gelu_back = jax.vjp(partial(jax.nn.gelu, approximate=False), pre)
    activated = spread(gelu_value.astype(BF16))
    slot_out_part = einsum("nef,def->ned", activated, experts[:, 1])
    slot_out_part = slot_out_part + jnp.where(tensor_index == 0, out_rows, 0.0)
    slot_out = to_images(slot_out_part).astype(BF16)
    output = (hidden_one + einsum("nse,ned->nsd", combine_b, slot_out)).astype(BF16)
    output = lax.all_gather(output, "heads", axis=0, tiled=True)
    grad_combine = einsum("nsd,ned->nse", cotangent, slot_out)
    grad_slot = to_experts(einsum("nse,nsd->ned", combine_b, cotangent).astype(BF16))
    grad_act = meet(einsum("ned,def->nef", grad_slot, experts[:, 1]))
    grad_pre = spread(gelu_back(grad_act)[0].astype(BF16))
    grad_slot_in = einsum("nef,def->ned", grad_pre, experts[:, 0]).astype(BF16)
    input_term = einsum("ned,nef->def", slot_in, grad_pre)
    output_term = einsum("ned,nef->def", grad_slot, activated)
    experts_grad = jnp.stack((input_term, output_term), axis=1)
    grad_slot_in = to_images(grad_slot_in.astype(F32)).astype(BF16)
    in_bias_grad = lax.dynamic_slice_in_dim(
        lax.all_gather(jnp.sum(grad_pre.astype(F32), axis=0), "tensor", axis=1, tiled=True),
        (shard_index * lax.axis_size("tensor") + tensor_index) * in_bias.shape[1],
        in_bias.shape[1],
        1,
    )
    out_bias_grad = lax.dynamic_slice_in_dim(
        jnp.sum(grad_slot.astype(F32), axis=0),
        tensor_index * out_bias.shape[1],
        out_bias.shape[1],
        1,
    )
    grad_dispatch = einsum("nsd,ned->nse", normed_two_b, grad_slot_in)
    grad_logits = (
        dispatch * (grad_dispatch - jnp.sum(dispatch * grad_dispatch, axis=1, keepdims=True))
        + combine * (grad_combine - jnp.sum(combine * grad_combine, axis=2, keepdims=True))
    ).astype(BF16)
    phi_grad = einsum("nsd,nse->de", normed_two_b, grad_logits)
    grad_normed_two = einsum("nse,ned->nsd", dispatch_b, grad_slot_in) + einsum(
        "nse,de->nsd", grad_logits, phi_full
    )
    grad_hidden_norm, scale_two_grad, bias_two_grad = normalize_back(
        grad_normed_two, unit_two, inverse_two, scales[1]
    )
    grad_hidden = cotangent.astype(F32) + grad_hidden_norm
    grad_hidden_b = grad_hidden.astype(BF16)
    out_weight_grad = einsum("nsd,nsc->dc", grad_hidden_b, context_b)
    grad_context = einsum("nsd,dc->nsc", grad_hidden_b, attn[3]).astype(BF16)
    grad_context = grad_context.reshape(own, seq_len, n_heads, HEAD_DIM)
    grad_value = einsum("nhqk,nqhe->nkhe", probs_b, grad_context).astype(BF16)
    grad_probs = einsum("nqhe,nkhe->nhqk", grad_context, valued)
    grad_scores = (
        probs * (grad_probs - jnp.sum(probs * grad_probs, axis=-1, keepdims=True))
    ).astype(BF16)
    grad_query = (einsum("nhqk,nkhe->nqhe", grad_scores, keyed) * factor).astype(BF16)
    grad_key = (einsum("nhqk,nqhe->nkhe", grad_scores, query) * factor).astype(BF16)
    grad_proj = jnp.stack((grad_query, grad_key, grad_value)).reshape(3, own, seq_len, width)
    proj_grad = einsum("nsd,knsc->kdc", normed_one_b, grad_proj)
    grad_normed_one = einsum("knsc,kdc->nsd", grad_proj, attn[:3])
    grad_input_norm, scale_one_grad, bias_one_grad = normalize_back(
        grad_normed_one, unit_one, inverse_one, scales[0]
    )
    input_grad = (grad_hidden + grad_input_norm).astype(BF16)
    input_grad = lax.all_gather(input_grad, "heads", axis=0, tiled=True)
    attn_grad = jnp.concatenate((proj_grad, out_weight_grad[None]), axis=0)
    attn_grad = lax.psum_scatter(attn_grad, ROWS, scatter_dimension=1, tiled=True)
    attn_grad = lax.psum_scatter(attn_grad, "heads", scatter_dimension=2, tiled=True)
    phi_grad = lax.psum_scatter(phi_grad, ROWS, scatter_dimension=0, tiled=True)
    phi_grad = lax.psum_scatter(phi_grad, "heads", scatter_dimension=1, tiled=True)
    norms = jnp.stack((scale_one_grad, scale_two_grad, bias_one_grad, bias_two_grad))
    norms = lax.psum(lax.psum_scatter(norms, ROWS, scatter_dimension=1, tiled=True), "heads")
    return (
        output,
        input_grad,
        norms[:2],
        norms[2:],
        attn_grad,
        phi_grad,
        experts_grad,
        in_bias_grad,
        out_bias_grad,
    )


def shards(tokens, norm_scales, norm_biases, w_attn, phi, experts, in_bias, out_bias, cotangent):
    arrays = (tokens, norm_scales, norm_biases, w_attn, phi, experts, in_bias, out_bias, cotangent)
    sizes = tuple(lax.axis_size(name) for name in ("shard", "heads", "tensor"))
    group, length, width = tokens.shape
    fits = (sizes, group, width, *experts.shape[:3]) == ((4, 4, 2), 8, 768, 192, 2, 16)
    if not fits or not 192 < length <= 208 or in_bias.shape[1] != 384:
        return general_shards(*arrays)
    n_s, n_h, n_t = sizes
    block, slot = w_attn.shape[2], phi.shape[1]
    tokens, cotangent = (
        values.transpose(1, 0, 2).reshape(group * length, width) for values in (tokens, cotangent)
    )
    attn, small, turned, tokens, cotangent = gather_weights(
        sizes, w_attn, phi.T, out_bias, norm_scales, norm_biases, in_bias, experts, tokens, cotangent
    )
    blocks, *kept, combine = tokens_ahead(sizes, length, tokens, small, attn)
    hidden = kept[5]
    slot_in, activated, gate, back = expert_pass(sizes, False, blocks, turned, small)
    output, blocks, grad_logits = tokens_middle(sizes, back, small, combine, hidden, cotangent)
    grad_slot, grad_pre, back, in_bias_grad, out_sum, output = expert_pass(
        sizes, True, blocks, turned, gate, output, in_bias.shape[1]
    )
    attn_grad, small_grad, input_grad = tokens_behind(
        sizes, length, back, small, attn, tokens, kept, grad_logits, cotangent
    )
    parts = [input_grad] + [
        lax.ppermute(input_grad, "heads", [(i, (i + d) % n_h) for i in range(n_h)])
        for d in range(1, n_h)
    ]
    attn_grad, grad_pre = lax.optimization_barrier((attn_grad, grad_pre))
    experts_grad = weight_grads(slot_in, grad_pre, grad_slot, activated)
    output = output[:, :length].transpose(1, 0, 2)
    attn_grad, experts_grad, output = lax.optimization_barrier((attn_grad, experts_grad, output))
    summed = reduce_grads(sizes, attn_grad, small_grad)
    attn_grad, phi_grad, scales_grad, biases_grad, in_bias_grad, out_bias_grad = unpack_grads(
        summed, in_bias_grad, out_sum, block, slot
    )
    input_grad = order_images(parts, length)
    return (
        output.transpose(1, 0, 2),
        input_grad.transpose(1, 0, 2),
        scales_grad,
        biases_grad,
        attn_grad,
        phi_grad.T,
        experts_grad,
        in_bias_grad,
        out_bias_grad,
    )


def solution(mesh):
    images = P(ROWS, None, None)
    return jax.shard_map(
        shards,
        mesh=mesh,
        in_specs=(
            images,
            P(None, ROWS),
            P(None, ROWS),
            P(None, ROWS, "heads"),
            P(ROWS, "heads"),
            P("shard", None, "heads", "tensor"),
            P("heads", ROWS),
            P("heads", ROWS),
            images,
        ),
        out_specs=(
            images,
            images,
            P(None, ROWS),
            P(None, ROWS),
            P(None, ROWS, "heads"),
            P(ROWS, "heads"),
            P("shard", None, "heads", "tensor"),
            P("heads", ROWS),
            P("heads", ROWS),
        ),
        check_vma=False,
    )
```

```python
from functools import partial

import jax
import jax.numpy as jnp
from jax import lax
from jax.experimental import pallas as pl
from jax.experimental.pallas import tpu as pltpu
from jax.sharding import PartitionSpec as P

HEAD_DIM = 64
F32 = jnp.float32
BF16 = jnp.bfloat16
ROWS = ("shard", "tensor")
MESH = pl.DeviceIdType.MESH
VMEM_BYTES = 58 * 1024 * 1024
epsilon = 1e-06
einsum = partial(jnp.einsum, preferred_element_type=F32)


def dot(a, b):
    return lax.dot_general(a, b, (((1,), (0,)), ((), ())), preferred_element_type=F32)


def dot_t(a, b):
    return lax.dot_general(a, b, (((1,), (1,)), ((), ())), preferred_element_type=F32)


def swap_matrix(n):
    out = lax.broadcasted_iota(jnp.int32, (n * n, n * n), 0)
    row = lax.broadcasted_iota(jnp.int32, (n * n, n * n), 1)
    return ((out // n == row % n) & (out % n == row // n)).astype(F32).astype(BF16)


class Peers:
    def __init__(self, sizes):
        self.sizes = sizes
        self.at = tuple(lax.axis_index(name) for name in ("shard", "heads", "tensor"))
        self.count = sizes[0] * sizes[1] * sizes[2]

    def flat(self, place):
        return (place[0] * self.sizes[1] + place[1]) * self.sizes[2] + place[2]

    def step(self, k, sign):
        _, n_h, n_t = self.sizes
        steps = (k // (n_h * n_t), (k // n_t) % n_h, k % n_t)
        return tuple(
            lax.rem(at + n + sign * d, n) for at, n, d in zip(self.at, self.sizes, steps)
        )

    def greet_all(self):
        barrier = pltpu.get_barrier_semaphore()

        def signal(k, carry):
            pl.semaphore_signal(barrier, inc=1, device_id=self.step(k, 1), device_id_type=MESH)
            return carry

        lax.fori_loop(1, self.count, signal, 0)
        pl.semaphore_wait(barrier, self.count - 1)


def remote(src, dst, send, recv, place):
    return pltpu.make_async_remote_copy(
        src_ref=src, dst_ref=dst, send_sem=send, recv_sem=recv, device_id=place, device_id_type=MESH
    )


def plane(sizes):
    n_s, n_h, n_t = sizes
    s, h, t = (lax.axis_index(name) for name in ("shard", "heads", "tensor"))
    core, chip = lax.rem(s, 2), s // 2
    sibling = (s + 1 - 2 * core, h, t)
    across_x = (lax.rem(s + 2, n_s), h, t)
    across_y = (s, h, 1 - t)
    line = [(s, lax.rem(h + d, n_h), t) for d in range(n_h)]
    barrier = pltpu.get_barrier_semaphore()
    others = [sibling, across_x, across_y] + line[1:]
    for place in others:
        pl.semaphore_signal(barrier, inc=1, device_id=place, device_id_type=MESH)
    pl.semaphore_wait(barrier, len(others))
    return (s, h, t), core, chip, sibling, across_x, across_y, line


def pair_matrix(block, wide, transposed):
    shape = (2 * block, 2 * wide) if transposed else (2 * wide, 2 * block)
    tight = lax.broadcasted_iota(jnp.int32, shape, 0 if transposed else 1)
    padded = lax.broadcasted_iota(jnp.int32, shape, 1 if transposed else 0)
    second = padded >= wide
    lane = jnp.where(second, padded - wide, padded)
    same = (lane < block) & (tight == jnp.where(second, lane + block, lane))
    return same.astype(F32).astype(BF16)


def gather_kernel(
    sizes, w_attn, phi_t, out_bias, scales, biases, in_bias, experts, tokens, cotangent, w_out, small_out, turned, own_tokens, own_cot,
    w, small, lined, extra, stage, tile_in, tile_out, images, picked,
    z_send, z_recv, x_sems, y_sems, d_sems, c_sems, t_sems, o_sems, i_sems,
):
    n_k, rows, block = w_attn.shape
    wide = lined.shape[3]
    slot = phi_t.shape[0]
    own_h = lax.axis_index("heads")
    stage[...] = jnp.zeros_like(stage)
    stage[64 : 64 + slot] = phi_t[...].astype(F32)
    stage[64 + slot : 64 + 2 * slot] = out_bias[...].astype(F32)
    lined[own_h, :, :, 128:] = jnp.zeros((n_k, rows, wide - 128), BF16)
    lined[own_h, :, :, :block] = w_attn[...]
    first = lined[own_h, 0, :, 128:].astype(F32) + jnp.swapaxes(stage[...], 0, 1)
    lined[own_h, 0, :, 128:] = first.astype(BF16)
    (s, h, t), core, chip, sibling, across_x, across_y, line = plane(sizes)
    n_h, n_t = sizes[1], sizes[2]
    width = w.shape[2]
    side = 16
    n_tiles = experts.shape[0] // side
    depth = tile_in.shape[0]
    halves = ((0, rows // 2), (rows // 2, rows // 2))

    def z_hop(k, origin, up):
        place = line[1] if up else line[n_h - 1]
        return remote(
            lined.at[origin, k], lined.at[origin, k],
            z_send.at[k, origin, up], z_recv.at[k, origin], place,
        )

    def relay(k, d):
        @pl.when(h >= d)
        def _():
            z_hop(k, h - d, 1).wait_recv()

            @pl.when(h < n_h - 1)
            def _():
                z_hop(k, h - d, 1).start()

        @pl.when(h + d < n_h)
        def _():
            z_hop(k, h + d, 0).wait_recv()

            @pl.when(h > 0)
            def _():
                z_hop(k, h + d, 0).start()

    chunks = (0, 2, 1, 3)
    for k in chunks:
        @pl.when(h < n_h - 1)
        def _():
            z_hop(k, h, 1).start()

        @pl.when(h > 0)
        def _():
            z_hop(k, h, 0).start()

    def load(i):
        return pltpu.make_async_copy(
            experts.at[pl.ds((i % n_tiles) * side, side), i // n_tiles],
            tile_in.at[i % depth],
            t_sems.at[0, i % depth],
        )

    def store(i):
        return pltpu.make_async_copy(
            tile_out.at[i % depth],
            turned.at[i // n_tiles, :, pl.ds((i % n_tiles) * side, side)],
            t_sems.at[1, i % depth],
        )

    image_loads = [
        pltpu.make_async_copy(source, images.at[j], i_sems.at[0, j])
        for j, source in enumerate((tokens, cotangent))
    ]
    for i in range(depth - 1):
        load(i).start()
    for copy in image_loads:
        copy.start()
    swap = swap_matrix(side)
    done = [0]

    def turn(count):
        def step(i, carry):
            load(i).wait()

            @pl.when(i + depth - 1 < 2 * n_tiles)
            def _():
                load(i + depth - 1).start()

            @pl.when(i >= depth)
            def _():
                store(i - depth).wait()

            rows_in = tile_in[i % depth].reshape(side * side, tile_in.shape[3])
            tile_out[i % depth] = dot(swap, rows_in).astype(BF16).reshape(tile_out.shape[1:])
            store(i).start()
            return carry

        last = min(done[0] + count, 2 * n_tiles)
        lax.fori_loop(done[0], last, step, 0)
        done[0] = last

    pair = pair_matrix(block, wide, False)
    shape = (n_h * wide, small.shape[1])
    row = lax.broadcasted_iota(jnp.int32, shape, 0)
    column = lax.broadcasted_iota(jnp.int32, shape, 1)
    lane, of = row % wide - block, row // wide
    beside = (lane >= 0) & (lane < 16) & (column == of * 16 + lane)
    beside |= (lane >= 16) & (lane < 32) & (column == n_h * 16 + of * 16 + lane - 16)
    beside = beside.astype(F32).astype(BF16)

    stage[...] = jnp.zeros_like(stage)
    stage[64:66] = scales[...].astype(F32)
    stage[66:68] = biases[...].astype(F32)
    norms = jnp.swapaxes(stage[...], 0, 1)
    pieces = []
    for j in range(in_bias.shape[1] // 64):
        shape = (in_bias.shape[1], 128)
        row = lax.broadcasted_iota(jnp.int32, shape, 0)
        column = lax.broadcasted_iota(jnp.int32, shape, 1)
        chosen = ((row == 64 * j + column) & (column < 64)).astype(F32).astype(BF16)
        pieces.append(dot(in_bias[...], chosen))
    extra[:, :128] = jnp.zeros((rows, 128), F32)
    extra[:, 128:] = jnp.concatenate(pieces, axis=0) + norms

    image_stores = [
        pltpu.make_async_copy(picked.at[j], target, i_sems.at[1, j])
        for j, target in enumerate((own_tokens, own_cot))
    ]

    def pick_images(j):
        own, padded = picked.shape[1:3]
        group = own * n_h
        lines = images.shape[1]
        image_loads[j].wait()
        step = 256 // group
        for first in range(0, padded, step):
            count = min(step, padded - first)
            taken = min(step * group, lines - first * group)
            shape = (own * count, taken)
            row = lax.broadcasted_iota(jnp.int32, shape, 0)
            column = lax.broadcasted_iota(jnp.int32, shape, 1)
            wanted = (row % count) * group + own * h + row // count
            chosen = (column == wanted).astype(F32).astype(BF16)
            source = images[j, first * group : first * group + taken]
            picked[j, :, first : first + count] = (
                dot(chosen, source).astype(BF16).reshape(own, count, images.shape[2])
            )
        image_stores[j].start()

    def at(k, place):
        first = pl.multiple_of((place[0] * n_t + place[2]) * rows, 16)
        lines = pl.ds(first, rows)
        return small.at[lines] if k == n_k else w.at[k, lines]

    def hop(q, origin, place, sems, j):
        return remote(at(q, origin), at(q, origin), sems.at[0, j], sems.at[1, j], place)

    def half_hop(q, origin, place, half):
        part = at(q, origin).at[pl.ds(*halves[half])]
        j = 2 * q + half
        return remote(part, part, d_sems.at[0, j], d_sems.at[1, j], place)

    me = (s, h, t)
    from_d = (across_x[0], h, across_y[2])
    sent = []

    def send(copy):
        copy.start()
        sent.append(copy)

    def assemble(k):
        for i in range(0, n_h, 2):
            lines = jnp.concatenate([lined[i, k], lined[i + 1, k]], axis=1)
            at(k, me)[:, i * block : (i + 2) * block] = dot(lines, pair).astype(BF16)
        if k == 0:
            lines = jnp.concatenate([lined[i, k] for i in range(n_h)], axis=1)
            at(n_k, me)[...] = (dot(lines, beside) + extra[...]).astype(BF16)
        for q in members(k):
            send(hop(q, me, across_x, x_sems, q))
            send(hop(q, me, across_y, y_sems, q))
            send(hop(q, me, sibling, c_sems, 4 * q))

    def members(k):
        return (0, n_k) if k == 0 else (k,)

    def relay_xy(k):
        for q in members(k):
            hop(q, across_x, across_x, x_sems, q).wait_recv()
            send(half_hop(q, across_x, across_y, 0))
            send(hop(q, across_x, sibling, c_sems, 4 * q + 1))
            hop(q, across_y, across_y, y_sems, q).wait_recv()
            send(half_hop(q, across_y, across_x, 1))
            send(hop(q, across_y, sibling, c_sems, 4 * q + 2))

    def relay_d(k):
        for q in members(k):
            half_hop(q, from_d, across_y, 0).wait_recv()
            half_hop(q, from_d, across_x, 1).wait_recv()
            send(hop(q, from_d, sibling, c_sems, 4 * q + 3))

    for wave in range(n_k + n_h - 2):
        for d in range(1, n_h):
            if 0 <= wave - d + 1 < n_k:
                relay(chunks[wave - d + 1], d)
        turn(2)
        i = wave - n_h + 2
        if i >= 0:
            assemble(chunks[i])
            if i in (1, 2):
                pick_images(i - 1)
            if i >= 1:
                relay_xy(chunks[i - 1])
            if i >= 2:
                relay_d(chunks[i - 2])
            turn(2)
    relay_xy(chunks[-1])
    relay_d(chunks[-2])
    turn(2 * n_tiles)
    relay_d(chunks[-1])
    stores = []
    for k in chunks:
        for q in members(k):
            for j in range(4):
                hop(q, me, sibling, c_sems, 4 * q + j).wait_recv()
            if q == n_k:
                stores.append(pltpu.make_async_copy(small, small_out, o_sems.at[q]))
            else:
                stores.append(pltpu.make_async_copy(w.at[q], w_out.at[q], o_sems.at[q]))
            stores[-1].start()
    for copy in sent:
        copy.wait_send()
    for origin in range(n_h):
        @pl.when((origin <= h) & (h < n_h - 1))
        def _():
            for k in range(n_k):
                z_hop(k, origin, 1).wait_send()

        @pl.when((origin >= h) & (h > 0))
        def _():
            for k in range(n_k):
                z_hop(k, origin, 0).wait_send()

    for i in range(depth):
        store(2 * n_tiles - depth + i).wait()
    for copy in image_stores:
        copy.wait()
    for copy in stores:
        copy.wait()


def gather_weights(
    sizes, w_attn, phi_t, out_bias, scales, biases, in_bias, experts, tokens, cotangent
):
    n_k, rows, _ = w_attn.shape
    wide = 256
    n_s, n_h, n_t = sizes
    width = n_s * n_t * rows
    vmem = pl.BlockSpec(memory_space=pltpu.VMEM)
    hbm = pl.BlockSpec(memory_space=pl.ANY)
    dma = pltpu.SemaphoreType.DMA
    hidden = experts.shape[3]
    small = (width, wide)
    images = jax.ShapeDtypeStruct((2, 208, width), BF16)
    return pl.pallas_call(
        partial(gather_kernel, sizes),
        out_shape=(
            jax.ShapeDtypeStruct((n_k, width, width), BF16),
            jax.ShapeDtypeStruct(small, BF16),
            jax.ShapeDtypeStruct((2, experts.shape[2], experts.shape[0], hidden), BF16),
            images, images,
        ),
        in_specs=[vmem] * 6 + [hbm] * 3,
        out_specs=(hbm,) * 5,
        scratch_shapes=[
            pltpu.VMEM((n_k, width, width), BF16),
            pltpu.VMEM(small, BF16),
            pltpu.VMEM((n_h, n_k, rows, wide), BF16),
            pltpu.VMEM((rows, wide), F32),
            pltpu.VMEM((128, rows), F32),
            pltpu.VMEM((4, 16, 16, hidden), BF16),
            pltpu.VMEM((4, 16, 16, hidden), BF16),
            pltpu.VMEM((2, *tokens.shape), BF16),
            pltpu.VMEM((2, *images.shape), BF16),
            dma((n_k, n_h, 2)), dma((n_k, n_h)), dma((2, n_k + 1)), dma((2, n_k + 1)),
            dma((2, 2 * (n_k + 1))), dma((2, 4 * (n_k + 1))), dma((2, 4)), dma((n_k + 1,)),
            dma((2, 2)),
        ],
        compiler_params=pltpu.CompilerParams(
            collective_id=3, has_side_effects=True, vmem_limit_bytes=VMEM_BYTES
        ),
        name="gather_weights",
    )(w_attn, phi_t, out_bias, scales, biases, in_bias, experts, tokens, cotangent)


def reduce_kernel(
    sizes, grads, small, out, core_in, core_small, met, met_small,
    d_in, d_small, x_in, x_small, y_in, y_small, pieces, z_in,
    c_sems, d_sems, x_sems, y_sems, z_send, z_recv,
):
    (s, h, t), core, chip, sibling, across_x, across_y, line = plane(sizes)
    n_k, width, _ = grads.shape
    n_s, n_h, n_t = sizes
    rows = width // (n_s * n_t)
    wide = pieces.shape[3]
    pair = n_t * rows
    half = rows // 2
    halves = (pl.ds(0, half), pl.ds(half, half))
    chunks = (0, 2, 1, 3)

    def members(k):
        return (0, n_k) if k == 0 else (k,)

    def pick(q, large, little):
        return little if q == n_k else large.at[q]

    def core_copy(q, x):
        first = pl.multiple_of((2 * x + 1 - core) * pair, 16)
        return remote(
            pick(q, grads, small).at[pl.ds(first, pair)],
            pick(q, core_in, core_small).at[x],
            c_sems.at[0, 2 * q + x], c_sems.at[1, 2 * q + x], sibling,
        )

    for k in chunks:
        for q in members(k):
            for x in range(2):
                core_copy(q, x).start()
    joined = pair_matrix(width // n_h, wide, True)
    shape = (small.shape[1], n_h * wide)
    row = lax.broadcasted_iota(jnp.int32, shape, 0)
    column = lax.broadcasted_iota(jnp.int32, shape, 1)
    lane, of = column % wide - width // n_h, column // wide
    beside = (lane >= 0) & (lane < 16) & (row == of * 16 + lane)
    beside |= (lane >= 16) & (lane < 20) & (row == n_h * 16 + lane - 16)
    beside = beside.astype(F32).astype(BF16)
    to_d, to_x, to_y = (d_in, d_small), (x_in, x_small), (y_in, y_small)
    sent = []

    def hop(q, kind, part, source, place):
        sems = {id(to_d): d_sems, id(to_x): x_sems, id(to_y): y_sems}[id(kind)]
        target = pick(q, *kind)
        target = target.at[part] if kind is to_d else target.at[halves[part]]
        j = 2 * q + part
        return remote(source, target, sems.at[0, j], sems.at[1, j], place)

    def send(copy):
        copy.start()
        sent.append(copy)

    def part_of(q, x, y, part):
        return pick(q, met, met_small).at[x, y].at[halves[part]]

    def arrived(q, kind, part):
        hop(q, kind, part, part_of(q, 0, 0, part), sibling).wait_recv()

    def open_up(q):
        part = pick(q, met, met_small)
        for x in range(2):
            core_copy(q, x).wait_recv()
            first = pl.multiple_of((2 * x + core) * pair, 16)
            own = pick(q, grads, small)[pl.ds(first, pair)].astype(F32)
            total = own + pick(q, core_in, core_small)[x].astype(F32)
            part[x] = total.astype(BF16).reshape(n_t, rows, total.shape[1])
        send(hop(q, to_d, 0, part_of(q, 1 - chip, 1 - t, 0), across_x))
        send(hop(q, to_d, 1, part_of(q, 1 - chip, 1 - t, 1), across_y))
        send(hop(q, to_x, 0, part_of(q, 1 - chip, t, 0), across_x))
        send(hop(q, to_y, 1, part_of(q, chip, 1 - t, 1), across_y))

    def pass_on(q):
        for part, kind, x, y, place in (
            (0, to_y, chip, 1 - t, across_y),
            (1, to_x, 1 - chip, t, across_x),
        ):
            arrived(q, to_d, part)
            block = part_of(q, x, y, part)
            total = block[...].astype(F32) + pick(q, *to_d)[part].astype(F32)
            block[...] = total.astype(BF16)
            send(hop(q, kind, part, block, place))

    def whole(q):
        for kind in (to_x, to_y):
            for part in range(2):
                arrived(q, kind, part)
        total = pick(q, met, met_small)[chip, t].astype(F32) + pick(q, *to_x)[...].astype(F32)
        return (total + pick(q, *to_y)[...].astype(F32)).astype(BF16)

    def z_copy(k, target, up):
        place = line[1] if up else line[n_h - 1]
        return remote(
            pieces.at[target, k], z_in.at[up, target, k],
            z_send.at[up, target, k], z_recv.at[up, target, k], place,
        )

    def pass_along(k, hops):
        for up in range(2):
            for target in range(n_h - 1, -1, -1) if up else range(n_h):
                further = target > h if up else target < h

                @pl.when(further & (h == (hops if up else n_h - 1 - hops)))
                def _():
                    if hops > 0:
                        z_copy(k, target, up).wait_recv()
                        total = pieces[target, k].astype(F32) + z_in[up, target, k].astype(F32)
                        pieces[target, k] = total.astype(BF16)
                    z_copy(k, target, up).start()

    def share_out(k):
        value = whole(k)
        columns = width // n_h
        if k == 0:
            little = dot(whole(n_k), beside)
        for i in range(0, n_h, 2):
            lanes = dot(value[:, i * columns : (i + 2) * columns], joined)
            if k == 0:
                lanes = lanes + little[:, i * wide : (i + 2) * wide]
            pieces[i, k] = lanes[:, :wide].astype(BF16)
            pieces[i + 1, k] = lanes[:, wide:].astype(BF16)
        pass_along(k, 0)

    for i in range(n_k + 2 + n_h - 2):
        if i < n_k:
            for q in members(chunks[i]):
                open_up(q)
        if 0 <= i - 1 < n_k:
            for q in members(chunks[i - 1]):
                pass_on(q)
        if 0 <= i - 2 < n_k:
            share_out(chunks[i - 2])
        for hops in range(1, n_h - 1):
            if 0 <= i - 2 - hops < n_k:
                pass_along(chunks[i - 2 - hops], hops)
    for k in chunks:
        out[k] = pieces[h, k].astype(F32)
        for up, there in ((1, h > 0), (0, h < n_h - 1)):
            @pl.when(there)
            def _():
                z_copy(k, h, up).wait_recv()
                out[k] = out[k] + z_in[up, h, k].astype(F32)

    for k in chunks:
        for q in members(k):
            for x in range(2):
                core_copy(q, x).wait_send()
    for copy in sent:
        copy.wait_send()
    for target in range(n_h):
        for up in range(2):
            @pl.when(target > h if up else target < h)
            def _():
                for k in range(n_k):
                    z_copy(k, target, up).wait_send()


def reduce_grads(sizes, grads, small):
    n_k, width, _ = grads.shape
    n_s, n_h, n_t = sizes
    rows, wide, thin = width // (n_s * n_t), 256, small.shape[1]
    vmem = pl.BlockSpec(memory_space=pltpu.VMEM)
    dma = pltpu.SemaphoreType.DMA

    def buffers(*lead):
        return [
            pltpu.VMEM((n_k, *lead, width), BF16),
            pltpu.VMEM((*lead, thin), BF16),
        ]

    return pl.pallas_call(
        partial(reduce_kernel, sizes),
        out_shape=jax.ShapeDtypeStruct((n_k, rows, wide), F32),
        in_specs=[vmem, vmem],
        out_specs=vmem,
        scratch_shapes=[
            *buffers(2, n_t * rows), *buffers(2, n_t, rows),
            *buffers(2, rows // 2), *buffers(rows), *buffers(rows),
            pltpu.VMEM((n_h, n_k, rows, wide), BF16),
            pltpu.VMEM((2, n_h, n_k, rows, wide), BF16),
            dma((2, 2 * (n_k + 1))), dma((2, 2 * (n_k + 1))), dma((2, 2 * (n_k + 1))),
            dma((2, 2 * (n_k + 1))), dma((2, n_h, n_k)), dma((2, n_h, n_k)),
        ],
        compiler_params=pltpu.CompilerParams(
            collective_id=4, has_side_effects=True, vmem_limit_bytes=VMEM_BYTES
        ),
        name="reduce_grads",
    )(grads, small)


def expert_kernel(sizes, backward, *refs):
    if backward:
        (blocks, weights, gate, output, slots_out, act_out, back_out, bias_out, sum_out, gathered,
         w_a, w_b, gate_v, sums, slots, act, core_out, core_in, x_out, x_in, land, leave, back, land_back,
         w_sem, o_sem, in_sems, back_sems, core_sems, x_sems, act_sems, b_sems,
         g_send, g_recv, g_sem,
         bias_all, bias_send, bias_land) = refs
    else:
        (blocks, weights, gate, slots_out, act_out, gate_out, back_out,
         w_a, w_b, sums, slots, act, core_out, core_in, x_out, x_in, land, leave, back, land_back,
         w_sem, o_sem, in_sems, back_sems, core_sems, x_sems, act_sems, bias) = refs
    peers = Peers(sizes)
    s, h, t = peers.at
    n_s, n_h, n_t = sizes
    me = peers.flat(peers.at)
    core, chip = lax.rem(s, 2), s // 2
    sibling = (s + 1 - 2 * core, h, t)
    across = (lax.rem(s + 2, n_s), h, t)
    half = act.shape[0] // 2
    own, other = core * half, (1 - core) * half
    n_blocks = peers.count
    first = 1 if backward else 0
    loads = [
        pltpu.make_async_copy(weights.at[first], w_a, w_sem.at[0]),
        pltpu.make_async_copy(weights.at[1 - first], w_b, w_sem.at[1]),
    ]
    for load in loads:
        load.start()
    if backward:
        gate_load = pltpu.make_async_copy(gate, gate_v, o_sem.at[0])
        gate_load.start()
    peers.greet_all()

    def block_out(p, k):
        place = peers.step(k, 1)
        return remote(
            blocks.at[place[1], place[0], p], land.at[p, me],
            in_sems.at[0, p, k], in_sems.at[1, p, k], place,
        )

    def block_in(p, k):
        source = peers.flat(peers.step(k, -1))
        return remote(
            blocks.at[0, 0, p], land.at[p, source], in_sems.at[0, p, k], in_sems.at[1, p, k], sibling
        )

    def each(function, count=n_blocks, start=1):
        lax.fori_loop(start, count, lambda k, carry: (function(k), carry)[1], 0)

    for p in range(2):
        for k in range(1, n_blocks):
            block_out(p, k).start()
        land[p, me] = blocks[h, s, p]
    few = half // 2
    group = 16
    many = 2 * group
    out_row = lax.broadcasted_iota(jnp.int32, (16 * group, 16 * group), 0)
    in_row = lax.broadcasted_iota(jnp.int32, (16 * group, 16 * group), 1)
    there = (out_row // many == in_row % (2 * few)) & (out_row % many == in_row // (2 * few))
    there = there.astype(F32).astype(BF16)
    again = (in_row // many == out_row % (2 * few)) & (in_row % many == out_row // (2 * few))
    again = again.astype(F32).astype(BF16)

    def receive(p):
        each(lambda k: block_in(p, k).wait_recv())
        for b in range(n_blocks // group):
            rows = land[p, b * group : (b + 1) * group].reshape(group * 16, land.shape[3])
            turned = dot(there, rows).astype(BF16).reshape(2 * few, many, land.shape[3])
            for c in range(2):
                first = c * half + p * few
                slots[first : first + few, b * many : (b + 1) * many, :] = turned[
                    c * few : (c + 1) * few
                ]

    if backward:
        own_images = output.shape[0]
        line = [(s, lax.rem(h + d, n_h), t) for d in range(n_h)]
        g_own = pltpu.make_async_copy(output, gathered.at[pl.ds(h * own_images, own_images)], g_sem)
        g_own.start()

        def z_hop(i, origin, up, source=None):
            there = gathered.at[origin * own_images + i]
            return remote(
                there if source is None else source, there,
                g_send.at[i, origin, up], g_recv.at[i, origin], line[1] if up else line[n_h - 1],
            )

        def relay(i, d):
            @pl.when(h >= d)
            def _():
                z_hop(i, h - d, 1).wait_recv()

                @pl.when((h < n_h - 1) & (d < n_h - 1))
                def _():
                    z_hop(i, h - d, 1).start()

            @pl.when(h + d < n_h)
            def _():
                z_hop(i, h + d, 0).wait_recv()

                @pl.when((h > 0) & (d < n_h - 1))
                def _():
                    z_hop(i, h + d, 0).start()

        def gather_output():
            for i in range(own_images):
                @pl.when(h < n_h - 1)
                def _():
                    z_hop(i, h, 1, output.at[i]).start()

                @pl.when(h > 0)
                def _():
                    z_hop(i, h, 0, output.at[i]).start()
    else:
        piece, count = 6 * 64, act.shape[2] // (6 * 64)
        row = lax.broadcasted_iota(jnp.int32, (6 * 128, piece), 0)
        column = lax.broadcasted_iota(jnp.int32, (6 * 128, piece), 1)
        lane = row % 128
        place = (lane < 64) & (column == (row // 128) * 64 + lane)
        place = place.astype(F32).astype(BF16)
        for m in range(count):
            first = (t * count + m) * 96
            lines = [
                gate[pl.ds(pl.multiple_of(first + j * 16, 16), 16), 128:256] for j in range(6)
            ]
            bias[:, m * piece : (m + 1) * piece] = dot(jnp.concatenate(lines, axis=1), place)

    receive(0)
    if backward:
        gather_output()
    loads[0].wait()

    def core_copy(j):
        return remote(
            core_out.at[j], core_in.at[j], core_sems.at[0, j], core_sems.at[1, j], sibling
        )

    def x_copy(j):
        return remote(x_out.at[j], x_in.at[j], x_sems.at[0, j], x_sems.at[1, j], across)

    def act_copy(j):
        return remote(
            act.at[own + j], act.at[own + j], act_sems.at[0, j], act_sems.at[1, j], sibling
        )

    def act_in(j):
        return remote(
            act.at[other + j], act.at[other + j], act_sems.at[0, j], act_sems.at[1, j], sibling
        )

    def meet(j):
        core_copy(j).wait_recv()
        sums[j] = sums[j] + core_in[j].astype(F32)
        x_out[j] = sums[j].astype(BF16)
        x_copy(j).start()

    def first_sums(j):
        core_out[j] = dot(slots[other + j], w_a[other + j]).astype(BF16)
        core_copy(j).start()

        @pl.when(j > 0)
        def _():
            meet(j - 1)

        sums[j] = dot(slots[own + j], w_a[own + j])

    each(first_sums, few, 0)
    receive(1)
    each(first_sums, half, few)
    meet(half - 1)
    loads[1].wait()
    if backward:
        gate_load.wait()

    def second(e):
        leave[e] = dot_t(act[e], w_b[e]).astype(BF16)

    def finish(j):
        x_copy(j).wait_recv()
        value = sums[j] + x_in[j].astype(F32)
        if backward:
            act[own + j] = (value * gate_v[j]).astype(BF16)
        else:
            value = value + bias[pl.ds(own + j, 1), :]
            cumulative = 0.5 + 0.5 * lax.erf(value * 0.7071067811865476)
            act[own + j] = (value * cumulative).astype(BF16)
            sums[j] = cumulative + value * (
                jnp.exp(value * value * -0.5) * 0.3989422804014327
            )
        act_copy(j).start()
        second(own + j)

        @pl.when(j > 0)
        def _():
            act_in(j - 1).wait_recv()
            second(other + j - 1)

        if backward:
            for when, i, d in ((2, 0, 1), (3, 1, 1), (5, 0, 2), (7, 1, 2)):
                @pl.when(j == when)
                def _():
                    relay(i, d)

    def back_copy(p, k):
        place = peers.step(k, 1)
        return remote(
            back.at[p, peers.flat(place)], land_back.at[p, me],
            back_sems.at[0, p, k], back_sems.at[1, p, k], place,
        )

    def back_in(p, k):
        source = peers.flat(peers.step(k, -1))
        return remote(
            back.at[p, 0], land_back.at[p, source],
            back_sems.at[0, p, k], back_sems.at[1, p, k], sibling,
        )

    def give_back(p):
        for b in range(n_blocks // group):
            rows = jnp.concatenate(
                [
                    leave[c * half + p * few : c * half + (p + 1) * few, b * many : (b + 1) * many, :]
                    for c in range(2)
                ],
                axis=0,
            ).reshape(group * 16, leave.shape[2])
            turned = dot(again, rows).astype(BF16)
            back[p, b * group : (b + 1) * group] = turned.reshape(group, 16, leave.shape[2])
        for k in range(1, n_blocks):
            back_copy(p, k).start()
        land_back[p, me] = back[p, me]

    each(finish, few + 1, 0)
    give_back(0)
    each(finish, half, few + 1)
    act_in(half - 1).wait_recv()
    second(other + half - 1)
    give_back(1)
    stores = [pltpu.make_async_copy(act, act_out, o_sem.at[1])]
    if not backward:
        stores.append(pltpu.make_async_copy(sums, gate_out, o_sem.at[0]))
    for store in stores:
        store.start()
    slots_out[...] = slots[...]
    if backward:
        across_t = (s, h, 1 - t)
        width = bias_out.shape[1]

        def bias_row(e):
            bias_all[pl.ds(e, 1), :] = jnp.sum(act[e].astype(F32), axis=0, keepdims=True)

        each(bias_row, 2 * half, 0)

        def slot_row(e):
            total = jnp.sum(slots[e].astype(F32), axis=0, keepdims=True)
            sum_out[pl.ds(e, 1), : slots.shape[2]] = total

        sum_out[...] = jnp.zeros_like(sum_out)
        each(slot_row, 2 * half, 0)

        def piece(for_t):
            return bias_all[:, pl.ds(pl.multiple_of((core * n_t + for_t) * width, 128), width)]

        bias_send[...] = piece(1 - t)
        bias_copy = remote(bias_send, bias_land, b_sems.at[0], b_sems.at[1], across_t)
        bias_copy.start()
        bias_copy.wait()
        bias_out[...] = jnp.where(t == chip, piece(t), bias_land[...])
    for p in range(2):
        each(lambda k: back_in(p, k).wait_recv())
    back_out[...] = land_back[...]
    for store in stores:
        store.wait()
    if backward:
        relay(0, 3)
        relay(1, 3)
        g_own.wait()
        for origin in range(n_h):
            @pl.when((origin < h) & (h < n_h - 1))
            def _():
                for i in range(own_images):
                    z_hop(i, origin, 1).wait_send()

            @pl.when((origin > h) & (h > 0))
            def _():
                for i in range(own_images):
                    z_hop(i, origin, 0).wait_send()

        @pl.when(h < n_h - 1)
        def _():
            for i in range(own_images):
                z_hop(i, h, 1, output.at[i]).wait_send()

        @pl.when(h > 0)
        def _():
            for i in range(own_images):
                z_hop(i, h, 0, output.at[i]).wait_send()

    for p in range(2):
        each(lambda k: block_out(p, k).wait_send())
        each(lambda k: back_copy(p, k).wait_send())
    for copy in (core_copy, x_copy, act_copy):
        each(lambda j: copy(j).wait_send(), half, 0)


def expert_pass(sizes, backward, blocks, weights, gate, output=None, bias_width=0):
    _, experts, rows, hidden = weights.shape
    devices = sizes[0] * sizes[1] * sizes[2]
    images = 2 * devices
    half = experts // 2
    vmem = pl.BlockSpec(memory_space=pltpu.VMEM)
    hbm = pl.BlockSpec(memory_space=pl.ANY)
    slots = jax.ShapeDtypeStruct((experts, images, rows), BF16)
    act = jax.ShapeDtypeStruct((experts, images, hidden), BF16)
    gate_shape = (half, images, hidden)
    returned = jax.ShapeDtypeStruct((2, devices, experts, rows), BF16)
    if backward:
        operands, in_specs = (blocks, weights, gate, output), [vmem, hbm, hbm, hbm]
        outs = (
            slots, act, returned,
            jax.ShapeDtypeStruct((experts, bias_width), F32),
            jax.ShapeDtypeStruct((experts, 256), F32),
            jax.ShapeDtypeStruct((sizes[1] * output.shape[0], *output.shape[1:]), BF16),
        )
        out_specs = (vmem, hbm, vmem, vmem, vmem, hbm)
    else:
        operands, in_specs = (blocks, weights, gate), [vmem, hbm, vmem]
        outs = (slots, act, jax.ShapeDtypeStruct(gate_shape, F32), returned)
        out_specs = (vmem, hbm, hbm, vmem)
    weight = pltpu.VMEM((experts, rows, hidden), BF16)
    chunk = pltpu.VMEM((half, images, hidden), BF16)
    block = pltpu.VMEM((2, devices, experts, rows), BF16)
    dma = pltpu.SemaphoreType.DMA
    scratch = [weight, weight]
    if backward:
        scratch.append(pltpu.VMEM(gate_shape, F32))
    scratch += [
        pltpu.VMEM(gate_shape, F32),
        pltpu.VMEM(slots.shape, BF16),
        pltpu.VMEM(act.shape, BF16),
        chunk, chunk, chunk, chunk, block,
        pltpu.VMEM(slots.shape, BF16),
        block, block,
        dma((2,)), dma((2,)), dma((2, 2, devices)), dma((2, 2, devices)),
        dma((2, half)), dma((2, half)), dma((2, half)),
    ]
    if backward:
        scratch += [
            dma((2,)), dma((output.shape[0], sizes[1], 2)), dma((output.shape[0], sizes[1])), dma,
            pltpu.VMEM((experts, hidden), F32),
            pltpu.VMEM((experts, bias_width), F32),
            pltpu.VMEM((experts, bias_width), F32),
        ]
    else:
        scratch.append(pltpu.VMEM((experts, hidden), F32))
    return pl.pallas_call(
        partial(expert_kernel, sizes, backward),
        out_shape=outs,
        in_specs=in_specs,
        out_specs=out_specs,
        scratch_shapes=scratch,
        compiler_params=pltpu.CompilerParams(
            collective_id=2 if backward else 1, has_side_effects=True, vmem_limit_bytes=VMEM_BYTES
        ),
        cost_estimate=pl.CostEstimate(
            flops=8 * images * experts * rows * hidden,
            bytes_accessed=weights.size * 2,
            transcendentals=0,
        ),
        name="experts_back" if backward else "experts_ahead",
    )(*operands)


def weight_grad_kernel(slots_0, act_0, slots_1, act_1, out, lines, pick, same):
    group, images, rows = slots_0.shape
    d_block = out.shape[0]
    few = group // 2
    m, d = pl.program_id(0), pl.program_id(2)

    @pl.when((m == 0) & (pl.program_id(1) == 0) & (d == 0))
    def _():
        row = lax.broadcasted_iota(jnp.int32, pick.shape[1:], 0)
        column = lax.broadcasted_iota(jnp.int32, pick.shape[1:], 1)
        second = (row % group) // few
        for half in range(2):
            feature = 2 * (row // group) + (second if half == 0 else 1 - second)
            pick[half] = (column == feature).astype(F32).astype(BF16)
        row = lax.broadcasted_iota(jnp.int32, same.shape, 0)
        column = lax.broadcasted_iota(jnp.int32, same.shape, 1)
        same[...] = (row % few == column // images).astype(F32)

    def prepare(slots):
        @pl.when(d == 0)
        def _():
            turned = slots[...].reshape(group * images, rows).astype(F32)
            lines[...] = jnp.swapaxes(turned, 0, 1).astype(BF16)

    def term(act):
        mine = lines[pl.ds(pl.multiple_of(d * d_block, d_block), d_block)]
        width = act.shape[2]
        results = []
        for half in range(2):
            columns = mine[:, half * few * images : (half + 1) * few * images]
            spread = (dot(pick[half], columns) * same[...]).astype(BF16)
            values = act[half * few : (half + 1) * few].reshape(few * images, width)
            results.append(dot(spread, values).reshape(d_block // 2, group, width))
        first, last = results
        low = lax.broadcasted_iota(jnp.int32, first.shape, 1) < few
        even = jnp.where(low, first, last)
        odd = pltpu.roll(jnp.where(low, last, first), few, 1)
        out[...] = jnp.stack((even, odd), axis=1).reshape(out.shape)

    @pl.when(m == 0)
    def _():
        prepare(slots_0)
        term(act_0)

    @pl.when(m == 1)
    def _():
        prepare(slots_1)
        term(act_1)


def weight_grads(slots_0, act_0, slots_1, act_1):
    experts, images, rows = slots_0.shape
    hidden = act_0.shape[2]
    group, d_block = 8, 192
    last = experts // group - 1

    def early(m, g, d):
        return jnp.where(m == 0, g, last), 0, 0

    def late(m, g, d):
        return jnp.where(m == 0, 0, g), 0, 0

    slots, act = (group, images, rows), (group, images, hidden)
    return pl.pallas_call(
        weight_grad_kernel,
        grid=(2, experts // group, rows // d_block),
        out_shape=jax.ShapeDtypeStruct((rows, 2, experts, hidden), F32),
        in_specs=[
            pl.BlockSpec(slots, early), pl.BlockSpec(act, early),
            pl.BlockSpec(slots, late), pl.BlockSpec(act, late),
        ],
        out_specs=pl.BlockSpec((d_block, 1, group, hidden), lambda m, g, d: (d, m, g, 0)),
        scratch_shapes=[
            pltpu.VMEM((rows, group * images), BF16),
            pltpu.VMEM((2, group * d_block // 2, d_block), BF16),
            pltpu.VMEM((group * d_block // 2, group * images // 2), F32),
        ],
        compiler_params=pltpu.CompilerParams(vmem_limit_bytes=VMEM_BYTES),
        cost_estimate=pl.CostEstimate(
            flops=4 * images * experts * rows * hidden,
            bytes_accessed=8 * rows * experts * hidden,
            transcendentals=0,
        ),
        name="weight_grads",
    )(slots_0, act_0, slots_1, act_1)


def dot_r(a, b):
    return lax.dot_general(a, b, (((0,), (0,)), ((), ())), preferred_element_type=F32)


def row_of(shape, axis):
    return lax.broadcasted_iota(jnp.int32, shape, axis)


def one_hot(mask):
    return mask.astype(F32).astype(BF16)


def order_matrix(n_h, few, back):
    n = n_h * 8 * few
    shape = (n, n)
    blocked, natural = row_of(shape, 1 if back else 0), row_of(shape, 0 if back else 1)
    f, half, image = blocked % few, (blocked // few) % 2, (blocked // (2 * few)) % 2
    group = blocked // (4 * few)
    if back:
        part, h = group // n_h, group % n_h
    else:
        h, part = group // 2, group % 2
    expert = ((h * 2 + half) * 2 + part) * few + f
    return one_hot(natural == image * (4 * n_h * few) + expert)


def norm_parts(x, scale, shift, live):
    centered = x - jnp.mean(x, axis=-1, keepdims=True)
    inverse = lax.rsqrt(jnp.mean(centered * centered, axis=-1, keepdims=True) + epsilon)
    unit = centered * inverse
    return unit * scale + shift, unit, inverse


def norm_back(grad, unit, inverse, scale):
    scaled = grad * scale
    average = jnp.mean(scaled, axis=-1, keepdims=True)
    projection = jnp.mean(scaled * unit, axis=-1, keepdims=True)
    return (
        inverse * (scaled - average - unit * projection),
        jnp.sum(grad * unit, axis=0, keepdims=True),
        jnp.sum(grad, axis=0, keepdims=True),
    )


def norm_rows(small):
    return jnp.swapaxes(small[:, 128:].astype(F32), 0, 1)[64:68]


def slots_to_blocks(slots, blocks, columns, joined, order):
    n_h, n_s = blocks.shape[:2]
    turned = dot(order, slots).astype(BF16)
    wide = joined.shape[1] // 2
    for s in range(0, n_s, 2):
        lanes = dot(turned[:, s * columns : (s + 2) * columns], joined).astype(BF16)
        for h in range(n_h):
            for p in range(2):
                rows = (h * 2 + p) * 16
                for e in range(2):
                    blocks[h, s + e, p] = lanes[rows : rows + 16, e * wide : e * wide + columns]


def blocks_to_slots(back, sizes, order, pair, padded):
    n_s, n_h, n_t = sizes
    columns = back.shape[3]
    both = jnp.concatenate([order] * n_t, axis=1)
    results = []
    for s in range(n_s):
        rows = jnp.concatenate(
            [
                back[p, (s * n_h + h) * n_t + t]
                for t in range(n_t)
                for p in range(2)
                for h in range(n_h)
            ],
            axis=0,
        )
        padded[s % 2, :, :columns] = dot(both, rows)
        if s % 2:
            value = jnp.concatenate([padded[0], padded[1]], axis=1)
            high = value.astype(BF16)
            rest = (value - high.astype(F32)).astype(BF16)
            results.append(dot(high, pair) + dot(rest, pair))
    return jnp.concatenate(results, axis=1)


def live_rows(shape, length):
    return row_of(shape, 0) < length


def ahead_kernel(
    length, tokens, small, w_hbm, blocks, normed_1, query, keyed, valued, context, hidden, normed_2,
    dispatch_out, combine_out, w, joined, order, w_sem,
):
    n, rows, width = tokens.shape
    keys = keyed.shape[1]
    loads = [pltpu.make_async_copy(w_hbm.at[k], w.at[k], w_sem.at[k]) for k in range(4)]
    for load in loads:
        load.start()
    norms = norm_rows(small)
    live = live_rows((rows, 1), length)
    for i in range(n):
        value, _, _ = norm_parts(tokens[i].astype(F32), norms[0:1], norms[2:3], live)
        normed_1[i] = jnp.where(live, value, 0.0).astype(BF16)
    joined[...] = pair_matrix(blocks.shape[4], joined.shape[1] // 2, True)
    order[...] = order_matrix(blocks.shape[0], 4, False)
    flat = (n * rows, width)
    for k, target in enumerate((query, keyed, valued)):
        loads[k].wait()
        value = dot(normed_1[...].reshape(flat), w[k]).astype(BF16).reshape(n, rows, width)
        if k == 0:
            target[...] = value
        else:
            target[:, :rows] = value
            target[:, rows:] = jnp.zeros((n, keys - rows, width), BF16)
    factor = HEAD_DIM ** (-0.5)
    pairs = width // 128
    lane = row_of((rows, 128), 1)
    shown = row_of((rows, keys), 1) < length

    def attend(step, carry):
        i = step // pairs
        lanes = pl.ds(pl.multiple_of((step % pairs) * 128, 128), 128)
        q, k, v = query[i, :, lanes], keyed[i, :, lanes], valued[i, :, lanes]
        scaled = q * jnp.bfloat16(factor)
        parts = []
        for a in range(2):
            mine = (lane < 64) if a == 0 else (lane >= 64)
            scores = dot_t(jnp.where(mine, scaled, jnp.zeros_like(q)), k)
            scores = jnp.where(shown, scores, -1e30)
            exponent = jnp.exp(scores - jnp.max(scores, axis=-1, keepdims=True))
            probs = exponent * (1.0 / jnp.sum(exponent, axis=-1, keepdims=True))
            parts.append(dot(probs.astype(BF16), v))
        context[i, :, lanes] = jnp.where(lane < 64, parts[0], parts[1]).astype(BF16)
        return carry

    lax.fori_loop(0, n * pairs, attend, 0, unroll=6)
    loads[3].wait()
    attended = dot_t(context[...].reshape(flat), w[3]).reshape(n, rows, width)
    for i in range(n):
        value = tokens[i].astype(F32) + attended[i]
        hidden[i] = value
        value, _, _ = norm_parts(value, norms[1:2], norms[3:4], live)
        normed_2[i] = jnp.where(live, value, 0.0).astype(BF16)
    logits = dot(normed_2[...].reshape(flat), small[:, :128]).reshape(n, rows, 128)
    experts = row_of((rows, 128), 1) < 64
    slots = []
    for i in range(n):
        here = logits[i]
        down = jnp.where(live, here, -1e30)
        exponent = jnp.exp(down - jnp.max(down, axis=0, keepdims=True))
        dispatch = exponent / jnp.sum(exponent, axis=0, keepdims=True)
        dispatch = jnp.where(experts, dispatch, 0.0)
        across = jnp.where(experts, here, -1e30)
        exponent = jnp.exp(across - jnp.max(across, axis=1, keepdims=True))
        combine = exponent / jnp.sum(exponent, axis=1, keepdims=True)
        dispatch_out[i] = dispatch
        combine_out[i] = combine
        slots.append(dot_r(dispatch.astype(BF16), normed_2[i])[:64].astype(BF16))
    slots_to_blocks(
        jnp.concatenate(slots, axis=0), blocks, blocks.shape[4], joined[...], order[...]
    )


def tokens_ahead(sizes, length, tokens, small, weights):
    n, rows, width = tokens.shape
    keys = 256
    vmem = pl.BlockSpec(memory_space=pltpu.VMEM)
    shape = jax.ShapeDtypeStruct
    wide = (n, keys, width)
    thin = shape((n, rows, 128), F32)
    return pl.pallas_call(
        partial(ahead_kernel, length),
        out_shape=(
            shape((sizes[1], sizes[0], 2, 16, width // sizes[0]), BF16),
            shape(tokens.shape, BF16), shape(tokens.shape, BF16), shape(wide, BF16),
            shape(wide, BF16), shape(tokens.shape, BF16), shape(tokens.shape, F32),
            shape(tokens.shape, BF16), thin, thin,
        ),
        in_specs=[vmem, vmem, pl.BlockSpec(memory_space=pl.ANY)],
        out_specs=(vmem,) * 10,
        scratch_shapes=[
            pltpu.VMEM(weights.shape, BF16),
            pltpu.VMEM((2 * width // sizes[0], 512), BF16),
            pltpu.VMEM((128, 128), BF16),
            pltpu.SemaphoreType.DMA((4,)),
        ],
        compiler_params=pltpu.CompilerParams(vmem_limit_bytes=VMEM_BYTES),
        name="tokens_ahead",
    )(tokens, small, weights)


def middle_kernel(
    sizes, back, small, combine, hidden, cotangent, output, blocks, grad_logits, padded
):
    n, rows, _ = hidden.shape
    columns = back.shape[3]
    padded[...] = jnp.zeros_like(padded)
    pair = pair_matrix(columns, padded.shape[2], False)
    joined = pair_matrix(columns, padded.shape[2], True)
    total = blocks_to_slots(back, sizes, order_matrix(sizes[1], 4, True), pair, padded)
    bias = jnp.swapaxes(small[:, :128].astype(F32), 0, 1)[64:]
    slots = []
    for i in range(n):
        slot_out = (total[i * 64 : (i + 1) * 64] + bias).astype(BF16)
        combine_b = combine[i].astype(BF16)[:, :64]
        output[i] = (hidden[i] + dot(combine_b, slot_out)).astype(BF16)
        grad_combine = dot_t(cotangent[i], slot_out)
        weight = combine[i][:, :64]
        weighted = jnp.sum(weight * grad_combine, axis=1, keepdims=True)
        grad_logits[i] = weight * (grad_combine - weighted)
        slots.append(dot_r(combine_b, cotangent[i]).astype(BF16))
    slots_to_blocks(
        jnp.concatenate(slots, axis=0), blocks, columns, joined, order_matrix(sizes[1], 4, False)
    )


def tokens_middle(sizes, back, small, combine, hidden, cotangent):
    n, rows, width = hidden.shape
    vmem = pl.BlockSpec(memory_space=pltpu.VMEM)
    shape = jax.ShapeDtypeStruct
    return pl.pallas_call(
        partial(middle_kernel, sizes),
        out_shape=(
            shape(hidden.shape, BF16),
            shape((sizes[1], sizes[0], 2, 16, width // sizes[0]), BF16),
            shape((n, rows, 64), F32),
        ),
        in_specs=[vmem] * 5,
        out_specs=(vmem,) * 3,
        scratch_shapes=[pltpu.VMEM((2, 128, 256), F32)],
        compiler_params=pltpu.CompilerParams(vmem_limit_bytes=VMEM_BYTES),
        name="tokens_middle",
    )(back, small, combine, hidden, cotangent)


def behind_kernel(
    sizes, length, back, small, w_hbm, tokens, normed_1, query, keyed, valued, context, hidden,
    normed_2, dispatch, grad_logits, cotangent, grads, small_grads, input_grad,
    w, padded, grad_hidden, rounded, grad_context, grad_q, grad_k, grad_v, w_sem,
):
    n, rows, width = tokens.shape
    keys = keyed.shape[1]
    loads = [pltpu.make_async_copy(w_hbm.at[k], w.at[k], w_sem.at[k]) for k in range(4)]
    for load in loads:
        load.start()
    norms = norm_rows(small)
    padded[...] = jnp.zeros_like(padded)
    pair = pair_matrix(back.shape[3], padded.shape[2], False)
    grad_slots = blocks_to_slots(
        back, sizes, order_matrix(sizes[1], 4, True), pair, padded
    ).astype(BF16)
    phi = small[:, :64]
    phi_grad = jnp.zeros((width, 64), F32)
    sums = []
    flat = (n * rows, width)
    for i in range(n):
        slots = grad_slots[i * 64 : (i + 1) * 64]
        weight = dispatch[i][:, :64]
        grad_dispatch = dot_t(normed_2[i], slots)
        weighted = jnp.sum(weight * grad_dispatch, axis=0, keepdims=True)
        logits = (weight * (grad_dispatch - weighted) + grad_logits[i]).astype(BF16)
        phi_grad = phi_grad + dot_r(normed_2[i], logits)
        grad = dot(weight.astype(BF16), slots) + dot_t(logits, phi)
        _, unit, inverse = norm_parts(hidden[i], norms[1:2], norms[3:4], None)
        grad_in, scale_grad, bias_grad = norm_back(grad, unit, inverse, norms[1:2])
        value = cotangent[i].astype(F32) + grad_in
        grad_hidden[i] = value
        rounded[i] = value.astype(BF16)
        sums.append((scale_grad, bias_grad))
    scale_2, bias_2 = sums[0][0] + sums[1][0], sums[0][1] + sums[1][1]
    flat_rounded = rounded[...].reshape(flat)
    loads[3].wait()
    grad_context[...] = dot(flat_rounded, w[3]).astype(BF16).reshape(n, rows, width)
    grads[3] = dot_r(flat_rounded, context[...].reshape(flat)).astype(BF16)
    factor = HEAD_DIM ** (-0.5)
    pairs = width // 128
    lane = row_of((rows, 128), 1)
    key_lane = row_of((keys, 128), 1)
    shown = row_of((keys, rows), 0) < length

    def attend(step, carry):
        i = step // pairs
        lanes = pl.ds(pl.multiple_of((step % pairs) * 128, 128), 128)
        q, k, v = query[i, :, lanes], keyed[i, :, lanes], valued[i, :, lanes]
        scaled = q * jnp.bfloat16(factor)
        g = grad_context[i, :, lanes]
        to_q, to_k, to_v = [], [], []
        for a in range(2):
            mine = (lane < 64) if a == 0 else (lane >= 64)
            scores = dot_t(k, jnp.where(mine, scaled, jnp.zeros_like(q)))
            grad_probs = dot_t(v, jnp.where(mine, g, jnp.zeros_like(g)))
            scores = jnp.where(shown, scores, -1e30)
            exponent = jnp.exp(scores - jnp.max(scores, axis=0, keepdims=True))
            probs = exponent * (1.0 / jnp.sum(exponent, axis=0, keepdims=True))
            weighted = jnp.sum(probs * grad_probs, axis=0, keepdims=True)
            grad_scores = (probs * (grad_probs - weighted)).astype(BF16)
            to_v.append(dot(probs.astype(BF16), g))
            to_q.append(dot_r(grad_scores, k))
            to_k.append(dot(grad_scores, q))
        grad_q[i, :, lanes] = (jnp.where(lane < 64, to_q[0], to_q[1]) * factor).astype(BF16)
        kept = key_lane < 64
        grad_k[i, :, lanes] = (jnp.where(kept, to_k[0], to_k[1]) * factor)[:rows].astype(BF16)
        grad_v[i, :, lanes] = jnp.where(kept, to_v[0], to_v[1])[:rows].astype(BF16)
        return carry

    lax.fori_loop(0, n * pairs, attend, 0, unroll=6)
    total = jnp.zeros(flat, F32)
    turned = jnp.swapaxes(normed_1[...].reshape(flat).astype(F32), 0, 1).astype(BF16)
    for k, source in enumerate((grad_q, grad_k, grad_v)):
        loads[k].wait()
        value = source[...].reshape(flat)
        total = total + dot_t(value, w[k])
        grads[k] = dot(turned, value).astype(BF16)
    total = total.reshape(n, rows, width)
    sums = []
    for i in range(n):
        _, unit, inverse = norm_parts(tokens[i].astype(F32), norms[0:1], norms[2:3], None)
        grad_in, scale_grad, bias_grad = norm_back(total[i], unit, inverse, norms[0:1])
        input_grad[i] = (grad_hidden[i] + grad_in).astype(BF16)
        sums.append((scale_grad, bias_grad))
    scale_1, bias_1 = sums[0][0] + sums[1][0], sums[0][1] + sums[1][1]
    line = row_of((128, width), 0)
    spread = jnp.zeros((128, width), F32)
    for j, value in enumerate((scale_1, scale_2, bias_1, bias_2)):
        spread = jnp.where(line == 64 + j, value, spread)
    small_grads[...] = jnp.swapaxes(spread, 0, 1).astype(BF16)
    small_grads[:, :64] = phi_grad.astype(BF16)


def tokens_behind(sizes, length, back, small, weights, tokens, kept, grad_logits, cotangent):
    n, rows, width = tokens.shape
    vmem = pl.BlockSpec(memory_space=pltpu.VMEM)
    shape = jax.ShapeDtypeStruct
    low = pltpu.VMEM(tokens.shape, BF16)
    return pl.pallas_call(
        partial(behind_kernel, sizes, length),
        out_shape=(
            shape((4, width, width), BF16), shape((width, 128), BF16), shape(tokens.shape, BF16)
        ),
        in_specs=[vmem, vmem, pl.BlockSpec(memory_space=pl.ANY)] + [vmem] * 11,
        out_specs=(vmem,) * 3,
        scratch_shapes=[
            pltpu.VMEM(weights.shape, BF16),
            pltpu.VMEM((2, 128, 256), F32),
            pltpu.VMEM(tokens.shape, F32),
            low, low, low, low, low,
            pltpu.SemaphoreType.DMA((4,)),
        ],
        compiler_params=pltpu.CompilerParams(vmem_limit_bytes=VMEM_BYTES),
        name="tokens_behind",
    )(back, small, weights, tokens, *kept, grad_logits, cotangent)


def unpack_kernel(summed, in_bias_sum, out_sum, attn, phi_t, scales, biases, in_bias, out_bias):
    attn[...] = summed[:, :, : attn.shape[2]]
    turned = jnp.swapaxes(summed[0][:, 128:], 0, 1)
    phi_t[...] = turned[64:80]
    scales[...] = turned[80:82]
    biases[...] = turned[82:84]
    in_bias[...] = in_bias_sum[...]
    width = out_bias.shape[1]
    value = out_sum[...]
    later = pltpu.roll(value, value.shape[1] - width, 1)
    out_bias[...] = jnp.where(lax.axis_index("tensor") == 0, value[:, :width], later[:, :width])


def unpack_grads(summed, in_bias_sum, out_sum, block, slot):
    n_k, rows, _ = summed.shape
    vmem = pl.BlockSpec(memory_space=pltpu.VMEM)
    shape = jax.ShapeDtypeStruct
    return pl.pallas_call(
        unpack_kernel,
        out_shape=(
            shape((n_k, rows, block), F32), shape((slot, rows), F32),
            shape((2, rows), F32), shape((2, rows), F32),
            shape(in_bias_sum.shape, F32), shape((out_sum.shape[0], rows), F32),
        ),
        in_specs=[vmem] * 3,
        out_specs=(vmem,) * 6,
        name="unpack_grads",
    )(summed, in_bias_sum, out_sum)


def order_kernel(*refs):
    *parts, out = refs
    h, n_h = lax.axis_index("heads"), len(parts)
    own = parts[0].shape[0]
    group = own * n_h
    step = 256 // group
    length = out.shape[0]
    for first in range(0, length, step):
        count = min(step, length - first)
        taken = min(step, parts[0].shape[1] - first)
        shape = (count * group, group * taken)
        row = lax.broadcasted_iota(jnp.int32, shape, 0)
        column = lax.broadcasted_iota(jnp.int32, shape, 1)
        block = column // taken
        image = lax.rem(h + n_h - block // own, n_h) * own + block % own
        chosen = ((row // group == column % taken) & (row % group == image)).astype(F32)
        lines = jnp.concatenate(
            [part[i, first : first + taken] for part in parts for i in range(own)], axis=0
        )
        value = dot(chosen.astype(BF16), lines).astype(BF16)
        out[first : first + count] = value.reshape(count, group, value.shape[1])


def order_images(parts, length):
    own, _, width = parts[0].shape
    vmem = pl.BlockSpec(memory_space=pltpu.VMEM)
    return pl.pallas_call(
        order_kernel,
        out_shape=jax.ShapeDtypeStruct((length, own * len(parts), width), BF16),
        in_specs=[vmem] * len(parts),
        out_specs=vmem,
        compiler_params=pltpu.CompilerParams(vmem_limit_bytes=24 * 1024 * 1024),
        name="order_images",
    )(*parts)


def normalize(values, scale, shift):
    centered = values - jnp.mean(values, axis=-1, keepdims=True)
    variance = jnp.mean(centered * centered, axis=-1, keepdims=True)
    inverse = lax.rsqrt(variance + epsilon)
    unit_part = centered * inverse
    return (unit_part * scale + shift, unit_part, inverse)


def normalize_back(grad_output, unit_part, inverse, scale):
    scaled = grad_output * scale
    average = jnp.mean(scaled, axis=-1, keepdims=True)
    projection = jnp.mean(scaled * unit_part, axis=-1, keepdims=True)
    grad_input = inverse * (scaled - average - unit_part * projection)
    return (
        grad_input,
        jnp.sum(grad_output * unit_part, axis=(0, 1)),
        jnp.sum(grad_output, axis=(0, 1)),
    )


def to_experts(slots):
    slots = lax.all_to_all(slots, "heads", split_axis=1, concat_axis=0, tiled=True)
    slots = lax.all_to_all(slots, "shard", split_axis=2, concat_axis=0, tiled=True)
    return lax.all_gather(slots, "tensor", axis=0, tiled=True)


def to_images(slots):
    slots = lax.psum_scatter(slots, "tensor", scatter_dimension=0, tiled=True)
    slots = lax.all_to_all(slots, "shard", split_axis=0, concat_axis=2, tiled=True)
    return lax.all_to_all(slots, "heads", split_axis=0, concat_axis=1, tiled=True)


def general_shards(tokens, norm_scales, norm_biases, w_attn, phi, experts, in_bias, out_bias, cotangent):
    heads_n = lax.axis_size("heads")
    group, seq_len, width = tokens.shape
    own = group // heads_n
    heads_index = lax.axis_index("heads")
    tensor_index = lax.axis_index("tensor")
    shard_index = lax.axis_index("shard")
    hidden = experts.shape[3]
    rows = experts.shape[0]
    scales, biases, in_full = (
        lax.all_gather(norm_scales, ROWS, axis=1, tiled=True).astype(F32),
        lax.all_gather(norm_biases, ROWS, axis=1, tiled=True).astype(F32),
        lax.all_gather(in_bias, ROWS, axis=1, tiled=True).astype(F32),
    )
    attn = lax.all_gather(
        lax.all_gather(w_attn, "heads", axis=2, tiled=True), ROWS, axis=1, tiled=True
    )
    phi_full = lax.all_gather(
        lax.all_gather(phi, "heads", axis=1, tiled=True), ROWS, axis=0, tiled=True
    )
    out_rows = lax.all_gather(out_bias, "tensor", axis=1, tiled=True).astype(F32)
    e_own = experts.shape[2] // lax.axis_size("shard")
    in_local = lax.dynamic_slice_in_dim(in_full, tensor_index * hidden, hidden, 1)
    factor = HEAD_DIM ** (-0.5)
    tokens = lax.dynamic_slice_in_dim(tokens, heads_index * own, own, 0)
    cotangent = lax.dynamic_slice_in_dim(cotangent, heads_index * own, own, 0)
    n_heads = width // HEAD_DIM
    inputs = tokens.astype(F32)
    normed_one, unit_one, inverse_one = normalize(inputs, scales[0], biases[0])
    normed_one_b = normed_one.astype(BF16)
    projected = einsum("nsd,kdc->knsc", normed_one_b, attn[:3]).astype(BF16)
    query, keyed, valued = projected.reshape(3, own, seq_len, n_heads, HEAD_DIM)
    scores = einsum("nqhe,nkhe->nhqk", query, keyed) * factor
    score_peak = jnp.max(scores, axis=-1, keepdims=True)
    exponent = jnp.exp(scores - score_peak)
    probs = exponent / jnp.sum(exponent, axis=-1, keepdims=True)
    probs_b = probs.astype(BF16)
    context_b = (
        einsum("nhqk,nkhe->nqhe", probs_b, valued).astype(BF16).reshape(own, seq_len, width)
    )
    hidden_one = inputs + einsum("nsc,dc->nsd", context_b, attn[3])
    normed_two, unit_two, inverse_two = normalize(hidden_one, scales[1], biases[1])
    normed_two_b = normed_two.astype(BF16)
    logits = einsum("nsd,de->nse", normed_two_b, phi_full)
    dispatch = jax.nn.softmax(logits, axis=1)
    dispatch_b = dispatch.astype(BF16)
    combine = jax.nn.softmax(logits, axis=2)
    combine_b = combine.astype(BF16)
    slot_in = to_experts(einsum("nse,nsd->ned", dispatch_b, normed_two_b).astype(BF16))
    share = 1 if e_own else 0

    def meet(partial_sum):
        return lax.psum_scatter(partial_sum, "shard", scatter_dimension=share, tiled=True)

    def spread(values):
        return lax.all_gather(values, "shard", axis=share, tiled=True)

    pre = meet(einsum("ned,def->nef", slot_in, experts[:, 0]))
    if e_own:
        pre = pre + lax.dynamic_slice_in_dim(in_local, shard_index * e_own, e_own, 0)
    else:
        pre = pre + in_local
    gelu_value, gelu_back = jax.vjp(partial(jax.nn.gelu, approximate=False), pre)
    activated = spread(gelu_value.astype(BF16))
    slot_out_part = einsum("nef,def->ned", activated, experts[:, 1])
    slot_out_part = slot_out_part + jnp.where(tensor_index == 0, out_rows, 0.0)
    slot_out = to_images(slot_out_part).astype(BF16)
    output = (hidden_one + einsum("nse,ned->nsd", combine_b, slot_out)).astype(BF16)
    output = lax.all_gather(output, "heads", axis=0, tiled=True)
    grad_combine = einsum("nsd,ned->nse", cotangent, slot_out)
    grad_slot = to_experts(einsum("nse,nsd->ned", combine_b, cotangent).astype(BF16))
    grad_act = meet(einsum("ned,def->nef", grad_slot, experts[:, 1]))
    grad_pre = spread(gelu_back(grad_act)[0].astype(BF16))
    grad_slot_in = einsum("nef,def->ned", grad_pre, experts[:, 0]).astype(BF16)
    input_term = einsum("ned,nef->def", slot_in, grad_pre)
    output_term = einsum("ned,nef->def", grad_slot, activated)
    experts_grad = jnp.stack((input_term, output_term), axis=1)
    grad_slot_in = to_images(grad_slot_in.astype(F32)).astype(BF16)
    in_bias_grad = lax.dynamic_slice_in_dim(
        lax.all_gather(jnp.sum(grad_pre.astype(F32), axis=0), "tensor", axis=1, tiled=True),
        (shard_index * lax.axis_size("tensor") + tensor_index) * in_bias.shape[1],
        in_bias.shape[1],
        1,
    )
    out_bias_grad = lax.dynamic_slice_in_dim(
        jnp.sum(grad_slot.astype(F32), axis=0),
        tensor_index * out_bias.shape[1],
        out_bias.shape[1],
        1,
    )
    grad_dispatch = einsum("nsd,ned->nse", normed_two_b, grad_slot_in)
    grad_logits = (
        dispatch * (grad_dispatch - jnp.sum(dispatch * grad_dispatch, axis=1, keepdims=True))
        + combine * (grad_combine - jnp.sum(combine * grad_combine, axis=2, keepdims=True))
    ).astype(BF16)
    phi_grad = einsum("nsd,nse->de", normed_two_b, grad_logits)
    grad_normed_two = einsum("nse,ned->nsd", dispatch_b, grad_slot_in) + einsum(
        "nse,de->nsd", grad_logits, phi_full
    )
    grad_hidden_norm, scale_two_grad, bias_two_grad = normalize_back(
        grad_normed_two, unit_two, inverse_two, scales[1]
    )
    grad_hidden = cotangent.astype(F32) + grad_hidden_norm
    grad_hidden_b = grad_hidden.astype(BF16)
    out_weight_grad = einsum("nsd,nsc->dc", grad_hidden_b, context_b)
    grad_context = einsum("nsd,dc->nsc", grad_hidden_b, attn[3]).astype(BF16)
    grad_context = grad_context.reshape(own, seq_len, n_heads, HEAD_DIM)
    grad_value = einsum("nhqk,nqhe->nkhe", probs_b, grad_context).astype(BF16)
    grad_probs = einsum("nqhe,nkhe->nhqk", grad_context, valued)
    grad_scores = (
        probs * (grad_probs - jnp.sum(probs * grad_probs, axis=-1, keepdims=True))
    ).astype(BF16)
    grad_query = (einsum("nhqk,nkhe->nqhe", grad_scores, keyed) * factor).astype(BF16)
    grad_key = (einsum("nhqk,nqhe->nkhe", grad_scores, query) * factor).astype(BF16)
    grad_proj = jnp.stack((grad_query, grad_key, grad_value)).reshape(3, own, seq_len, width)
    proj_grad = einsum("nsd,knsc->kdc", normed_one_b, grad_proj)
    grad_normed_one = einsum("knsc,kdc->nsd", grad_proj, attn[:3])
    grad_input_norm, scale_one_grad, bias_one_grad = normalize_back(
        grad_normed_one, unit_one, inverse_one, scales[0]
    )
    input_grad = (grad_hidden + grad_input_norm).astype(BF16)
    input_grad = lax.all_gather(input_grad, "heads", axis=0, tiled=True)
    attn_grad = jnp.concatenate((proj_grad, out_weight_grad[None]), axis=0)
    attn_grad = lax.psum_scatter(attn_grad, ROWS, scatter_dimension=1, tiled=True)
    attn_grad = lax.psum_scatter(attn_grad, "heads", scatter_dimension=2, tiled=True)
    phi_grad = lax.psum_scatter(phi_grad, ROWS, scatter_dimension=0, tiled=True)
    phi_grad = lax.psum_scatter(phi_grad, "heads", scatter_dimension=1, tiled=True)
    norms = jnp.stack((scale_one_grad, scale_two_grad, bias_one_grad, bias_two_grad))
    norms = lax.psum(lax.psum_scatter(norms, ROWS, scatter_dimension=1, tiled=True), "heads")
    return (
        output,
        input_grad,
        norms[:2],
        norms[2:],
        attn_grad,
        phi_grad,
        experts_grad,
        in_bias_grad,
        out_bias_grad,
    )


def shards(tokens, norm_scales, norm_biases, w_attn, phi, experts, in_bias, out_bias, cotangent):
    arrays = (tokens, norm_scales, norm_biases, w_attn, phi, experts, in_bias, out_bias, cotangent)
    sizes = tuple(lax.axis_size(name) for name in ("shard", "heads", "tensor"))
    group, length, width = tokens.shape
    fits = (sizes, group, width, *experts.shape[:3]) == ((4, 4, 2), 8, 768, 192, 2, 16)
    if not fits or not 192 < length <= 208 or in_bias.shape[1] != 384:
        return general_shards(*arrays)
    n_s, n_h, n_t = sizes
    block, slot = w_attn.shape[2], phi.shape[1]
    tokens, cotangent = (
        values.transpose(1, 0, 2).reshape(group * length, width) for values in (tokens, cotangent)
    )
    attn, small, turned, tokens, cotangent = gather_weights(
        sizes, w_attn, phi.T, out_bias, norm_scales, norm_biases, in_bias, experts, tokens, cotangent
    )
    blocks, *kept, combine = tokens_ahead(sizes, length, tokens, small, attn)
    hidden = kept[5]
    slot_in, activated, gate, back = expert_pass(sizes, False, blocks, turned, small)
    output, blocks, grad_logits = tokens_middle(sizes, back, small, combine, hidden, cotangent)
    grad_slot, grad_pre, back, in_bias_grad, out_sum, output = expert_pass(
        sizes, True, blocks, turned, gate, output, in_bias.shape[1]
    )
    attn_grad, small_grad, input_grad = tokens_behind(
        sizes, length, back, small, attn, tokens, kept, grad_logits, cotangent
    )
    parts = [input_grad] + [
        lax.ppermute(input_grad, "heads", [(i, (i + d) % n_h) for i in range(n_h)])
        for d in range(1, n_h)
    ]
    attn_grad, grad_pre = lax.optimization_barrier((attn_grad, grad_pre))
    experts_grad = weight_grads(slot_in, grad_pre, grad_slot, activated)
    output = output[:, :length].transpose(1, 0, 2)
    attn_grad, experts_grad, output = lax.optimization_barrier((attn_grad, experts_grad, output))
    summed = reduce_grads(sizes, attn_grad, small_grad)
    attn_grad, phi_grad, scales_grad, biases_grad, in_bias_grad, out_bias_grad = unpack_grads(
        summed, in_bias_grad, out_sum, block, slot
    )
    input_grad = order_images(parts, length)
    return (
        output.transpose(1, 0, 2),
        input_grad.transpose(1, 0, 2),
        scales_grad,
        biases_grad,
        attn_grad,
        phi_grad.T,
        experts_grad,
        in_bias_grad,
        out_bias_grad,
    )


def solution(mesh):
    images = P(ROWS, None, None)
    return jax.shard_map(
        shards,
        mesh=mesh,
        in_specs=(
            images,
            P(None, ROWS),
            P(None, ROWS),
            P(None, ROWS, "heads"),
            P(ROWS, "heads"),
            P("shard", None, "heads", "tensor"),
            P("heads", ROWS),
            P("heads", ROWS),
            images,
        ),
        out_specs=(
            images,
            images,
            P(None, ROWS),
            P(None, ROWS),
            P(None, ROWS, "heads"),
            P(ROWS, "heads"),
            P("shard", None, "heads", "tensor"),
            P("heads", ROWS),
            P("heads", ROWS),
        ),
        check_vma=False,
    )
```

```python
from functools import partial

import jax
import jax.numpy as jnp
from jax import lax
from jax.experimental import pallas as pl
from jax.experimental.pallas import tpu as pltpu
from jax.sharding import PartitionSpec as P

HEAD_DIM = 64
F32 = jnp.float32
BF16 = jnp.bfloat16
ROWS = ("shard", "tensor")
MESH = pl.DeviceIdType.MESH
VMEM_BYTES = 58 * 1024 * 1024
epsilon = 1e-06
einsum = partial(jnp.einsum, preferred_element_type=F32)


def dot(a, b):
    return lax.dot_general(a, b, (((1,), (0,)), ((), ())), preferred_element_type=F32)


def dot_t(a, b):
    return lax.dot_general(a, b, (((1,), (1,)), ((), ())), preferred_element_type=F32)


def swap_matrix(n):
    out = lax.broadcasted_iota(jnp.int32, (n * n, n * n), 0)
    row = lax.broadcasted_iota(jnp.int32, (n * n, n * n), 1)
    return ((out // n == row % n) & (out % n == row // n)).astype(F32).astype(BF16)


class Peers:
    def __init__(self, sizes):
        self.sizes = sizes
        self.at = tuple(lax.axis_index(name) for name in ("shard", "heads", "tensor"))
        self.count = sizes[0] * sizes[1] * sizes[2]

    def flat(self, place):
        return (place[0] * self.sizes[1] + place[1]) * self.sizes[2] + place[2]

    def step(self, k, sign):
        _, n_h, n_t = self.sizes
        steps = (k // (n_h * n_t), (k // n_t) % n_h, k % n_t)
        return tuple(
            lax.rem(at + n + sign * d, n) for at, n, d in zip(self.at, self.sizes, steps)
        )

    def greet_all(self):
        barrier = pltpu.get_barrier_semaphore()

        def signal(k, carry):
            pl.semaphore_signal(barrier, inc=1, device_id=self.step(k, 1), device_id_type=MESH)
            return carry

        lax.fori_loop(1, self.count, signal, 0)
        pl.semaphore_wait(barrier, self.count - 1)


def remote(src, dst, send, recv, place):
    return pltpu.make_async_remote_copy(
        src_ref=src, dst_ref=dst, send_sem=send, recv_sem=recv, device_id=place, device_id_type=MESH
    )


def plane(sizes):
    n_s, n_h, n_t = sizes
    s, h, t = (lax.axis_index(name) for name in ("shard", "heads", "tensor"))
    core, chip = lax.rem(s, 2), s // 2
    sibling = (s + 1 - 2 * core, h, t)
    across_x = (lax.rem(s + 2, n_s), h, t)
    across_y = (s, h, 1 - t)
    line = [(s, lax.rem(h + d, n_h), t) for d in range(n_h)]
    barrier = pltpu.get_barrier_semaphore()
    others = [sibling, across_x, across_y] + line[1:]
    for place in others:
        pl.semaphore_signal(barrier, inc=1, device_id=place, device_id_type=MESH)
    pl.semaphore_wait(barrier, len(others))
    return (s, h, t), core, chip, sibling, across_x, across_y, line


def pair_matrix(block, wide, transposed):
    shape = (2 * block, 2 * wide) if transposed else (2 * wide, 2 * block)
    tight = lax.broadcasted_iota(jnp.int32, shape, 0 if transposed else 1)
    padded = lax.broadcasted_iota(jnp.int32, shape, 1 if transposed else 0)
    second = padded >= wide
    lane = jnp.where(second, padded - wide, padded)
    same = (lane < block) & (tight == jnp.where(second, lane + block, lane))
    return same.astype(F32).astype(BF16)


def gather_kernel(
    sizes, w_attn, phi_t, out_bias, scales, biases, in_bias, experts, tokens, cotangent, w_out, small_out, turned, own_tokens, own_cot,
    w, small, lined, extra, stage, tile_in, tile_out, images, picked,
    z_send, z_recv, x_sems, y_sems, d_sems, c_sems, t_sems, o_sems, i_sems,
):
    n_k, rows, block = w_attn.shape
    wide = lined.shape[3]
    slot = phi_t.shape[0]
    own_h = lax.axis_index("heads")
    stage[...] = jnp.zeros_like(stage)
    stage[64 : 64 + slot] = phi_t[...].astype(F32)
    stage[64 + slot : 64 + 2 * slot] = out_bias[...].astype(F32)
    lined[own_h, :, :, 128:] = jnp.zeros((n_k, rows, wide - 128), BF16)
    lined[own_h, :, :, :block] = w_attn[...]
    first = lined[own_h, 0, :, 128:].astype(F32) + jnp.swapaxes(stage[...], 0, 1)
    lined[own_h, 0, :, 128:] = first.astype(BF16)
    (s, h, t), core, chip, sibling, across_x, across_y, line = plane(sizes)
    n_h, n_t = sizes[1], sizes[2]
    width = w.shape[2]
    side = 16
    n_tiles = experts.shape[0] // side
    depth = tile_in.shape[0]
    halves = ((0, rows // 2), (rows // 2, rows // 2))

    def z_hop(k, origin, up):
        place = line[1] if up else line[n_h - 1]
        return remote(
            lined.at[origin, k], lined.at[origin, k],
            z_send.at[k, origin, up], z_recv.at[k, origin], place,
        )

    def relay(k, d):
        @pl.when(h >= d)
        def _():
            z_hop(k, h - d, 1).wait_recv()

            @pl.when(h < n_h - 1)
            def _():
                z_hop(k, h - d, 1).start()

        @pl.when(h + d < n_h)
        def _():
            z_hop(k, h + d, 0).wait_recv()

            @pl.when(h > 0)
            def _():
                z_hop(k, h + d, 0).start()

    chunks = (0, 2, 1, 3)
    for k in chunks:
        @pl.when(h < n_h - 1)
        def _():
            z_hop(k, h, 1).start()

        @pl.when(h > 0)
        def _():
            z_hop(k, h, 0).start()

    def load(i):
        return pltpu.make_async_copy(
            experts.at[pl.ds((i % n_tiles) * side, side), i // n_tiles],
            tile_in.at[i % depth],
            t_sems.at[0, i % depth],
        )

    def store(i):
        return pltpu.make_async_copy(
            tile_out.at[i % depth],
            turned.at[i // n_tiles, :, pl.ds((i % n_tiles) * side, side)],
            t_sems.at[1, i % depth],
        )

    image_loads = [
        pltpu.make_async_copy(source, images.at[j], i_sems.at[0, j])
        for j, source in enumerate((tokens, cotangent))
    ]
    for i in range(depth - 1):
        load(i).start()
    for copy in image_loads:
        copy.start()
    swap = swap_matrix(side)
    done = [0]

    def turn(count):
        def step(i, carry):
            load(i).wait()

            @pl.when(i + depth - 1 < 2 * n_tiles)
            def _():
                load(i + depth - 1).start()

            @pl.when(i >= depth)
            def _():
                store(i - depth).wait()

            rows_in = tile_in[i % depth].reshape(side * side, tile_in.shape[3])
            tile_out[i % depth] = dot(swap, rows_in).astype(BF16).reshape(tile_out.shape[1:])
            store(i).start()
            return carry

        last = min(done[0] + count, 2 * n_tiles)
        lax.fori_loop(done[0], last, step, 0)
        done[0] = last

    pair = pair_matrix(block, wide, False)
    shape = (n_h * wide, small.shape[1])
    row = lax.broadcasted_iota(jnp.int32, shape, 0)
    column = lax.broadcasted_iota(jnp.int32, shape, 1)
    lane, of = row % wide - block, row // wide
    beside = (lane >= 0) & (lane < 16) & (column == of * 16 + lane)
    beside |= (lane >= 16) & (lane < 32) & (column == n_h * 16 + of * 16 + lane - 16)
    beside = beside.astype(F32).astype(BF16)

    stage[...] = jnp.zeros_like(stage)
    stage[64:66] = scales[...].astype(F32)
    stage[66:68] = biases[...].astype(F32)
    norms = jnp.swapaxes(stage[...], 0, 1)
    pieces = []
    for j in range(in_bias.shape[1] // 64):
        shape = (in_bias.shape[1], 128)
        row = lax.broadcasted_iota(jnp.int32, shape, 0)
        column = lax.broadcasted_iota(jnp.int32, shape, 1)
        chosen = ((row == 64 * j + column) & (column < 64)).astype(F32).astype(BF16)
        pieces.append(dot(in_bias[...], chosen))
    extra[:, :128] = jnp.zeros((rows, 128), F32)
    extra[:, 128:] = jnp.concatenate(pieces, axis=0) + norms

    image_stores = [
        pltpu.make_async_copy(picked.at[j], target, i_sems.at[1, j])
        for j, target in enumerate((own_tokens, own_cot))
    ]

    def pick_images(j):
        own, padded = picked.shape[1:3]
        group = own * n_h
        lines = images.shape[1]
        image_loads[j].wait()
        step = 256 // group
        for first in range(0, padded, step):
            count = min(step, padded - first)
            taken = min(step * group, lines - first * group)
            shape = (own * count, taken)
            row = lax.broadcasted_iota(jnp.int32, shape, 0)
            column = lax.broadcasted_iota(jnp.int32, shape, 1)
            wanted = (row % count) * group + own * h + row // count
            chosen = (column == wanted).astype(F32).astype(BF16)
            source = images[j, first * group : first * group + taken]
            picked[j, :, first : first + count] = (
                dot(chosen, source).astype(BF16).reshape(own, count, images.shape[2])
            )
        image_stores[j].start()

    def at(k, place):
        first = pl.multiple_of((place[0] * n_t + place[2]) * rows, 16)
        lines = pl.ds(first, rows)
        return small.at[lines] if k == n_k else w.at[k, lines]

    def hop(q, origin, place, sems, j):
        return remote(at(q, origin), at(q, origin), sems.at[0, j], sems.at[1, j], place)

    def half_hop(q, origin, place, half):
        part = at(q, origin).at[pl.ds(*halves[half])]
        j = 2 * q + half
        return remote(part, part, d_sems.at[0, j], d_sems.at[1, j], place)

    me = (s, h, t)
    from_d = (across_x[0], h, across_y[2])
    sent = []

    def send(copy):
        copy.start()
        sent.append(copy)

    def assemble(k):
        for i in range(0, n_h, 2):
            lines = jnp.concatenate([lined[i, k], lined[i + 1, k]], axis=1)
            at(k, me)[:, i * block : (i + 2) * block] = dot(lines, pair).astype(BF16)
        if k == 0:
            lines = jnp.concatenate([lined[i, k] for i in range(n_h)], axis=1)
            at(n_k, me)[...] = (dot(lines, beside) + extra[...]).astype(BF16)
        for q in members(k):
            send(hop(q, me, across_x, x_sems, q))
            send(hop(q, me, across_y, y_sems, q))
            send(hop(q, me, sibling, c_sems, 4 * q))

    def members(k):
        return (0, n_k) if k == 0 else (k,)

    def relay_xy(k):
        for q in members(k):
            hop(q, across_x, across_x, x_sems, q).wait_recv()
            send(half_hop(q, across_x, across_y, 0))
            send(hop(q, across_x, sibling, c_sems, 4 * q + 1))
            hop(q, across_y, across_y, y_sems, q).wait_recv()
            send(half_hop(q, across_y, across_x, 1))
            send(hop(q, across_y, sibling, c_sems, 4 * q + 2))

    def relay_d(k):
        for q in members(k):
            half_hop(q, from_d, across_y, 0).wait_recv()
            half_hop(q, from_d, across_x, 1).wait_recv()
            send(hop(q, from_d, sibling, c_sems, 4 * q + 3))

    for wave in range(n_k + n_h - 2):
        for d in range(1, n_h):
            if 0 <= wave - d + 1 < n_k:
                relay(chunks[wave - d + 1], d)
        turn(2)
        i = wave - n_h + 2
        if i >= 0:
            assemble(chunks[i])
            if i in (1, 2):
                pick_images(i - 1)
            if i >= 1:
                relay_xy(chunks[i - 1])
            if i >= 2:
                relay_d(chunks[i - 2])
            turn(2)
    relay_xy(chunks[-1])
    relay_d(chunks[-2])
    turn(2 * n_tiles)
    relay_d(chunks[-1])
    stores = []
    for k in chunks:
        for q in members(k):
            for j in range(4):
                hop(q, me, sibling, c_sems, 4 * q + j).wait_recv()
            if q == n_k:
                stores.append(pltpu.make_async_copy(small, small_out, o_sems.at[q]))
            else:
                stores.append(pltpu.make_async_copy(w.at[q], w_out.at[q], o_sems.at[q]))
            stores[-1].start()
    for copy in sent:
        copy.wait_send()
    for origin in range(n_h):
        @pl.when((origin <= h) & (h < n_h - 1))
        def _():
            for k in range(n_k):
                z_hop(k, origin, 1).wait_send()

        @pl.when((origin >= h) & (h > 0))
        def _():
            for k in range(n_k):
                z_hop(k, origin, 0).wait_send()

    for i in range(depth):
        store(2 * n_tiles - depth + i).wait()
    for copy in image_stores:
        copy.wait()
    for copy in stores:
        copy.wait()


def gather_weights(
    sizes, w_attn, phi_t, out_bias, scales, biases, in_bias, experts, tokens, cotangent
):
    n_k, rows, _ = w_attn.shape
    wide = 256
    n_s, n_h, n_t = sizes
    width = n_s * n_t * rows
    vmem = pl.BlockSpec(memory_space=pltpu.VMEM)
    hbm = pl.BlockSpec(memory_space=pl.ANY)
    dma = pltpu.SemaphoreType.DMA
    hidden = experts.shape[3]
    small = (width, wide)
    images = jax.ShapeDtypeStruct((2, 208, width), BF16)
    return pl.pallas_call(
        partial(gather_kernel, sizes),
        out_shape=(
            jax.ShapeDtypeStruct((n_k, width, width), BF16),
            jax.ShapeDtypeStruct(small, BF16),
            jax.ShapeDtypeStruct((2, experts.shape[2], experts.shape[0], hidden), BF16),
            images, images,
        ),
        in_specs=[vmem] * 6 + [hbm] * 3,
        out_specs=(hbm,) * 5,
        scratch_shapes=[
            pltpu.VMEM((n_k, width, width), BF16),
            pltpu.VMEM(small, BF16),
            pltpu.VMEM((n_h, n_k, rows, wide), BF16),
            pltpu.VMEM((rows, wide), F32),
            pltpu.VMEM((128, rows), F32),
            pltpu.VMEM((4, 16, 16, hidden), BF16),
            pltpu.VMEM((4, 16, 16, hidden), BF16),
            pltpu.VMEM((2, *tokens.shape), BF16),
            pltpu.VMEM((2, *images.shape), BF16),
            dma((n_k, n_h, 2)), dma((n_k, n_h)), dma((2, n_k + 1)), dma((2, n_k + 1)),
            dma((2, 2 * (n_k + 1))), dma((2, 4 * (n_k + 1))), dma((2, 4)), dma((n_k + 1,)),
            dma((2, 2)),
        ],
        compiler_params=pltpu.CompilerParams(
            collective_id=3, has_side_effects=True, vmem_limit_bytes=VMEM_BYTES
        ),
        name="gather_weights",
    )(w_attn, phi_t, out_bias, scales, biases, in_bias, experts, tokens, cotangent)


def reduce_kernel(
    sizes, grads, small, out, core_in, core_small, met, met_small,
    d_in, d_small, x_in, x_small, y_in, y_small, pieces, z_in,
    c_sems, d_sems, x_sems, y_sems, z_send, z_recv,
):
    (s, h, t), core, chip, sibling, across_x, across_y, line = plane(sizes)
    n_k, width, _ = grads.shape
    n_s, n_h, n_t = sizes
    rows = width // (n_s * n_t)
    wide = pieces.shape[3]
    pair = n_t * rows
    half = rows // 2
    halves = (pl.ds(0, half), pl.ds(half, half))
    chunks = (0, 2, 1, 3)

    def members(k):
        return (0, n_k) if k == 0 else (k,)

    def pick(q, large, little):
        return little if q == n_k else large.at[q]

    def core_copy(q, x):
        first = pl.multiple_of((2 * x + 1 - core) * pair, 16)
        return remote(
            pick(q, grads, small).at[pl.ds(first, pair)],
            pick(q, core_in, core_small).at[x],
            c_sems.at[0, 2 * q + x], c_sems.at[1, 2 * q + x], sibling,
        )

    for k in chunks:
        for q in members(k):
            for x in range(2):
                core_copy(q, x).start()
    joined = pair_matrix(width // n_h, wide, True)
    shape = (small.shape[1], n_h * wide)
    row = lax.broadcasted_iota(jnp.int32, shape, 0)
    column = lax.broadcasted_iota(jnp.int32, shape, 1)
    lane, of = column % wide - width // n_h, column // wide
    beside = (lane >= 0) & (lane < 16) & (row == of * 16 + lane)
    beside |= (lane >= 16) & (lane < 20) & (row == n_h * 16 + lane - 16)
    beside = beside.astype(F32).astype(BF16)
    to_d, to_x, to_y = (d_in, d_small), (x_in, x_small), (y_in, y_small)
    sent = []

    def hop(q, kind, part, source, place):
        sems = {id(to_d): d_sems, id(to_x): x_sems, id(to_y): y_sems}[id(kind)]
        target = pick(q, *kind)
        target = target.at[part] if kind is to_d else target.at[halves[part]]
        j = 2 * q + part
        return remote(source, target, sems.at[0, j], sems.at[1, j], place)

    def send(copy):
        copy.start()
        sent.append(copy)

    def part_of(q, x, y, part):
        return pick(q, met, met_small).at[x, y].at[halves[part]]

    def arrived(q, kind, part):
        hop(q, kind, part, part_of(q, 0, 0, part), sibling).wait_recv()

    def open_up(q):
        part = pick(q, met, met_small)
        for x in range(2):
            core_copy(q, x).wait_recv()
            first = pl.multiple_of((2 * x + core) * pair, 16)
            own = pick(q, grads, small)[pl.ds(first, pair)].astype(F32)
            total = own + pick(q, core_in, core_small)[x].astype(F32)
            part[x] = total.astype(BF16).reshape(n_t, rows, total.shape[1])
        send(hop(q, to_d, 0, part_of(q, 1 - chip, 1 - t, 0), across_x))
        send(hop(q, to_d, 1, part_of(q, 1 - chip, 1 - t, 1), across_y))
        send(hop(q, to_x, 0, part_of(q, 1 - chip, t, 0), across_x))
        send(hop(q, to_y, 1, part_of(q, chip, 1 - t, 1), across_y))

    def pass_on(q):
        for part, kind, x, y, place in (
            (0, to_y, chip, 1 - t, across_y),
            (1, to_x, 1 - chip, t, across_x),
        ):
            arrived(q, to_d, part)
            block = part_of(q, x, y, part)
            total = block[...].astype(F32) + pick(q, *to_d)[part].astype(F32)
            block[...] = total.astype(BF16)
            send(hop(q, kind, part, block, place))

    def whole(q):
        for kind in (to_x, to_y):
            for part in range(2):
                arrived(q, kind, part)
        total = pick(q, met, met_small)[chip, t].astype(F32) + pick(q, *to_x)[...].astype(F32)
        return (total + pick(q, *to_y)[...].astype(F32)).astype(BF16)

    def z_copy(k, target, up):
        place = line[1] if up else line[n_h - 1]
        return remote(
            pieces.at[target, k], z_in.at[up, target, k],
            z_send.at[up, target, k], z_recv.at[up, target, k], place,
        )

    def pass_along(k, hops):
        for up in range(2):
            for target in range(n_h - 1, -1, -1) if up else range(n_h):
                further = target > h if up else target < h

                @pl.when(further & (h == (hops if up else n_h - 1 - hops)))
                def _():
                    if hops > 0:
                        z_copy(k, target, up).wait_recv()
                        total = pieces[target, k].astype(F32) + z_in[up, target, k].astype(F32)
                        pieces[target, k] = total.astype(BF16)
                    z_copy(k, target, up).start()

    def share_out(k):
        value = whole(k)
        columns = width // n_h
        if k == 0:
            little = dot(whole(n_k), beside)
        for i in range(0, n_h, 2):
            lanes = dot(value[:, i * columns : (i + 2) * columns], joined)
            if k == 0:
                lanes = lanes + little[:, i * wide : (i + 2) * wide]
            pieces[i, k] = lanes[:, :wide].astype(BF16)
            pieces[i + 1, k] = lanes[:, wide:].astype(BF16)
        pass_along(k, 0)

    for i in range(n_k + 2 + n_h - 2):
        if i < n_k:
            for q in members(chunks[i]):
                open_up(q)
        if 0 <= i - 1 < n_k:
            for q in members(chunks[i - 1]):
                pass_on(q)
        if 0 <= i - 2 < n_k:
            share_out(chunks[i - 2])
        for hops in range(1, n_h - 1):
            if 0 <= i - 2 - hops < n_k:
                pass_along(chunks[i - 2 - hops], hops)
    for k in chunks:
        out[k] = pieces[h, k].astype(F32)
        for up, there in ((1, h > 0), (0, h < n_h - 1)):
            @pl.when(there)
            def _():
                z_copy(k, h, up).wait_recv()
                out[k] = out[k] + z_in[up, h, k].astype(F32)

    for k in chunks:
        for q in members(k):
            for x in range(2):
                core_copy(q, x).wait_send()
    for copy in sent:
        copy.wait_send()
    for target in range(n_h):
        for up in range(2):
            @pl.when(target > h if up else target < h)
            def _():
                for k in range(n_k):
                    z_copy(k, target, up).wait_send()


def reduce_grads(sizes, grads, small):
    n_k, width, _ = grads.shape
    n_s, n_h, n_t = sizes
    rows, wide, thin = width // (n_s * n_t), 256, small.shape[1]
    vmem = pl.BlockSpec(memory_space=pltpu.VMEM)
    dma = pltpu.SemaphoreType.DMA

    def buffers(*lead):
        return [
            pltpu.VMEM((n_k, *lead, width), BF16),
            pltpu.VMEM((*lead, thin), BF16),
        ]

    return pl.pallas_call(
        partial(reduce_kernel, sizes),
        out_shape=jax.ShapeDtypeStruct((n_k, rows, wide), F32),
        in_specs=[vmem, vmem],
        out_specs=vmem,
        scratch_shapes=[
            *buffers(2, n_t * rows), *buffers(2, n_t, rows),
            *buffers(2, rows // 2), *buffers(rows), *buffers(rows),
            pltpu.VMEM((n_h, n_k, rows, wide), BF16),
            pltpu.VMEM((2, n_h, n_k, rows, wide), BF16),
            dma((2, 2 * (n_k + 1))), dma((2, 2 * (n_k + 1))), dma((2, 2 * (n_k + 1))),
            dma((2, 2 * (n_k + 1))), dma((2, n_h, n_k)), dma((2, n_h, n_k)),
        ],
        compiler_params=pltpu.CompilerParams(
            collective_id=4, has_side_effects=True, vmem_limit_bytes=VMEM_BYTES
        ),
        name="reduce_grads",
    )(grads, small)


def experts_kernel(
    sizes, blocks_0, weights, small, combine, hidden, cotangent,
    slots_0_out, act_0_out, slots_1_out, act_1_out, back_out, bias_out, sum_out, grad_logits,
    gathered,
    w_0, w_1, gate, sums, slots_both, act_both, core_out, core_both, x_out, x_both, land_both, leave,
    back, back_both, blocks_1, output, combine_v, hidden_v, cotangent_v, padded, bias, bias_all,
    bias_send, bias_land,
    w_sem, o_sem, m_sem, in_both, return_both, core_sem, x_sem, act_sem, b_sems, g_send, g_recv, g_sem,
):
    peers = Peers(sizes)
    s, h, t = peers.at
    n_s, n_h, n_t = sizes
    me = peers.flat(peers.at)
    core, chip = lax.rem(s, 2), s // 2
    sibling = (s + 1 - 2 * core, h, t)
    across = (lax.rem(s + 2, n_s), h, t)
    half = act_both.shape[1] // 2
    own, other = core * half, (1 - core) * half
    n_blocks = peers.count
    loads = [
        pltpu.make_async_copy(weights.at[0], w_0, w_sem.at[0]),
        pltpu.make_async_copy(weights.at[1], w_1, w_sem.at[1]),
    ]
    kept = [
        pltpu.make_async_copy(source, target, m_sem.at[j])
        for j, (source, target) in enumerate(
            ((combine, combine_v), (hidden, hidden_v), (cotangent, cotangent_v))
        )
    ]
    for load in loads + kept:
        load.start()
    few = half // 2
    group = 16
    many = 2 * group
    peers.greet_all()

    def each(function, count=n_blocks, start=1):
        lax.fori_loop(start, count, lambda k, carry: (function(k), carry)[1], 0)

    out_row = lax.broadcasted_iota(jnp.int32, (16 * group, 16 * group), 0)
    in_row = lax.broadcasted_iota(jnp.int32, (16 * group, 16 * group), 1)
    there = (out_row // many == in_row % (2 * few)) & (out_row % many == in_row // (2 * few))
    there = there.astype(F32).astype(BF16)
    again = (in_row // many == out_row % (2 * few)) & (in_row % many == out_row // (2 * few))
    again = again.astype(F32).astype(BF16)
    stores = []

    def run(backward):
        n = 1 if backward else 0
        blocks = blocks_1 if backward else blocks_0
        w_a, w_b = (w_1, w_0) if backward else (w_0, w_1)
        slots, act, core_in, x_in, land, land_back = (
            both.at[n] for both in (slots_both, act_both, core_both, x_both, land_both, back_both)
        )
        in_sems, back_sems, core_sems, x_sems, act_sems = (
            both.at[n] for both in (in_both, return_both, core_sem, x_sem, act_sem)
        )
        def block_out(p, k):
            place = peers.step(k, 1)
            return remote(
                blocks.at[place[1], place[0], p], land.at[p, me],
                in_sems.at[0, p, k], in_sems.at[1, p, k], place,
            )

        def block_in(p, k):
            source = peers.flat(peers.step(k, -1))
            return remote(
                blocks.at[0, 0, p], land.at[p, source], in_sems.at[0, p, k], in_sems.at[1, p, k], sibling
            )

        for p in range(2):
            for k in range(1, n_blocks):
                block_out(p, k).start()
            land[p, me] = blocks[h, s, p]
        def receive(p):
            each(lambda k: block_in(p, k).wait_recv())
            for b in range(n_blocks // group):
                rows = land[p, b * group : (b + 1) * group].reshape(group * 16, land.shape[3])
                turned = dot(there, rows).astype(BF16).reshape(2 * few, many, land.shape[3])
                for c in range(2):
                    first = c * half + p * few
                    slots[first : first + few, b * many : (b + 1) * many, :] = turned[
                        c * few : (c + 1) * few
                    ]

        if backward:
            own_images = output.shape[0]
            line = [(s, lax.rem(h + d, n_h), t) for d in range(n_h)]
            g_own = pltpu.make_async_copy(output, gathered.at[pl.ds(h * own_images, own_images)], g_sem)
            g_own.start()

            def z_hop(i, origin, up, source=None):
                there = gathered.at[origin * own_images + i]
                return remote(
                    there if source is None else source, there,
                    g_send.at[i, origin, up], g_recv.at[i, origin], line[1] if up else line[n_h - 1],
                )

            def relay(i, d):
                @pl.when(h >= d)
                def _():
                    z_hop(i, h - d, 1).wait_recv()

                    @pl.when((h < n_h - 1) & (d < n_h - 1))
                    def _():
                        z_hop(i, h - d, 1).start()

                @pl.when(h + d < n_h)
                def _():
                    z_hop(i, h + d, 0).wait_recv()

                    @pl.when((h > 0) & (d < n_h - 1))
                    def _():
                        z_hop(i, h + d, 0).start()

            def gather_output():
                for i in range(own_images):
                    @pl.when(h < n_h - 1)
                    def _():
                        z_hop(i, h, 1, output.at[i]).start()

                    @pl.when(h > 0)
                    def _():
                        z_hop(i, h, 0, output.at[i]).start()
        else:
            piece, count = 6 * 64, act.shape[2] // (6 * 64)
            row = lax.broadcasted_iota(jnp.int32, (6 * 128, piece), 0)
            column = lax.broadcasted_iota(jnp.int32, (6 * 128, piece), 1)
            lane = row % 128
            place = (lane < 64) & (column == (row // 128) * 64 + lane)
            place = place.astype(F32).astype(BF16)
            for m in range(count):
                first = (t * count + m) * 96
                lines = [
                    small[pl.ds(pl.multiple_of(first + j * 16, 16), 16), 128:256] for j in range(6)
                ]
                bias[:, m * piece : (m + 1) * piece] = dot(jnp.concatenate(lines, axis=1), place)

        receive(0)
        if backward:
            gather_output()
        if not backward:
            loads[0].wait()

        def core_copy(j):
            return remote(
                core_out.at[j], core_in.at[j], core_sems.at[0, j], core_sems.at[1, j], sibling
            )

        def x_copy(j):
            return remote(x_out.at[j], x_in.at[j], x_sems.at[0, j], x_sems.at[1, j], across)

        def act_copy(j):
            return remote(
                act.at[own + j], act.at[own + j], act_sems.at[0, j], act_sems.at[1, j], sibling
            )

        def act_in(j):
            return remote(
                act.at[other + j], act.at[other + j], act_sems.at[0, j], act_sems.at[1, j], sibling
            )

        def meet(j):
            core_copy(j).wait_recv()
            sums[j] = sums[j] + core_in[j].astype(F32)
            x_out[j] = sums[j].astype(BF16)
            x_copy(j).start()

        def first_sums(j):
            core_out[j] = dot(slots[other + j], w_a[other + j]).astype(BF16)
            core_copy(j).start()

            @pl.when(j > 0)
            def _():
                meet(j - 1)

            sums[j] = dot(slots[own + j], w_a[own + j])

        each(first_sums, few, 0)
        receive(1)
        each(first_sums, half, few)
        meet(half - 1)
        if not backward:
            loads[1].wait()

        def second(e):
            leave[e] = dot_t(act[e], w_b[e]).astype(BF16)

        def finish(j):
            x_copy(j).wait_recv()
            value = sums[j] + x_in[j].astype(F32)
            if backward:
                act[own + j] = (value * gate[j]).astype(BF16)
            else:
                value = value + bias[pl.ds(own + j, 1), :]
                cumulative = 0.5 + 0.5 * lax.erf(value * 0.7071067811865476)
                act[own + j] = (value * cumulative).astype(BF16)
                gate[j] = cumulative + value * (
                    jnp.exp(value * value * -0.5) * 0.3989422804014327
                )
            act_copy(j).start()
            second(own + j)

            @pl.when(j > 0)
            def _():
                act_in(j - 1).wait_recv()
                second(other + j - 1)

            if backward:
                for when, i, d in ((2, 0, 1), (3, 1, 1), (5, 0, 2), (7, 1, 2)):
                    @pl.when(j == when)
                    def _():
                        relay(i, d)

        def back_copy(p, k):
            place = peers.step(k, 1)
            return remote(
                back.at[p, peers.flat(place)], land_back.at[p, me],
                back_sems.at[0, p, k], back_sems.at[1, p, k], place,
            )

        def back_in(p, k):
            source = peers.flat(peers.step(k, -1))
            return remote(
                back.at[p, 0], land_back.at[p, source],
                back_sems.at[0, p, k], back_sems.at[1, p, k], sibling,
            )

        def give_back(p):
            for b in range(n_blocks // group):
                rows = jnp.concatenate(
                    [
                        leave[c * half + p * few : c * half + (p + 1) * few, b * many : (b + 1) * many, :]
                        for c in range(2)
                    ],
                    axis=0,
                ).reshape(group * 16, leave.shape[2])
                turned = dot(again, rows).astype(BF16)
                back[p, b * group : (b + 1) * group] = turned.reshape(group, 16, leave.shape[2])
            for k in range(1, n_blocks):
                back_copy(p, k).start()
            land_back[p, me] = back[p, me]

        each(finish, few + 1, 0)
        give_back(0)
        each(finish, half, few + 1)
        act_in(half - 1).wait_recv()
        second(other + half - 1)
        give_back(1)
        outs = (slots_1_out, act_1_out) if backward else (slots_0_out, act_0_out)
        for j, (source, target) in enumerate(zip((slots, act), outs)):
            stores.append(pltpu.make_async_copy(source, target, o_sem.at[n, j]))
            stores[-1].start()
        if backward:
            across_t = (s, h, 1 - t)
            width = bias_out.shape[1]

            def bias_row(e):
                bias_all[pl.ds(e, 1), :] = jnp.sum(act[e].astype(F32), axis=0, keepdims=True)

            each(bias_row, 2 * half, 0)

            def slot_row(e):
                total = jnp.sum(slots[e].astype(F32), axis=0, keepdims=True)
                sum_out[pl.ds(e, 1), : slots.shape[2]] = total

            sum_out[...] = jnp.zeros_like(sum_out)
            each(slot_row, 2 * half, 0)

            def piece(for_t):
                return bias_all[:, pl.ds(pl.multiple_of((core * n_t + for_t) * width, 128), width)]

            bias_send[...] = piece(1 - t)
            bias_copy = remote(bias_send, bias_land, b_sems.at[0], b_sems.at[1], across_t)
            bias_copy.start()
            bias_copy.wait()
            bias_out[...] = jnp.where(t == chip, piece(t), bias_land[...])
        for p in range(2):
            each(lambda k: back_in(p, k).wait_recv())
        if backward:
            back_out[...] = land_back[...]
            relay(0, 3)
            relay(1, 3)
            g_own.wait()
            for origin in range(n_h):
                @pl.when((origin < h) & (h < n_h - 1))
                def _():
                    for i in range(own_images):
                        z_hop(i, origin, 1).wait_send()

                @pl.when((origin > h) & (h > 0))
                def _():
                    for i in range(own_images):
                        z_hop(i, origin, 0).wait_send()

            @pl.when(h < n_h - 1)
            def _():
                for i in range(own_images):
                    z_hop(i, h, 1, output.at[i]).wait_send()

            @pl.when(h > 0)
            def _():
                for i in range(own_images):
                    z_hop(i, h, 0, output.at[i]).wait_send()

        for p in range(2):
            each(lambda k: block_out(p, k).wait_send())
            each(lambda k: back_copy(p, k).wait_send())
        for copy in (core_copy, x_copy, act_copy):
            each(lambda j: copy(j).wait_send(), half, 0)

    run(False)
    for copy in kept:
        copy.wait()
    middle_kernel(
        sizes, back_both.at[0], small, combine_v, hidden_v, cotangent_v, output, blocks_1, grad_logits,
        padded,
    )
    run(True)
    for store in stores:
        store.wait()


def experts_pass(sizes, blocks, weights, small, combine, hidden, cotangent, bias_width):
    _, experts, rows, width = weights.shape
    devices = sizes[0] * sizes[1] * sizes[2]
    images = 2 * devices
    half = experts // 2
    vmem = pl.BlockSpec(memory_space=pltpu.VMEM)
    hbm = pl.BlockSpec(memory_space=pl.ANY)
    shape, dma = jax.ShapeDtypeStruct, pltpu.SemaphoreType.DMA
    slots, act = (experts, images, rows), (experts, images, width)
    chunk = (half, images, width)
    block = (2, devices, experts, rows)
    own = hidden.shape[0]
    weight = pltpu.VMEM((experts, rows, width), BF16)
    return pl.pallas_call(
        partial(experts_kernel, sizes),
        out_shape=(
            shape(slots, BF16), shape(act, BF16), shape(slots, BF16), shape(act, BF16),
            shape(block, BF16), shape((experts, bias_width), F32), shape((experts, 256), F32),
            shape((own, hidden.shape[1], 64), F32),
            shape((sizes[1] * own, *hidden.shape[1:]), BF16),
        ),
        in_specs=[vmem, hbm, vmem, hbm, hbm, hbm],
        out_specs=(hbm, hbm, hbm, hbm, vmem, vmem, vmem, vmem, hbm),
        scratch_shapes=[
            weight, weight,
            pltpu.VMEM(chunk, F32), pltpu.VMEM(chunk, F32),
            pltpu.VMEM((2, *slots), BF16), pltpu.VMEM((2, *act), BF16),
            pltpu.VMEM(chunk, BF16), pltpu.VMEM((2, *chunk), BF16),
            pltpu.VMEM(chunk, BF16), pltpu.VMEM((2, *chunk), BF16),
            pltpu.VMEM((2, *block), BF16), pltpu.VMEM(slots, BF16),
            pltpu.VMEM(block, BF16), pltpu.VMEM((2, *block), BF16),
            pltpu.VMEM(blocks.shape, BF16), pltpu.VMEM(hidden.shape, BF16),
            pltpu.VMEM(combine.shape, F32), pltpu.VMEM(hidden.shape, F32),
            pltpu.VMEM(cotangent.shape, BF16), pltpu.VMEM((2, 128, 256), F32),
            pltpu.VMEM((experts, width), F32), pltpu.VMEM((experts, width), F32),
            pltpu.VMEM((experts, bias_width), F32), pltpu.VMEM((experts, bias_width), F32),
            dma((2,)), dma((2, 2)), dma((3,)), dma((2, 2, 2, devices)), dma((2, 2, 2, devices)),
            dma((2, 2, half)), dma((2, 2, half)), dma((2, 2, half)), dma((2,)),
            dma((own, sizes[1], 2)), dma((own, sizes[1])), dma,
        ],
        compiler_params=pltpu.CompilerParams(
            collective_id=1, has_side_effects=True, vmem_limit_bytes=VMEM_BYTES
        ),
        name="experts",
    )(blocks, weights, small, combine, hidden, cotangent)


def weight_grad_kernel(slots_0, act_0, slots_1, act_1, out, lines, pick, same):
    group, images, rows = slots_0.shape
    d_block = out.shape[0]
    few = group // 2
    m, d = pl.program_id(0), pl.program_id(2)

    @pl.when((m == 0) & (pl.program_id(1) == 0) & (d == 0))
    def _():
        row = lax.broadcasted_iota(jnp.int32, pick.shape[1:], 0)
        column = lax.broadcasted_iota(jnp.int32, pick.shape[1:], 1)
        second = (row % group) // few
        for half in range(2):
            feature = 2 * (row // group) + (second if half == 0 else 1 - second)
            pick[half] = (column == feature).astype(F32).astype(BF16)
        row = lax.broadcasted_iota(jnp.int32, same.shape, 0)
        column = lax.broadcasted_iota(jnp.int32, same.shape, 1)
        same[...] = (row % few == column // images).astype(F32)

    def prepare(slots):
        @pl.when(d == 0)
        def _():
            turned = slots[...].reshape(group * images, rows).astype(F32)
            lines[...] = jnp.swapaxes(turned, 0, 1).astype(BF16)

    def term(act):
        mine = lines[pl.ds(pl.multiple_of(d * d_block, d_block), d_block)]
        width = act.shape[2]
        results = []
        for half in range(2):
            columns = mine[:, half * few * images : (half + 1) * few * images]
            spread = (dot(pick[half], columns) * same[...]).astype(BF16)
            values = act[half * few : (half + 1) * few].reshape(few * images, width)
            results.append(dot(spread, values).reshape(d_block // 2, group, width))
        first, last = results
        low = lax.broadcasted_iota(jnp.int32, first.shape, 1) < few
        even = jnp.where(low, first, last)
        odd = pltpu.roll(jnp.where(low, last, first), few, 1)
        out[...] = jnp.stack((even, odd), axis=1).reshape(out.shape)

    @pl.when(m == 0)
    def _():
        prepare(slots_0)
        term(act_0)

    @pl.when(m == 1)
    def _():
        prepare(slots_1)
        term(act_1)


def weight_grads(slots_0, act_0, slots_1, act_1):
    experts, images, rows = slots_0.shape
    hidden = act_0.shape[2]
    group, d_block = 8, 192
    last = experts // group - 1

    def early(m, g, d):
        return jnp.where(m == 0, g, last), 0, 0

    def late(m, g, d):
        return jnp.where(m == 0, 0, g), 0, 0

    slots, act = (group, images, rows), (group, images, hidden)
    return pl.pallas_call(
        weight_grad_kernel,
        grid=(2, experts // group, rows // d_block),
        out_shape=jax.ShapeDtypeStruct((rows, 2, experts, hidden), F32),
        in_specs=[
            pl.BlockSpec(slots, early), pl.BlockSpec(act, early),
            pl.BlockSpec(slots, late), pl.BlockSpec(act, late),
        ],
        out_specs=pl.BlockSpec((d_block, 1, group, hidden), lambda m, g, d: (d, m, g, 0)),
        scratch_shapes=[
            pltpu.VMEM((rows, group * images), BF16),
            pltpu.VMEM((2, group * d_block // 2, d_block), BF16),
            pltpu.VMEM((group * d_block // 2, group * images // 2), F32),
        ],
        compiler_params=pltpu.CompilerParams(vmem_limit_bytes=VMEM_BYTES),
        cost_estimate=pl.CostEstimate(
            flops=4 * images * experts * rows * hidden,
            bytes_accessed=8 * rows * experts * hidden,
            transcendentals=0,
        ),
        name="weight_grads",
    )(slots_0, act_0, slots_1, act_1)


def dot_r(a, b):
    return lax.dot_general(a, b, (((0,), (0,)), ((), ())), preferred_element_type=F32)


def row_of(shape, axis):
    return lax.broadcasted_iota(jnp.int32, shape, axis)


def one_hot(mask):
    return mask.astype(F32).astype(BF16)


def order_matrix(n_h, few, back):
    n = n_h * 8 * few
    shape = (n, n)
    blocked, natural = row_of(shape, 1 if back else 0), row_of(shape, 0 if back else 1)
    f, half, image = blocked % few, (blocked // few) % 2, (blocked // (2 * few)) % 2
    group = blocked // (4 * few)
    if back:
        part, h = group // n_h, group % n_h
    else:
        h, part = group // 2, group % 2
    expert = ((h * 2 + half) * 2 + part) * few + f
    return one_hot(natural == image * (4 * n_h * few) + expert)


def norm_parts(x, scale, shift, live):
    centered = x - jnp.mean(x, axis=-1, keepdims=True)
    inverse = lax.rsqrt(jnp.mean(centered * centered, axis=-1, keepdims=True) + epsilon)
    unit = centered * inverse
    return unit * scale + shift, unit, inverse


def norm_back(grad, unit, inverse, scale):
    scaled = grad * scale
    average = jnp.mean(scaled, axis=-1, keepdims=True)
    projection = jnp.mean(scaled * unit, axis=-1, keepdims=True)
    return (
        inverse * (scaled - average - unit * projection),
        jnp.sum(grad * unit, axis=0, keepdims=True),
        jnp.sum(grad, axis=0, keepdims=True),
    )


def norm_rows(small):
    return jnp.swapaxes(small[:, 128:].astype(F32), 0, 1)[64:68]


def slots_to_blocks(slots, blocks, columns, joined, order):
    n_h, n_s = blocks.shape[:2]
    turned = dot(order, slots).astype(BF16)
    wide = joined.shape[1] // 2
    for s in range(0, n_s, 2):
        lanes = dot(turned[:, s * columns : (s + 2) * columns], joined).astype(BF16)
        for h in range(n_h):
            for p in range(2):
                rows = (h * 2 + p) * 16
                for e in range(2):
                    blocks[h, s + e, p] = lanes[rows : rows + 16, e * wide : e * wide + columns]


def blocks_to_slots(back, sizes, order, pair, padded):
    n_s, n_h, n_t = sizes
    columns = back.shape[3]
    both = jnp.concatenate([order] * n_t, axis=1)
    results = []
    for s in range(n_s):
        rows = jnp.concatenate(
            [
                back[p, (s * n_h + h) * n_t + t]
                for t in range(n_t)
                for p in range(2)
                for h in range(n_h)
            ],
            axis=0,
        )
        padded[s % 2, :, :columns] = dot(both, rows)
        if s % 2:
            value = jnp.concatenate([padded[0], padded[1]], axis=1)
            high = value.astype(BF16)
            rest = (value - high.astype(F32)).astype(BF16)
            results.append(dot(high, pair) + dot(rest, pair))
    return jnp.concatenate(results, axis=1)


def live_rows(shape, length):
    return row_of(shape, 0) < length


def ahead_kernel(
    length, tokens, small, w_hbm, blocks, normed_1, query, keyed, valued, context, hidden, normed_2,
    dispatch_out, combine_out, w, joined, order, w_sem,
):
    n, rows, width = tokens.shape
    keys = keyed.shape[1]
    loads = [pltpu.make_async_copy(w_hbm.at[k], w.at[k], w_sem.at[k]) for k in range(4)]
    for load in loads:
        load.start()
    norms = norm_rows(small)
    live = live_rows((rows, 1), length)
    for i in range(n):
        value, _, _ = norm_parts(tokens[i].astype(F32), norms[0:1], norms[2:3], live)
        normed_1[i] = jnp.where(live, value, 0.0).astype(BF16)
    joined[...] = pair_matrix(blocks.shape[4], joined.shape[1] // 2, True)
    order[...] = order_matrix(blocks.shape[0], 4, False)
    flat = (n * rows, width)
    for k, target in enumerate((query, keyed, valued)):
        loads[k].wait()
        value = dot(normed_1[...].reshape(flat), w[k]).astype(BF16).reshape(n, rows, width)
        if k == 0:
            target[...] = value
        else:
            target[:, :rows] = value
            target[:, rows:] = jnp.zeros((n, keys - rows, width), BF16)
    factor = HEAD_DIM ** (-0.5)
    pairs = width // 128
    lane = row_of((rows, 128), 1)
    shown = row_of((rows, keys), 1) < length

    def attend(step, carry):
        i = step // pairs
        lanes = pl.ds(pl.multiple_of((step % pairs) * 128, 128), 128)
        q, k, v = query[i, :, lanes], keyed[i, :, lanes], valued[i, :, lanes]
        scaled = q * jnp.bfloat16(factor)
        parts = []
        for a in range(2):
            mine = (lane < 64) if a == 0 else (lane >= 64)
            scores = dot_t(jnp.where(mine, scaled, jnp.zeros_like(q)), k)
            scores = jnp.where(shown, scores, -1e30)
            exponent = jnp.exp(scores - jnp.max(scores, axis=-1, keepdims=True))
            probs = exponent * (1.0 / jnp.sum(exponent, axis=-1, keepdims=True))
            parts.append(dot(probs.astype(BF16), v))
        context[i, :, lanes] = jnp.where(lane < 64, parts[0], parts[1]).astype(BF16)
        return carry

    lax.fori_loop(0, n * pairs, attend, 0, unroll=6)
    loads[3].wait()
    attended = dot_t(context[...].reshape(flat), w[3]).reshape(n, rows, width)
    for i in range(n):
        value = tokens[i].astype(F32) + attended[i]
        hidden[i] = value
        value, _, _ = norm_parts(value, norms[1:2], norms[3:4], live)
        normed_2[i] = jnp.where(live, value, 0.0).astype(BF16)
    logits = dot(normed_2[...].reshape(flat), small[:, :128]).reshape(n, rows, 128)
    experts = row_of((rows, 128), 1) < 64
    slots = []
    for i in range(n):
        here = logits[i]
        down = jnp.where(live, here, -1e30)
        exponent = jnp.exp(down - jnp.max(down, axis=0, keepdims=True))
        dispatch = exponent / jnp.sum(exponent, axis=0, keepdims=True)
        dispatch = jnp.where(experts, dispatch, 0.0)
        across = jnp.where(experts, here, -1e30)
        exponent = jnp.exp(across - jnp.max(across, axis=1, keepdims=True))
        combine = exponent / jnp.sum(exponent, axis=1, keepdims=True)
        dispatch_out[i] = dispatch
        combine_out[i] = combine
        slots.append(dot_r(dispatch.astype(BF16), normed_2[i])[:64].astype(BF16))
    slots_to_blocks(
        jnp.concatenate(slots, axis=0), blocks, blocks.shape[4], joined[...], order[...]
    )


def tokens_ahead(sizes, length, tokens, small, weights):
    n, rows, width = tokens.shape
    keys = 256
    vmem = pl.BlockSpec(memory_space=pltpu.VMEM)
    shape = jax.ShapeDtypeStruct
    wide = (n, keys, width)
    thin = shape((n, rows, 128), F32)
    return pl.pallas_call(
        partial(ahead_kernel, length),
        out_shape=(
            shape((sizes[1], sizes[0], 2, 16, width // sizes[0]), BF16),
            shape(tokens.shape, BF16), shape(tokens.shape, BF16), shape(wide, BF16),
            shape(wide, BF16), shape(tokens.shape, BF16), shape(tokens.shape, F32),
            shape(tokens.shape, BF16), thin, thin,
        ),
        in_specs=[vmem, vmem, pl.BlockSpec(memory_space=pl.ANY)],
        out_specs=(vmem,) * 10,
        scratch_shapes=[
            pltpu.VMEM(weights.shape, BF16),
            pltpu.VMEM((2 * width // sizes[0], 512), BF16),
            pltpu.VMEM((128, 128), BF16),
            pltpu.SemaphoreType.DMA((4,)),
        ],
        compiler_params=pltpu.CompilerParams(vmem_limit_bytes=VMEM_BYTES),
        name="tokens_ahead",
    )(tokens, small, weights)


def middle_kernel(
    sizes, back, small, combine, hidden, cotangent, output, blocks, grad_logits, padded
):
    n, rows, _ = hidden.shape
    columns = back.shape[3]
    padded[...] = jnp.zeros_like(padded)
    pair = pair_matrix(columns, padded.shape[2], False)
    joined = pair_matrix(columns, padded.shape[2], True)
    total = blocks_to_slots(back, sizes, order_matrix(sizes[1], 4, True), pair, padded)
    bias = jnp.swapaxes(small[:, :128].astype(F32), 0, 1)[64:]
    slots = []
    for i in range(n):
        slot_out = (total[i * 64 : (i + 1) * 64] + bias).astype(BF16)
        combine_b = combine[i].astype(BF16)[:, :64]
        output[i] = (hidden[i] + dot(combine_b, slot_out)).astype(BF16)
        grad_combine = dot_t(cotangent[i], slot_out)
        weight = combine[i][:, :64]
        weighted = jnp.sum(weight * grad_combine, axis=1, keepdims=True)
        grad_logits[i] = weight * (grad_combine - weighted)
        slots.append(dot_r(combine_b, cotangent[i]).astype(BF16))
    slots_to_blocks(
        jnp.concatenate(slots, axis=0), blocks, columns, joined, order_matrix(sizes[1], 4, False)
    )


def behind_kernel(
    sizes, length, back, small, w_hbm, tokens, normed_1, query, keyed, valued, context, hidden,
    normed_2, dispatch, grad_logits, cotangent, grads, small_grads, input_grad,
    w, padded, grad_hidden, rounded, grad_context, grad_q, grad_k, grad_v, w_sem,
):
    n, rows, width = tokens.shape
    keys = keyed.shape[1]
    loads = [pltpu.make_async_copy(w_hbm.at[k], w.at[k], w_sem.at[k]) for k in range(4)]
    for load in loads:
        load.start()
    norms = norm_rows(small)
    padded[...] = jnp.zeros_like(padded)
    pair = pair_matrix(back.shape[3], padded.shape[2], False)
    grad_slots = blocks_to_slots(
        back, sizes, order_matrix(sizes[1], 4, True), pair, padded
    ).astype(BF16)
    phi = small[:, :64]
    phi_grad = jnp.zeros((width, 64), F32)
    sums = []
    flat = (n * rows, width)
    for i in range(n):
        slots = grad_slots[i * 64 : (i + 1) * 64]
        weight = dispatch[i][:, :64]
        grad_dispatch = dot_t(normed_2[i], slots)
        weighted = jnp.sum(weight * grad_dispatch, axis=0, keepdims=True)
        logits = (weight * (grad_dispatch - weighted) + grad_logits[i]).astype(BF16)
        phi_grad = phi_grad + dot_r(normed_2[i], logits)
        grad = dot(weight.astype(BF16), slots) + dot_t(logits, phi)
        _, unit, inverse = norm_parts(hidden[i], norms[1:2], norms[3:4], None)
        grad_in, scale_grad, bias_grad = norm_back(grad, unit, inverse, norms[1:2])
        value = cotangent[i].astype(F32) + grad_in
        grad_hidden[i] = value
        rounded[i] = value.astype(BF16)
        sums.append((scale_grad, bias_grad))
    scale_2, bias_2 = sums[0][0] + sums[1][0], sums[0][1] + sums[1][1]
    flat_rounded = rounded[...].reshape(flat)
    loads[3].wait()
    grad_context[...] = dot(flat_rounded, w[3]).astype(BF16).reshape(n, rows, width)
    grads[3] = dot_r(flat_rounded, context[...].reshape(flat)).astype(BF16)
    factor = HEAD_DIM ** (-0.5)
    pairs = width // 128
    lane = row_of((rows, 128), 1)
    key_lane = row_of((keys, 128), 1)
    shown = row_of((keys, rows), 0) < length

    def attend(step, carry):
        i = step // pairs
        lanes = pl.ds(pl.multiple_of((step % pairs) * 128, 128), 128)
        q, k, v = query[i, :, lanes], keyed[i, :, lanes], valued[i, :, lanes]
        scaled = q * jnp.bfloat16(factor)
        g = grad_context[i, :, lanes]
        to_q, to_k, to_v = [], [], []
        for a in range(2):
            mine = (lane < 64) if a == 0 else (lane >= 64)
            scores = dot_t(k, jnp.where(mine, scaled, jnp.zeros_like(q)))
            grad_probs = dot_t(v, jnp.where(mine, g, jnp.zeros_like(g)))
            scores = jnp.where(shown, scores, -1e30)
            exponent = jnp.exp(scores - jnp.max(scores, axis=0, keepdims=True))
            probs = exponent * (1.0 / jnp.sum(exponent, axis=0, keepdims=True))
            weighted = jnp.sum(probs * grad_probs, axis=0, keepdims=True)
            grad_scores = (probs * (grad_probs - weighted)).astype(BF16)
            to_v.append(dot(probs.astype(BF16), g))
            to_q.append(dot_r(grad_scores, k))
            to_k.append(dot(grad_scores, q))
        grad_q[i, :, lanes] = (jnp.where(lane < 64, to_q[0], to_q[1]) * factor).astype(BF16)
        kept = key_lane < 64
        grad_k[i, :, lanes] = (jnp.where(kept, to_k[0], to_k[1]) * factor)[:rows].astype(BF16)
        grad_v[i, :, lanes] = jnp.where(kept, to_v[0], to_v[1])[:rows].astype(BF16)
        return carry

    lax.fori_loop(0, n * pairs, attend, 0, unroll=6)
    total = jnp.zeros(flat, F32)
    turned = jnp.swapaxes(normed_1[...].reshape(flat).astype(F32), 0, 1).astype(BF16)
    for k, source in enumerate((grad_q, grad_k, grad_v)):
        loads[k].wait()
        value = source[...].reshape(flat)
        total = total + dot_t(value, w[k])
        grads[k] = dot(turned, value).astype(BF16)
    total = total.reshape(n, rows, width)
    sums = []
    for i in range(n):
        _, unit, inverse = norm_parts(tokens[i].astype(F32), norms[0:1], norms[2:3], None)
        grad_in, scale_grad, bias_grad = norm_back(total[i], unit, inverse, norms[0:1])
        input_grad[i] = (grad_hidden[i] + grad_in).astype(BF16)
        sums.append((scale_grad, bias_grad))
    scale_1, bias_1 = sums[0][0] + sums[1][0], sums[0][1] + sums[1][1]
    line = row_of((128, width), 0)
    spread = jnp.zeros((128, width), F32)
    for j, value in enumerate((scale_1, scale_2, bias_1, bias_2)):
        spread = jnp.where(line == 64 + j, value, spread)
    small_grads[...] = jnp.swapaxes(spread, 0, 1).astype(BF16)
    small_grads[:, :64] = phi_grad.astype(BF16)


def tokens_behind(sizes, length, back, small, weights, tokens, kept, grad_logits, cotangent):
    n, rows, width = tokens.shape
    vmem = pl.BlockSpec(memory_space=pltpu.VMEM)
    shape = jax.ShapeDtypeStruct
    low = pltpu.VMEM(tokens.shape, BF16)
    return pl.pallas_call(
        partial(behind_kernel, sizes, length),
        out_shape=(
            shape((4, width, width), BF16), shape((width, 128), BF16), shape(tokens.shape, BF16)
        ),
        in_specs=[vmem, vmem, pl.BlockSpec(memory_space=pl.ANY)] + [vmem] * 11,
        out_specs=(vmem,) * 3,
        scratch_shapes=[
            pltpu.VMEM(weights.shape, BF16),
            pltpu.VMEM((2, 128, 256), F32),
            pltpu.VMEM(tokens.shape, F32),
            low, low, low, low, low,
            pltpu.SemaphoreType.DMA((4,)),
        ],
        compiler_params=pltpu.CompilerParams(vmem_limit_bytes=VMEM_BYTES),
        name="tokens_behind",
    )(back, small, weights, tokens, *kept, grad_logits, cotangent)


def unpack_kernel(summed, in_bias_sum, out_sum, attn, phi_t, scales, biases, in_bias, out_bias):
    attn[...] = summed[:, :, : attn.shape[2]]
    turned = jnp.swapaxes(summed[0][:, 128:], 0, 1)
    phi_t[...] = turned[64:80]
    scales[...] = turned[80:82]
    biases[...] = turned[82:84]
    in_bias[...] = in_bias_sum[...]
    width = out_bias.shape[1]
    value = out_sum[...]
    later = pltpu.roll(value, value.shape[1] - width, 1)
    out_bias[...] = jnp.where(lax.axis_index("tensor") == 0, value[:, :width], later[:, :width])


def unpack_grads(summed, in_bias_sum, out_sum, block, slot):
    n_k, rows, _ = summed.shape
    vmem = pl.BlockSpec(memory_space=pltpu.VMEM)
    shape = jax.ShapeDtypeStruct
    return pl.pallas_call(
        unpack_kernel,
        out_shape=(
            shape((n_k, rows, block), F32), shape((slot, rows), F32),
            shape((2, rows), F32), shape((2, rows), F32),
            shape(in_bias_sum.shape, F32), shape((out_sum.shape[0], rows), F32),
        ),
        in_specs=[vmem] * 3,
        out_specs=(vmem,) * 6,
        name="unpack_grads",
    )(summed, in_bias_sum, out_sum)


def order_kernel(*refs):
    *parts, out = refs
    h, n_h = lax.axis_index("heads"), len(parts)
    own = parts[0].shape[0]
    group = own * n_h
    step = 256 // group
    length = out.shape[0]
    for first in range(0, length, step):
        count = min(step, length - first)
        taken = min(step, parts[0].shape[1] - first)
        shape = (count * group, group * taken)
        row = lax.broadcasted_iota(jnp.int32, shape, 0)
        column = lax.broadcasted_iota(jnp.int32, shape, 1)
        block = column // taken
        image = lax.rem(h + n_h - block // own, n_h) * own + block % own
        chosen = ((row // group == column % taken) & (row % group == image)).astype(F32)
        lines = jnp.concatenate(
            [part[i, first : first + taken] for part in parts for i in range(own)], axis=0
        )
        value = dot(chosen.astype(BF16), lines).astype(BF16)
        out[first : first + count] = value.reshape(count, group, value.shape[1])


def order_images(parts, length):
    own, _, width = parts[0].shape
    vmem = pl.BlockSpec(memory_space=pltpu.VMEM)
    return pl.pallas_call(
        order_kernel,
        out_shape=jax.ShapeDtypeStruct((length, own * len(parts), width), BF16),
        in_specs=[vmem] * len(parts),
        out_specs=vmem,
        compiler_params=pltpu.CompilerParams(vmem_limit_bytes=24 * 1024 * 1024),
        name="order_images",
    )(*parts)


def normalize(values, scale, shift):
    centered = values - jnp.mean(values, axis=-1, keepdims=True)
    variance = jnp.mean(centered * centered, axis=-1, keepdims=True)
    inverse = lax.rsqrt(variance + epsilon)
    unit_part = centered * inverse
    return (unit_part * scale + shift, unit_part, inverse)


def normalize_back(grad_output, unit_part, inverse, scale):
    scaled = grad_output * scale
    average = jnp.mean(scaled, axis=-1, keepdims=True)
    projection = jnp.mean(scaled * unit_part, axis=-1, keepdims=True)
    grad_input = inverse * (scaled - average - unit_part * projection)
    return (
        grad_input,
        jnp.sum(grad_output * unit_part, axis=(0, 1)),
        jnp.sum(grad_output, axis=(0, 1)),
    )


def to_experts(slots):
    slots = lax.all_to_all(slots, "heads", split_axis=1, concat_axis=0, tiled=True)
    slots = lax.all_to_all(slots, "shard", split_axis=2, concat_axis=0, tiled=True)
    return lax.all_gather(slots, "tensor", axis=0, tiled=True)


def to_images(slots):
    slots = lax.psum_scatter(slots, "tensor", scatter_dimension=0, tiled=True)
    slots = lax.all_to_all(slots, "shard", split_axis=0, concat_axis=2, tiled=True)
    return lax.all_to_all(slots, "heads", split_axis=0, concat_axis=1, tiled=True)


def general_shards(tokens, norm_scales, norm_biases, w_attn, phi, experts, in_bias, out_bias, cotangent):
    heads_n = lax.axis_size("heads")
    group, seq_len, width = tokens.shape
    own = group // heads_n
    heads_index = lax.axis_index("heads")
    tensor_index = lax.axis_index("tensor")
    shard_index = lax.axis_index("shard")
    hidden = experts.shape[3]
    rows = experts.shape[0]
    scales, biases, in_full = (
        lax.all_gather(norm_scales, ROWS, axis=1, tiled=True).astype(F32),
        lax.all_gather(norm_biases, ROWS, axis=1, tiled=True).astype(F32),
        lax.all_gather(in_bias, ROWS, axis=1, tiled=True).astype(F32),
    )
    attn = lax.all_gather(
        lax.all_gather(w_attn, "heads", axis=2, tiled=True), ROWS, axis=1, tiled=True
    )
    phi_full = lax.all_gather(
        lax.all_gather(phi, "heads", axis=1, tiled=True), ROWS, axis=0, tiled=True
    )
    out_rows = lax.all_gather(out_bias, "tensor", axis=1, tiled=True).astype(F32)
    e_own = experts.shape[2] // lax.axis_size("shard")
    in_local = lax.dynamic_slice_in_dim(in_full, tensor_index * hidden, hidden, 1)
    factor = HEAD_DIM ** (-0.5)
    tokens = lax.dynamic_slice_in_dim(tokens, heads_index * own, own, 0)
    cotangent = lax.dynamic_slice_in_dim(cotangent, heads_index * own, own, 0)
    n_heads = width // HEAD_DIM
    inputs = tokens.astype(F32)
    normed_one, unit_one, inverse_one = normalize(inputs, scales[0], biases[0])
    normed_one_b = normed_one.astype(BF16)
    projected = einsum("nsd,kdc->knsc", normed_one_b, attn[:3]).astype(BF16)
    query, keyed, valued = projected.reshape(3, own, seq_len, n_heads, HEAD_DIM)
    scores = einsum("nqhe,nkhe->nhqk", query, keyed) * factor
    score_peak = jnp.max(scores, axis=-1, keepdims=True)
    exponent = jnp.exp(scores - score_peak)
    probs = exponent / jnp.sum(exponent, axis=-1, keepdims=True)
    probs_b = probs.astype(BF16)
    context_b = (
        einsum("nhqk,nkhe->nqhe", probs_b, valued).astype(BF16).reshape(own, seq_len, width)
    )
    hidden_one = inputs + einsum("nsc,dc->nsd", context_b, attn[3])
    normed_two, unit_two, inverse_two = normalize(hidden_one, scales[1], biases[1])
    normed_two_b = normed_two.astype(BF16)
    logits = einsum("nsd,de->nse", normed_two_b, phi_full)
    dispatch = jax.nn.softmax(logits, axis=1)
    dispatch_b = dispatch.astype(BF16)
    combine = jax.nn.softmax(logits, axis=2)
    combine_b = combine.astype(BF16)
    slot_in = to_experts(einsum("nse,nsd->ned", dispatch_b, normed_two_b).astype(BF16))
    share = 1 if e_own else 0

    def meet(partial_sum):
        return lax.psum_scatter(partial_sum, "shard", scatter_dimension=share, tiled=True)

    def spread(values):
        return lax.all_gather(values, "shard", axis=share, tiled=True)

    pre = meet(einsum("ned,def->nef", slot_in, experts[:, 0]))
    if e_own:
        pre = pre + lax.dynamic_slice_in_dim(in_local, shard_index * e_own, e_own, 0)
    else:
        pre = pre + in_local
    gelu_value, gelu_back = jax.vjp(partial(jax.nn.gelu, approximate=False), pre)
    activated = spread(gelu_value.astype(BF16))
    slot_out_part = einsum("nef,def->ned", activated, experts[:, 1])
    slot_out_part = slot_out_part + jnp.where(tensor_index == 0, out_rows, 0.0)
    slot_out = to_images(slot_out_part).astype(BF16)
    output = (hidden_one + einsum("nse,ned->nsd", combine_b, slot_out)).astype(BF16)
    output = lax.all_gather(output, "heads", axis=0, tiled=True)
    grad_combine = einsum("nsd,ned->nse", cotangent, slot_out)
    grad_slot = to_experts(einsum("nse,nsd->ned", combine_b, cotangent).astype(BF16))
    grad_act = meet(einsum("ned,def->nef", grad_slot, experts[:, 1]))
    grad_pre = spread(gelu_back(grad_act)[0].astype(BF16))
    grad_slot_in = einsum("nef,def->ned", grad_pre, experts[:, 0]).astype(BF16)
    input_term = einsum("ned,nef->def", slot_in, grad_pre)
    output_term = einsum("ned,nef->def", grad_slot, activated)
    experts_grad = jnp.stack((input_term, output_term), axis=1)
    grad_slot_in = to_images(grad_slot_in.astype(F32)).astype(BF16)
    in_bias_grad = lax.dynamic_slice_in_dim(
        lax.all_gather(jnp.sum(grad_pre.astype(F32), axis=0), "tensor", axis=1, tiled=True),
        (shard_index * lax.axis_size("tensor") + tensor_index) * in_bias.shape[1],
        in_bias.shape[1],
        1,
    )
    out_bias_grad = lax.dynamic_slice_in_dim(
        jnp.sum(grad_slot.astype(F32), axis=0),
        tensor_index * out_bias.shape[1],
        out_bias.shape[1],
        1,
    )
    grad_dispatch = einsum("nsd,ned->nse", normed_two_b, grad_slot_in)
    grad_logits = (
        dispatch * (grad_dispatch - jnp.sum(dispatch * grad_dispatch, axis=1, keepdims=True))
        + combine * (grad_combine - jnp.sum(combine * grad_combine, axis=2, keepdims=True))
    ).astype(BF16)
    phi_grad = einsum("nsd,nse->de", normed_two_b, grad_logits)
    grad_normed_two = einsum("nse,ned->nsd", dispatch_b, grad_slot_in) + einsum(
        "nse,de->nsd", grad_logits, phi_full
    )
    grad_hidden_norm, scale_two_grad, bias_two_grad = normalize_back(
        grad_normed_two, unit_two, inverse_two, scales[1]
    )
    grad_hidden = cotangent.astype(F32) + grad_hidden_norm
    grad_hidden_b = grad_hidden.astype(BF16)
    out_weight_grad = einsum("nsd,nsc->dc", grad_hidden_b, context_b)
    grad_context = einsum("nsd,dc->nsc", grad_hidden_b, attn[3]).astype(BF16)
    grad_context = grad_context.reshape(own, seq_len, n_heads, HEAD_DIM)
    grad_value = einsum("nhqk,nqhe->nkhe", probs_b, grad_context).astype(BF16)
    grad_probs = einsum("nqhe,nkhe->nhqk", grad_context, valued)
    grad_scores = (
        probs * (grad_probs - jnp.sum(probs * grad_probs, axis=-1, keepdims=True))
    ).astype(BF16)
    grad_query = (einsum("nhqk,nkhe->nqhe", grad_scores, keyed) * factor).astype(BF16)
    grad_key = (einsum("nhqk,nqhe->nkhe", grad_scores, query) * factor).astype(BF16)
    grad_proj = jnp.stack((grad_query, grad_key, grad_value)).reshape(3, own, seq_len, width)
    proj_grad = einsum("nsd,knsc->kdc", normed_one_b, grad_proj)
    grad_normed_one = einsum("knsc,kdc->nsd", grad_proj, attn[:3])
    grad_input_norm, scale_one_grad, bias_one_grad = normalize_back(
        grad_normed_one, unit_one, inverse_one, scales[0]
    )
    input_grad = (grad_hidden + grad_input_norm).astype(BF16)
    input_grad = lax.all_gather(input_grad, "heads", axis=0, tiled=True)
    attn_grad = jnp.concatenate((proj_grad, out_weight_grad[None]), axis=0)
    attn_grad = lax.psum_scatter(attn_grad, ROWS, scatter_dimension=1, tiled=True)
    attn_grad = lax.psum_scatter(attn_grad, "heads", scatter_dimension=2, tiled=True)
    phi_grad = lax.psum_scatter(phi_grad, ROWS, scatter_dimension=0, tiled=True)
    phi_grad = lax.psum_scatter(phi_grad, "heads", scatter_dimension=1, tiled=True)
    norms = jnp.stack((scale_one_grad, scale_two_grad, bias_one_grad, bias_two_grad))
    norms = lax.psum(lax.psum_scatter(norms, ROWS, scatter_dimension=1, tiled=True), "heads")
    return (
        output,
        input_grad,
        norms[:2],
        norms[2:],
        attn_grad,
        phi_grad,
        experts_grad,
        in_bias_grad,
        out_bias_grad,
    )


def shards(tokens, norm_scales, norm_biases, w_attn, phi, experts, in_bias, out_bias, cotangent):
    arrays = (tokens, norm_scales, norm_biases, w_attn, phi, experts, in_bias, out_bias, cotangent)
    sizes = tuple(lax.axis_size(name) for name in ("shard", "heads", "tensor"))
    group, length, width = tokens.shape
    fits = (sizes, group, width, *experts.shape[:3]) == ((4, 4, 2), 8, 768, 192, 2, 16)
    if not fits or not 192 < length <= 208 or in_bias.shape[1] != 384:
        return general_shards(*arrays)
    n_s, n_h, n_t = sizes
    block, slot = w_attn.shape[2], phi.shape[1]
    tokens, cotangent = (
        values.transpose(1, 0, 2).reshape(group * length, width) for values in (tokens, cotangent)
    )
    attn, small, turned, tokens, cotangent = gather_weights(
        sizes, w_attn, phi.T, out_bias, norm_scales, norm_biases, in_bias, experts, tokens, cotangent
    )
    blocks, *kept, combine = tokens_ahead(sizes, length, tokens, small, attn)
    hidden = kept[5]
    slot_in, activated, grad_slot, grad_pre, back, in_bias_grad, out_sum, grad_logits, output = (
        experts_pass(
            sizes, blocks, turned, small, combine, hidden, cotangent, in_bias.shape[1]
        )
    )
    attn_grad, small_grad, input_grad = tokens_behind(
        sizes, length, back, small, attn, tokens, kept, grad_logits, cotangent
    )
    parts = [input_grad] + [
        lax.ppermute(input_grad, "heads", [(i, (i + d) % n_h) for i in range(n_h)])
        for d in range(1, n_h)
    ]
    attn_grad, grad_pre = lax.optimization_barrier((attn_grad, grad_pre))
    experts_grad = weight_grads(slot_in, grad_pre, grad_slot, activated)
    output = output[:, :length].transpose(1, 0, 2)
    attn_grad, experts_grad, output = lax.optimization_barrier((attn_grad, experts_grad, output))
    summed = reduce_grads(sizes, attn_grad, small_grad)
    attn_grad, phi_grad, scales_grad, biases_grad, in_bias_grad, out_bias_grad = unpack_grads(
        summed, in_bias_grad, out_sum, block, slot
    )
    input_grad = order_images(parts, length)
    return (
        output.transpose(1, 0, 2),
        input_grad.transpose(1, 0, 2),
        scales_grad,
        biases_grad,
        attn_grad,
        phi_grad.T,
        experts_grad,
        in_bias_grad,
        out_bias_grad,
    )


def solution(mesh):
    images = P(ROWS, None, None)
    return jax.shard_map(
        shards,
        mesh=mesh,
        in_specs=(
            images,
            P(None, ROWS),
            P(None, ROWS),
            P(None, ROWS, "heads"),
            P(ROWS, "heads"),
            P("shard", None, "heads", "tensor"),
            P("heads", ROWS),
            P("heads", ROWS),
            images,
        ),
        out_specs=(
            images,
            images,
            P(None, ROWS),
            P(None, ROWS),
            P(None, ROWS, "heads"),
            P(ROWS, "heads"),
            P("shard", None, "heads", "tensor"),
            P("heads", ROWS),
            P("heads", ROWS),
        ),
        check_vma=False,
    )
```

```python
from functools import partial

import jax
import jax.numpy as jnp
from jax import lax
from jax.experimental import pallas as pl
from jax.experimental.pallas import tpu as pltpu
from jax.sharding import PartitionSpec as P

HEAD_DIM = 64
F32 = jnp.float32
BF16 = jnp.bfloat16
ROWS = ("shard", "tensor")
MESH = pl.DeviceIdType.MESH
VMEM_BYTES = 58 * 1024 * 1024
epsilon = 1e-06
einsum = partial(jnp.einsum, preferred_element_type=F32)


def dot(a, b):
    return lax.dot_general(a, b, (((1,), (0,)), ((), ())), preferred_element_type=F32)


def dot_t(a, b):
    return lax.dot_general(a, b, (((1,), (1,)), ((), ())), preferred_element_type=F32)


def swap_matrix(n):
    out = lax.broadcasted_iota(jnp.int32, (n * n, n * n), 0)
    row = lax.broadcasted_iota(jnp.int32, (n * n, n * n), 1)
    return ((out // n == row % n) & (out % n == row // n)).astype(F32).astype(BF16)


class Peers:
    def __init__(self, sizes):
        self.sizes = sizes
        self.at = tuple(lax.axis_index(name) for name in ("shard", "heads", "tensor"))
        self.count = sizes[0] * sizes[1] * sizes[2]

    def flat(self, place):
        return (place[0] * self.sizes[1] + place[1]) * self.sizes[2] + place[2]

    def step(self, k, sign):
        _, n_h, n_t = self.sizes
        steps = (k // (n_h * n_t), (k // n_t) % n_h, k % n_t)
        return tuple(
            lax.rem(at + n + sign * d, n) for at, n, d in zip(self.at, self.sizes, steps)
        )

    def greet_all(self):
        barrier = pltpu.get_barrier_semaphore()

        def signal(k, carry):
            pl.semaphore_signal(barrier, inc=1, device_id=self.step(k, 1), device_id_type=MESH)
            return carry

        lax.fori_loop(1, self.count, signal, 0)
        pl.semaphore_wait(barrier, self.count - 1)


def remote(src, dst, send, recv, place):
    return pltpu.make_async_remote_copy(
        src_ref=src, dst_ref=dst, send_sem=send, recv_sem=recv, device_id=place, device_id_type=MESH
    )


def plane(sizes):
    n_s, n_h, n_t = sizes
    s, h, t = (lax.axis_index(name) for name in ("shard", "heads", "tensor"))
    core, chip = lax.rem(s, 2), s // 2
    sibling = (s + 1 - 2 * core, h, t)
    across_x = (lax.rem(s + 2, n_s), h, t)
    across_y = (s, h, 1 - t)
    line = [(s, lax.rem(h + d, n_h), t) for d in range(n_h)]
    barrier = pltpu.get_barrier_semaphore()
    others = [sibling, across_x, across_y] + line[1:]
    for place in others:
        pl.semaphore_signal(barrier, inc=1, device_id=place, device_id_type=MESH)
    pl.semaphore_wait(barrier, len(others))
    return (s, h, t), core, chip, sibling, across_x, across_y, line


def pair_matrix(block, wide, transposed):
    shape = (2 * block, 2 * wide) if transposed else (2 * wide, 2 * block)
    tight = lax.broadcasted_iota(jnp.int32, shape, 0 if transposed else 1)
    padded = lax.broadcasted_iota(jnp.int32, shape, 1 if transposed else 0)
    second = padded >= wide
    lane = jnp.where(second, padded - wide, padded)
    same = (lane < block) & (tight == jnp.where(second, lane + block, lane))
    return same.astype(F32).astype(BF16)


def gather_kernel(
    sizes, length, w_attn, phi_t, out_bias, scales, biases, in_bias, experts, tokens, cotangent,
    w_out, small_out, turned, own_tokens, own_cot, blocks, dispatch, combine, *refs,
):
    held_out, refs = refs[:7], refs[7:]
    held, refs = refs[:7], refs[7:]
    (joined, order, w, small, lined, extra, stage, tile_in, tile_out, images, picked,
     z_send, z_recv, x_sems, y_sems, d_sems, c_sems, t_sems, o_sems, i_sems, h_sems) = refs
    n_k, rows, block = w_attn.shape
    wide = lined.shape[3]
    slot = phi_t.shape[0]
    own_h = lax.axis_index("heads")
    stage[...] = jnp.zeros_like(stage)
    stage[64 : 64 + slot] = phi_t[...].astype(F32)
    stage[64 + slot : 64 + 2 * slot] = out_bias[...].astype(F32)
    lined[own_h, :, :, 128:] = jnp.zeros((n_k, rows, wide - 128), BF16)
    lined[own_h, :, :, :block] = w_attn[...]
    first = lined[own_h, 0, :, 128:].astype(F32) + jnp.swapaxes(stage[...], 0, 1)
    lined[own_h, 0, :, 128:] = first.astype(BF16)
    (s, h, t), core, chip, sibling, across_x, across_y, line = plane(sizes)
    n_h, n_t = sizes[1], sizes[2]
    width = w.shape[2]
    side = 16
    n_tiles = experts.shape[0] // side
    depth = tile_in.shape[0]
    halves = ((0, rows // 2), (rows // 2, rows // 2))

    def z_hop(k, origin, up):
        place = line[1] if up else line[n_h - 1]
        return remote(
            lined.at[origin, k], lined.at[origin, k],
            z_send.at[k, origin, up], z_recv.at[k, origin], place,
        )

    def relay(k, d):
        @pl.when(h >= d)
        def _():
            z_hop(k, h - d, 1).wait_recv()

            @pl.when(h < n_h - 1)
            def _():
                z_hop(k, h - d, 1).start()

        @pl.when(h + d < n_h)
        def _():
            z_hop(k, h + d, 0).wait_recv()

            @pl.when(h > 0)
            def _():
                z_hop(k, h + d, 0).start()

    chunks = (0, 2, 1, 3)
    for k in chunks:
        @pl.when(h < n_h - 1)
        def _():
            z_hop(k, h, 1).start()

        @pl.when(h > 0)
        def _():
            z_hop(k, h, 0).start()

    def load(i):
        return pltpu.make_async_copy(
            experts.at[pl.ds((i % n_tiles) * side, side), i // n_tiles],
            tile_in.at[i % depth],
            t_sems.at[0, i % depth],
        )

    def store(i):
        return pltpu.make_async_copy(
            tile_out.at[i % depth],
            turned.at[i // n_tiles, :, pl.ds((i % n_tiles) * side, side)],
            t_sems.at[1, i % depth],
        )

    image_loads = [
        pltpu.make_async_copy(source, images.at[j], i_sems.at[0, j])
        for j, source in enumerate((tokens, cotangent))
    ]
    for i in range(depth - 1):
        load(i).start()
    for copy in image_loads:
        copy.start()
    swap = swap_matrix(side)
    done = [0]

    def turn(count):
        def step(i, carry):
            load(i).wait()

            @pl.when(i + depth - 1 < 2 * n_tiles)
            def _():
                load(i + depth - 1).start()

            @pl.when(i >= depth)
            def _():
                store(i - depth).wait()

            rows_in = tile_in[i % depth].reshape(side * side, tile_in.shape[3])
            tile_out[i % depth] = dot(swap, rows_in).astype(BF16).reshape(tile_out.shape[1:])
            store(i).start()
            return carry

        last = min(done[0] + count, 2 * n_tiles)
        lax.fori_loop(done[0], last, step, 0)
        done[0] = last

    pair = pair_matrix(block, wide, False)
    shape = (n_h * wide, small.shape[1])
    row = lax.broadcasted_iota(jnp.int32, shape, 0)
    column = lax.broadcasted_iota(jnp.int32, shape, 1)
    lane, of = row % wide - block, row // wide
    beside = (lane >= 0) & (lane < 16) & (column == of * 16 + lane)
    beside |= (lane >= 16) & (lane < 32) & (column == n_h * 16 + of * 16 + lane - 16)
    beside = beside.astype(F32).astype(BF16)

    stage[...] = jnp.zeros_like(stage)
    stage[64:66] = scales[...].astype(F32)
    stage[66:68] = biases[...].astype(F32)
    norms = jnp.swapaxes(stage[...], 0, 1)
    pieces = []
    for j in range(in_bias.shape[1] // 64):
        shape = (in_bias.shape[1], 128)
        row = lax.broadcasted_iota(jnp.int32, shape, 0)
        column = lax.broadcasted_iota(jnp.int32, shape, 1)
        chosen = ((row == 64 * j + column) & (column < 64)).astype(F32).astype(BF16)
        pieces.append(dot(in_bias[...], chosen))
    extra[:, :128] = jnp.zeros((rows, 128), F32)
    extra[:, 128:] = jnp.concatenate(pieces, axis=0) + norms

    image_stores = [
        pltpu.make_async_copy(picked.at[j], target, i_sems.at[1, j])
        for j, target in enumerate((own_tokens, own_cot))
    ]

    def pick_images(j):
        own, padded = picked.shape[1:3]
        group = own * n_h
        lines = images.shape[1]
        image_loads[j].wait()
        step = 256 // group
        for first in range(0, padded, step):
            count = min(step, padded - first)
            taken = min(step * group, lines - first * group)
            shape = (own * count, taken)
            row = lax.broadcasted_iota(jnp.int32, shape, 0)
            column = lax.broadcasted_iota(jnp.int32, shape, 1)
            wanted = (row % count) * group + own * h + row // count
            chosen = (column == wanted).astype(F32).astype(BF16)
            source = images[j, first * group : first * group + taken]
            picked[j, :, first : first + count] = (
                dot(chosen, source).astype(BF16).reshape(own, count, images.shape[2])
            )
        image_stores[j].start()

    def at(k, place):
        first = pl.multiple_of((place[0] * n_t + place[2]) * rows, 16)
        lines = pl.ds(first, rows)
        return small.at[lines] if k == n_k else w.at[k, lines]

    def hop(q, origin, place, sems, j):
        return remote(at(q, origin), at(q, origin), sems.at[0, j], sems.at[1, j], place)

    def half_hop(q, origin, place, half):
        part = at(q, origin).at[pl.ds(*halves[half])]
        j = 2 * q + half
        return remote(part, part, d_sems.at[0, j], d_sems.at[1, j], place)

    me = (s, h, t)
    from_d = (across_x[0], h, across_y[2])
    sent = []

    def send(copy):
        copy.start()
        sent.append(copy)

    def assemble(k):
        for i in range(0, n_h, 2):
            lines = jnp.concatenate([lined[i, k], lined[i + 1, k]], axis=1)
            at(k, me)[:, i * block : (i + 2) * block] = dot(lines, pair).astype(BF16)
        if k == 0:
            lines = jnp.concatenate([lined[i, k] for i in range(n_h)], axis=1)
            at(n_k, me)[...] = (dot(lines, beside) + extra[...]).astype(BF16)
        for q in members(k):
            send(hop(q, me, across_x, x_sems, q))
            send(hop(q, me, across_y, y_sems, q))
            send(hop(q, me, sibling, c_sems, 4 * q))

    def members(k):
        return (0, n_k) if k == 0 else (k,)

    def relay_xy(k):
        for q in members(k):
            hop(q, across_x, across_x, x_sems, q).wait_recv()
            send(half_hop(q, across_x, across_y, 0))
            send(hop(q, across_x, sibling, c_sems, 4 * q + 1))
            hop(q, across_y, across_y, y_sems, q).wait_recv()
            send(half_hop(q, across_y, across_x, 1))
            send(hop(q, across_y, sibling, c_sems, 4 * q + 2))

    def relay_d(k):
        for q in members(k):
            half_hop(q, from_d, across_y, 0).wait_recv()
            half_hop(q, from_d, across_x, 1).wait_recv()
            send(hop(q, from_d, sibling, c_sems, 4 * q + 3))

    for wave in range(n_k + n_h - 2):
        for d in range(1, n_h):
            if 0 <= wave - d + 1 < n_k:
                relay(chunks[wave - d + 1], d)
        turn(2)
        i = wave - n_h + 2
        if i >= 0:
            assemble(chunks[i])
            if i in (1, 2):
                pick_images(i - 1)
            if i >= 1:
                relay_xy(chunks[i - 1])
            if i >= 2:
                relay_d(chunks[i - 2])
            turn(2)
    stores = []

    def arrive(q):
        for j in range(4):
            hop(q, me, sibling, c_sems, 4 * q + j).wait_recv()
        if q == n_k:
            stores.append(pltpu.make_async_copy(small, small_out, o_sems.at[q]))
        else:
            stores.append(pltpu.make_async_copy(w.at[q], w_out.at[q], o_sems.at[q]))
        stores[-1].start()

    def keep(first, last):
        for j in range(first, last):
            stores.append(pltpu.make_async_copy(held[j], held_out[j], h_sems.at[j]))
            stores[-1].start()

    ahead = Ahead(
        length, picked.at[0], small, w, blocks, dispatch, combine, held, joined, order
    )
    arrive(n_k)
    ahead.first_norm()
    relay_xy(chunks[-1])
    relay_d(chunks[-2])
    arrive(0)
    ahead.project(0)
    turn(2 * n_tiles)
    relay_d(chunks[-1])
    arrive(2)
    ahead.project(2)
    arrive(1)
    ahead.project(1)
    keep(0, 4)
    ahead.attend()
    arrive(3)
    ahead.finish()
    keep(4, 7)
    for copy in sent:
        copy.wait_send()
    for origin in range(n_h):
        @pl.when((origin <= h) & (h < n_h - 1))
        def _():
            for k in range(n_k):
                z_hop(k, origin, 1).wait_send()

        @pl.when((origin >= h) & (h > 0))
        def _():
            for k in range(n_k):
                z_hop(k, origin, 0).wait_send()

    for i in range(depth):
        store(2 * n_tiles - depth + i).wait()
    for copy in image_stores:
        copy.wait()
    for copy in stores:
        copy.wait()


def gather_weights(
    sizes, length, w_attn, phi_t, out_bias, scales, biases, in_bias, experts, tokens, cotangent
):
    n_k, rows, _ = w_attn.shape
    wide = 256
    n_s, n_h, n_t = sizes
    width = n_s * n_t * rows
    vmem = pl.BlockSpec(memory_space=pltpu.VMEM)
    hbm = pl.BlockSpec(memory_space=pl.ANY)
    dma = pltpu.SemaphoreType.DMA
    hidden = experts.shape[3]
    small = (width, wide)
    images = jax.ShapeDtypeStruct((2, 208, width), BF16)
    shape = jax.ShapeDtypeStruct
    keys = shape((2, 256, width), BF16)
    thin = shape((2, 208, 128), F32)
    held = (images, images, keys, keys, images, shape(images.shape, F32), images)
    return pl.pallas_call(
        partial(gather_kernel, sizes, length),
        out_shape=(
            jax.ShapeDtypeStruct((n_k, width, width), BF16),
            jax.ShapeDtypeStruct(small, BF16),
            jax.ShapeDtypeStruct((2, experts.shape[2], experts.shape[0], hidden), BF16),
            images, images, shape((n_h, n_s, 2, 16, width // n_s), BF16), thin, thin, *held,
        ),
        in_specs=[vmem] * 6 + [hbm] * 3,
        out_specs=(hbm,) * 5 + (vmem,) * 3 + (hbm,) * 7,
        scratch_shapes=[
            *[pltpu.VMEM(value.shape, value.dtype) for value in held],
            pltpu.VMEM((2 * width // n_s, 512), BF16),
            pltpu.VMEM((128, 128), BF16),
            pltpu.VMEM((n_k, width, width), BF16),
            pltpu.VMEM(small, BF16),
            pltpu.VMEM((n_h, n_k, rows, wide), BF16),
            pltpu.VMEM((rows, wide), F32),
            pltpu.VMEM((128, rows), F32),
            pltpu.VMEM((4, 16, 16, hidden), BF16),
            pltpu.VMEM((4, 16, 16, hidden), BF16),
            pltpu.VMEM((2, *tokens.shape), BF16),
            pltpu.VMEM((2, *images.shape), BF16),
            dma((n_k, n_h, 2)), dma((n_k, n_h)), dma((2, n_k + 1)), dma((2, n_k + 1)),
            dma((2, 2 * (n_k + 1))), dma((2, 4 * (n_k + 1))), dma((2, 4)), dma((n_k + 1,)),
            dma((2, 2)), dma((7,)),
        ],
        compiler_params=pltpu.CompilerParams(
            collective_id=3, has_side_effects=True, vmem_limit_bytes=VMEM_BYTES
        ),
        name="gather_weights",
    )(w_attn, phi_t, out_bias, scales, biases, in_bias, experts, tokens, cotangent)


def reduce_kernel(
    sizes, grads, small, out, core_in, core_small, met, met_small,
    d_in, d_small, x_in, x_small, y_in, y_small, pieces, z_in,
    c_sems, d_sems, x_sems, y_sems, z_send, z_recv,
):
    (s, h, t), core, chip, sibling, across_x, across_y, line = plane(sizes)
    n_k, width, _ = grads.shape
    n_s, n_h, n_t = sizes
    rows = width // (n_s * n_t)
    wide = pieces.shape[3]
    pair = n_t * rows
    half = rows // 2
    halves = (pl.ds(0, half), pl.ds(half, half))
    chunks = (0, 2, 1, 3)

    def members(k):
        return (0, n_k) if k == 0 else (k,)

    def pick(q, large, little):
        return little if q == n_k else large.at[q]

    def core_copy(q, x):
        first = pl.multiple_of((2 * x + 1 - core) * pair, 16)
        return remote(
            pick(q, grads, small).at[pl.ds(first, pair)],
            pick(q, core_in, core_small).at[x],
            c_sems.at[0, 2 * q + x], c_sems.at[1, 2 * q + x], sibling,
        )

    for k in chunks:
        for q in members(k):
            for x in range(2):
                core_copy(q, x).start()
    joined = pair_matrix(width // n_h, wide, True)
    shape = (small.shape[1], n_h * wide)
    row = lax.broadcasted_iota(jnp.int32, shape, 0)
    column = lax.broadcasted_iota(jnp.int32, shape, 1)
    lane, of = column % wide - width // n_h, column // wide
    beside = (lane >= 0) & (lane < 16) & (row == of * 16 + lane)
    beside |= (lane >= 16) & (lane < 20) & (row == n_h * 16 + lane - 16)
    beside = beside.astype(F32).astype(BF16)
    to_d, to_x, to_y = (d_in, d_small), (x_in, x_small), (y_in, y_small)
    sent = []

    def hop(q, kind, part, source, place):
        sems = {id(to_d): d_sems, id(to_x): x_sems, id(to_y): y_sems}[id(kind)]
        target = pick(q, *kind)
        target = target.at[part] if kind is to_d else target.at[halves[part]]
        j = 2 * q + part
        return remote(source, target, sems.at[0, j], sems.at[1, j], place)

    def send(copy):
        copy.start()
        sent.append(copy)

    def part_of(q, x, y, part):
        return pick(q, met, met_small).at[x, y].at[halves[part]]

    def arrived(q, kind, part):
        hop(q, kind, part, part_of(q, 0, 0, part), sibling).wait_recv()

    def open_up(q):
        part = pick(q, met, met_small)
        for x in range(2):
            core_copy(q, x).wait_recv()
            first = pl.multiple_of((2 * x + core) * pair, 16)
            own = pick(q, grads, small)[pl.ds(first, pair)].astype(F32)
            total = own + pick(q, core_in, core_small)[x].astype(F32)
            part[x] = total.astype(BF16).reshape(n_t, rows, total.shape[1])
        send(hop(q, to_d, 0, part_of(q, 1 - chip, 1 - t, 0), across_x))
        send(hop(q, to_d, 1, part_of(q, 1 - chip, 1 - t, 1), across_y))
        send(hop(q, to_x, 0, part_of(q, 1 - chip, t, 0), across_x))
        send(hop(q, to_y, 1, part_of(q, chip, 1 - t, 1), across_y))

    def pass_on(q):
        for part, kind, x, y, place in (
            (0, to_y, chip, 1 - t, across_y),
            (1, to_x, 1 - chip, t, across_x),
        ):
            arrived(q, to_d, part)
            block = part_of(q, x, y, part)
            total = block[...].astype(F32) + pick(q, *to_d)[part].astype(F32)
            block[...] = total.astype(BF16)
            send(hop(q, kind, part, block, place))

    def whole(q):
        for kind in (to_x, to_y):
            for part in range(2):
                arrived(q, kind, part)
        total = pick(q, met, met_small)[chip, t].astype(F32) + pick(q, *to_x)[...].astype(F32)
        return (total + pick(q, *to_y)[...].astype(F32)).astype(BF16)

    def z_copy(k, target, up):
        place = line[1] if up else line[n_h - 1]
        return remote(
            pieces.at[target, k], z_in.at[up, target, k],
            z_send.at[up, target, k], z_recv.at[up, target, k], place,
        )

    def pass_along(k, hops):
        for up in range(2):
            for target in range(n_h - 1, -1, -1) if up else range(n_h):
                further = target > h if up else target < h

                @pl.when(further & (h == (hops if up else n_h - 1 - hops)))
                def _():
                    if hops > 0:
                        z_copy(k, target, up).wait_recv()
                        total = pieces[target, k].astype(F32) + z_in[up, target, k].astype(F32)
                        pieces[target, k] = total.astype(BF16)
                    z_copy(k, target, up).start()

    def share_out(k):
        value = whole(k)
        columns = width // n_h
        if k == 0:
            little = dot(whole(n_k), beside)
        for i in range(0, n_h, 2):
            lanes = dot(value[:, i * columns : (i + 2) * columns], joined)
            if k == 0:
                lanes = lanes + little[:, i * wide : (i + 2) * wide]
            pieces[i, k] = lanes[:, :wide].astype(BF16)
            pieces[i + 1, k] = lanes[:, wide:].astype(BF16)
        pass_along(k, 0)

    for i in range(n_k + 2 + n_h - 2):
        if i < n_k:
            for q in members(chunks[i]):
                open_up(q)
        if 0 <= i - 1 < n_k:
            for q in members(chunks[i - 1]):
                pass_on(q)
        if 0 <= i - 2 < n_k:
            share_out(chunks[i - 2])
        for hops in range(1, n_h - 1):
            if 0 <= i - 2 - hops < n_k:
                pass_along(chunks[i - 2 - hops], hops)
    for k in chunks:
        out[k] = pieces[h, k].astype(F32)
        for up, there in ((1, h > 0), (0, h < n_h - 1)):
            @pl.when(there)
            def _():
                z_copy(k, h, up).wait_recv()
                out[k] = out[k] + z_in[up, h, k].astype(F32)

    for k in chunks:
        for q in members(k):
            for x in range(2):
                core_copy(q, x).wait_send()
    for copy in sent:
        copy.wait_send()
    for target in range(n_h):
        for up in range(2):
            @pl.when(target > h if up else target < h)
            def _():
                for k in range(n_k):
                    z_copy(k, target, up).wait_send()


def reduce_grads(sizes, grads, small):
    n_k, width, _ = grads.shape
    n_s, n_h, n_t = sizes
    rows, wide, thin = width // (n_s * n_t), 256, small.shape[1]
    vmem = pl.BlockSpec(memory_space=pltpu.VMEM)
    dma = pltpu.SemaphoreType.DMA

    def buffers(*lead):
        return [
            pltpu.VMEM((n_k, *lead, width), BF16),
            pltpu.VMEM((*lead, thin), BF16),
        ]

    return pl.pallas_call(
        partial(reduce_kernel, sizes),
        out_shape=jax.ShapeDtypeStruct((n_k, rows, wide), F32),
        in_specs=[vmem, vmem],
        out_specs=vmem,
        scratch_shapes=[
            *buffers(2, n_t * rows), *buffers(2, n_t, rows),
            *buffers(2, rows // 2), *buffers(rows), *buffers(rows),
            pltpu.VMEM((n_h, n_k, rows, wide), BF16),
            pltpu.VMEM((2, n_h, n_k, rows, wide), BF16),
            dma((2, 2 * (n_k + 1))), dma((2, 2 * (n_k + 1))), dma((2, 2 * (n_k + 1))),
            dma((2, 2 * (n_k + 1))), dma((2, n_h, n_k)), dma((2, n_h, n_k)),
        ],
        compiler_params=pltpu.CompilerParams(
            collective_id=4, has_side_effects=True, vmem_limit_bytes=VMEM_BYTES
        ),
        name="reduce_grads",
    )(grads, small)


def experts_kernel(
    sizes, blocks_0, weights, small, combine, hidden, cotangent,
    slots_0_out, act_0_out, slots_1_out, act_1_out, back_out, bias_out, sum_out, grad_logits,
    gathered,
    w_0, w_1, gate, sums, slots_both, act_both, core_out, core_both, x_out, x_both, land_both, leave,
    back, back_both, blocks_1, output, combine_v, hidden_v, cotangent_v, padded, bias, bias_all,
    bias_send, bias_land,
    w_sem, o_sem, m_sem, in_both, return_both, core_sem, x_sem, act_sem, b_sems, g_send, g_recv, g_sem,
):
    peers = Peers(sizes)
    s, h, t = peers.at
    n_s, n_h, n_t = sizes
    me = peers.flat(peers.at)
    core, chip = lax.rem(s, 2), s // 2
    sibling = (s + 1 - 2 * core, h, t)
    across = (lax.rem(s + 2, n_s), h, t)
    half = act_both.shape[1] // 2
    own, other = core * half, (1 - core) * half
    n_blocks = peers.count
    loads = [
        pltpu.make_async_copy(weights.at[0], w_0, w_sem.at[0]),
        pltpu.make_async_copy(weights.at[1], w_1, w_sem.at[1]),
    ]
    kept = [
        pltpu.make_async_copy(source, target, m_sem.at[j])
        for j, (source, target) in enumerate(
            ((combine, combine_v), (hidden, hidden_v), (cotangent, cotangent_v))
        )
    ]
    for load in loads + kept:
        load.start()
    few = half // 2
    group = 16
    many = 2 * group
    peers.greet_all()

    def each(function, count=n_blocks, start=1):
        lax.fori_loop(start, count, lambda k, carry: (function(k), carry)[1], 0)

    out_row = lax.broadcasted_iota(jnp.int32, (16 * group, 16 * group), 0)
    in_row = lax.broadcasted_iota(jnp.int32, (16 * group, 16 * group), 1)
    there = (out_row // many == in_row % (2 * few)) & (out_row % many == in_row // (2 * few))
    there = there.astype(F32).astype(BF16)
    again = (in_row // many == out_row % (2 * few)) & (in_row % many == out_row // (2 * few))
    again = again.astype(F32).astype(BF16)
    stores = []

    def run(backward):
        n = 1 if backward else 0
        blocks = blocks_1 if backward else blocks_0
        w_a, w_b = (w_1, w_0) if backward else (w_0, w_1)
        slots, act, core_in, x_in, land, land_back = (
            both.at[n] for both in (slots_both, act_both, core_both, x_both, land_both, back_both)
        )
        in_sems, back_sems, core_sems, x_sems, act_sems = (
            both.at[n] for both in (in_both, return_both, core_sem, x_sem, act_sem)
        )
        def block_out(p, k):
            place = peers.step(k, 1)
            return remote(
                blocks.at[place[1], place[0], p], land.at[p, me],
                in_sems.at[0, p, k], in_sems.at[1, p, k], place,
            )

        def block_in(p, k):
            source = peers.flat(peers.step(k, -1))
            return remote(
                blocks.at[0, 0, p], land.at[p, source], in_sems.at[0, p, k], in_sems.at[1, p, k], sibling
            )

        for p in range(2):
            for k in range(1, n_blocks):
                block_out(p, k).start()
            land[p, me] = blocks[h, s, p]
        def receive(p):
            each(lambda k: block_in(p, k).wait_recv())
            for b in range(n_blocks // group):
                rows = land[p, b * group : (b + 1) * group].reshape(group * 16, land.shape[3])
                turned = dot(there, rows).astype(BF16).reshape(2 * few, many, land.shape[3])
                for c in range(2):
                    first = c * half + p * few
                    slots[first : first + few, b * many : (b + 1) * many, :] = turned[
                        c * few : (c + 1) * few
                    ]

        if backward:
            own_images = output.shape[0]
            line = [(s, lax.rem(h + d, n_h), t) for d in range(n_h)]
            g_own = pltpu.make_async_copy(output, gathered.at[pl.ds(h * own_images, own_images)], g_sem)
            g_own.start()

            def z_hop(i, origin, up, source=None):
                there = gathered.at[origin * own_images + i]
                return remote(
                    there if source is None else source, there,
                    g_send.at[i, origin, up], g_recv.at[i, origin], line[1] if up else line[n_h - 1],
                )

            def relay(i, d):
                @pl.when(h >= d)
                def _():
                    z_hop(i, h - d, 1).wait_recv()

                    @pl.when((h < n_h - 1) & (d < n_h - 1))
                    def _():
                        z_hop(i, h - d, 1).start()

                @pl.when(h + d < n_h)
                def _():
                    z_hop(i, h + d, 0).wait_recv()

                    @pl.when((h > 0) & (d < n_h - 1))
                    def _():
                        z_hop(i, h + d, 0).start()

            def gather_output():
                for i in range(own_images):
                    @pl.when(h < n_h - 1)
                    def _():
                        z_hop(i, h, 1, output.at[i]).start()

                    @pl.when(h > 0)
                    def _():
                        z_hop(i, h, 0, output.at[i]).start()
        else:
            piece, count = 6 * 64, act.shape[2] // (6 * 64)
            row = lax.broadcasted_iota(jnp.int32, (6 * 128, piece), 0)
            column = lax.broadcasted_iota(jnp.int32, (6 * 128, piece), 1)
            lane = row % 128
            place = (lane < 64) & (column == (row // 128) * 64 + lane)
            place = place.astype(F32).astype(BF16)
            for m in range(count):
                first = (t * count + m) * 96
                lines = [
                    small[pl.ds(pl.multiple_of(first + j * 16, 16), 16), 128:256] for j in range(6)
                ]
                bias[:, m * piece : (m + 1) * piece] = dot(jnp.concatenate(lines, axis=1), place)

        receive(0)
        if backward:
            gather_output()
        if not backward:
            loads[0].wait()

        def core_copy(j):
            return remote(
                core_out.at[j], core_in.at[j], core_sems.at[0, j], core_sems.at[1, j], sibling
            )

        def x_copy(j):
            return remote(x_out.at[j], x_in.at[j], x_sems.at[0, j], x_sems.at[1, j], across)

        def act_copy(j):
            return remote(
                act.at[own + j], act.at[own + j], act_sems.at[0, j], act_sems.at[1, j], sibling
            )

        def act_in(j):
            return remote(
                act.at[other + j], act.at[other + j], act_sems.at[0, j], act_sems.at[1, j], sibling
            )

        def meet(j):
            core_copy(j).wait_recv()
            sums[j] = sums[j] + core_in[j].astype(F32)
            x_out[j] = sums[j].astype(BF16)
            x_copy(j).start()

        def first_sums(j):
            core_out[j] = dot(slots[other + j], w_a[other + j]).astype(BF16)
            core_copy(j).start()

            @pl.when(j > 0)
            def _():
                meet(j - 1)

            sums[j] = dot(slots[own + j], w_a[own + j])

        each(first_sums, few, 0)
        receive(1)
        each(first_sums, half, few)
        meet(half - 1)
        if not backward:
            loads[1].wait()

        def second(e):
            leave[e] = dot_t(act[e], w_b[e]).astype(BF16)

        def finish(j):
            x_copy(j).wait_recv()
            value = sums[j] + x_in[j].astype(F32)
            if backward:
                act[own + j] = (value * gate[j]).astype(BF16)
            else:
                value = value + bias[pl.ds(own + j, 1), :]
                cumulative = 0.5 + 0.5 * lax.erf(value * 0.7071067811865476)
                act[own + j] = (value * cumulative).astype(BF16)
                gate[j] = cumulative + value * (
                    jnp.exp(value * value * -0.5) * 0.3989422804014327
                )
            act_copy(j).start()
            second(own + j)

            @pl.when(j > 0)
            def _():
                act_in(j - 1).wait_recv()
                second(other + j - 1)

            if backward:
                for when, i, d in ((2, 0, 1), (3, 1, 1), (5, 0, 2), (7, 1, 2)):
                    @pl.when(j == when)
                    def _():
                        relay(i, d)

        def back_copy(p, k):
            place = peers.step(k, 1)
            return remote(
                back.at[p, peers.flat(place)], land_back.at[p, me],
                back_sems.at[0, p, k], back_sems.at[1, p, k], place,
            )

        def back_in(p, k):
            source = peers.flat(peers.step(k, -1))
            return remote(
                back.at[p, 0], land_back.at[p, source],
                back_sems.at[0, p, k], back_sems.at[1, p, k], sibling,
            )

        def give_back(p):
            for b in range(n_blocks // group):
                rows = jnp.concatenate(
                    [
                        leave[c * half + p * few : c * half + (p + 1) * few, b * many : (b + 1) * many, :]
                        for c in range(2)
                    ],
                    axis=0,
                ).reshape(group * 16, leave.shape[2])
                turned = dot(again, rows).astype(BF16)
                back[p, b * group : (b + 1) * group] = turned.reshape(group, 16, leave.shape[2])
            for k in range(1, n_blocks):
                back_copy(p, k).start()
            land_back[p, me] = back[p, me]

        each(finish, few + 1, 0)
        give_back(0)
        each(finish, half, few + 1)
        act_in(half - 1).wait_recv()
        second(other + half - 1)
        give_back(1)
        outs = (slots_1_out, act_1_out) if backward else (slots_0_out, act_0_out)
        for j, (source, target) in enumerate(zip((slots, act), outs)):
            stores.append(pltpu.make_async_copy(source, target, o_sem.at[n, j]))
            stores[-1].start()
        if backward:
            across_t = (s, h, 1 - t)
            width = bias_out.shape[1]

            def bias_row(e):
                bias_all[pl.ds(e, 1), :] = jnp.sum(act[e].astype(F32), axis=0, keepdims=True)

            each(bias_row, 2 * half, 0)

            def slot_row(e):
                total = jnp.sum(slots[e].astype(F32), axis=0, keepdims=True)
                sum_out[pl.ds(e, 1), : slots.shape[2]] = total

            sum_out[...] = jnp.zeros_like(sum_out)
            each(slot_row, 2 * half, 0)

            def piece(for_t):
                return bias_all[:, pl.ds(pl.multiple_of((core * n_t + for_t) * width, 128), width)]

            bias_send[...] = piece(1 - t)
            bias_copy = remote(bias_send, bias_land, b_sems.at[0], b_sems.at[1], across_t)
            bias_copy.start()
            bias_copy.wait()
            bias_out[...] = jnp.where(t == chip, piece(t), bias_land[...])
        for p in range(2):
            each(lambda k: back_in(p, k).wait_recv())
        if backward:
            back_out[...] = land_back[...]
            relay(0, 3)
            relay(1, 3)
            g_own.wait()
            for origin in range(n_h):
                @pl.when((origin < h) & (h < n_h - 1))
                def _():
                    for i in range(own_images):
                        z_hop(i, origin, 1).wait_send()

                @pl.when((origin > h) & (h > 0))
                def _():
                    for i in range(own_images):
                        z_hop(i, origin, 0).wait_send()

            @pl.when(h < n_h - 1)
            def _():
                for i in range(own_images):
                    z_hop(i, h, 1, output.at[i]).wait_send()

            @pl.when(h > 0)
            def _():
                for i in range(own_images):
                    z_hop(i, h, 0, output.at[i]).wait_send()

        for p in range(2):
            each(lambda k: block_out(p, k).wait_send())
            each(lambda k: back_copy(p, k).wait_send())
        for copy in (core_copy, x_copy, act_copy):
            each(lambda j: copy(j).wait_send(), half, 0)

    run(False)
    for copy in kept:
        copy.wait()
    middle_kernel(
        sizes, back_both.at[0], small, combine_v, hidden_v, cotangent_v, output, blocks_1, grad_logits,
        padded,
    )
    run(True)
    for store in stores:
        store.wait()


def experts_pass(sizes, blocks, weights, small, combine, hidden, cotangent, bias_width):
    _, experts, rows, width = weights.shape
    devices = sizes[0] * sizes[1] * sizes[2]
    images = 2 * devices
    half = experts // 2
    vmem = pl.BlockSpec(memory_space=pltpu.VMEM)
    hbm = pl.BlockSpec(memory_space=pl.ANY)
    shape, dma = jax.ShapeDtypeStruct, pltpu.SemaphoreType.DMA
    slots, act = (experts, images, rows), (experts, images, width)
    chunk = (half, images, width)
    block = (2, devices, experts, rows)
    own = hidden.shape[0]
    weight = pltpu.VMEM((experts, rows, width), BF16)
    return pl.pallas_call(
        partial(experts_kernel, sizes),
        out_shape=(
            shape(slots, BF16), shape(act, BF16), shape(slots, BF16), shape(act, BF16),
            shape(block, BF16), shape((experts, bias_width), F32), shape((experts, 256), F32),
            shape((own, hidden.shape[1], 64), F32),
            shape((sizes[1] * own, *hidden.shape[1:]), BF16),
        ),
        in_specs=[vmem, hbm, vmem, hbm, hbm, hbm],
        out_specs=(hbm, hbm, hbm, hbm, vmem, vmem, vmem, vmem, hbm),
        scratch_shapes=[
            weight, weight,
            pltpu.VMEM(chunk, F32), pltpu.VMEM(chunk, F32),
            pltpu.VMEM((2, *slots), BF16), pltpu.VMEM((2, *act), BF16),
            pltpu.VMEM(chunk, BF16), pltpu.VMEM((2, *chunk), BF16),
            pltpu.VMEM(chunk, BF16), pltpu.VMEM((2, *chunk), BF16),
            pltpu.VMEM((2, *block), BF16), pltpu.VMEM(slots, BF16),
            pltpu.VMEM(block, BF16), pltpu.VMEM((2, *block), BF16),
            pltpu.VMEM(blocks.shape, BF16), pltpu.VMEM(hidden.shape, BF16),
            pltpu.VMEM(combine.shape, F32), pltpu.VMEM(hidden.shape, F32),
            pltpu.VMEM(cotangent.shape, BF16), pltpu.VMEM((2, 128, 256), F32),
            pltpu.VMEM((experts, width), F32), pltpu.VMEM((experts, width), F32),
            pltpu.VMEM((experts, bias_width), F32), pltpu.VMEM((experts, bias_width), F32),
            dma((2,)), dma((2, 2)), dma((3,)), dma((2, 2, 2, devices)), dma((2, 2, 2, devices)),
            dma((2, 2, half)), dma((2, 2, half)), dma((2, 2, half)), dma((2,)),
            dma((own, sizes[1], 2)), dma((own, sizes[1])), dma,
        ],
        compiler_params=pltpu.CompilerParams(
            collective_id=1, has_side_effects=True, vmem_limit_bytes=VMEM_BYTES
        ),
        name="experts",
    )(blocks, weights, small, combine, hidden, cotangent)


def weight_grad_kernel(slots_0, act_0, slots_1, act_1, out, lines, pick, same):
    group, images, rows = slots_0.shape
    d_block = out.shape[0]
    few = group // 2
    m, d = pl.program_id(0), pl.program_id(2)

    @pl.when((m == 0) & (pl.program_id(1) == 0) & (d == 0))
    def _():
        row = lax.broadcasted_iota(jnp.int32, pick.shape[1:], 0)
        column = lax.broadcasted_iota(jnp.int32, pick.shape[1:], 1)
        second = (row % group) // few
        for half in range(2):
            feature = 2 * (row // group) + (second if half == 0 else 1 - second)
            pick[half] = (column == feature).astype(F32).astype(BF16)
        row = lax.broadcasted_iota(jnp.int32, same.shape, 0)
        column = lax.broadcasted_iota(jnp.int32, same.shape, 1)
        same[...] = (row % few == column // images).astype(F32)

    def prepare(slots):
        @pl.when(d == 0)
        def _():
            turned = slots[...].reshape(group * images, rows).astype(F32)
            lines[...] = jnp.swapaxes(turned, 0, 1).astype(BF16)

    def term(act):
        mine = lines[pl.ds(pl.multiple_of(d * d_block, d_block), d_block)]
        width = act.shape[2]
        results = []
        for half in range(2):
            columns = mine[:, half * few * images : (half + 1) * few * images]
            spread = (dot(pick[half], columns) * same[...]).astype(BF16)
            values = act[half * few : (half + 1) * few].reshape(few * images, width)
            results.append(dot(spread, values).reshape(d_block // 2, group, width))
        first, last = results
        low = lax.broadcasted_iota(jnp.int32, first.shape, 1) < few
        even = jnp.where(low, first, last)
        odd = pltpu.roll(jnp.where(low, last, first), few, 1)
        out[...] = jnp.stack((even, odd), axis=1).reshape(out.shape)

    @pl.when(m == 0)
    def _():
        prepare(slots_0)
        term(act_0)

    @pl.when(m == 1)
    def _():
        prepare(slots_1)
        term(act_1)


def weight_grads(slots_0, act_0, slots_1, act_1):
    experts, images, rows = slots_0.shape
    hidden = act_0.shape[2]
    group, d_block = 8, 192
    last = experts // group - 1

    def early(m, g, d):
        return jnp.where(m == 0, g, last), 0, 0

    def late(m, g, d):
        return jnp.where(m == 0, 0, g), 0, 0

    slots, act = (group, images, rows), (group, images, hidden)
    return pl.pallas_call(
        weight_grad_kernel,
        grid=(2, experts // group, rows // d_block),
        out_shape=jax.ShapeDtypeStruct((rows, 2, experts, hidden), F32),
        in_specs=[
            pl.BlockSpec(slots, early), pl.BlockSpec(act, early),
            pl.BlockSpec(slots, late), pl.BlockSpec(act, late),
        ],
        out_specs=pl.BlockSpec((d_block, 1, group, hidden), lambda m, g, d: (d, m, g, 0)),
        scratch_shapes=[
            pltpu.VMEM((rows, group * images), BF16),
            pltpu.VMEM((2, group * d_block // 2, d_block), BF16),
            pltpu.VMEM((group * d_block // 2, group * images // 2), F32),
        ],
        compiler_params=pltpu.CompilerParams(vmem_limit_bytes=VMEM_BYTES),
        cost_estimate=pl.CostEstimate(
            flops=4 * images * experts * rows * hidden,
            bytes_accessed=8 * rows * experts * hidden,
            transcendentals=0,
        ),
        name="weight_grads",
    )(slots_0, act_0, slots_1, act_1)


def dot_r(a, b):
    return lax.dot_general(a, b, (((0,), (0,)), ((), ())), preferred_element_type=F32)


def row_of(shape, axis):
    return lax.broadcasted_iota(jnp.int32, shape, axis)


def one_hot(mask):
    return mask.astype(F32).astype(BF16)


def order_matrix(n_h, few, back):
    n = n_h * 8 * few
    shape = (n, n)
    blocked, natural = row_of(shape, 1 if back else 0), row_of(shape, 0 if back else 1)
    f, half, image = blocked % few, (blocked // few) % 2, (blocked // (2 * few)) % 2
    group = blocked // (4 * few)
    if back:
        part, h = group // n_h, group % n_h
    else:
        h, part = group // 2, group % 2
    expert = ((h * 2 + half) * 2 + part) * few + f
    return one_hot(natural == image * (4 * n_h * few) + expert)


def norm_parts(x, scale, shift, live):
    centered = x - jnp.mean(x, axis=-1, keepdims=True)
    inverse = lax.rsqrt(jnp.mean(centered * centered, axis=-1, keepdims=True) + epsilon)
    unit = centered * inverse
    return unit * scale + shift, unit, inverse


def norm_back(grad, unit, inverse, scale):
    scaled = grad * scale
    average = jnp.mean(scaled, axis=-1, keepdims=True)
    projection = jnp.mean(scaled * unit, axis=-1, keepdims=True)
    return (
        inverse * (scaled - average - unit * projection),
        jnp.sum(grad * unit, axis=0, keepdims=True),
        jnp.sum(grad, axis=0, keepdims=True),
    )


def norm_rows(small):
    return jnp.swapaxes(small[:, 128:].astype(F32), 0, 1)[64:68]


def slots_to_blocks(slots, blocks, columns, joined, order):
    n_h, n_s = blocks.shape[:2]
    turned = dot(order, slots).astype(BF16)
    wide = joined.shape[1] // 2
    for s in range(0, n_s, 2):
        lanes = dot(turned[:, s * columns : (s + 2) * columns], joined).astype(BF16)
        for h in range(n_h):
            for p in range(2):
                rows = (h * 2 + p) * 16
                for e in range(2):
                    blocks[h, s + e, p] = lanes[rows : rows + 16, e * wide : e * wide + columns]


def blocks_to_slots(back, sizes, order, pair, padded):
    n_s, n_h, n_t = sizes
    columns = back.shape[3]
    both = jnp.concatenate([order] * n_t, axis=1)
    results = []
    for s in range(n_s):
        rows = jnp.concatenate(
            [
                back[p, (s * n_h + h) * n_t + t]
                for t in range(n_t)
                for p in range(2)
                for h in range(n_h)
            ],
            axis=0,
        )
        padded[s % 2, :, :columns] = dot(both, rows)
        if s % 2:
            value = jnp.concatenate([padded[0], padded[1]], axis=1)
            high = value.astype(BF16)
            rest = (value - high.astype(F32)).astype(BF16)
            results.append(dot(high, pair) + dot(rest, pair))
    return jnp.concatenate(results, axis=1)


def live_rows(shape, length):
    return row_of(shape, 0) < length


class Ahead:
    def __init__(self, length, tokens, small, w, blocks, dispatch, combine, held, joined, order):
        self.length, self.tokens, self.small, self.w = length, tokens, small, w
        self.blocks, self.dispatch, self.combine = blocks, dispatch, combine
        self.normed_1, self.query, self.keyed, self.valued = held[:4]
        self.context, self.hidden, self.normed_2 = held[4:]
        self.joined, self.order = joined, order
        self.n, self.rows, self.width = tokens.shape
        self.live = live_rows((self.rows, 1), length)

    def first_norm(self):
        self.norms = norm_rows(self.small)
        for i in range(self.n):
            value, _, _ = norm_parts(
                self.tokens[i].astype(F32), self.norms[0:1], self.norms[2:3], self.live
            )
            self.normed_1[i] = jnp.where(self.live, value, 0.0).astype(BF16)
        self.joined[...] = pair_matrix(self.blocks.shape[4], self.joined.shape[1] // 2, True)
        self.order[...] = order_matrix(self.blocks.shape[0], 4, False)

    def project(self, k):
        n, rows, width = self.n, self.rows, self.width
        flat = self.normed_1[...].reshape(n * rows, width)
        value = dot(flat, self.w[k]).astype(BF16).reshape(n, rows, width)
        if k == 0:
            self.query[...] = value
        else:
            target = self.keyed if k == 1 else self.valued
            keys = target.shape[1]
            target[:, :rows] = value
            target[:, rows:] = jnp.zeros((n, keys - rows, width), BF16)

    def attend(self):
        query, keyed, valued, context = self.query, self.keyed, self.valued, self.context
        rows, keys = self.rows, keyed.shape[1]
        factor = HEAD_DIM ** (-0.5)
        pairs = self.width // 128
        lane = row_of((rows, 128), 1)
        shown = row_of((rows, keys), 1) < self.length

        def attend(step, carry):
            i = step // pairs
            lanes = pl.ds(pl.multiple_of((step % pairs) * 128, 128), 128)
            q, k, v = query[i, :, lanes], keyed[i, :, lanes], valued[i, :, lanes]
            scaled = q * jnp.bfloat16(factor)
            parts = []
            for a in range(2):
                mine = (lane < 64) if a == 0 else (lane >= 64)
                scores = dot_t(jnp.where(mine, scaled, jnp.zeros_like(q)), k)
                scores = jnp.where(shown, scores, -1e30)
                exponent = jnp.exp(scores - jnp.max(scores, axis=-1, keepdims=True))
                probs = exponent * (1.0 / jnp.sum(exponent, axis=-1, keepdims=True))
                parts.append(dot(probs.astype(BF16), v))
            context[i, :, lanes] = jnp.where(lane < 64, parts[0], parts[1]).astype(BF16)
            return carry

        lax.fori_loop(0, self.n * pairs, attend, 0, unroll=6)

    def finish(self):
        n, rows, width = self.n, self.rows, self.width
        flat = (n * rows, width)
        live = self.live
        attended = dot_t(self.context[...].reshape(flat), self.w[3]).reshape(n, rows, width)
        for i in range(n):
            value = self.tokens[i].astype(F32) + attended[i]
            self.hidden[i] = value
            value, _, _ = norm_parts(value, self.norms[1:2], self.norms[3:4], live)
            self.normed_2[i] = jnp.where(live, value, 0.0).astype(BF16)
        logits = dot(self.normed_2[...].reshape(flat), self.small[:, :128]).reshape(n, rows, 128)
        experts = row_of((rows, 128), 1) < 64
        slots = []
        for i in range(n):
            here = logits[i]
            down = jnp.where(live, here, -1e30)
            exponent = jnp.exp(down - jnp.max(down, axis=0, keepdims=True))
            dispatch = exponent / jnp.sum(exponent, axis=0, keepdims=True)
            dispatch = jnp.where(experts, dispatch, 0.0)
            across = jnp.where(experts, here, -1e30)
            exponent = jnp.exp(across - jnp.max(across, axis=1, keepdims=True))
            combine = exponent / jnp.sum(exponent, axis=1, keepdims=True)
            self.dispatch[i] = dispatch
            self.combine[i] = combine
            slots.append(dot_r(dispatch.astype(BF16), self.normed_2[i])[:64].astype(BF16))
        slots_to_blocks(
            jnp.concatenate(slots, axis=0), self.blocks, self.blocks.shape[4], self.joined[...],
            self.order[...],
        )


def middle_kernel(
    sizes, back, small, combine, hidden, cotangent, output, blocks, grad_logits, padded
):
    n, rows, _ = hidden.shape
    columns = back.shape[3]
    padded[...] = jnp.zeros_like(padded)
    pair = pair_matrix(columns, padded.shape[2], False)
    joined = pair_matrix(columns, padded.shape[2], True)
    total = blocks_to_slots(back, sizes, order_matrix(sizes[1], 4, True), pair, padded)
    bias = jnp.swapaxes(small[:, :128].astype(F32), 0, 1)[64:]
    slots = []
    for i in range(n):
        slot_out = (total[i * 64 : (i + 1) * 64] + bias).astype(BF16)
        combine_b = combine[i].astype(BF16)[:, :64]
        output[i] = (hidden[i] + dot(combine_b, slot_out)).astype(BF16)
        grad_combine = dot_t(cotangent[i], slot_out)
        weight = combine[i][:, :64]
        weighted = jnp.sum(weight * grad_combine, axis=1, keepdims=True)
        grad_logits[i] = weight * (grad_combine - weighted)
        slots.append(dot_r(combine_b, cotangent[i]).astype(BF16))
    slots_to_blocks(
        jnp.concatenate(slots, axis=0), blocks, columns, joined, order_matrix(sizes[1], 4, False)
    )


def behind_kernel(
    sizes, length, back, small, w_hbm, *refs,
):
    later, refs = refs[:6], refs[6:]
    (hidden, normed_2, dispatch, grad_logits, cotangent, grads_out, small_grads, input_grad,
     w, padded, grad_hidden, rounded, grad_context, grad_q, grad_k, grad_v, grads, *refs) = refs
    held, (w_sem, l_sem, g_sem) = refs[:6], refs[6:]
    n, rows, width = hidden.shape
    later_loads = [
        pltpu.make_async_copy(source, target, l_sem.at[j])
        for j, (source, target) in enumerate(zip(later, held))
    ]
    context, query, keyed, valued, normed_1, tokens = held
    keys = keyed.shape[1]
    loads = [pltpu.make_async_copy(w_hbm.at[k], w.at[k], w_sem.at[k]) for k in range(4)]
    for load in loads[3:] + later_loads + loads[:3]:
        load.start()
    norms = norm_rows(small)
    padded[...] = jnp.zeros_like(padded)
    pair = pair_matrix(back.shape[3], padded.shape[2], False)
    grad_slots = blocks_to_slots(
        back, sizes, order_matrix(sizes[1], 4, True), pair, padded
    ).astype(BF16)
    phi = small[:, :64]
    phi_grad = jnp.zeros((width, 64), F32)
    sums = []
    flat = (n * rows, width)
    for i in range(n):
        slots = grad_slots[i * 64 : (i + 1) * 64]
        weight = dispatch[i][:, :64]
        grad_dispatch = dot_t(normed_2[i], slots)
        weighted = jnp.sum(weight * grad_dispatch, axis=0, keepdims=True)
        logits = (weight * (grad_dispatch - weighted) + grad_logits[i]).astype(BF16)
        phi_grad = phi_grad + dot_r(normed_2[i], logits)
        grad = dot(weight.astype(BF16), slots) + dot_t(logits, phi)
        _, unit, inverse = norm_parts(hidden[i], norms[1:2], norms[3:4], None)
        grad_in, scale_grad, bias_grad = norm_back(grad, unit, inverse, norms[1:2])
        value = cotangent[i].astype(F32) + grad_in
        grad_hidden[i] = value
        rounded[i] = value.astype(BF16)
        sums.append((scale_grad, bias_grad))
    scale_2, bias_2 = sums[0][0] + sums[1][0], sums[0][1] + sums[1][1]
    flat_rounded = rounded[...].reshape(flat)
    loads[3].wait()
    grad_context[...] = dot(flat_rounded, w[3]).astype(BF16).reshape(n, rows, width)
    later_loads[0].wait()
    grads[3] = dot_r(flat_rounded, context[...].reshape(flat)).astype(BF16)
    stores = [pltpu.make_async_copy(grads.at[k], grads_out.at[k], g_sem.at[k]) for k in range(4)]
    stores[3].start()
    for load in later_loads[1:4]:
        load.wait()
    factor = HEAD_DIM ** (-0.5)
    pairs = width // 128
    lane = row_of((rows, 128), 1)
    key_lane = row_of((keys, 128), 1)
    shown = row_of((keys, rows), 0) < length

    def attend(step, carry):
        i = step // pairs
        lanes = pl.ds(pl.multiple_of((step % pairs) * 128, 128), 128)
        q, k, v = query[i, :, lanes], keyed[i, :, lanes], valued[i, :, lanes]
        scaled = q * jnp.bfloat16(factor)
        g = grad_context[i, :, lanes]
        to_q, to_k, to_v = [], [], []
        for a in range(2):
            mine = (lane < 64) if a == 0 else (lane >= 64)
            scores = dot_t(k, jnp.where(mine, scaled, jnp.zeros_like(q)))
            grad_probs = dot_t(v, jnp.where(mine, g, jnp.zeros_like(g)))
            scores = jnp.where(shown, scores, -1e30)
            exponent = jnp.exp(scores - jnp.max(scores, axis=0, keepdims=True))
            probs = exponent * (1.0 / jnp.sum(exponent, axis=0, keepdims=True))
            weighted = jnp.sum(probs * grad_probs, axis=0, keepdims=True)
            grad_scores = (probs * (grad_probs - weighted)).astype(BF16)
            to_v.append(dot(probs.astype(BF16), g))
            to_q.append(dot_r(grad_scores, k))
            to_k.append(dot(grad_scores, q))
        grad_q[i, :, lanes] = (jnp.where(lane < 64, to_q[0], to_q[1]) * factor).astype(BF16)
        kept = key_lane < 64
        grad_k[i, :, lanes] = (jnp.where(kept, to_k[0], to_k[1]) * factor)[:rows].astype(BF16)
        grad_v[i, :, lanes] = jnp.where(kept, to_v[0], to_v[1])[:rows].astype(BF16)
        return carry

    lax.fori_loop(0, n * pairs, attend, 0, unroll=6)
    for load in later_loads[4:]:
        load.wait()
    total = jnp.zeros(flat, F32)
    turned = jnp.swapaxes(normed_1[...].reshape(flat).astype(F32), 0, 1).astype(BF16)
    for k, source in enumerate((grad_q, grad_k, grad_v)):
        loads[k].wait()
        value = source[...].reshape(flat)
        total = total + dot_t(value, w[k])
        grads[k] = dot(turned, value).astype(BF16)
        stores[k].start()
    total = total.reshape(n, rows, width)
    sums = []
    for i in range(n):
        _, unit, inverse = norm_parts(tokens[i].astype(F32), norms[0:1], norms[2:3], None)
        grad_in, scale_grad, bias_grad = norm_back(total[i], unit, inverse, norms[0:1])
        input_grad[i] = (grad_hidden[i] + grad_in).astype(BF16)
        sums.append((scale_grad, bias_grad))
    scale_1, bias_1 = sums[0][0] + sums[1][0], sums[0][1] + sums[1][1]
    line = row_of((128, width), 0)
    spread = jnp.zeros((128, width), F32)
    for j, value in enumerate((scale_1, scale_2, bias_1, bias_2)):
        spread = jnp.where(line == 64 + j, value, spread)
    small_grads[...] = jnp.swapaxes(spread, 0, 1).astype(BF16)
    small_grads[:, :64] = phi_grad.astype(BF16)
    for store in stores:
        store.wait()


def tokens_behind(sizes, length, back, small, weights, later, kept, grad_logits, cotangent):
    tokens = later[-1]
    n, rows, width = tokens.shape
    vmem, hbm = pl.BlockSpec(memory_space=pltpu.VMEM), pl.BlockSpec(memory_space=pl.ANY)
    shape = jax.ShapeDtypeStruct
    low = pltpu.VMEM(tokens.shape, BF16)
    return pl.pallas_call(
        partial(behind_kernel, sizes, length),
        out_shape=(
            shape((4, width, width), BF16), shape((width, 128), BF16), shape(tokens.shape, BF16)
        ),
        in_specs=[vmem, vmem] + [hbm] * 7 + [vmem] * 5,
        out_specs=(hbm, vmem, vmem),
        scratch_shapes=[
            pltpu.VMEM(weights.shape, BF16),
            pltpu.VMEM((2, 128, 256), F32),
            pltpu.VMEM(tokens.shape, F32),
            low, low, low, low, low,
            pltpu.VMEM((4, width, width), BF16),
            *[pltpu.VMEM(value.shape, BF16) for value in later],
            pltpu.SemaphoreType.DMA((4,)), pltpu.SemaphoreType.DMA((6,)),
            pltpu.SemaphoreType.DMA((4,)),
        ],
        compiler_params=pltpu.CompilerParams(vmem_limit_bytes=VMEM_BYTES),
        name="tokens_behind",
    )(back, small, weights, *later, *kept, grad_logits, cotangent)


def unpack_kernel(summed, in_bias_sum, out_sum, attn, phi_t, scales, biases, in_bias, out_bias):
    attn[...] = summed[:, :, : attn.shape[2]]
    turned = jnp.swapaxes(summed[0][:, 128:], 0, 1)
    phi_t[...] = turned[64:80]
    scales[...] = turned[80:82]
    biases[...] = turned[82:84]
    in_bias[...] = in_bias_sum[...]
    width = out_bias.shape[1]
    value = out_sum[...]
    later = pltpu.roll(value, value.shape[1] - width, 1)
    out_bias[...] = jnp.where(lax.axis_index("tensor") == 0, value[:, :width], later[:, :width])


def unpack_grads(summed, in_bias_sum, out_sum, block, slot):
    n_k, rows, _ = summed.shape
    vmem = pl.BlockSpec(memory_space=pltpu.VMEM)
    shape = jax.ShapeDtypeStruct
    return pl.pallas_call(
        unpack_kernel,
        out_shape=(
            shape((n_k, rows, block), F32), shape((slot, rows), F32),
            shape((2, rows), F32), shape((2, rows), F32),
            shape(in_bias_sum.shape, F32), shape((out_sum.shape[0], rows), F32),
        ),
        in_specs=[vmem] * 3,
        out_specs=(vmem,) * 6,
        name="unpack_grads",
    )(summed, in_bias_sum, out_sum)


def order_kernel(*refs):
    *parts, out = refs
    h, n_h = lax.axis_index("heads"), len(parts)
    own = parts[0].shape[0]
    group = own * n_h
    step = 256 // group
    length = out.shape[0]
    for first in range(0, length, step):
        count = min(step, length - first)
        taken = min(step, parts[0].shape[1] - first)
        shape = (count * group, group * taken)
        row = lax.broadcasted_iota(jnp.int32, shape, 0)
        column = lax.broadcasted_iota(jnp.int32, shape, 1)
        block = column // taken
        image = lax.rem(h + n_h - block // own, n_h) * own + block % own
        chosen = ((row // group == column % taken) & (row % group == image)).astype(F32)
        lines = jnp.concatenate(
            [part[i, first : first + taken] for part in parts for i in range(own)], axis=0
        )
        value = dot(chosen.astype(BF16), lines).astype(BF16)
        out[first : first + count] = value.reshape(count, group, value.shape[1])


def order_images(parts, length):
    own, _, width = parts[0].shape
    vmem = pl.BlockSpec(memory_space=pltpu.VMEM)
    return pl.pallas_call(
        order_kernel,
        out_shape=jax.ShapeDtypeStruct((length, own * len(parts), width), BF16),
        in_specs=[vmem] * len(parts),
        out_specs=vmem,
        compiler_params=pltpu.CompilerParams(vmem_limit_bytes=24 * 1024 * 1024),
        name="order_images",
    )(*parts)


def normalize(values, scale, shift):
    centered = values - jnp.mean(values, axis=-1, keepdims=True)
    variance = jnp.mean(centered * centered, axis=-1, keepdims=True)
    inverse = lax.rsqrt(variance + epsilon)
    unit_part = centered * inverse
    return (unit_part * scale + shift, unit_part, inverse)


def normalize_back(grad_output, unit_part, inverse, scale):
    scaled = grad_output * scale
    average = jnp.mean(scaled, axis=-1, keepdims=True)
    projection = jnp.mean(scaled * unit_part, axis=-1, keepdims=True)
    grad_input = inverse * (scaled - average - unit_part * projection)
    return (
        grad_input,
        jnp.sum(grad_output * unit_part, axis=(0, 1)),
        jnp.sum(grad_output, axis=(0, 1)),
    )


def to_experts(slots):
    slots = lax.all_to_all(slots, "heads", split_axis=1, concat_axis=0, tiled=True)
    slots = lax.all_to_all(slots, "shard", split_axis=2, concat_axis=0, tiled=True)
    return lax.all_gather(slots, "tensor", axis=0, tiled=True)


def to_images(slots):
    slots = lax.psum_scatter(slots, "tensor", scatter_dimension=0, tiled=True)
    slots = lax.all_to_all(slots, "shard", split_axis=0, concat_axis=2, tiled=True)
    return lax.all_to_all(slots, "heads", split_axis=0, concat_axis=1, tiled=True)


def general_shards(tokens, norm_scales, norm_biases, w_attn, phi, experts, in_bias, out_bias, cotangent):
    heads_n = lax.axis_size("heads")
    group, seq_len, width = tokens.shape
    own = group // heads_n
    heads_index = lax.axis_index("heads")
    tensor_index = lax.axis_index("tensor")
    shard_index = lax.axis_index("shard")
    hidden = experts.shape[3]
    rows = experts.shape[0]
    scales, biases, in_full = (
        lax.all_gather(norm_scales, ROWS, axis=1, tiled=True).astype(F32),
        lax.all_gather(norm_biases, ROWS, axis=1, tiled=True).astype(F32),
        lax.all_gather(in_bias, ROWS, axis=1, tiled=True).astype(F32),
    )
    attn = lax.all_gather(
        lax.all_gather(w_attn, "heads", axis=2, tiled=True), ROWS, axis=1, tiled=True
    )
    phi_full = lax.all_gather(
        lax.all_gather(phi, "heads", axis=1, tiled=True), ROWS, axis=0, tiled=True
    )
    out_rows = lax.all_gather(out_bias, "tensor", axis=1, tiled=True).astype(F32)
    e_own = experts.shape[2] // lax.axis_size("shard")
    in_local = lax.dynamic_slice_in_dim(in_full, tensor_index * hidden, hidden, 1)
    factor = HEAD_DIM ** (-0.5)
    tokens = lax.dynamic_slice_in_dim(tokens, heads_index * own, own, 0)
    cotangent = lax.dynamic_slice_in_dim(cotangent, heads_index * own, own, 0)
    n_heads = width // HEAD_DIM
    inputs = tokens.astype(F32)
    normed_one, unit_one, inverse_one = normalize(inputs, scales[0], biases[0])
    normed_one_b = normed_one.astype(BF16)
    projected = einsum("nsd,kdc->knsc", normed_one_b, attn[:3]).astype(BF16)
    query, keyed, valued = projected.reshape(3, own, seq_len, n_heads, HEAD_DIM)
    scores = einsum("nqhe,nkhe->nhqk", query, keyed) * factor
    score_peak = jnp.max(scores, axis=-1, keepdims=True)
    exponent = jnp.exp(scores - score_peak)
    probs = exponent / jnp.sum(exponent, axis=-1, keepdims=True)
    probs_b = probs.astype(BF16)
    context_b = (
        einsum("nhqk,nkhe->nqhe", probs_b, valued).astype(BF16).reshape(own, seq_len, width)
    )
    hidden_one = inputs + einsum("nsc,dc->nsd", context_b, attn[3])
    normed_two, unit_two, inverse_two = normalize(hidden_one, scales[1], biases[1])
    normed_two_b = normed_two.astype(BF16)
    logits = einsum("nsd,de->nse", normed_two_b, phi_full)
    dispatch = jax.nn.softmax(logits, axis=1)
    dispatch_b = dispatch.astype(BF16)
    combine = jax.nn.softmax(logits, axis=2)
    combine_b = combine.astype(BF16)
    slot_in = to_experts(einsum("nse,nsd->ned", dispatch_b, normed_two_b).astype(BF16))
    share = 1 if e_own else 0

    def meet(partial_sum):
        return lax.psum_scatter(partial_sum, "shard", scatter_dimension=share, tiled=True)

    def spread(values):
        return lax.all_gather(values, "shard", axis=share, tiled=True)

    pre = meet(einsum("ned,def->nef", slot_in, experts[:, 0]))
    if e_own:
        pre = pre + lax.dynamic_slice_in_dim(in_local, shard_index * e_own, e_own, 0)
    else:
        pre = pre + in_local
    gelu_value, gelu_back = jax.vjp(partial(jax.nn.gelu, approximate=False), pre)
    activated = spread(gelu_value.astype(BF16))
    slot_out_part = einsum("nef,def->ned", activated, experts[:, 1])
    slot_out_part = slot_out_part + jnp.where(tensor_index == 0, out_rows, 0.0)
    slot_out = to_images(slot_out_part).astype(BF16)
    output = (hidden_one + einsum("nse,ned->nsd", combine_b, slot_out)).astype(BF16)
    output = lax.all_gather(output, "heads", axis=0, tiled=True)
    grad_combine = einsum("nsd,ned->nse", cotangent, slot_out)
    grad_slot = to_experts(einsum("nse,nsd->ned", combine_b, cotangent).astype(BF16))
    grad_act = meet(einsum("ned,def->nef", grad_slot, experts[:, 1]))
    grad_pre = spread(gelu_back(grad_act)[0].astype(BF16))
    grad_slot_in = einsum("nef,def->ned", grad_pre, experts[:, 0]).astype(BF16)
    input_term = einsum("ned,nef->def", slot_in, grad_pre)
    output_term = einsum("ned,nef->def", grad_slot, activated)
    experts_grad = jnp.stack((input_term, output_term), axis=1)
    grad_slot_in = to_images(grad_slot_in.astype(F32)).astype(BF16)
    in_bias_grad = lax.dynamic_slice_in_dim(
        lax.all_gather(jnp.sum(grad_pre.astype(F32), axis=0), "tensor", axis=1, tiled=True),
        (shard_index * lax.axis_size("tensor") + tensor_index) * in_bias.shape[1],
        in_bias.shape[1],
        1,
    )
    out_bias_grad = lax.dynamic_slice_in_dim(
        jnp.sum(grad_slot.astype(F32), axis=0),
        tensor_index * out_bias.shape[1],
        out_bias.shape[1],
        1,
    )
    grad_dispatch = einsum("nsd,ned->nse", normed_two_b, grad_slot_in)
    grad_logits = (
        dispatch * (grad_dispatch - jnp.sum(dispatch * grad_dispatch, axis=1, keepdims=True))
        + combine * (grad_combine - jnp.sum(combine * grad_combine, axis=2, keepdims=True))
    ).astype(BF16)
    phi_grad = einsum("nsd,nse->de", normed_two_b, grad_logits)
    grad_normed_two = einsum("nse,ned->nsd", dispatch_b, grad_slot_in) + einsum(
        "nse,de->nsd", grad_logits, phi_full
    )
    grad_hidden_norm, scale_two_grad, bias_two_grad = normalize_back(
        grad_normed_two, unit_two, inverse_two, scales[1]
    )
    grad_hidden = cotangent.astype(F32) + grad_hidden_norm
    grad_hidden_b = grad_hidden.astype(BF16)
    out_weight_grad = einsum("nsd,nsc->dc", grad_hidden_b, context_b)
    grad_context = einsum("nsd,dc->nsc", grad_hidden_b, attn[3]).astype(BF16)
    grad_context = grad_context.reshape(own, seq_len, n_heads, HEAD_DIM)
    grad_value = einsum("nhqk,nqhe->nkhe", probs_b, grad_context).astype(BF16)
    grad_probs = einsum("nqhe,nkhe->nhqk", grad_context, valued)
    grad_scores = (
        probs * (grad_probs - jnp.sum(probs * grad_probs, axis=-1, keepdims=True))
    ).astype(BF16)
    grad_query = (einsum("nhqk,nkhe->nqhe", grad_scores, keyed) * factor).astype(BF16)
    grad_key = (einsum("nhqk,nqhe->nkhe", grad_scores, query) * factor).astype(BF16)
    grad_proj = jnp.stack((grad_query, grad_key, grad_value)).reshape(3, own, seq_len, width)
    proj_grad = einsum("nsd,knsc->kdc", normed_one_b, grad_proj)
    grad_normed_one = einsum("knsc,kdc->nsd", grad_proj, attn[:3])
    grad_input_norm, scale_one_grad, bias_one_grad = normalize_back(
        grad_normed_one, unit_one, inverse_one, scales[0]
    )
    input_grad = (grad_hidden + grad_input_norm).astype(BF16)
    input_grad = lax.all_gather(input_grad, "heads", axis=0, tiled=True)
    attn_grad = jnp.concatenate((proj_grad, out_weight_grad[None]), axis=0)
    attn_grad = lax.psum_scatter(attn_grad, ROWS, scatter_dimension=1, tiled=True)
    attn_grad = lax.psum_scatter(attn_grad, "heads", scatter_dimension=2, tiled=True)
    phi_grad = lax.psum_scatter(phi_grad, ROWS, scatter_dimension=0, tiled=True)
    phi_grad = lax.psum_scatter(phi_grad, "heads", scatter_dimension=1, tiled=True)
    norms = jnp.stack((scale_one_grad, scale_two_grad, bias_one_grad, bias_two_grad))
    norms = lax.psum(lax.psum_scatter(norms, ROWS, scatter_dimension=1, tiled=True), "heads")
    return (
        output,
        input_grad,
        norms[:2],
        norms[2:],
        attn_grad,
        phi_grad,
        experts_grad,
        in_bias_grad,
        out_bias_grad,
    )


def shards(tokens, norm_scales, norm_biases, w_attn, phi, experts, in_bias, out_bias, cotangent):
    arrays = (tokens, norm_scales, norm_biases, w_attn, phi, experts, in_bias, out_bias, cotangent)
    sizes = tuple(lax.axis_size(name) for name in ("shard", "heads", "tensor"))
    group, length, width = tokens.shape
    fits = (sizes, group, width, *experts.shape[:3]) == ((4, 4, 2), 8, 768, 192, 2, 16)
    if not fits or not 192 < length <= 208 or in_bias.shape[1] != 384:
        return general_shards(*arrays)
    n_s, n_h, n_t = sizes
    block, slot = w_attn.shape[2], phi.shape[1]
    tokens, cotangent = (
        values.transpose(1, 0, 2).reshape(group * length, width) for values in (tokens, cotangent)
    )
    attn, small, turned, tokens, cotangent, blocks, dispatch, combine, *held = gather_weights(
        sizes, length, w_attn, phi.T, out_bias, norm_scales, norm_biases, in_bias, experts, tokens,
        cotangent,
    )
    normed_1, query, keyed, valued, context, hidden, normed_2 = held
    slot_in, activated, grad_slot, grad_pre, back, in_bias_grad, out_sum, grad_logits, output = (
        experts_pass(
            sizes, blocks, turned, small, combine, hidden, cotangent, in_bias.shape[1]
        )
    )
    attn_grad, small_grad, input_grad = tokens_behind(
        sizes, length, back, small, attn, (context, query, keyed, valued, normed_1, tokens),
        (hidden, normed_2, dispatch), grad_logits, cotangent,
    )
    parts = [input_grad] + [
        lax.ppermute(input_grad, "heads", [(i, (i + d) % n_h) for i in range(n_h)])
        for d in range(1, n_h)
    ]
    attn_grad, grad_pre = lax.optimization_barrier((attn_grad, grad_pre))
    experts_grad = weight_grads(slot_in, grad_pre, grad_slot, activated)
    output = output[:, :length].transpose(1, 0, 2)
    attn_grad, experts_grad, output = lax.optimization_barrier((attn_grad, experts_grad, output))
    summed = reduce_grads(sizes, attn_grad, small_grad)
    attn_grad, phi_grad, scales_grad, biases_grad, in_bias_grad, out_bias_grad = unpack_grads(
        summed, in_bias_grad, out_sum, block, slot
    )
    input_grad = order_images(parts, length)
    return (
        output.transpose(1, 0, 2),
        input_grad.transpose(1, 0, 2),
        scales_grad,
        biases_grad,
        attn_grad,
        phi_grad.T,
        experts_grad,
        in_bias_grad,
        out_bias_grad,
    )


def solution(mesh):
    images = P(ROWS, None, None)
    return jax.shard_map(
        shards,
        mesh=mesh,
        in_specs=(
            images,
            P(None, ROWS),
            P(None, ROWS),
            P(None, ROWS, "heads"),
            P(ROWS, "heads"),
            P("shard", None, "heads", "tensor"),
            P("heads", ROWS),
            P("heads", ROWS),
            images,
        ),
        out_specs=(
            images,
            images,
            P(None, ROWS),
            P(None, ROWS),
            P(None, ROWS, "heads"),
            P(ROWS, "heads"),
            P("shard", None, "heads", "tensor"),
            P("heads", ROWS),
            P("heads", ROWS),
        ),
        check_vma=False,
    )
```

```python
from functools import partial

import jax
import jax.numpy as jnp
from jax import lax
from jax.experimental import pallas as pl
from jax.experimental.pallas import tpu as pltpu
from jax.sharding import PartitionSpec as P

HEAD_DIM = 64
F32 = jnp.float32
BF16 = jnp.bfloat16
ROWS = ("shard", "tensor")
MESH = pl.DeviceIdType.MESH
VMEM_BYTES = 58 * 1024 * 1024
epsilon = 1e-06
einsum = partial(jnp.einsum, preferred_element_type=F32)


def dot(a, b):
    return lax.dot_general(a, b, (((1,), (0,)), ((), ())), preferred_element_type=F32)


def dot_t(a, b):
    return lax.dot_general(a, b, (((1,), (1,)), ((), ())), preferred_element_type=F32)


def swap_matrix(n):
    out = lax.broadcasted_iota(jnp.int32, (n * n, n * n), 0)
    row = lax.broadcasted_iota(jnp.int32, (n * n, n * n), 1)
    return ((out // n == row % n) & (out % n == row // n)).astype(F32).astype(BF16)


class Peers:
    def __init__(self, sizes):
        self.sizes = sizes
        self.at = tuple(lax.axis_index(name) for name in ("shard", "heads", "tensor"))
        self.count = sizes[0] * sizes[1] * sizes[2]

    def flat(self, place):
        return (place[0] * self.sizes[1] + place[1]) * self.sizes[2] + place[2]

    def step(self, k, sign):
        _, n_h, n_t = self.sizes
        steps = (k // (n_h * n_t), (k // n_t) % n_h, k % n_t)
        return tuple(
            lax.rem(at + n + sign * d, n) for at, n, d in zip(self.at, self.sizes, steps)
        )

    def greet_all(self):
        barrier = pltpu.get_barrier_semaphore()

        def signal(k, carry):
            pl.semaphore_signal(barrier, inc=1, device_id=self.step(k, 1), device_id_type=MESH)
            return carry

        lax.fori_loop(1, self.count, signal, 0)
        pl.semaphore_wait(barrier, self.count - 1)


def remote(src, dst, send, recv, place):
    return pltpu.make_async_remote_copy(
        src_ref=src, dst_ref=dst, send_sem=send, recv_sem=recv, device_id=place, device_id_type=MESH
    )


def plane(sizes):
    n_s, n_h, n_t = sizes
    s, h, t = (lax.axis_index(name) for name in ("shard", "heads", "tensor"))
    core, chip = lax.rem(s, 2), s // 2
    sibling = (s + 1 - 2 * core, h, t)
    across_x = (lax.rem(s + 2, n_s), h, t)
    across_y = (s, h, 1 - t)
    line = [(s, lax.rem(h + d, n_h), t) for d in range(n_h)]
    barrier = pltpu.get_barrier_semaphore()
    others = [sibling, across_x, across_y] + line[1:]
    for place in others:
        pl.semaphore_signal(barrier, inc=1, device_id=place, device_id_type=MESH)
    pl.semaphore_wait(barrier, len(others))
    return (s, h, t), core, chip, sibling, across_x, across_y, line


def pair_matrix(block, wide, transposed):
    shape = (2 * block, 2 * wide) if transposed else (2 * wide, 2 * block)
    tight = lax.broadcasted_iota(jnp.int32, shape, 0 if transposed else 1)
    padded = lax.broadcasted_iota(jnp.int32, shape, 1 if transposed else 0)
    second = padded >= wide
    lane = jnp.where(second, padded - wide, padded)
    same = (lane < block) & (tight == jnp.where(second, lane + block, lane))
    return same.astype(F32).astype(BF16)


def gather_kernel(
    sizes, length, w_attn, phi_t, out_bias, scales, biases, in_bias, experts, tokens, cotangent,
    w_out, small_out, turned, own_tokens, own_cot, blocks, dispatch, combine, *refs,
):
    held_out, refs = refs[:7], refs[7:]
    held, refs = refs[:7], refs[7:]
    (joined, order, w, small, lined, extra, stage, tile_in, tile_out, images, picked,
     z_send, z_recv, x_sems, y_sems, d_sems, c_sems, t_sems, o_sems, i_sems, h_sems) = refs
    n_k, rows, block = w_attn.shape
    wide = lined.shape[3]
    slot = phi_t.shape[0]
    own_h = lax.axis_index("heads")
    stage[...] = jnp.zeros_like(stage)
    stage[64 : 64 + slot] = phi_t[...].astype(F32)
    stage[64 + slot : 64 + 2 * slot] = out_bias[...].astype(F32)
    lined[own_h, :, :, 128:] = jnp.zeros((n_k, rows, wide - 128), BF16)
    lined[own_h, :, :, :block] = w_attn[...]
    first = lined[own_h, 0, :, 128:].astype(F32) + jnp.swapaxes(stage[...], 0, 1)
    lined[own_h, 0, :, 128:] = first.astype(BF16)
    (s, h, t), core, chip, sibling, across_x, across_y, line = plane(sizes)
    n_h, n_t = sizes[1], sizes[2]
    width = w.shape[2]
    side = 16
    n_tiles = experts.shape[0] // side
    depth = tile_in.shape[0]
    halves = ((0, rows // 2), (rows // 2, rows // 2))

    def z_hop(k, origin, up):
        place = line[1] if up else line[n_h - 1]
        return remote(
            lined.at[origin, k], lined.at[origin, k],
            z_send.at[k, origin, up], z_recv.at[k, origin], place,
        )

    def relay(k, d):
        @pl.when(h >= d)
        def _():
            z_hop(k, h - d, 1).wait_recv()

            @pl.when(h < n_h - 1)
            def _():
                z_hop(k, h - d, 1).start()

        @pl.when(h + d < n_h)
        def _():
            z_hop(k, h + d, 0).wait_recv()

            @pl.when(h > 0)
            def _():
                z_hop(k, h + d, 0).start()

    chunks = (0, 2, 1, 3)
    for k in chunks:
        @pl.when(h < n_h - 1)
        def _():
            z_hop(k, h, 1).start()

        @pl.when(h > 0)
        def _():
            z_hop(k, h, 0).start()

    def load(i):
        return pltpu.make_async_copy(
            experts.at[pl.ds((i % n_tiles) * side, side), i // n_tiles],
            tile_in.at[i % depth],
            t_sems.at[0, i % depth],
        )

    def store(i):
        return pltpu.make_async_copy(
            tile_out.at[i % depth],
            turned.at[i // n_tiles, :, pl.ds((i % n_tiles) * side, side)],
            t_sems.at[1, i % depth],
        )

    image_loads = [
        pltpu.make_async_copy(source, images.at[j], i_sems.at[0, j])
        for j, source in enumerate((tokens, cotangent))
    ]
    for i in range(depth - 1):
        load(i).start()
    for copy in image_loads:
        copy.start()
    swap = swap_matrix(side)
    done = [0]

    def turn(count):
        def step(i, carry):
            load(i).wait()

            @pl.when(i + depth - 1 < 2 * n_tiles)
            def _():
                load(i + depth - 1).start()

            @pl.when(i >= depth)
            def _():
                store(i - depth).wait()

            rows_in = tile_in[i % depth].reshape(side * side, tile_in.shape[3])
            tile_out[i % depth] = dot(swap, rows_in).astype(BF16).reshape(tile_out.shape[1:])
            store(i).start()
            return carry

        last = min(done[0] + count, 2 * n_tiles)
        lax.fori_loop(done[0], last, step, 0)
        done[0] = last

    pair = pair_matrix(block, wide, False)
    shape = (n_h * wide, small.shape[1])
    row = lax.broadcasted_iota(jnp.int32, shape, 0)
    column = lax.broadcasted_iota(jnp.int32, shape, 1)
    lane, of = row % wide - block, row // wide
    beside = (lane >= 0) & (lane < 16) & (column == of * 16 + lane)
    beside |= (lane >= 16) & (lane < 32) & (column == n_h * 16 + of * 16 + lane - 16)
    beside = beside.astype(F32).astype(BF16)

    stage[...] = jnp.zeros_like(stage)
    stage[64:66] = scales[...].astype(F32)
    stage[66:68] = biases[...].astype(F32)
    norms = jnp.swapaxes(stage[...], 0, 1)
    pieces = []
    for j in range(in_bias.shape[1] // 64):
        shape = (in_bias.shape[1], 128)
        row = lax.broadcasted_iota(jnp.int32, shape, 0)
        column = lax.broadcasted_iota(jnp.int32, shape, 1)
        chosen = ((row == 64 * j + column) & (column < 64)).astype(F32).astype(BF16)
        pieces.append(dot(in_bias[...], chosen))
    extra[:, :128] = jnp.zeros((rows, 128), F32)
    extra[:, 128:] = jnp.concatenate(pieces, axis=0) + norms

    image_stores = [
        pltpu.make_async_copy(picked.at[j], target, i_sems.at[1, j])
        for j, target in enumerate((own_tokens, own_cot))
    ]

    def pick_images(j):
        own, padded = picked.shape[1:3]
        group = own * n_h
        lines = images.shape[1]
        image_loads[j].wait()
        step = 256 // group
        for first in range(0, padded, step):
            count = min(step, padded - first)
            taken = min(step * group, lines - first * group)
            shape = (own * count, taken)
            row = lax.broadcasted_iota(jnp.int32, shape, 0)
            column = lax.broadcasted_iota(jnp.int32, shape, 1)
            wanted = (row % count) * group + own * h + row // count
            chosen = (column == wanted).astype(F32).astype(BF16)
            source = images[j, first * group : first * group + taken]
            picked[j, :, first : first + count] = (
                dot(chosen, source).astype(BF16).reshape(own, count, images.shape[2])
            )
        image_stores[j].start()

    def at(k, place):
        first = pl.multiple_of((place[0] * n_t + place[2]) * rows, 16)
        lines = pl.ds(first, rows)
        return small.at[lines] if k == n_k else w.at[k, lines]

    def hop(q, origin, place, sems, j):
        return remote(at(q, origin), at(q, origin), sems.at[0, j], sems.at[1, j], place)

    def half_hop(q, origin, place, half):
        part = at(q, origin).at[pl.ds(*halves[half])]
        j = 2 * q + half
        return remote(part, part, d_sems.at[0, j], d_sems.at[1, j], place)

    me = (s, h, t)
    from_d = (across_x[0], h, across_y[2])
    sent = []

    def send(copy):
        copy.start()
        sent.append(copy)

    def assemble(k):
        for i in range(0, n_h, 2):
            lines = jnp.concatenate([lined[i, k], lined[i + 1, k]], axis=1)
            at(k, me)[:, i * block : (i + 2) * block] = dot(lines, pair).astype(BF16)
        if k == 0:
            lines = jnp.concatenate([lined[i, k] for i in range(n_h)], axis=1)
            at(n_k, me)[...] = (dot(lines, beside) + extra[...]).astype(BF16)
        for q in members(k):
            send(hop(q, me, across_x, x_sems, q))
            send(hop(q, me, across_y, y_sems, q))
            send(hop(q, me, sibling, c_sems, 4 * q))

    def members(k):
        return (0, n_k) if k == 0 else (k,)

    def relay_xy(k):
        for q in members(k):
            hop(q, across_x, across_x, x_sems, q).wait_recv()
            send(half_hop(q, across_x, across_y, 0))
            send(hop(q, across_x, sibling, c_sems, 4 * q + 1))
            hop(q, across_y, across_y, y_sems, q).wait_recv()
            send(half_hop(q, across_y, across_x, 1))
            send(hop(q, across_y, sibling, c_sems, 4 * q + 2))

    def relay_d(k):
        for q in members(k):
            half_hop(q, from_d, across_y, 0).wait_recv()
            half_hop(q, from_d, across_x, 1).wait_recv()
            send(hop(q, from_d, sibling, c_sems, 4 * q + 3))

    for wave in range(n_k + n_h - 2):
        for d in range(1, n_h):
            if 0 <= wave - d + 1 < n_k:
                relay(chunks[wave - d + 1], d)
        turn(2)
        i = wave - n_h + 2
        if i >= 0:
            assemble(chunks[i])
            if i in (1, 2):
                pick_images(i - 1)
            if i >= 1:
                relay_xy(chunks[i - 1])
            if i >= 2:
                relay_d(chunks[i - 2])
            turn(2)
    stores = []

    def arrive(q):
        for j in range(4):
            hop(q, me, sibling, c_sems, 4 * q + j).wait_recv()
        if q == n_k:
            stores.append(pltpu.make_async_copy(small, small_out, o_sems.at[q]))
        else:
            stores.append(pltpu.make_async_copy(w.at[q], w_out.at[q], o_sems.at[q]))
        stores[-1].start()

    def keep(first, last):
        for j in range(first, last):
            stores.append(pltpu.make_async_copy(held[j], held_out[j], h_sems.at[j]))
            stores[-1].start()

    ahead = Ahead(
        length, picked.at[0], small, w, blocks, dispatch, combine, held, joined, order
    )
    arrive(n_k)
    ahead.first_norm()
    relay_xy(chunks[-1])
    relay_d(chunks[-2])
    arrive(0)
    ahead.project(0)
    turn(2 * n_tiles)
    arrive(2)
    ahead.project(2)
    arrive(1)
    ahead.project(1)
    relay_d(chunks[-1])
    keep(0, 4)
    ahead.attend()
    arrive(3)
    ahead.finish()
    keep(4, 7)
    for copy in sent:
        copy.wait_send()
    for origin in range(n_h):
        @pl.when((origin <= h) & (h < n_h - 1))
        def _():
            for k in range(n_k):
                z_hop(k, origin, 1).wait_send()

        @pl.when((origin >= h) & (h > 0))
        def _():
            for k in range(n_k):
                z_hop(k, origin, 0).wait_send()

    for i in range(depth):
        store(2 * n_tiles - depth + i).wait()
    for copy in image_stores:
        copy.wait()
    for copy in stores:
        copy.wait()


def gather_weights(
    sizes, length, w_attn, phi_t, out_bias, scales, biases, in_bias, experts, tokens, cotangent
):
    n_k, rows, _ = w_attn.shape
    wide = 256
    n_s, n_h, n_t = sizes
    width = n_s * n_t * rows
    vmem = pl.BlockSpec(memory_space=pltpu.VMEM)
    hbm = pl.BlockSpec(memory_space=pl.ANY)
    dma = pltpu.SemaphoreType.DMA
    hidden = experts.shape[3]
    small = (width, wide)
    images = jax.ShapeDtypeStruct((2, 208, width), BF16)
    shape = jax.ShapeDtypeStruct
    keys = shape((2, 256, width), BF16)
    thin = shape((2, 208, 128), F32)
    held = (images, images, keys, keys, images, shape(images.shape, F32), images)
    return pl.pallas_call(
        partial(gather_kernel, sizes, length),
        out_shape=(
            jax.ShapeDtypeStruct((n_k, width, width), BF16),
            jax.ShapeDtypeStruct(small, BF16),
            jax.ShapeDtypeStruct((2, experts.shape[2], experts.shape[0], hidden), BF16),
            images, images, shape((n_h, n_s, 2, 16, width // n_s), BF16), thin, thin, *held,
        ),
        in_specs=[vmem] * 6 + [hbm] * 3,
        out_specs=(hbm,) * 5 + (vmem,) * 3 + (hbm,) * 7,
        scratch_shapes=[
            *[pltpu.VMEM(value.shape, value.dtype) for value in held],
            pltpu.VMEM((2 * width // n_s, 512), BF16),
            pltpu.VMEM((128, 128), BF16),
            pltpu.VMEM((n_k, width, width), BF16),
            pltpu.VMEM(small, BF16),
            pltpu.VMEM((n_h, n_k, rows, wide), BF16),
            pltpu.VMEM((rows, wide), F32),
            pltpu.VMEM((128, rows), F32),
            pltpu.VMEM((4, 16, 16, hidden), BF16),
            pltpu.VMEM((4, 16, 16, hidden), BF16),
            pltpu.VMEM((2, *tokens.shape), BF16),
            pltpu.VMEM((2, *images.shape), BF16),
            dma((n_k, n_h, 2)), dma((n_k, n_h)), dma((2, n_k + 1)), dma((2, n_k + 1)),
            dma((2, 2 * (n_k + 1))), dma((2, 4 * (n_k + 1))), dma((2, 4)), dma((n_k + 1,)),
            dma((2, 2)), dma((7,)),
        ],
        compiler_params=pltpu.CompilerParams(
            collective_id=3, has_side_effects=True, vmem_limit_bytes=VMEM_BYTES
        ),
        name="gather_weights",
    )(w_attn, phi_t, out_bias, scales, biases, in_bias, experts, tokens, cotangent)


def reduce_kernel(
    sizes, grads, small, out, core_in, core_small, met, met_small,
    d_in, d_small, x_in, x_small, y_in, y_small, pieces, z_in,
    c_sems, d_sems, x_sems, y_sems, z_send, z_recv,
):
    (s, h, t), core, chip, sibling, across_x, across_y, line = plane(sizes)
    n_k, width, _ = grads.shape
    n_s, n_h, n_t = sizes
    rows = width // (n_s * n_t)
    wide = pieces.shape[3]
    pair = n_t * rows
    half = rows // 2
    halves = (pl.ds(0, half), pl.ds(half, half))
    chunks = (0, 2, 1, 3)

    def members(k):
        return (0, n_k) if k == 0 else (k,)

    def pick(q, large, little):
        return little if q == n_k else large.at[q]

    def core_copy(q, x):
        first = pl.multiple_of((2 * x + 1 - core) * pair, 16)
        return remote(
            pick(q, grads, small).at[pl.ds(first, pair)],
            pick(q, core_in, core_small).at[x],
            c_sems.at[0, 2 * q + x], c_sems.at[1, 2 * q + x], sibling,
        )

    for k in chunks:
        for q in members(k):
            for x in range(2):
                core_copy(q, x).start()
    joined = pair_matrix(width // n_h, wide, True)
    shape = (small.shape[1], n_h * wide)
    row = lax.broadcasted_iota(jnp.int32, shape, 0)
    column = lax.broadcasted_iota(jnp.int32, shape, 1)
    lane, of = column % wide - width // n_h, column // wide
    beside = (lane >= 0) & (lane < 16) & (row == of * 16 + lane)
    beside |= (lane >= 16) & (lane < 20) & (row == n_h * 16 + lane - 16)
    beside = beside.astype(F32).astype(BF16)
    to_d, to_x, to_y = (d_in, d_small), (x_in, x_small), (y_in, y_small)
    sent = []

    def hop(q, kind, part, source, place):
        sems = {id(to_d): d_sems, id(to_x): x_sems, id(to_y): y_sems}[id(kind)]
        target = pick(q, *kind)
        target = target.at[part] if kind is to_d else target.at[halves[part]]
        j = 2 * q + part
        return remote(source, target, sems.at[0, j], sems.at[1, j], place)

    def send(copy):
        copy.start()
        sent.append(copy)

    def part_of(q, x, y, part):
        return pick(q, met, met_small).at[x, y].at[halves[part]]

    def arrived(q, kind, part):
        hop(q, kind, part, part_of(q, 0, 0, part), sibling).wait_recv()

    def open_up(q):
        part = pick(q, met, met_small)
        for x in range(2):
            core_copy(q, x).wait_recv()
            first = pl.multiple_of((2 * x + core) * pair, 16)
            own = pick(q, grads, small)[pl.ds(first, pair)].astype(F32)
            total = own + pick(q, core_in, core_small)[x].astype(F32)
            part[x] = total.astype(BF16).reshape(n_t, rows, total.shape[1])
        send(hop(q, to_d, 0, part_of(q, 1 - chip, 1 - t, 0), across_x))
        send(hop(q, to_d, 1, part_of(q, 1 - chip, 1 - t, 1), across_y))
        send(hop(q, to_x, 0, part_of(q, 1 - chip, t, 0), across_x))
        send(hop(q, to_y, 1, part_of(q, chip, 1 - t, 1), across_y))

    def pass_on(q):
        for part, kind, x, y, place in (
            (0, to_y, chip, 1 - t, across_y),
            (1, to_x, 1 - chip, t, across_x),
        ):
            arrived(q, to_d, part)
            block = part_of(q, x, y, part)
            total = block[...].astype(F32) + pick(q, *to_d)[part].astype(F32)
            block[...] = total.astype(BF16)
            send(hop(q, kind, part, block, place))

    def whole(q):
        for kind in (to_x, to_y):
            for part in range(2):
                arrived(q, kind, part)
        total = pick(q, met, met_small)[chip, t].astype(F32) + pick(q, *to_x)[...].astype(F32)
        return (total + pick(q, *to_y)[...].astype(F32)).astype(BF16)

    def z_copy(k, target, up):
        place = line[1] if up else line[n_h - 1]
        return remote(
            pieces.at[target, k], z_in.at[up, target, k],
            z_send.at[up, target, k], z_recv.at[up, target, k], place,
        )

    def pass_along(k, hops):
        for up in range(2):
            for target in range(n_h - 1, -1, -1) if up else range(n_h):
                further = target > h if up else target < h

                @pl.when(further & (h == (hops if up else n_h - 1 - hops)))
                def _():
                    if hops > 0:
                        z_copy(k, target, up).wait_recv()
                        total = pieces[target, k].astype(F32) + z_in[up, target, k].astype(F32)
                        pieces[target, k] = total.astype(BF16)
                    z_copy(k, target, up).start()

    def share_out(k):
        value = whole(k)
        columns = width // n_h
        if k == 0:
            little = dot(whole(n_k), beside)
        for i in range(0, n_h, 2):
            lanes = dot(value[:, i * columns : (i + 2) * columns], joined)
            if k == 0:
                lanes = lanes + little[:, i * wide : (i + 2) * wide]
            pieces[i, k] = lanes[:, :wide].astype(BF16)
            pieces[i + 1, k] = lanes[:, wide:].astype(BF16)
        pass_along(k, 0)

    for i in range(n_k + 2 + n_h - 2):
        if i < n_k:
            for q in members(chunks[i]):
                open_up(q)
        if 0 <= i - 1 < n_k:
            for q in members(chunks[i - 1]):
                pass_on(q)
        if 0 <= i - 2 < n_k:
            share_out(chunks[i - 2])
        for hops in range(1, n_h - 1):
            if 0 <= i - 2 - hops < n_k:
                pass_along(chunks[i - 2 - hops], hops)
    for k in chunks:
        out[k] = pieces[h, k].astype(F32)
        for up, there in ((1, h > 0), (0, h < n_h - 1)):
            @pl.when(there)
            def _():
                z_copy(k, h, up).wait_recv()
                out[k] = out[k] + z_in[up, h, k].astype(F32)

    for k in chunks:
        for q in members(k):
            for x in range(2):
                core_copy(q, x).wait_send()
    for copy in sent:
        copy.wait_send()
    for target in range(n_h):
        for up in range(2):
            @pl.when(target > h if up else target < h)
            def _():
                for k in range(n_k):
                    z_copy(k, target, up).wait_send()


def reduce_grads(sizes, grads, small):
    n_k, width, _ = grads.shape
    n_s, n_h, n_t = sizes
    rows, wide, thin = width // (n_s * n_t), 256, small.shape[1]
    vmem = pl.BlockSpec(memory_space=pltpu.VMEM)
    dma = pltpu.SemaphoreType.DMA

    def buffers(*lead):
        return [
            pltpu.VMEM((n_k, *lead, width), BF16),
            pltpu.VMEM((*lead, thin), BF16),
        ]

    return pl.pallas_call(
        partial(reduce_kernel, sizes),
        out_shape=jax.ShapeDtypeStruct((n_k, rows, wide), F32),
        in_specs=[vmem, vmem],
        out_specs=vmem,
        scratch_shapes=[
            *buffers(2, n_t * rows), *buffers(2, n_t, rows),
            *buffers(2, rows // 2), *buffers(rows), *buffers(rows),
            pltpu.VMEM((n_h, n_k, rows, wide), BF16),
            pltpu.VMEM((2, n_h, n_k, rows, wide), BF16),
            dma((2, 2 * (n_k + 1))), dma((2, 2 * (n_k + 1))), dma((2, 2 * (n_k + 1))),
            dma((2, 2 * (n_k + 1))), dma((2, n_h, n_k)), dma((2, n_h, n_k)),
        ],
        compiler_params=pltpu.CompilerParams(
            collective_id=4, has_side_effects=True, vmem_limit_bytes=VMEM_BYTES
        ),
        name="reduce_grads",
    )(grads, small)


def experts_kernel(
    sizes, blocks_0, weights, small, combine, hidden, cotangent,
    slots_0_out, act_0_out, slots_1_out, act_1_out, back_out, bias_out, sum_out, grad_logits,
    gathered,
    w_0, w_1, gate, sums, slots_both, act_both, core_out, core_both, x_out, x_both, land_both, leave,
    back, back_both, blocks_1, output, combine_v, hidden_v, cotangent_v, padded, bias, bias_all,
    bias_send, bias_land,
    w_sem, o_sem, m_sem, in_both, return_both, core_sem, x_sem, act_sem, b_sems, g_send, g_recv, g_sem,
):
    peers = Peers(sizes)
    s, h, t = peers.at
    n_s, n_h, n_t = sizes
    me = peers.flat(peers.at)
    core, chip = lax.rem(s, 2), s // 2
    sibling = (s + 1 - 2 * core, h, t)
    across = (lax.rem(s + 2, n_s), h, t)
    half = act_both.shape[1] // 2
    own, other = core * half, (1 - core) * half
    n_blocks = peers.count
    loads = [
        pltpu.make_async_copy(weights.at[0], w_0, w_sem.at[0]),
        pltpu.make_async_copy(weights.at[1], w_1, w_sem.at[1]),
    ]
    kept = [
        pltpu.make_async_copy(source, target, m_sem.at[j])
        for j, (source, target) in enumerate(
            ((combine, combine_v), (hidden, hidden_v), (cotangent, cotangent_v))
        )
    ]
    for load in loads + kept:
        load.start()
    few = half // 2
    group = 16
    many = 2 * group
    peers.greet_all()

    def each(function, count=n_blocks, start=1):
        lax.fori_loop(start, count, lambda k, carry: (function(k), carry)[1], 0)

    out_row = lax.broadcasted_iota(jnp.int32, (16 * group, 16 * group), 0)
    in_row = lax.broadcasted_iota(jnp.int32, (16 * group, 16 * group), 1)
    there = (out_row // many == in_row % (2 * few)) & (out_row % many == in_row // (2 * few))
    there = there.astype(F32).astype(BF16)
    again = (in_row // many == out_row % (2 * few)) & (in_row % many == out_row // (2 * few))
    again = again.astype(F32).astype(BF16)
    stores = []

    def run(backward):
        n = 1 if backward else 0
        blocks = blocks_1 if backward else blocks_0
        w_a, w_b = (w_1, w_0) if backward else (w_0, w_1)
        slots, act, core_in, x_in, land, land_back = (
            both.at[n] for both in (slots_both, act_both, core_both, x_both, land_both, back_both)
        )
        in_sems, back_sems, core_sems, x_sems, act_sems = (
            both.at[n] for both in (in_both, return_both, core_sem, x_sem, act_sem)
        )
        def block_out(p, k):
            place = peers.step(k, 1)
            return remote(
                blocks.at[place[1], place[0], p], land.at[p, me],
                in_sems.at[0, p, k], in_sems.at[1, p, k], place,
            )

        def block_in(p, k):
            source = peers.flat(peers.step(k, -1))
            return remote(
                blocks.at[0, 0, p], land.at[p, source], in_sems.at[0, p, k], in_sems.at[1, p, k], sibling
            )

        for p in range(2):
            for k in range(1, n_blocks):
                block_out(p, k).start()
            land[p, me] = blocks[h, s, p]
        def receive(p):
            each(lambda k: block_in(p, k).wait_recv())
            for b in range(n_blocks // group):
                rows = land[p, b * group : (b + 1) * group].reshape(group * 16, land.shape[3])
                turned = dot(there, rows).astype(BF16).reshape(2 * few, many, land.shape[3])
                for c in range(2):
                    first = c * half + p * few
                    slots[first : first + few, b * many : (b + 1) * many, :] = turned[
                        c * few : (c + 1) * few
                    ]

        if backward:
            own_images = output.shape[0]
            line = [(s, lax.rem(h + d, n_h), t) for d in range(n_h)]
            g_own = pltpu.make_async_copy(output, gathered.at[pl.ds(h * own_images, own_images)], g_sem)
            g_own.start()

            def z_hop(i, origin, up, source=None):
                there = gathered.at[origin * own_images + i]
                return remote(
                    there if source is None else source, there,
                    g_send.at[i, origin, up], g_recv.at[i, origin], line[1] if up else line[n_h - 1],
                )

            def relay(i, d):
                @pl.when(h >= d)
                def _():
                    z_hop(i, h - d, 1).wait_recv()

                    @pl.when((h < n_h - 1) & (d < n_h - 1))
                    def _():
                        z_hop(i, h - d, 1).start()

                @pl.when(h + d < n_h)
                def _():
                    z_hop(i, h + d, 0).wait_recv()

                    @pl.when((h > 0) & (d < n_h - 1))
                    def _():
                        z_hop(i, h + d, 0).start()

            def gather_output():
                for i in range(own_images):
                    @pl.when(h < n_h - 1)
                    def _():
                        z_hop(i, h, 1, output.at[i]).start()

                    @pl.when(h > 0)
                    def _():
                        z_hop(i, h, 0, output.at[i]).start()
        else:
            piece, count = 6 * 64, act.shape[2] // (6 * 64)
            row = lax.broadcasted_iota(jnp.int32, (6 * 128, piece), 0)
            column = lax.broadcasted_iota(jnp.int32, (6 * 128, piece), 1)
            lane = row % 128
            place = (lane < 64) & (column == (row // 128) * 64 + lane)
            place = place.astype(F32).astype(BF16)
            for m in range(count):
                first = (t * count + m) * 96
                lines = [
                    small[pl.ds(pl.multiple_of(first + j * 16, 16), 16), 128:256] for j in range(6)
                ]
                bias[:, m * piece : (m + 1) * piece] = dot(jnp.concatenate(lines, axis=1), place)

        receive(0)
        if backward:
            gather_output()
        if not backward:
            loads[0].wait()

        def core_copy(j):
            return remote(
                core_out.at[j], core_in.at[j], core_sems.at[0, j], core_sems.at[1, j], sibling
            )

        def x_copy(j):
            return remote(x_out.at[j], x_in.at[j], x_sems.at[0, j], x_sems.at[1, j], across)

        def act_copy(j):
            return remote(
                act.at[own + j], act.at[own + j], act_sems.at[0, j], act_sems.at[1, j], sibling
            )

        def act_in(j):
            return remote(
                act.at[other + j], act.at[other + j], act_sems.at[0, j], act_sems.at[1, j], sibling
            )

        def meet(j):
            core_copy(j).wait_recv()
            sums[j] = sums[j] + core_in[j].astype(F32)
            x_out[j] = sums[j].astype(BF16)
            x_copy(j).start()

        def first_sums(j):
            core_out[j] = dot(slots[other + j], w_a[other + j]).astype(BF16)
            core_copy(j).start()

            @pl.when(j > 0)
            def _():
                meet(j - 1)

            sums[j] = dot(slots[own + j], w_a[own + j])

        each(first_sums, few, 0)
        receive(1)
        each(first_sums, half, few)
        meet(half - 1)
        if not backward:
            loads[1].wait()

        def second(e):
            leave[e] = dot_t(act[e], w_b[e]).astype(BF16)

        def finish(j):
            x_copy(j).wait_recv()
            value = sums[j] + x_in[j].astype(F32)
            if backward:
                act[own + j] = (value * gate[j]).astype(BF16)
            else:
                value = value + bias[pl.ds(own + j, 1), :]
                cumulative = 0.5 + 0.5 * lax.erf(value * 0.7071067811865476)
                act[own + j] = (value * cumulative).astype(BF16)
                gate[j] = cumulative + value * (
                    jnp.exp(value * value * -0.5) * 0.3989422804014327
                )
            act_copy(j).start()
            second(own + j)

            @pl.when(j > 0)
            def _():
                act_in(j - 1).wait_recv()
                second(other + j - 1)

            if backward:
                for when, i, d in ((2, 0, 1), (3, 1, 1), (5, 0, 2), (7, 1, 2)):
                    @pl.when(j == when)
                    def _():
                        relay(i, d)

        def back_copy(p, k):
            place = peers.step(k, 1)
            return remote(
                back.at[p, peers.flat(place)], land_back.at[p, me],
                back_sems.at[0, p, k], back_sems.at[1, p, k], place,
            )

        def back_in(p, k):
            source = peers.flat(peers.step(k, -1))
            return remote(
                back.at[p, 0], land_back.at[p, source],
                back_sems.at[0, p, k], back_sems.at[1, p, k], sibling,
            )

        def give_back(p):
            for b in range(n_blocks // group):
                rows = jnp.concatenate(
                    [
                        leave[c * half + p * few : c * half + (p + 1) * few, b * many : (b + 1) * many, :]
                        for c in range(2)
                    ],
                    axis=0,
                ).reshape(group * 16, leave.shape[2])
                turned = dot(again, rows).astype(BF16)
                back[p, b * group : (b + 1) * group] = turned.reshape(group, 16, leave.shape[2])
            for k in range(1, n_blocks):
                back_copy(p, k).start()
            land_back[p, me] = back[p, me]

        each(finish, few + 1, 0)
        give_back(0)
        each(finish, half, few + 1)
        act_in(half - 1).wait_recv()
        second(other + half - 1)
        give_back(1)
        outs = (slots_1_out, act_1_out) if backward else (slots_0_out, act_0_out)
        for j, (source, target) in enumerate(zip((slots, act), outs)):
            stores.append(pltpu.make_async_copy(source, target, o_sem.at[n, j]))
            stores[-1].start()
        if backward:
            across_t = (s, h, 1 - t)
            width = bias_out.shape[1]

            def bias_row(e):
                bias_all[pl.ds(e, 1), :] = jnp.sum(act[e].astype(F32), axis=0, keepdims=True)

            each(bias_row, 2 * half, 0)

            def slot_row(e):
                total = jnp.sum(slots[e].astype(F32), axis=0, keepdims=True)
                sum_out[pl.ds(e, 1), : slots.shape[2]] = total

            sum_out[...] = jnp.zeros_like(sum_out)
            each(slot_row, 2 * half, 0)

            def piece(for_t):
                return bias_all[:, pl.ds(pl.multiple_of((core * n_t + for_t) * width, 128), width)]

            bias_send[...] = piece(1 - t)
            bias_copy = remote(bias_send, bias_land, b_sems.at[0], b_sems.at[1], across_t)
            bias_copy.start()
            bias_copy.wait()
            bias_out[...] = jnp.where(t == chip, piece(t), bias_land[...])
        for p in range(2):
            each(lambda k: back_in(p, k).wait_recv())
        if backward:
            back_out[...] = land_back[...]
            relay(0, 3)
            relay(1, 3)
            g_own.wait()
            for origin in range(n_h):
                @pl.when((origin < h) & (h < n_h - 1))
                def _():
                    for i in range(own_images):
                        z_hop(i, origin, 1).wait_send()

                @pl.when((origin > h) & (h > 0))
                def _():
                    for i in range(own_images):
                        z_hop(i, origin, 0).wait_send()

            @pl.when(h < n_h - 1)
            def _():
                for i in range(own_images):
                    z_hop(i, h, 1, output.at[i]).wait_send()

            @pl.when(h > 0)
            def _():
                for i in range(own_images):
                    z_hop(i, h, 0, output.at[i]).wait_send()

        for p in range(2):
            each(lambda k: block_out(p, k).wait_send())
            each(lambda k: back_copy(p, k).wait_send())
        for copy in (core_copy, x_copy, act_copy):
            each(lambda j: copy(j).wait_send(), half, 0)

    run(False)
    for copy in kept:
        copy.wait()
    middle_kernel(
        sizes, back_both.at[0], small, combine_v, hidden_v, cotangent_v, output, blocks_1, grad_logits,
        padded,
    )
    run(True)
    for store in stores:
        store.wait()


def experts_pass(sizes, blocks, weights, small, combine, hidden, cotangent, bias_width):
    _, experts, rows, width = weights.shape
    devices = sizes[0] * sizes[1] * sizes[2]
    images = 2 * devices
    half = experts // 2
    vmem = pl.BlockSpec(memory_space=pltpu.VMEM)
    hbm = pl.BlockSpec(memory_space=pl.ANY)
    shape, dma = jax.ShapeDtypeStruct, pltpu.SemaphoreType.DMA
    slots, act = (experts, images, rows), (experts, images, width)
    chunk = (half, images, width)
    block = (2, devices, experts, rows)
    own = hidden.shape[0]
    weight = pltpu.VMEM((experts, rows, width), BF16)
    return pl.pallas_call(
        partial(experts_kernel, sizes),
        out_shape=(
            shape(slots, BF16), shape(act, BF16), shape(slots, BF16), shape(act, BF16),
            shape(block, BF16), shape((experts, bias_width), F32), shape((experts, 256), F32),
            shape((own, hidden.shape[1], 64), F32),
            shape((sizes[1] * own, *hidden.shape[1:]), BF16),
        ),
        in_specs=[vmem, hbm, vmem, hbm, hbm, hbm],
        out_specs=(hbm, hbm, hbm, hbm, vmem, vmem, vmem, vmem, hbm),
        scratch_shapes=[
            weight, weight,
            pltpu.VMEM(chunk, F32), pltpu.VMEM(chunk, F32),
            pltpu.VMEM((2, *slots), BF16), pltpu.VMEM((2, *act), BF16),
            pltpu.VMEM(chunk, BF16), pltpu.VMEM((2, *chunk), BF16),
            pltpu.VMEM(chunk, BF16), pltpu.VMEM((2, *chunk), BF16),
            pltpu.VMEM((2, *block), BF16), pltpu.VMEM(slots, BF16),
            pltpu.VMEM(block, BF16), pltpu.VMEM((2, *block), BF16),
            pltpu.VMEM(blocks.shape, BF16), pltpu.VMEM(hidden.shape, BF16),
            pltpu.VMEM(combine.shape, F32), pltpu.VMEM(hidden.shape, F32),
            pltpu.VMEM(cotangent.shape, BF16), pltpu.VMEM((2, 128, 256), F32),
            pltpu.VMEM((experts, width), F32), pltpu.VMEM((experts, width), F32),
            pltpu.VMEM((experts, bias_width), F32), pltpu.VMEM((experts, bias_width), F32),
            dma((2,)), dma((2, 2)), dma((3,)), dma((2, 2, 2, devices)), dma((2, 2, 2, devices)),
            dma((2, 2, half)), dma((2, 2, half)), dma((2, 2, half)), dma((2,)),
            dma((own, sizes[1], 2)), dma((own, sizes[1])), dma,
        ],
        compiler_params=pltpu.CompilerParams(
            collective_id=1, has_side_effects=True, vmem_limit_bytes=VMEM_BYTES
        ),
        name="experts",
    )(blocks, weights, small, combine, hidden, cotangent)


def weight_grad_kernel(slots_0, act_0, slots_1, act_1, out, lines, pick, same):
    group, images, rows = slots_0.shape
    d_block = out.shape[0]
    few = group // 2
    m, d = pl.program_id(0), pl.program_id(2)

    @pl.when((m == 0) & (pl.program_id(1) == 0) & (d == 0))
    def _():
        row = lax.broadcasted_iota(jnp.int32, pick.shape[1:], 0)
        column = lax.broadcasted_iota(jnp.int32, pick.shape[1:], 1)
        second = (row % group) // few
        for half in range(2):
            feature = 2 * (row // group) + (second if half == 0 else 1 - second)
            pick[half] = (column == feature).astype(F32).astype(BF16)
        row = lax.broadcasted_iota(jnp.int32, same.shape, 0)
        column = lax.broadcasted_iota(jnp.int32, same.shape, 1)
        same[...] = (row % few == column // images).astype(F32)

    def prepare(slots):
        @pl.when(d == 0)
        def _():
            turned = slots[...].reshape(group * images, rows).astype(F32)
            lines[...] = jnp.swapaxes(turned, 0, 1).astype(BF16)

    def term(act):
        mine = lines[pl.ds(pl.multiple_of(d * d_block, d_block), d_block)]
        width = act.shape[2]
        results = []
        for half in range(2):
            columns = mine[:, half * few * images : (half + 1) * few * images]
            spread = (dot(pick[half], columns) * same[...]).astype(BF16)
            values = act[half * few : (half + 1) * few].reshape(few * images, width)
            results.append(dot(spread, values).reshape(d_block // 2, group, width))
        first, last = results
        low = lax.broadcasted_iota(jnp.int32, first.shape, 1) < few
        even = jnp.where(low, first, last)
        odd = pltpu.roll(jnp.where(low, last, first), few, 1)
        out[...] = jnp.stack((even, odd), axis=1).reshape(out.shape)

    @pl.when(m == 0)
    def _():
        prepare(slots_0)
        term(act_0)

    @pl.when(m == 1)
    def _():
        prepare(slots_1)
        term(act_1)


def weight_grads(slots_0, act_0, slots_1, act_1):
    experts, images, rows = slots_0.shape
    hidden = act_0.shape[2]
    group, d_block = 8, 192
    last = experts // group - 1

    def early(m, g, d):
        return jnp.where(m == 0, g, last), 0, 0

    def late(m, g, d):
        return jnp.where(m == 0, 0, g), 0, 0

    slots, act = (group, images, rows), (group, images, hidden)
    return pl.pallas_call(
        weight_grad_kernel,
        grid=(2, experts // group, rows // d_block),
        out_shape=jax.ShapeDtypeStruct((rows, 2, experts, hidden), F32),
        in_specs=[
            pl.BlockSpec(slots, early), pl.BlockSpec(act, early),
            pl.BlockSpec(slots, late), pl.BlockSpec(act, late),
        ],
        out_specs=pl.BlockSpec((d_block, 1, group, hidden), lambda m, g, d: (d, m, g, 0)),
        scratch_shapes=[
            pltpu.VMEM((rows, group * images), BF16),
            pltpu.VMEM((2, group * d_block // 2, d_block), BF16),
            pltpu.VMEM((group * d_block // 2, group * images // 2), F32),
        ],
        compiler_params=pltpu.CompilerParams(vmem_limit_bytes=VMEM_BYTES),
        cost_estimate=pl.CostEstimate(
            flops=4 * images * experts * rows * hidden,
            bytes_accessed=8 * rows * experts * hidden,
            transcendentals=0,
        ),
        name="weight_grads",
    )(slots_0, act_0, slots_1, act_1)


def dot_r(a, b):
    return lax.dot_general(a, b, (((0,), (0,)), ((), ())), preferred_element_type=F32)


def row_of(shape, axis):
    return lax.broadcasted_iota(jnp.int32, shape, axis)


def one_hot(mask):
    return mask.astype(F32).astype(BF16)


def order_matrix(n_h, few, back):
    n = n_h * 8 * few
    shape = (n, n)
    blocked, natural = row_of(shape, 1 if back else 0), row_of(shape, 0 if back else 1)
    f, half, image = blocked % few, (blocked // few) % 2, (blocked // (2 * few)) % 2
    group = blocked // (4 * few)
    if back:
        part, h = group // n_h, group % n_h
    else:
        h, part = group // 2, group % 2
    expert = ((h * 2 + half) * 2 + part) * few + f
    return one_hot(natural == image * (4 * n_h * few) + expert)


def norm_parts(x, scale, shift, live):
    centered = x - jnp.mean(x, axis=-1, keepdims=True)
    inverse = lax.rsqrt(jnp.mean(centered * centered, axis=-1, keepdims=True) + epsilon)
    unit = centered * inverse
    return unit * scale + shift, unit, inverse


def norm_back(grad, unit, inverse, scale):
    scaled = grad * scale
    average = jnp.mean(scaled, axis=-1, keepdims=True)
    projection = jnp.mean(scaled * unit, axis=-1, keepdims=True)
    return (
        inverse * (scaled - average - unit * projection),
        jnp.sum(grad * unit, axis=0, keepdims=True),
        jnp.sum(grad, axis=0, keepdims=True),
    )


def norm_rows(small):
    return jnp.swapaxes(small[:, 128:].astype(F32), 0, 1)[64:68]


def slots_to_blocks(slots, blocks, columns, joined, order):
    n_h, n_s = blocks.shape[:2]
    turned = dot(order, slots).astype(BF16)
    wide = joined.shape[1] // 2
    for s in range(0, n_s, 2):
        lanes = dot(turned[:, s * columns : (s + 2) * columns], joined).astype(BF16)
        for h in range(n_h):
            for p in range(2):
                rows = (h * 2 + p) * 16
                for e in range(2):
                    blocks[h, s + e, p] = lanes[rows : rows + 16, e * wide : e * wide + columns]


def blocks_to_slots(back, sizes, order, pair, padded):
    n_s, n_h, n_t = sizes
    columns = back.shape[3]
    both = jnp.concatenate([order] * n_t, axis=1)
    results = []
    for s in range(n_s):
        rows = jnp.concatenate(
            [
                back[p, (s * n_h + h) * n_t + t]
                for t in range(n_t)
                for p in range(2)
                for h in range(n_h)
            ],
            axis=0,
        )
        padded[s % 2, :, :columns] = dot(both, rows)
        if s % 2:
            value = jnp.concatenate([padded[0], padded[1]], axis=1)
            high = value.astype(BF16)
            rest = (value - high.astype(F32)).astype(BF16)
            results.append(dot(high, pair) + dot(rest, pair))
    return jnp.concatenate(results, axis=1)


def live_rows(shape, length):
    return row_of(shape, 0) < length


class Ahead:
    def __init__(self, length, tokens, small, w, blocks, dispatch, combine, held, joined, order):
        self.length, self.tokens, self.small, self.w = length, tokens, small, w
        self.blocks, self.dispatch, self.combine = blocks, dispatch, combine
        self.normed_1, self.query, self.keyed, self.valued = held[:4]
        self.context, self.hidden, self.normed_2 = held[4:]
        self.joined, self.order = joined, order
        self.n, self.rows, self.width = tokens.shape
        self.live = live_rows((self.rows, 1), length)

    def first_norm(self):
        self.norms = norm_rows(self.small)
        for i in range(self.n):
            value, _, _ = norm_parts(
                self.tokens[i].astype(F32), self.norms[0:1], self.norms[2:3], self.live
            )
            self.normed_1[i] = jnp.where(self.live, value, 0.0).astype(BF16)
        self.joined[...] = pair_matrix(self.blocks.shape[4], self.joined.shape[1] // 2, True)
        self.order[...] = order_matrix(self.blocks.shape[0], 4, False)

    def project(self, k):
        n, rows, width = self.n, self.rows, self.width
        flat = self.normed_1[...].reshape(n * rows, width)
        value = dot(flat, self.w[k]).astype(BF16).reshape(n, rows, width)
        if k == 0:
            self.query[...] = value
        else:
            target = self.keyed if k == 1 else self.valued
            keys = target.shape[1]
            target[:, :rows] = value
            target[:, rows:] = jnp.zeros((n, keys - rows, width), BF16)

    def attend(self):
        query, keyed, valued, context = self.query, self.keyed, self.valued, self.context
        rows, keys = self.rows, keyed.shape[1]
        factor = HEAD_DIM ** (-0.5)
        pairs = self.width // 128
        lane = row_of((rows, 128), 1)
        shown = row_of((rows, keys), 1) < self.length

        def attend(step, carry):
            i = step // pairs
            lanes = pl.ds(pl.multiple_of((step % pairs) * 128, 128), 128)
            q, k, v = query[i, :, lanes], keyed[i, :, lanes], valued[i, :, lanes]
            scaled = q * jnp.bfloat16(factor)
            parts = []
            for a in range(2):
                mine = (lane < 64) if a == 0 else (lane >= 64)
                scores = dot_t(jnp.where(mine, scaled, jnp.zeros_like(q)), k)
                scores = jnp.where(shown, scores, -1e30)
                exponent = jnp.exp(scores - jnp.max(scores, axis=-1, keepdims=True))
                probs = exponent * (1.0 / jnp.sum(exponent, axis=-1, keepdims=True))
                parts.append(dot(probs.astype(BF16), v))
            context[i, :, lanes] = jnp.where(lane < 64, parts[0], parts[1]).astype(BF16)
            return carry

        lax.fori_loop(0, self.n * pairs, attend, 0, unroll=6)

    def finish(self):
        n, rows, width = self.n, self.rows, self.width
        flat = (n * rows, width)
        live = self.live
        attended = dot_t(self.context[...].reshape(flat), self.w[3]).reshape(n, rows, width)
        for i in range(n):
            value = self.tokens[i].astype(F32) + attended[i]
            self.hidden[i] = value
            value, _, _ = norm_parts(value, self.norms[1:2], self.norms[3:4], live)
            self.normed_2[i] = jnp.where(live, value, 0.0).astype(BF16)
        logits = dot(self.normed_2[...].reshape(flat), self.small[:, :128]).reshape(n, rows, 128)
        experts = row_of((rows, 128), 1) < 64
        slots = []
        for i in range(n):
            here = logits[i]
            down = jnp.where(live, here, -1e30)
            exponent = jnp.exp(down - jnp.max(down, axis=0, keepdims=True))
            dispatch = exponent / jnp.sum(exponent, axis=0, keepdims=True)
            dispatch = jnp.where(experts, dispatch, 0.0)
            across = jnp.where(experts, here, -1e30)
            exponent = jnp.exp(across - jnp.max(across, axis=1, keepdims=True))
            combine = exponent / jnp.sum(exponent, axis=1, keepdims=True)
            self.dispatch[i] = dispatch
            self.combine[i] = combine
            slots.append(dot_r(dispatch.astype(BF16), self.normed_2[i])[:64].astype(BF16))
        slots_to_blocks(
            jnp.concatenate(slots, axis=0), self.blocks, self.blocks.shape[4], self.joined[...],
            self.order[...],
        )


def middle_kernel(
    sizes, back, small, combine, hidden, cotangent, output, blocks, grad_logits, padded
):
    n, rows, _ = hidden.shape
    columns = back.shape[3]
    padded[...] = jnp.zeros_like(padded)
    pair = pair_matrix(columns, padded.shape[2], False)
    joined = pair_matrix(columns, padded.shape[2], True)
    total = blocks_to_slots(back, sizes, order_matrix(sizes[1], 4, True), pair, padded)
    bias = jnp.swapaxes(small[:, :128].astype(F32), 0, 1)[64:]
    slots = []
    for i in range(n):
        slot_out = (total[i * 64 : (i + 1) * 64] + bias).astype(BF16)
        combine_b = combine[i].astype(BF16)[:, :64]
        output[i] = (hidden[i] + dot(combine_b, slot_out)).astype(BF16)
        grad_combine = dot_t(cotangent[i], slot_out)
        weight = combine[i][:, :64]
        weighted = jnp.sum(weight * grad_combine, axis=1, keepdims=True)
        grad_logits[i] = weight * (grad_combine - weighted)
        slots.append(dot_r(combine_b, cotangent[i]).astype(BF16))
    slots_to_blocks(
        jnp.concatenate(slots, axis=0), blocks, columns, joined, order_matrix(sizes[1], 4, False)
    )


def behind_kernel(
    sizes, length, back, small, w_hbm, *refs,
):
    later, refs = refs[:6], refs[6:]
    (hidden, normed_2, dispatch, grad_logits, cotangent, grads_out, small_grads, input_grad,
     w, padded, grad_hidden, rounded, grad_context, grad_q, grad_k, grad_v, grads, *refs) = refs
    held, (w_sem, l_sem, g_sem) = refs[:6], refs[6:]
    n, rows, width = hidden.shape
    later_loads = [
        pltpu.make_async_copy(source, target, l_sem.at[j])
        for j, (source, target) in enumerate(zip(later, held))
    ]
    context, query, keyed, valued, normed_1, tokens = held
    keys = keyed.shape[1]
    loads = [pltpu.make_async_copy(w_hbm.at[k], w.at[k], w_sem.at[k]) for k in range(4)]
    for load in loads[3:] + later_loads + loads[:3]:
        load.start()
    norms = norm_rows(small)
    padded[...] = jnp.zeros_like(padded)
    pair = pair_matrix(back.shape[3], padded.shape[2], False)
    grad_slots = blocks_to_slots(
        back, sizes, order_matrix(sizes[1], 4, True), pair, padded
    ).astype(BF16)
    phi = small[:, :64]
    phi_grad = jnp.zeros((width, 64), F32)
    sums = []
    flat = (n * rows, width)
    for i in range(n):
        slots = grad_slots[i * 64 : (i + 1) * 64]
        weight = dispatch[i][:, :64]
        grad_dispatch = dot_t(normed_2[i], slots)
        weighted = jnp.sum(weight * grad_dispatch, axis=0, keepdims=True)
        logits = (weight * (grad_dispatch - weighted) + grad_logits[i]).astype(BF16)
        phi_grad = phi_grad + dot_r(normed_2[i], logits)
        grad = dot(weight.astype(BF16), slots) + dot_t(logits, phi)
        _, unit, inverse = norm_parts(hidden[i], norms[1:2], norms[3:4], None)
        grad_in, scale_grad, bias_grad = norm_back(grad, unit, inverse, norms[1:2])
        value = cotangent[i].astype(F32) + grad_in
        grad_hidden[i] = value
        rounded[i] = value.astype(BF16)
        sums.append((scale_grad, bias_grad))
    scale_2, bias_2 = sums[0][0] + sums[1][0], sums[0][1] + sums[1][1]
    flat_rounded = rounded[...].reshape(flat)
    loads[3].wait()
    grad_context[...] = dot(flat_rounded, w[3]).astype(BF16).reshape(n, rows, width)
    later_loads[0].wait()
    grads[3] = dot_r(flat_rounded, context[...].reshape(flat)).astype(BF16)
    stores = [pltpu.make_async_copy(grads.at[k], grads_out.at[k], g_sem.at[k]) for k in range(4)]
    stores[3].start()
    for load in later_loads[1:4]:
        load.wait()
    factor = HEAD_DIM ** (-0.5)
    pairs = width // 128
    lane = row_of((rows, 128), 1)
    key_lane = row_of((keys, 128), 1)
    shown = row_of((keys, rows), 0) < length

    def attend(step, carry):
        i = step // pairs
        lanes = pl.ds(pl.multiple_of((step % pairs) * 128, 128), 128)
        q, k, v = query[i, :, lanes], keyed[i, :, lanes], valued[i, :, lanes]
        scaled = q * jnp.bfloat16(factor)
        g = grad_context[i, :, lanes]
        to_q, to_k, to_v = [], [], []
        for a in range(2):
            mine = (lane < 64) if a == 0 else (lane >= 64)
            scores = dot_t(k, jnp.where(mine, scaled, jnp.zeros_like(q)))
            grad_probs = dot_t(v, jnp.where(mine, g, jnp.zeros_like(g)))
            scores = jnp.where(shown, scores, -1e30)
            exponent = jnp.exp(scores - jnp.max(scores, axis=0, keepdims=True))
            probs = exponent * (1.0 / jnp.sum(exponent, axis=0, keepdims=True))
            weighted = jnp.sum(probs * grad_probs, axis=0, keepdims=True)
            grad_scores = (probs * (grad_probs - weighted)).astype(BF16)
            to_v.append(dot(probs.astype(BF16), g))
            to_q.append(dot_r(grad_scores, k))
            to_k.append(dot(grad_scores, q))
        grad_q[i, :, lanes] = (jnp.where(lane < 64, to_q[0], to_q[1]) * factor).astype(BF16)
        kept = key_lane < 64
        grad_k[i, :, lanes] = (jnp.where(kept, to_k[0], to_k[1]) * factor)[:rows].astype(BF16)
        grad_v[i, :, lanes] = jnp.where(kept, to_v[0], to_v[1])[:rows].astype(BF16)
        return carry

    lax.fori_loop(0, n * pairs, attend, 0, unroll=6)
    for load in later_loads[4:]:
        load.wait()
    total = jnp.zeros(flat, F32)
    turned = jnp.swapaxes(normed_1[...].reshape(flat).astype(F32), 0, 1).astype(BF16)
    for k, source in enumerate((grad_q, grad_k, grad_v)):
        loads[k].wait()
        value = source[...].reshape(flat)
        total = total + dot_t(value, w[k])
        grads[k] = dot(turned, value).astype(BF16)
        stores[k].start()
    total = total.reshape(n, rows, width)
    sums = []
    for i in range(n):
        _, unit, inverse = norm_parts(tokens[i].astype(F32), norms[0:1], norms[2:3], None)
        grad_in, scale_grad, bias_grad = norm_back(total[i], unit, inverse, norms[0:1])
        input_grad[i] = (grad_hidden[i] + grad_in).astype(BF16)
        sums.append((scale_grad, bias_grad))
    scale_1, bias_1 = sums[0][0] + sums[1][0], sums[0][1] + sums[1][1]
    line = row_of((128, width), 0)
    spread = jnp.zeros((128, width), F32)
    for j, value in enumerate((scale_1, scale_2, bias_1, bias_2)):
        spread = jnp.where(line == 64 + j, value, spread)
    small_grads[...] = jnp.swapaxes(spread, 0, 1).astype(BF16)
    small_grads[:, :64] = phi_grad.astype(BF16)
    for store in stores:
        store.wait()


def tokens_behind(sizes, length, back, small, weights, later, kept, grad_logits, cotangent):
    tokens = later[-1]
    n, rows, width = tokens.shape
    vmem, hbm = pl.BlockSpec(memory_space=pltpu.VMEM), pl.BlockSpec(memory_space=pl.ANY)
    shape = jax.ShapeDtypeStruct
    low = pltpu.VMEM(tokens.shape, BF16)
    return pl.pallas_call(
        partial(behind_kernel, sizes, length),
        out_shape=(
            shape((4, width, width), BF16), shape((width, 128), BF16), shape(tokens.shape, BF16)
        ),
        in_specs=[vmem, vmem] + [hbm] * 7 + [vmem] * 5,
        out_specs=(hbm, vmem, vmem),
        scratch_shapes=[
            pltpu.VMEM(weights.shape, BF16),
            pltpu.VMEM((2, 128, 256), F32),
            pltpu.VMEM(tokens.shape, F32),
            low, low, low, low, low,
            pltpu.VMEM((4, width, width), BF16),
            *[pltpu.VMEM(value.shape, BF16) for value in later],
            pltpu.SemaphoreType.DMA((4,)), pltpu.SemaphoreType.DMA((6,)),
            pltpu.SemaphoreType.DMA((4,)),
        ],
        compiler_params=pltpu.CompilerParams(vmem_limit_bytes=VMEM_BYTES),
        name="tokens_behind",
    )(back, small, weights, *later, *kept, grad_logits, cotangent)


def unpack_kernel(summed, in_bias_sum, out_sum, attn, phi_t, scales, biases, in_bias, out_bias):
    attn[...] = summed[:, :, : attn.shape[2]]
    turned = jnp.swapaxes(summed[0][:, 128:], 0, 1)
    phi_t[...] = turned[64:80]
    scales[...] = turned[80:82]
    biases[...] = turned[82:84]
    in_bias[...] = in_bias_sum[...]
    width = out_bias.shape[1]
    value = out_sum[...]
    later = pltpu.roll(value, value.shape[1] - width, 1)
    out_bias[...] = jnp.where(lax.axis_index("tensor") == 0, value[:, :width], later[:, :width])


def order_kernel(mine, below, above, below_2, above_2, far, out):
    h = lax.axis_index("heads")
    own, rows, width = mine.shape
    group = out.shape[1]
    first_h, low = h == 0, h < 2
    inner = (h == 1) | (h == 2)
    origins = (
        h,
        jnp.where(first_h, h + 1, h - 1),
        jnp.where(low, h + 2, h - 2),
        jnp.where(inner, h + 1, 3 - h),
    )
    step = 256 // group
    length = out.shape[0]
    for first in range(0, length, step):
        count = min(step, length - first)
        taken = min(step, rows - first)
        shape = (count * group, own * taken)
        row = lax.broadcasted_iota(jnp.int32, shape, 0)
        column = lax.broadcasted_iota(jnp.int32, shape, 1)
        there = row // group == column % taken
        image = row % group - column // taken
        chosen = [(there & (image == origin * own)).astype(F32) for origin in origins]

        def lines(part):
            return [part[i, first : first + taken] for i in range(own)]

        def either(condition, one, other):
            return [jnp.where(condition, a, b) for a, b in zip(lines(one), lines(other))]

        values = lines(mine) + either(first_h, above, below)
        values += either(low, above_2, below_2) + either(inner, above, far)
        value = dot(
            jnp.concatenate(chosen, axis=1).astype(BF16), jnp.concatenate(values, axis=0)
        ).astype(BF16)
        out[first : first + count] = value.reshape(count, group, width)


def last_kernel(summed, in_bias_sum, out_sum, *refs):
    unpack_kernel(summed, in_bias_sum, out_sum, *refs[6:12])
    order_kernel(*refs[:6], refs[12])


def last_results(summed, in_bias_sum, out_sum, parts, block, slot, group, length):
    n_k, rows, _ = summed.shape
    vmem = pl.BlockSpec(memory_space=pltpu.VMEM)
    shape = jax.ShapeDtypeStruct
    return pl.pallas_call(
        last_kernel,
        out_shape=(
            shape((n_k, rows, block), F32), shape((slot, rows), F32),
            shape((2, rows), F32), shape((2, rows), F32),
            shape(in_bias_sum.shape, F32), shape((out_sum.shape[0], rows), F32),
            shape((length, group, parts[0].shape[2]), BF16),
        ),
        in_specs=[vmem] * 9,
        out_specs=(vmem,) * 7,
        compiler_params=pltpu.CompilerParams(vmem_limit_bytes=24 * 1024 * 1024),
        name="last_results",
    )(summed, in_bias_sum, out_sum, *parts)


def normalize(values, scale, shift):
    centered = values - jnp.mean(values, axis=-1, keepdims=True)
    variance = jnp.mean(centered * centered, axis=-1, keepdims=True)
    inverse = lax.rsqrt(variance + epsilon)
    unit_part = centered * inverse
    return (unit_part * scale + shift, unit_part, inverse)


def normalize_back(grad_output, unit_part, inverse, scale):
    scaled = grad_output * scale
    average = jnp.mean(scaled, axis=-1, keepdims=True)
    projection = jnp.mean(scaled * unit_part, axis=-1, keepdims=True)
    grad_input = inverse * (scaled - average - unit_part * projection)
    return (
        grad_input,
        jnp.sum(grad_output * unit_part, axis=(0, 1)),
        jnp.sum(grad_output, axis=(0, 1)),
    )


def to_experts(slots):
    slots = lax.all_to_all(slots, "heads", split_axis=1, concat_axis=0, tiled=True)
    slots = lax.all_to_all(slots, "shard", split_axis=2, concat_axis=0, tiled=True)
    return lax.all_gather(slots, "tensor", axis=0, tiled=True)


def to_images(slots):
    slots = lax.psum_scatter(slots, "tensor", scatter_dimension=0, tiled=True)
    slots = lax.all_to_all(slots, "shard", split_axis=0, concat_axis=2, tiled=True)
    return lax.all_to_all(slots, "heads", split_axis=0, concat_axis=1, tiled=True)


def general_shards(tokens, norm_scales, norm_biases, w_attn, phi, experts, in_bias, out_bias, cotangent):
    heads_n = lax.axis_size("heads")
    group, seq_len, width = tokens.shape
    own = group // heads_n
    heads_index = lax.axis_index("heads")
    tensor_index = lax.axis_index("tensor")
    shard_index = lax.axis_index("shard")
    hidden = experts.shape[3]
    rows = experts.shape[0]
    scales, biases, in_full = (
        lax.all_gather(norm_scales, ROWS, axis=1, tiled=True).astype(F32),
        lax.all_gather(norm_biases, ROWS, axis=1, tiled=True).astype(F32),
        lax.all_gather(in_bias, ROWS, axis=1, tiled=True).astype(F32),
    )
    attn = lax.all_gather(
        lax.all_gather(w_attn, "heads", axis=2, tiled=True), ROWS, axis=1, tiled=True
    )
    phi_full = lax.all_gather(
        lax.all_gather(phi, "heads", axis=1, tiled=True), ROWS, axis=0, tiled=True
    )
    out_rows = lax.all_gather(out_bias, "tensor", axis=1, tiled=True).astype(F32)
    e_own = experts.shape[2] // lax.axis_size("shard")
    in_local = lax.dynamic_slice_in_dim(in_full, tensor_index * hidden, hidden, 1)
    factor = HEAD_DIM ** (-0.5)
    tokens = lax.dynamic_slice_in_dim(tokens, heads_index * own, own, 0)
    cotangent = lax.dynamic_slice_in_dim(cotangent, heads_index * own, own, 0)
    n_heads = width // HEAD_DIM
    inputs = tokens.astype(F32)
    normed_one, unit_one, inverse_one = normalize(inputs, scales[0], biases[0])
    normed_one_b = normed_one.astype(BF16)
    projected = einsum("nsd,kdc->knsc", normed_one_b, attn[:3]).astype(BF16)
    query, keyed, valued = projected.reshape(3, own, seq_len, n_heads, HEAD_DIM)
    scores = einsum("nqhe,nkhe->nhqk", query, keyed) * factor
    score_peak = jnp.max(scores, axis=-1, keepdims=True)
    exponent = jnp.exp(scores - score_peak)
    probs = exponent / jnp.sum(exponent, axis=-1, keepdims=True)
    probs_b = probs.astype(BF16)
    context_b = (
        einsum("nhqk,nkhe->nqhe", probs_b, valued).astype(BF16).reshape(own, seq_len, width)
    )
    hidden_one = inputs + einsum("nsc,dc->nsd", context_b, attn[3])
    normed_two, unit_two, inverse_two = normalize(hidden_one, scales[1], biases[1])
    normed_two_b = normed_two.astype(BF16)
    logits = einsum("nsd,de->nse", normed_two_b, phi_full)
    dispatch = jax.nn.softmax(logits, axis=1)
    dispatch_b = dispatch.astype(BF16)
    combine = jax.nn.softmax(logits, axis=2)
    combine_b = combine.astype(BF16)
    slot_in = to_experts(einsum("nse,nsd->ned", dispatch_b, normed_two_b).astype(BF16))
    share = 1 if e_own else 0

    def meet(partial_sum):
        return lax.psum_scatter(partial_sum, "shard", scatter_dimension=share, tiled=True)

    def spread(values):
        return lax.all_gather(values, "shard", axis=share, tiled=True)

    pre = meet(einsum("ned,def->nef", slot_in, experts[:, 0]))
    if e_own:
        pre = pre + lax.dynamic_slice_in_dim(in_local, shard_index * e_own, e_own, 0)
    else:
        pre = pre + in_local
    gelu_value, gelu_back = jax.vjp(partial(jax.nn.gelu, approximate=False), pre)
    activated = spread(gelu_value.astype(BF16))
    slot_out_part = einsum("nef,def->ned", activated, experts[:, 1])
    slot_out_part = slot_out_part + jnp.where(tensor_index == 0, out_rows, 0.0)
    slot_out = to_images(slot_out_part).astype(BF16)
    output = (hidden_one + einsum("nse,ned->nsd", combine_b, slot_out)).astype(BF16)
    output = lax.all_gather(output, "heads", axis=0, tiled=True)
    grad_combine = einsum("nsd,ned->nse", cotangent, slot_out)
    grad_slot = to_experts(einsum("nse,nsd->ned", combine_b, cotangent).astype(BF16))
    grad_act = meet(einsum("ned,def->nef", grad_slot, experts[:, 1]))
    grad_pre = spread(gelu_back(grad_act)[0].astype(BF16))
    grad_slot_in = einsum("nef,def->ned", grad_pre, experts[:, 0]).astype(BF16)
    input_term = einsum("ned,nef->def", slot_in, grad_pre)
    output_term = einsum("ned,nef->def", grad_slot, activated)
    experts_grad = jnp.stack((input_term, output_term), axis=1)
    grad_slot_in = to_images(grad_slot_in.astype(F32)).astype(BF16)
    in_bias_grad = lax.dynamic_slice_in_dim(
        lax.all_gather(jnp.sum(grad_pre.astype(F32), axis=0), "tensor", axis=1, tiled=True),
        (shard_index * lax.axis_size("tensor") + tensor_index) * in_bias.shape[1],
        in_bias.shape[1],
        1,
    )
    out_bias_grad = lax.dynamic_slice_in_dim(
        jnp.sum(grad_slot.astype(F32), axis=0),
        tensor_index * out_bias.shape[1],
        out_bias.shape[1],
        1,
    )
    grad_dispatch = einsum("nsd,ned->nse", normed_two_b, grad_slot_in)
    grad_logits = (
        dispatch * (grad_dispatch - jnp.sum(dispatch * grad_dispatch, axis=1, keepdims=True))
        + combine * (grad_combine - jnp.sum(combine * grad_combine, axis=2, keepdims=True))
    ).astype(BF16)
    phi_grad = einsum("nsd,nse->de", normed_two_b, grad_logits)
    grad_normed_two = einsum("nse,ned->nsd", dispatch_b, grad_slot_in) + einsum(
        "nse,de->nsd", grad_logits, phi_full
    )
    grad_hidden_norm, scale_two_grad, bias_two_grad = normalize_back(
        grad_normed_two, unit_two, inverse_two, scales[1]
    )
    grad_hidden = cotangent.astype(F32) + grad_hidden_norm
    grad_hidden_b = grad_hidden.astype(BF16)
    out_weight_grad = einsum("nsd,nsc->dc", grad_hidden_b, context_b)
    grad_context = einsum("nsd,dc->nsc", grad_hidden_b, attn[3]).astype(BF16)
    grad_context = grad_context.reshape(own, seq_len, n_heads, HEAD_DIM)
    grad_value = einsum("nhqk,nqhe->nkhe", probs_b, grad_context).astype(BF16)
    grad_probs = einsum("nqhe,nkhe->nhqk", grad_context, valued)
    grad_scores = (
        probs * (grad_probs - jnp.sum(probs * grad_probs, axis=-1, keepdims=True))
    ).astype(BF16)
    grad_query = (einsum("nhqk,nkhe->nqhe", grad_scores, keyed) * factor).astype(BF16)
    grad_key = (einsum("nhqk,nqhe->nkhe", grad_scores, query) * factor).astype(BF16)
    grad_proj = jnp.stack((grad_query, grad_key, grad_value)).reshape(3, own, seq_len, width)
    proj_grad = einsum("nsd,knsc->kdc", normed_one_b, grad_proj)
    grad_normed_one = einsum("knsc,kdc->nsd", grad_proj, attn[:3])
    grad_input_norm, scale_one_grad, bias_one_grad = normalize_back(
        grad_normed_one, unit_one, inverse_one, scales[0]
    )
    input_grad = (grad_hidden + grad_input_norm).astype(BF16)
    input_grad = lax.all_gather(input_grad, "heads", axis=0, tiled=True)
    attn_grad = jnp.concatenate((proj_grad, out_weight_grad[None]), axis=0)
    attn_grad = lax.psum_scatter(attn_grad, ROWS, scatter_dimension=1, tiled=True)
    attn_grad = lax.psum_scatter(attn_grad, "heads", scatter_dimension=2, tiled=True)
    phi_grad = lax.psum_scatter(phi_grad, ROWS, scatter_dimension=0, tiled=True)
    phi_grad = lax.psum_scatter(phi_grad, "heads", scatter_dimension=1, tiled=True)
    norms = jnp.stack((scale_one_grad, scale_two_grad, bias_one_grad, bias_two_grad))
    norms = lax.psum(lax.psum_scatter(norms, ROWS, scatter_dimension=1, tiled=True), "heads")
    return (
        output,
        input_grad,
        norms[:2],
        norms[2:],
        attn_grad,
        phi_grad,
        experts_grad,
        in_bias_grad,
        out_bias_grad,
    )


def shards(tokens, norm_scales, norm_biases, w_attn, phi, experts, in_bias, out_bias, cotangent):
    arrays = (tokens, norm_scales, norm_biases, w_attn, phi, experts, in_bias, out_bias, cotangent)
    sizes = tuple(lax.axis_size(name) for name in ("shard", "heads", "tensor"))
    group, length, width = tokens.shape
    fits = (sizes, group, width, *experts.shape[:3]) == ((4, 4, 2), 8, 768, 192, 2, 16)
    if not fits or not 192 < length <= 208 or in_bias.shape[1] != 384:
        return general_shards(*arrays)
    n_s, n_h, n_t = sizes
    block, slot = w_attn.shape[2], phi.shape[1]
    tokens, cotangent = (
        values.transpose(1, 0, 2).reshape(group * length, width) for values in (tokens, cotangent)
    )
    attn, small, turned, tokens, cotangent, blocks, dispatch, combine, *held = gather_weights(
        sizes, length, w_attn, phi.T, out_bias, norm_scales, norm_biases, in_bias, experts, tokens,
        cotangent,
    )
    normed_1, query, keyed, valued, context, hidden, normed_2 = held
    slot_in, activated, grad_slot, grad_pre, back, in_bias_grad, out_sum, grad_logits, output = (
        experts_pass(
            sizes, blocks, turned, small, combine, hidden, cotangent, in_bias.shape[1]
        )
    )
    attn_grad, small_grad, input_grad = tokens_behind(
        sizes, length, back, small, attn, (context, query, keyed, valued, normed_1, tokens),
        (hidden, normed_2, dispatch), grad_logits, cotangent,
    )
    def along(values, places):
        return lax.ppermute(values, "heads", places)

    up = [(i, i + 1) for i in range(n_h - 1)]
    down = [(i + 1, i) for i in range(n_h - 1)]
    below, above = along(input_grad, up), along(input_grad, down)
    attn_grad, grad_pre = lax.optimization_barrier((attn_grad, grad_pre))
    experts_grad = weight_grads(slot_in, grad_pre, grad_slot, activated)
    output = output[:, :length].transpose(1, 0, 2)
    attn_grad, experts_grad, output, input_grad, below, above = lax.optimization_barrier(
        (attn_grad, experts_grad, output, input_grad, below, above)
    )
    parts = [
        input_grad, below, above, along(below, up[1:]), along(above, down[:-1]),
        along(input_grad, [(0, n_h - 1), (n_h - 1, 0)]),
    ]
    summed = reduce_grads(sizes, attn_grad, small_grad)
    attn_grad, phi_grad, scales_grad, biases_grad, in_bias_grad, out_bias_grad, input_grad = (
        last_results(summed, in_bias_grad, out_sum, parts, block, slot, group, length)
    )
    return (
        output.transpose(1, 0, 2),
        input_grad.transpose(1, 0, 2),
        scales_grad,
        biases_grad,
        attn_grad,
        phi_grad.T,
        experts_grad,
        in_bias_grad,
        out_bias_grad,
    )


def solution(mesh):
    images = P(ROWS, None, None)
    return jax.shard_map(
        shards,
        mesh=mesh,
        in_specs=(
            images,
            P(None, ROWS),
            P(None, ROWS),
            P(None, ROWS, "heads"),
            P(ROWS, "heads"),
            P("shard", None, "heads", "tensor"),
            P("heads", ROWS),
            P("heads", ROWS),
            images,
        ),
        out_specs=(
            images,
            images,
            P(None, ROWS),
            P(None, ROWS),
            P(None, ROWS, "heads"),
            P(ROWS, "heads"),
            P("shard", None, "heads", "tensor"),
            P("heads", ROWS),
            P("heads", ROWS),
        ),
        check_vma=False,
    )
```

```python
from functools import partial

import jax
import jax.numpy as jnp
from jax import lax
from jax.experimental import pallas as pl
from jax.experimental.pallas import tpu as pltpu
from jax.sharding import PartitionSpec as P

HEAD_DIM = 64
F32 = jnp.float32
BF16 = jnp.bfloat16
ROWS = ("shard", "tensor")
MESH = pl.DeviceIdType.MESH
VMEM_BYTES = 58 * 1024 * 1024
epsilon = 1e-06
einsum = partial(jnp.einsum, preferred_element_type=F32)


def dot(a, b):
    return lax.dot_general(a, b, (((1,), (0,)), ((), ())), preferred_element_type=F32)


def dot_t(a, b):
    return lax.dot_general(a, b, (((1,), (1,)), ((), ())), preferred_element_type=F32)


def swap_matrix(n):
    out = lax.broadcasted_iota(jnp.int32, (n * n, n * n), 0)
    row = lax.broadcasted_iota(jnp.int32, (n * n, n * n), 1)
    return ((out // n == row % n) & (out % n == row // n)).astype(F32).astype(BF16)


class Peers:
    def __init__(self, sizes):
        self.sizes = sizes
        self.at = tuple(lax.axis_index(name) for name in ("shard", "heads", "tensor"))
        self.count = sizes[0] * sizes[1] * sizes[2]

    def flat(self, place):
        return (place[0] * self.sizes[1] + place[1]) * self.sizes[2] + place[2]

    def step(self, k, sign):
        _, n_h, n_t = self.sizes
        steps = (k // (n_h * n_t), (k // n_t) % n_h, k % n_t)
        return tuple(
            lax.rem(at + n + sign * d, n) for at, n, d in zip(self.at, self.sizes, steps)
        )

    def greet_all(self):
        barrier = pltpu.get_barrier_semaphore()

        def signal(k, carry):
            pl.semaphore_signal(barrier, inc=1, device_id=self.step(k, 1), device_id_type=MESH)
            return carry

        lax.fori_loop(1, self.count, signal, 0)
        pl.semaphore_wait(barrier, self.count - 1)


def remote(src, dst, send, recv, place):
    return pltpu.make_async_remote_copy(
        src_ref=src, dst_ref=dst, send_sem=send, recv_sem=recv, device_id=place, device_id_type=MESH
    )


def plane(sizes):
    n_s, n_h, n_t = sizes
    s, h, t = (lax.axis_index(name) for name in ("shard", "heads", "tensor"))
    core, chip = lax.rem(s, 2), s // 2
    sibling = (s + 1 - 2 * core, h, t)
    across_x = (lax.rem(s + 2, n_s), h, t)
    across_y = (s, h, 1 - t)
    line = [(s, lax.rem(h + d, n_h), t) for d in range(n_h)]
    barrier = pltpu.get_barrier_semaphore()
    others = [sibling, across_x, across_y] + line[1:]
    for place in others:
        pl.semaphore_signal(barrier, inc=1, device_id=place, device_id_type=MESH)
    pl.semaphore_wait(barrier, len(others))
    return (s, h, t), core, chip, sibling, across_x, across_y, line


def pair_matrix(block, wide, transposed):
    shape = (2 * block, 2 * wide) if transposed else (2 * wide, 2 * block)
    tight = lax.broadcasted_iota(jnp.int32, shape, 0 if transposed else 1)
    padded = lax.broadcasted_iota(jnp.int32, shape, 1 if transposed else 0)
    second = padded >= wide
    lane = jnp.where(second, padded - wide, padded)
    same = (lane < block) & (tight == jnp.where(second, lane + block, lane))
    return same.astype(F32).astype(BF16)


def gather_kernel(
    sizes, length, w_attn, phi_t, out_bias, scales, biases, in_bias, experts, tokens, cotangent,
    w_out, small_out, turned, own_tokens, own_cot, blocks, dispatch, combine, *refs,
):
    held_out, refs = refs[:7], refs[7:]
    held, refs = refs[:7], refs[7:]
    (joined, order, w, small, lined, extra, stage, tile_in, tile_out, images, picked,
     z_send, z_recv, x_sems, y_sems, d_sems, c_sems, t_sems, o_sems, i_sems, h_sems) = refs
    n_k, rows, block = w_attn.shape
    wide = lined.shape[3]
    slot = phi_t.shape[0]
    own_h = lax.axis_index("heads")
    stage[...] = jnp.zeros_like(stage)
    stage[64 : 64 + slot] = phi_t[...].astype(F32)
    stage[64 + slot : 64 + 2 * slot] = out_bias[...].astype(F32)
    lined[own_h, :, :, 128:] = jnp.zeros((n_k, rows, wide - 128), BF16)
    lined[own_h, :, :, :block] = w_attn[...]
    first = lined[own_h, 0, :, 128:].astype(F32) + jnp.swapaxes(stage[...], 0, 1)
    lined[own_h, 0, :, 128:] = first.astype(BF16)
    (s, h, t), core, chip, sibling, across_x, across_y, line = plane(sizes)
    n_h, n_t = sizes[1], sizes[2]
    width = w.shape[2]
    side = 16
    n_tiles = experts.shape[0] // side
    depth = tile_in.shape[0]
    halves = ((0, rows // 2), (rows // 2, rows // 2))

    def z_hop(k, origin, up):
        place = line[1] if up else line[n_h - 1]
        return remote(
            lined.at[origin, k], lined.at[origin, k],
            z_send.at[k, origin, up], z_recv.at[k, origin], place,
        )

    def relay(k, d):
        @pl.when(h >= d)
        def _():
            z_hop(k, h - d, 1).wait_recv()

            @pl.when(h < n_h - 1)
            def _():
                z_hop(k, h - d, 1).start()

        @pl.when(h + d < n_h)
        def _():
            z_hop(k, h + d, 0).wait_recv()

            @pl.when(h > 0)
            def _():
                z_hop(k, h + d, 0).start()

    chunks = (0, 2, 1, 3)
    for k in chunks:
        @pl.when(h < n_h - 1)
        def _():
            z_hop(k, h, 1).start()

        @pl.when(h > 0)
        def _():
            z_hop(k, h, 0).start()

    def load(i):
        return pltpu.make_async_copy(
            experts.at[pl.ds((i % n_tiles) * side, side), i // n_tiles],
            tile_in.at[i % depth],
            t_sems.at[0, i % depth],
        )

    def store(i):
        return pltpu.make_async_copy(
            tile_out.at[i % depth],
            turned.at[i // n_tiles, :, pl.ds((i % n_tiles) * side, side)],
            t_sems.at[1, i % depth],
        )

    image_loads = [
        pltpu.make_async_copy(source, images.at[j], i_sems.at[0, j])
        for j, source in enumerate((tokens, cotangent))
    ]
    for i in range(depth - 1):
        load(i).start()
    for copy in image_loads:
        copy.start()
    swap = swap_matrix(side)
    done = [0]

    def turn(count):
        def step(i, carry):
            load(i).wait()

            @pl.when(i + depth - 1 < 2 * n_tiles)
            def _():
                load(i + depth - 1).start()

            @pl.when(i >= depth)
            def _():
                store(i - depth).wait()

            rows_in = tile_in[i % depth].reshape(side * side, tile_in.shape[3])
            tile_out[i % depth] = dot(swap, rows_in).astype(BF16).reshape(tile_out.shape[1:])
            store(i).start()
            return carry

        last = min(done[0] + count, 2 * n_tiles)
        lax.fori_loop(done[0], last, step, 0)
        done[0] = last

    pair = pair_matrix(block, wide, False)
    shape = (n_h * wide, small.shape[1])
    row = lax.broadcasted_iota(jnp.int32, shape, 0)
    column = lax.broadcasted_iota(jnp.int32, shape, 1)
    lane, of = row % wide - block, row // wide
    beside = (lane >= 0) & (lane < 16) & (column == of * 16 + lane)
    beside |= (lane >= 16) & (lane < 32) & (column == n_h * 16 + of * 16 + lane - 16)
    beside = beside.astype(F32).astype(BF16)

    stage[...] = jnp.zeros_like(stage)
    stage[64:66] = scales[...].astype(F32)
    stage[66:68] = biases[...].astype(F32)
    norms = jnp.swapaxes(stage[...], 0, 1)
    pieces = []
    for j in range(in_bias.shape[1] // 64):
        shape = (in_bias.shape[1], 128)
        row = lax.broadcasted_iota(jnp.int32, shape, 0)
        column = lax.broadcasted_iota(jnp.int32, shape, 1)
        chosen = ((row == 64 * j + column) & (column < 64)).astype(F32).astype(BF16)
        pieces.append(dot(in_bias[...], chosen))
    extra[:, :128] = jnp.zeros((rows, 128), F32)
    extra[:, 128:] = jnp.concatenate(pieces, axis=0) + norms

    image_stores = [
        pltpu.make_async_copy(picked.at[j], target, i_sems.at[1, j])
        for j, target in enumerate((own_tokens, own_cot))
    ]

    def pick_images(j):
        own, padded = picked.shape[1:3]
        group = own * n_h
        lines = images.shape[1]
        image_loads[j].wait()
        step = 256 // group
        for first in range(0, padded, step):
            count = min(step, padded - first)
            taken = min(step * group, lines - first * group)
            shape = (own * count, taken)
            row = lax.broadcasted_iota(jnp.int32, shape, 0)
            column = lax.broadcasted_iota(jnp.int32, shape, 1)
            wanted = (row % count) * group + own * h + row // count
            chosen = (column == wanted).astype(F32).astype(BF16)
            source = images[j, first * group : first * group + taken]
            picked[j, :, first : first + count] = (
                dot(chosen, source).astype(BF16).reshape(own, count, images.shape[2])
            )
        image_stores[j].start()

    def at(k, place):
        first = pl.multiple_of((place[0] * n_t + place[2]) * rows, 16)
        lines = pl.ds(first, rows)
        return small.at[lines] if k == n_k else w.at[k, lines]

    def hop(q, origin, place, sems, j):
        return remote(at(q, origin), at(q, origin), sems.at[0, j], sems.at[1, j], place)

    def half_hop(q, origin, place, half):
        part = at(q, origin).at[pl.ds(*halves[half])]
        j = 2 * q + half
        return remote(part, part, d_sems.at[0, j], d_sems.at[1, j], place)

    me = (s, h, t)
    from_d = (across_x[0], h, across_y[2])
    sent = []

    def send(copy):
        copy.start()
        sent.append(copy)

    def assemble(k):
        for i in range(0, n_h, 2):
            lines = jnp.concatenate([lined[i, k], lined[i + 1, k]], axis=1)
            at(k, me)[:, i * block : (i + 2) * block] = dot(lines, pair).astype(BF16)
        if k == 0:
            lines = jnp.concatenate([lined[i, k] for i in range(n_h)], axis=1)
            at(n_k, me)[...] = (dot(lines, beside) + extra[...]).astype(BF16)
        for q in members(k):
            send(hop(q, me, across_x, x_sems, q))
            send(hop(q, me, across_y, y_sems, q))
            send(hop(q, me, sibling, c_sems, 4 * q))

    def members(k):
        return (0, n_k) if k == 0 else (k,)

    def relay_xy(k):
        for q in members(k):
            hop(q, across_x, across_x, x_sems, q).wait_recv()
            send(half_hop(q, across_x, across_y, 0))
            send(hop(q, across_x, sibling, c_sems, 4 * q + 1))
            hop(q, across_y, across_y, y_sems, q).wait_recv()
            send(half_hop(q, across_y, across_x, 1))
            send(hop(q, across_y, sibling, c_sems, 4 * q + 2))

    def relay_d(k):
        for q in members(k):
            half_hop(q, from_d, across_y, 0).wait_recv()
            half_hop(q, from_d, across_x, 1).wait_recv()
            send(hop(q, from_d, sibling, c_sems, 4 * q + 3))

    for wave in range(n_k + n_h - 2):
        for d in range(1, n_h):
            if 0 <= wave - d + 1 < n_k:
                relay(chunks[wave - d + 1], d)
        turn(2)
        i = wave - n_h + 2
        if i >= 0:
            assemble(chunks[i])
            if i in (1, 2):
                pick_images(i - 1)
            if i >= 1:
                relay_xy(chunks[i - 1])
            if i >= 2:
                relay_d(chunks[i - 2])
            turn(2)
    stores = []

    def arrive(q):
        for j in range(4):
            hop(q, me, sibling, c_sems, 4 * q + j).wait_recv()
        if q == n_k:
            stores.append(pltpu.make_async_copy(small, small_out, o_sems.at[q]))
        else:
            stores.append(pltpu.make_async_copy(w.at[q], w_out.at[q], o_sems.at[q]))
        stores[-1].start()

    def keep(first, last):
        for j in range(first, last):
            stores.append(pltpu.make_async_copy(held[j], held_out[j], h_sems.at[j]))
            stores[-1].start()

    ahead = Ahead(
        length, picked.at[0], small, w, blocks, dispatch, combine, held, joined, order
    )
    arrive(n_k)
    ahead.first_norm()
    relay_xy(chunks[-1])
    relay_d(chunks[-2])
    arrive(0)
    ahead.project(0)
    turn(2 * n_tiles)
    arrive(2)
    ahead.project(2)
    arrive(1)
    ahead.project(1)
    relay_d(chunks[-1])
    keep(0, 4)
    ahead.attend()
    arrive(3)
    ahead.finish()
    keep(4, 7)
    for copy in sent:
        copy.wait_send()
    for origin in range(n_h):
        @pl.when((origin <= h) & (h < n_h - 1))
        def _():
            for k in range(n_k):
                z_hop(k, origin, 1).wait_send()

        @pl.when((origin >= h) & (h > 0))
        def _():
            for k in range(n_k):
                z_hop(k, origin, 0).wait_send()

    for i in range(depth):
        store(2 * n_tiles - depth + i).wait()
    for copy in image_stores:
        copy.wait()
    for copy in stores:
        copy.wait()


def gather_weights(
    sizes, length, w_attn, phi_t, out_bias, scales, biases, in_bias, experts, tokens, cotangent
):
    n_k, rows, _ = w_attn.shape
    wide = 256
    n_s, n_h, n_t = sizes
    width = n_s * n_t * rows
    vmem = pl.BlockSpec(memory_space=pltpu.VMEM)
    hbm = pl.BlockSpec(memory_space=pl.ANY)
    dma = pltpu.SemaphoreType.DMA
    hidden = experts.shape[3]
    small = (width, wide)
    images = jax.ShapeDtypeStruct((2, 208, width), BF16)
    shape = jax.ShapeDtypeStruct
    keys = shape((2, 256, width), BF16)
    thin = shape((2, 208, 128), F32)
    held = (images, images, keys, keys, images, shape(images.shape, F32), images)
    return pl.pallas_call(
        partial(gather_kernel, sizes, length),
        out_shape=(
            jax.ShapeDtypeStruct((n_k, width, width), BF16),
            jax.ShapeDtypeStruct(small, BF16),
            jax.ShapeDtypeStruct((2, experts.shape[2], experts.shape[0], hidden), BF16),
            images, images, shape((n_h, n_s, 2, 16, width // n_s), BF16), thin, thin, *held,
        ),
        in_specs=[vmem] * 6 + [hbm] * 3,
        out_specs=(hbm,) * 5 + (vmem,) * 3 + (hbm,) * 7,
        scratch_shapes=[
            *[pltpu.VMEM(value.shape, value.dtype) for value in held],
            pltpu.VMEM((2 * width // n_s, 512), BF16),
            pltpu.VMEM((128, 128), BF16),
            pltpu.VMEM((n_k, width, width), BF16),
            pltpu.VMEM(small, BF16),
            pltpu.VMEM((n_h, n_k, rows, wide), BF16),
            pltpu.VMEM((rows, wide), F32),
            pltpu.VMEM((128, rows), F32),
            pltpu.VMEM((4, 16, 16, hidden), BF16),
            pltpu.VMEM((4, 16, 16, hidden), BF16),
            pltpu.VMEM((2, *tokens.shape), BF16),
            pltpu.VMEM((2, *images.shape), BF16),
            dma((n_k, n_h, 2)), dma((n_k, n_h)), dma((2, n_k + 1)), dma((2, n_k + 1)),
            dma((2, 2 * (n_k + 1))), dma((2, 4 * (n_k + 1))), dma((2, 4)), dma((n_k + 1,)),
            dma((2, 2)), dma((7,)),
        ],
        compiler_params=pltpu.CompilerParams(
            collective_id=3, has_side_effects=True, vmem_limit_bytes=VMEM_BYTES
        ),
        name="gather_weights",
    )(w_attn, phi_t, out_bias, scales, biases, in_bias, experts, tokens, cotangent)


def reduce_kernel(
    sizes, stored, small, out, grads, load_sems, core_in, core_small, met, met_small,
    d_in, d_small, x_in, x_small, y_in, y_small, pieces, z_in,
    c_sems, d_sems, x_sems, y_sems, z_send, z_recv,
):
    loads = [
        pltpu.make_async_copy(stored.at[k], grads.at[k], load_sems.at[k]) for k in range(4)
    ]
    for k in (0, 2, 1, 3):
        loads[k].start()
    (s, h, t), core, chip, sibling, across_x, across_y, line = plane(sizes)
    n_k, width, _ = grads.shape
    n_s, n_h, n_t = sizes
    rows = width // (n_s * n_t)
    wide = pieces.shape[3]
    pair = n_t * rows
    half = rows // 2
    halves = (pl.ds(0, half), pl.ds(half, half))
    chunks = (0, 2, 1, 3)

    def members(k):
        return (0, n_k) if k == 0 else (k,)

    def pick(q, large, little):
        return little if q == n_k else large.at[q]

    def core_copy(q, x):
        first = pl.multiple_of((2 * x + 1 - core) * pair, 16)
        return remote(
            pick(q, stored, small).at[pl.ds(first, pair)],
            pick(q, core_in, core_small).at[x],
            c_sems.at[0, 2 * q + x], c_sems.at[1, 2 * q + x], sibling,
        )

    for k in chunks:
        for q in members(k):
            for x in range(2):
                core_copy(q, x).start()
    joined = pair_matrix(width // n_h, wide, True)
    shape = (small.shape[1], n_h * wide)
    row = lax.broadcasted_iota(jnp.int32, shape, 0)
    column = lax.broadcasted_iota(jnp.int32, shape, 1)
    lane, of = column % wide - width // n_h, column // wide
    beside = (lane >= 0) & (lane < 16) & (row == of * 16 + lane)
    beside |= (lane >= 16) & (lane < 20) & (row == n_h * 16 + lane - 16)
    beside = beside.astype(F32).astype(BF16)
    to_d, to_x, to_y = (d_in, d_small), (x_in, x_small), (y_in, y_small)
    sent = []

    def hop(q, kind, part, source, place):
        sems = {id(to_d): d_sems, id(to_x): x_sems, id(to_y): y_sems}[id(kind)]
        target = pick(q, *kind)
        target = target.at[part] if kind is to_d else target.at[halves[part]]
        j = 2 * q + part
        return remote(source, target, sems.at[0, j], sems.at[1, j], place)

    def send(copy):
        copy.start()
        sent.append(copy)

    def part_of(q, x, y, part):
        return pick(q, met, met_small).at[x, y].at[halves[part]]

    def arrived(q, kind, part):
        hop(q, kind, part, part_of(q, 0, 0, part), sibling).wait_recv()

    def open_up(q):
        part = pick(q, met, met_small)
        if q < n_k:
            loads[q].wait()
        for x in range(2):
            core_copy(q, x).wait_recv()
            first = pl.multiple_of((2 * x + core) * pair, 16)
            own = pick(q, grads, small)[pl.ds(first, pair)].astype(F32)
            total = own + pick(q, core_in, core_small)[x].astype(F32)
            part[x] = total.astype(BF16).reshape(n_t, rows, total.shape[1])
        send(hop(q, to_d, 0, part_of(q, 1 - chip, 1 - t, 0), across_x))
        send(hop(q, to_d, 1, part_of(q, 1 - chip, 1 - t, 1), across_y))
        send(hop(q, to_x, 0, part_of(q, 1 - chip, t, 0), across_x))
        send(hop(q, to_y, 1, part_of(q, chip, 1 - t, 1), across_y))

    def pass_on(q):
        for part, kind, x, y, place in (
            (0, to_y, chip, 1 - t, across_y),
            (1, to_x, 1 - chip, t, across_x),
        ):
            arrived(q, to_d, part)
            block = part_of(q, x, y, part)
            total = block[...].astype(F32) + pick(q, *to_d)[part].astype(F32)
            block[...] = total.astype(BF16)
            send(hop(q, kind, part, block, place))

    def whole(q):
        for kind in (to_x, to_y):
            for part in range(2):
                arrived(q, kind, part)
        total = pick(q, met, met_small)[chip, t].astype(F32) + pick(q, *to_x)[...].astype(F32)
        return (total + pick(q, *to_y)[...].astype(F32)).astype(BF16)

    def z_copy(k, target, up):
        place = line[1] if up else line[n_h - 1]
        return remote(
            pieces.at[target, k], z_in.at[up, target, k],
            z_send.at[up, target, k], z_recv.at[up, target, k], place,
        )

    def pass_along(k, hops):
        for up in range(2):
            for target in range(n_h - 1, -1, -1) if up else range(n_h):
                further = target > h if up else target < h

                @pl.when(further & (h == (hops if up else n_h - 1 - hops)))
                def _():
                    if hops > 0:
                        z_copy(k, target, up).wait_recv()
                        total = pieces[target, k].astype(F32) + z_in[up, target, k].astype(F32)
                        pieces[target, k] = total.astype(BF16)
                    z_copy(k, target, up).start()

    def share_out(k):
        value = whole(k)
        columns = width // n_h
        if k == 0:
            little = dot(whole(n_k), beside)
        for i in range(0, n_h, 2):
            lanes = dot(value[:, i * columns : (i + 2) * columns], joined)
            if k == 0:
                lanes = lanes + little[:, i * wide : (i + 2) * wide]
            pieces[i, k] = lanes[:, :wide].astype(BF16)
            pieces[i + 1, k] = lanes[:, wide:].astype(BF16)
        pass_along(k, 0)

    for i in range(n_k + 2 + n_h - 2):
        if i < n_k:
            for q in members(chunks[i]):
                open_up(q)
        if 0 <= i - 1 < n_k:
            for q in members(chunks[i - 1]):
                pass_on(q)
        if 0 <= i - 2 < n_k:
            share_out(chunks[i - 2])
        for hops in range(1, n_h - 1):
            if 0 <= i - 2 - hops < n_k:
                pass_along(chunks[i - 2 - hops], hops)
    for k in chunks:
        out[k] = pieces[h, k].astype(F32)
        for up, there in ((1, h > 0), (0, h < n_h - 1)):
            @pl.when(there)
            def _():
                z_copy(k, h, up).wait_recv()
                out[k] = out[k] + z_in[up, h, k].astype(F32)

    for k in chunks:
        for q in members(k):
            for x in range(2):
                core_copy(q, x).wait_send()
    for copy in sent:
        copy.wait_send()
    for target in range(n_h):
        for up in range(2):
            @pl.when(target > h if up else target < h)
            def _():
                for k in range(n_k):
                    z_copy(k, target, up).wait_send()


def reduce_grads(sizes, grads, small):
    n_k, width, _ = grads.shape
    n_s, n_h, n_t = sizes
    rows, wide, thin = width // (n_s * n_t), 256, small.shape[1]
    vmem = pl.BlockSpec(memory_space=pltpu.VMEM)
    dma = pltpu.SemaphoreType.DMA

    def buffers(*lead):
        return [
            pltpu.VMEM((n_k, *lead, width), BF16),
            pltpu.VMEM((*lead, thin), BF16),
        ]

    return pl.pallas_call(
        partial(reduce_kernel, sizes),
        out_shape=jax.ShapeDtypeStruct((n_k, rows, wide), F32),
        in_specs=[pl.BlockSpec(memory_space=pl.ANY), vmem],
        out_specs=vmem,
        scratch_shapes=[
            pltpu.VMEM(grads.shape, BF16), dma((n_k,)),
            *buffers(2, n_t * rows), *buffers(2, n_t, rows),
            *buffers(2, rows // 2), *buffers(rows), *buffers(rows),
            pltpu.VMEM((n_h, n_k, rows, wide), BF16),
            pltpu.VMEM((2, n_h, n_k, rows, wide), BF16),
            dma((2, 2 * (n_k + 1))), dma((2, 2 * (n_k + 1))), dma((2, 2 * (n_k + 1))),
            dma((2, 2 * (n_k + 1))), dma((2, n_h, n_k)), dma((2, n_h, n_k)),
        ],
        compiler_params=pltpu.CompilerParams(
            collective_id=4, has_side_effects=True, vmem_limit_bytes=VMEM_BYTES
        ),
        name="reduce_grads",
    )(grads, small)


def experts_kernel(
    sizes, blocks_0, weights, small, combine, hidden, cotangent,
    slots_0_out, act_0_out, slots_1_out, act_1_out, back_out, bias_out, sum_out, grad_logits,
    gathered,
    w_0, w_1, gate, sums, slots_both, act_both, core_out, core_both, x_out, x_both, land_both, leave,
    back, back_both, blocks_1, output, combine_v, hidden_v, cotangent_v, padded, bias, bias_all,
    bias_send, bias_land,
    w_sem, o_sem, m_sem, in_both, return_both, core_sem, x_sem, act_sem, b_sems, g_send, g_recv, g_sem,
):
    peers = Peers(sizes)
    s, h, t = peers.at
    n_s, n_h, n_t = sizes
    me = peers.flat(peers.at)
    core, chip = lax.rem(s, 2), s // 2
    sibling = (s + 1 - 2 * core, h, t)
    across = (lax.rem(s + 2, n_s), h, t)
    half = act_both.shape[1] // 2
    own, other = core * half, (1 - core) * half
    n_blocks = peers.count
    loads = [
        pltpu.make_async_copy(weights.at[0], w_0, w_sem.at[0]),
        pltpu.make_async_copy(weights.at[1], w_1, w_sem.at[1]),
    ]
    kept = [
        pltpu.make_async_copy(source, target, m_sem.at[j])
        for j, (source, target) in enumerate(
            ((combine, combine_v), (hidden, hidden_v), (cotangent, cotangent_v))
        )
    ]
    for load in loads + kept:
        load.start()
    few = half // 2
    group = 16
    many = 2 * group
    peers.greet_all()

    def each(function, count=n_blocks, start=1):
        lax.fori_loop(start, count, lambda k, carry: (function(k), carry)[1], 0)

    out_row = lax.broadcasted_iota(jnp.int32, (16 * group, 16 * group), 0)
    in_row = lax.broadcasted_iota(jnp.int32, (16 * group, 16 * group), 1)
    there = (out_row // many == in_row % (2 * few)) & (out_row % many == in_row // (2 * few))
    there = there.astype(F32).astype(BF16)
    again = (in_row // many == out_row % (2 * few)) & (in_row % many == out_row // (2 * few))
    again = again.astype(F32).astype(BF16)
    stores = []

    def run(backward):
        n = 1 if backward else 0
        blocks = blocks_1 if backward else blocks_0
        w_a, w_b = (w_1, w_0) if backward else (w_0, w_1)
        slots, act, core_in, x_in, land, land_back = (
            both.at[n] for both in (slots_both, act_both, core_both, x_both, land_both, back_both)
        )
        in_sems, back_sems, core_sems, x_sems, act_sems = (
            both.at[n] for both in (in_both, return_both, core_sem, x_sem, act_sem)
        )
        def block_out(p, k):
            place = peers.step(k, 1)
            return remote(
                blocks.at[place[1], place[0], p], land.at[p, me],
                in_sems.at[0, p, k], in_sems.at[1, p, k], place,
            )

        def block_in(p, k):
            source = peers.flat(peers.step(k, -1))
            return remote(
                blocks.at[0, 0, p], land.at[p, source], in_sems.at[0, p, k], in_sems.at[1, p, k], sibling
            )

        for p in range(2):
            for k in range(1, n_blocks):
                block_out(p, k).start()
            land[p, me] = blocks[h, s, p]
        def receive(p):
            each(lambda k: block_in(p, k).wait_recv())
            for b in range(n_blocks // group):
                rows = land[p, b * group : (b + 1) * group].reshape(group * 16, land.shape[3])
                turned = dot(there, rows).astype(BF16).reshape(2 * few, many, land.shape[3])
                for c in range(2):
                    first = c * half + p * few
                    slots[first : first + few, b * many : (b + 1) * many, :] = turned[
                        c * few : (c + 1) * few
                    ]

        if backward:
            own_images = output.shape[0]
            line = [(s, lax.rem(h + d, n_h), t) for d in range(n_h)]
            g_own = pltpu.make_async_copy(output, gathered.at[pl.ds(h * own_images, own_images)], g_sem)
            g_own.start()

            def z_hop(i, origin, up, source=None):
                there = gathered.at[origin * own_images + i]
                return remote(
                    there if source is None else source, there,
                    g_send.at[i, origin, up], g_recv.at[i, origin], line[1] if up else line[n_h - 1],
                )

            def relay(i, d):
                @pl.when(h >= d)
                def _():
                    z_hop(i, h - d, 1).wait_recv()

                    @pl.when((h < n_h - 1) & (d < n_h - 1))
                    def _():
                        z_hop(i, h - d, 1).start()

                @pl.when(h + d < n_h)
                def _():
                    z_hop(i, h + d, 0).wait_recv()

                    @pl.when((h > 0) & (d < n_h - 1))
                    def _():
                        z_hop(i, h + d, 0).start()

            def gather_output():
                for i in range(own_images):
                    @pl.when(h < n_h - 1)
                    def _():
                        z_hop(i, h, 1, output.at[i]).start()

                    @pl.when(h > 0)
                    def _():
                        z_hop(i, h, 0, output.at[i]).start()
        else:
            piece, count = 6 * 64, act.shape[2] // (6 * 64)
            row = lax.broadcasted_iota(jnp.int32, (6 * 128, piece), 0)
            column = lax.broadcasted_iota(jnp.int32, (6 * 128, piece), 1)
            lane = row % 128
            place = (lane < 64) & (column == (row // 128) * 64 + lane)
            place = place.astype(F32).astype(BF16)
            for m in range(count):
                first = (t * count + m) * 96
                lines = [
                    small[pl.ds(pl.multiple_of(first + j * 16, 16), 16), 128:256] for j in range(6)
                ]
                bias[:, m * piece : (m + 1) * piece] = dot(jnp.concatenate(lines, axis=1), place)

        receive(0)
        if backward:
            gather_output()
        if not backward:
            loads[0].wait()

        def core_copy(j):
            return remote(
                core_out.at[j], core_in.at[j], core_sems.at[0, j], core_sems.at[1, j], sibling
            )

        def x_copy(j):
            return remote(x_out.at[j], x_in.at[j], x_sems.at[0, j], x_sems.at[1, j], across)

        def act_copy(j):
            return remote(
                act.at[own + j], act.at[own + j], act_sems.at[0, j], act_sems.at[1, j], sibling
            )

        def act_in(j):
            return remote(
                act.at[other + j], act.at[other + j], act_sems.at[0, j], act_sems.at[1, j], sibling
            )

        def meet(j):
            core_copy(j).wait_recv()
            sums[j] = sums[j] + core_in[j].astype(F32)
            x_out[j] = sums[j].astype(BF16)
            x_copy(j).start()

        def first_sums(j):
            core_out[j] = dot(slots[other + j], w_a[other + j]).astype(BF16)
            core_copy(j).start()

            @pl.when(j > 0)
            def _():
                meet(j - 1)

            sums[j] = dot(slots[own + j], w_a[own + j])

        each(first_sums, few, 0)
        receive(1)
        each(first_sums, half, few)
        meet(half - 1)
        if not backward:
            loads[1].wait()

        def second(e):
            leave[e] = dot_t(act[e], w_b[e]).astype(BF16)

        def finish(j):
            x_copy(j).wait_recv()
            value = sums[j] + x_in[j].astype(F32)
            if backward:
                act[own + j] = (value * gate[j]).astype(BF16)
            else:
                value = value + bias[pl.ds(own + j, 1), :]
                cumulative = 0.5 + 0.5 * lax.erf(value * 0.7071067811865476)
                act[own + j] = (value * cumulative).astype(BF16)
                gate[j] = cumulative + value * (
                    jnp.exp(value * value * -0.5) * 0.3989422804014327
                )
            act_copy(j).start()
            second(own + j)

            @pl.when(j > 0)
            def _():
                act_in(j - 1).wait_recv()
                second(other + j - 1)

            if backward:
                for when, i, d in ((2, 0, 1), (3, 1, 1), (5, 0, 2), (7, 1, 2)):
                    @pl.when(j == when)
                    def _():
                        relay(i, d)

        def back_copy(p, k):
            place = peers.step(k, 1)
            return remote(
                back.at[p, peers.flat(place)], land_back.at[p, me],
                back_sems.at[0, p, k], back_sems.at[1, p, k], place,
            )

        def back_in(p, k):
            source = peers.flat(peers.step(k, -1))
            return remote(
                back.at[p, 0], land_back.at[p, source],
                back_sems.at[0, p, k], back_sems.at[1, p, k], sibling,
            )

        def give_back(p):
            for b in range(n_blocks // group):
                rows = jnp.concatenate(
                    [
                        leave[c * half + p * few : c * half + (p + 1) * few, b * many : (b + 1) * many, :]
                        for c in range(2)
                    ],
                    axis=0,
                ).reshape(group * 16, leave.shape[2])
                turned = dot(again, rows).astype(BF16)
                back[p, b * group : (b + 1) * group] = turned.reshape(group, 16, leave.shape[2])
            for k in range(1, n_blocks):
                back_copy(p, k).start()
            land_back[p, me] = back[p, me]

        each(finish, few + 1, 0)
        give_back(0)
        each(finish, half, few + 1)
        act_in(half - 1).wait_recv()
        second(other + half - 1)
        give_back(1)
        outs = (slots_1_out, act_1_out) if backward else (slots_0_out, act_0_out)
        for j, (source, target) in enumerate(zip((slots, act), outs)):
            stores.append(pltpu.make_async_copy(source, target, o_sem.at[n, j]))
            stores[-1].start()
        if backward:
            across_t = (s, h, 1 - t)
            width = bias_out.shape[1]

            def bias_row(e):
                bias_all[pl.ds(e, 1), :] = jnp.sum(act[e].astype(F32), axis=0, keepdims=True)

            each(bias_row, 2 * half, 0)

            def slot_row(e):
                total = jnp.sum(slots[e].astype(F32), axis=0, keepdims=True)
                sum_out[pl.ds(e, 1), : slots.shape[2]] = total

            sum_out[...] = jnp.zeros_like(sum_out)
            each(slot_row, 2 * half, 0)

            def piece(for_t):
                return bias_all[:, pl.ds(pl.multiple_of((core * n_t + for_t) * width, 128), width)]

            bias_send[...] = piece(1 - t)
            bias_copy = remote(bias_send, bias_land, b_sems.at[0], b_sems.at[1], across_t)
            bias_copy.start()
            bias_copy.wait()
            bias_out[...] = jnp.where(t == chip, piece(t), bias_land[...])
        for p in range(2):
            each(lambda k: back_in(p, k).wait_recv())
        if backward:
            back_out[...] = land_back[...]
            relay(0, 3)
            relay(1, 3)
            g_own.wait()
            for origin in range(n_h):
                @pl.when((origin < h) & (h < n_h - 1))
                def _():
                    for i in range(own_images):
                        z_hop(i, origin, 1).wait_send()

                @pl.when((origin > h) & (h > 0))
                def _():
                    for i in range(own_images):
                        z_hop(i, origin, 0).wait_send()

            @pl.when(h < n_h - 1)
            def _():
                for i in range(own_images):
                    z_hop(i, h, 1, output.at[i]).wait_send()

            @pl.when(h > 0)
            def _():
                for i in range(own_images):
                    z_hop(i, h, 0, output.at[i]).wait_send()

        for p in range(2):
            each(lambda k: block_out(p, k).wait_send())
            each(lambda k: back_copy(p, k).wait_send())
        for copy in (core_copy, x_copy, act_copy):
            each(lambda j: copy(j).wait_send(), half, 0)

    run(False)
    for copy in kept:
        copy.wait()
    middle_kernel(
        sizes, back_both.at[0], small, combine_v, hidden_v, cotangent_v, output, blocks_1, grad_logits,
        padded,
    )
    run(True)
    for store in stores:
        store.wait()


def experts_pass(sizes, blocks, weights, small, combine, hidden, cotangent, bias_width):
    _, experts, rows, width = weights.shape
    devices = sizes[0] * sizes[1] * sizes[2]
    images = 2 * devices
    half = experts // 2
    vmem = pl.BlockSpec(memory_space=pltpu.VMEM)
    hbm = pl.BlockSpec(memory_space=pl.ANY)
    shape, dma = jax.ShapeDtypeStruct, pltpu.SemaphoreType.DMA
    slots, act = (experts, images, rows), (experts, images, width)
    chunk = (half, images, width)
    block = (2, devices, experts, rows)
    own = hidden.shape[0]
    weight = pltpu.VMEM((experts, rows, width), BF16)
    return pl.pallas_call(
        partial(experts_kernel, sizes),
        out_shape=(
            shape(slots, BF16), shape(act, BF16), shape(slots, BF16), shape(act, BF16),
            shape(block, BF16), shape((experts, bias_width), F32), shape((experts, 256), F32),
            shape((own, hidden.shape[1], 64), F32),
            shape((sizes[1] * own, *hidden.shape[1:]), BF16),
        ),
        in_specs=[vmem, hbm, vmem, hbm, hbm, hbm],
        out_specs=(hbm, hbm, hbm, hbm, vmem, vmem, vmem, vmem, hbm),
        scratch_shapes=[
            weight, weight,
            pltpu.VMEM(chunk, F32), pltpu.VMEM(chunk, F32),
            pltpu.VMEM((2, *slots), BF16), pltpu.VMEM((2, *act), BF16),
            pltpu.VMEM(chunk, BF16), pltpu.VMEM((2, *chunk), BF16),
            pltpu.VMEM(chunk, BF16), pltpu.VMEM((2, *chunk), BF16),
            pltpu.VMEM((2, *block), BF16), pltpu.VMEM(slots, BF16),
            pltpu.VMEM(block, BF16), pltpu.VMEM((2, *block), BF16),
            pltpu.VMEM(blocks.shape, BF16), pltpu.VMEM(hidden.shape, BF16),
            pltpu.VMEM(combine.shape, F32), pltpu.VMEM(hidden.shape, F32),
            pltpu.VMEM(cotangent.shape, BF16), pltpu.VMEM((2, 128, 256), F32),
            pltpu.VMEM((experts, width), F32), pltpu.VMEM((experts, width), F32),
            pltpu.VMEM((experts, bias_width), F32), pltpu.VMEM((experts, bias_width), F32),
            dma((2,)), dma((2, 2)), dma((3,)), dma((2, 2, 2, devices)), dma((2, 2, 2, devices)),
            dma((2, 2, half)), dma((2, 2, half)), dma((2, 2, half)), dma((2,)),
            dma((own, sizes[1], 2)), dma((own, sizes[1])), dma,
        ],
        compiler_params=pltpu.CompilerParams(
            collective_id=1, has_side_effects=True, vmem_limit_bytes=VMEM_BYTES
        ),
        name="experts",
    )(blocks, weights, small, combine, hidden, cotangent)


def weight_grad_kernel(slots_0, act_0, slots_1, act_1, out, lines, pick, same):
    group, images, rows = slots_0.shape
    d_block = out.shape[0]
    few = group // 2
    m, d = pl.program_id(0), pl.program_id(2)

    @pl.when((m == 0) & (pl.program_id(1) == 0) & (d == 0))
    def _():
        row = lax.broadcasted_iota(jnp.int32, pick.shape[1:], 0)
        column = lax.broadcasted_iota(jnp.int32, pick.shape[1:], 1)
        second = (row % group) // few
        for half in range(2):
            feature = 2 * (row // group) + (second if half == 0 else 1 - second)
            pick[half] = (column == feature).astype(F32).astype(BF16)
        row = lax.broadcasted_iota(jnp.int32, same.shape, 0)
        column = lax.broadcasted_iota(jnp.int32, same.shape, 1)
        same[...] = (row % few == column // images).astype(F32)

    def prepare(slots):
        @pl.when(d == 0)
        def _():
            turned = slots[...].reshape(group * images, rows).astype(F32)
            lines[...] = jnp.swapaxes(turned, 0, 1).astype(BF16)

    def term(act):
        mine = lines[pl.ds(pl.multiple_of(d * d_block, d_block), d_block)]
        width = act.shape[2]
        results = []
        for half in range(2):
            columns = mine[:, half * few * images : (half + 1) * few * images]
            spread = (dot(pick[half], columns) * same[...]).astype(BF16)
            values = act[half * few : (half + 1) * few].reshape(few * images, width)
            results.append(dot(spread, values).reshape(d_block // 2, group, width))
        first, last = results
        low = lax.broadcasted_iota(jnp.int32, first.shape, 1) < few
        even = jnp.where(low, first, last)
        odd = pltpu.roll(jnp.where(low, last, first), few, 1)
        out[...] = jnp.stack((even, odd), axis=1).reshape(out.shape)

    @pl.when(m == 0)
    def _():
        prepare(slots_0)
        term(act_0)

    @pl.when(m == 1)
    def _():
        prepare(slots_1)
        term(act_1)


def weight_grads(slots_0, act_0, slots_1, act_1):
    experts, images, rows = slots_0.shape
    hidden = act_0.shape[2]
    group, d_block = 8, 192
    last = experts // group - 1

    def early(m, g, d):
        return jnp.where(m == 0, g, last), 0, 0

    def late(m, g, d):
        return jnp.where(m == 0, 0, g), 0, 0

    slots, act = (group, images, rows), (group, images, hidden)
    return pl.pallas_call(
        weight_grad_kernel,
        grid=(2, experts // group, rows // d_block),
        out_shape=jax.ShapeDtypeStruct((rows, 2, experts, hidden), F32),
        in_specs=[
            pl.BlockSpec(slots, early), pl.BlockSpec(act, early),
            pl.BlockSpec(slots, late), pl.BlockSpec(act, late),
        ],
        out_specs=pl.BlockSpec((d_block, 1, group, hidden), lambda m, g, d: (d, m, g, 0)),
        scratch_shapes=[
            pltpu.VMEM((rows, group * images), BF16),
            pltpu.VMEM((2, group * d_block // 2, d_block), BF16),
            pltpu.VMEM((group * d_block // 2, group * images // 2), F32),
        ],
        compiler_params=pltpu.CompilerParams(vmem_limit_bytes=VMEM_BYTES),
        cost_estimate=pl.CostEstimate(
            flops=4 * images * experts * rows * hidden,
            bytes_accessed=8 * rows * experts * hidden,
            transcendentals=0,
        ),
        name="weight_grads",
    )(slots_0, act_0, slots_1, act_1)


def dot_r(a, b):
    return lax.dot_general(a, b, (((0,), (0,)), ((), ())), preferred_element_type=F32)


def row_of(shape, axis):
    return lax.broadcasted_iota(jnp.int32, shape, axis)


def one_hot(mask):
    return mask.astype(F32).astype(BF16)


def order_matrix(n_h, few, back):
    n = n_h * 8 * few
    shape = (n, n)
    blocked, natural = row_of(shape, 1 if back else 0), row_of(shape, 0 if back else 1)
    f, half, image = blocked % few, (blocked // few) % 2, (blocked // (2 * few)) % 2
    group = blocked // (4 * few)
    if back:
        part, h = group // n_h, group % n_h
    else:
        h, part = group // 2, group % 2
    expert = ((h * 2 + half) * 2 + part) * few + f
    return one_hot(natural == image * (4 * n_h * few) + expert)


def norm_parts(x, scale, shift, live):
    centered = x - jnp.mean(x, axis=-1, keepdims=True)
    inverse = lax.rsqrt(jnp.mean(centered * centered, axis=-1, keepdims=True) + epsilon)
    unit = centered * inverse
    return unit * scale + shift, unit, inverse


def norm_back(grad, unit, inverse, scale):
    scaled = grad * scale
    average = jnp.mean(scaled, axis=-1, keepdims=True)
    projection = jnp.mean(scaled * unit, axis=-1, keepdims=True)
    return (
        inverse * (scaled - average - unit * projection),
        jnp.sum(grad * unit, axis=0, keepdims=True),
        jnp.sum(grad, axis=0, keepdims=True),
    )


def norm_rows(small):
    return jnp.swapaxes(small[:, 128:].astype(F32), 0, 1)[64:68]


def slots_to_blocks(slots, blocks, columns, joined, order):
    n_h, n_s = blocks.shape[:2]
    turned = dot(order, slots).astype(BF16)
    wide = joined.shape[1] // 2
    for s in range(0, n_s, 2):
        lanes = dot(turned[:, s * columns : (s + 2) * columns], joined).astype(BF16)
        for h in range(n_h):
            for p in range(2):
                rows = (h * 2 + p) * 16
                for e in range(2):
                    blocks[h, s + e, p] = lanes[rows : rows + 16, e * wide : e * wide + columns]


def blocks_to_slots(back, sizes, order, pair, padded):
    n_s, n_h, n_t = sizes
    columns = back.shape[3]
    both = jnp.concatenate([order] * n_t, axis=1)
    results = []
    for s in range(n_s):
        rows = jnp.concatenate(
            [
                back[p, (s * n_h + h) * n_t + t]
                for t in range(n_t)
                for p in range(2)
                for h in range(n_h)
            ],
            axis=0,
        )
        padded[s % 2, :, :columns] = dot(both, rows)
        if s % 2:
            value = jnp.concatenate([padded[0], padded[1]], axis=1)
            high = value.astype(BF16)
            rest = (value - high.astype(F32)).astype(BF16)
            results.append(dot(high, pair) + dot(rest, pair))
    return jnp.concatenate(results, axis=1)


def live_rows(shape, length):
    return row_of(shape, 0) < length


class Ahead:
    def __init__(self, length, tokens, small, w, blocks, dispatch, combine, held, joined, order):
        self.length, self.tokens, self.small, self.w = length, tokens, small, w
        self.blocks, self.dispatch, self.combine = blocks, dispatch, combine
        self.normed_1, self.query, self.keyed, self.valued = held[:4]
        self.context, self.hidden, self.normed_2 = held[4:]
        self.joined, self.order = joined, order
        self.n, self.rows, self.width = tokens.shape
        self.live = live_rows((self.rows, 1), length)

    def first_norm(self):
        self.norms = norm_rows(self.small)
        for i in range(self.n):
            value, _, _ = norm_parts(
                self.tokens[i].astype(F32), self.norms[0:1], self.norms[2:3], self.live
            )
            self.normed_1[i] = jnp.where(self.live, value, 0.0).astype(BF16)
        self.joined[...] = pair_matrix(self.blocks.shape[4], self.joined.shape[1] // 2, True)
        self.order[...] = order_matrix(self.blocks.shape[0], 4, False)

    def project(self, k):
        n, rows, width = self.n, self.rows, self.width
        flat = self.normed_1[...].reshape(n * rows, width)
        value = dot(flat, self.w[k]).astype(BF16).reshape(n, rows, width)
        if k == 0:
            self.query[...] = value
        else:
            target = self.keyed if k == 1 else self.valued
            keys = target.shape[1]
            target[:, :rows] = value
            target[:, rows:] = jnp.zeros((n, keys - rows, width), BF16)

    def attend(self):
        query, keyed, valued, context = self.query, self.keyed, self.valued, self.context
        rows, keys = self.rows, keyed.shape[1]
        factor = HEAD_DIM ** (-0.5)
        pairs = self.width // 128
        lane = row_of((rows, 128), 1)
        shown = row_of((rows, keys), 1) < self.length

        def attend(step, carry):
            i = step // pairs
            lanes = pl.ds(pl.multiple_of((step % pairs) * 128, 128), 128)
            q, k, v = query[i, :, lanes], keyed[i, :, lanes], valued[i, :, lanes]
            scaled = q * jnp.bfloat16(factor)
            parts = []
            for a in range(2):
                mine = (lane < 64) if a == 0 else (lane >= 64)
                scores = dot_t(jnp.where(mine, scaled, jnp.zeros_like(q)), k)
                scores = jnp.where(shown, scores, -1e30)
                exponent = jnp.exp(scores - jnp.max(scores, axis=-1, keepdims=True))
                probs = exponent * (1.0 / jnp.sum(exponent, axis=-1, keepdims=True))
                parts.append(dot(probs.astype(BF16), v))
            context[i, :, lanes] = jnp.where(lane < 64, parts[0], parts[1]).astype(BF16)
            return carry

        lax.fori_loop(0, self.n * pairs, attend, 0, unroll=6)

    def finish(self):
        n, rows, width = self.n, self.rows, self.width
        flat = (n * rows, width)
        live = self.live
        attended = dot_t(self.context[...].reshape(flat), self.w[3]).reshape(n, rows, width)
        for i in range(n):
            value = self.tokens[i].astype(F32) + attended[i]
            self.hidden[i] = value
            value, _, _ = norm_parts(value, self.norms[1:2], self.norms[3:4], live)
            self.normed_2[i] = jnp.where(live, value, 0.0).astype(BF16)
        logits = dot(self.normed_2[...].reshape(flat), self.small[:, :128]).reshape(n, rows, 128)
        experts = row_of((rows, 128), 1) < 64
        slots = []
        for i in range(n):
            here = logits[i]
            down = jnp.where(live, here, -1e30)
            exponent = jnp.exp(down - jnp.max(down, axis=0, keepdims=True))
            dispatch = exponent / jnp.sum(exponent, axis=0, keepdims=True)
            dispatch = jnp.where(experts, dispatch, 0.0)
            across = jnp.where(experts, here, -1e30)
            exponent = jnp.exp(across - jnp.max(across, axis=1, keepdims=True))
            combine = exponent / jnp.sum(exponent, axis=1, keepdims=True)
            self.dispatch[i] = dispatch
            self.combine[i] = combine
            slots.append(dot_r(dispatch.astype(BF16), self.normed_2[i])[:64].astype(BF16))
        slots_to_blocks(
            jnp.concatenate(slots, axis=0), self.blocks, self.blocks.shape[4], self.joined[...],
            self.order[...],
        )


def middle_kernel(
    sizes, back, small, combine, hidden, cotangent, output, blocks, grad_logits, padded
):
    n, rows, _ = hidden.shape
    columns = back.shape[3]
    padded[...] = jnp.zeros_like(padded)
    pair = pair_matrix(columns, padded.shape[2], False)
    joined = pair_matrix(columns, padded.shape[2], True)
    total = blocks_to_slots(back, sizes, order_matrix(sizes[1], 4, True), pair, padded)
    bias = jnp.swapaxes(small[:, :128].astype(F32), 0, 1)[64:]
    slots = []
    for i in range(n):
        slot_out = (total[i * 64 : (i + 1) * 64] + bias).astype(BF16)
        combine_b = combine[i].astype(BF16)[:, :64]
        output[i] = (hidden[i] + dot(combine_b, slot_out)).astype(BF16)
        grad_combine = dot_t(cotangent[i], slot_out)
        weight = combine[i][:, :64]
        weighted = jnp.sum(weight * grad_combine, axis=1, keepdims=True)
        grad_logits[i] = weight * (grad_combine - weighted)
        slots.append(dot_r(combine_b, cotangent[i]).astype(BF16))
    slots_to_blocks(
        jnp.concatenate(slots, axis=0), blocks, columns, joined, order_matrix(sizes[1], 4, False)
    )


def behind_kernel(
    sizes, length, back, small, w_hbm, *refs,
):
    later, refs = refs[:9], refs[9:]
    (dispatch, grad_logits, grads_out, small_grads, input_grad,
     w, padded, grad_hidden, rounded, grad_context, grad_q, grad_k, grad_v, grads, *refs) = refs
    held, (w_sem, l_sem, g_sem) = refs[:9], refs[9:]
    n, rows, width = grad_hidden.shape
    later_loads = [
        pltpu.make_async_copy(source, target, l_sem.at[j])
        for j, (source, target) in enumerate(zip(later, held))
    ]
    context, query, keyed, valued, normed_1, tokens, hidden, normed_2, cotangent = held
    keys = keyed.shape[1]
    loads = [pltpu.make_async_copy(w_hbm.at[k], w.at[k], w_sem.at[k]) for k in range(4)]
    for load in later_loads[6:] + loads[3:] + later_loads[:6] + loads[:3]:
        load.start()
    norms = norm_rows(small)
    padded[...] = jnp.zeros_like(padded)
    pair = pair_matrix(back.shape[3], padded.shape[2], False)
    grad_slots = blocks_to_slots(
        back, sizes, order_matrix(sizes[1], 4, True), pair, padded
    ).astype(BF16)
    phi = small[:, :64]
    phi_grad = jnp.zeros((width, 64), F32)
    sums = []
    flat = (n * rows, width)
    for load in later_loads[6:]:
        load.wait()
    for i in range(n):
        slots = grad_slots[i * 64 : (i + 1) * 64]
        weight = dispatch[i][:, :64]
        grad_dispatch = dot_t(normed_2[i], slots)
        weighted = jnp.sum(weight * grad_dispatch, axis=0, keepdims=True)
        logits = (weight * (grad_dispatch - weighted) + grad_logits[i]).astype(BF16)
        phi_grad = phi_grad + dot_r(normed_2[i], logits)
        grad = dot(weight.astype(BF16), slots) + dot_t(logits, phi)
        _, unit, inverse = norm_parts(hidden[i], norms[1:2], norms[3:4], None)
        grad_in, scale_grad, bias_grad = norm_back(grad, unit, inverse, norms[1:2])
        value = cotangent[i].astype(F32) + grad_in
        grad_hidden[i] = value
        rounded[i] = value.astype(BF16)
        sums.append((scale_grad, bias_grad))
    scale_2, bias_2 = sums[0][0] + sums[1][0], sums[0][1] + sums[1][1]
    flat_rounded = rounded[...].reshape(flat)
    loads[3].wait()
    grad_context[...] = dot(flat_rounded, w[3]).astype(BF16).reshape(n, rows, width)
    later_loads[0].wait()
    grads[3] = dot_r(flat_rounded, context[...].reshape(flat)).astype(BF16)
    stores = [pltpu.make_async_copy(grads.at[k], grads_out.at[k], g_sem.at[k]) for k in range(4)]
    stores[3].start()
    for load in later_loads[1:4]:
        load.wait()
    factor = HEAD_DIM ** (-0.5)
    pairs = width // 128
    lane = row_of((rows, 128), 1)
    key_lane = row_of((keys, 128), 1)
    shown = row_of((keys, rows), 0) < length

    def attend(step, carry):
        i = step // pairs
        lanes = pl.ds(pl.multiple_of((step % pairs) * 128, 128), 128)
        q, k, v = query[i, :, lanes], keyed[i, :, lanes], valued[i, :, lanes]
        scaled = q * jnp.bfloat16(factor)
        g = grad_context[i, :, lanes]
        to_q, to_k, to_v = [], [], []
        for a in range(2):
            mine = (lane < 64) if a == 0 else (lane >= 64)
            scores = dot_t(k, jnp.where(mine, scaled, jnp.zeros_like(q)))
            grad_probs = dot_t(v, jnp.where(mine, g, jnp.zeros_like(g)))
            scores = jnp.where(shown, scores, -1e30)
            exponent = jnp.exp(scores - jnp.max(scores, axis=0, keepdims=True))
            probs = exponent * (1.0 / jnp.sum(exponent, axis=0, keepdims=True))
            weighted = jnp.sum(probs * grad_probs, axis=0, keepdims=True)
            grad_scores = (probs * (grad_probs - weighted)).astype(BF16)
            to_v.append(dot(probs.astype(BF16), g))
            to_q.append(dot_r(grad_scores, k))
            to_k.append(dot(grad_scores, q))
        grad_q[i, :, lanes] = (jnp.where(lane < 64, to_q[0], to_q[1]) * factor).astype(BF16)
        kept = key_lane < 64
        grad_k[i, :, lanes] = (jnp.where(kept, to_k[0], to_k[1]) * factor)[:rows].astype(BF16)
        grad_v[i, :, lanes] = jnp.where(kept, to_v[0], to_v[1])[:rows].astype(BF16)
        return carry

    lax.fori_loop(0, n * pairs, attend, 0, unroll=6)
    for load in later_loads[4:6]:
        load.wait()
    total = jnp.zeros(flat, F32)
    turned = jnp.swapaxes(normed_1[...].reshape(flat).astype(F32), 0, 1).astype(BF16)
    for k, source in enumerate((grad_q, grad_k, grad_v)):
        loads[k].wait()
        value = source[...].reshape(flat)
        total = total + dot_t(value, w[k])
        grads[k] = dot(turned, value).astype(BF16)
        stores[k].start()
    total = total.reshape(n, rows, width)
    sums = []
    for i in range(n):
        _, unit, inverse = norm_parts(tokens[i].astype(F32), norms[0:1], norms[2:3], None)
        grad_in, scale_grad, bias_grad = norm_back(total[i], unit, inverse, norms[0:1])
        input_grad[i] = (grad_hidden[i] + grad_in).astype(BF16)
        sums.append((scale_grad, bias_grad))
    scale_1, bias_1 = sums[0][0] + sums[1][0], sums[0][1] + sums[1][1]
    line = row_of((128, width), 0)
    spread = jnp.zeros((128, width), F32)
    for j, value in enumerate((scale_1, scale_2, bias_1, bias_2)):
        spread = jnp.where(line == 64 + j, value, spread)
    small_grads[...] = jnp.swapaxes(spread, 0, 1).astype(BF16)
    small_grads[:, :64] = phi_grad.astype(BF16)
    for store in stores:
        store.wait()


def tokens_behind(sizes, length, back, small, weights, later, dispatch, grad_logits):
    tokens = later[5]
    n, rows, width = tokens.shape
    vmem, hbm = pl.BlockSpec(memory_space=pltpu.VMEM), pl.BlockSpec(memory_space=pl.ANY)
    shape = jax.ShapeDtypeStruct
    low = pltpu.VMEM(tokens.shape, BF16)
    return pl.pallas_call(
        partial(behind_kernel, sizes, length),
        out_shape=(
            shape((4, width, width), BF16), shape((width, 128), BF16), shape(tokens.shape, BF16)
        ),
        in_specs=[vmem, vmem] + [hbm] * 10 + [vmem] * 2,
        out_specs=(hbm, vmem, vmem),
        scratch_shapes=[
            pltpu.VMEM(weights.shape, BF16),
            pltpu.VMEM((2, 128, 256), F32),
            pltpu.VMEM(tokens.shape, F32),
            low, low, low, low, low,
            pltpu.VMEM((4, width, width), BF16),
            *[pltpu.VMEM(value.shape, value.dtype) for value in later],
            pltpu.SemaphoreType.DMA((4,)), pltpu.SemaphoreType.DMA((9,)),
            pltpu.SemaphoreType.DMA((4,)),
        ],
        compiler_params=pltpu.CompilerParams(vmem_limit_bytes=VMEM_BYTES),
        name="tokens_behind",
    )(back, small, weights, *later, dispatch, grad_logits)


def unpack_kernel(summed, in_bias_sum, out_sum, attn, phi_t, scales, biases, in_bias, out_bias):
    attn[...] = summed[:, :, : attn.shape[2]]
    turned = jnp.swapaxes(summed[0][:, 128:], 0, 1)
    phi_t[...] = turned[64:80]
    scales[...] = turned[80:82]
    biases[...] = turned[82:84]
    in_bias[...] = in_bias_sum[...]
    width = out_bias.shape[1]
    value = out_sum[...]
    later = pltpu.roll(value, value.shape[1] - width, 1)
    out_bias[...] = jnp.where(lax.axis_index("tensor") == 0, value[:, :width], later[:, :width])


def order_kernel(mine, below, above, below_2, above_2, far, out):
    h = lax.axis_index("heads")
    own, rows, width = mine.shape
    group = out.shape[1]
    first_h, low = h == 0, h < 2
    inner = (h == 1) | (h == 2)
    origins = (
        h,
        jnp.where(first_h, h + 1, h - 1),
        jnp.where(low, h + 2, h - 2),
        jnp.where(inner, h + 1, 3 - h),
    )
    step = 256 // group
    length = out.shape[0]
    for first in range(0, length, step):
        count = min(step, length - first)
        taken = min(step, rows - first)
        shape = (count * group, own * taken)
        row = lax.broadcasted_iota(jnp.int32, shape, 0)
        column = lax.broadcasted_iota(jnp.int32, shape, 1)
        there = row // group == column % taken
        image = row % group - column // taken
        chosen = [(there & (image == origin * own)).astype(F32) for origin in origins]

        def lines(part):
            return [part[i, first : first + taken] for i in range(own)]

        def either(condition, one, other):
            return [jnp.where(condition, a, b) for a, b in zip(lines(one), lines(other))]

        values = lines(mine) + either(first_h, above, below)
        values += either(low, above_2, below_2) + either(inner, above, far)
        value = dot(
            jnp.concatenate(chosen, axis=1).astype(BF16), jnp.concatenate(values, axis=0)
        ).astype(BF16)
        out[first : first + count] = value.reshape(count, group, width)


def last_kernel(summed, in_bias_sum, out_sum, *refs):
    unpack_kernel(summed, in_bias_sum, out_sum, *refs[6:12])
    order_kernel(*refs[:6], refs[12])


def last_results(summed, in_bias_sum, out_sum, parts, block, slot, group, length):
    n_k, rows, _ = summed.shape
    vmem = pl.BlockSpec(memory_space=pltpu.VMEM)
    shape = jax.ShapeDtypeStruct
    return pl.pallas_call(
        last_kernel,
        out_shape=(
            shape((n_k, rows, block), F32), shape((slot, rows), F32),
            shape((2, rows), F32), shape((2, rows), F32),
            shape(in_bias_sum.shape, F32), shape((out_sum.shape[0], rows), F32),
            shape((length, group, parts[0].shape[2]), BF16),
        ),
        in_specs=[vmem] * 9,
        out_specs=(vmem,) * 7,
        compiler_params=pltpu.CompilerParams(vmem_limit_bytes=24 * 1024 * 1024),
        name="last_results",
    )(summed, in_bias_sum, out_sum, *parts)


def normalize(values, scale, shift):
    centered = values - jnp.mean(values, axis=-1, keepdims=True)
    variance = jnp.mean(centered * centered, axis=-1, keepdims=True)
    inverse = lax.rsqrt(variance + epsilon)
    unit_part = centered * inverse
    return (unit_part * scale + shift, unit_part, inverse)


def normalize_back(grad_output, unit_part, inverse, scale):
    scaled = grad_output * scale
    average = jnp.mean(scaled, axis=-1, keepdims=True)
    projection = jnp.mean(scaled * unit_part, axis=-1, keepdims=True)
    grad_input = inverse * (scaled - average - unit_part * projection)
    return (
        grad_input,
        jnp.sum(grad_output * unit_part, axis=(0, 1)),
        jnp.sum(grad_output, axis=(0, 1)),
    )


def to_experts(slots):
    slots = lax.all_to_all(slots, "heads", split_axis=1, concat_axis=0, tiled=True)
    slots = lax.all_to_all(slots, "shard", split_axis=2, concat_axis=0, tiled=True)
    return lax.all_gather(slots, "tensor", axis=0, tiled=True)


def to_images(slots):
    slots = lax.psum_scatter(slots, "tensor", scatter_dimension=0, tiled=True)
    slots = lax.all_to_all(slots, "shard", split_axis=0, concat_axis=2, tiled=True)
    return lax.all_to_all(slots, "heads", split_axis=0, concat_axis=1, tiled=True)


def general_shards(tokens, norm_scales, norm_biases, w_attn, phi, experts, in_bias, out_bias, cotangent):
    heads_n = lax.axis_size("heads")
    group, seq_len, width = tokens.shape
    own = group // heads_n
    heads_index = lax.axis_index("heads")
    tensor_index = lax.axis_index("tensor")
    shard_index = lax.axis_index("shard")
    hidden = experts.shape[3]
    rows = experts.shape[0]
    scales, biases, in_full = (
        lax.all_gather(norm_scales, ROWS, axis=1, tiled=True).astype(F32),
        lax.all_gather(norm_biases, ROWS, axis=1, tiled=True).astype(F32),
        lax.all_gather(in_bias, ROWS, axis=1, tiled=True).astype(F32),
    )
    attn = lax.all_gather(
        lax.all_gather(w_attn, "heads", axis=2, tiled=True), ROWS, axis=1, tiled=True
    )
    phi_full = lax.all_gather(
        lax.all_gather(phi, "heads", axis=1, tiled=True), ROWS, axis=0, tiled=True
    )
    out_rows = lax.all_gather(out_bias, "tensor", axis=1, tiled=True).astype(F32)
    e_own = experts.shape[2] // lax.axis_size("shard")
    in_local = lax.dynamic_slice_in_dim(in_full, tensor_index * hidden, hidden, 1)
    factor = HEAD_DIM ** (-0.5)
    tokens = lax.dynamic_slice_in_dim(tokens, heads_index * own, own, 0)
    cotangent = lax.dynamic_slice_in_dim(cotangent, heads_index * own, own, 0)
    n_heads = width // HEAD_DIM
    inputs = tokens.astype(F32)
    normed_one, unit_one, inverse_one = normalize(inputs, scales[0], biases[0])
    normed_one_b = normed_one.astype(BF16)
    projected = einsum("nsd,kdc->knsc", normed_one_b, attn[:3]).astype(BF16)
    query, keyed, valued = projected.reshape(3, own, seq_len, n_heads, HEAD_DIM)
    scores = einsum("nqhe,nkhe->nhqk", query, keyed) * factor
    score_peak = jnp.max(scores, axis=-1, keepdims=True)
    exponent = jnp.exp(scores - score_peak)
    probs = exponent / jnp.sum(exponent, axis=-1, keepdims=True)
    probs_b = probs.astype(BF16)
    context_b = (
        einsum("nhqk,nkhe->nqhe", probs_b, valued).astype(BF16).reshape(own, seq_len, width)
    )
    hidden_one = inputs + einsum("nsc,dc->nsd", context_b, attn[3])
    normed_two, unit_two, inverse_two = normalize(hidden_one, scales[1], biases[1])
    normed_two_b = normed_two.astype(BF16)
    logits = einsum("nsd,de->nse", normed_two_b, phi_full)
    dispatch = jax.nn.softmax(logits, axis=1)
    dispatch_b = dispatch.astype(BF16)
    combine = jax.nn.softmax(logits, axis=2)
    combine_b = combine.astype(BF16)
    slot_in = to_experts(einsum("nse,nsd->ned", dispatch_b, normed_two_b).astype(BF16))
    share = 1 if e_own else 0

    def meet(partial_sum):
        return lax.psum_scatter(partial_sum, "shard", scatter_dimension=share, tiled=True)

    def spread(values):
        return lax.all_gather(values, "shard", axis=share, tiled=True)

    pre = meet(einsum("ned,def->nef", slot_in, experts[:, 0]))
    if e_own:
        pre = pre + lax.dynamic_slice_in_dim(in_local, shard_index * e_own, e_own, 0)
    else:
        pre = pre + in_local
    gelu_value, gelu_back = jax.vjp(partial(jax.nn.gelu, approximate=False), pre)
    activated = spread(gelu_value.astype(BF16))
    slot_out_part = einsum("nef,def->ned", activated, experts[:, 1])
    slot_out_part = slot_out_part + jnp.where(tensor_index == 0, out_rows, 0.0)
    slot_out = to_images(slot_out_part).astype(BF16)
    output = (hidden_one + einsum("nse,ned->nsd", combine_b, slot_out)).astype(BF16)
    output = lax.all_gather(output, "heads", axis=0, tiled=True)
    grad_combine = einsum("nsd,ned->nse", cotangent, slot_out)
    grad_slot = to_experts(einsum("nse,nsd->ned", combine_b, cotangent).astype(BF16))
    grad_act = meet(einsum("ned,def->nef", grad_slot, experts[:, 1]))
    grad_pre = spread(gelu_back(grad_act)[0].astype(BF16))
    grad_slot_in = einsum("nef,def->ned", grad_pre, experts[:, 0]).astype(BF16)
    input_term = einsum("ned,nef->def", slot_in, grad_pre)
    output_term = einsum("ned,nef->def", grad_slot, activated)
    experts_grad = jnp.stack((input_term, output_term), axis=1)
    grad_slot_in = to_images(grad_slot_in.astype(F32)).astype(BF16)
    in_bias_grad = lax.dynamic_slice_in_dim(
        lax.all_gather(jnp.sum(grad_pre.astype(F32), axis=0), "tensor", axis=1, tiled=True),
        (shard_index * lax.axis_size("tensor") + tensor_index) * in_bias.shape[1],
        in_bias.shape[1],
        1,
    )
    out_bias_grad = lax.dynamic_slice_in_dim(
        jnp.sum(grad_slot.astype(F32), axis=0),
        tensor_index * out_bias.shape[1],
        out_bias.shape[1],
        1,
    )
    grad_dispatch = einsum("nsd,ned->nse", normed_two_b, grad_slot_in)
    grad_logits = (
        dispatch * (grad_dispatch - jnp.sum(dispatch * grad_dispatch, axis=1, keepdims=True))
        + combine * (grad_combine - jnp.sum(combine * grad_combine, axis=2, keepdims=True))
    ).astype(BF16)
    phi_grad = einsum("nsd,nse->de", normed_two_b, grad_logits)
    grad_normed_two = einsum("nse,ned->nsd", dispatch_b, grad_slot_in) + einsum(
        "nse,de->nsd", grad_logits, phi_full
    )
    grad_hidden_norm, scale_two_grad, bias_two_grad = normalize_back(
        grad_normed_two, unit_two, inverse_two, scales[1]
    )
    grad_hidden = cotangent.astype(F32) + grad_hidden_norm
    grad_hidden_b = grad_hidden.astype(BF16)
    out_weight_grad = einsum("nsd,nsc->dc", grad_hidden_b, context_b)
    grad_context = einsum("nsd,dc->nsc", grad_hidden_b, attn[3]).astype(BF16)
    grad_context = grad_context.reshape(own, seq_len, n_heads, HEAD_DIM)
    grad_value = einsum("nhqk,nqhe->nkhe", probs_b, grad_context).astype(BF16)
    grad_probs = einsum("nqhe,nkhe->nhqk", grad_context, valued)
    grad_scores = (
        probs * (grad_probs - jnp.sum(probs * grad_probs, axis=-1, keepdims=True))
    ).astype(BF16)
    grad_query = (einsum("nhqk,nkhe->nqhe", grad_scores, keyed) * factor).astype(BF16)
    grad_key = (einsum("nhqk,nqhe->nkhe", grad_scores, query) * factor).astype(BF16)
    grad_proj = jnp.stack((grad_query, grad_key, grad_value)).reshape(3, own, seq_len, width)
    proj_grad = einsum("nsd,knsc->kdc", normed_one_b, grad_proj)
    grad_normed_one = einsum("knsc,kdc->nsd", grad_proj, attn[:3])
    grad_input_norm, scale_one_grad, bias_one_grad = normalize_back(
        grad_normed_one, unit_one, inverse_one, scales[0]
    )
    input_grad = (grad_hidden + grad_input_norm).astype(BF16)
    input_grad = lax.all_gather(input_grad, "heads", axis=0, tiled=True)
    attn_grad = jnp.concatenate((proj_grad, out_weight_grad[None]), axis=0)
    attn_grad = lax.psum_scatter(attn_grad, ROWS, scatter_dimension=1, tiled=True)
    attn_grad = lax.psum_scatter(attn_grad, "heads", scatter_dimension=2, tiled=True)
    phi_grad = lax.psum_scatter(phi_grad, ROWS, scatter_dimension=0, tiled=True)
    phi_grad = lax.psum_scatter(phi_grad, "heads", scatter_dimension=1, tiled=True)
    norms = jnp.stack((scale_one_grad, scale_two_grad, bias_one_grad, bias_two_grad))
    norms = lax.psum(lax.psum_scatter(norms, ROWS, scatter_dimension=1, tiled=True), "heads")
    return (
        output,
        input_grad,
        norms[:2],
        norms[2:],
        attn_grad,
        phi_grad,
        experts_grad,
        in_bias_grad,
        out_bias_grad,
    )


def shards(tokens, norm_scales, norm_biases, w_attn, phi, experts, in_bias, out_bias, cotangent):
    arrays = (tokens, norm_scales, norm_biases, w_attn, phi, experts, in_bias, out_bias, cotangent)
    sizes = tuple(lax.axis_size(name) for name in ("shard", "heads", "tensor"))
    group, length, width = tokens.shape
    fits = (sizes, group, width, *experts.shape[:3]) == ((4, 4, 2), 8, 768, 192, 2, 16)
    if not fits or not 192 < length <= 208 or in_bias.shape[1] != 384:
        return general_shards(*arrays)
    n_s, n_h, n_t = sizes
    block, slot = w_attn.shape[2], phi.shape[1]
    tokens, cotangent = (
        values.transpose(1, 0, 2).reshape(group * length, width) for values in (tokens, cotangent)
    )
    attn, small, turned, tokens, cotangent, blocks, dispatch, combine, *held = gather_weights(
        sizes, length, w_attn, phi.T, out_bias, norm_scales, norm_biases, in_bias, experts, tokens,
        cotangent,
    )
    normed_1, query, keyed, valued, context, hidden, normed_2 = held
    slot_in, activated, grad_slot, grad_pre, back, in_bias_grad, out_sum, grad_logits, output = (
        experts_pass(
            sizes, blocks, turned, small, combine, hidden, cotangent, in_bias.shape[1]
        )
    )
    attn_grad, small_grad, input_grad = tokens_behind(
        sizes, length, back, small, attn,
        (context, query, keyed, valued, normed_1, tokens, hidden, normed_2, cotangent),
        dispatch, grad_logits,
    )
    def along(values, places):
        return lax.ppermute(values, "heads", places)

    up = [(i, i + 1) for i in range(n_h - 1)]
    down = [(i + 1, i) for i in range(n_h - 1)]
    below, above = along(input_grad, up), along(input_grad, down)
    attn_grad, grad_pre = lax.optimization_barrier((attn_grad, grad_pre))
    experts_grad = weight_grads(slot_in, grad_pre, grad_slot, activated)
    output = output[:, :length].transpose(1, 0, 2)
    attn_grad, experts_grad, output, input_grad, below, above = lax.optimization_barrier(
        (attn_grad, experts_grad, output, input_grad, below, above)
    )
    parts = [
        input_grad, below, above, along(below, up[1:]), along(above, down[:-1]),
        along(input_grad, [(0, n_h - 1), (n_h - 1, 0)]),
    ]
    summed = reduce_grads(sizes, attn_grad, small_grad)
    attn_grad, phi_grad, scales_grad, biases_grad, in_bias_grad, out_bias_grad, input_grad = (
        last_results(summed, in_bias_grad, out_sum, parts, block, slot, group, length)
    )
    return (
        output.transpose(1, 0, 2),
        input_grad.transpose(1, 0, 2),
        scales_grad,
        biases_grad,
        attn_grad,
        phi_grad.T,
        experts_grad,
        in_bias_grad,
        out_bias_grad,
    )


def solution(mesh):
    images = P(ROWS, None, None)
    return jax.shard_map(
        shards,
        mesh=mesh,
        in_specs=(
            images,
            P(None, ROWS),
            P(None, ROWS),
            P(None, ROWS, "heads"),
            P(ROWS, "heads"),
            P("shard", None, "heads", "tensor"),
            P("heads", ROWS),
            P("heads", ROWS),
            images,
        ),
        out_specs=(
            images,
            images,
            P(None, ROWS),
            P(None, ROWS),
            P(None, ROWS, "heads"),
            P(ROWS, "heads"),
            P("shard", None, "heads", "tensor"),
            P("heads", ROWS),
            P("heads", ROWS),
        ),
        check_vma=False,
    )
```

```python
from functools import partial

import jax
import jax.numpy as jnp
from jax import lax
from jax.experimental import pallas as pl
from jax.experimental.pallas import tpu as pltpu
from jax.sharding import PartitionSpec as P

HEAD_DIM = 64
F32 = jnp.float32
BF16 = jnp.bfloat16
ROWS = ("shard", "tensor")
MESH = pl.DeviceIdType.MESH
VMEM_BYTES = 58 * 1024 * 1024
epsilon = 1e-06
einsum = partial(jnp.einsum, preferred_element_type=F32)


def dot(a, b):
    return lax.dot_general(a, b, (((1,), (0,)), ((), ())), preferred_element_type=F32)


def dot_t(a, b):
    return lax.dot_general(a, b, (((1,), (1,)), ((), ())), preferred_element_type=F32)


def swap_matrix(n):
    out = lax.broadcasted_iota(jnp.int32, (n * n, n * n), 0)
    row = lax.broadcasted_iota(jnp.int32, (n * n, n * n), 1)
    return ((out // n == row % n) & (out % n == row // n)).astype(F32).astype(BF16)


class Peers:
    def __init__(self, sizes):
        self.sizes = sizes
        self.at = tuple(lax.axis_index(name) for name in ("shard", "heads", "tensor"))
        self.count = sizes[0] * sizes[1] * sizes[2]

    def flat(self, place):
        return (place[0] * self.sizes[1] + place[1]) * self.sizes[2] + place[2]

    def step(self, k, sign):
        _, n_h, n_t = self.sizes
        steps = (k // (n_h * n_t), (k // n_t) % n_h, k % n_t)
        return tuple(
            lax.rem(at + n + sign * d, n) for at, n, d in zip(self.at, self.sizes, steps)
        )

    def greet_all(self):
        barrier = pltpu.get_barrier_semaphore()

        def signal(k, carry):
            pl.semaphore_signal(barrier, inc=1, device_id=self.step(k, 1), device_id_type=MESH)
            return carry

        lax.fori_loop(1, self.count, signal, 0)
        pl.semaphore_wait(barrier, self.count - 1)


def remote(src, dst, send, recv, place):
    return pltpu.make_async_remote_copy(
        src_ref=src, dst_ref=dst, send_sem=send, recv_sem=recv, device_id=place, device_id_type=MESH
    )


def plane(sizes):
    n_s, n_h, n_t = sizes
    s, h, t = (lax.axis_index(name) for name in ("shard", "heads", "tensor"))
    core, chip = lax.rem(s, 2), s // 2
    sibling = (s + 1 - 2 * core, h, t)
    across_x = (lax.rem(s + 2, n_s), h, t)
    across_y = (s, h, 1 - t)
    line = [(s, lax.rem(h + d, n_h), t) for d in range(n_h)]
    barrier = pltpu.get_barrier_semaphore()
    others = [sibling, across_x, across_y] + line[1:]
    for place in others:
        pl.semaphore_signal(barrier, inc=1, device_id=place, device_id_type=MESH)
    pl.semaphore_wait(barrier, len(others))
    return (s, h, t), core, chip, sibling, across_x, across_y, line


def pair_matrix(block, wide, transposed):
    shape = (2 * block, 2 * wide) if transposed else (2 * wide, 2 * block)
    tight = lax.broadcasted_iota(jnp.int32, shape, 0 if transposed else 1)
    padded = lax.broadcasted_iota(jnp.int32, shape, 1 if transposed else 0)
    second = padded >= wide
    lane = jnp.where(second, padded - wide, padded)
    same = (lane < block) & (tight == jnp.where(second, lane + block, lane))
    return same.astype(F32).astype(BF16)


def gather_kernel(
    sizes, length, w_attn, phi_t, out_bias, scales, biases, in_bias, experts, tokens, cotangent,
    w_out, small_out, turned, own_tokens, own_cot, blocks, dispatch, combine, *refs,
):
    held_out, refs = refs[:7], refs[7:]
    held, refs = refs[:7], refs[7:]
    (joined, order, w, small, lined, extra, stage, tile_in, tile_out, images, picked,
     z_send, z_recv, x_sems, y_sems, d_sems, c_sems, t_sems, o_sems, i_sems, h_sems) = refs
    n_k, rows, block = w_attn.shape
    wide = lined.shape[3]
    slot = phi_t.shape[0]
    own_h = lax.axis_index("heads")
    stage[...] = jnp.zeros_like(stage)
    stage[64 : 64 + slot] = phi_t[...].astype(F32)
    stage[64 + slot : 64 + 2 * slot] = out_bias[...].astype(F32)
    lined[own_h, :, :, 128:] = jnp.zeros((n_k, rows, wide - 128), BF16)
    lined[own_h, :, :, :block] = w_attn[...]
    first = lined[own_h, 0, :, 128:].astype(F32) + jnp.swapaxes(stage[...], 0, 1)
    lined[own_h, 0, :, 128:] = first.astype(BF16)
    (s, h, t), core, chip, sibling, across_x, across_y, line = plane(sizes)
    n_h, n_t = sizes[1], sizes[2]
    width = w.shape[2]
    side = 16
    n_tiles = experts.shape[0] // side
    depth = tile_in.shape[0]
    halves = ((0, rows // 2), (rows // 2, rows // 2))

    def z_hop(k, origin, up):
        place = line[1] if up else line[n_h - 1]
        return remote(
            lined.at[origin, k], lined.at[origin, k],
            z_send.at[k, origin, up], z_recv.at[k, origin], place,
        )

    def relay(k, d):
        @pl.when(h >= d)
        def _():
            z_hop(k, h - d, 1).wait_recv()

            @pl.when(h < n_h - 1)
            def _():
                z_hop(k, h - d, 1).start()

        @pl.when(h + d < n_h)
        def _():
            z_hop(k, h + d, 0).wait_recv()

            @pl.when(h > 0)
            def _():
                z_hop(k, h + d, 0).start()

    chunks = (0, 2, 1, 3)
    for k in chunks:
        @pl.when(h < n_h - 1)
        def _():
            z_hop(k, h, 1).start()

        @pl.when(h > 0)
        def _():
            z_hop(k, h, 0).start()

    def load(i):
        return pltpu.make_async_copy(
            experts.at[pl.ds((i % n_tiles) * side, side), i // n_tiles],
            tile_in.at[i % depth],
            t_sems.at[0, i % depth],
        )

    def store(i):
        return pltpu.make_async_copy(
            tile_out.at[i % depth],
            turned.at[i // n_tiles, :, pl.ds((i % n_tiles) * side, side)],
            t_sems.at[1, i % depth],
        )

    image_loads = [
        pltpu.make_async_copy(source, images.at[j], i_sems.at[0, j])
        for j, source in enumerate((tokens, cotangent))
    ]
    for i in range(depth - 1):
        load(i).start()
    for copy in image_loads:
        copy.start()
    swap = swap_matrix(side)
    done = [0]

    def turn(count):
        def step(i, carry):
            load(i).wait()

            @pl.when(i + depth - 1 < 2 * n_tiles)
            def _():
                load(i + depth - 1).start()

            @pl.when(i >= depth)
            def _():
                store(i - depth).wait()

            rows_in = tile_in[i % depth].reshape(side * side, tile_in.shape[3])
            tile_out[i % depth] = dot(swap, rows_in).astype(BF16).reshape(tile_out.shape[1:])
            store(i).start()
            return carry

        last = min(done[0] + count, 2 * n_tiles)
        lax.fori_loop(done[0], last, step, 0)
        done[0] = last

    pair = pair_matrix(block, wide, False)
    shape = (n_h * wide, small.shape[1])
    row = lax.broadcasted_iota(jnp.int32, shape, 0)
    column = lax.broadcasted_iota(jnp.int32, shape, 1)
    lane, of = row % wide - block, row // wide
    beside = (lane >= 0) & (lane < 16) & (column == of * 16 + lane)
    beside |= (lane >= 16) & (lane < 32) & (column == n_h * 16 + of * 16 + lane - 16)
    beside = beside.astype(F32).astype(BF16)

    stage[...] = jnp.zeros_like(stage)
    stage[64:66] = scales[...].astype(F32)
    stage[66:68] = biases[...].astype(F32)
    norms = jnp.swapaxes(stage[...], 0, 1)
    pieces = []
    for j in range(in_bias.shape[1] // 64):
        shape = (in_bias.shape[1], 128)
        row = lax.broadcasted_iota(jnp.int32, shape, 0)
        column = lax.broadcasted_iota(jnp.int32, shape, 1)
        chosen = ((row == 64 * j + column) & (column < 64)).astype(F32).astype(BF16)
        pieces.append(dot(in_bias[...], chosen))
    extra[:, :128] = jnp.zeros((rows, 128), F32)
    extra[:, 128:] = jnp.concatenate(pieces, axis=0) + norms

    image_stores = [
        pltpu.make_async_copy(picked.at[j], target, i_sems.at[1, j])
        for j, target in enumerate((own_tokens, own_cot))
    ]

    def pick_images(j):
        own, padded = picked.shape[1:3]
        group = own * n_h
        lines = images.shape[1]
        image_loads[j].wait()
        step = 256 // group
        for first in range(0, padded, step):
            count = min(step, padded - first)
            taken = min(step * group, lines - first * group)
            shape = (own * count, taken)
            row = lax.broadcasted_iota(jnp.int32, shape, 0)
            column = lax.broadcasted_iota(jnp.int32, shape, 1)
            wanted = (row % count) * group + own * h + row // count
            chosen = (column == wanted).astype(F32).astype(BF16)
            source = images[j, first * group : first * group + taken]
            picked[j, :, first : first + count] = (
                dot(chosen, source).astype(BF16).reshape(own, count, images.shape[2])
            )
        image_stores[j].start()

    def at(k, place):
        first = pl.multiple_of((place[0] * n_t + place[2]) * rows, 16)
        lines = pl.ds(first, rows)
        return small.at[lines] if k == n_k else w.at[k, lines]

    def hop(q, origin, place, sems, j):
        return remote(at(q, origin), at(q, origin), sems.at[0, j], sems.at[1, j], place)

    def half_hop(q, origin, place, half):
        part = at(q, origin).at[pl.ds(*halves[half])]
        j = 2 * q + half
        return remote(part, part, d_sems.at[0, j], d_sems.at[1, j], place)

    me = (s, h, t)
    from_d = (across_x[0], h, across_y[2])
    sent = []

    def send(copy):
        copy.start()
        sent.append(copy)

    def assemble(k):
        for i in range(0, n_h, 2):
            lines = jnp.concatenate([lined[i, k], lined[i + 1, k]], axis=1)
            at(k, me)[:, i * block : (i + 2) * block] = dot(lines, pair).astype(BF16)
        if k == 0:
            lines = jnp.concatenate([lined[i, k] for i in range(n_h)], axis=1)
            at(n_k, me)[...] = (dot(lines, beside) + extra[...]).astype(BF16)
        for q in members(k):
            send(hop(q, me, across_x, x_sems, q))
            send(hop(q, me, across_y, y_sems, q))
            send(hop(q, me, sibling, c_sems, 4 * q))

    def members(k):
        return (0, n_k) if k == 0 else (k,)

    def relay_xy(k):
        for q in members(k):
            hop(q, across_x, across_x, x_sems, q).wait_recv()
            send(half_hop(q, across_x, across_y, 0))
            send(hop(q, across_x, sibling, c_sems, 4 * q + 1))
            hop(q, across_y, across_y, y_sems, q).wait_recv()
            send(half_hop(q, across_y, across_x, 1))
            send(hop(q, across_y, sibling, c_sems, 4 * q + 2))

    def relay_d(k):
        for q in members(k):
            half_hop(q, from_d, across_y, 0).wait_recv()
            half_hop(q, from_d, across_x, 1).wait_recv()
            send(hop(q, from_d, sibling, c_sems, 4 * q + 3))

    for wave in range(n_k + n_h - 2):
        for d in range(1, n_h):
            if 0 <= wave - d + 1 < n_k:
                relay(chunks[wave - d + 1], d)
        turn(2)
        i = wave - n_h + 2
        if i >= 0:
            assemble(chunks[i])
            if i in (1, 2):
                pick_images(i - 1)
            if i >= 1:
                relay_xy(chunks[i - 1])
            if i >= 2:
                relay_d(chunks[i - 2])
            turn(2)
    stores = []

    def arrive(q):
        for j in range(4):
            hop(q, me, sibling, c_sems, 4 * q + j).wait_recv()
        if q == n_k:
            stores.append(pltpu.make_async_copy(small, small_out, o_sems.at[q]))
        else:
            stores.append(pltpu.make_async_copy(w.at[q], w_out.at[q], o_sems.at[q]))
        stores[-1].start()

    def keep(first, last):
        for j in range(first, last):
            stores.append(pltpu.make_async_copy(held[j], held_out[j], h_sems.at[j]))
            stores[-1].start()

    ahead = Ahead(
        length, picked.at[0], small, w, blocks, dispatch, combine, held, joined, order
    )
    arrive(n_k)
    ahead.first_norm()
    relay_xy(chunks[-1])
    relay_d(chunks[-2])
    arrive(0)
    ahead.project(0)
    turn(2 * n_tiles)
    arrive(2)
    ahead.project(2)
    arrive(1)
    ahead.project(1)
    relay_d(chunks[-1])
    keep(0, 4)
    ahead.attend()
    arrive(3)
    ahead.finish()
    keep(4, 7)
    for copy in sent:
        copy.wait_send()
    for origin in range(n_h):
        @pl.when((origin <= h) & (h < n_h - 1))
        def _():
            for k in range(n_k):
                z_hop(k, origin, 1).wait_send()

        @pl.when((origin >= h) & (h > 0))
        def _():
            for k in range(n_k):
                z_hop(k, origin, 0).wait_send()

    for i in range(depth):
        store(2 * n_tiles - depth + i).wait()
    for copy in image_stores:
        copy.wait()
    for copy in stores:
        copy.wait()


def gather_weights(
    sizes, length, w_attn, phi_t, out_bias, scales, biases, in_bias, experts, tokens, cotangent
):
    n_k, rows, _ = w_attn.shape
    wide = 256
    n_s, n_h, n_t = sizes
    width = n_s * n_t * rows
    vmem = pl.BlockSpec(memory_space=pltpu.VMEM)
    hbm = pl.BlockSpec(memory_space=pl.ANY)
    dma = pltpu.SemaphoreType.DMA
    hidden = experts.shape[3]
    small = (width, wide)
    images = jax.ShapeDtypeStruct((2, 208, width), BF16)
    shape = jax.ShapeDtypeStruct
    keys = shape((2, 256, width), BF16)
    thin = shape((2, 208, 128), F32)
    held = (images, images, keys, keys, images, shape(images.shape, F32), images)
    return pl.pallas_call(
        partial(gather_kernel, sizes, length),
        out_shape=(
            jax.ShapeDtypeStruct((n_k, width, width), BF16),
            jax.ShapeDtypeStruct(small, BF16),
            jax.ShapeDtypeStruct((2, experts.shape[2], experts.shape[0], hidden), BF16),
            images, images, shape((n_h, n_s, 2, 16, width // n_s), BF16), thin, thin, *held,
        ),
        in_specs=[vmem] * 6 + [hbm] * 3,
        out_specs=(hbm,) * 5 + (vmem,) * 3 + (hbm,) * 7,
        scratch_shapes=[
            *[pltpu.VMEM(value.shape, value.dtype) for value in held],
            pltpu.VMEM((2 * width // n_s, 512), BF16),
            pltpu.VMEM((128, 128), BF16),
            pltpu.VMEM((n_k, width, width), BF16),
            pltpu.VMEM(small, BF16),
            pltpu.VMEM((n_h, n_k, rows, wide), BF16),
            pltpu.VMEM((rows, wide), F32),
            pltpu.VMEM((128, rows), F32),
            pltpu.VMEM((4, 16, 16, hidden), BF16),
            pltpu.VMEM((4, 16, 16, hidden), BF16),
            pltpu.VMEM((2, *tokens.shape), BF16),
            pltpu.VMEM((2, *images.shape), BF16),
            dma((n_k, n_h, 2)), dma((n_k, n_h)), dma((2, n_k + 1)), dma((2, n_k + 1)),
            dma((2, 2 * (n_k + 1))), dma((2, 4 * (n_k + 1))), dma((2, 4)), dma((n_k + 1,)),
            dma((2, 2)), dma((7,)),
        ],
        compiler_params=pltpu.CompilerParams(
            collective_id=3, has_side_effects=True, vmem_limit_bytes=VMEM_BYTES
        ),
        name="gather_weights",
    )(w_attn, phi_t, out_bias, scales, biases, in_bias, experts, tokens, cotangent)


def reduce_kernel(
    sizes, stored, small, out, grads, load_sems, core_in, core_small, met, met_small,
    d_in, d_small, x_in, x_small, y_in, y_small, pieces, z_in,
    c_sems, d_sems, x_sems, y_sems, z_send, z_recv,
):
    loads = [
        pltpu.make_async_copy(stored.at[k], grads.at[k], load_sems.at[k]) for k in range(4)
    ]
    for k in (0, 2, 1, 3):
        loads[k].start()
    (s, h, t), core, chip, sibling, across_x, across_y, line = plane(sizes)
    n_k, width, _ = grads.shape
    n_s, n_h, n_t = sizes
    rows = width // (n_s * n_t)
    wide = pieces.shape[3]
    pair = n_t * rows
    half = rows // 2
    halves = (pl.ds(0, half), pl.ds(half, half))
    chunks = (0, 2, 1, 3)

    def members(k):
        return (0, n_k) if k == 0 else (k,)

    def pick(q, large, little):
        return little if q == n_k else large.at[q]

    def core_copy(q, x):
        first = pl.multiple_of((2 * x + 1 - core) * pair, 16)
        return remote(
            pick(q, stored, small).at[pl.ds(first, pair)],
            pick(q, core_in, core_small).at[x],
            c_sems.at[0, 2 * q + x], c_sems.at[1, 2 * q + x], sibling,
        )

    for k in chunks:
        for q in members(k):
            for x in range(2):
                core_copy(q, x).start()
    joined = pair_matrix(width // n_h, wide, True)
    shape = (small.shape[1], n_h * wide)
    row = lax.broadcasted_iota(jnp.int32, shape, 0)
    column = lax.broadcasted_iota(jnp.int32, shape, 1)
    lane, of = column % wide - width // n_h, column // wide
    beside = (lane >= 0) & (lane < 16) & (row == of * 16 + lane)
    beside |= (lane >= 16) & (lane < 20) & (row == n_h * 16 + lane - 16)
    beside = beside.astype(F32).astype(BF16)
    to_d, to_x, to_y = (d_in, d_small), (x_in, x_small), (y_in, y_small)
    sent = []

    def hop(q, kind, part, source, place):
        sems = {id(to_d): d_sems, id(to_x): x_sems, id(to_y): y_sems}[id(kind)]
        target = pick(q, *kind)
        target = target.at[part] if kind is to_d else target.at[halves[part]]
        j = 2 * q + part
        return remote(source, target, sems.at[0, j], sems.at[1, j], place)

    def send(copy):
        copy.start()
        sent.append(copy)

    def part_of(q, x, y, part):
        return pick(q, met, met_small).at[x, y].at[halves[part]]

    def arrived(q, kind, part):
        hop(q, kind, part, part_of(q, 0, 0, part), sibling).wait_recv()

    def open_up(q):
        part = pick(q, met, met_small)
        if q < n_k:
            loads[q].wait()
        for x in range(2):
            core_copy(q, x).wait_recv()
            first = pl.multiple_of((2 * x + core) * pair, 16)
            own = pick(q, grads, small)[pl.ds(first, pair)].astype(F32)
            total = own + pick(q, core_in, core_small)[x].astype(F32)
            part[x] = total.astype(BF16).reshape(n_t, rows, total.shape[1])
        send(hop(q, to_d, 0, part_of(q, 1 - chip, 1 - t, 0), across_x))
        send(hop(q, to_d, 1, part_of(q, 1 - chip, 1 - t, 1), across_y))
        send(hop(q, to_x, 0, part_of(q, 1 - chip, t, 0), across_x))
        send(hop(q, to_y, 1, part_of(q, chip, 1 - t, 1), across_y))

    def pass_on(q):
        for part, kind, x, y, place in (
            (0, to_y, chip, 1 - t, across_y),
            (1, to_x, 1 - chip, t, across_x),
        ):
            arrived(q, to_d, part)
            block = part_of(q, x, y, part)
            total = block[...].astype(F32) + pick(q, *to_d)[part].astype(F32)
            block[...] = total.astype(BF16)
            send(hop(q, kind, part, block, place))

    def whole(q):
        for kind in (to_x, to_y):
            for part in range(2):
                arrived(q, kind, part)
        total = pick(q, met, met_small)[chip, t].astype(F32) + pick(q, *to_x)[...].astype(F32)
        return (total + pick(q, *to_y)[...].astype(F32)).astype(BF16)

    def z_copy(k, target, up):
        place = line[1] if up else line[n_h - 1]
        return remote(
            pieces.at[target, k], z_in.at[up, target, k],
            z_send.at[up, target, k], z_recv.at[up, target, k], place,
        )

    def pass_along(k, hops):
        for up in range(2):
            for target in range(n_h - 1, -1, -1) if up else range(n_h):
                further = target > h if up else target < h

                @pl.when(further & (h == (hops if up else n_h - 1 - hops)))
                def _():
                    if hops > 0:
                        z_copy(k, target, up).wait_recv()
                        total = pieces[target, k].astype(F32) + z_in[up, target, k].astype(F32)
                        pieces[target, k] = total.astype(BF16)
                    z_copy(k, target, up).start()

    def share_out(k):
        value = whole(k)
        columns = width // n_h
        if k == 0:
            little = dot(whole(n_k), beside)
        for i in range(0, n_h, 2):
            lanes = dot(value[:, i * columns : (i + 2) * columns], joined)
            if k == 0:
                lanes = lanes + little[:, i * wide : (i + 2) * wide]
            pieces[i, k] = lanes[:, :wide].astype(BF16)
            pieces[i + 1, k] = lanes[:, wide:].astype(BF16)
        pass_along(k, 0)

    for i in range(n_k + 2 + n_h - 2):
        if i < n_k:
            for q in members(chunks[i]):
                open_up(q)
        if 0 <= i - 1 < n_k:
            for q in members(chunks[i - 1]):
                pass_on(q)
        if 0 <= i - 2 < n_k:
            share_out(chunks[i - 2])
        for hops in range(1, n_h - 1):
            if 0 <= i - 2 - hops < n_k:
                pass_along(chunks[i - 2 - hops], hops)
    for k in chunks:
        out[k] = pieces[h, k].astype(F32)
        for up, there in ((1, h > 0), (0, h < n_h - 1)):
            @pl.when(there)
            def _():
                z_copy(k, h, up).wait_recv()
                out[k] = out[k] + z_in[up, h, k].astype(F32)

    for k in chunks:
        for q in members(k):
            for x in range(2):
                core_copy(q, x).wait_send()
    for copy in sent:
        copy.wait_send()
    for target in range(n_h):
        for up in range(2):
            @pl.when(target > h if up else target < h)
            def _():
                for k in range(n_k):
                    z_copy(k, target, up).wait_send()


def reduce_grads(sizes, grads, small):
    n_k, width, _ = grads.shape
    n_s, n_h, n_t = sizes
    rows, wide, thin = width // (n_s * n_t), 256, small.shape[1]
    vmem = pl.BlockSpec(memory_space=pltpu.VMEM)
    dma = pltpu.SemaphoreType.DMA

    def buffers(*lead):
        return [
            pltpu.VMEM((n_k, *lead, width), BF16),
            pltpu.VMEM((*lead, thin), BF16),
        ]

    return pl.pallas_call(
        partial(reduce_kernel, sizes),
        out_shape=jax.ShapeDtypeStruct((n_k, rows, wide), F32),
        in_specs=[pl.BlockSpec(memory_space=pl.ANY), vmem],
        out_specs=vmem,
        scratch_shapes=[
            pltpu.VMEM(grads.shape, BF16), dma((n_k,)),
            *buffers(2, n_t * rows), *buffers(2, n_t, rows),
            *buffers(2, rows // 2), *buffers(rows), *buffers(rows),
            pltpu.VMEM((n_h, n_k, rows, wide), BF16),
            pltpu.VMEM((2, n_h, n_k, rows, wide), BF16),
            dma((2, 2 * (n_k + 1))), dma((2, 2 * (n_k + 1))), dma((2, 2 * (n_k + 1))),
            dma((2, 2 * (n_k + 1))), dma((2, n_h, n_k)), dma((2, n_h, n_k)),
        ],
        compiler_params=pltpu.CompilerParams(
            collective_id=4, has_side_effects=True, vmem_limit_bytes=VMEM_BYTES
        ),
        name="reduce_grads",
    )(grads, small)


def experts_kernel(
    sizes, blocks_0, weights, small, combine, hidden, cotangent,
    slots_0_out, act_0_out, slots_1_out, act_1_out, back_out, bias_out, sum_out, grad_logits,
    gathered,
    w_0, w_1, gate, sums, slots_both, act_both, core_out, core_both, x_out, x_both, land_both, leave,
    back, back_both, blocks_1, output, combine_v, hidden_v, cotangent_v, padded, bias, bias_all,
    bias_send, bias_land,
    w_sem, o_sem, m_sem, in_both, return_both, core_sem, x_sem, act_sem, b_sems, g_send, g_recv, g_sem,
):
    peers = Peers(sizes)
    s, h, t = peers.at
    n_s, n_h, n_t = sizes
    me = peers.flat(peers.at)
    core, chip = lax.rem(s, 2), s // 2
    sibling = (s + 1 - 2 * core, h, t)
    across = (lax.rem(s + 2, n_s), h, t)
    half = act_both.shape[1] // 2
    own, other = core * half, (1 - core) * half
    n_blocks = peers.count
    loads = [
        pltpu.make_async_copy(weights.at[0], w_0, w_sem.at[0]),
        pltpu.make_async_copy(weights.at[1], w_1, w_sem.at[1]),
    ]
    kept = [
        pltpu.make_async_copy(source, target, m_sem.at[j])
        for j, (source, target) in enumerate(
            ((combine, combine_v), (hidden, hidden_v), (cotangent, cotangent_v))
        )
    ]
    for load in loads + kept:
        load.start()
    few = half // 2
    group = 16
    many = 2 * group
    peers.greet_all()

    def each(function, count=n_blocks, start=1):
        lax.fori_loop(start, count, lambda k, carry: (function(k), carry)[1], 0)

    turns = []
    stores = []

    def run(backward):
        n = 1 if backward else 0
        blocks = blocks_1 if backward else blocks_0
        w_a, w_b = (w_1, w_0) if backward else (w_0, w_1)
        slots, act, core_in, x_in, land, land_back = (
            both.at[n] for both in (slots_both, act_both, core_both, x_both, land_both, back_both)
        )
        in_sems, back_sems, core_sems, x_sems, act_sems = (
            both.at[n] for both in (in_both, return_both, core_sem, x_sem, act_sem)
        )
        def block_out(p, k):
            place = peers.step(k, 1)
            return remote(
                blocks.at[place[1], place[0], p], land.at[p, me],
                in_sems.at[0, p, k], in_sems.at[1, p, k], place,
            )

        def block_in(p, k):
            source = peers.flat(peers.step(k, -1))
            return remote(
                blocks.at[0, 0, p], land.at[p, source], in_sems.at[0, p, k], in_sems.at[1, p, k], sibling
            )

        for p in range(2):
            for k in range(1, n_blocks):
                block_out(p, k).start()
            land[p, me] = blocks[h, s, p]
        if not turns:
            out_row = lax.broadcasted_iota(jnp.int32, (16 * group, 16 * group), 0)
            in_row = lax.broadcasted_iota(jnp.int32, (16 * group, 16 * group), 1)
            there = (out_row // many == in_row % (2 * few)) & (out_row % many == in_row // (2 * few))
            there = there.astype(F32).astype(BF16)
            again = (in_row // many == out_row % (2 * few)) & (in_row % many == out_row // (2 * few))
            again = again.astype(F32).astype(BF16)
            turns.extend((there, again))
        there, again = turns
        def receive(p):
            each(lambda k: block_in(p, k).wait_recv())
            for b in range(n_blocks // group):
                rows = land[p, b * group : (b + 1) * group].reshape(group * 16, land.shape[3])
                turned = dot(there, rows).astype(BF16).reshape(2 * few, many, land.shape[3])
                for c in range(2):
                    first = c * half + p * few
                    slots[first : first + few, b * many : (b + 1) * many, :] = turned[
                        c * few : (c + 1) * few
                    ]

        if backward:
            own_images = output.shape[0]
            line = [(s, lax.rem(h + d, n_h), t) for d in range(n_h)]
            g_own = pltpu.make_async_copy(output, gathered.at[pl.ds(h * own_images, own_images)], g_sem)
            g_own.start()

            def z_hop(i, origin, up, source=None):
                there = gathered.at[origin * own_images + i]
                return remote(
                    there if source is None else source, there,
                    g_send.at[i, origin, up], g_recv.at[i, origin], line[1] if up else line[n_h - 1],
                )

            def relay(i, d):
                @pl.when(h >= d)
                def _():
                    z_hop(i, h - d, 1).wait_recv()

                    @pl.when((h < n_h - 1) & (d < n_h - 1))
                    def _():
                        z_hop(i, h - d, 1).start()

                @pl.when(h + d < n_h)
                def _():
                    z_hop(i, h + d, 0).wait_recv()

                    @pl.when((h > 0) & (d < n_h - 1))
                    def _():
                        z_hop(i, h + d, 0).start()

            def gather_output():
                for i in range(own_images):
                    @pl.when(h < n_h - 1)
                    def _():
                        z_hop(i, h, 1, output.at[i]).start()

                    @pl.when(h > 0)
                    def _():
                        z_hop(i, h, 0, output.at[i]).start()
        else:
            piece, count = 6 * 64, act.shape[2] // (6 * 64)
            row = lax.broadcasted_iota(jnp.int32, (6 * 128, piece), 0)
            column = lax.broadcasted_iota(jnp.int32, (6 * 128, piece), 1)
            lane = row % 128
            place = (lane < 64) & (column == (row // 128) * 64 + lane)
            place = place.astype(F32).astype(BF16)
            for m in range(count):
                first = (t * count + m) * 96
                lines = [
                    small[pl.ds(pl.multiple_of(first + j * 16, 16), 16), 128:256] for j in range(6)
                ]
                bias[:, m * piece : (m + 1) * piece] = dot(jnp.concatenate(lines, axis=1), place)

        receive(0)
        if backward:
            gather_output()
        if not backward:
            loads[0].wait()

        def core_copy(j):
            return remote(
                core_out.at[j], core_in.at[j], core_sems.at[0, j], core_sems.at[1, j], sibling
            )

        def x_copy(j):
            return remote(x_out.at[j], x_in.at[j], x_sems.at[0, j], x_sems.at[1, j], across)

        def act_copy(j):
            return remote(
                act.at[own + j], act.at[own + j], act_sems.at[0, j], act_sems.at[1, j], sibling
            )

        def act_in(j):
            return remote(
                act.at[other + j], act.at[other + j], act_sems.at[0, j], act_sems.at[1, j], sibling
            )

        def meet(j):
            core_copy(j).wait_recv()
            sums[j] = sums[j] + core_in[j].astype(F32)
            x_out[j] = sums[j].astype(BF16)
            x_copy(j).start()

        def first_sums(j):
            core_out[j] = dot(slots[other + j], w_a[other + j]).astype(BF16)
            core_copy(j).start()

            @pl.when(j > 0)
            def _():
                meet(j - 1)

            sums[j] = dot(slots[own + j], w_a[own + j])

        each(first_sums, few, 0)
        receive(1)
        each(first_sums, half, few)
        meet(half - 1)
        if not backward:
            loads[1].wait()

        def second(e):
            leave[e] = dot_t(act[e], w_b[e]).astype(BF16)

        def finish(j):
            x_copy(j).wait_recv()
            value = sums[j] + x_in[j].astype(F32)
            if backward:
                act[own + j] = (value * gate[j]).astype(BF16)
            else:
                value = value + bias[pl.ds(own + j, 1), :]
                cumulative = 0.5 + 0.5 * lax.erf(value * 0.7071067811865476)
                act[own + j] = (value * cumulative).astype(BF16)
                gate[j] = cumulative + value * (
                    jnp.exp(value * value * -0.5) * 0.3989422804014327
                )
            act_copy(j).start()
            second(own + j)

            @pl.when(j > 0)
            def _():
                act_in(j - 1).wait_recv()
                second(other + j - 1)

            if backward:
                for when, i, d in ((2, 0, 1), (3, 1, 1), (5, 0, 2), (7, 1, 2)):
                    @pl.when(j == when)
                    def _():
                        relay(i, d)

        def back_copy(p, k):
            place = peers.step(k, 1)
            return remote(
                back.at[p, peers.flat(place)], land_back.at[p, me],
                back_sems.at[0, p, k], back_sems.at[1, p, k], place,
            )

        def back_in(p, k):
            source = peers.flat(peers.step(k, -1))
            return remote(
                back.at[p, 0], land_back.at[p, source],
                back_sems.at[0, p, k], back_sems.at[1, p, k], sibling,
            )

        def give_back(p):
            for b in range(n_blocks // group):
                rows = jnp.concatenate(
                    [
                        leave[c * half + p * few : c * half + (p + 1) * few, b * many : (b + 1) * many, :]
                        for c in range(2)
                    ],
                    axis=0,
                ).reshape(group * 16, leave.shape[2])
                turned = dot(again, rows).astype(BF16)
                back[p, b * group : (b + 1) * group] = turned.reshape(group, 16, leave.shape[2])
            for k in range(1, n_blocks):
                back_copy(p, k).start()
            land_back[p, me] = back[p, me]

        each(finish, few + 1, 0)
        give_back(0)
        each(finish, half, few + 1)
        act_in(half - 1).wait_recv()
        second(other + half - 1)
        give_back(1)
        outs = (slots_1_out, act_1_out) if backward else (slots_0_out, act_0_out)
        for j, (source, target) in enumerate(zip((slots, act), outs)):
            stores.append(pltpu.make_async_copy(source, target, o_sem.at[n, j]))
            stores[-1].start()
        if backward:
            across_t = (s, h, 1 - t)
            width = bias_out.shape[1]

            def bias_row(e):
                bias_all[pl.ds(e, 1), :] = jnp.sum(act[e].astype(F32), axis=0, keepdims=True)

            each(bias_row, 2 * half, 0)

            def slot_row(e):
                total = jnp.sum(slots[e].astype(F32), axis=0, keepdims=True)
                sum_out[pl.ds(e, 1), : slots.shape[2]] = total

            sum_out[...] = jnp.zeros_like(sum_out)
            each(slot_row, 2 * half, 0)

            def piece(for_t):
                return bias_all[:, pl.ds(pl.multiple_of((core * n_t + for_t) * width, 128), width)]

            bias_send[...] = piece(1 - t)
            bias_copy = remote(bias_send, bias_land, b_sems.at[0], b_sems.at[1], across_t)
            bias_copy.start()
            bias_copy.wait()
            bias_out[...] = jnp.where(t == chip, piece(t), bias_land[...])
        for p in range(2):
            each(lambda k: back_in(p, k).wait_recv())
        if backward:
            back_out[...] = land_back[...]
            relay(0, 3)
            relay(1, 3)
            g_own.wait()
            for origin in range(n_h):
                @pl.when((origin < h) & (h < n_h - 1))
                def _():
                    for i in range(own_images):
                        z_hop(i, origin, 1).wait_send()

                @pl.when((origin > h) & (h > 0))
                def _():
                    for i in range(own_images):
                        z_hop(i, origin, 0).wait_send()

            @pl.when(h < n_h - 1)
            def _():
                for i in range(own_images):
                    z_hop(i, h, 1, output.at[i]).wait_send()

            @pl.when(h > 0)
            def _():
                for i in range(own_images):
                    z_hop(i, h, 0, output.at[i]).wait_send()

        for p in range(2):
            each(lambda k: block_out(p, k).wait_send())
            each(lambda k: back_copy(p, k).wait_send())
        for copy in (core_copy, x_copy, act_copy):
            each(lambda j: copy(j).wait_send(), half, 0)

    run(False)
    for copy in kept:
        copy.wait()
    middle_kernel(
        sizes, back_both.at[0], small, combine_v, hidden_v, cotangent_v, output, blocks_1, grad_logits,
        padded,
    )
    run(True)
    for store in stores:
        store.wait()


def experts_pass(sizes, blocks, weights, small, combine, hidden, cotangent, bias_width):
    _, experts, rows, width = weights.shape
    devices = sizes[0] * sizes[1] * sizes[2]
    images = 2 * devices
    half = experts // 2
    vmem = pl.BlockSpec(memory_space=pltpu.VMEM)
    hbm = pl.BlockSpec(memory_space=pl.ANY)
    shape, dma = jax.ShapeDtypeStruct, pltpu.SemaphoreType.DMA
    slots, act = (experts, images, rows), (experts, images, width)
    chunk = (half, images, width)
    block = (2, devices, experts, rows)
    own = hidden.shape[0]
    weight = pltpu.VMEM((experts, rows, width), BF16)
    return pl.pallas_call(
        partial(experts_kernel, sizes),
        out_shape=(
            shape(slots, BF16), shape(act, BF16), shape(slots, BF16), shape(act, BF16),
            shape(block, BF16), shape((experts, bias_width), F32), shape((experts, 256), F32),
            shape((own, hidden.shape[1], 64), F32),
            shape((sizes[1] * own, *hidden.shape[1:]), BF16),
        ),
        in_specs=[vmem, hbm, vmem, hbm, hbm, hbm],
        out_specs=(hbm, hbm, hbm, hbm, vmem, vmem, vmem, vmem, hbm),
        scratch_shapes=[
            weight, weight,
            pltpu.VMEM(chunk, F32), pltpu.VMEM(chunk, F32),
            pltpu.VMEM((2, *slots), BF16), pltpu.VMEM((2, *act), BF16),
            pltpu.VMEM(chunk, BF16), pltpu.VMEM((2, *chunk), BF16),
            pltpu.VMEM(chunk, BF16), pltpu.VMEM((2, *chunk), BF16),
            pltpu.VMEM((2, *block), BF16), pltpu.VMEM(slots, BF16),
            pltpu.VMEM(block, BF16), pltpu.VMEM((2, *block), BF16),
            pltpu.VMEM(blocks.shape, BF16), pltpu.VMEM(hidden.shape, BF16),
            pltpu.VMEM(combine.shape, F32), pltpu.VMEM(hidden.shape, F32),
            pltpu.VMEM(cotangent.shape, BF16), pltpu.VMEM((2, 128, 256), F32),
            pltpu.VMEM((experts, width), F32), pltpu.VMEM((experts, width), F32),
            pltpu.VMEM((experts, bias_width), F32), pltpu.VMEM((experts, bias_width), F32),
            dma((2,)), dma((2, 2)), dma((3,)), dma((2, 2, 2, devices)), dma((2, 2, 2, devices)),
            dma((2, 2, half)), dma((2, 2, half)), dma((2, 2, half)), dma((2,)),
            dma((own, sizes[1], 2)), dma((own, sizes[1])), dma,
        ],
        compiler_params=pltpu.CompilerParams(
            collective_id=1, has_side_effects=True, vmem_limit_bytes=VMEM_BYTES
        ),
        name="experts",
    )(blocks, weights, small, combine, hidden, cotangent)


def weight_grad_kernel(slots_0, act_0, slots_1, act_1, out, lines, pick, same):
    group, images, rows = slots_0.shape
    d_block = out.shape[0]
    few = group // 2
    m, d = pl.program_id(0), pl.program_id(2)

    @pl.when((m == 0) & (pl.program_id(1) == 0) & (d == 0))
    def _():
        row = lax.broadcasted_iota(jnp.int32, pick.shape[1:], 0)
        column = lax.broadcasted_iota(jnp.int32, pick.shape[1:], 1)
        second = (row % group) // few
        for half in range(2):
            feature = 2 * (row // group) + (second if half == 0 else 1 - second)
            pick[half] = (column == feature).astype(F32).astype(BF16)
        row = lax.broadcasted_iota(jnp.int32, same.shape, 0)
        column = lax.broadcasted_iota(jnp.int32, same.shape, 1)
        same[...] = (row % few == column // images).astype(F32)

    def prepare(slots):
        @pl.when(d == 0)
        def _():
            turned = slots[...].reshape(group * images, rows).astype(F32)
            lines[...] = jnp.swapaxes(turned, 0, 1).astype(BF16)

    def term(act):
        mine = lines[pl.ds(pl.multiple_of(d * d_block, d_block), d_block)]
        width = act.shape[2]
        results = []
        for half in range(2):
            columns = mine[:, half * few * images : (half + 1) * few * images]
            spread = (dot(pick[half], columns) * same[...]).astype(BF16)
            values = act[half * few : (half + 1) * few].reshape(few * images, width)
            results.append(dot(spread, values).reshape(d_block // 2, group, width))
        first, last = results
        low = lax.broadcasted_iota(jnp.int32, first.shape, 1) < few
        even = jnp.where(low, first, last)
        odd = pltpu.roll(jnp.where(low, last, first), few, 1)
        out[...] = jnp.stack((even, odd), axis=1).reshape(out.shape)

    @pl.when(m == 0)
    def _():
        prepare(slots_0)
        term(act_0)

    @pl.when(m == 1)
    def _():
        prepare(slots_1)
        term(act_1)


def weight_grads(slots_0, act_0, slots_1, act_1):
    experts, images, rows = slots_0.shape
    hidden = act_0.shape[2]
    group, d_block = 8, 192
    last = experts // group - 1

    def early(m, g, d):
        return jnp.where(m == 0, g, last), 0, 0

    def late(m, g, d):
        return jnp.where(m == 0, 0, g), 0, 0

    slots, act = (group, images, rows), (group, images, hidden)
    return pl.pallas_call(
        weight_grad_kernel,
        grid=(2, experts // group, rows // d_block),
        out_shape=jax.ShapeDtypeStruct((rows, 2, experts, hidden), F32),
        in_specs=[
            pl.BlockSpec(slots, early), pl.BlockSpec(act, early),
            pl.BlockSpec(slots, late), pl.BlockSpec(act, late),
        ],
        out_specs=pl.BlockSpec((d_block, 1, group, hidden), lambda m, g, d: (d, m, g, 0)),
        scratch_shapes=[
            pltpu.VMEM((rows, group * images), BF16),
            pltpu.VMEM((2, group * d_block // 2, d_block), BF16),
            pltpu.VMEM((group * d_block // 2, group * images // 2), F32),
        ],
        compiler_params=pltpu.CompilerParams(vmem_limit_bytes=VMEM_BYTES),
        cost_estimate=pl.CostEstimate(
            flops=4 * images * experts * rows * hidden,
            bytes_accessed=8 * rows * experts * hidden,
            transcendentals=0,
        ),
        name="weight_grads",
    )(slots_0, act_0, slots_1, act_1)


def dot_r(a, b):
    return lax.dot_general(a, b, (((0,), (0,)), ((), ())), preferred_element_type=F32)


def row_of(shape, axis):
    return lax.broadcasted_iota(jnp.int32, shape, axis)


def one_hot(mask):
    return mask.astype(F32).astype(BF16)


def order_matrix(n_h, few, back):
    n = n_h * 8 * few
    shape = (n, n)
    blocked, natural = row_of(shape, 1 if back else 0), row_of(shape, 0 if back else 1)
    f, half, image = blocked % few, (blocked // few) % 2, (blocked // (2 * few)) % 2
    group = blocked // (4 * few)
    if back:
        part, h = group // n_h, group % n_h
    else:
        h, part = group // 2, group % 2
    expert = ((h * 2 + half) * 2 + part) * few + f
    return one_hot(natural == image * (4 * n_h * few) + expert)


def norm_parts(x, scale, shift, live):
    centered = x - jnp.mean(x, axis=-1, keepdims=True)
    inverse = lax.rsqrt(jnp.mean(centered * centered, axis=-1, keepdims=True) + epsilon)
    unit = centered * inverse
    return unit * scale + shift, unit, inverse


def norm_back(grad, unit, inverse, scale):
    scaled = grad * scale
    average = jnp.mean(scaled, axis=-1, keepdims=True)
    projection = jnp.mean(scaled * unit, axis=-1, keepdims=True)
    return (
        inverse * (scaled - average - unit * projection),
        jnp.sum(grad * unit, axis=0, keepdims=True),
        jnp.sum(grad, axis=0, keepdims=True),
    )


def norm_rows(small):
    return jnp.swapaxes(small[:, 128:].astype(F32), 0, 1)[64:68]


def slots_to_blocks(slots, blocks, columns, joined, order):
    n_h, n_s = blocks.shape[:2]
    turned = dot(order, slots).astype(BF16)
    wide = joined.shape[1] // 2
    for s in range(0, n_s, 2):
        lanes = dot(turned[:, s * columns : (s + 2) * columns], joined).astype(BF16)
        for h in range(n_h):
            for p in range(2):
                rows = (h * 2 + p) * 16
                for e in range(2):
                    blocks[h, s + e, p] = lanes[rows : rows + 16, e * wide : e * wide + columns]


def blocks_to_slots(back, sizes, order, pair, padded):
    n_s, n_h, n_t = sizes
    columns = back.shape[3]
    both = jnp.concatenate([order] * n_t, axis=1)
    results = []
    for s in range(n_s):
        rows = jnp.concatenate(
            [
                back[p, (s * n_h + h) * n_t + t]
                for t in range(n_t)
                for p in range(2)
                for h in range(n_h)
            ],
            axis=0,
        )
        padded[s % 2, :, :columns] = dot(both, rows)
        if s % 2:
            value = jnp.concatenate([padded[0], padded[1]], axis=1)
            high = value.astype(BF16)
            rest = (value - high.astype(F32)).astype(BF16)
            results.append(dot(high, pair) + dot(rest, pair))
    return jnp.concatenate(results, axis=1)


def live_rows(shape, length):
    return row_of(shape, 0) < length


class Ahead:
    def __init__(self, length, tokens, small, w, blocks, dispatch, combine, held, joined, order):
        self.length, self.tokens, self.small, self.w = length, tokens, small, w
        self.blocks, self.dispatch, self.combine = blocks, dispatch, combine
        self.normed_1, self.query, self.keyed, self.valued = held[:4]
        self.context, self.hidden, self.normed_2 = held[4:]
        self.joined, self.order = joined, order
        self.n, self.rows, self.width = tokens.shape
        self.live = live_rows((self.rows, 1), length)

    def first_norm(self):
        self.norms = norm_rows(self.small)
        for i in range(self.n):
            value, _, _ = norm_parts(
                self.tokens[i].astype(F32), self.norms[0:1], self.norms[2:3], self.live
            )
            self.normed_1[i] = jnp.where(self.live, value, 0.0).astype(BF16)
        self.joined[...] = pair_matrix(self.blocks.shape[4], self.joined.shape[1] // 2, True)
        self.order[...] = order_matrix(self.blocks.shape[0], 4, False)

    def project(self, k):
        n, rows, width = self.n, self.rows, self.width
        flat = self.normed_1[...].reshape(n * rows, width)
        value = dot(flat, self.w[k]).astype(BF16).reshape(n, rows, width)
        if k == 0:
            self.query[...] = value
        else:
            target = self.keyed if k == 1 else self.valued
            keys = target.shape[1]
            target[:, :rows] = value
            target[:, rows:] = jnp.zeros((n, keys - rows, width), BF16)

    def attend(self):
        query, keyed, valued, context = self.query, self.keyed, self.valued, self.context
        rows, keys = self.rows, keyed.shape[1]
        factor = HEAD_DIM ** (-0.5)
        pairs = self.width // 128
        lane = row_of((rows, 128), 1)
        shown = row_of((rows, keys), 1) < self.length

        def attend(step, carry):
            i = step // pairs
            lanes = pl.ds(pl.multiple_of((step % pairs) * 128, 128), 128)
            q, k, v = query[i, :, lanes], keyed[i, :, lanes], valued[i, :, lanes]
            scaled = q * jnp.bfloat16(factor)
            parts = []
            for a in range(2):
                mine = (lane < 64) if a == 0 else (lane >= 64)
                scores = dot_t(jnp.where(mine, scaled, jnp.zeros_like(q)), k)
                scores = jnp.where(shown, scores, -1e30)
                exponent = jnp.exp(scores - jnp.max(scores, axis=-1, keepdims=True))
                probs = exponent * (1.0 / jnp.sum(exponent, axis=-1, keepdims=True))
                parts.append(dot(probs.astype(BF16), v))
            context[i, :, lanes] = jnp.where(lane < 64, parts[0], parts[1]).astype(BF16)
            return carry

        lax.fori_loop(0, self.n * pairs, attend, 0, unroll=6)

    def finish(self):
        n, rows, width = self.n, self.rows, self.width
        flat = (n * rows, width)
        live = self.live
        attended = dot_t(self.context[...].reshape(flat), self.w[3]).reshape(n, rows, width)
        for i in range(n):
            value = self.tokens[i].astype(F32) + attended[i]
            self.hidden[i] = value
            value, _, _ = norm_parts(value, self.norms[1:2], self.norms[3:4], live)
            self.normed_2[i] = jnp.where(live, value, 0.0).astype(BF16)
        logits = dot(self.normed_2[...].reshape(flat), self.small[:, :128]).reshape(n, rows, 128)
        experts = row_of((rows, 128), 1) < 64
        slots = []
        for i in range(n):
            here = logits[i]
            down = jnp.where(live, here, -1e30)
            exponent = jnp.exp(down - jnp.max(down, axis=0, keepdims=True))
            dispatch = exponent / jnp.sum(exponent, axis=0, keepdims=True)
            dispatch = jnp.where(experts, dispatch, 0.0)
            across = jnp.where(experts, here, -1e30)
            exponent = jnp.exp(across - jnp.max(across, axis=1, keepdims=True))
            combine = exponent / jnp.sum(exponent, axis=1, keepdims=True)
            self.dispatch[i] = dispatch
            self.combine[i] = combine
            slots.append(dot_r(dispatch.astype(BF16), self.normed_2[i])[:64].astype(BF16))
        slots_to_blocks(
            jnp.concatenate(slots, axis=0), self.blocks, self.blocks.shape[4], self.joined[...],
            self.order[...],
        )


def middle_kernel(
    sizes, back, small, combine, hidden, cotangent, output, blocks, grad_logits, padded
):
    n, rows, _ = hidden.shape
    columns = back.shape[3]
    padded[...] = jnp.zeros_like(padded)
    pair = pair_matrix(columns, padded.shape[2], False)
    joined = pair_matrix(columns, padded.shape[2], True)
    total = blocks_to_slots(back, sizes, order_matrix(sizes[1], 4, True), pair, padded)
    bias = jnp.swapaxes(small[:, :128].astype(F32), 0, 1)[64:]
    slots = []
    for i in range(n):
        slot_out = (total[i * 64 : (i + 1) * 64] + bias).astype(BF16)
        combine_b = combine[i].astype(BF16)[:, :64]
        output[i] = (hidden[i] + dot(combine_b, slot_out)).astype(BF16)
        grad_combine = dot_t(cotangent[i], slot_out)
        weight = combine[i][:, :64]
        weighted = jnp.sum(weight * grad_combine, axis=1, keepdims=True)
        grad_logits[i] = weight * (grad_combine - weighted)
        slots.append(dot_r(combine_b, cotangent[i]).astype(BF16))
    slots_to_blocks(
        jnp.concatenate(slots, axis=0), blocks, columns, joined, order_matrix(sizes[1], 4, False)
    )


def behind_kernel(
    sizes, length, back, small, w_hbm, *refs,
):
    later, refs = refs[:9], refs[9:]
    (dispatch, grad_logits, grads_out, small_grads, input_grad,
     w, padded, grad_hidden, rounded, grad_context, grad_q, grad_k, grad_v, grads, *refs) = refs
    held, (w_sem, l_sem, g_sem) = refs[:9], refs[9:]
    n, rows, width = grad_hidden.shape
    later_loads = [
        pltpu.make_async_copy(source, target, l_sem.at[j])
        for j, (source, target) in enumerate(zip(later, held))
    ]
    context, query, keyed, valued, normed_1, tokens, hidden, normed_2, cotangent = held
    keys = keyed.shape[1]
    loads = [pltpu.make_async_copy(w_hbm.at[k], w.at[k], w_sem.at[k]) for k in range(4)]
    for load in later_loads[6:] + loads[3:] + later_loads[:6] + loads[:3]:
        load.start()
    norms = norm_rows(small)
    padded[...] = jnp.zeros_like(padded)
    pair = pair_matrix(back.shape[3], padded.shape[2], False)
    grad_slots = blocks_to_slots(
        back, sizes, order_matrix(sizes[1], 4, True), pair, padded
    ).astype(BF16)
    phi = small[:, :64]
    phi_grad = jnp.zeros((width, 64), F32)
    sums = []
    flat = (n * rows, width)
    for load in later_loads[6:]:
        load.wait()
    for i in range(n):
        slots = grad_slots[i * 64 : (i + 1) * 64]
        weight = dispatch[i][:, :64]
        grad_dispatch = dot_t(normed_2[i], slots)
        weighted = jnp.sum(weight * grad_dispatch, axis=0, keepdims=True)
        logits = (weight * (grad_dispatch - weighted) + grad_logits[i]).astype(BF16)
        phi_grad = phi_grad + dot_r(normed_2[i], logits)
        grad = dot(weight.astype(BF16), slots) + dot_t(logits, phi)
        _, unit, inverse = norm_parts(hidden[i], norms[1:2], norms[3:4], None)
        grad_in, scale_grad, bias_grad = norm_back(grad, unit, inverse, norms[1:2])
        value = cotangent[i].astype(F32) + grad_in
        grad_hidden[i] = value
        rounded[i] = value.astype(BF16)
        sums.append((scale_grad, bias_grad))
    scale_2, bias_2 = sums[0][0] + sums[1][0], sums[0][1] + sums[1][1]
    flat_rounded = rounded[...].reshape(flat)
    loads[3].wait()
    grad_context[...] = dot(flat_rounded, w[3]).astype(BF16).reshape(n, rows, width)
    later_loads[0].wait()
    grads[3] = dot_r(flat_rounded, context[...].reshape(flat)).astype(BF16)
    stores = [pltpu.make_async_copy(grads.at[k], grads_out.at[k], g_sem.at[k]) for k in range(4)]
    stores[3].start()
    for load in later_loads[1:4]:
        load.wait()
    factor = HEAD_DIM ** (-0.5)
    pairs = width // 128
    lane = row_of((rows, 128), 1)
    key_lane = row_of((keys, 128), 1)
    shown = row_of((keys, rows), 0) < length

    def attend(step, carry):
        i = step // pairs
        lanes = pl.ds(pl.multiple_of((step % pairs) * 128, 128), 128)
        q, k, v = query[i, :, lanes], keyed[i, :, lanes], valued[i, :, lanes]
        scaled = q * jnp.bfloat16(factor)
        g = grad_context[i, :, lanes]
        to_q, to_k, to_v = [], [], []
        for a in range(2):
            mine = (lane < 64) if a == 0 else (lane >= 64)
            scores = dot_t(k, jnp.where(mine, scaled, jnp.zeros_like(q)))
            grad_probs = dot_t(v, jnp.where(mine, g, jnp.zeros_like(g)))
            scores = jnp.where(shown, scores, -1e30)
            exponent = jnp.exp(scores - jnp.max(scores, axis=0, keepdims=True))
            probs = exponent * (1.0 / jnp.sum(exponent, axis=0, keepdims=True))
            weighted = jnp.sum(probs * grad_probs, axis=0, keepdims=True)
            grad_scores = (probs * (grad_probs - weighted)).astype(BF16)
            to_v.append(dot(probs.astype(BF16), g))
            to_q.append(dot_r(grad_scores, k))
            to_k.append(dot(grad_scores, q))
        grad_q[i, :, lanes] = (jnp.where(lane < 64, to_q[0], to_q[1]) * factor).astype(BF16)
        kept = key_lane < 64
        grad_k[i, :, lanes] = (jnp.where(kept, to_k[0], to_k[1]) * factor)[:rows].astype(BF16)
        grad_v[i, :, lanes] = jnp.where(kept, to_v[0], to_v[1])[:rows].astype(BF16)
        return carry

    lax.fori_loop(0, n * pairs, attend, 0, unroll=6)
    for load in later_loads[4:6]:
        load.wait()
    total = jnp.zeros(flat, F32)
    turned = jnp.swapaxes(normed_1[...].reshape(flat).astype(F32), 0, 1).astype(BF16)
    for k, source in enumerate((grad_q, grad_k, grad_v)):
        loads[k].wait()
        value = source[...].reshape(flat)
        total = total + dot_t(value, w[k])
        grads[k] = dot(turned, value).astype(BF16)
        stores[k].start()
    total = total.reshape(n, rows, width)
    sums = []
    for i in range(n):
        _, unit, inverse = norm_parts(tokens[i].astype(F32), norms[0:1], norms[2:3], None)
        grad_in, scale_grad, bias_grad = norm_back(total[i], unit, inverse, norms[0:1])
        input_grad[i] = (grad_hidden[i] + grad_in).astype(BF16)
        sums.append((scale_grad, bias_grad))
    scale_1, bias_1 = sums[0][0] + sums[1][0], sums[0][1] + sums[1][1]
    line = row_of((128, width), 0)
    spread = jnp.zeros((128, width), F32)
    for j, value in enumerate((scale_1, scale_2, bias_1, bias_2)):
        spread = jnp.where(line == 64 + j, value, spread)
    small_grads[...] = jnp.swapaxes(spread, 0, 1).astype(BF16)
    small_grads[:, :64] = phi_grad.astype(BF16)
    for store in stores:
        store.wait()


def tokens_behind(sizes, length, back, small, weights, later, dispatch, grad_logits):
    tokens = later[5]
    n, rows, width = tokens.shape
    vmem, hbm = pl.BlockSpec(memory_space=pltpu.VMEM), pl.BlockSpec(memory_space=pl.ANY)
    shape = jax.ShapeDtypeStruct
    low = pltpu.VMEM(tokens.shape, BF16)
    return pl.pallas_call(
        partial(behind_kernel, sizes, length),
        out_shape=(
            shape((4, width, width), BF16), shape((width, 128), BF16), shape(tokens.shape, BF16)
        ),
        in_specs=[vmem, vmem] + [hbm] * 10 + [vmem] * 2,
        out_specs=(hbm, vmem, vmem),
        scratch_shapes=[
            pltpu.VMEM(weights.shape, BF16),
            pltpu.VMEM((2, 128, 256), F32),
            pltpu.VMEM(tokens.shape, F32),
            low, low, low, low, low,
            pltpu.VMEM((4, width, width), BF16),
            *[pltpu.VMEM(value.shape, value.dtype) for value in later],
            pltpu.SemaphoreType.DMA((4,)), pltpu.SemaphoreType.DMA((9,)),
            pltpu.SemaphoreType.DMA((4,)),
        ],
        compiler_params=pltpu.CompilerParams(vmem_limit_bytes=VMEM_BYTES),
        name="tokens_behind",
    )(back, small, weights, *later, dispatch, grad_logits)


def unpack_kernel(summed, in_bias_sum, out_sum, attn, phi_t, scales, biases, in_bias, out_bias):
    attn[...] = summed[:, :, : attn.shape[2]]
    turned = jnp.swapaxes(summed[0][:, 128:], 0, 1)
    phi_t[...] = turned[64:80]
    scales[...] = turned[80:82]
    biases[...] = turned[82:84]
    in_bias[...] = in_bias_sum[...]
    width = out_bias.shape[1]
    value = out_sum[...]
    later = pltpu.roll(value, value.shape[1] - width, 1)
    out_bias[...] = jnp.where(lax.axis_index("tensor") == 0, value[:, :width], later[:, :width])


def order_kernel(mine, below, above, below_2, above_2, far, out):
    h = lax.axis_index("heads")
    own, rows, width = mine.shape
    group = out.shape[1]
    first_h, low = h == 0, h < 2
    inner = (h == 1) | (h == 2)
    origins = (
        h,
        jnp.where(first_h, h + 1, h - 1),
        jnp.where(low, h + 2, h - 2),
        jnp.where(inner, h + 1, 3 - h),
    )
    step = 256 // group
    length = out.shape[0]
    for first in range(0, length, step):
        count = min(step, length - first)
        taken = min(step, rows - first)
        shape = (count * group, own * taken)
        row = lax.broadcasted_iota(jnp.int32, shape, 0)
        column = lax.broadcasted_iota(jnp.int32, shape, 1)
        there = row // group == column % taken
        image = row % group - column // taken
        chosen = [(there & (image == origin * own)).astype(F32) for origin in origins]

        def lines(part):
            return [part[i, first : first + taken] for i in range(own)]

        def either(condition, one, other):
            return [jnp.where(condition, a, b) for a, b in zip(lines(one), lines(other))]

        values = lines(mine) + either(first_h, above, below)
        values += either(low, above_2, below_2) + either(inner, above, far)
        value = dot(
            jnp.concatenate(chosen, axis=1).astype(BF16), jnp.concatenate(values, axis=0)
        ).astype(BF16)
        out[first : first + count] = value.reshape(count, group, width)


def last_kernel(summed, in_bias_sum, out_sum, *refs):
    unpack_kernel(summed, in_bias_sum, out_sum, *refs[6:12])
    order_kernel(*refs[:6], refs[12])


def last_results(summed, in_bias_sum, out_sum, parts, block, slot, group, length):
    n_k, rows, _ = summed.shape
    vmem = pl.BlockSpec(memory_space=pltpu.VMEM)
    shape = jax.ShapeDtypeStruct
    return pl.pallas_call(
        last_kernel,
        out_shape=(
            shape((n_k, rows, block), F32), shape((slot, rows), F32),
            shape((2, rows), F32), shape((2, rows), F32),
            shape(in_bias_sum.shape, F32), shape((out_sum.shape[0], rows), F32),
            shape((length, group, parts[0].shape[2]), BF16),
        ),
        in_specs=[vmem] * 9,
        out_specs=(vmem,) * 7,
        compiler_params=pltpu.CompilerParams(vmem_limit_bytes=24 * 1024 * 1024),
        name="last_results",
    )(summed, in_bias_sum, out_sum, *parts)


def normalize(values, scale, shift):
    centered = values - jnp.mean(values, axis=-1, keepdims=True)
    variance = jnp.mean(centered * centered, axis=-1, keepdims=True)
    inverse = lax.rsqrt(variance + epsilon)
    unit_part = centered * inverse
    return (unit_part * scale + shift, unit_part, inverse)


def normalize_back(grad_output, unit_part, inverse, scale):
    scaled = grad_output * scale
    average = jnp.mean(scaled, axis=-1, keepdims=True)
    projection = jnp.mean(scaled * unit_part, axis=-1, keepdims=True)
    grad_input = inverse * (scaled - average - unit_part * projection)
    return (
        grad_input,
        jnp.sum(grad_output * unit_part, axis=(0, 1)),
        jnp.sum(grad_output, axis=(0, 1)),
    )


def to_experts(slots):
    slots = lax.all_to_all(slots, "heads", split_axis=1, concat_axis=0, tiled=True)
    slots = lax.all_to_all(slots, "shard", split_axis=2, concat_axis=0, tiled=True)
    return lax.all_gather(slots, "tensor", axis=0, tiled=True)


def to_images(slots):
    slots = lax.psum_scatter(slots, "tensor", scatter_dimension=0, tiled=True)
    slots = lax.all_to_all(slots, "shard", split_axis=0, concat_axis=2, tiled=True)
    return lax.all_to_all(slots, "heads", split_axis=0, concat_axis=1, tiled=True)


def general_shards(tokens, norm_scales, norm_biases, w_attn, phi, experts, in_bias, out_bias, cotangent):
    heads_n = lax.axis_size("heads")
    group, seq_len, width = tokens.shape
    own = group // heads_n
    heads_index = lax.axis_index("heads")
    tensor_index = lax.axis_index("tensor")
    shard_index = lax.axis_index("shard")
    hidden = experts.shape[3]
    rows = experts.shape[0]
    scales, biases, in_full = (
        lax.all_gather(norm_scales, ROWS, axis=1, tiled=True).astype(F32),
        lax.all_gather(norm_biases, ROWS, axis=1, tiled=True).astype(F32),
        lax.all_gather(in_bias, ROWS, axis=1, tiled=True).astype(F32),
    )
    attn = lax.all_gather(
        lax.all_gather(w_attn, "heads", axis=2, tiled=True), ROWS, axis=1, tiled=True
    )
    phi_full = lax.all_gather(
        lax.all_gather(phi, "heads", axis=1, tiled=True), ROWS, axis=0, tiled=True
    )
    out_rows = lax.all_gather(out_bias, "tensor", axis=1, tiled=True).astype(F32)
    e_own = experts.shape[2] // lax.axis_size("shard")
    in_local = lax.dynamic_slice_in_dim(in_full, tensor_index * hidden, hidden, 1)
    factor = HEAD_DIM ** (-0.5)
    tokens = lax.dynamic_slice_in_dim(tokens, heads_index * own, own, 0)
    cotangent = lax.dynamic_slice_in_dim(cotangent, heads_index * own, own, 0)
    n_heads = width // HEAD_DIM
    inputs = tokens.astype(F32)
    normed_one, unit_one, inverse_one = normalize(inputs, scales[0], biases[0])
    normed_one_b = normed_one.astype(BF16)
    projected = einsum("nsd,kdc->knsc", normed_one_b, attn[:3]).astype(BF16)
    query, keyed, valued = projected.reshape(3, own, seq_len, n_heads, HEAD_DIM)
    scores = einsum("nqhe,nkhe->nhqk", query, keyed) * factor
    score_peak = jnp.max(scores, axis=-1, keepdims=True)
    exponent = jnp.exp(scores - score_peak)
    probs = exponent / jnp.sum(exponent, axis=-1, keepdims=True)
    probs_b = probs.astype(BF16)
    context_b = (
        einsum("nhqk,nkhe->nqhe", probs_b, valued).astype(BF16).reshape(own, seq_len, width)
    )
    hidden_one = inputs + einsum("nsc,dc->nsd", context_b, attn[3])
    normed_two, unit_two, inverse_two = normalize(hidden_one, scales[1], biases[1])
    normed_two_b = normed_two.astype(BF16)
    logits = einsum("nsd,de->nse", normed_two_b, phi_full)
    dispatch = jax.nn.softmax(logits, axis=1)
    dispatch_b = dispatch.astype(BF16)
    combine = jax.nn.softmax(logits, axis=2)
    combine_b = combine.astype(BF16)
    slot_in = to_experts(einsum("nse,nsd->ned", dispatch_b, normed_two_b).astype(BF16))
    share = 1 if e_own else 0

    def meet(partial_sum):
        return lax.psum_scatter(partial_sum, "shard", scatter_dimension=share, tiled=True)

    def spread(values):
        return lax.all_gather(values, "shard", axis=share, tiled=True)

    pre = meet(einsum("ned,def->nef", slot_in, experts[:, 0]))
    if e_own:
        pre = pre + lax.dynamic_slice_in_dim(in_local, shard_index * e_own, e_own, 0)
    else:
        pre = pre + in_local
    gelu_value, gelu_back = jax.vjp(partial(jax.nn.gelu, approximate=False), pre)
    activated = spread(gelu_value.astype(BF16))
    slot_out_part = einsum("nef,def->ned", activated, experts[:, 1])
    slot_out_part = slot_out_part + jnp.where(tensor_index == 0, out_rows, 0.0)
    slot_out = to_images(slot_out_part).astype(BF16)
    output = (hidden_one + einsum("nse,ned->nsd", combine_b, slot_out)).astype(BF16)
    output = lax.all_gather(output, "heads", axis=0, tiled=True)
    grad_combine = einsum("nsd,ned->nse", cotangent, slot_out)
    grad_slot = to_experts(einsum("nse,nsd->ned", combine_b, cotangent).astype(BF16))
    grad_act = meet(einsum("ned,def->nef", grad_slot, experts[:, 1]))
    grad_pre = spread(gelu_back(grad_act)[0].astype(BF16))
    grad_slot_in = einsum("nef,def->ned", grad_pre, experts[:, 0]).astype(BF16)
    input_term = einsum("ned,nef->def", slot_in, grad_pre)
    output_term = einsum("ned,nef->def", grad_slot, activated)
    experts_grad = jnp.stack((input_term, output_term), axis=1)
    grad_slot_in = to_images(grad_slot_in.astype(F32)).astype(BF16)
    in_bias_grad = lax.dynamic_slice_in_dim(
        lax.all_gather(jnp.sum(grad_pre.astype(F32), axis=0), "tensor", axis=1, tiled=True),
        (shard_index * lax.axis_size("tensor") + tensor_index) * in_bias.shape[1],
        in_bias.shape[1],
        1,
    )
    out_bias_grad = lax.dynamic_slice_in_dim(
        jnp.sum(grad_slot.astype(F32), axis=0),
        tensor_index * out_bias.shape[1],
        out_bias.shape[1],
        1,
    )
    grad_dispatch = einsum("nsd,ned->nse", normed_two_b, grad_slot_in)
    grad_logits = (
        dispatch * (grad_dispatch - jnp.sum(dispatch * grad_dispatch, axis=1, keepdims=True))
        + combine * (grad_combine - jnp.sum(combine * grad_combine, axis=2, keepdims=True))
    ).astype(BF16)
    phi_grad = einsum("nsd,nse->de", normed_two_b, grad_logits)
    grad_normed_two = einsum("nse,ned->nsd", dispatch_b, grad_slot_in) + einsum(
        "nse,de->nsd", grad_logits, phi_full
    )
    grad_hidden_norm, scale_two_grad, bias_two_grad = normalize_back(
        grad_normed_two, unit_two, inverse_two, scales[1]
    )
    grad_hidden = cotangent.astype(F32) + grad_hidden_norm
    grad_hidden_b = grad_hidden.astype(BF16)
    out_weight_grad = einsum("nsd,nsc->dc", grad_hidden_b, context_b)
    grad_context = einsum("nsd,dc->nsc", grad_hidden_b, attn[3]).astype(BF16)
    grad_context = grad_context.reshape(own, seq_len, n_heads, HEAD_DIM)
    grad_value = einsum("nhqk,nqhe->nkhe", probs_b, grad_context).astype(BF16)
    grad_probs = einsum("nqhe,nkhe->nhqk", grad_context, valued)
    grad_scores = (
        probs * (grad_probs - jnp.sum(probs * grad_probs, axis=-1, keepdims=True))
    ).astype(BF16)
    grad_query = (einsum("nhqk,nkhe->nqhe", grad_scores, keyed) * factor).astype(BF16)
    grad_key = (einsum("nhqk,nqhe->nkhe", grad_scores, query) * factor).astype(BF16)
    grad_proj = jnp.stack((grad_query, grad_key, grad_value)).reshape(3, own, seq_len, width)
    proj_grad = einsum("nsd,knsc->kdc", normed_one_b, grad_proj)
    grad_normed_one = einsum("knsc,kdc->nsd", grad_proj, attn[:3])
    grad_input_norm, scale_one_grad, bias_one_grad = normalize_back(
        grad_normed_one, unit_one, inverse_one, scales[0]
    )
    input_grad = (grad_hidden + grad_input_norm).astype(BF16)
    input_grad = lax.all_gather(input_grad, "heads", axis=0, tiled=True)
    attn_grad = jnp.concatenate((proj_grad, out_weight_grad[None]), axis=0)
    attn_grad = lax.psum_scatter(attn_grad, ROWS, scatter_dimension=1, tiled=True)
    attn_grad = lax.psum_scatter(attn_grad, "heads", scatter_dimension=2, tiled=True)
    phi_grad = lax.psum_scatter(phi_grad, ROWS, scatter_dimension=0, tiled=True)
    phi_grad = lax.psum_scatter(phi_grad, "heads", scatter_dimension=1, tiled=True)
    norms = jnp.stack((scale_one_grad, scale_two_grad, bias_one_grad, bias_two_grad))
    norms = lax.psum(lax.psum_scatter(norms, ROWS, scatter_dimension=1, tiled=True), "heads")
    return (
        output,
        input_grad,
        norms[:2],
        norms[2:],
        attn_grad,
        phi_grad,
        experts_grad,
        in_bias_grad,
        out_bias_grad,
    )


def shards(tokens, norm_scales, norm_biases, w_attn, phi, experts, in_bias, out_bias, cotangent):
    arrays = (tokens, norm_scales, norm_biases, w_attn, phi, experts, in_bias, out_bias, cotangent)
    sizes = tuple(lax.axis_size(name) for name in ("shard", "heads", "tensor"))
    group, length, width = tokens.shape
    fits = (sizes, group, width, *experts.shape[:3]) == ((4, 4, 2), 8, 768, 192, 2, 16)
    if not fits or not 192 < length <= 208 or in_bias.shape[1] != 384:
        return general_shards(*arrays)
    n_s, n_h, n_t = sizes
    block, slot = w_attn.shape[2], phi.shape[1]
    tokens, cotangent = (
        values.transpose(1, 0, 2).reshape(group * length, width) for values in (tokens, cotangent)
    )
    attn, small, turned, tokens, cotangent, blocks, dispatch, combine, *held = gather_weights(
        sizes, length, w_attn, phi.T, out_bias, norm_scales, norm_biases, in_bias, experts, tokens,
        cotangent,
    )
    normed_1, query, keyed, valued, context, hidden, normed_2 = held
    slot_in, activated, grad_slot, grad_pre, back, in_bias_grad, out_sum, grad_logits, output = (
        experts_pass(
            sizes, blocks, turned, small, combine, hidden, cotangent, in_bias.shape[1]
        )
    )
    attn_grad, small_grad, input_grad = tokens_behind(
        sizes, length, back, small, attn,
        (context, query, keyed, valued, normed_1, tokens, hidden, normed_2, cotangent),
        dispatch, grad_logits,
    )
    def along(values, places):
        return lax.ppermute(values, "heads", places)

    up = [(i, i + 1) for i in range(n_h - 1)]
    down = [(i + 1, i) for i in range(n_h - 1)]
    below, above = along(input_grad, up), along(input_grad, down)
    attn_grad, grad_pre = lax.optimization_barrier((attn_grad, grad_pre))
    experts_grad = weight_grads(slot_in, grad_pre, grad_slot, activated)
    output = output[:, :length].transpose(1, 0, 2)
    attn_grad, experts_grad, output, input_grad, below, above = lax.optimization_barrier(
        (attn_grad, experts_grad, output, input_grad, below, above)
    )
    parts = [
        input_grad, below, above, along(below, up[1:]), along(above, down[:-1]),
        along(input_grad, [(0, n_h - 1), (n_h - 1, 0)]),
    ]
    summed = reduce_grads(sizes, attn_grad, small_grad)
    attn_grad, phi_grad, scales_grad, biases_grad, in_bias_grad, out_bias_grad, input_grad = (
        last_results(summed, in_bias_grad, out_sum, parts, block, slot, group, length)
    )
    return (
        output.transpose(1, 0, 2),
        input_grad.transpose(1, 0, 2),
        scales_grad,
        biases_grad,
        attn_grad,
        phi_grad.T,
        experts_grad,
        in_bias_grad,
        out_bias_grad,
    )


def solution(mesh):
    images = P(ROWS, None, None)
    return jax.shard_map(
        shards,
        mesh=mesh,
        in_specs=(
            images,
            P(None, ROWS),
            P(None, ROWS),
            P(None, ROWS, "heads"),
            P(ROWS, "heads"),
            P("shard", None, "heads", "tensor"),
            P("heads", ROWS),
            P("heads", ROWS),
            images,
        ),
        out_specs=(
            images,
            images,
            P(None, ROWS),
            P(None, ROWS),
            P(None, ROWS, "heads"),
            P(ROWS, "heads"),
            P("shard", None, "heads", "tensor"),
            P("heads", ROWS),
            P("heads", ROWS),
        ),
        check_vma=False,
    )
```
